32 devices in a mesh: group: 2 (over x), depth: 2 (over core), col: 8 (over z, y).
Axes of the slice: x: 2, y: 2, z: 4, core: 2. Of those that a mesh axis runs over, the one named last changes fastest.
Arguments:
- alignment_activations: bfloat16 [256, 32, 256], P(('group', 'depth'), 'col'), parts along dimension 0, may hold values from -8 to 8
- alignment_mask: int32 [256, 32], P(('group', 'depth'), 'col'), parts along dimension 0, may hold values from 0 to 1, as said below
- pair_activation_input: bfloat16 [64, 32, 128], P(('group', 'col'), 'depth'), parts along dimension 0, may hold values from -6 to 6
- pair_update_mask: int32 [64, 32], P(('group', 'col'), 'depth'), parts along dimension 0, may hold values 0 or 1
- pair_output_gradient: bfloat16 [64, 32, 128], P(('group', 'col'), 'depth'), parts along dimension 0, may hold values from -6 to 6
- layer_scale_factor: float32 [256], replicated, may hold values from 0.25 to 1.75
- first_projector: bfloat16 [256, 32], replicated, may hold values from -0.375 to 0.375
- second_projector: bfloat16 [256, 32], replicated, may hold values from -0.375 to 0.375
- output_weight: bfloat16 [1024, 128], replicated, may hold values from -1.5 to 1.5
- pair_norm_gain: float32 [128], replicated, may hold values from 0.25 to 1.75
- hidden_weight: bfloat16 [128, 512], replicated, may hold values from -0.5 to 0.5
- back_weight: bfloat16 [512, 128], replicated, may hold values from -0.25 to 0.25
Outputs:
- features_derivative: bfloat16 [256, 32, 256], P(('group', 'depth'), 'col'), parts along dimension 0
- couple_features_derivative: bfloat16 [64, 32, 128], P(('group', 'col'), 'depth'), parts along dimension 0
- first_projector_derivative: float32 [512, 32], P('group'), parts along dimension 0
- second_projector_derivative: float32 [512, 32], P('group'), parts along dimension 0
- result_matrix_derivative: float32 [2048, 128], P('group'), parts along dimension 0
- middle_matrix_derivative: float32 [256, 512], P('group'), parts along dimension 0
- final_matrix_derivative: float32 [1024, 128], P('group'), parts along dimension 0
The draws below stay inside these ranges and needn't reach their ends.
There are 2 independent parts, one for each index of `group`. The reference program is written for one: setup_inputs(seed, part) draws one part's arguments, and reference() takes and returns one part's arrays. A program takes and returns all parts, laid end to end along the dimension named above; an argument that names none is the same for every part. Nothing has to cross between parts.
Inputs may be any that keep to these rules, and one draw needn't show every extreme that they name: `alignment_mask`: sequence 0 is present at every residue.
All inputs are finite; a program needn't handle non-finite values. No bound on the sum of `pair_update_mask` on one device may be relied on, other than what follows from the above.
Results may differ from the reference program's by a relative error of at most 0.014.
Values may be sent and summed in bfloat16 or wider, within the bound.
No kernel may reach another device: no remote copies, remote signals or barrier semaphores. Data moves between devices by JAX's collectives and lax.ppermute only.
A program may use at most 64 MiB of HBM per device.

```python
import jax
import jax.numpy as jnp
from jax import lax

FEATURE_COUNT = 256
PROJECTOR_WIDTH = 32
CZ = 128
HID = 512
RES_DEV = 4
ALIGNED_COUNT = 128
CROP_LENGTH = 32
OUTER = 1024
N_COL = 8


def draw_alignment_activations(key, part):
    random_seed_factor, random_seed_start = jax.random.split(key, 2)
    feature_factor = jnp.exp(jax.random.uniform(random_seed_factor, (FEATURE_COUNT,), jnp.float32, -1.2, 1.2))
    entries_drawn = jax.random.normal(random_seed_start, (ALIGNED_COUNT, CROP_LENGTH, FEATURE_COUNT), jnp.float32) * feature_factor
    return jnp.clip(entries_drawn, -8.0, 8.0).astype(jnp.bfloat16)


def draw_alignment_mask(key, part):
    seq_index = jnp.arange(ALIGNED_COUNT, dtype=jnp.int32)
    limits = 150 + 800 * seq_index // ALIGNED_COUNT
    tickets = jax.random.randint(key, (ALIGNED_COUNT, CROP_LENGTH), 0, 1000, dtype=jnp.int32)
    present = (tickets < limits[:, None]).astype(jnp.int32)
    return present.at[0].set(1)


def touch_ends(array, rng, smallest, top_value):
    spot = [jax.random.randint(jax.random.fold_in(rng, axis), (), 0, length) for axis, length in enumerate(array.shape)]
    widest = array.shape.index(max(array.shape))
    neighbour = spot[:widest] + [(spot[widest] + 1) % array.shape[widest]] + spot[widest + 1:]
    return array.at[tuple(spot)].set(smallest).at[tuple(neighbour)].set(top_value)


def block_scale(stream_key, shape, cuts, smallest, largest):
    level = 1.0
    for axis_at, parts in cuts:
        steps = jax.random.uniform(jax.random.fold_in(jax.random.fold_in(stream_key, 6), axis_at), (parts,), jnp.float32, smallest / len(cuts), largest / len(cuts))
        level = level * jnp.repeat(jnp.exp(steps), shape[axis_at] // parts).reshape((-1,) + (1,) * (len(shape) - 1 - axis_at))
    return level


def gaussian(key, dims, width, reach, cuts=(), held_as=jnp.bfloat16):
    gain = block_scale(key, dims, cuts, -0.22, 0.18) if cuts else 1.0
    entries = jax.random.normal(key, dims, jnp.float32) * width * gain
    return jnp.minimum(jnp.maximum(entries, -reach), reach).astype(held_as)


def setup_inputs(seed: int = 0, part: int = 0) -> dict:
    splits = jax.random.split(jax.random.key(seed), 13)
    part_keys = jax.random.split(jax.random.fold_in(splits[12], part), 13)
    alignment_activations = draw_alignment_activations(jax.random.fold_in(jax.random.fold_in(splits[12], part), 71), part)
    alignment_mask = draw_alignment_mask(jax.random.fold_in(jax.random.fold_in(splits[12], part), 71), part)
    pair_activation_input = gaussian(part_keys[2], (CROP_LENGTH, CROP_LENGTH, CZ), 1.0, 6.0, ((0, 8), (1, 2)))
    pair_update_mask = touch_ends((jax.random.randint(part_keys[3], (CROP_LENGTH, CROP_LENGTH), 0, 8) < 7).astype(jnp.int32), jax.random.fold_in(part_keys[3], 1), 0, 1)
    pair_output_gradient = gaussian(part_keys[4], (CROP_LENGTH, CROP_LENGTH, CZ), 1.0, 6.0, ((0, 8), (1, 2)))
    layer_scale_factor = jnp.clip(1.0 + 0.15 * jax.random.normal(splits[5], (FEATURE_COUNT,), jnp.float32), 0.25, 1.75)
    first_projector = gaussian(splits[6], (FEATURE_COUNT, PROJECTOR_WIDTH), FEATURE_COUNT ** -0.5, 0.375)
    second_projector = gaussian(splits[7], (FEATURE_COUNT, PROJECTOR_WIDTH), FEATURE_COUNT ** -0.5, 0.375)
    output_weight = gaussian(splits[8], (OUTER, CZ), 16 ** -0.5, 1.5)
    pair_norm_gain = jnp.clip(1.0 + 0.15 * jax.random.normal(splits[9], (CZ,), jnp.float32), 0.25, 1.75)
    hidden_weight = gaussian(splits[10], (CZ, HID), CZ ** -0.5, 0.5)
    back_weight = gaussian(splits[11], (HID, CZ), HID ** -0.5, 0.25)
    return dict(alignment_activations=alignment_activations, alignment_mask=alignment_mask, pair_activation_input=pair_activation_input, pair_update_mask=pair_update_mask, pair_output_gradient=pair_output_gradient, layer_scale_factor=layer_scale_factor, first_projector=first_projector, second_projector=second_projector, output_weight=output_weight, pair_norm_gain=pair_norm_gain, hidden_weight=hidden_weight, back_weight=back_weight)


epsilon = 1e-05
highest = lax.Precision.HIGHEST

def norm_pieces(entries_drawn):
    center = entries_drawn - lax.optimization_barrier(jnp.mean(entries_drawn, axis=-1, keepdims=True))
    inv_std = lax.rsqrt(lax.optimization_barrier(jnp.mean(center * center, axis=-1, keepdims=True)) + epsilon)
    return (center * inv_std, inv_std)

def standardize_adjoint(grad_scaled, scaled, inv_std):
    mean_grad = lax.optimization_barrier(jnp.mean(grad_scaled, axis=-1, keepdims=True))
    mean_cross = lax.optimization_barrier(jnp.mean(grad_scaled * scaled, axis=-1, keepdims=True))
    return inv_std * (grad_scaled - mean_grad - scaled * mean_cross)

def silu_pieces(pre_act):
    sigma = jax.nn.sigmoid(pre_act)
    return (pre_act * sigma, sigma * (1.0 + pre_act * (1.0 - sigma)))

def return_journey(entries_drawn):
    return lax.optimization_barrier(entries_drawn.astype(jnp.bfloat16)).astype(jnp.float32)

def reference(alignment_activations, alignment_mask, pair_activation_input, pair_update_mask, pair_output_gradient, layer_scale_factor, first_projector, second_projector, output_weight, pair_norm_gain, hidden_weight, back_weight):
    standardized_features, reciprocal_spread = norm_pieces(alignment_activations.astype(jnp.float32))
    normalized_broad = return_journey(standardized_features * layer_scale_factor)
    mask_unconverted = alignment_mask.astype(jnp.float32)
    mask_floating = mask_unconverted[:, :, None]
    left_wide = return_journey(jnp.einsum('src,ck->srk', normalized_broad, first_projector.astype(jnp.float32)) * mask_floating)
    right_wide = return_journey(jnp.einsum('src,ck->srk', normalized_broad, second_projector.astype(jnp.float32)) * mask_floating)
    out_wide = output_weight.astype(jnp.float32)
    starts = jnp.arange(N_COL, dtype=jnp.int32) * RES_DEV

    def row_block(acc_state, start_row):
        grad_right, grad_out, grad_hid, grad_bk = acc_state
        left_rows = lax.dynamic_slice_in_dim(left_wide, start_row, RES_DEV, 1)
        mask_rows = lax.dynamic_slice_in_dim(mask_unconverted, start_row, RES_DEV, 1)
        act_rows = lax.dynamic_slice_in_dim(pair_activation_input, start_row, RES_DEV, 0).astype(jnp.float32)
        grad_rows = lax.dynamic_slice_in_dim(pair_output_gradient, start_row, RES_DEV, 0)
        pmask_rows = lax.dynamic_slice_in_dim(pair_update_mask, start_row, RES_DEV, 0)
        outer_sum = jnp.einsum('sic,sjd->ijcd', left_rows, right_wide).reshape(RES_DEV * CROP_LENGTH, OUTER)
        pair_count = jnp.einsum('si,sj->ij', mask_rows, mask_unconverted).reshape(RES_DEV * CROP_LENGTH, 1)
        projected = jnp.dot(outer_sum, out_wide, precision=highest)
        mid_act = act_rows.reshape(RES_DEV * CROP_LENGTH, CZ) + projected / pair_count
        pair_scaled, pair_inv = norm_pieces(mid_act)
        pair_normed = (pair_scaled * pair_norm_gain).astype(jnp.bfloat16)
        pre_act = jnp.dot(pair_normed, hidden_weight, preferred_element_type=jnp.float32)
        act_value, act_slope = silu_pieces(pre_act)
        hidden = act_value.astype(jnp.bfloat16)
        masked_grad = (grad_rows * pmask_rows.astype(jnp.bfloat16)[:, :, None]).reshape(RES_DEV * CROP_LENGTH, CZ)
        grad_bk = grad_bk + jnp.dot(hidden.T, masked_grad, preferred_element_type=jnp.float32)
        back_prod = jnp.dot(masked_grad, back_weight.T, preferred_element_type=jnp.float32)
        grad_hidden = (back_prod * act_slope).astype(jnp.bfloat16)
        grad_hid = grad_hid + jnp.dot(pair_normed.T, grad_hidden, preferred_element_type=jnp.float32)
        grad_scaled = jnp.dot(grad_hidden, hidden_weight.T, preferred_element_type=jnp.float32) * pair_norm_gain
        grad_mid = grad_rows.reshape(RES_DEV * CROP_LENGTH, CZ).astype(jnp.float32) + standardize_adjoint(grad_scaled, pair_scaled, pair_inv)
        grad_opm = (grad_mid / pair_count).astype(jnp.bfloat16)
        grad_out = grad_out + jnp.dot(outer_sum.T, grad_opm.astype(jnp.float32), precision=highest)
        grad_outer = return_journey(jnp.dot(grad_opm, output_weight.T, preferred_element_type=jnp.float32)).reshape(RES_DEV, CROP_LENGTH, PROJECTOR_WIDTH, PROJECTOR_WIDTH)
        grad_left_rows = jnp.einsum('ijcd,sjd->sic', grad_outer, right_wide)
        grad_right = grad_right + jnp.einsum('ijcd,sic->sjd', grad_outer, left_rows)
        pair_rows = grad_mid.astype(jnp.bfloat16).reshape(RES_DEV, CROP_LENGTH, CZ)
        return ((grad_right, grad_out, grad_hid, grad_bk), (pair_rows, grad_left_rows))
    init_state = (jnp.zeros((ALIGNED_COUNT, CROP_LENGTH, PROJECTOR_WIDTH), jnp.float32), jnp.zeros((OUTER, CZ), jnp.float32), jnp.zeros((CZ, HID), jnp.float32), jnp.zeros((HID, CZ), jnp.float32))
    final_state, (pair_blocks, left_blocks) = lax.scan(row_block, init_state, starts)
    grad_right_acc, result_matrix_derivative, middle_matrix_derivative, final_matrix_derivative = final_state
    couple_features_derivative = pair_blocks.reshape(CROP_LENGTH, CROP_LENGTH, CZ)
    grad_left_acc = jnp.transpose(left_blocks, (1, 0, 2, 3)).reshape(ALIGNED_COUNT, CROP_LENGTH, PROJECTOR_WIDTH)
    grad_left = return_journey(grad_left_acc * mask_floating)
    grad_right = return_journey(grad_right_acc * mask_floating)
    first_projector_derivative = jnp.einsum('src,srk->ck', normalized_broad, grad_left)
    second_projector_derivative = jnp.einsum('src,srk->ck', normalized_broad, grad_right)
    standardized_derivative = jnp.einsum('srk,ck->src', grad_left, first_projector.astype(jnp.float32))
    standardized_derivative = standardized_derivative + jnp.einsum('srk,ck->src', grad_right, second_projector.astype(jnp.float32))
    features_derivative = standardize_adjoint(standardized_derivative * layer_scale_factor, standardized_features, reciprocal_spread).astype(jnp.bfloat16)
    return (features_derivative, couple_features_derivative, first_projector_derivative, second_projector_derivative, result_matrix_derivative, middle_matrix_derivative, final_matrix_derivative)
```

```python
import jax
import jax.numpy as jnp
from jax import lax
from jax.sharding import PartitionSpec as P

epsilon = 1e-05
highest = lax.Precision.HIGHEST


def norm_pieces(entries_drawn):
    center = entries_drawn - jnp.mean(entries_drawn, axis=-1, keepdims=True)
    inv_std = lax.rsqrt(jnp.mean(center * center, axis=-1, keepdims=True) + epsilon)
    return (center * inv_std, inv_std)


def standardize_adjoint(grad_scaled, scaled, inv_std):
    mean_grad = jnp.mean(grad_scaled, axis=-1, keepdims=True)
    mean_cross = jnp.mean(grad_scaled * scaled, axis=-1, keepdims=True)
    return inv_std * (grad_scaled - mean_grad - scaled * mean_cross)


def silu_pieces(pre_act):
    sigma = jax.nn.sigmoid(pre_act)
    return (pre_act * sigma, sigma * (1.0 + pre_act * (1.0 - sigma)))


def split_plan(
    alignment_activations,
    alignment_mask,
    pair_activation_input,
    pair_update_mask,
    pair_output_gradient,
    layer_scale_factor,
    first_projector,
    second_projector,
    output_weight,
    pair_norm_gain,
    hidden_weight,
    back_weight,
):
    sequence_row_block, residue_row_block, channel_total = alignment_activations.shape
    proj_width = first_projector.shape[1]
    outer_width = proj_width * proj_width
    depth_count = lax.axis_size("depth")
    residues = residue_row_block * lax.axis_size("col")
    pair_cols = pair_activation_input.shape[1]
    pair_width = pair_activation_input.shape[2]
    col_block = min(64, pair_cols)
    block_count = pair_cols // col_block
    standardized_features, reciprocal_spread = norm_pieces(
        alignment_activations.astype(jnp.float32)
    )
    normalized_rows = (standardized_features * layer_scale_factor).astype(jnp.bfloat16)
    mask_floating = alignment_mask.astype(jnp.float32)
    left_proj = (
        jnp.dot(normalized_rows, first_projector, preferred_element_type=jnp.float32)
        * mask_floating[:, :, None]
    ).astype(jnp.bfloat16)
    right_proj = (
        jnp.dot(normalized_rows, second_projector, preferred_element_type=jnp.float32)
        * mask_floating[:, :, None]
    ).astype(jnp.bfloat16)
    right_flat = right_proj.reshape(sequence_row_block, residue_row_block * proj_width)
    mask_converted = alignment_mask.astype(jnp.bfloat16)
    seq_total = left_proj.shape[0]
    gathered, gathered_mask = (
        lax.all_gather(right_flat, "col", axis=1, tiled=True),
        lax.all_gather(mask_converted, "col", axis=1, tiled=True),
    )
    right_blocks = gathered.reshape(seq_total, depth_count, pair_cols, proj_width)
    mask_blocks = gathered_mask.reshape(seq_total, depth_count, pair_cols)
    block_depth = right_blocks.shape[1]
    out_wide = output_weight.astype(jnp.float32)

    def partial_outer(col_start):
        right_piece = lax.dynamic_slice_in_dim(right_blocks, col_start, col_block, 2)
        outer_part = jnp.einsum(
            "sic,sejd->iejcd", left_proj, right_piece, preferred_element_type=jnp.float32
        )
        return (
            outer_part.reshape(residue_row_block, block_depth, col_block, outer_width),
            right_piece,
        )

    def forward_step(step_index, loop_state):
        projected, pair_count = loop_state
        col_start = step_index * col_block
        outer_part, right_piece = partial_outer(col_start)
        mask_piece = lax.dynamic_slice_in_dim(mask_blocks, col_start, col_block, 2).astype(
            jnp.float32
        )
        count_part = jnp.einsum("si,sej->iej", mask_floating, mask_piece, precision=highest)
        outer_mine, count_mine = (
            lax.psum_scatter(
                outer_part.astype(jnp.bfloat16), "depth", scatter_dimension=1, tiled=True
            ).astype(jnp.float32),
            lax.psum_scatter(
                count_part.astype(jnp.bfloat16), "depth", scatter_dimension=1, tiled=True
            ).astype(jnp.float32),
        )
        proj_mine = jnp.dot(
            outer_mine.reshape(residue_row_block * col_block, outer_width),
            out_wide,
            precision=highest,
        )
        proj_mine = proj_mine.reshape(residue_row_block, col_block, pair_width)
        count_mine = count_mine.reshape(residue_row_block, col_block)
        projected = lax.dynamic_update_slice_in_dim(projected, proj_mine, col_start, 1)
        pair_count = lax.dynamic_update_slice_in_dim(pair_count, count_mine, col_start, 1)
        return (projected, pair_count)

    projected, pair_count = lax.fori_loop(
        0,
        block_count,
        forward_step,
        (
            jnp.zeros((residue_row_block, pair_cols, pair_width), jnp.float32),
            jnp.zeros((residue_row_block, pair_cols), jnp.float32),
        ),
    )
    count_column = pair_count.reshape(residue_row_block * pair_cols, 1)
    mid_act = (
        pair_activation_input.reshape(residue_row_block * pair_cols, pair_width).astype(jnp.float32)
        + projected.reshape(residue_row_block * pair_cols, pair_width) / count_column
    )
    pair_scaled, pair_inv = norm_pieces(mid_act)
    pair_normed = (pair_scaled * pair_norm_gain).astype(jnp.bfloat16)
    pre_act = jnp.dot(pair_normed, hidden_weight, preferred_element_type=jnp.float32)
    act_value, act_slope = silu_pieces(pre_act)
    hidden = act_value.astype(jnp.bfloat16)
    masked_grad = (
        pair_output_gradient * pair_update_mask.astype(jnp.bfloat16)[:, :, None]
    ).reshape(residue_row_block * pair_cols, pair_width)
    final_matrix_derivative = jnp.dot(hidden.T, masked_grad, preferred_element_type=jnp.float32)
    back_prod = jnp.dot(masked_grad, back_weight.T, preferred_element_type=jnp.float32)
    grad_hidden = (back_prod * act_slope).astype(jnp.bfloat16)
    middle_matrix_derivative = jnp.dot(
        pair_normed.T, grad_hidden, preferred_element_type=jnp.float32
    )
    grad_scaled = (
        jnp.dot(grad_hidden, hidden_weight.T, preferred_element_type=jnp.float32) * pair_norm_gain
    )
    grad_mid = pair_output_gradient.reshape(residue_row_block * pair_cols, pair_width).astype(
        jnp.float32
    ) + standardize_adjoint(grad_scaled, pair_scaled, pair_inv)
    couple_features_derivative = grad_mid.astype(jnp.bfloat16).reshape(
        residue_row_block, pair_cols, pair_width
    )
    grad_opm = (
        (grad_mid / count_column)
        .astype(jnp.bfloat16)
        .reshape(residue_row_block, pair_cols, pair_width)
    )
    full_opm = lax.all_gather(grad_opm, "depth", axis=1, tiled=True).reshape(
        residue_row_block, depth_count, pair_cols, pair_width
    )

    def backward_step(step_index, loop_state):
        grad_left_acc, grad_out, right_term = loop_state
        col_start = step_index * col_block
        outer_part, right_piece = partial_outer(col_start)
        opm_piece = lax.dynamic_slice_in_dim(full_opm, col_start, col_block, 2).reshape(
            residue_row_block * block_depth * col_block, pair_width
        )
        grad_out = grad_out + jnp.dot(
            outer_part.reshape(residue_row_block * block_depth * col_block, outer_width).T,
            opm_piece.astype(jnp.float32),
            precision=highest,
        )
        grad_outer = jnp.dot(opm_piece, output_weight.T, preferred_element_type=jnp.float32).astype(
            jnp.bfloat16
        )
        grad_outer = grad_outer.reshape(
            residue_row_block, block_depth, col_block, proj_width, proj_width
        )
        grad_left_acc = grad_left_acc + jnp.einsum(
            "iejcd,sejd->sic", grad_outer, right_piece, preferred_element_type=jnp.float32
        )
        piece_term = jnp.einsum(
            "iejcd,sic->ejsd", grad_outer, left_proj, preferred_element_type=jnp.float32
        )
        piece_term = piece_term.reshape(block_depth, col_block, seq_total * proj_width)
        right_term = lax.dynamic_update_slice_in_dim(right_term, piece_term, col_start, 1)
        return (grad_left_acc, grad_out, right_term)

    grad_left_acc, result_matrix_derivative, right_term = lax.fori_loop(
        0,
        block_count,
        backward_step,
        (
            jnp.zeros((seq_total, residue_row_block, proj_width), jnp.float32),
            jnp.zeros((outer_width, pair_width), jnp.float32),
            jnp.zeros((block_depth, pair_cols, seq_total * proj_width), jnp.float32),
        ),
    )
    grad_right_sum = lax.psum_scatter(
        right_term.reshape(residues, seq_total * proj_width), "col", scatter_dimension=0, tiled=True
    )
    grad_right_acc = jnp.transpose(
        grad_right_sum.reshape(residue_row_block, seq_total, proj_width), (1, 0, 2)
    )
    grad_left = (grad_left_acc * mask_floating[:, :, None]).astype(jnp.bfloat16)
    grad_right = (grad_right_acc * mask_floating[:, :, None]).astype(jnp.bfloat16)
    normed_rows = normalized_rows.reshape(sequence_row_block * residue_row_block, channel_total)
    first_projector_derivative = jnp.dot(
        normed_rows.T,
        grad_left.reshape(sequence_row_block * residue_row_block, proj_width),
        preferred_element_type=jnp.float32,
    )
    second_projector_derivative = jnp.dot(
        normed_rows.T,
        grad_right.reshape(sequence_row_block * residue_row_block, proj_width),
        preferred_element_type=jnp.float32,
    )
    standardized_derivative = jnp.dot(
        grad_left, first_projector.T, preferred_element_type=jnp.float32
    ) + jnp.dot(grad_right, second_projector.T, preferred_element_type=jnp.float32)
    features_derivative = standardize_adjoint(
        standardized_derivative * layer_scale_factor, standardized_features, reciprocal_spread
    ).astype(jnp.bfloat16)
    weight_sums = lax.psum(
        (
            first_projector_derivative,
            second_projector_derivative,
            result_matrix_derivative,
            middle_matrix_derivative,
            final_matrix_derivative,
        ),
        ("depth", "col"),
    )
    return (
        features_derivative,
        couple_features_derivative,
        weight_sums[0],
        weight_sums[1],
        weight_sums[2],
        weight_sums[3],
        weight_sums[4],
    )


FEW_RESIDUES = 32


def swap_depth(block):
    return lax.ppermute(block, "depth", [(0, 1), (1, 0)])


def from_partners(block):
    count = lax.axis_size("col")
    return [block] + [
        lax.ppermute(block, "col", [(source, source ^ step) for source in range(count)])
        for step in range(1, count)
    ]


def in_order(blocks):
    me = lax.axis_index("col")
    step = 1
    while step < len(blocks):
        swap = (me & step) != 0
        blocks = [
            jnp.where(swap, blocks[place ^ step], blocks[place]) for place in range(len(blocks))
        ]
        step *= 2
    return jnp.stack(blocks)


def pairwise_sum(blocks):
    while len(blocks) > 1:
        blocks = [blocks[at] + blocks[at + 1] for at in range(0, len(blocks), 2)]
    return blocks[0]


def whole_plan(
    alignment_activations,
    alignment_mask,
    pair_activation_input,
    pair_update_mask,
    pair_output_gradient,
    layer_scale_factor,
    first_projector,
    second_projector,
    output_weight,
    pair_norm_gain,
    hidden_weight,
    back_weight,
):
    seq_rows, res_rows, channel_total = alignment_activations.shape
    proj_width = first_projector.shape[1]
    outer_width = proj_width * proj_width
    cols = lax.axis_size("col")
    depths = lax.axis_size("depth")
    residues = res_rows * cols
    pair_cols, pair_width = pair_activation_input.shape[1:]
    flat_pairs = res_rows * pair_cols
    proj_lanes = res_rows * proj_width
    me_col = lax.axis_index("col")
    me_depth = lax.axis_index("depth")

    standardized_features, reciprocal_spread = norm_pieces(
        alignment_activations.astype(jnp.float32)
    )
    normalized_rows = (standardized_features * layer_scale_factor).astype(jnp.bfloat16)
    mask_floating = alignment_mask.astype(jnp.float32)
    both = jnp.concatenate([first_projector, second_projector], axis=1)
    proj = (
        jnp.dot(normalized_rows, both, preferred_element_type=jnp.float32)
        * mask_floating[:, :, None]
    ).astype(jnp.bfloat16)
    left_mine = proj[:, :, :proj_width].reshape(seq_rows, proj_lanes)
    right_mine = proj[:, :, proj_width:].reshape(seq_rows, proj_lanes)
    masks = jnp.zeros((16, pair_width), jnp.bfloat16)
    masks = masks.at[:res_rows, :seq_rows].set(alignment_mask.T.astype(jnp.bfloat16))
    masks = masks.at[res_rows, :flat_pairs].set(
        pair_update_mask.reshape(flat_pairs).astype(jnp.bfloat16)
    )
    sent = jnp.concatenate(
        [
            left_mine,
            right_mine,
            pair_activation_input.reshape(flat_pairs, pair_width),
            pair_output_gradient.reshape(flat_pairs, pair_width),
            masks,
        ]
    )
    mine = in_order(from_partners(sent))
    other = swap_depth(mine)
    got = jnp.where(
        me_depth == 0, jnp.stack([mine, other]), jnp.stack([other, mine])
    )
    cuts = [0]
    for rows in (seq_rows, seq_rows, flat_pairs, flat_pairs, 16):
        cuts.append(cuts[-1] + rows)
    left, right, act, grad, masks = [got[:, :, a:b] for a, b in zip(cuts[:-1], cuts[1:])]
    seqs = depths * seq_rows
    left = jnp.transpose(left, (0, 2, 1, 3)).reshape(seqs, residues, proj_width)
    right = jnp.transpose(right, (0, 2, 1, 3)).reshape(seqs, residues, proj_width)
    act = act.reshape(-1, pair_width).astype(jnp.float32)
    grad = grad.reshape(-1, pair_width)
    seq_mask = masks[:, :, :res_rows, :seq_rows].reshape(depths, residues, seq_rows)
    seq_mask = jnp.transpose(seq_mask, (0, 2, 1)).reshape(seqs, residues)
    pair_mask = masks[:, :, res_rows, :flat_pairs].reshape(-1, 1)
    right_halves = right.reshape(seqs, depths, pair_cols, proj_width)
    outer = (
        jnp.einsum("sic,sejd->eijcd", left, right_halves, preferred_element_type=jnp.float32)
        .reshape(-1, outer_width)
        .astype(jnp.bfloat16)
    )
    counts = jnp.einsum(
        "si,sej->eij",
        seq_mask,
        seq_mask.reshape(seqs, depths, pair_cols),
        preferred_element_type=jnp.float32,
    ).reshape(-1, 1)
    mid_act = act + jnp.dot(outer, output_weight, preferred_element_type=jnp.float32) / counts
    pair_scaled, pair_inv = norm_pieces(mid_act)
    pair_normed = (pair_scaled * pair_norm_gain).astype(jnp.bfloat16)
    pre_act = jnp.dot(pair_normed, hidden_weight, preferred_element_type=jnp.float32)
    act_value, act_slope = silu_pieces(pre_act)
    hidden = act_value.astype(jnp.bfloat16)
    masked_grad = grad * pair_mask
    final_matrix_derivative = jnp.dot(hidden.T, masked_grad, preferred_element_type=jnp.float32)
    back_prod = jnp.dot(masked_grad, back_weight.T, preferred_element_type=jnp.float32)
    grad_hidden = (back_prod * act_slope).astype(jnp.bfloat16)
    middle_matrix_derivative = jnp.dot(
        pair_normed.T, grad_hidden, preferred_element_type=jnp.float32
    )
    grad_scaled = (
        jnp.dot(grad_hidden, hidden_weight.T, preferred_element_type=jnp.float32) * pair_norm_gain
    )
    grad_mid = grad.astype(jnp.float32) + standardize_adjoint(grad_scaled, pair_scaled, pair_inv)
    couple_features_derivative = lax.dynamic_slice_in_dim(
        grad_mid.astype(jnp.bfloat16), (me_depth * cols + me_col) * flat_pairs, flat_pairs
    ).reshape(res_rows, pair_cols, pair_width)
    grad_opm = (grad_mid / counts).astype(jnp.bfloat16)
    result_matrix_derivative = jnp.dot(outer.T, grad_opm, preferred_element_type=jnp.float32)
    opm = grad_opm.reshape(depths, residues, pair_cols, pair_width)
    left_here = lax.dynamic_slice_in_dim(left, me_depth * seq_rows, seq_rows)
    right_here = lax.dynamic_slice_in_dim(right, me_depth * seq_rows, seq_rows)
    opm_rows = lax.dynamic_slice_in_dim(opm, me_col * res_rows, res_rows, 1)
    opm_cols = lax.dynamic_slice_in_dim(
        jnp.transpose(opm, (1, 0, 2, 3)).reshape(residues, residues, pair_width),
        me_col * res_rows,
        res_rows,
        1,
    )

    def outer_gradient(piece):
        return (
            jnp.dot(piece, output_weight.T, preferred_element_type=jnp.float32)
            .astype(jnp.bfloat16)
            .reshape(piece.shape[:-1] + (proj_width, proj_width))
        )

    grad_left_acc = jnp.einsum(
        "eijcd,sejd->sic",
        outer_gradient(opm_rows),
        right_here.reshape(seq_rows, depths, pair_cols, proj_width),
        preferred_element_type=jnp.float32,
    )
    grad_right_acc = jnp.einsum(
        "ijcd,sic->sjd", outer_gradient(opm_cols), left_here, preferred_element_type=jnp.float32
    )
    grad_left = (grad_left_acc * mask_floating[:, :, None]).astype(jnp.bfloat16)
    grad_right = (grad_right_acc * mask_floating[:, :, None]).astype(jnp.bfloat16)
    grad_both = jnp.concatenate([grad_left, grad_right], axis=2)
    grad_flat = grad_both.reshape(seq_rows * res_rows, 2 * proj_width)
    normed_flat = normalized_rows.reshape(seq_rows * res_rows, channel_total)
    part = jnp.dot(grad_flat.T, normed_flat, preferred_element_type=jnp.float32)
    part = (part + swap_depth(part)).astype(jnp.bfloat16)
    total = pairwise_sum([block.astype(jnp.float32) for block in from_partners(part)])
    standardized_derivative = jnp.dot(
        grad_flat, both.T, preferred_element_type=jnp.float32
    ).reshape(seq_rows, res_rows, channel_total)
    features_derivative = standardize_adjoint(
        standardized_derivative * layer_scale_factor, standardized_features, reciprocal_spread
    ).astype(jnp.bfloat16)
    return (
        features_derivative,
        couple_features_derivative,
        total[:proj_width].T,
        total[proj_width:].T,
        result_matrix_derivative,
        middle_matrix_derivative,
        final_matrix_derivative,
    )


def on_device(alignment_activations, *others):
    residues = alignment_activations.shape[1] * lax.axis_size("col")
    plan = whole_plan if residues <= FEW_RESIDUES else split_plan
    return plan(alignment_activations, *others)


def solution(mesh):
    in_specs = (
        P(("group", "depth"), "col", None),
        P(("group", "depth"), "col"),
        P(("group", "col"), "depth", None),
        P(("group", "col"), "depth"),
        P(("group", "col"), "depth", None),
        P(),
        P(),
        P(),
        P(),
        P(),
        P(),
        P(),
    )
    out_specs = (
        P(("group", "depth"), "col", None),
        P(("group", "col"), "depth", None),
        P("group", None),
        P("group", None),
        P("group", None),
        P("group", None),
        P("group", None),
    )
    return jax.shard_map(
        on_device, mesh=mesh, in_specs=in_specs, out_specs=out_specs, check_vma=False
    )
```

```python
import functools

import jax
import jax.numpy as jnp
from jax import lax
from jax.experimental import pallas as pl
from jax.experimental.pallas import tpu as pltpu
from jax.sharding import PartitionSpec as P

epsilon = 1e-05
highest = lax.Precision.HIGHEST


def norm_pieces(entries_drawn):
    center = entries_drawn - jnp.mean(entries_drawn, axis=-1, keepdims=True)
    inv_std = lax.rsqrt(jnp.mean(center * center, axis=-1, keepdims=True) + epsilon)
    return (center * inv_std, inv_std)


def standardize_adjoint(grad_scaled, scaled, inv_std):
    mean_grad = jnp.mean(grad_scaled, axis=-1, keepdims=True)
    mean_cross = jnp.mean(grad_scaled * scaled, axis=-1, keepdims=True)
    return inv_std * (grad_scaled - mean_grad - scaled * mean_cross)


def silu_pieces(pre_act):
    sigma = jax.nn.sigmoid(pre_act)
    return (pre_act * sigma, sigma * (1.0 + pre_act * (1.0 - sigma)))


def split_plan(
    alignment_activations,
    alignment_mask,
    pair_activation_input,
    pair_update_mask,
    pair_output_gradient,
    layer_scale_factor,
    first_projector,
    second_projector,
    output_weight,
    pair_norm_gain,
    hidden_weight,
    back_weight,
):
    sequence_row_block, residue_row_block, channel_total = alignment_activations.shape
    proj_width = first_projector.shape[1]
    outer_width = proj_width * proj_width
    depth_count = lax.axis_size("depth")
    residues = residue_row_block * lax.axis_size("col")
    pair_cols = pair_activation_input.shape[1]
    pair_width = pair_activation_input.shape[2]
    col_block = min(64, pair_cols)
    block_count = pair_cols // col_block
    standardized_features, reciprocal_spread = norm_pieces(
        alignment_activations.astype(jnp.float32)
    )
    normalized_rows = (standardized_features * layer_scale_factor).astype(jnp.bfloat16)
    mask_floating = alignment_mask.astype(jnp.float32)
    left_proj = (
        jnp.dot(normalized_rows, first_projector, preferred_element_type=jnp.float32)
        * mask_floating[:, :, None]
    ).astype(jnp.bfloat16)
    right_proj = (
        jnp.dot(normalized_rows, second_projector, preferred_element_type=jnp.float32)
        * mask_floating[:, :, None]
    ).astype(jnp.bfloat16)
    right_flat = right_proj.reshape(sequence_row_block, residue_row_block * proj_width)
    mask_converted = alignment_mask.astype(jnp.bfloat16)
    seq_total = left_proj.shape[0]
    gathered, gathered_mask = (
        lax.all_gather(right_flat, "col", axis=1, tiled=True),
        lax.all_gather(mask_converted, "col", axis=1, tiled=True),
    )
    right_blocks = gathered.reshape(seq_total, depth_count, pair_cols, proj_width)
    mask_blocks = gathered_mask.reshape(seq_total, depth_count, pair_cols)
    block_depth = right_blocks.shape[1]
    out_wide = output_weight.astype(jnp.float32)

    def partial_outer(col_start):
        right_piece = lax.dynamic_slice_in_dim(right_blocks, col_start, col_block, 2)
        outer_part = jnp.einsum(
            "sic,sejd->iejcd", left_proj, right_piece, preferred_element_type=jnp.float32
        )
        return (
            outer_part.reshape(residue_row_block, block_depth, col_block, outer_width),
            right_piece,
        )

    def forward_step(step_index, loop_state):
        projected, pair_count = loop_state
        col_start = step_index * col_block
        outer_part, right_piece = partial_outer(col_start)
        mask_piece = lax.dynamic_slice_in_dim(mask_blocks, col_start, col_block, 2).astype(
            jnp.float32
        )
        count_part = jnp.einsum("si,sej->iej", mask_floating, mask_piece, precision=highest)
        outer_mine, count_mine = (
            lax.psum_scatter(
                outer_part.astype(jnp.bfloat16), "depth", scatter_dimension=1, tiled=True
            ).astype(jnp.float32),
            lax.psum_scatter(
                count_part.astype(jnp.bfloat16), "depth", scatter_dimension=1, tiled=True
            ).astype(jnp.float32),
        )
        proj_mine = jnp.dot(
            outer_mine.reshape(residue_row_block * col_block, outer_width),
            out_wide,
            precision=highest,
        )
        proj_mine = proj_mine.reshape(residue_row_block, col_block, pair_width)
        count_mine = count_mine.reshape(residue_row_block, col_block)
        projected = lax.dynamic_update_slice_in_dim(projected, proj_mine, col_start, 1)
        pair_count = lax.dynamic_update_slice_in_dim(pair_count, count_mine, col_start, 1)
        return (projected, pair_count)

    projected, pair_count = lax.fori_loop(
        0,
        block_count,
        forward_step,
        (
            jnp.zeros((residue_row_block, pair_cols, pair_width), jnp.float32),
            jnp.zeros((residue_row_block, pair_cols), jnp.float32),
        ),
    )
    count_column = pair_count.reshape(residue_row_block * pair_cols, 1)
    mid_act = (
        pair_activation_input.reshape(residue_row_block * pair_cols, pair_width).astype(jnp.float32)
        + projected.reshape(residue_row_block * pair_cols, pair_width) / count_column
    )
    pair_scaled, pair_inv = norm_pieces(mid_act)
    pair_normed = (pair_scaled * pair_norm_gain).astype(jnp.bfloat16)
    pre_act = jnp.dot(pair_normed, hidden_weight, preferred_element_type=jnp.float32)
    act_value, act_slope = silu_pieces(pre_act)
    hidden = act_value.astype(jnp.bfloat16)
    masked_grad = (
        pair_output_gradient * pair_update_mask.astype(jnp.bfloat16)[:, :, None]
    ).reshape(residue_row_block * pair_cols, pair_width)
    final_matrix_derivative = jnp.dot(hidden.T, masked_grad, preferred_element_type=jnp.float32)
    back_prod = jnp.dot(masked_grad, back_weight.T, preferred_element_type=jnp.float32)
    grad_hidden = (back_prod * act_slope).astype(jnp.bfloat16)
    middle_matrix_derivative = jnp.dot(
        pair_normed.T, grad_hidden, preferred_element_type=jnp.float32
    )
    grad_scaled = (
        jnp.dot(grad_hidden, hidden_weight.T, preferred_element_type=jnp.float32) * pair_norm_gain
    )
    grad_mid = pair_output_gradient.reshape(residue_row_block * pair_cols, pair_width).astype(
        jnp.float32
    ) + standardize_adjoint(grad_scaled, pair_scaled, pair_inv)
    couple_features_derivative = grad_mid.astype(jnp.bfloat16).reshape(
        residue_row_block, pair_cols, pair_width
    )
    grad_opm = (
        (grad_mid / count_column)
        .astype(jnp.bfloat16)
        .reshape(residue_row_block, pair_cols, pair_width)
    )
    full_opm = lax.all_gather(grad_opm, "depth", axis=1, tiled=True).reshape(
        residue_row_block, depth_count, pair_cols, pair_width
    )

    def backward_step(step_index, loop_state):
        grad_left_acc, grad_out, right_term = loop_state
        col_start = step_index * col_block
        outer_part, right_piece = partial_outer(col_start)
        opm_piece = lax.dynamic_slice_in_dim(full_opm, col_start, col_block, 2).reshape(
            residue_row_block * block_depth * col_block, pair_width
        )
        grad_out = grad_out + jnp.dot(
            outer_part.reshape(residue_row_block * block_depth * col_block, outer_width).T,
            opm_piece.astype(jnp.float32),
            precision=highest,
        )
        grad_outer = jnp.dot(opm_piece, output_weight.T, preferred_element_type=jnp.float32).astype(
            jnp.bfloat16
        )
        grad_outer = grad_outer.reshape(
            residue_row_block, block_depth, col_block, proj_width, proj_width
        )
        grad_left_acc = grad_left_acc + jnp.einsum(
            "iejcd,sejd->sic", grad_outer, right_piece, preferred_element_type=jnp.float32
        )
        piece_term = jnp.einsum(
            "iejcd,sic->ejsd", grad_outer, left_proj, preferred_element_type=jnp.float32
        )
        piece_term = piece_term.reshape(block_depth, col_block, seq_total * proj_width)
        right_term = lax.dynamic_update_slice_in_dim(right_term, piece_term, col_start, 1)
        return (grad_left_acc, grad_out, right_term)

    grad_left_acc, result_matrix_derivative, right_term = lax.fori_loop(
        0,
        block_count,
        backward_step,
        (
            jnp.zeros((seq_total, residue_row_block, proj_width), jnp.float32),
            jnp.zeros((outer_width, pair_width), jnp.float32),
            jnp.zeros((block_depth, pair_cols, seq_total * proj_width), jnp.float32),
        ),
    )
    grad_right_sum = lax.psum_scatter(
        right_term.reshape(residues, seq_total * proj_width), "col", scatter_dimension=0, tiled=True
    )
    grad_right_acc = jnp.transpose(
        grad_right_sum.reshape(residue_row_block, seq_total, proj_width), (1, 0, 2)
    )
    grad_left = (grad_left_acc * mask_floating[:, :, None]).astype(jnp.bfloat16)
    grad_right = (grad_right_acc * mask_floating[:, :, None]).astype(jnp.bfloat16)
    normed_rows = normalized_rows.reshape(sequence_row_block * residue_row_block, channel_total)
    first_projector_derivative = jnp.dot(
        normed_rows.T,
        grad_left.reshape(sequence_row_block * residue_row_block, proj_width),
        preferred_element_type=jnp.float32,
    )
    second_projector_derivative = jnp.dot(
        normed_rows.T,
        grad_right.reshape(sequence_row_block * residue_row_block, proj_width),
        preferred_element_type=jnp.float32,
    )
    standardized_derivative = jnp.dot(
        grad_left, first_projector.T, preferred_element_type=jnp.float32
    ) + jnp.dot(grad_right, second_projector.T, preferred_element_type=jnp.float32)
    features_derivative = standardize_adjoint(
        standardized_derivative * layer_scale_factor, standardized_features, reciprocal_spread
    ).astype(jnp.bfloat16)
    weight_sums = lax.psum(
        (
            first_projector_derivative,
            second_projector_derivative,
            result_matrix_derivative,
            middle_matrix_derivative,
            final_matrix_derivative,
        ),
        ("depth", "col"),
    )
    return (
        features_derivative,
        couple_features_derivative,
        weight_sums[0],
        weight_sums[1],
        weight_sums[2],
        weight_sums[3],
        weight_sums[4],
    )


FEW_RESIDUES = 32
MASK_ROWS = 16


def butterfly(blocks, group):
    lane_group = lax.broadcasted_iota(jnp.int32, blocks[0].shape, 1) // group
    width = 4 * group
    for bit in (2, 1):
        low = (lane_group & bit) == 0
        swapped = list(blocks)
        for at in range(4):
            if at & bit:
                continue
            here, there = blocks[at], blocks[at | bit]
            moving = jnp.where(low, there, here)
            if bit == 2:
                moved = pltpu.roll(moving, 2 * group, 1)
            else:
                moved = jnp.where(
                    low, pltpu.roll(moving, width - group, 1), pltpu.roll(moving, group, 1)
                )
            swapped[at] = jnp.where(low, here, moved)
            swapped[at | bit] = jnp.where(low, moved, there)
        blocks = swapped
    return blocks


def pre_kernel(
    ids_ref,
    x_ref,
    mask_ref,
    act_ref,
    pmask_ref,
    grad_ref,
    scale_ref,
    proj_ref,
    sent_ref,
    normed_ref,
    scaled_ref,
    inv_ref,
    lanes_ref,
    wide_ref,
    tile_ref,
    turned_ref,
):
    seqs, res = mask_ref.shape
    lanes = proj_ref.shape[1] // 2
    group = lanes // res
    pairs = act_ref.shape[0]
    scaled, inv = norm_pieces(x_ref[...].astype(jnp.float32))
    scaled_ref[...] = scaled
    inv_ref[...] = inv
    normed = (scaled * scale_ref[...]).astype(jnp.bfloat16)
    normed_ref[...] = normed
    wide = jnp.dot(normed, proj_ref[...], preferred_element_type=jnp.float32)
    for at in range(2):
        wide_ref[at] = wide[:, at * lanes : (at + 1) * lanes]
    lane_group = lax.broadcasted_iota(jnp.int32, (seqs, lanes), 1) // group
    mask = mask_ref[...].astype(jnp.float32)
    both = [jnp.zeros((seqs, lanes), jnp.float32) for _ in range(2)]
    mask_lanes = jnp.zeros((seqs, lanes), jnp.float32)
    for r in range(res):
        mine = lane_group == r
        both = [
            jnp.where(mine, wide_ref[at, pl.ds(r, seqs, stride=res), :], both[at])
            for at in range(2)
        ]
        mask_lanes = jnp.where(mine, mask[:, r : r + 1], mask_lanes)
    lanes_ref[...] = mask_lanes
    left = (both[0] * mask_lanes).astype(jnp.bfloat16)
    right = (both[1] * mask_lanes).astype(jnp.bfloat16)
    spread = (
        lax.broadcasted_iota(jnp.int32, (seqs, lanes), 1)
        == lax.broadcasted_iota(jnp.int32, (seqs, lanes), 0) + ids_ref[0] * seqs
    ).astype(jnp.float32)
    turned_ref[...] = lax.dot_general(
        mask_lanes, spread, (((0,), (0,)), ((), ())), preferred_element_type=jnp.float32
    )
    tile_ref[...] = jnp.zeros(tile_ref.shape, jnp.float32)
    tile_ref[0:res, :] = turned_ref[pl.ds(0, res, stride=group), :]
    tile_ref[res : 2 * res, 0 : pmask_ref.shape[1]] = pmask_ref[...].astype(jnp.float32)
    tile = tile_ref[...].astype(jnp.bfloat16)
    act = act_ref[...]
    grad = grad_ref[...]
    for at in range(sent_ref.shape[0]):
        sent_ref[at, 0:seqs, :] = left
        sent_ref[at, seqs : 2 * seqs, :] = right
        sent_ref[at, 2 * seqs : 2 * seqs + pairs, :] = act
        sent_ref[at, 2 * seqs + pairs : 2 * seqs + 2 * pairs, :] = grad
        sent_ref[at, 2 * seqs + 2 * pairs :, :] = tile


def main_kernel(
    sizes,
    ids_ref,
    mine_ref,
    other_ref,
    wout_ref,
    wturn_ref,
    gain_ref,
    hid_ref,
    back_ref,
    normed_ref,
    scaled_ref,
    inv_ref,
    lanes_ref,
    scale_ref,
    proj_ref,
    couple_ref,
    part_ref,
    dout_ref,
    dhid_ref,
    dback_ref,
    feat_ref,
    got_ref,
    leftn_ref,
    rightt_ref,
    leftt_ref,
    turn_ref,
    outer_ref,
    maskt_ref,
    cnt_ref,
    cntl_ref,
    pml_ref,
    pm_ref,
    proj_out_ref,
    pn_ref,
    gh_ref,
    hidden_ref,
    mg_ref,
    gmid_ref,
    gf_ref,
    grow_ref,
    gcol_ref,
    gor_ref,
    goc_ref,
    gs_ref,
):
    seqs, res, pair_cols, width = sizes
    depths, cols = got_ref.shape[0], got_ref.shape[1]
    residues = cols * res
    lanes = res * width
    per = res * pair_cols
    half = residues * pair_cols
    pairs = depths * half
    all_seqs = depths * seqs
    me_depth = ids_ref[0]
    me_col = ids_ref[1]
    f32, bf16 = jnp.float32, jnp.bfloat16

    got_ref[me_depth] = mine_ref[...]
    got_ref[1 - me_depth] = other_ref[...]

    for e in range(depths):
        for k in range(cols):
            leftn_ref[e * seqs : (e + 1) * seqs, k * lanes : (k + 1) * lanes] = got_ref[
                e, k, 0:seqs, :
            ]
    for at, out in ((0, leftt_ref), (1, rightt_ref)):
        for k in range(cols):
            block = jnp.concatenate(
                [got_ref[e, k, at * seqs : (at + 1) * seqs, :] for e in range(depths)], axis=0
            ).astype(f32)
            turn_ref[k * lanes : (k + 1) * lanes, :] = block.T
        for d in range(width):
            out[d * residues : (d + 1) * residues, :] = turn_ref[
                pl.ds(d, residues, stride=width), :
            ].astype(bf16)

    base = 2 * seqs + 2 * per
    pair_lane = lax.broadcasted_iota(jnp.int32, (pair_cols, lanes), 1)
    pair_row = lax.broadcasted_iota(jnp.int32, (pair_cols, lanes), 0)
    for k in range(cols):
        tiles = [got_ref[e, k, base : base + MASK_ROWS, :].astype(f32) for e in range(depths)]
        maskt_ref[k * res : (k + 1) * res, :] = tiles[0][0:res] + tiles[1][0:res]
        for e in range(depths):
            for r in range(res):
                row = tiles[e][res + r : res + r + 1, :]
                first = e * half + (k * res + r) * pair_cols
                pml_ref[first : first + pair_cols, :] = jnp.where(
                    pair_lane == pair_row, row, 0.0
                ).astype(bf16)
    maskt = maskt_ref[...]
    for e in range(depths):
        cols_mask = maskt[e * pair_cols : (e + 1) * pair_cols, :]
        for i in range(residues):
            first = e * half + i * pair_cols
            cntl_ref[first : first + pair_cols, :] = (maskt[i : i + 1, :] * cols_mask).astype(bf16)
    ones = jnp.ones((lanes, lanes), bf16)
    cnt_ref[...] = jnp.dot(cntl_ref[...], ones, preferred_element_type=f32)
    pm_ref[...] = jnp.dot(pml_ref[...], ones, preferred_element_type=f32).astype(bf16)

    for dh in range(width // 4):
        prod = jnp.dot(
            rightt_ref[dh * 4 * residues : (dh + 1) * 4 * residues, :],
            leftn_ref[...],
            preferred_element_type=f32,
        )
        for k in range(cols):
            piece = prod[:, k * lanes : (k + 1) * lanes]
            turned = butterfly(
                [piece[a * residues : (a + 1) * residues] for a in range(4)], width
            )
            for il in range(res):
                block = turned[il].astype(bf16)
                for e in range(depths):
                    first = e * half + (k * res + il) * pair_cols
                    outer_ref[first : first + pair_cols, dh * lanes : (dh + 1) * lanes] = block[
                        e * pair_cols : (e + 1) * pair_cols
                    ]
    proj_out_ref[...] = jnp.dot(outer_ref[...], wturn_ref[...], preferred_element_type=f32)

    gain = gain_ref[...]
    chunk = 2 * per
    for at in range(pairs // chunk):
        rows = slice(at * chunk, (at + 1) * chunk)
        e, k = divmod(2 * at, cols)
        first = 2 * seqs
        act = jnp.concatenate(
            [got_ref[e, k + b, first : first + per, :] for b in range(2)], axis=0
        ).astype(f32)
        grad = jnp.concatenate(
            [got_ref[e, k + b, first + per : first + 2 * per, :] for b in range(2)], axis=0
        )
        count = cnt_ref[rows, :]
        mid = act + proj_out_ref[rows, :] / count
        scaled, inv = norm_pieces(mid)
        normed = (scaled * gain).astype(bf16)
        pn_ref[rows, :] = normed
        pre = jnp.dot(normed, hid_ref[...], preferred_element_type=f32)
        value, slope = silu_pieces(pre)
        hidden_ref[rows, :] = value.astype(bf16)
        masked = grad * pm_ref[rows, :]
        mg_ref[rows, :] = masked
        back = lax.dot_general(
            masked, back_ref[...], (((1,), (1,)), ((), ())), preferred_element_type=f32
        )
        ghid = (back * slope).astype(bf16)
        gh_ref[rows, :] = ghid
        gsc = (
            lax.dot_general(
                ghid, hid_ref[...], (((1,), (1,)), ((), ())), preferred_element_type=f32
            )
            * gain
        )
        gmid = grad.astype(f32) + standardize_adjoint(gsc, scaled, inv)
        gmid_ref[rows, :] = gmid
        gf_ref[rows, :] = (gmid / count).astype(bf16).astype(f32)
    start = pl.multiple_of(me_depth * half + me_col * per, per)
    couple_ref[...] = gmid_ref[pl.ds(start, per), :].astype(bf16)

    for il in range(res):
        for e in range(depths):
            first = pl.multiple_of(e * half + (me_col * res + il) * pair_cols, pair_cols)
            grow_ref[il * residues + e * pair_cols : il * residues + (e + 1) * pair_cols, :] = (
                gf_ref[pl.ds(first, pair_cols), :].astype(bf16)
            )
    my_half = (me_col * res) // pair_cols
    my_first = me_col * res - my_half * pair_cols
    for jl in range(res):
        gcol_ref[jl * residues : (jl + 1) * residues, :] = gf_ref[
            pl.ds(my_half * half + my_first + jl, residues, stride=pair_cols), :
        ].astype(bf16)
    for lhs, weight, out in ((grow_ref, wturn_ref, gor_ref), (gcol_ref, wout_ref, goc_ref)):
        for dh in range(width // 4):
            piece = lax.dot_general(
                lhs[...],
                weight[dh * lanes : (dh + 1) * lanes, :],
                (((1,), (1,)), ((), ())),
                preferred_element_type=f32,
            )
            turned = butterfly(
                [piece[a * residues : (a + 1) * residues] for a in range(4)], width
            )
            for dl in range(4):
                first = (dh * 4 + dl) * residues
                out[first : first + residues, :] = turned[dl].astype(bf16)
    sums = [
        lax.dot_general(lhs[...], rhs[...], (((0,), (0,)), ((), ())), preferred_element_type=f32)
        for lhs, rhs in ((rightt_ref, gor_ref), (leftt_ref, goc_ref))
    ]
    mask_lanes = lanes_ref[...]
    upper = me_depth == 0
    sums = [
        (jnp.where(upper, total[:seqs], total[seqs:]) * mask_lanes).astype(bf16).astype(f32)
        for total in sums
    ]
    lane_group = lax.broadcasted_iota(jnp.int32, (seqs, lanes), 1) // width
    for r in range(res):
        for at in range(2):
            gs_ref[at, pl.ds(r, seqs, stride=res), :] = jnp.where(
                lane_group == r, sums[at], 0.0
            )
    spread = jnp.concatenate([gs_ref[0], gs_ref[1]], axis=1).astype(bf16)
    cross = lax.dot_general(
        spread, normed_ref[...], (((0,), (0,)), ((), ())), preferred_element_type=f32
    )
    for at in range(2):
        total = cross[at * lanes : at * lanes + width]
        for r in range(1, res):
            total = total + cross[at * lanes + r * width : at * lanes + (r + 1) * width]
        part_ref[at * width : (at + 1) * width, :] = total
    back = lax.dot_general(
        spread, proj_ref[...], (((1,), (1,)), ((), ())), preferred_element_type=f32
    )
    feat_ref[...] = standardize_adjoint(
        back * scale_ref[...], scaled_ref[...], inv_ref[...]
    ).astype(bf16)

    opm = gf_ref[...].astype(bf16)
    turn_ref[...] = lax.dot_general(
        outer_ref[...], opm, (((0,), (0,)), ((), ())), preferred_element_type=f32
    )
    for c in range(width):
        dout_ref[c * width : (c + 1) * width, :] = turn_ref[pl.ds(c, width, stride=width), :]
    dhid_ref[...] = lax.dot_general(
        pn_ref[...], gh_ref[...], (((0,), (0,)), ((), ())), preferred_element_type=f32
    )
    dback_ref[...] = lax.dot_general(
        hidden_ref[...], mg_ref[...], (((0,), (0,)), ((), ())), preferred_element_type=f32
    )


def swap_depth(block):
    return lax.ppermute(block, "depth", [(0, 1), (1, 0)])


def pairwise_sum(blocks):
    while len(blocks) > 1:
        blocks = [blocks[at] + blocks[at + 1] for at in range(0, len(blocks), 2)]
    return blocks[0]


def whole_plan(
    alignment_activations,
    alignment_mask,
    pair_activation_input,
    pair_update_mask,
    pair_output_gradient,
    layer_scale_factor,
    first_projector,
    second_projector,
    output_weight,
    pair_norm_gain,
    hidden_weight,
    back_weight,
):
    seqs, res, channels = alignment_activations.shape
    width = first_projector.shape[1]
    outer_width = width * width
    cols = lax.axis_size("col")
    depths = lax.axis_size("depth")
    residues = res * cols
    pair_cols, pair_width = pair_activation_input.shape[1:]
    hid = hidden_weight.shape[1]
    per = res * pair_cols
    pairs = residues * residues
    lanes = res * width
    rows = 2 * seqs + 2 * per + MASK_ROWS
    f32, bf16 = jnp.float32, jnp.bfloat16
    ids = jnp.stack([lax.axis_index("depth"), lax.axis_index("col")]).astype(jnp.int32)
    smem = pl.BlockSpec(memory_space=pltpu.SMEM)
    vmem = pl.BlockSpec(memory_space=pltpu.VMEM)
    scale = layer_scale_factor.reshape(1, channels)
    proj = jnp.concatenate([first_projector] * res + [second_projector] * res, axis=1)
    wturn = jnp.transpose(output_weight.reshape(width, width, pair_width), (1, 0, 2)).reshape(
        outer_width, pair_width
    )
    shape = jax.ShapeDtypeStruct
    sent, normed, scaled, inv, mask_lanes = pl.pallas_call(
        pre_kernel,
        out_shape=(
            shape((cols, rows, pair_width), bf16),
            shape((seqs * res, channels), bf16),
            shape((seqs * res, channels), f32),
            shape((seqs * res, 1), f32),
            shape((seqs, lanes), f32),
        ),
        in_specs=[smem] + [vmem] * 7,
        out_specs=[vmem] * 5,
        scratch_shapes=[
            pltpu.VMEM((2, seqs * res, lanes), f32),
            pltpu.VMEM((MASK_ROWS, lanes), f32),
            pltpu.VMEM((lanes, lanes), f32),
        ],
        compiler_params=pltpu.CompilerParams(vmem_limit_bytes=40 * 2**20),
        name="project",
    )(
        ids,
        alignment_activations.reshape(seqs * res, channels),
        alignment_mask,
        pair_activation_input.reshape(per, pair_width),
        pair_update_mask,
        pair_output_gradient.reshape(per, pair_width),
        scale,
        proj,
    )
    mine = lax.all_to_all(sent, "col", 0, 0)
    other = swap_depth(mine)
    couple, part, dout, dhid, dback, feat = pl.pallas_call(
        functools.partial(main_kernel, (seqs, res, pair_cols, width)),
        out_shape=(
            shape((per, pair_width), bf16),
            shape((2 * width, channels), f32),
            shape((outer_width, pair_width), f32),
            shape((pair_width, hid), f32),
            shape((hid, pair_width), f32),
            shape((seqs * res, channels), bf16),
        ),
        in_specs=[smem] + [vmem] * 13,
        out_specs=[vmem] * 6,
        scratch_shapes=[
            pltpu.VMEM((depths, cols, rows, pair_width), bf16),
            pltpu.VMEM((depths * seqs, residues * width), bf16),
            pltpu.VMEM((residues * width, depths * seqs), bf16),
            pltpu.VMEM((residues * width, depths * seqs), bf16),
            pltpu.VMEM((residues * width, depths * seqs), f32),
            pltpu.VMEM((pairs, outer_width), bf16),
            pltpu.VMEM((residues, depths * seqs), f32),
            pltpu.VMEM((pairs, lanes), f32),
            pltpu.VMEM((pairs, lanes), bf16),
            pltpu.VMEM((pairs, lanes), bf16),
            pltpu.VMEM((pairs, lanes), bf16),
            pltpu.VMEM((pairs, pair_width), f32),
            pltpu.VMEM((pairs, pair_width), bf16),
            pltpu.VMEM((pairs, hid), bf16),
            pltpu.VMEM((pairs, hid), bf16),
            pltpu.VMEM((pairs, pair_width), bf16),
            pltpu.VMEM((pairs, pair_width), f32),
            pltpu.VMEM((pairs, pair_width), f32),
            pltpu.VMEM((res * residues, pair_width), bf16),
            pltpu.VMEM((res * residues, pair_width), bf16),
            pltpu.VMEM((residues * width, lanes), bf16),
            pltpu.VMEM((residues * width, lanes), bf16),
            pltpu.VMEM((2, seqs * res, lanes), f32),
        ],
        compiler_params=pltpu.CompilerParams(vmem_limit_bytes=40 * 2**20),
        name="pair_work",
    )(
        ids,
        mine,
        other,
        output_weight,
        wturn,
        pair_norm_gain.reshape(1, pair_width),
        hidden_weight,
        back_weight,
        normed,
        scaled,
        inv,
        mask_lanes,
        scale,
        proj,
    )
    part = part.reshape(depths * cols, -1, channels)
    pieces = lax.all_to_all(part, ("depth", "col"), 0, 0)
    summed = jnp.sum(pieces, axis=0, keepdims=True)
    total = lax.all_to_all(
        jnp.broadcast_to(summed, part.shape), ("depth", "col"), 0, 0
    ).reshape(2 * width, channels)
    return (
        feat.reshape(seqs, res, channels),
        couple.reshape(res, pair_cols, pair_width),
        total[:width].T,
        total[width:].T,
        dout,
        dhid,
        dback,
    )


def on_device(alignment_activations, *others):
    residues = alignment_activations.shape[1] * lax.axis_size("col")
    plan = whole_plan if residues <= FEW_RESIDUES else split_plan
    return plan(alignment_activations, *others)


def solution(mesh):
    in_specs = (
        P(("group", "depth"), "col", None),
        P(("group", "depth"), "col"),
        P(("group", "col"), "depth", None),
        P(("group", "col"), "depth"),
        P(("group", "col"), "depth", None),
        P(),
        P(),
        P(),
        P(),
        P(),
        P(),
        P(),
    )
    out_specs = (
        P(("group", "depth"), "col", None),
        P(("group", "col"), "depth", None),
        P("group", None),
        P("group", None),
        P("group", None),
        P("group", None),
        P("group", None),
    )
    return jax.shard_map(
        on_device, mesh=mesh, in_specs=in_specs, out_specs=out_specs, check_vma=False
    )
```

```python
import functools

import jax
import jax.numpy as jnp
from jax import lax
from jax.experimental import pallas as pl
from jax.experimental.pallas import tpu as pltpu
from jax.sharding import PartitionSpec as P

epsilon = 1e-05
highest = lax.Precision.HIGHEST


def norm_pieces(entries_drawn):
    center = entries_drawn - jnp.mean(entries_drawn, axis=-1, keepdims=True)
    inv_std = lax.rsqrt(jnp.mean(center * center, axis=-1, keepdims=True) + epsilon)
    return (center * inv_std, inv_std)


def standardize_adjoint(grad_scaled, scaled, inv_std):
    mean_grad = jnp.mean(grad_scaled, axis=-1, keepdims=True)
    mean_cross = jnp.mean(grad_scaled * scaled, axis=-1, keepdims=True)
    return inv_std * (grad_scaled - mean_grad - scaled * mean_cross)


def silu_pieces(pre_act):
    sigma = jax.nn.sigmoid(pre_act)
    return (pre_act * sigma, sigma * (1.0 + pre_act * (1.0 - sigma)))


def split_plan(
    alignment_activations,
    alignment_mask,
    pair_activation_input,
    pair_update_mask,
    pair_output_gradient,
    layer_scale_factor,
    first_projector,
    second_projector,
    output_weight,
    pair_norm_gain,
    hidden_weight,
    back_weight,
):
    sequence_row_block, residue_row_block, channel_total = alignment_activations.shape
    proj_width = first_projector.shape[1]
    outer_width = proj_width * proj_width
    depth_count = lax.axis_size("depth")
    residues = residue_row_block * lax.axis_size("col")
    pair_cols = pair_activation_input.shape[1]
    pair_width = pair_activation_input.shape[2]
    col_block = min(64, pair_cols)
    block_count = pair_cols // col_block
    standardized_features, reciprocal_spread = norm_pieces(
        alignment_activations.astype(jnp.float32)
    )
    normalized_rows = (standardized_features * layer_scale_factor).astype(jnp.bfloat16)
    mask_floating = alignment_mask.astype(jnp.float32)
    left_proj = (
        jnp.dot(normalized_rows, first_projector, preferred_element_type=jnp.float32)
        * mask_floating[:, :, None]
    ).astype(jnp.bfloat16)
    right_proj = (
        jnp.dot(normalized_rows, second_projector, preferred_element_type=jnp.float32)
        * mask_floating[:, :, None]
    ).astype(jnp.bfloat16)
    right_flat = right_proj.reshape(sequence_row_block, residue_row_block * proj_width)
    mask_converted = alignment_mask.astype(jnp.bfloat16)
    seq_total = left_proj.shape[0]
    gathered, gathered_mask = (
        lax.all_gather(right_flat, "col", axis=1, tiled=True),
        lax.all_gather(mask_converted, "col", axis=1, tiled=True),
    )
    right_blocks = gathered.reshape(seq_total, depth_count, pair_cols, proj_width)
    mask_blocks = gathered_mask.reshape(seq_total, depth_count, pair_cols)
    block_depth = right_blocks.shape[1]
    out_wide = output_weight.astype(jnp.float32)

    def partial_outer(col_start):
        right_piece = lax.dynamic_slice_in_dim(right_blocks, col_start, col_block, 2)
        outer_part = jnp.einsum(
            "sic,sejd->iejcd", left_proj, right_piece, preferred_element_type=jnp.float32
        )
        return (
            outer_part.reshape(residue_row_block, block_depth, col_block, outer_width),
            right_piece,
        )

    def forward_step(step_index, loop_state):
        projected, pair_count = loop_state
        col_start = step_index * col_block
        outer_part, right_piece = partial_outer(col_start)
        mask_piece = lax.dynamic_slice_in_dim(mask_blocks, col_start, col_block, 2).astype(
            jnp.float32
        )
        count_part = jnp.einsum("si,sej->iej", mask_floating, mask_piece, precision=highest)
        outer_mine, count_mine = (
            lax.psum_scatter(
                outer_part.astype(jnp.bfloat16), "depth", scatter_dimension=1, tiled=True
            ).astype(jnp.float32),
            lax.psum_scatter(
                count_part.astype(jnp.bfloat16), "depth", scatter_dimension=1, tiled=True
            ).astype(jnp.float32),
        )
        proj_mine = jnp.dot(
            outer_mine.reshape(residue_row_block * col_block, outer_width),
            out_wide,
            precision=highest,
        )
        proj_mine = proj_mine.reshape(residue_row_block, col_block, pair_width)
        count_mine = count_mine.reshape(residue_row_block, col_block)
        projected = lax.dynamic_update_slice_in_dim(projected, proj_mine, col_start, 1)
        pair_count = lax.dynamic_update_slice_in_dim(pair_count, count_mine, col_start, 1)
        return (projected, pair_count)

    projected, pair_count = lax.fori_loop(
        0,
        block_count,
        forward_step,
        (
            jnp.zeros((residue_row_block, pair_cols, pair_width), jnp.float32),
            jnp.zeros((residue_row_block, pair_cols), jnp.float32),
        ),
    )
    count_column = pair_count.reshape(residue_row_block * pair_cols, 1)
    mid_act = (
        pair_activation_input.reshape(residue_row_block * pair_cols, pair_width).astype(jnp.float32)
        + projected.reshape(residue_row_block * pair_cols, pair_width) / count_column
    )
    pair_scaled, pair_inv = norm_pieces(mid_act)
    pair_normed = (pair_scaled * pair_norm_gain).astype(jnp.bfloat16)
    pre_act = jnp.dot(pair_normed, hidden_weight, preferred_element_type=jnp.float32)
    act_value, act_slope = silu_pieces(pre_act)
    hidden = act_value.astype(jnp.bfloat16)
    masked_grad = (
        pair_output_gradient * pair_update_mask.astype(jnp.bfloat16)[:, :, None]
    ).reshape(residue_row_block * pair_cols, pair_width)
    final_matrix_derivative = jnp.dot(hidden.T, masked_grad, preferred_element_type=jnp.float32)
    back_prod = jnp.dot(masked_grad, back_weight.T, preferred_element_type=jnp.float32)
    grad_hidden = (back_prod * act_slope).astype(jnp.bfloat16)
    middle_matrix_derivative = jnp.dot(
        pair_normed.T, grad_hidden, preferred_element_type=jnp.float32
    )
    grad_scaled = (
        jnp.dot(grad_hidden, hidden_weight.T, preferred_element_type=jnp.float32) * pair_norm_gain
    )
    grad_mid = pair_output_gradient.reshape(residue_row_block * pair_cols, pair_width).astype(
        jnp.float32
    ) + standardize_adjoint(grad_scaled, pair_scaled, pair_inv)
    couple_features_derivative = grad_mid.astype(jnp.bfloat16).reshape(
        residue_row_block, pair_cols, pair_width
    )
    grad_opm = (
        (grad_mid / count_column)
        .astype(jnp.bfloat16)
        .reshape(residue_row_block, pair_cols, pair_width)
    )
    full_opm = lax.all_gather(grad_opm, "depth", axis=1, tiled=True).reshape(
        residue_row_block, depth_count, pair_cols, pair_width
    )

    def backward_step(step_index, loop_state):
        grad_left_acc, grad_out, right_term = loop_state
        col_start = step_index * col_block
        outer_part, right_piece = partial_outer(col_start)
        opm_piece = lax.dynamic_slice_in_dim(full_opm, col_start, col_block, 2).reshape(
            residue_row_block * block_depth * col_block, pair_width
        )
        grad_out = grad_out + jnp.dot(
            outer_part.reshape(residue_row_block * block_depth * col_block, outer_width).T,
            opm_piece.astype(jnp.float32),
            precision=highest,
        )
        grad_outer = jnp.dot(opm_piece, output_weight.T, preferred_element_type=jnp.float32).astype(
            jnp.bfloat16
        )
        grad_outer = grad_outer.reshape(
            residue_row_block, block_depth, col_block, proj_width, proj_width
        )
        grad_left_acc = grad_left_acc + jnp.einsum(
            "iejcd,sejd->sic", grad_outer, right_piece, preferred_element_type=jnp.float32
        )
        piece_term = jnp.einsum(
            "iejcd,sic->ejsd", grad_outer, left_proj, preferred_element_type=jnp.float32
        )
        piece_term = piece_term.reshape(block_depth, col_block, seq_total * proj_width)
        right_term = lax.dynamic_update_slice_in_dim(right_term, piece_term, col_start, 1)
        return (grad_left_acc, grad_out, right_term)

    grad_left_acc, result_matrix_derivative, right_term = lax.fori_loop(
        0,
        block_count,
        backward_step,
        (
            jnp.zeros((seq_total, residue_row_block, proj_width), jnp.float32),
            jnp.zeros((outer_width, pair_width), jnp.float32),
            jnp.zeros((block_depth, pair_cols, seq_total * proj_width), jnp.float32),
        ),
    )
    grad_right_sum = lax.psum_scatter(
        right_term.reshape(residues, seq_total * proj_width), "col", scatter_dimension=0, tiled=True
    )
    grad_right_acc = jnp.transpose(
        grad_right_sum.reshape(residue_row_block, seq_total, proj_width), (1, 0, 2)
    )
    grad_left = (grad_left_acc * mask_floating[:, :, None]).astype(jnp.bfloat16)
    grad_right = (grad_right_acc * mask_floating[:, :, None]).astype(jnp.bfloat16)
    normed_rows = normalized_rows.reshape(sequence_row_block * residue_row_block, channel_total)
    first_projector_derivative = jnp.dot(
        normed_rows.T,
        grad_left.reshape(sequence_row_block * residue_row_block, proj_width),
        preferred_element_type=jnp.float32,
    )
    second_projector_derivative = jnp.dot(
        normed_rows.T,
        grad_right.reshape(sequence_row_block * residue_row_block, proj_width),
        preferred_element_type=jnp.float32,
    )
    standardized_derivative = jnp.dot(
        grad_left, first_projector.T, preferred_element_type=jnp.float32
    ) + jnp.dot(grad_right, second_projector.T, preferred_element_type=jnp.float32)
    features_derivative = standardize_adjoint(
        standardized_derivative * layer_scale_factor, standardized_features, reciprocal_spread
    ).astype(jnp.bfloat16)
    weight_sums = lax.psum(
        (
            first_projector_derivative,
            second_projector_derivative,
            result_matrix_derivative,
            middle_matrix_derivative,
            final_matrix_derivative,
        ),
        ("depth", "col"),
    )
    return (
        features_derivative,
        couple_features_derivative,
        weight_sums[0],
        weight_sums[1],
        weight_sums[2],
        weight_sums[3],
        weight_sums[4],
    )


FEW_RESIDUES = 32
MASK_ROWS = 16


def butterfly(blocks, group):
    lane_group = lax.broadcasted_iota(jnp.int32, blocks[0].shape, 1) // group
    width = 4 * group
    for bit in (2, 1):
        low = (lane_group & bit) == 0
        swapped = list(blocks)
        for at in range(4):
            if at & bit:
                continue
            here, there = blocks[at], blocks[at | bit]
            moving = jnp.where(low, there, here)
            if bit == 2:
                moved = pltpu.roll(moving, 2 * group, 1)
            else:
                moved = jnp.where(
                    low, pltpu.roll(moving, width - group, 1), pltpu.roll(moving, group, 1)
                )
            swapped[at] = jnp.where(low, here, moved)
            swapped[at | bit] = jnp.where(low, moved, there)
        blocks = swapped
    return blocks


def wide_projector(first_ref, second_ref, copies):
    return jnp.concatenate([first_ref[...]] * copies + [second_ref[...]] * copies, axis=0)


def pre_kernel(
    ids_ref,
    x_ref,
    maskt_ref,
    pmask_ref,
    scale_ref,
    first_ref,
    second_ref,
    sent_ref,
    normed_ref,
    scaled_ref,
    inv_ref,
    lanes_ref,
    wide_ref,
    tile_ref,
):
    res, seqs = maskt_ref.shape
    lanes = sent_ref.shape[2]
    group = lanes // res
    scaled, inv = norm_pieces(x_ref[...].astype(jnp.float32))
    scaled_ref[...] = scaled
    inv_ref[...] = inv
    normed = (scaled * scale_ref[...]).astype(jnp.bfloat16)
    normed_ref[...] = normed
    wide = lax.dot_general(
        normed,
        wide_projector(first_ref, second_ref, res),
        (((1,), (1,)), ((), ())),
        preferred_element_type=jnp.float32,
    )
    for at in range(2):
        wide_ref[at] = wide[:, at * lanes : (at + 1) * lanes]
    tile_ref[...] = jnp.zeros(tile_ref.shape, jnp.float32)
    mask = maskt_ref[...].astype(jnp.float32)
    tile_ref[0:res, 0:seqs] = mask
    spread = (
        lax.broadcasted_iota(jnp.int32, (MASK_ROWS, lanes), 1) // group
        == lax.broadcasted_iota(jnp.int32, (MASK_ROWS, lanes), 0)
    ).astype(jnp.float32)
    mask_lanes = lax.dot_general(
        tile_ref[...], spread, (((0,), (0,)), ((), ())), preferred_element_type=jnp.float32
    )[:seqs]
    lanes_ref[...] = mask_lanes
    twice = jnp.concatenate([mask] * (lanes // seqs), axis=1)
    here = lax.broadcasted_iota(jnp.int32, (res, lanes), 1) // seqs == ids_ref[0]
    tile_ref[0:res, :] = jnp.where(here, twice, 0.0)
    tile_ref[res : 2 * res, 0 : pmask_ref.shape[1]] = pmask_ref[...].astype(jnp.float32)
    lane_group = lax.broadcasted_iota(jnp.int32, (seqs, lanes), 1) // group
    for at in range(2):
        both = wide_ref[at, pl.ds(0, seqs, stride=res), :]
        for r in range(1, res):
            both = jnp.where(
                lane_group == r, wide_ref[at, pl.ds(r, seqs, stride=res), :], both
            )
        sent_ref[0, at * seqs : (at + 1) * seqs, :] = (both * mask_lanes).astype(jnp.bfloat16)
    sent_ref[0, 2 * seqs :, :] = tile_ref[...].astype(jnp.bfloat16)


def main_kernel(
    sizes,
    orders,
    ids_ref,
    mine_ref,
    other_ref,
    pmine_ref,
    pother_ref,
    wout_ref,
    wturn_ref,
    gain_ref,
    hid_ref,
    back_ref,
    normed_ref,
    lanes_ref,
    couple_ref,
    part_ref,
    outer_ref,
    opm_ref,
    pn_ref,
    gh_ref,
    hidden_ref,
    mg_ref,
    spread_ref,
    got_ref,
    pgot_ref,
    leftn_ref,
    rightt_ref,
    leftt_ref,
    turn_ref,
    maskt_ref,
    cnt_ref,
    cntl_ref,
    pml_ref,
    pm_ref,
    proj_out_ref,
    gmid_ref,
    gf_ref,
    grow_ref,
    gcol_ref,
    gor_ref,
    goc_ref,
    gs_ref,
):
    seqs, res, pair_cols, width = sizes
    depths, cols = got_ref.shape[0], got_ref.shape[1]
    residues = cols * res
    lanes = res * width
    per = res * pair_cols
    half = residues * pair_cols
    pairs = depths * half
    me_depth = ids_ref[0]
    me_col = ids_ref[1]
    f32, bf16 = jnp.float32, jnp.bfloat16

    for into, mine, other, order in (
        (got_ref, mine_ref, other_ref, orders[0]),
        (pgot_ref, pmine_ref, pother_ref, orders[1]),
    ):
        for at, partner in enumerate(order):
            into[me_depth, me_col ^ partner] = mine[at]
            into[1 - me_depth, me_col ^ partner] = other[at]

    for e in range(depths):
        for k in range(cols):
            leftn_ref[e * seqs : (e + 1) * seqs, k * lanes : (k + 1) * lanes] = got_ref[
                e, k, 0:seqs, :
            ]
    for at, out in ((0, leftt_ref), (1, rightt_ref)):
        for k in range(cols):
            block = jnp.concatenate(
                [got_ref[e, k, at * seqs : (at + 1) * seqs, :] for e in range(depths)], axis=0
            ).astype(f32)
            turn_ref[k * lanes : (k + 1) * lanes, :] = block.T
        for d in range(width):
            out[d * residues : (d + 1) * residues, :] = turn_ref[
                pl.ds(d, residues, stride=width), :
            ].astype(bf16)

    base = 2 * seqs
    pair_lane = lax.broadcasted_iota(jnp.int32, (pair_cols, lanes), 1)
    pair_row = lax.broadcasted_iota(jnp.int32, (pair_cols, lanes), 0)
    for k in range(cols):
        tiles = [got_ref[e, k, base : base + MASK_ROWS, :].astype(f32) for e in range(depths)]
        maskt_ref[k * res : (k + 1) * res, :] = tiles[0][0:res] + tiles[1][0:res]
        for e in range(depths):
            for r in range(res):
                row = tiles[e][res + r : res + r + 1, :]
                first = e * half + (k * res + r) * pair_cols
                pml_ref[first : first + pair_cols, :] = jnp.where(
                    pair_lane == pair_row, row, 0.0
                ).astype(bf16)
    maskt = maskt_ref[...]
    for e in range(depths):
        cols_mask = maskt[e * pair_cols : (e + 1) * pair_cols, :]
        for i in range(residues):
            first = e * half + i * pair_cols
            cntl_ref[first : first + pair_cols, :] = (maskt[i : i + 1, :] * cols_mask).astype(bf16)
    ones = jnp.ones((lanes, lanes), bf16)
    cnt_ref[...] = jnp.dot(cntl_ref[...], ones, preferred_element_type=f32)
    pm_ref[...] = jnp.dot(pml_ref[...], ones, preferred_element_type=f32).astype(bf16)

    for dh in range(width // 4):
        prod = jnp.dot(
            rightt_ref[dh * 4 * residues : (dh + 1) * 4 * residues, :],
            leftn_ref[...],
            preferred_element_type=f32,
        )
        for k in range(cols):
            piece = prod[:, k * lanes : (k + 1) * lanes]
            turned = butterfly(
                [piece[a * residues : (a + 1) * residues] for a in range(4)], width
            )
            for il in range(res):
                block = turned[il].astype(bf16)
                for e in range(depths):
                    first = e * half + (k * res + il) * pair_cols
                    outer_ref[first : first + pair_cols, dh * lanes : (dh + 1) * lanes] = block[
                        e * pair_cols : (e + 1) * pair_cols
                    ]
    proj_out_ref[...] = jnp.dot(outer_ref[...], wturn_ref[...], preferred_element_type=f32)

    gain = gain_ref[...]
    chunk = 2 * per
    for at in range(pairs // chunk):
        rows = slice(at * chunk, (at + 1) * chunk)
        e, k = divmod(2 * at, cols)
        act, grad = [
            jnp.concatenate(
                [pgot_ref[e, k + b, at * per : (at + 1) * per, :] for b in range(2)], axis=0
            )
            for at in range(2)
        ]
        act = act.astype(f32)
        count = cnt_ref[rows, :]
        mid = act + proj_out_ref[rows, :] / count
        scaled, inv = norm_pieces(mid)
        normed = (scaled * gain).astype(bf16)
        pn_ref[rows, :] = normed
        pre = jnp.dot(normed, hid_ref[...], preferred_element_type=f32)
        value, slope = silu_pieces(pre)
        hidden_ref[rows, :] = value.astype(bf16)
        masked = grad * pm_ref[rows, :]
        mg_ref[rows, :] = masked
        back = lax.dot_general(
            masked, back_ref[...], (((1,), (1,)), ((), ())), preferred_element_type=f32
        )
        ghid = (back * slope).astype(bf16)
        gh_ref[rows, :] = ghid
        gsc = (
            lax.dot_general(
                ghid, hid_ref[...], (((1,), (1,)), ((), ())), preferred_element_type=f32
            )
            * gain
        )
        gmid = grad.astype(f32) + standardize_adjoint(gsc, scaled, inv)
        gmid_ref[rows, :] = gmid
        opm = (gmid / count).astype(bf16)
        opm_ref[rows, :] = opm
        gf_ref[rows, :] = opm.astype(f32)
    start = pl.multiple_of(me_depth * half + me_col * per, per)
    couple_ref[...] = gmid_ref[pl.ds(start, per), :].astype(bf16)

    for il in range(res):
        for e in range(depths):
            first = pl.multiple_of(e * half + (me_col * res + il) * pair_cols, pair_cols)
            grow_ref[il * residues + e * pair_cols : il * residues + (e + 1) * pair_cols, :] = (
                gf_ref[pl.ds(first, pair_cols), :].astype(bf16)
            )
    my_half = (me_col * res) // pair_cols
    my_first = me_col * res - my_half * pair_cols
    for jl in range(res):
        gcol_ref[jl * residues : (jl + 1) * residues, :] = gf_ref[
            pl.ds(my_half * half + my_first + jl, residues, stride=pair_cols), :
        ].astype(bf16)
    for lhs, weight, out in ((grow_ref, wturn_ref, gor_ref), (gcol_ref, wout_ref, goc_ref)):
        for dh in range(width // 4):
            piece = lax.dot_general(
                lhs[...],
                weight[dh * lanes : (dh + 1) * lanes, :],
                (((1,), (1,)), ((), ())),
                preferred_element_type=f32,
            )
            turned = butterfly(
                [piece[a * residues : (a + 1) * residues] for a in range(4)], width
            )
            for dl in range(4):
                first = (dh * 4 + dl) * residues
                out[first : first + residues, :] = turned[dl].astype(bf16)
    sums = [
        lax.dot_general(lhs[...], rhs[...], (((0,), (0,)), ((), ())), preferred_element_type=f32)
        for lhs, rhs in ((rightt_ref, gor_ref), (leftt_ref, goc_ref))
    ]
    mask_lanes = lanes_ref[...]
    upper = me_depth == 0
    sums = [
        (jnp.where(upper, total[:seqs], total[seqs:]) * mask_lanes).astype(bf16).astype(f32)
        for total in sums
    ]
    lane_group = lax.broadcasted_iota(jnp.int32, (seqs, lanes), 1) // width
    for r in range(res):
        for at in range(2):
            gs_ref[at, pl.ds(r, seqs, stride=res), :] = jnp.where(
                lane_group == r, sums[at], 0.0
            )
    spread = jnp.concatenate([gs_ref[0], gs_ref[1]], axis=1).astype(bf16)
    spread_ref[...] = spread
    cross = lax.dot_general(
        spread, normed_ref[...], (((0,), (0,)), ((), ())), preferred_element_type=f32
    )
    for at in range(2):
        total = cross[at * lanes : at * lanes + width]
        for r in range(1, res):
            total = total + cross[at * lanes + r * width : at * lanes + (r + 1) * width]
        part_ref[at * width : (at + 1) * width, :] = total.astype(bf16)


def out_weight_kernel(outer_ref, opm_ref, dout_ref, turn_ref):
    width = int(dout_ref.shape[0] ** 0.5 + 0.5)
    turn_ref[...] = lax.dot_general(
        outer_ref[...], opm_ref[...], (((0,), (0,)), ((), ())), preferred_element_type=jnp.float32
    )
    for c in range(width):
        dout_ref[c * width : (c + 1) * width, :] = turn_ref[pl.ds(c, width, stride=width), :]


def transition_weight_kernel(pn_ref, gh_ref, hidden_ref, mg_ref, dhid_ref, dback_ref):
    for lhs, rhs, out in ((pn_ref, gh_ref, dhid_ref), (hidden_ref, mg_ref, dback_ref)):
        out[...] = lax.dot_general(
            lhs[...], rhs[...], (((0,), (0,)), ((), ())), preferred_element_type=jnp.float32
        )


def feature_kernel(
    copies, spread_ref, first_ref, second_ref, scale_ref, scaled_ref, inv_ref, feat_ref
):
    back = jnp.dot(
        spread_ref[...],
        wide_projector(first_ref, second_ref, copies),
        preferred_element_type=jnp.float32,
    )
    feat_ref[...] = standardize_adjoint(
        back * scale_ref[...], scaled_ref[...], inv_ref[...]
    ).astype(jnp.bfloat16)


def swap_depth(block):
    return lax.ppermute(block, "depth", [(0, 1), (1, 0)])


def swap_col(block, partner):
    count = lax.axis_size("col")
    return lax.ppermute(block, "col", [(at, at ^ partner) for at in range(count)])


def doubled(block, steps):
    order = [0]
    for step in steps:
        block = jnp.concatenate([block, swap_col(block, step)])
        order = order + [partner ^ step for partner in order]
    return block, tuple(order)


def whole_plan(
    alignment_activations,
    alignment_mask,
    pair_activation_input,
    pair_update_mask,
    pair_output_gradient,
    layer_scale_factor,
    first_projector,
    second_projector,
    output_weight,
    pair_norm_gain,
    hidden_weight,
    back_weight,
):
    seqs, res, channels = alignment_activations.shape
    width = first_projector.shape[1]
    outer_width = width * width
    cols = lax.axis_size("col")
    depths = lax.axis_size("depth")
    residues = res * cols
    pair_cols, pair_width = pair_activation_input.shape[1:]
    hid = hidden_weight.shape[1]
    per = res * pair_cols
    pairs = residues * residues
    lanes = res * width
    rows = 2 * seqs + MASK_ROWS
    f32, bf16 = jnp.float32, jnp.bfloat16
    ids = jnp.stack([lax.axis_index("depth"), lax.axis_index("col")]).astype(jnp.int32)
    smem = pl.BlockSpec(memory_space=pltpu.SMEM)
    vmem = pl.BlockSpec(memory_space=pltpu.VMEM)
    params = pltpu.CompilerParams(vmem_limit_bytes=40 * 2**20)
    scale = layer_scale_factor.reshape(1, channels)
    first, second = first_projector.T, second_projector.T
    wturn = jnp.transpose(output_weight.reshape(width, width, pair_width), (1, 0, 2)).reshape(
        outer_width, pair_width
    )
    shape = jax.ShapeDtypeStruct
    pair_arrays = jnp.concatenate(
        [
            pair_activation_input.reshape(1, per, pair_width),
            pair_output_gradient.reshape(1, per, pair_width),
        ],
        axis=1,
    )
    pmine, porder = doubled(pair_arrays, (1, 4, 2))
    sent, normed, scaled, inv, mask_lanes = pl.pallas_call(
        pre_kernel,
        out_shape=(
            shape((1, rows, pair_width), bf16),
            shape((seqs * res, channels), bf16),
            shape((seqs * res, channels), f32),
            shape((seqs * res, 1), f32),
            shape((seqs, lanes), f32),
        ),
        in_specs=[smem] + [vmem] * 6,
        out_specs=[vmem] * 5,
        scratch_shapes=[
            pltpu.VMEM((2, seqs * res, lanes), f32),
            pltpu.VMEM((MASK_ROWS, lanes), f32),
        ],
        compiler_params=params,
        name="project",
    )(
        ids,
        alignment_activations.reshape(seqs * res, channels),
        alignment_mask.T,
        pair_update_mask,
        scale,
        first,
        second,
    )
    mine, order = doubled(sent, (4, 2, 1))
    other = swap_depth(mine)
    pother = swap_depth(pmine)
    couple, part, outer, opm, pn, gh, hidden, mg, spread = pl.pallas_call(
        functools.partial(main_kernel, (seqs, res, pair_cols, width), (order, porder)),
        out_shape=(
            shape((per, pair_width), bf16),
            shape((2 * width, channels), bf16),
            shape((pairs, outer_width), bf16),
            shape((pairs, pair_width), bf16),
            shape((pairs, pair_width), bf16),
            shape((pairs, hid), bf16),
            shape((pairs, hid), bf16),
            shape((pairs, pair_width), bf16),
            shape((seqs * res, 2 * lanes), bf16),
        ),
        in_specs=[smem] + [vmem] * 11,
        out_specs=[vmem] * 9,
        scratch_shapes=[
            pltpu.VMEM((depths, cols, rows, pair_width), bf16),
            pltpu.VMEM((depths, cols, 2 * per, pair_width), bf16),
            pltpu.VMEM((depths * seqs, residues * width), bf16),
            pltpu.VMEM((residues * width, depths * seqs), bf16),
            pltpu.VMEM((residues * width, depths * seqs), bf16),
            pltpu.VMEM((residues * width, depths * seqs), f32),
            pltpu.VMEM((residues, depths * seqs), f32),
            pltpu.VMEM((pairs, lanes), f32),
            pltpu.VMEM((pairs, lanes), bf16),
            pltpu.VMEM((pairs, lanes), bf16),
            pltpu.VMEM((pairs, lanes), bf16),
            pltpu.VMEM((pairs, pair_width), f32),
            pltpu.VMEM((pairs, pair_width), f32),
            pltpu.VMEM((pairs, pair_width), f32),
            pltpu.VMEM((res * residues, pair_width), bf16),
            pltpu.VMEM((res * residues, pair_width), bf16),
            pltpu.VMEM((residues * width, lanes), bf16),
            pltpu.VMEM((residues * width, lanes), bf16),
            pltpu.VMEM((2, seqs * res, lanes), f32),
        ],
        compiler_params=params,
        name="pair_work",
    )(
        ids,
        mine,
        other,
        pmine,
        pother,
        output_weight,
        wturn,
        pair_norm_gain.reshape(1, pair_width),
        hidden_weight,
        back_weight,
        normed,
        mask_lanes,
    )
    total = part.astype(f32)

    def add_partner(total, step, beside):
        kept = lax.optimization_barrier(total.astype(bf16))
        came = swap_col(kept, step) if step else swap_depth(kept)
        came, beside = lax.optimization_barrier((came, beside))
        return kept.astype(f32) + came.astype(f32), beside

    feat = pl.pallas_call(
        functools.partial(feature_kernel, res),
        out_shape=shape((seqs * res, channels), bf16),
        in_specs=[vmem] * 6,
        out_specs=vmem,
        compiler_params=params,
        name="features",
    )(spread, first, second, scale, scaled, inv)
    total, feat = add_partner(total, 0, feat)
    dout = pl.pallas_call(
        out_weight_kernel,
        out_shape=shape((outer_width, pair_width), f32),
        in_specs=[vmem] * 2,
        out_specs=vmem,
        scratch_shapes=[pltpu.VMEM((outer_width, pair_width), f32)],
        compiler_params=params,
        name="out_weight",
    )(outer, opm)
    total, dout = add_partner(total, 4, dout)
    dhid, dback = pl.pallas_call(
        transition_weight_kernel,
        out_shape=(shape((pair_width, hid), f32), shape((hid, pair_width), f32)),
        in_specs=[vmem] * 4,
        out_specs=[vmem] * 2,
        compiler_params=params,
        name="transition_weights",
    )(pn, gh, hidden, mg)
    total, (dhid, dback) = add_partner(total, 2, (dhid, dback))
    total, _ = add_partner(total, 1, ())
    return (
        feat.reshape(seqs, res, channels),
        couple.reshape(res, pair_cols, pair_width),
        total[:width].T,
        total[width:].T,
        dout,
        dhid,
        dback,
    )


def on_device(alignment_activations, *others):
    residues = alignment_activations.shape[1] * lax.axis_size("col")
    plan = whole_plan if residues <= FEW_RESIDUES else split_plan
    return plan(alignment_activations, *others)


def solution(mesh):
    in_specs = (
        P(("group", "depth"), "col", None),
        P(("group", "depth"), "col"),
        P(("group", "col"), "depth", None),
        P(("group", "col"), "depth"),
        P(("group", "col"), "depth", None),
        P(),
        P(),
        P(),
        P(),
        P(),
        P(),
        P(),
    )
    out_specs = (
        P(("group", "depth"), "col", None),
        P(("group", "col"), "depth", None),
        P("group", None),
        P("group", None),
        P("group", None),
        P("group", None),
        P("group", None),
    )
    return jax.shard_map(
        on_device, mesh=mesh, in_specs=in_specs, out_specs=out_specs, check_vma=False
    )
```

```python
import functools

import jax
import jax.numpy as jnp
from jax import lax
from jax.experimental import pallas as pl
from jax.experimental.pallas import tpu as pltpu
from jax.sharding import PartitionSpec as P

epsilon = 1e-05
highest = lax.Precision.HIGHEST


def norm_pieces(entries_drawn):
    center = entries_drawn - jnp.mean(entries_drawn, axis=-1, keepdims=True)
    inv_std = lax.rsqrt(jnp.mean(center * center, axis=-1, keepdims=True) + epsilon)
    return (center * inv_std, inv_std)


def standardize_adjoint(grad_scaled, scaled, inv_std):
    mean_grad = jnp.mean(grad_scaled, axis=-1, keepdims=True)
    mean_cross = jnp.mean(grad_scaled * scaled, axis=-1, keepdims=True)
    return inv_std * (grad_scaled - mean_grad - scaled * mean_cross)


def silu_pieces(pre_act):
    sigma = jax.nn.sigmoid(pre_act)
    return (pre_act * sigma, sigma * (1.0 + pre_act * (1.0 - sigma)))


def split_plan(
    alignment_activations,
    alignment_mask,
    pair_activation_input,
    pair_update_mask,
    pair_output_gradient,
    layer_scale_factor,
    first_projector,
    second_projector,
    output_weight,
    pair_norm_gain,
    hidden_weight,
    back_weight,
):
    sequence_row_block, residue_row_block, channel_total = alignment_activations.shape
    proj_width = first_projector.shape[1]
    outer_width = proj_width * proj_width
    depth_count = lax.axis_size("depth")
    residues = residue_row_block * lax.axis_size("col")
    pair_cols = pair_activation_input.shape[1]
    pair_width = pair_activation_input.shape[2]
    col_block = min(64, pair_cols)
    block_count = pair_cols // col_block
    standardized_features, reciprocal_spread = norm_pieces(
        alignment_activations.astype(jnp.float32)
    )
    normalized_rows = (standardized_features * layer_scale_factor).astype(jnp.bfloat16)
    mask_floating = alignment_mask.astype(jnp.float32)
    left_proj = (
        jnp.dot(normalized_rows, first_projector, preferred_element_type=jnp.float32)
        * mask_floating[:, :, None]
    ).astype(jnp.bfloat16)
    right_proj = (
        jnp.dot(normalized_rows, second_projector, preferred_element_type=jnp.float32)
        * mask_floating[:, :, None]
    ).astype(jnp.bfloat16)
    right_flat = right_proj.reshape(sequence_row_block, residue_row_block * proj_width)
    mask_converted = alignment_mask.astype(jnp.bfloat16)
    seq_total = left_proj.shape[0]
    gathered, gathered_mask = (
        lax.all_gather(right_flat, "col", axis=1, tiled=True),
        lax.all_gather(mask_converted, "col", axis=1, tiled=True),
    )
    right_blocks = gathered.reshape(seq_total, depth_count, pair_cols, proj_width)
    mask_blocks = gathered_mask.reshape(seq_total, depth_count, pair_cols)
    block_depth = right_blocks.shape[1]
    out_wide = output_weight.astype(jnp.float32)

    def partial_outer(col_start):
        right_piece = lax.dynamic_slice_in_dim(right_blocks, col_start, col_block, 2)
        outer_part = jnp.einsum(
            "sic,sejd->iejcd", left_proj, right_piece, preferred_element_type=jnp.float32
        )
        return (
            outer_part.reshape(residue_row_block, block_depth, col_block, outer_width),
            right_piece,
        )

    def forward_step(step_index, loop_state):
        projected, pair_count = loop_state
        col_start = step_index * col_block
        outer_part, right_piece = partial_outer(col_start)
        mask_piece = lax.dynamic_slice_in_dim(mask_blocks, col_start, col_block, 2).astype(
            jnp.float32
        )
        count_part = jnp.einsum("si,sej->iej", mask_floating, mask_piece, precision=highest)
        outer_mine, count_mine = (
            lax.psum_scatter(
                outer_part.astype(jnp.bfloat16), "depth", scatter_dimension=1, tiled=True
            ).astype(jnp.float32),
            lax.psum_scatter(
                count_part.astype(jnp.bfloat16), "depth", scatter_dimension=1, tiled=True
            ).astype(jnp.float32),
        )
        proj_mine = jnp.dot(
            outer_mine.reshape(residue_row_block * col_block, outer_width),
            out_wide,
            precision=highest,
        )
        proj_mine = proj_mine.reshape(residue_row_block, col_block, pair_width)
        count_mine = count_mine.reshape(residue_row_block, col_block)
        projected = lax.dynamic_update_slice_in_dim(projected, proj_mine, col_start, 1)
        pair_count = lax.dynamic_update_slice_in_dim(pair_count, count_mine, col_start, 1)
        return (projected, pair_count)

    projected, pair_count = lax.fori_loop(
        0,
        block_count,
        forward_step,
        (
            jnp.zeros((residue_row_block, pair_cols, pair_width), jnp.float32),
            jnp.zeros((residue_row_block, pair_cols), jnp.float32),
        ),
    )
    count_column = pair_count.reshape(residue_row_block * pair_cols, 1)
    mid_act = (
        pair_activation_input.reshape(residue_row_block * pair_cols, pair_width).astype(jnp.float32)
        + projected.reshape(residue_row_block * pair_cols, pair_width) / count_column
    )
    pair_scaled, pair_inv = norm_pieces(mid_act)
    pair_normed = (pair_scaled * pair_norm_gain).astype(jnp.bfloat16)
    pre_act = jnp.dot(pair_normed, hidden_weight, preferred_element_type=jnp.float32)
    act_value, act_slope = silu_pieces(pre_act)
    hidden = act_value.astype(jnp.bfloat16)
    masked_grad = (
        pair_output_gradient * pair_update_mask.astype(jnp.bfloat16)[:, :, None]
    ).reshape(residue_row_block * pair_cols, pair_width)
    final_matrix_derivative = jnp.dot(hidden.T, masked_grad, preferred_element_type=jnp.float32)
    back_prod = jnp.dot(masked_grad, back_weight.T, preferred_element_type=jnp.float32)
    grad_hidden = (back_prod * act_slope).astype(jnp.bfloat16)
    middle_matrix_derivative = jnp.dot(
        pair_normed.T, grad_hidden, preferred_element_type=jnp.float32
    )
    grad_scaled = (
        jnp.dot(grad_hidden, hidden_weight.T, preferred_element_type=jnp.float32) * pair_norm_gain
    )
    grad_mid = pair_output_gradient.reshape(residue_row_block * pair_cols, pair_width).astype(
        jnp.float32
    ) + standardize_adjoint(grad_scaled, pair_scaled, pair_inv)
    couple_features_derivative = grad_mid.astype(jnp.bfloat16).reshape(
        residue_row_block, pair_cols, pair_width
    )
    grad_opm = (
        (grad_mid / count_column)
        .astype(jnp.bfloat16)
        .reshape(residue_row_block, pair_cols, pair_width)
    )
    full_opm = lax.all_gather(grad_opm, "depth", axis=1, tiled=True).reshape(
        residue_row_block, depth_count, pair_cols, pair_width
    )

    def backward_step(step_index, loop_state):
        grad_left_acc, grad_out, right_term = loop_state
        col_start = step_index * col_block
        outer_part, right_piece = partial_outer(col_start)
        opm_piece = lax.dynamic_slice_in_dim(full_opm, col_start, col_block, 2).reshape(
            residue_row_block * block_depth * col_block, pair_width
        )
        grad_out = grad_out + jnp.dot(
            outer_part.reshape(residue_row_block * block_depth * col_block, outer_width).T,
            opm_piece.astype(jnp.float32),
            precision=highest,
        )
        grad_outer = jnp.dot(opm_piece, output_weight.T, preferred_element_type=jnp.float32).astype(
            jnp.bfloat16
        )
        grad_outer = grad_outer.reshape(
            residue_row_block, block_depth, col_block, proj_width, proj_width
        )
        grad_left_acc = grad_left_acc + jnp.einsum(
            "iejcd,sejd->sic", grad_outer, right_piece, preferred_element_type=jnp.float32
        )
        piece_term = jnp.einsum(
            "iejcd,sic->ejsd", grad_outer, left_proj, preferred_element_type=jnp.float32
        )
        piece_term = piece_term.reshape(block_depth, col_block, seq_total * proj_width)
        right_term = lax.dynamic_update_slice_in_dim(right_term, piece_term, col_start, 1)
        return (grad_left_acc, grad_out, right_term)

    grad_left_acc, result_matrix_derivative, right_term = lax.fori_loop(
        0,
        block_count,
        backward_step,
        (
            jnp.zeros((seq_total, residue_row_block, proj_width), jnp.float32),
            jnp.zeros((outer_width, pair_width), jnp.float32),
            jnp.zeros((block_depth, pair_cols, seq_total * proj_width), jnp.float32),
        ),
    )
    grad_right_sum = lax.psum_scatter(
        right_term.reshape(residues, seq_total * proj_width), "col", scatter_dimension=0, tiled=True
    )
    grad_right_acc = jnp.transpose(
        grad_right_sum.reshape(residue_row_block, seq_total, proj_width), (1, 0, 2)
    )
    grad_left = (grad_left_acc * mask_floating[:, :, None]).astype(jnp.bfloat16)
    grad_right = (grad_right_acc * mask_floating[:, :, None]).astype(jnp.bfloat16)
    normed_rows = normalized_rows.reshape(sequence_row_block * residue_row_block, channel_total)
    first_projector_derivative = jnp.dot(
        normed_rows.T,
        grad_left.reshape(sequence_row_block * residue_row_block, proj_width),
        preferred_element_type=jnp.float32,
    )
    second_projector_derivative = jnp.dot(
        normed_rows.T,
        grad_right.reshape(sequence_row_block * residue_row_block, proj_width),
        preferred_element_type=jnp.float32,
    )
    standardized_derivative = jnp.dot(
        grad_left, first_projector.T, preferred_element_type=jnp.float32
    ) + jnp.dot(grad_right, second_projector.T, preferred_element_type=jnp.float32)
    features_derivative = standardize_adjoint(
        standardized_derivative * layer_scale_factor, standardized_features, reciprocal_spread
    ).astype(jnp.bfloat16)
    weight_sums = lax.psum(
        (
            first_projector_derivative,
            second_projector_derivative,
            result_matrix_derivative,
            middle_matrix_derivative,
            final_matrix_derivative,
        ),
        ("depth", "col"),
    )
    return (
        features_derivative,
        couple_features_derivative,
        weight_sums[0],
        weight_sums[1],
        weight_sums[2],
        weight_sums[3],
        weight_sums[4],
    )


FEW_RESIDUES = 32
MASK_ROWS = 16


def butterfly(blocks, group):
    lane_group = lax.broadcasted_iota(jnp.int32, blocks[0].shape, 1) // group
    width = 4 * group
    for bit in (2, 1):
        low = (lane_group & bit) == 0
        swapped = list(blocks)
        for at in range(4):
            if at & bit:
                continue
            here, there = blocks[at], blocks[at | bit]
            moving = jnp.where(low, there, here)
            if bit == 2:
                moved = pltpu.roll(moving, 2 * group, 1)
            else:
                moved = jnp.where(
                    low, pltpu.roll(moving, width - group, 1), pltpu.roll(moving, group, 1)
                )
            swapped[at] = jnp.where(low, here, moved)
            swapped[at | bit] = jnp.where(low, moved, there)
        blocks = swapped
    return blocks


def wide_projector(first_ref, second_ref, copies):
    return jnp.concatenate([first_ref[...]] * copies + [second_ref[...]] * copies, axis=0)


def pre_kernel(
    ids_ref,
    x_hbm,
    maskt_hbm,
    pmask_hbm,
    scale_hbm,
    first_hbm,
    second_hbm,
    sent_ref,
    normed_ref,
    scaled_ref,
    inv_ref,
    lanes_ref,
    wide_ref,
    tile_ref,
    x_ref,
    maskt_ref,
    pmask_ref,
    scale_ref,
    first_ref,
    second_ref,
    sems,
):
    copies = [
        pltpu.make_async_copy(source, target, sems.at[at])
        for at, (source, target) in enumerate(
            (
                (x_hbm, x_ref),
                (maskt_hbm, maskt_ref),
                (pmask_hbm, pmask_ref),
                (scale_hbm, scale_ref),
                (first_hbm, first_ref),
                (second_hbm, second_ref),
            )
        )
    ]
    for copy in copies:
        copy.start()
    for copy in copies:
        copy.wait()
    res, seqs = maskt_ref.shape
    lanes = sent_ref.shape[2]
    group = lanes // res
    scaled, inv = norm_pieces(
        x_ref[...].astype(jnp.float32).reshape(seqs * res, x_ref.shape[2])
    )
    scaled_ref[...] = scaled
    inv_ref[...] = inv
    normed = (scaled * scale_ref[...]).astype(jnp.bfloat16)
    normed_ref[...] = normed
    wide = lax.dot_general(
        normed,
        wide_projector(first_ref, second_ref, res),
        (((1,), (1,)), ((), ())),
        preferred_element_type=jnp.float32,
    )
    for at in range(2):
        wide_ref[at] = wide[:, at * lanes : (at + 1) * lanes]
    tile_ref[...] = jnp.zeros(tile_ref.shape, jnp.float32)
    mask = maskt_ref[...].astype(jnp.float32)
    tile_ref[0:res, 0:seqs] = mask
    spread = (
        lax.broadcasted_iota(jnp.int32, (MASK_ROWS, lanes), 1) // group
        == lax.broadcasted_iota(jnp.int32, (MASK_ROWS, lanes), 0)
    ).astype(jnp.float32)
    mask_lanes = lax.dot_general(
        tile_ref[...], spread, (((0,), (0,)), ((), ())), preferred_element_type=jnp.float32
    )[:seqs]
    lanes_ref[...] = mask_lanes
    twice = jnp.concatenate([mask] * (lanes // seqs), axis=1)
    here = lax.broadcasted_iota(jnp.int32, (res, lanes), 1) // seqs == ids_ref[0]
    tile_ref[0:res, :] = jnp.where(here, twice, 0.0)
    tile_ref[res : 2 * res, 0 : pmask_ref.shape[1]] = pmask_ref[...].astype(jnp.float32)
    lane_group = lax.broadcasted_iota(jnp.int32, (seqs, lanes), 1) // group
    for at in range(2):
        both = wide_ref[at, pl.ds(0, seqs, stride=res), :]
        for r in range(1, res):
            both = jnp.where(
                lane_group == r, wide_ref[at, pl.ds(r, seqs, stride=res), :], both
            )
        sent_ref[0, at * seqs : (at + 1) * seqs, :] = (both * mask_lanes).astype(jnp.bfloat16)
    sent_ref[0, 2 * seqs :, :] = tile_ref[...].astype(jnp.bfloat16)


def main_kernel(
    sizes,
    orders,
    ids_ref,
    mine_ref,
    other_ref,
    pmine_ref,
    pother_ref,
    wout_ref,
    wturn_ref,
    gain_ref,
    hid_ref,
    back_ref,
    normed_ref,
    lanes_ref,
    couple_ref,
    part_ref,
    outer_ref,
    opm_ref,
    pn_ref,
    gh_ref,
    hidden_ref,
    mg_ref,
    spread_ref,
    got_ref,
    pgot_ref,
    leftn_ref,
    rightt_ref,
    leftt_ref,
    turn_ref,
    maskt_ref,
    cnt_ref,
    cntl_ref,
    pml_ref,
    pm_ref,
    proj_out_ref,
    gmid_ref,
    gf_ref,
    grow_ref,
    gcol_ref,
    gor_ref,
    goc_ref,
    gs_ref,
):
    seqs, res, pair_cols, width = sizes
    depths, cols = got_ref.shape[0], got_ref.shape[1]
    residues = cols * res
    lanes = res * width
    per = res * pair_cols
    half = residues * pair_cols
    pairs = depths * half
    me_depth = ids_ref[0]
    me_col = ids_ref[1]
    f32, bf16 = jnp.float32, jnp.bfloat16

    for into, mine, other, order in (
        (got_ref, mine_ref, other_ref, orders[0]),
        (pgot_ref, pmine_ref, pother_ref, orders[1]),
    ):
        for at, partner in enumerate(order):
            into[me_depth, me_col ^ partner] = mine[at]
            into[1 - me_depth, me_col ^ partner] = other[at]

    for e in range(depths):
        for k in range(cols):
            leftn_ref[e * seqs : (e + 1) * seqs, k * lanes : (k + 1) * lanes] = got_ref[
                e, k, 0:seqs, :
            ]
    for at, out in ((0, leftt_ref), (1, rightt_ref)):
        for k in range(cols):
            block = jnp.concatenate(
                [got_ref[e, k, at * seqs : (at + 1) * seqs, :] for e in range(depths)], axis=0
            ).astype(f32)
            turn_ref[k * lanes : (k + 1) * lanes, :] = block.T
        for d in range(width):
            out[d * residues : (d + 1) * residues, :] = turn_ref[
                pl.ds(d, residues, stride=width), :
            ].astype(bf16)

    base = 2 * seqs
    pair_lane = lax.broadcasted_iota(jnp.int32, (pair_cols, lanes), 1)
    pair_row = lax.broadcasted_iota(jnp.int32, (pair_cols, lanes), 0)
    for k in range(cols):
        tiles = [got_ref[e, k, base : base + MASK_ROWS, :].astype(f32) for e in range(depths)]
        maskt_ref[k * res : (k + 1) * res, :] = tiles[0][0:res] + tiles[1][0:res]
        for e in range(depths):
            for r in range(res):
                row = tiles[e][res + r : res + r + 1, :]
                first = e * half + (k * res + r) * pair_cols
                pml_ref[first : first + pair_cols, :] = jnp.where(
                    pair_lane == pair_row, row, 0.0
                ).astype(bf16)
    maskt = maskt_ref[...]
    for e in range(depths):
        cols_mask = maskt[e * pair_cols : (e + 1) * pair_cols, :]
        for i in range(residues):
            first = e * half + i * pair_cols
            cntl_ref[first : first + pair_cols, :] = (maskt[i : i + 1, :] * cols_mask).astype(bf16)
    ones = jnp.ones((lanes, lanes), bf16)
    cnt_ref[...] = jnp.dot(cntl_ref[...], ones, preferred_element_type=f32)
    pm_ref[...] = jnp.dot(pml_ref[...], ones, preferred_element_type=f32).astype(bf16)

    for dh in range(width // 4):
        prod = jnp.dot(
            rightt_ref[dh * 4 * residues : (dh + 1) * 4 * residues, :],
            leftn_ref[...],
            preferred_element_type=f32,
        )
        for k in range(cols):
            piece = prod[:, k * lanes : (k + 1) * lanes]
            turned = butterfly(
                [piece[a * residues : (a + 1) * residues] for a in range(4)], width
            )
            for il in range(res):
                block = turned[il].astype(bf16)
                for e in range(depths):
                    first = e * half + (k * res + il) * pair_cols
                    outer_ref[first : first + pair_cols, dh * lanes : (dh + 1) * lanes] = block[
                        e * pair_cols : (e + 1) * pair_cols
                    ]
    proj_out_ref[...] = jnp.dot(outer_ref[...], wturn_ref[...], preferred_element_type=f32)

    gain = gain_ref[...]
    chunk = 2 * per
    for at in range(pairs // chunk):
        rows = slice(at * chunk, (at + 1) * chunk)
        e, k = divmod(2 * at, cols)
        act, grad = [
            jnp.concatenate(
                [pgot_ref[e, k + b, at * per : (at + 1) * per, :] for b in range(2)], axis=0
            )
            for at in range(2)
        ]
        act = act.astype(f32)
        count = cnt_ref[rows, :]
        mid = act + proj_out_ref[rows, :] / count
        scaled, inv = norm_pieces(mid)
        normed = (scaled * gain).astype(bf16)
        pn_ref[rows, :] = normed
        pre = jnp.dot(normed, hid_ref[...], preferred_element_type=f32)
        value, slope = silu_pieces(pre)
        hidden_ref[rows, :] = value.astype(bf16)
        masked = grad * pm_ref[rows, :]
        mg_ref[rows, :] = masked
        back = lax.dot_general(
            masked, back_ref[...], (((1,), (1,)), ((), ())), preferred_element_type=f32
        )
        ghid = (back * slope).astype(bf16)
        gh_ref[rows, :] = ghid
        gsc = (
            lax.dot_general(
                ghid, hid_ref[...], (((1,), (1,)), ((), ())), preferred_element_type=f32
            )
            * gain
        )
        gmid = grad.astype(f32) + standardize_adjoint(gsc, scaled, inv)
        gmid_ref[rows, :] = gmid
        opm = (gmid / count).astype(bf16)
        opm_ref[rows, :] = opm
        gf_ref[rows, :] = opm.astype(f32)
    start = pl.multiple_of(me_depth * half + me_col * per, per)
    couple_ref[...] = gmid_ref[pl.ds(start, per), :].astype(bf16)

    for il in range(res):
        for e in range(depths):
            first = pl.multiple_of(e * half + (me_col * res + il) * pair_cols, pair_cols)
            grow_ref[il * residues + e * pair_cols : il * residues + (e + 1) * pair_cols, :] = (
                gf_ref[pl.ds(first, pair_cols), :].astype(bf16)
            )
    my_half = (me_col * res) // pair_cols
    my_first = me_col * res - my_half * pair_cols
    for jl in range(res):
        gcol_ref[jl * residues : (jl + 1) * residues, :] = gf_ref[
            pl.ds(my_half * half + my_first + jl, residues, stride=pair_cols), :
        ].astype(bf16)
    for lhs, weight, out in ((grow_ref, wturn_ref, gor_ref), (gcol_ref, wout_ref, goc_ref)):
        for dh in range(width // 4):
            piece = lax.dot_general(
                lhs[...],
                weight[dh * lanes : (dh + 1) * lanes, :],
                (((1,), (1,)), ((), ())),
                preferred_element_type=f32,
            )
            turned = butterfly(
                [piece[a * residues : (a + 1) * residues] for a in range(4)], width
            )
            for dl in range(4):
                first = (dh * 4 + dl) * residues
                out[first : first + residues, :] = turned[dl].astype(bf16)
    sums = [
        lax.dot_general(lhs[...], rhs[...], (((0,), (0,)), ((), ())), preferred_element_type=f32)
        for lhs, rhs in ((rightt_ref, gor_ref), (leftt_ref, goc_ref))
    ]
    mask_lanes = lanes_ref[...]
    upper = me_depth == 0
    sums = [
        (jnp.where(upper, total[:seqs], total[seqs:]) * mask_lanes).astype(bf16).astype(f32)
        for total in sums
    ]
    lane_group = lax.broadcasted_iota(jnp.int32, (seqs, lanes), 1) // width
    for r in range(res):
        for at in range(2):
            gs_ref[at, pl.ds(r, seqs, stride=res), :] = jnp.where(
                lane_group == r, sums[at], 0.0
            )
    spread = jnp.concatenate([gs_ref[0], gs_ref[1]], axis=1).astype(bf16)
    spread_ref[...] = spread
    cross = lax.dot_general(
        spread, normed_ref[...], (((0,), (0,)), ((), ())), preferred_element_type=f32
    )
    for at in range(2):
        total = cross[at * lanes : at * lanes + width]
        for r in range(1, res):
            total = total + cross[at * lanes + r * width : at * lanes + (r + 1) * width]
        part_ref[at * width : (at + 1) * width, :] = total.astype(bf16)


def out_weight_kernel(outer_ref, opm_ref, dout_ref, turn_ref):
    width = int(dout_ref.shape[0] ** 0.5 + 0.5)
    turn_ref[...] = lax.dot_general(
        outer_ref[...], opm_ref[...], (((0,), (0,)), ((), ())), preferred_element_type=jnp.float32
    )
    for c in range(width):
        dout_ref[c * width : (c + 1) * width, :] = turn_ref[pl.ds(c, width, stride=width), :]


def transition_weight_kernel(pn_ref, gh_ref, hidden_ref, mg_ref, dhid_ref, dback_ref):
    for lhs, rhs, out in ((pn_ref, gh_ref, dhid_ref), (hidden_ref, mg_ref, dback_ref)):
        out[...] = lax.dot_general(
            lhs[...], rhs[...], (((0,), (0,)), ((), ())), preferred_element_type=jnp.float32
        )


def feature_kernel(
    copies, spread_ref, first_ref, second_ref, scale_ref, scaled_ref, inv_ref, feat_ref
):
    back = jnp.dot(
        spread_ref[...],
        wide_projector(first_ref, second_ref, copies),
        preferred_element_type=jnp.float32,
    )
    feat_ref[...] = standardize_adjoint(
        back * scale_ref[...], scaled_ref[...], inv_ref[...]
    ).astype(jnp.bfloat16)


def swap_depth(block):
    return lax.ppermute(block, "depth", [(0, 1), (1, 0)])


def pairwise_sum(blocks):
    while len(blocks) > 1:
        blocks = [blocks[at] + blocks[at + 1] for at in range(0, len(blocks), 2)]
    return blocks[0]


def swap_col(block, partner):
    count = lax.axis_size("col")
    return lax.ppermute(block, "col", [(at, at ^ partner) for at in range(count)])


def gathered(block, rounds):
    order = [0]
    for partners in rounds:
        came = [swap_col(block, partner) for partner in partners]
        block = jnp.concatenate([block] + came)
        order = order + [at ^ partner for partner in partners for at in order]
    return block, tuple(order)


def whole_plan(
    alignment_activations,
    alignment_mask,
    pair_activation_input,
    pair_update_mask,
    pair_output_gradient,
    layer_scale_factor,
    first_projector,
    second_projector,
    output_weight,
    pair_norm_gain,
    hidden_weight,
    back_weight,
):
    seqs, res, channels = alignment_activations.shape
    width = first_projector.shape[1]
    outer_width = width * width
    cols = lax.axis_size("col")
    depths = lax.axis_size("depth")
    residues = res * cols
    pair_cols, pair_width = pair_activation_input.shape[1:]
    hid = hidden_weight.shape[1]
    per = res * pair_cols
    pairs = residues * residues
    lanes = res * width
    rows = 2 * seqs + MASK_ROWS
    f32, bf16 = jnp.float32, jnp.bfloat16
    ids = jnp.stack([lax.axis_index("depth"), lax.axis_index("col")]).astype(jnp.int32)
    smem = pl.BlockSpec(memory_space=pltpu.SMEM)
    vmem = pl.BlockSpec(memory_space=pltpu.VMEM)
    params = pltpu.CompilerParams(vmem_limit_bytes=40 * 2**20)
    scale = layer_scale_factor.reshape(1, channels)
    first, second = first_projector.T, second_projector.T
    wturn = jnp.transpose(output_weight.reshape(width, width, pair_width), (1, 0, 2)).reshape(
        outer_width, pair_width
    )
    shape = jax.ShapeDtypeStruct
    pair_arrays = jnp.concatenate(
        [
            pair_activation_input.reshape(1, per, pair_width),
            pair_output_gradient.reshape(1, per, pair_width),
        ],
        axis=1,
    )
    pmine, porder = gathered(pair_arrays, ((1,), (4,), (2,)))
    sent, normed, scaled, inv, mask_lanes = pl.pallas_call(
        pre_kernel,
        out_shape=(
            shape((1, rows, pair_width), bf16),
            shape((seqs * res, channels), bf16),
            shape((seqs * res, channels), f32),
            shape((seqs * res, 1), f32),
            shape((seqs, lanes), f32),
        ),
        in_specs=[smem] + [pl.BlockSpec(memory_space=pltpu.HBM)] * 6,
        out_specs=[vmem] * 5,
        scratch_shapes=[
            pltpu.VMEM((2, seqs * res, lanes), f32),
            pltpu.VMEM((MASK_ROWS, lanes), f32),
            pltpu.VMEM((seqs, res, channels), bf16),
            pltpu.VMEM((res, seqs), jnp.int32),
            pltpu.VMEM((res, pair_cols), jnp.int32),
            pltpu.VMEM((1, channels), f32),
            pltpu.VMEM((width, channels), bf16),
            pltpu.VMEM((width, channels), bf16),
            pltpu.SemaphoreType.DMA((6,)),
        ],
        compiler_params=params,
        name="project",
    )(
        ids,
        *[
            pltpu.with_memory_space_constraint(array, pltpu.HBM)
            for array in (
                alignment_activations,
                alignment_mask.T,
                pair_update_mask,
                scale,
                first,
                second,
            )
        ],
    )
    mine, order = gathered(sent, ((6, 4, 2), (1,)))
    other = swap_depth(mine)
    pother = swap_depth(pmine)
    couple, part, outer, opm, pn, gh, hidden, mg, spread = pl.pallas_call(
        functools.partial(main_kernel, (seqs, res, pair_cols, width), (order, porder)),
        out_shape=(
            shape((per, pair_width), bf16),
            shape((2 * width, channels), bf16),
            shape((pairs, outer_width), bf16),
            shape((pairs, pair_width), bf16),
            shape((pairs, pair_width), bf16),
            shape((pairs, hid), bf16),
            shape((pairs, hid), bf16),
            shape((pairs, pair_width), bf16),
            shape((seqs * res, 2 * lanes), bf16),
        ),
        in_specs=[smem] + [vmem] * 11,
        out_specs=[vmem] * 9,
        scratch_shapes=[
            pltpu.VMEM((depths, cols, rows, pair_width), bf16),
            pltpu.VMEM((depths, cols, 2 * per, pair_width), bf16),
            pltpu.VMEM((depths * seqs, residues * width), bf16),
            pltpu.VMEM((residues * width, depths * seqs), bf16),
            pltpu.VMEM((residues * width, depths * seqs), bf16),
            pltpu.VMEM((residues * width, depths * seqs), f32),
            pltpu.VMEM((residues, depths * seqs), f32),
            pltpu.VMEM((pairs, lanes), f32),
            pltpu.VMEM((pairs, lanes), bf16),
            pltpu.VMEM((pairs, lanes), bf16),
            pltpu.VMEM((pairs, lanes), bf16),
            pltpu.VMEM((pairs, pair_width), f32),
            pltpu.VMEM((pairs, pair_width), f32),
            pltpu.VMEM((pairs, pair_width), f32),
            pltpu.VMEM((res * residues, pair_width), bf16),
            pltpu.VMEM((res * residues, pair_width), bf16),
            pltpu.VMEM((residues * width, lanes), bf16),
            pltpu.VMEM((residues * width, lanes), bf16),
            pltpu.VMEM((2, seqs * res, lanes), f32),
        ],
        compiler_params=params,
        name="pair_work",
    )(
        ids,
        mine,
        other,
        pmine,
        pother,
        output_weight,
        wturn,
        pair_norm_gain.reshape(1, pair_width),
        hidden_weight,
        back_weight,
        normed,
        mask_lanes,
    )
    total = part.astype(f32)

    def add_partners(total, partners, beside):
        kept = lax.optimization_barrier(total.astype(bf16))
        came = [swap_col(kept, at) if at else swap_depth(kept) for at in partners]
        came, beside = lax.optimization_barrier((came, beside))
        return pairwise_sum([block.astype(f32) for block in [kept] + came]), beside

    feat = pl.pallas_call(
        functools.partial(feature_kernel, res),
        out_shape=shape((seqs * res, channels), bf16),
        in_specs=[vmem] * 6,
        out_specs=vmem,
        compiler_params=params,
        name="features",
    )(spread, first, second, scale, scaled, inv)
    total, feat = add_partners(total, (0,), feat)
    dout = pl.pallas_call(
        out_weight_kernel,
        out_shape=shape((outer_width, pair_width), f32),
        in_specs=[vmem] * 2,
        out_specs=vmem,
        scratch_shapes=[pltpu.VMEM((outer_width, pair_width), f32)],
        compiler_params=params,
        name="out_weight",
    )(outer, opm)
    total, dout = add_partners(total, (2, 4, 6), dout)
    dhid, dback = pl.pallas_call(
        transition_weight_kernel,
        out_shape=(shape((pair_width, hid), f32), shape((hid, pair_width), f32)),
        in_specs=[vmem] * 4,
        out_specs=[vmem] * 2,
        compiler_params=params,
        name="transition_weights",
    )(pn, gh, hidden, mg)
    total, (dhid, dback) = add_partners(total, (1,), (dhid, dback))
    return (
        feat.reshape(seqs, res, channels),
        couple.reshape(res, pair_cols, pair_width),
        total[:width].T,
        total[width:].T,
        dout,
        dhid,
        dback,
    )


def on_device(alignment_activations, *others):
    residues = alignment_activations.shape[1] * lax.axis_size("col")
    plan = whole_plan if residues <= FEW_RESIDUES else split_plan
    return plan(alignment_activations, *others)


def solution(mesh):
    in_specs = (
        P(("group", "depth"), "col", None),
        P(("group", "depth"), "col"),
        P(("group", "col"), "depth", None),
        P(("group", "col"), "depth"),
        P(("group", "col"), "depth", None),
        P(),
        P(),
        P(),
        P(),
        P(),
        P(),
        P(),
    )
    out_specs = (
        P(("group", "depth"), "col", None),
        P(("group", "col"), "depth", None),
        P("group", None),
        P("group", None),
        P("group", None),
        P("group", None),
        P("group", None),
    )
    return jax.shard_map(
        on_device, mesh=mesh, in_specs=in_specs, out_specs=out_specs, check_vma=False
    )
```

```python
import functools

import jax
import jax.numpy as jnp
from jax import lax
from jax.experimental import pallas as pl
from jax.experimental.pallas import tpu as pltpu
from jax.sharding import PartitionSpec as P

epsilon = 1e-05
highest = lax.Precision.HIGHEST


def norm_pieces(entries_drawn):
    center = entries_drawn - jnp.mean(entries_drawn, axis=-1, keepdims=True)
    inv_std = lax.rsqrt(jnp.mean(center * center, axis=-1, keepdims=True) + epsilon)
    return (center * inv_std, inv_std)


def standardize_adjoint(grad_scaled, scaled, inv_std):
    mean_grad = jnp.mean(grad_scaled, axis=-1, keepdims=True)
    mean_cross = jnp.mean(grad_scaled * scaled, axis=-1, keepdims=True)
    return inv_std * (grad_scaled - mean_grad - scaled * mean_cross)


def silu_pieces(pre_act):
    sigma = jax.nn.sigmoid(pre_act)
    return (pre_act * sigma, sigma * (1.0 + pre_act * (1.0 - sigma)))


def split_plan(
    alignment_activations,
    alignment_mask,
    pair_activation_input,
    pair_update_mask,
    pair_output_gradient,
    layer_scale_factor,
    first_projector,
    second_projector,
    output_weight,
    pair_norm_gain,
    hidden_weight,
    back_weight,
):
    sequence_row_block, residue_row_block, channel_total = alignment_activations.shape
    proj_width = first_projector.shape[1]
    outer_width = proj_width * proj_width
    depth_count = lax.axis_size("depth")
    residues = residue_row_block * lax.axis_size("col")
    pair_cols = pair_activation_input.shape[1]
    pair_width = pair_activation_input.shape[2]
    col_block = min(64, pair_cols)
    block_count = pair_cols // col_block
    standardized_features, reciprocal_spread = norm_pieces(
        alignment_activations.astype(jnp.float32)
    )
    normalized_rows = (standardized_features * layer_scale_factor).astype(jnp.bfloat16)
    mask_floating = alignment_mask.astype(jnp.float32)
    left_proj = (
        jnp.dot(normalized_rows, first_projector, preferred_element_type=jnp.float32)
        * mask_floating[:, :, None]
    ).astype(jnp.bfloat16)
    right_proj = (
        jnp.dot(normalized_rows, second_projector, preferred_element_type=jnp.float32)
        * mask_floating[:, :, None]
    ).astype(jnp.bfloat16)
    right_flat = right_proj.reshape(sequence_row_block, residue_row_block * proj_width)
    mask_converted = alignment_mask.astype(jnp.bfloat16)
    seq_total = left_proj.shape[0]
    gathered, gathered_mask = (
        lax.all_gather(right_flat, "col", axis=1, tiled=True),
        lax.all_gather(mask_converted, "col", axis=1, tiled=True),
    )
    right_blocks = gathered.reshape(seq_total, depth_count, pair_cols, proj_width)
    mask_blocks = gathered_mask.reshape(seq_total, depth_count, pair_cols)
    block_depth = right_blocks.shape[1]
    out_wide = output_weight.astype(jnp.float32)

    def partial_outer(col_start):
        right_piece = lax.dynamic_slice_in_dim(right_blocks, col_start, col_block, 2)
        outer_part = jnp.einsum(
            "sic,sejd->iejcd", left_proj, right_piece, preferred_element_type=jnp.float32
        )
        return (
            outer_part.reshape(residue_row_block, block_depth, col_block, outer_width),
            right_piece,
        )

    def forward_step(step_index, loop_state):
        projected, pair_count = loop_state
        col_start = step_index * col_block
        outer_part, right_piece = partial_outer(col_start)
        mask_piece = lax.dynamic_slice_in_dim(mask_blocks, col_start, col_block, 2).astype(
            jnp.float32
        )
        count_part = jnp.einsum("si,sej->iej", mask_floating, mask_piece, precision=highest)
        outer_mine, count_mine = (
            lax.psum_scatter(
                outer_part.astype(jnp.bfloat16), "depth", scatter_dimension=1, tiled=True
            ).astype(jnp.float32),
            lax.psum_scatter(
                count_part.astype(jnp.bfloat16), "depth", scatter_dimension=1, tiled=True
            ).astype(jnp.float32),
        )
        proj_mine = jnp.dot(
            outer_mine.reshape(residue_row_block * col_block, outer_width),
            out_wide,
            precision=highest,
        )
        proj_mine = proj_mine.reshape(residue_row_block, col_block, pair_width)
        count_mine = count_mine.reshape(residue_row_block, col_block)
        projected = lax.dynamic_update_slice_in_dim(projected, proj_mine, col_start, 1)
        pair_count = lax.dynamic_update_slice_in_dim(pair_count, count_mine, col_start, 1)
        return (projected, pair_count)

    projected, pair_count = lax.fori_loop(
        0,
        block_count,
        forward_step,
        (
            jnp.zeros((residue_row_block, pair_cols, pair_width), jnp.float32),
            jnp.zeros((residue_row_block, pair_cols), jnp.float32),
        ),
    )
    count_column = pair_count.reshape(residue_row_block * pair_cols, 1)
    mid_act = (
        pair_activation_input.reshape(residue_row_block * pair_cols, pair_width).astype(jnp.float32)
        + projected.reshape(residue_row_block * pair_cols, pair_width) / count_column
    )
    pair_scaled, pair_inv = norm_pieces(mid_act)
    pair_normed = (pair_scaled * pair_norm_gain).astype(jnp.bfloat16)
    pre_act = jnp.dot(pair_normed, hidden_weight, preferred_element_type=jnp.float32)
    act_value, act_slope = silu_pieces(pre_act)
    hidden = act_value.astype(jnp.bfloat16)
    masked_grad = (
        pair_output_gradient * pair_update_mask.astype(jnp.bfloat16)[:, :, None]
    ).reshape(residue_row_block * pair_cols, pair_width)
    final_matrix_derivative = jnp.dot(hidden.T, masked_grad, preferred_element_type=jnp.float32)
    back_prod = jnp.dot(masked_grad, back_weight.T, preferred_element_type=jnp.float32)
    grad_hidden = (back_prod * act_slope).astype(jnp.bfloat16)
    middle_matrix_derivative = jnp.dot(
        pair_normed.T, grad_hidden, preferred_element_type=jnp.float32
    )
    grad_scaled = (
        jnp.dot(grad_hidden, hidden_weight.T, preferred_element_type=jnp.float32) * pair_norm_gain
    )
    grad_mid = pair_output_gradient.reshape(residue_row_block * pair_cols, pair_width).astype(
        jnp.float32
    ) + standardize_adjoint(grad_scaled, pair_scaled, pair_inv)
    couple_features_derivative = grad_mid.astype(jnp.bfloat16).reshape(
        residue_row_block, pair_cols, pair_width
    )
    grad_opm = (
        (grad_mid / count_column)
        .astype(jnp.bfloat16)
        .reshape(residue_row_block, pair_cols, pair_width)
    )
    full_opm = lax.all_gather(grad_opm, "depth", axis=1, tiled=True).reshape(
        residue_row_block, depth_count, pair_cols, pair_width
    )

    def backward_step(step_index, loop_state):
        grad_left_acc, grad_out, right_term = loop_state
        col_start = step_index * col_block
        outer_part, right_piece = partial_outer(col_start)
        opm_piece = lax.dynamic_slice_in_dim(full_opm, col_start, col_block, 2).reshape(
            residue_row_block * block_depth * col_block, pair_width
        )
        grad_out = grad_out + jnp.dot(
            outer_part.reshape(residue_row_block * block_depth * col_block, outer_width).T,
            opm_piece.astype(jnp.float32),
            precision=highest,
        )
        grad_outer = jnp.dot(opm_piece, output_weight.T, preferred_element_type=jnp.float32).astype(
            jnp.bfloat16
        )
        grad_outer = grad_outer.reshape(
            residue_row_block, block_depth, col_block, proj_width, proj_width
        )
        grad_left_acc = grad_left_acc + jnp.einsum(
            "iejcd,sejd->sic", grad_outer, right_piece, preferred_element_type=jnp.float32
        )
        piece_term = jnp.einsum(
            "iejcd,sic->ejsd", grad_outer, left_proj, preferred_element_type=jnp.float32
        )
        piece_term = piece_term.reshape(block_depth, col_block, seq_total * proj_width)
        right_term = lax.dynamic_update_slice_in_dim(right_term, piece_term, col_start, 1)
        return (grad_left_acc, grad_out, right_term)

    grad_left_acc, result_matrix_derivative, right_term = lax.fori_loop(
        0,
        block_count,
        backward_step,
        (
            jnp.zeros((seq_total, residue_row_block, proj_width), jnp.float32),
            jnp.zeros((outer_width, pair_width), jnp.float32),
            jnp.zeros((block_depth, pair_cols, seq_total * proj_width), jnp.float32),
        ),
    )
    grad_right_sum = lax.psum_scatter(
        right_term.reshape(residues, seq_total * proj_width), "col", scatter_dimension=0, tiled=True
    )
    grad_right_acc = jnp.transpose(
        grad_right_sum.reshape(residue_row_block, seq_total, proj_width), (1, 0, 2)
    )
    grad_left = (grad_left_acc * mask_floating[:, :, None]).astype(jnp.bfloat16)
    grad_right = (grad_right_acc * mask_floating[:, :, None]).astype(jnp.bfloat16)
    normed_rows = normalized_rows.reshape(sequence_row_block * residue_row_block, channel_total)
    first_projector_derivative = jnp.dot(
        normed_rows.T,
        grad_left.reshape(sequence_row_block * residue_row_block, proj_width),
        preferred_element_type=jnp.float32,
    )
    second_projector_derivative = jnp.dot(
        normed_rows.T,
        grad_right.reshape(sequence_row_block * residue_row_block, proj_width),
        preferred_element_type=jnp.float32,
    )
    standardized_derivative = jnp.dot(
        grad_left, first_projector.T, preferred_element_type=jnp.float32
    ) + jnp.dot(grad_right, second_projector.T, preferred_element_type=jnp.float32)
    features_derivative = standardize_adjoint(
        standardized_derivative * layer_scale_factor, standardized_features, reciprocal_spread
    ).astype(jnp.bfloat16)
    weight_sums = lax.psum(
        (
            first_projector_derivative,
            second_projector_derivative,
            result_matrix_derivative,
            middle_matrix_derivative,
            final_matrix_derivative,
        ),
        ("depth", "col"),
    )
    return (
        features_derivative,
        couple_features_derivative,
        weight_sums[0],
        weight_sums[1],
        weight_sums[2],
        weight_sums[3],
        weight_sums[4],
    )


FEW_RESIDUES = 32
MASK_ROWS = 16
Z_PARTNERS = (2, 4, 6)
Y_PARTNER = 1


def butterfly(blocks, group):
    lane_group = lax.broadcasted_iota(jnp.int32, blocks[0].shape, 1) // group
    width = 4 * group
    for bit in (2, 1):
        low = (lane_group & bit) == 0
        swapped = list(blocks)
        for at in range(4):
            if at & bit:
                continue
            here, there = blocks[at], blocks[at | bit]
            moving = jnp.where(low, there, here)
            if bit == 2:
                moved = pltpu.roll(moving, 2 * group, 1)
            else:
                moved = jnp.where(
                    low, pltpu.roll(moving, width - group, 1), pltpu.roll(moving, group, 1)
                )
            swapped[at] = jnp.where(low, here, moved)
            swapped[at | bit] = jnp.where(low, moved, there)
        blocks = swapped
    return blocks


def wide_projector(first_ref, second_ref, copies):
    return jnp.concatenate([first_ref[...]] * copies + [second_ref[...]] * copies, axis=0)


def pre_kernel(
    ids_ref,
    x_hbm,
    maskt_hbm,
    pmask_hbm,
    scale_hbm,
    first_hbm,
    second_hbm,
    act_hbm,
    grad_hbm,
    sent_ref,
    normed_ref,
    scaled_ref,
    inv_ref,
    lanes_ref,
    wide_ref,
    tile_ref,
    x_ref,
    maskt_ref,
    pmask_ref,
    scale_ref,
    first_ref,
    second_ref,
    sems,
):
    res, seqs = maskt_ref.shape
    pairs = act_hbm.shape[0]
    first_pair = 2 * seqs + MASK_ROWS
    copies = [
        pltpu.make_async_copy(source, target, sems.at[at])
        for at, (source, target) in enumerate(
            (
                (x_hbm, x_ref),
                (maskt_hbm, maskt_ref),
                (pmask_hbm, pmask_ref),
                (scale_hbm, scale_ref),
                (first_hbm, first_ref),
                (second_hbm, second_ref),
                (act_hbm, sent_ref.at[0, pl.ds(first_pair, pairs), :]),
                (grad_hbm, sent_ref.at[0, pl.ds(first_pair + pairs, pairs), :]),
            )
        )
    ]
    for copy in copies:
        copy.start()
    for copy in copies:
        copy.wait()
    lanes = sent_ref.shape[2]
    group = lanes // res
    scaled, inv = norm_pieces(
        x_ref[...].astype(jnp.float32).reshape(seqs * res, x_ref.shape[2])
    )
    scaled_ref[...] = scaled
    inv_ref[...] = inv
    normed = (scaled * scale_ref[...]).astype(jnp.bfloat16)
    normed_ref[...] = normed
    wide = lax.dot_general(
        normed,
        wide_projector(first_ref, second_ref, res),
        (((1,), (1,)), ((), ())),
        preferred_element_type=jnp.float32,
    )
    for at in range(2):
        wide_ref[at] = wide[:, at * lanes : (at + 1) * lanes]
    tile_ref[...] = jnp.zeros(tile_ref.shape, jnp.float32)
    mask = maskt_ref[...].astype(jnp.float32)
    tile_ref[0:res, 0:seqs] = mask
    spread = (
        lax.broadcasted_iota(jnp.int32, (MASK_ROWS, lanes), 1) // group
        == lax.broadcasted_iota(jnp.int32, (MASK_ROWS, lanes), 0)
    ).astype(jnp.float32)
    mask_lanes = lax.dot_general(
        tile_ref[...], spread, (((0,), (0,)), ((), ())), preferred_element_type=jnp.float32
    )[:seqs]
    lanes_ref[...] = mask_lanes
    twice = jnp.concatenate([mask] * (lanes // seqs), axis=1)
    here = lax.broadcasted_iota(jnp.int32, (res, lanes), 1) // seqs == ids_ref[0]
    tile_ref[0:res, :] = jnp.where(here, twice, 0.0)
    tile_ref[res : 2 * res, 0 : pmask_ref.shape[1]] = pmask_ref[...].astype(jnp.float32)
    lane_group = lax.broadcasted_iota(jnp.int32, (seqs, lanes), 1) // group
    for at in range(2):
        both = wide_ref[at, pl.ds(0, seqs, stride=res), :]
        for r in range(1, res):
            both = jnp.where(
                lane_group == r, wide_ref[at, pl.ds(r, seqs, stride=res), :], both
            )
        sent_ref[0, at * seqs : (at + 1) * seqs, :] = (both * mask_lanes).astype(jnp.bfloat16)
    sent_ref[0, 2 * seqs : first_pair, :] = tile_ref[...].astype(jnp.bfloat16)


def outer_kernel(
    sizes,
    orders,
    ids_ref,
    near_ref,
    far_ref,
    other_near_ref,
    other_far_ref,
    wturn_ref,
    outer_ref,
    proj_out_ref,
    cnt_ref,
    pm_ref,
    rightt_ref,
    leftt_ref,
    got_ref,
    leftn_ref,
    mine_ref,
    turn_ref,
    maskt_ref,
    cntl_ref,
    pml_ref,
):
    seqs, res, pair_cols, width = sizes
    depths, cols = got_ref.shape[0], got_ref.shape[1]
    residues = cols * res
    lanes = res * width
    half_cols = pair_cols // res
    me_depth = ids_ref[0]
    me_col = ids_ref[1]
    f32, bf16 = jnp.float32, jnp.bfloat16

    for order, mine, other in zip(orders, (near_ref, far_ref), (other_near_ref, other_far_ref)):
        for at, partner in enumerate(order):
            got_ref[me_depth, me_col ^ partner] = mine[at]
            got_ref[1 - me_depth, me_col ^ partner] = other[at]

    for e in range(depths):
        for k in range(cols):
            leftn_ref[e * seqs : (e + 1) * seqs, k * lanes : (k + 1) * lanes] = got_ref[
                e, k, 0:seqs, :
            ]
    for at, out in ((0, leftt_ref), (1, rightt_ref)):
        for k in range(cols):
            block = got_ref[me_depth, k, at * seqs : (at + 1) * seqs, :].astype(f32)
            turn_ref[k * lanes : (k + 1) * lanes, 0:seqs] = block.T
        for d in range(width):
            out[d * residues : (d + 1) * residues, :] = turn_ref[
                pl.ds(d, residues, stride=width), :
            ].astype(bf16)
    for k in range(half_cols):
        block = jnp.concatenate(
            [
                got_ref[e, me_depth * half_cols + k, seqs : 2 * seqs, :]
                for e in range(depths)
            ],
            axis=0,
        ).astype(f32)
        turn_ref[k * lanes : (k + 1) * lanes, :] = block.T
    for d in range(width):
        mine_ref[d * pair_cols : (d + 1) * pair_cols, :] = turn_ref[
            pl.ds(d, pair_cols, stride=width), :
        ].astype(bf16)

    base = 2 * seqs
    pair_lane = lax.broadcasted_iota(jnp.int32, (pair_cols, lanes), 1)
    pair_row = lax.broadcasted_iota(jnp.int32, (pair_cols, lanes), 0)
    for k in range(cols):
        tiles = [got_ref[e, k, base : base + MASK_ROWS, :].astype(f32) for e in range(depths)]
        maskt_ref[k * res : (k + 1) * res, :] = tiles[0][0:res] + tiles[1][0:res]
        own = got_ref[me_depth, k, base : base + MASK_ROWS, :].astype(f32)
        for r in range(res):
            row = own[res + r : res + r + 1, :]
            first = (k * res + r) * pair_cols
            pml_ref[first : first + pair_cols, :] = jnp.where(
                pair_lane == pair_row, row, 0.0
            ).astype(bf16)
    maskt = maskt_ref[...]
    cols_mask = maskt_ref[pl.ds(pl.multiple_of(me_depth * pair_cols, pair_cols), pair_cols), :]
    for i in range(residues):
        cntl_ref[i * pair_cols : (i + 1) * pair_cols, :] = (maskt[i : i + 1, :] * cols_mask).astype(
            bf16
        )
    ones = jnp.ones((lanes, lanes), bf16)
    cnt_ref[...] = jnp.dot(cntl_ref[...], ones, preferred_element_type=f32)
    pm_ref[...] = jnp.dot(pml_ref[...], ones, preferred_element_type=f32).astype(bf16)

    for dh in range(width // 4):
        prod = jnp.dot(
            mine_ref[dh * 4 * pair_cols : (dh + 1) * 4 * pair_cols, :],
            leftn_ref[...],
            preferred_element_type=f32,
        )
        for k in range(cols):
            piece = prod[:, k * lanes : (k + 1) * lanes]
            turned = butterfly(
                [piece[a * pair_cols : (a + 1) * pair_cols] for a in range(4)], width
            )
            for il in range(res):
                first = (k * res + il) * pair_cols
                outer_ref[first : first + pair_cols, dh * lanes : (dh + 1) * lanes] = turned[
                    il
                ].astype(bf16)
    proj_out_ref[...] = jnp.dot(outer_ref[...], wturn_ref[...], preferred_element_type=f32)


def transition_kernel(
    sizes,
    orders,
    ids_ref,
    near_ref,
    far_ref,
    proj_out_ref,
    cnt_ref,
    pm_ref,
    gain_ref,
    hid_ref,
    back_ref,
    couple_ref,
    opm_ref,
    pn_ref,
    gh_ref,
    hidden_ref,
    mg_ref,
    pgot_ref,
    gmid_ref,
):
    seqs, res, pair_cols, width = sizes
    per = res * pair_cols
    cols = pgot_ref.shape[0]
    me_col = ids_ref[1]
    f32, bf16 = jnp.float32, jnp.bfloat16
    for order, mine in zip(orders, (near_ref, far_ref)):
        for at, partner in enumerate(order):
            pgot_ref[me_col ^ partner] = mine[at]
    gain = gain_ref[...]
    chunk = 2 * per
    for at in range(cols // 2):
        rows = slice(at * chunk, (at + 1) * chunk)
        act, grad = [
            jnp.concatenate(
                [pgot_ref[2 * at + b, w * per : (w + 1) * per, :] for b in range(2)], axis=0
            )
            for w in range(2)
        ]
        count = cnt_ref[rows, :]
        mid = act.astype(f32) + proj_out_ref[rows, :] / count
        scaled, inv = norm_pieces(mid)
        normed = (scaled * gain).astype(bf16)
        pn_ref[rows, :] = normed
        pre = jnp.dot(normed, hid_ref[...], preferred_element_type=f32)
        value, slope = silu_pieces(pre)
        hidden_ref[rows, :] = value.astype(bf16)
        masked = grad * pm_ref[rows, :]
        mg_ref[rows, :] = masked
        back = lax.dot_general(
            masked, back_ref[...], (((1,), (1,)), ((), ())), preferred_element_type=f32
        )
        ghid = (back * slope).astype(bf16)
        gh_ref[rows, :] = ghid
        gsc = (
            lax.dot_general(
                ghid, hid_ref[...], (((1,), (1,)), ((), ())), preferred_element_type=f32
            )
            * gain
        )
        gmid = grad.astype(f32) + standardize_adjoint(gsc, scaled, inv)
        gmid_ref[rows, :] = gmid
        opm_ref[rows, :] = (gmid / count).astype(bf16)
    couple_ref[...] = gmid_ref[pl.ds(pl.multiple_of(me_col * per, per), per), :].astype(bf16)


def projector_kernel(
    sizes,
    ids_ref,
    opm_ref,
    other_opm_ref,
    rightt_ref,
    leftt_ref,
    wout_ref,
    wturn_ref,
    normed_ref,
    lanes_ref,
    part_ref,
    spread_ref,
    gf_ref,
    grow_ref,
    gcol_ref,
    gor_ref,
    goc_ref,
    gs_ref,
):
    seqs, res, pair_cols, width = sizes
    depths, half = gf_ref.shape[0], gf_ref.shape[1]
    residues = half // pair_cols
    lanes = res * width
    me_depth = ids_ref[0]
    me_col = ids_ref[1]
    f32, bf16 = jnp.float32, jnp.bfloat16
    gf_ref[me_depth] = opm_ref[...].astype(f32)
    gf_ref[1 - me_depth] = other_opm_ref[...].astype(f32)

    for il in range(res):
        for e in range(depths):
            first = pl.multiple_of((me_col * res + il) * pair_cols, pair_cols)
            grow_ref[il * residues + e * pair_cols : il * residues + (e + 1) * pair_cols, :] = (
                gf_ref[e, pl.ds(first, pair_cols), :].astype(bf16)
            )
    my_half = (me_col * res) // pair_cols
    my_first = me_col * res - my_half * pair_cols
    for jl in range(res):
        gcol_ref[jl * residues : (jl + 1) * residues, :] = gf_ref[
            my_half, pl.ds(my_first + jl, residues, stride=pair_cols), :
        ].astype(bf16)
    for lhs, weight, out in ((grow_ref, wturn_ref, gor_ref), (gcol_ref, wout_ref, goc_ref)):
        for dh in range(width // 4):
            piece = lax.dot_general(
                lhs[...],
                weight[dh * lanes : (dh + 1) * lanes, :],
                (((1,), (1,)), ((), ())),
                preferred_element_type=f32,
            )
            turned = butterfly(
                [piece[a * residues : (a + 1) * residues] for a in range(4)], width
            )
            for dl in range(4):
                first = (dh * 4 + dl) * residues
                out[first : first + residues, :] = turned[dl].astype(bf16)
    mask_lanes = lanes_ref[...]
    lane_group = lax.broadcasted_iota(jnp.int32, (seqs, lanes), 1) // width
    for at, (lhs, rhs) in enumerate(((rightt_ref, gor_ref), (leftt_ref, goc_ref))):
        total = lax.dot_general(
            lhs[...], rhs[...], (((0,), (0,)), ((), ())), preferred_element_type=f32
        )[:seqs]
        total = (total * mask_lanes).astype(bf16).astype(f32)
        for r in range(res):
            gs_ref[at, pl.ds(r, seqs, stride=res), :] = jnp.where(lane_group == r, total, 0.0)
    spread = jnp.concatenate([gs_ref[0], gs_ref[1]], axis=1).astype(bf16)
    spread_ref[...] = spread
    cross = lax.dot_general(
        spread, normed_ref[...], (((0,), (0,)), ((), ())), preferred_element_type=f32
    )
    for at in range(2):
        total = cross[at * lanes : at * lanes + width]
        for r in range(1, res):
            total = total + cross[at * lanes + r * width : at * lanes + (r + 1) * width]
        part_ref[at * width : (at + 1) * width, :] = total.astype(bf16)


def out_weight_kernel(outer_ref, opm_ref, dout_ref, turn_ref):
    width = int(dout_ref.shape[0] ** 0.5 + 0.5)
    turn_ref[...] = lax.dot_general(
        outer_ref[...], opm_ref[...], (((0,), (0,)), ((), ())), preferred_element_type=jnp.float32
    )
    for c in range(width):
        dout_ref[c * width : (c + 1) * width, :] = turn_ref[
            pl.ds(c, width, stride=width), :
        ].astype(jnp.bfloat16)


def transition_weight_kernel(pn_ref, gh_ref, hidden_ref, mg_ref, dhid_ref, dback_ref):
    for lhs, rhs, out in ((pn_ref, gh_ref, dhid_ref), (hidden_ref, mg_ref, dback_ref)):
        out[...] = lax.dot_general(
            lhs[...], rhs[...], (((0,), (0,)), ((), ())), preferred_element_type=jnp.float32
        ).astype(jnp.bfloat16)


def feature_kernel(
    copies, spread_ref, first_ref, second_ref, scale_ref, scaled_ref, inv_ref, feat_ref
):
    back = jnp.dot(
        spread_ref[...],
        wide_projector(first_ref, second_ref, copies),
        preferred_element_type=jnp.float32,
    )
    feat_ref[...] = standardize_adjoint(
        back * scale_ref[...], scaled_ref[...], inv_ref[...]
    ).astype(jnp.bfloat16)


def swap_depth(block):
    return lax.ppermute(block, "depth", [(0, 1), (1, 0)])


def pairwise_sum(blocks):
    while len(blocks) > 1:
        blocks = [blocks[at] + blocks[at + 1] for at in range(0, len(blocks), 2)]
    return blocks[0]


def swap_col(block, partner):
    count = lax.axis_size("col")
    return lax.ppermute(block, "col", [(at, at ^ partner) for at in range(count)])


def whole_plan(
    alignment_activations,
    alignment_mask,
    pair_activation_input,
    pair_update_mask,
    pair_output_gradient,
    layer_scale_factor,
    first_projector,
    second_projector,
    output_weight,
    pair_norm_gain,
    hidden_weight,
    back_weight,
):
    seqs, res, channels = alignment_activations.shape
    width = first_projector.shape[1]
    outer_width = width * width
    cols = lax.axis_size("col")
    depths = lax.axis_size("depth")
    residues = res * cols
    pair_cols, pair_width = pair_activation_input.shape[1:]
    hid = hidden_weight.shape[1]
    per = res * pair_cols
    lanes = res * width
    near_rows = 2 * seqs + MASK_ROWS
    rows = near_rows + 2 * per
    half = residues * pair_cols
    f32, bf16 = jnp.float32, jnp.bfloat16
    ids = jnp.stack([lax.axis_index("depth"), lax.axis_index("col")]).astype(jnp.int32)
    smem = pl.BlockSpec(memory_space=pltpu.SMEM)
    vmem = pl.BlockSpec(memory_space=pltpu.VMEM)
    params = pltpu.CompilerParams(vmem_limit_bytes=40 * 2**20)
    scale = layer_scale_factor.reshape(1, channels)
    first, second = first_projector.T, second_projector.T
    wturn = jnp.transpose(output_weight.reshape(width, width, pair_width), (1, 0, 2)).reshape(
        outer_width, pair_width
    )
    shape = jax.ShapeDtypeStruct
    sent, normed, scaled, inv, mask_lanes = pl.pallas_call(
        pre_kernel,
        out_shape=(
            shape((1, rows, pair_width), bf16),
            shape((seqs * res, channels), bf16),
            shape((seqs * res, channels), f32),
            shape((seqs * res, 1), f32),
            shape((seqs, lanes), f32),
        ),
        in_specs=[smem] + [pl.BlockSpec(memory_space=pltpu.HBM)] * 8,
        out_specs=[vmem] * 5,
        scratch_shapes=[
            pltpu.VMEM((2, seqs * res, lanes), f32),
            pltpu.VMEM((MASK_ROWS, lanes), f32),
            pltpu.VMEM((seqs, res, channels), bf16),
            pltpu.VMEM((res, seqs), jnp.int32),
            pltpu.VMEM((res, pair_cols), jnp.int32),
            pltpu.VMEM((1, channels), f32),
            pltpu.VMEM((width, channels), bf16),
            pltpu.VMEM((width, channels), bf16),
            pltpu.SemaphoreType.DMA((8,)),
        ],
        compiler_params=params,
        name="project",
    )(
        ids,
        *[
            pltpu.with_memory_space_constraint(array, pltpu.HBM)
            for array in (
                alignment_activations,
                alignment_mask.T,
                pair_update_mask,
                scale,
                first,
                second,
                pair_activation_input.reshape(per, pair_width),
                pair_output_gradient.reshape(per, pair_width),
            )
        ],
    )
    near_order = (0,) + Z_PARTNERS
    far_order = tuple(at ^ Y_PARTNER for at in near_order)
    blocks = [sent] + [swap_col(sent, partner) for partner in Z_PARTNERS]
    near = jnp.concatenate([block[:, :near_rows] for block in blocks])
    pair_near = jnp.concatenate([block[:, near_rows:] for block in blocks])
    far = swap_col(near, Y_PARTNER)
    pair_far = swap_col(pair_near, Y_PARTNER)
    sizes = (seqs, res, pair_cols, width)
    orders = (near_order, far_order)
    outer, proj_out, cnt, pm, rightt, leftt = pl.pallas_call(
        functools.partial(outer_kernel, sizes, orders),
        out_shape=(
            shape((half, outer_width), bf16),
            shape((half, pair_width), f32),
            shape((half, lanes), f32),
            shape((half, lanes), bf16),
            shape((residues * width, depths * seqs), bf16),
            shape((residues * width, depths * seqs), bf16),
        ),
        in_specs=[smem] + [vmem] * 5,
        out_specs=[vmem] * 6,
        scratch_shapes=[
            pltpu.VMEM((depths, cols, near_rows, pair_width), bf16),
            pltpu.VMEM((depths * seqs, residues * width), bf16),
            pltpu.VMEM((pair_cols * width, depths * seqs), bf16),
            pltpu.VMEM((residues * width, depths * seqs), f32),
            pltpu.VMEM((residues, depths * seqs), f32),
            pltpu.VMEM((half, lanes), bf16),
            pltpu.VMEM((half, lanes), bf16),
        ],
        compiler_params=params,
        name="outer_products",
    )(ids, near, far, swap_depth(near), swap_depth(far), wturn)
    couple, opm, pn, gh, hidden, mg = pl.pallas_call(
        functools.partial(transition_kernel, sizes, orders),
        out_shape=(
            shape((per, pair_width), bf16),
            shape((half, pair_width), bf16),
            shape((half, pair_width), bf16),
            shape((half, hid), bf16),
            shape((half, hid), bf16),
            shape((half, pair_width), bf16),
        ),
        in_specs=[smem] + [vmem] * 8,
        out_specs=[vmem] * 6,
        scratch_shapes=[
            pltpu.VMEM((cols, 2 * per, pair_width), bf16),
            pltpu.VMEM((half, pair_width), f32),
        ],
        compiler_params=params,
        name="transition",
    )(
        ids,
        pair_near,
        pair_far,
        proj_out,
        cnt,
        pm,
        pair_norm_gain.reshape(1, pair_width),
        hidden_weight,
        back_weight,
    )
    dout = pl.pallas_call(
        out_weight_kernel,
        out_shape=shape((outer_width, pair_width), bf16),
        in_specs=[vmem] * 2,
        out_specs=vmem,
        scratch_shapes=[pltpu.VMEM((outer_width, pair_width), f32)],
        compiler_params=params,
        name="out_weight",
    )(outer, opm)
    other_opm, dout = lax.optimization_barrier((swap_depth(opm), dout))
    part, spread = pl.pallas_call(
        functools.partial(projector_kernel, sizes),
        out_shape=(
            shape((2 * width, channels), bf16),
            shape((seqs * res, 2 * lanes), bf16),
        ),
        in_specs=[smem] + [vmem] * 8,
        out_specs=[vmem] * 2,
        scratch_shapes=[
            pltpu.VMEM((depths, half, pair_width), f32),
            pltpu.VMEM((res * residues, pair_width), bf16),
            pltpu.VMEM((res * residues, pair_width), bf16),
            pltpu.VMEM((residues * width, lanes), bf16),
            pltpu.VMEM((residues * width, lanes), bf16),
            pltpu.VMEM((2, seqs * res, lanes), f32),
        ],
        compiler_params=params,
        name="projector_parts",
    )(ids, opm, other_opm, rightt, leftt, output_weight, wturn, normed, mask_lanes)
    feat = pl.pallas_call(
        functools.partial(feature_kernel, res),
        out_shape=shape((seqs * res, channels), bf16),
        in_specs=[vmem] * 6,
        out_specs=vmem,
        compiler_params=params,
        name="features",
    )(spread, first, second, scale, scaled, inv)
    dhid, dback = pl.pallas_call(
        transition_weight_kernel,
        out_shape=(shape((pair_width, hid), bf16), shape((hid, pair_width), bf16)),
        in_specs=[vmem] * 4,
        out_specs=[vmem] * 2,
        compiler_params=params,
        name="transition_weights",
    )(pn, gh, hidden, mg)
    total = part.astype(f32)
    for partners in ((0,), Z_PARTNERS, (Y_PARTNER,)):
        kept = lax.optimization_barrier(total.astype(bf16))
        came = [swap_col(kept, at) if at else swap_depth(kept) for at in partners]
        if partners == Z_PARTNERS:
            came, dhid, dback = lax.optimization_barrier((came, dhid, dback))
        total = pairwise_sum([block.astype(f32) for block in [kept] + came])
    dout, dhid, dback = [
        block.astype(f32) + swap_depth(block).astype(f32) for block in (dout, dhid, dback)
    ]
    return (
        feat.reshape(seqs, res, channels),
        couple.reshape(res, pair_cols, pair_width),
        total[:width].T,
        total[width:].T,
        dout,
        dhid,
        dback,
    )


def on_device(alignment_activations, *others):
    cols = lax.axis_size("col")
    residues = alignment_activations.shape[1] * cols
    plan = whole_plan if cols == 8 and residues <= FEW_RESIDUES else split_plan
    return plan(alignment_activations, *others)


def solution(mesh):
    in_specs = (
        P(("group", "depth"), "col", None),
        P(("group", "depth"), "col"),
        P(("group", "col"), "depth", None),
        P(("group", "col"), "depth"),
        P(("group", "col"), "depth", None),
        P(),
        P(),
        P(),
        P(),
        P(),
        P(),
        P(),
    )
    out_specs = (
        P(("group", "depth"), "col", None),
        P(("group", "col"), "depth", None),
        P("group", None),
        P("group", None),
        P("group", None),
        P("group", None),
        P("group", None),
    )
    return jax.shard_map(
        on_device, mesh=mesh, in_specs=in_specs, out_specs=out_specs, check_vma=False
    )
```

```python
import functools

import jax
import jax.numpy as jnp
from jax import lax
from jax.experimental import pallas as pl
from jax.experimental.pallas import tpu as pltpu
from jax.sharding import PartitionSpec as P

epsilon = 1e-05
highest = lax.Precision.HIGHEST


def norm_pieces(entries_drawn):
    center = entries_drawn - jnp.mean(entries_drawn, axis=-1, keepdims=True)
    inv_std = lax.rsqrt(jnp.mean(center * center, axis=-1, keepdims=True) + epsilon)
    return (center * inv_std, inv_std)


def standardize_adjoint(grad_scaled, scaled, inv_std):
    mean_grad = jnp.mean(grad_scaled, axis=-1, keepdims=True)
    mean_cross = jnp.mean(grad_scaled * scaled, axis=-1, keepdims=True)
    return inv_std * (grad_scaled - mean_grad - scaled * mean_cross)


def silu_pieces(pre_act):
    sigma = jax.nn.sigmoid(pre_act)
    return (pre_act * sigma, sigma * (1.0 + pre_act * (1.0 - sigma)))


def split_plan(
    alignment_activations,
    alignment_mask,
    pair_activation_input,
    pair_update_mask,
    pair_output_gradient,
    layer_scale_factor,
    first_projector,
    second_projector,
    output_weight,
    pair_norm_gain,
    hidden_weight,
    back_weight,
):
    sequence_row_block, residue_row_block, channel_total = alignment_activations.shape
    proj_width = first_projector.shape[1]
    outer_width = proj_width * proj_width
    depth_count = lax.axis_size("depth")
    residues = residue_row_block * lax.axis_size("col")
    pair_cols = pair_activation_input.shape[1]
    pair_width = pair_activation_input.shape[2]
    col_block = min(64, pair_cols)
    block_count = pair_cols // col_block
    standardized_features, reciprocal_spread = norm_pieces(
        alignment_activations.astype(jnp.float32)
    )
    normalized_rows = (standardized_features * layer_scale_factor).astype(jnp.bfloat16)
    mask_floating = alignment_mask.astype(jnp.float32)
    left_proj = (
        jnp.dot(normalized_rows, first_projector, preferred_element_type=jnp.float32)
        * mask_floating[:, :, None]
    ).astype(jnp.bfloat16)
    right_proj = (
        jnp.dot(normalized_rows, second_projector, preferred_element_type=jnp.float32)
        * mask_floating[:, :, None]
    ).astype(jnp.bfloat16)
    right_flat = right_proj.reshape(sequence_row_block, residue_row_block * proj_width)
    mask_converted = alignment_mask.astype(jnp.bfloat16)
    seq_total = left_proj.shape[0]
    gathered, gathered_mask = (
        lax.all_gather(right_flat, "col", axis=1, tiled=True),
        lax.all_gather(mask_converted, "col", axis=1, tiled=True),
    )
    right_blocks = gathered.reshape(seq_total, depth_count, pair_cols, proj_width)
    mask_blocks = gathered_mask.reshape(seq_total, depth_count, pair_cols)
    block_depth = right_blocks.shape[1]
    out_wide = output_weight.astype(jnp.float32)

    def partial_outer(col_start):
        right_piece = lax.dynamic_slice_in_dim(right_blocks, col_start, col_block, 2)
        outer_part = jnp.einsum(
            "sic,sejd->iejcd", left_proj, right_piece, preferred_element_type=jnp.float32
        )
        return (
            outer_part.reshape(residue_row_block, block_depth, col_block, outer_width),
            right_piece,
        )

    def forward_step(step_index, loop_state):
        projected, pair_count = loop_state
        col_start = step_index * col_block
        outer_part, right_piece = partial_outer(col_start)
        mask_piece = lax.dynamic_slice_in_dim(mask_blocks, col_start, col_block, 2).astype(
            jnp.float32
        )
        count_part = jnp.einsum("si,sej->iej", mask_floating, mask_piece, precision=highest)
        outer_mine, count_mine = (
            lax.psum_scatter(
                outer_part.astype(jnp.bfloat16), "depth", scatter_dimension=1, tiled=True
            ).astype(jnp.float32),
            lax.psum_scatter(
                count_part.astype(jnp.bfloat16), "depth", scatter_dimension=1, tiled=True
            ).astype(jnp.float32),
        )
        proj_mine = jnp.dot(
            outer_mine.reshape(residue_row_block * col_block, outer_width),
            out_wide,
            precision=highest,
        )
        proj_mine = proj_mine.reshape(residue_row_block, col_block, pair_width)
        count_mine = count_mine.reshape(residue_row_block, col_block)
        projected = lax.dynamic_update_slice_in_dim(projected, proj_mine, col_start, 1)
        pair_count = lax.dynamic_update_slice_in_dim(pair_count, count_mine, col_start, 1)
        return (projected, pair_count)

    projected, pair_count = lax.fori_loop(
        0,
        block_count,
        forward_step,
        (
            jnp.zeros((residue_row_block, pair_cols, pair_width), jnp.float32),
            jnp.zeros((residue_row_block, pair_cols), jnp.float32),
        ),
    )
    count_column = pair_count.reshape(residue_row_block * pair_cols, 1)
    mid_act = (
        pair_activation_input.reshape(residue_row_block * pair_cols, pair_width).astype(jnp.float32)
        + projected.reshape(residue_row_block * pair_cols, pair_width) / count_column
    )
    pair_scaled, pair_inv = norm_pieces(mid_act)
    pair_normed = (pair_scaled * pair_norm_gain).astype(jnp.bfloat16)
    pre_act = jnp.dot(pair_normed, hidden_weight, preferred_element_type=jnp.float32)
    act_value, act_slope = silu_pieces(pre_act)
    hidden = act_value.astype(jnp.bfloat16)
    masked_grad = (
        pair_output_gradient * pair_update_mask.astype(jnp.bfloat16)[:, :, None]
    ).reshape(residue_row_block * pair_cols, pair_width)
    final_matrix_derivative = jnp.dot(hidden.T, masked_grad, preferred_element_type=jnp.float32)
    back_prod = jnp.dot(masked_grad, back_weight.T, preferred_element_type=jnp.float32)
    grad_hidden = (back_prod * act_slope).astype(jnp.bfloat16)
    middle_matrix_derivative = jnp.dot(
        pair_normed.T, grad_hidden, preferred_element_type=jnp.float32
    )
    grad_scaled = (
        jnp.dot(grad_hidden, hidden_weight.T, preferred_element_type=jnp.float32) * pair_norm_gain
    )
    grad_mid = pair_output_gradient.reshape(residue_row_block * pair_cols, pair_width).astype(
        jnp.float32
    ) + standardize_adjoint(grad_scaled, pair_scaled, pair_inv)
    couple_features_derivative = grad_mid.astype(jnp.bfloat16).reshape(
        residue_row_block, pair_cols, pair_width
    )
    grad_opm = (
        (grad_mid / count_column)
        .astype(jnp.bfloat16)
        .reshape(residue_row_block, pair_cols, pair_width)
    )
    full_opm = lax.all_gather(grad_opm, "depth", axis=1, tiled=True).reshape(
        residue_row_block, depth_count, pair_cols, pair_width
    )

    def backward_step(step_index, loop_state):
        grad_left_acc, grad_out, right_term = loop_state
        col_start = step_index * col_block
        outer_part, right_piece = partial_outer(col_start)
        opm_piece = lax.dynamic_slice_in_dim(full_opm, col_start, col_block, 2).reshape(
            residue_row_block * block_depth * col_block, pair_width
        )
        grad_out = grad_out + jnp.dot(
            outer_part.reshape(residue_row_block * block_depth * col_block, outer_width).T,
            opm_piece.astype(jnp.float32),
            precision=highest,
        )
        grad_outer = jnp.dot(opm_piece, output_weight.T, preferred_element_type=jnp.float32).astype(
            jnp.bfloat16
        )
        grad_outer = grad_outer.reshape(
            residue_row_block, block_depth, col_block, proj_width, proj_width
        )
        grad_left_acc = grad_left_acc + jnp.einsum(
            "iejcd,sejd->sic", grad_outer, right_piece, preferred_element_type=jnp.float32
        )
        piece_term = jnp.einsum(
            "iejcd,sic->ejsd", grad_outer, left_proj, preferred_element_type=jnp.float32
        )
        piece_term = piece_term.reshape(block_depth, col_block, seq_total * proj_width)
        right_term = lax.dynamic_update_slice_in_dim(right_term, piece_term, col_start, 1)
        return (grad_left_acc, grad_out, right_term)

    grad_left_acc, result_matrix_derivative, right_term = lax.fori_loop(
        0,
        block_count,
        backward_step,
        (
            jnp.zeros((seq_total, residue_row_block, proj_width), jnp.float32),
            jnp.zeros((outer_width, pair_width), jnp.float32),
            jnp.zeros((block_depth, pair_cols, seq_total * proj_width), jnp.float32),
        ),
    )
    grad_right_sum = lax.psum_scatter(
        right_term.reshape(residues, seq_total * proj_width), "col", scatter_dimension=0, tiled=True
    )
    grad_right_acc = jnp.transpose(
        grad_right_sum.reshape(residue_row_block, seq_total, proj_width), (1, 0, 2)
    )
    grad_left = (grad_left_acc * mask_floating[:, :, None]).astype(jnp.bfloat16)
    grad_right = (grad_right_acc * mask_floating[:, :, None]).astype(jnp.bfloat16)
    normed_rows = normalized_rows.reshape(sequence_row_block * residue_row_block, channel_total)
    first_projector_derivative = jnp.dot(
        normed_rows.T,
        grad_left.reshape(sequence_row_block * residue_row_block, proj_width),
        preferred_element_type=jnp.float32,
    )
    second_projector_derivative = jnp.dot(
        normed_rows.T,
        grad_right.reshape(sequence_row_block * residue_row_block, proj_width),
        preferred_element_type=jnp.float32,
    )
    standardized_derivative = jnp.dot(
        grad_left, first_projector.T, preferred_element_type=jnp.float32
    ) + jnp.dot(grad_right, second_projector.T, preferred_element_type=jnp.float32)
    features_derivative = standardize_adjoint(
        standardized_derivative * layer_scale_factor, standardized_features, reciprocal_spread
    ).astype(jnp.bfloat16)
    weight_sums = lax.psum(
        (
            first_projector_derivative,
            second_projector_derivative,
            result_matrix_derivative,
            middle_matrix_derivative,
            final_matrix_derivative,
        ),
        ("depth", "col"),
    )
    return (
        features_derivative,
        couple_features_derivative,
        weight_sums[0],
        weight_sums[1],
        weight_sums[2],
        weight_sums[3],
        weight_sums[4],
    )


FEW_RESIDUES = 32
MASK_ROWS = 16
Z_PARTNERS = (2, 4, 6)
Y_PARTNER = 1


def butterfly(blocks, group):
    lane_group = lax.broadcasted_iota(jnp.int32, blocks[0].shape, 1) // group
    width = 4 * group
    for bit in (2, 1):
        low = (lane_group & bit) == 0
        swapped = list(blocks)
        for at in range(4):
            if at & bit:
                continue
            here, there = blocks[at], blocks[at | bit]
            moving = jnp.where(low, there, here)
            if bit == 2:
                moved = pltpu.roll(moving, 2 * group, 1)
            else:
                moved = jnp.where(
                    low, pltpu.roll(moving, width - group, 1), pltpu.roll(moving, group, 1)
                )
            swapped[at] = jnp.where(low, here, moved)
            swapped[at | bit] = jnp.where(low, moved, there)
        blocks = swapped
    return blocks


def wide_projector(first_ref, second_ref, copies):
    return jnp.concatenate([first_ref[...]] * copies + [second_ref[...]] * copies, axis=0)


def pre_kernel(
    ids_ref,
    x_hbm,
    maskt_hbm,
    pmask_hbm,
    scale_hbm,
    first_hbm,
    second_hbm,
    gain_hbm,
    act_hbm,
    grad_hbm,
    sent_ref,
    pairs_ref,
    scale_ref,
    first_ref,
    second_ref,
    gain_ref,
    normed_ref,
    scaled_ref,
    inv_ref,
    lanes_ref,
    wide_ref,
    tile_ref,
    x_ref,
    maskt_ref,
    pmask_ref,
    sems,
):
    res, seqs = maskt_ref.shape
    pairs = act_hbm.shape[0]
    copies = [
        pltpu.make_async_copy(source, target, sems.at[at])
        for at, (source, target) in enumerate(
            (
                (x_hbm, x_ref),
                (maskt_hbm, maskt_ref),
                (pmask_hbm, pmask_ref),
                (scale_hbm, scale_ref),
                (first_hbm, first_ref),
                (second_hbm, second_ref),
                (gain_hbm, gain_ref),
                (act_hbm, pairs_ref.at[0, pl.ds(0, pairs), :]),
                (grad_hbm, pairs_ref.at[0, pl.ds(pairs, pairs), :]),
            )
        )
    ]
    for copy in copies:
        copy.start()
    for copy in copies:
        copy.wait()
    lanes = sent_ref.shape[2]
    group = lanes // res
    scaled, inv = norm_pieces(
        x_ref[...].astype(jnp.float32).reshape(seqs * res, x_ref.shape[2])
    )
    scaled_ref[...] = scaled
    inv_ref[...] = inv
    normed = (scaled * scale_ref[...]).astype(jnp.bfloat16)
    normed_ref[...] = normed
    wide = lax.dot_general(
        normed,
        wide_projector(first_ref, second_ref, res),
        (((1,), (1,)), ((), ())),
        preferred_element_type=jnp.float32,
    )
    for at in range(2):
        wide_ref[at] = wide[:, at * lanes : (at + 1) * lanes]
    tile_ref[...] = jnp.zeros(tile_ref.shape, jnp.float32)
    mask = maskt_ref[...].astype(jnp.float32)
    tile_ref[0:res, 0:seqs] = mask
    spread = (
        lax.broadcasted_iota(jnp.int32, (MASK_ROWS, lanes), 1) // group
        == lax.broadcasted_iota(jnp.int32, (MASK_ROWS, lanes), 0)
    ).astype(jnp.float32)
    mask_lanes = lax.dot_general(
        tile_ref[...], spread, (((0,), (0,)), ((), ())), preferred_element_type=jnp.float32
    )[:seqs]
    lanes_ref[...] = mask_lanes
    twice = jnp.concatenate([mask] * (lanes // seqs), axis=1)
    here = lax.broadcasted_iota(jnp.int32, (res, lanes), 1) // seqs == ids_ref[0]
    tile_ref[0:res, :] = jnp.where(here, twice, 0.0)
    tile_ref[res : 2 * res, 0 : pmask_ref.shape[1]] = pmask_ref[...].astype(jnp.float32)
    lane_group = lax.broadcasted_iota(jnp.int32, (seqs, lanes), 1) // group
    for at in range(2):
        both = wide_ref[at, pl.ds(0, seqs, stride=res), :]
        for r in range(1, res):
            both = jnp.where(
                lane_group == r, wide_ref[at, pl.ds(r, seqs, stride=res), :], both
            )
        sent_ref[0, at * seqs : (at + 1) * seqs, :] = (both * mask_lanes).astype(jnp.bfloat16)
    sent_ref[0, 2 * seqs :, :] = tile_ref[...].astype(jnp.bfloat16)


def outer_kernel(
    sizes,
    orders,
    ids_ref,
    near_ref,
    far_ref,
    other_near_ref,
    other_far_ref,
    wturn_ref,
    outer_ref,
    proj_out_ref,
    cnt_ref,
    pm_ref,
    got_ref,
    leftn_ref,
    mine_ref,
    turn_ref,
    maskt_ref,
    cntl_ref,
    pml_ref,
):
    seqs, res, pair_cols, width = sizes
    depths, cols = got_ref.shape[0], got_ref.shape[1]
    residues = cols * res
    lanes = res * width
    half_cols = pair_cols // res
    me_depth = ids_ref[0]
    me_col = ids_ref[1]
    f32, bf16 = jnp.float32, jnp.bfloat16

    for order, mine, other in zip(orders, (near_ref, far_ref), (other_near_ref, other_far_ref)):
        for at, partner in enumerate(order):
            got_ref[me_depth, me_col ^ partner] = mine[at]
            got_ref[1 - me_depth, me_col ^ partner] = other[at]

    for e in range(depths):
        for k in range(cols):
            leftn_ref[e * seqs : (e + 1) * seqs, k * lanes : (k + 1) * lanes] = got_ref[
                e, k, 0:seqs, :
            ]
    for k in range(half_cols):
        block = jnp.concatenate(
            [
                got_ref[e, me_depth * half_cols + k, seqs : 2 * seqs, :]
                for e in range(depths)
            ],
            axis=0,
        ).astype(f32)
        turn_ref[k * lanes : (k + 1) * lanes, :] = block.T
    for d in range(width):
        mine_ref[d * pair_cols : (d + 1) * pair_cols, :] = turn_ref[
            pl.ds(d, pair_cols, stride=width), :
        ].astype(bf16)

    base = 2 * seqs
    pair_lane = lax.broadcasted_iota(jnp.int32, (pair_cols, lanes), 1)
    pair_row = lax.broadcasted_iota(jnp.int32, (pair_cols, lanes), 0)
    for k in range(cols):
        tiles = [got_ref[e, k, base : base + MASK_ROWS, :].astype(f32) for e in range(depths)]
        maskt_ref[k * res : (k + 1) * res, :] = tiles[0][0:res] + tiles[1][0:res]
        own = got_ref[me_depth, k, base : base + MASK_ROWS, :].astype(f32)
        for r in range(res):
            row = own[res + r : res + r + 1, :]
            first = (k * res + r) * pair_cols
            pml_ref[first : first + pair_cols, :] = jnp.where(
                pair_lane == pair_row, row, 0.0
            ).astype(bf16)
    maskt = maskt_ref[...]
    cols_mask = maskt_ref[pl.ds(pl.multiple_of(me_depth * pair_cols, pair_cols), pair_cols), :]
    for i in range(residues):
        cntl_ref[i * pair_cols : (i + 1) * pair_cols, :] = (maskt[i : i + 1, :] * cols_mask).astype(
            bf16
        )
    ones = jnp.ones((lanes, lanes), bf16)
    cnt_ref[...] = jnp.dot(cntl_ref[...], ones, preferred_element_type=f32)
    pm_ref[...] = jnp.dot(pml_ref[...], ones, preferred_element_type=f32).astype(bf16)

    for dh in range(width // 4):
        prod = jnp.dot(
            mine_ref[dh * 4 * pair_cols : (dh + 1) * 4 * pair_cols, :],
            leftn_ref[...],
            preferred_element_type=f32,
        )
        for k in range(cols):
            piece = prod[:, k * lanes : (k + 1) * lanes]
            turned = butterfly(
                [piece[a * pair_cols : (a + 1) * pair_cols] for a in range(4)], width
            )
            for il in range(res):
                first = (k * res + il) * pair_cols
                outer_ref[first : first + pair_cols, dh * lanes : (dh + 1) * lanes] = turned[
                    il
                ].astype(bf16)
    proj_out_ref[...] = jnp.dot(outer_ref[...], wturn_ref[...], preferred_element_type=f32)


def turn_kernel(sizes, orders, ids_ref, near_ref, far_ref, rightt_ref, leftt_ref, turn_ref):
    seqs, res, _, width = sizes
    lanes = res * width
    residues = turn_ref.shape[0] // width
    me_col = ids_ref[1]
    for at, out in ((0, leftt_ref), (1, rightt_ref)):
        for order, blocks in zip(orders, (near_ref, far_ref)):
            for place, partner in enumerate(order):
                block = blocks[place, at * seqs : (at + 1) * seqs, :].astype(jnp.float32)
                block = jnp.concatenate([block] * (lanes // seqs), axis=0)
                first = pl.multiple_of((me_col ^ partner) * lanes, lanes)
                turn_ref[pl.ds(first, lanes), :] = block.T
        for d in range(width):
            out[d * residues : (d + 1) * residues, :] = turn_ref[
                pl.ds(d, residues, stride=width), :
            ].astype(jnp.bfloat16)


def transition_kernel(
    sizes,
    orders,
    ids_ref,
    near_ref,
    far_ref,
    proj_out_ref,
    cnt_ref,
    pm_ref,
    gain_ref,
    hid_ref,
    back_ref,
    couple_ref,
    opm_ref,
    pn_ref,
    gh_ref,
    hidden_ref,
    mg_ref,
    pgot_ref,
    gmid_ref,
):
    seqs, res, pair_cols, width = sizes
    per = res * pair_cols
    cols = pgot_ref.shape[0]
    me_col = ids_ref[1]
    f32, bf16 = jnp.float32, jnp.bfloat16
    for order, mine in zip(orders, (near_ref, far_ref)):
        for at, partner in enumerate(order):
            pgot_ref[me_col ^ partner] = mine[at]
    gain = gain_ref[...]
    chunk = 2 * per
    for at in range(cols // 2):
        rows = slice(at * chunk, (at + 1) * chunk)
        act, grad = [
            jnp.concatenate(
                [pgot_ref[2 * at + b, w * per : (w + 1) * per, :] for b in range(2)], axis=0
            )
            for w in range(2)
        ]
        count = cnt_ref[rows, :]
        mid = act.astype(f32) + proj_out_ref[rows, :] / count
        scaled, inv = norm_pieces(mid)
        normed = (scaled * gain).astype(bf16)
        pn_ref[rows, :] = normed
        pre = jnp.dot(normed, hid_ref[...], preferred_element_type=f32)
        value, slope = silu_pieces(pre)
        hidden_ref[rows, :] = value.astype(bf16)
        masked = grad * pm_ref[rows, :]
        mg_ref[rows, :] = masked
        back = lax.dot_general(
            masked, back_ref[...], (((1,), (1,)), ((), ())), preferred_element_type=f32
        )
        ghid = (back * slope).astype(bf16)
        gh_ref[rows, :] = ghid
        gsc = (
            lax.dot_general(
                ghid, hid_ref[...], (((1,), (1,)), ((), ())), preferred_element_type=f32
            )
            * gain
        )
        gmid = grad.astype(f32) + standardize_adjoint(gsc, scaled, inv)
        gmid_ref[rows, :] = gmid
        opm_ref[rows, :] = (gmid / count).astype(bf16)
    couple_ref[...] = gmid_ref[pl.ds(pl.multiple_of(me_col * per, per), per), :].astype(bf16)


def projector_kernel(
    sizes,
    ids_ref,
    opm_ref,
    other_opm_ref,
    rightt_ref,
    leftt_ref,
    wout_ref,
    wturn_ref,
    normed_ref,
    lanes_ref,
    part_ref,
    spread_ref,
    gf_ref,
    grow_ref,
    gcol_ref,
    gor_ref,
    goc_ref,
    gs_ref,
):
    seqs, res, pair_cols, width = sizes
    depths, half = gf_ref.shape[0], gf_ref.shape[1]
    residues = half // pair_cols
    lanes = res * width
    me_depth = ids_ref[0]
    me_col = ids_ref[1]
    f32, bf16 = jnp.float32, jnp.bfloat16
    gf_ref[me_depth] = opm_ref[...].astype(f32)
    gf_ref[1 - me_depth] = other_opm_ref[...].astype(f32)

    for il in range(res):
        for e in range(depths):
            first = pl.multiple_of((me_col * res + il) * pair_cols, pair_cols)
            grow_ref[il * residues + e * pair_cols : il * residues + (e + 1) * pair_cols, :] = (
                gf_ref[e, pl.ds(first, pair_cols), :].astype(bf16)
            )
    my_half = (me_col * res) // pair_cols
    my_first = me_col * res - my_half * pair_cols
    for jl in range(res):
        gcol_ref[jl * residues : (jl + 1) * residues, :] = gf_ref[
            my_half, pl.ds(my_first + jl, residues, stride=pair_cols), :
        ].astype(bf16)
    for lhs, weight, out in ((grow_ref, wturn_ref, gor_ref), (gcol_ref, wout_ref, goc_ref)):
        for dh in range(width // 4):
            piece = lax.dot_general(
                lhs[...],
                weight[dh * lanes : (dh + 1) * lanes, :],
                (((1,), (1,)), ((), ())),
                preferred_element_type=f32,
            )
            turned = butterfly(
                [piece[a * residues : (a + 1) * residues] for a in range(4)], width
            )
            for dl in range(4):
                first = (dh * 4 + dl) * residues
                out[first : first + residues, :] = turned[dl].astype(bf16)
    mask_lanes = lanes_ref[...]
    lane_group = lax.broadcasted_iota(jnp.int32, (seqs, lanes), 1) // width
    for at, (lhs, rhs) in enumerate(((rightt_ref, gor_ref), (leftt_ref, goc_ref))):
        total = lax.dot_general(
            lhs[...], rhs[...], (((0,), (0,)), ((), ())), preferred_element_type=f32
        )[:seqs]
        total = (total * mask_lanes).astype(bf16).astype(f32)
        for r in range(res):
            gs_ref[at, pl.ds(r, seqs, stride=res), :] = jnp.where(lane_group == r, total, 0.0)
    spread = jnp.concatenate([gs_ref[0], gs_ref[1]], axis=1).astype(bf16)
    spread_ref[...] = spread
    cross = lax.dot_general(
        spread, normed_ref[...], (((0,), (0,)), ((), ())), preferred_element_type=f32
    )
    for at in range(2):
        total = cross[at * lanes : at * lanes + width]
        for r in range(1, res):
            total = total + cross[at * lanes + r * width : at * lanes + (r + 1) * width]
        part_ref[at * width : (at + 1) * width, :] = total.astype(bf16)


def out_weight_kernel(outer_ref, opm_ref, dout_ref, turn_ref):
    width = int(dout_ref.shape[0] ** 0.5 + 0.5)
    turn_ref[...] = lax.dot_general(
        outer_ref[...], opm_ref[...], (((0,), (0,)), ((), ())), preferred_element_type=jnp.float32
    )
    for c in range(width):
        dout_ref[c * width : (c + 1) * width, :] = turn_ref[
            pl.ds(c, width, stride=width), :
        ].astype(jnp.bfloat16)


def transition_weight_kernel(pn_ref, gh_ref, hidden_ref, mg_ref, dhid_ref, dback_ref):
    for lhs, rhs, out in ((pn_ref, gh_ref, dhid_ref), (hidden_ref, mg_ref, dback_ref)):
        out[...] = lax.dot_general(
            lhs[...], rhs[...], (((0,), (0,)), ((), ())), preferred_element_type=jnp.float32
        ).astype(jnp.bfloat16)


def sum_kernel(*refs):
    for mine, other, out in zip(refs[0:3], refs[3:6], refs[6:9]):
        out[...] = mine[...].astype(jnp.float32) + other[...].astype(jnp.float32)


def feature_kernel(
    copies, spread_ref, first_ref, second_ref, scale_ref, scaled_ref, inv_ref, feat_ref
):
    back = jnp.dot(
        spread_ref[...],
        wide_projector(first_ref, second_ref, copies),
        preferred_element_type=jnp.float32,
    )
    feat_ref[...] = standardize_adjoint(
        back * scale_ref[...], scaled_ref[...], inv_ref[...]
    ).astype(jnp.bfloat16)


def swap_depth(block):
    return lax.ppermute(block, "depth", [(0, 1), (1, 0)])


def pairwise_sum(blocks):
    while len(blocks) > 1:
        blocks = [blocks[at] + blocks[at + 1] for at in range(0, len(blocks), 2)]
    return blocks[0]


def swap_col(block, partner):
    count = lax.axis_size("col")
    return lax.ppermute(block, "col", [(at, at ^ partner) for at in range(count)])


def swap_both(block, partner):
    count = lax.axis_size("col")
    pairs = [
        (depth * count + at, (1 - depth) * count + (at ^ partner))
        for depth in range(2)
        for at in range(count)
    ]
    return lax.ppermute(block, ("depth", "col"), pairs)


def whole_plan(
    alignment_activations,
    alignment_mask,
    pair_activation_input,
    pair_update_mask,
    pair_output_gradient,
    layer_scale_factor,
    first_projector,
    second_projector,
    output_weight,
    pair_norm_gain,
    hidden_weight,
    back_weight,
):
    seqs, res, channels = alignment_activations.shape
    width = first_projector.shape[1]
    outer_width = width * width
    cols = lax.axis_size("col")
    depths = lax.axis_size("depth")
    residues = res * cols
    pair_cols, pair_width = pair_activation_input.shape[1:]
    hid = hidden_weight.shape[1]
    per = res * pair_cols
    lanes = res * width
    rows = 2 * seqs + MASK_ROWS
    half = residues * pair_cols
    f32, bf16 = jnp.float32, jnp.bfloat16
    ids = jnp.stack([lax.axis_index("depth"), lax.axis_index("col")]).astype(jnp.int32)
    smem = pl.BlockSpec(memory_space=pltpu.SMEM)
    vmem = pl.BlockSpec(memory_space=pltpu.VMEM)
    params = pltpu.CompilerParams(vmem_limit_bytes=16 * 2**20)
    scale = layer_scale_factor.reshape(1, channels)
    first, second = first_projector.T, second_projector.T
    wturn = jnp.transpose(output_weight.reshape(width, width, pair_width), (1, 0, 2)).reshape(
        outer_width, pair_width
    )
    shape = jax.ShapeDtypeStruct
    sent, sent_pairs, scale, first, second, gain, normed, scaled, inv, mask_lanes = pl.pallas_call(
        pre_kernel,
        out_shape=(
            shape((1, rows, pair_width), bf16),
            shape((1, 2 * per, pair_width), bf16),
            shape((1, channels), f32),
            shape((width, channels), bf16),
            shape((width, channels), bf16),
            shape((1, pair_width), f32),
            shape((seqs * res, channels), bf16),
            shape((seqs * res, channels), f32),
            shape((seqs * res, 1), f32),
            shape((seqs, lanes), f32),
        ),
        in_specs=[smem] + [pl.BlockSpec(memory_space=pltpu.HBM)] * 9,
        out_specs=[vmem] * 10,
        scratch_shapes=[
            pltpu.VMEM((2, seqs * res, lanes), f32),
            pltpu.VMEM((MASK_ROWS, lanes), f32),
            pltpu.VMEM((seqs, res, channels), bf16),
            pltpu.VMEM((res, seqs), jnp.int32),
            pltpu.VMEM((res, pair_cols), jnp.int32),
            pltpu.SemaphoreType.DMA((9,)),
        ],
        compiler_params=params,
        name="project",
    )(
        ids,
        *[
            pltpu.with_memory_space_constraint(array, pltpu.HBM)
            for array in (
                alignment_activations,
                alignment_mask.T,
                pair_update_mask,
                scale,
                first,
                second,
                pair_norm_gain.reshape(1, pair_width),
                pair_activation_input.reshape(per, pair_width),
                pair_output_gradient.reshape(per, pair_width),
            )
        ],
    )
    near_order = (0,) + Z_PARTNERS
    far_order = tuple(at ^ Y_PARTNER for at in near_order)
    came = [swap_col(sent, partner) for partner in Z_PARTNERS]
    came[0], sent_pairs = lax.optimization_barrier((came[0], sent_pairs))
    near = jnp.concatenate([sent] + came)
    pair_near = jnp.concatenate(
        [sent_pairs] + [swap_col(sent_pairs, partner) for partner in Z_PARTNERS]
    )
    far = swap_col(near, Y_PARTNER)
    pair_far = swap_col(pair_near, Y_PARTNER)
    sizes = (seqs, res, pair_cols, width)
    orders = (near_order, far_order)
    outer, proj_out, cnt, pm = pl.pallas_call(
        functools.partial(outer_kernel, sizes, orders),
        out_shape=(
            shape((half, outer_width), bf16),
            shape((half, pair_width), f32),
            shape((half, lanes), f32),
            shape((half, lanes), bf16),
        ),
        in_specs=[smem] + [vmem] * 5,
        out_specs=[vmem] * 4,
        scratch_shapes=[
            pltpu.VMEM((depths, cols, rows, pair_width), bf16),
            pltpu.VMEM((depths * seqs, residues * width), bf16),
            pltpu.VMEM((pair_cols * width, depths * seqs), bf16),
            pltpu.VMEM((pair_cols * width, depths * seqs), f32),
            pltpu.VMEM((residues, depths * seqs), f32),
            pltpu.VMEM((half, lanes), bf16),
            pltpu.VMEM((half, lanes), bf16),
        ],
        compiler_params=params,
        name="outer_products",
    )(ids, near, far, swap_depth(near), swap_depth(far), wturn)
    near, far, proj_out = lax.optimization_barrier((near, far, proj_out))
    rightt, leftt = pl.pallas_call(
        functools.partial(turn_kernel, sizes, orders),
        out_shape=(
            shape((residues * width, depths * seqs), bf16),
            shape((residues * width, depths * seqs), bf16),
        ),
        in_specs=[smem] + [vmem] * 2,
        out_specs=[vmem] * 2,
        scratch_shapes=[pltpu.VMEM((residues * width, depths * seqs), f32)],
        compiler_params=params,
        name="turned",
    )(ids, near, far)
    pair_far, rightt, leftt, proj_out = lax.optimization_barrier(
        (pair_far, rightt, leftt, proj_out)
    )
    couple, opm, pn, gh, hidden, mg = pl.pallas_call(
        functools.partial(transition_kernel, sizes, orders),
        out_shape=(
            shape((per, pair_width), bf16),
            shape((half, pair_width), bf16),
            shape((half, pair_width), bf16),
            shape((half, hid), bf16),
            shape((half, hid), bf16),
            shape((half, pair_width), bf16),
        ),
        in_specs=[smem] + [vmem] * 8,
        out_specs=[vmem] * 6,
        scratch_shapes=[
            pltpu.VMEM((cols, 2 * per, pair_width), bf16),
            pltpu.VMEM((half, pair_width), f32),
        ],
        compiler_params=params,
        name="transition",
    )(
        ids,
        pair_near,
        pair_far,
        proj_out,
        cnt,
        pm,
        gain,
        hidden_weight,
        back_weight,
    )
    dout = pl.pallas_call(
        out_weight_kernel,
        out_shape=shape((outer_width, pair_width), bf16),
        in_specs=[vmem] * 2,
        out_specs=vmem,
        scratch_shapes=[pltpu.VMEM((outer_width, pair_width), f32)],
        compiler_params=params,
        name="out_weight",
    )(outer, opm)
    dhid, dback = pl.pallas_call(
        transition_weight_kernel,
        out_shape=(shape((pair_width, hid), bf16), shape((hid, pair_width), bf16)),
        in_specs=[vmem] * 4,
        out_specs=[vmem] * 2,
        compiler_params=params,
        name="transition_weights",
    )(pn, gh, hidden, mg)
    other_opm, dout, dhid, dback = lax.optimization_barrier((swap_depth(opm), dout, dhid, dback))
    other_weights = [swap_depth(block) for block in (dout, dhid, dback)]
    part, spread = pl.pallas_call(
        functools.partial(projector_kernel, sizes),
        out_shape=(
            shape((2 * width, channels), bf16),
            shape((seqs * res, 2 * lanes), bf16),
        ),
        in_specs=[smem] + [vmem] * 8,
        out_specs=[vmem] * 2,
        scratch_shapes=[
            pltpu.VMEM((depths, half, pair_width), f32),
            pltpu.VMEM((res * residues, pair_width), bf16),
            pltpu.VMEM((res * residues, pair_width), bf16),
            pltpu.VMEM((residues * width, lanes), bf16),
            pltpu.VMEM((residues * width, lanes), bf16),
            pltpu.VMEM((2, seqs * res, lanes), f32),
        ],
        compiler_params=params,
        name="projector_parts",
    )(ids, opm, other_opm, rightt, leftt, output_weight, wturn, normed, mask_lanes)
    feat = pl.pallas_call(
        functools.partial(feature_kernel, res),
        out_shape=shape((seqs * res, channels), bf16),
        in_specs=[vmem] * 6,
        out_specs=vmem,
        compiler_params=params,
        name="features",
    )(spread, first, second, scale, scaled, inv)
    dout, dhid, dback = pl.pallas_call(
        sum_kernel,
        out_shape=(
            shape((outer_width, pair_width), f32),
            shape((pair_width, hid), f32),
            shape((hid, pair_width), f32),
        ),
        in_specs=[vmem] * 6,
        out_specs=[vmem] * 3,
        compiler_params=params,
        name="sums_over_depth",
    )(dout, dhid, dback, *other_weights)
    total = part.astype(f32)
    kept = lax.optimization_barrier(total.astype(bf16))
    near_ones = [swap_depth(kept), swap_col(kept, Y_PARTNER), swap_both(kept, Y_PARTNER)]
    near_ones, feat = lax.optimization_barrier((near_ones, feat))
    total = pairwise_sum([block.astype(f32) for block in [kept] + near_ones])
    kept = lax.optimization_barrier(total.astype(bf16))
    far_ones = [swap_col(kept, partner) for partner in Z_PARTNERS]
    far_ones, dout, dhid, dback = lax.optimization_barrier((far_ones, dout, dhid, dback))
    total = pairwise_sum([block.astype(f32) for block in [kept] + far_ones])
    return (
        feat.reshape(seqs, res, channels),
        couple.reshape(res, pair_cols, pair_width),
        total[:width].T,
        total[width:].T,
        dout,
        dhid,
        dback,
    )


def on_device(alignment_activations, *others):
    cols = lax.axis_size("col")
    residues = alignment_activations.shape[1] * cols
    plan = whole_plan if cols == 8 and residues <= FEW_RESIDUES else split_plan
    return plan(alignment_activations, *others)


def solution(mesh):
    in_specs = (
        P(("group", "depth"), "col", None),
        P(("group", "depth"), "col"),
        P(("group", "col"), "depth", None),
        P(("group", "col"), "depth"),
        P(("group", "col"), "depth", None),
        P(),
        P(),
        P(),
        P(),
        P(),
        P(),
        P(),
    )
    out_specs = (
        P(("group", "depth"), "col", None),
        P(("group", "col"), "depth", None),
        P("group", None),
        P("group", None),
        P("group", None),
        P("group", None),
        P("group", None),
    )
    return jax.shard_map(
        on_device, mesh=mesh, in_specs=in_specs, out_specs=out_specs, check_vma=False
    )
```

```python
import functools

import jax
import jax.numpy as jnp
from jax import lax
from jax.experimental import pallas as pl
from jax.experimental.pallas import tpu as pltpu
from jax.sharding import PartitionSpec as P

epsilon = 1e-05
highest = lax.Precision.HIGHEST


def norm_pieces(entries_drawn):
    center = entries_drawn - jnp.mean(entries_drawn, axis=-1, keepdims=True)
    inv_std = lax.rsqrt(jnp.mean(center * center, axis=-1, keepdims=True) + epsilon)
    return (center * inv_std, inv_std)


def standardize_adjoint(grad_scaled, scaled, inv_std):
    mean_grad = jnp.mean(grad_scaled, axis=-1, keepdims=True)
    mean_cross = jnp.mean(grad_scaled * scaled, axis=-1, keepdims=True)
    return inv_std * (grad_scaled - mean_grad - scaled * mean_cross)


def silu_pieces(pre_act):
    sigma = jax.nn.sigmoid(pre_act)
    return (pre_act * sigma, sigma * (1.0 + pre_act * (1.0 - sigma)))


def split_plan(
    alignment_activations,
    alignment_mask,
    pair_activation_input,
    pair_update_mask,
    pair_output_gradient,
    layer_scale_factor,
    first_projector,
    second_projector,
    output_weight,
    pair_norm_gain,
    hidden_weight,
    back_weight,
):
    sequence_row_block, residue_row_block, channel_total = alignment_activations.shape
    proj_width = first_projector.shape[1]
    outer_width = proj_width * proj_width
    depth_count = lax.axis_size("depth")
    residues = residue_row_block * lax.axis_size("col")
    pair_cols = pair_activation_input.shape[1]
    pair_width = pair_activation_input.shape[2]
    col_block = min(64, pair_cols)
    block_count = pair_cols // col_block
    standardized_features, reciprocal_spread = norm_pieces(
        alignment_activations.astype(jnp.float32)
    )
    normalized_rows = (standardized_features * layer_scale_factor).astype(jnp.bfloat16)
    mask_floating = alignment_mask.astype(jnp.float32)
    left_proj = (
        jnp.dot(normalized_rows, first_projector, preferred_element_type=jnp.float32)
        * mask_floating[:, :, None]
    ).astype(jnp.bfloat16)
    right_proj = (
        jnp.dot(normalized_rows, second_projector, preferred_element_type=jnp.float32)
        * mask_floating[:, :, None]
    ).astype(jnp.bfloat16)
    right_flat = right_proj.reshape(sequence_row_block, residue_row_block * proj_width)
    mask_converted = alignment_mask.astype(jnp.bfloat16)
    seq_total = left_proj.shape[0]
    gathered, gathered_mask = (
        lax.all_gather(right_flat, "col", axis=1, tiled=True),
        lax.all_gather(mask_converted, "col", axis=1, tiled=True),
    )
    right_blocks = gathered.reshape(seq_total, depth_count, pair_cols, proj_width)
    mask_blocks = gathered_mask.reshape(seq_total, depth_count, pair_cols)
    block_depth = right_blocks.shape[1]
    out_wide = output_weight.astype(jnp.float32)

    def partial_outer(col_start):
        right_piece = lax.dynamic_slice_in_dim(right_blocks, col_start, col_block, 2)
        outer_part = jnp.einsum(
            "sic,sejd->iejcd", left_proj, right_piece, preferred_element_type=jnp.float32
        )
        return (
            outer_part.reshape(residue_row_block, block_depth, col_block, outer_width),
            right_piece,
        )

    def forward_step(step_index, loop_state):
        projected, pair_count = loop_state
        col_start = step_index * col_block
        outer_part, right_piece = partial_outer(col_start)
        mask_piece = lax.dynamic_slice_in_dim(mask_blocks, col_start, col_block, 2).astype(
            jnp.float32
        )
        count_part = jnp.einsum("si,sej->iej", mask_floating, mask_piece, precision=highest)
        outer_mine, count_mine = (
            lax.psum_scatter(
                outer_part.astype(jnp.bfloat16), "depth", scatter_dimension=1, tiled=True
            ).astype(jnp.float32),
            lax.psum_scatter(
                count_part.astype(jnp.bfloat16), "depth", scatter_dimension=1, tiled=True
            ).astype(jnp.float32),
        )
        proj_mine = jnp.dot(
            outer_mine.reshape(residue_row_block * col_block, outer_width),
            out_wide,
            precision=highest,
        )
        proj_mine = proj_mine.reshape(residue_row_block, col_block, pair_width)
        count_mine = count_mine.reshape(residue_row_block, col_block)
        projected = lax.dynamic_update_slice_in_dim(projected, proj_mine, col_start, 1)
        pair_count = lax.dynamic_update_slice_in_dim(pair_count, count_mine, col_start, 1)
        return (projected, pair_count)

    projected, pair_count = lax.fori_loop(
        0,
        block_count,
        forward_step,
        (
            jnp.zeros((residue_row_block, pair_cols, pair_width), jnp.float32),
            jnp.zeros((residue_row_block, pair_cols), jnp.float32),
        ),
    )
    count_column = pair_count.reshape(residue_row_block * pair_cols, 1)
    mid_act = (
        pair_activation_input.reshape(residue_row_block * pair_cols, pair_width).astype(jnp.float32)
        + projected.reshape(residue_row_block * pair_cols, pair_width) / count_column
    )
    pair_scaled, pair_inv = norm_pieces(mid_act)
    pair_normed = (pair_scaled * pair_norm_gain).astype(jnp.bfloat16)
    pre_act = jnp.dot(pair_normed, hidden_weight, preferred_element_type=jnp.float32)
    act_value, act_slope = silu_pieces(pre_act)
    hidden = act_value.astype(jnp.bfloat16)
    masked_grad = (
        pair_output_gradient * pair_update_mask.astype(jnp.bfloat16)[:, :, None]
    ).reshape(residue_row_block * pair_cols, pair_width)
    final_matrix_derivative = jnp.dot(hidden.T, masked_grad, preferred_element_type=jnp.float32)
    back_prod = jnp.dot(masked_grad, back_weight.T, preferred_element_type=jnp.float32)
    grad_hidden = (back_prod * act_slope).astype(jnp.bfloat16)
    middle_matrix_derivative = jnp.dot(
        pair_normed.T, grad_hidden, preferred_element_type=jnp.float32
    )
    grad_scaled = (
        jnp.dot(grad_hidden, hidden_weight.T, preferred_element_type=jnp.float32) * pair_norm_gain
    )
    grad_mid = pair_output_gradient.reshape(residue_row_block * pair_cols, pair_width).astype(
        jnp.float32
    ) + standardize_adjoint(grad_scaled, pair_scaled, pair_inv)
    couple_features_derivative = grad_mid.astype(jnp.bfloat16).reshape(
        residue_row_block, pair_cols, pair_width
    )
    grad_opm = (
        (grad_mid / count_column)
        .astype(jnp.bfloat16)
        .reshape(residue_row_block, pair_cols, pair_width)
    )
    full_opm = lax.all_gather(grad_opm, "depth", axis=1, tiled=True).reshape(
        residue_row_block, depth_count, pair_cols, pair_width
    )

    def backward_step(step_index, loop_state):
        grad_left_acc, grad_out, right_term = loop_state
        col_start = step_index * col_block
        outer_part, right_piece = partial_outer(col_start)
        opm_piece = lax.dynamic_slice_in_dim(full_opm, col_start, col_block, 2).reshape(
            residue_row_block * block_depth * col_block, pair_width
        )
        grad_out = grad_out + jnp.dot(
            outer_part.reshape(residue_row_block * block_depth * col_block, outer_width).T,
            opm_piece.astype(jnp.float32),
            precision=highest,
        )
        grad_outer = jnp.dot(opm_piece, output_weight.T, preferred_element_type=jnp.float32).astype(
            jnp.bfloat16
        )
        grad_outer = grad_outer.reshape(
            residue_row_block, block_depth, col_block, proj_width, proj_width
        )
        grad_left_acc = grad_left_acc + jnp.einsum(
            "iejcd,sejd->sic", grad_outer, right_piece, preferred_element_type=jnp.float32
        )
        piece_term = jnp.einsum(
            "iejcd,sic->ejsd", grad_outer, left_proj, preferred_element_type=jnp.float32
        )
        piece_term = piece_term.reshape(block_depth, col_block, seq_total * proj_width)
        right_term = lax.dynamic_update_slice_in_dim(right_term, piece_term, col_start, 1)
        return (grad_left_acc, grad_out, right_term)

    grad_left_acc, result_matrix_derivative, right_term = lax.fori_loop(
        0,
        block_count,
        backward_step,
        (
            jnp.zeros((seq_total, residue_row_block, proj_width), jnp.float32),
            jnp.zeros((outer_width, pair_width), jnp.float32),
            jnp.zeros((block_depth, pair_cols, seq_total * proj_width), jnp.float32),
        ),
    )
    grad_right_sum = lax.psum_scatter(
        right_term.reshape(residues, seq_total * proj_width), "col", scatter_dimension=0, tiled=True
    )
    grad_right_acc = jnp.transpose(
        grad_right_sum.reshape(residue_row_block, seq_total, proj_width), (1, 0, 2)
    )
    grad_left = (grad_left_acc * mask_floating[:, :, None]).astype(jnp.bfloat16)
    grad_right = (grad_right_acc * mask_floating[:, :, None]).astype(jnp.bfloat16)
    normed_rows = normalized_rows.reshape(sequence_row_block * residue_row_block, channel_total)
    first_projector_derivative = jnp.dot(
        normed_rows.T,
        grad_left.reshape(sequence_row_block * residue_row_block, proj_width),
        preferred_element_type=jnp.float32,
    )
    second_projector_derivative = jnp.dot(
        normed_rows.T,
        grad_right.reshape(sequence_row_block * residue_row_block, proj_width),
        preferred_element_type=jnp.float32,
    )
    standardized_derivative = jnp.dot(
        grad_left, first_projector.T, preferred_element_type=jnp.float32
    ) + jnp.dot(grad_right, second_projector.T, preferred_element_type=jnp.float32)
    features_derivative = standardize_adjoint(
        standardized_derivative * layer_scale_factor, standardized_features, reciprocal_spread
    ).astype(jnp.bfloat16)
    weight_sums = lax.psum(
        (
            first_projector_derivative,
            second_projector_derivative,
            result_matrix_derivative,
            middle_matrix_derivative,
            final_matrix_derivative,
        ),
        ("depth", "col"),
    )
    return (
        features_derivative,
        couple_features_derivative,
        weight_sums[0],
        weight_sums[1],
        weight_sums[2],
        weight_sums[3],
        weight_sums[4],
    )


FEW_RESIDUES = 32
MASK_ROWS = 16
Y_PARTNER = 1


def butterfly(blocks, group):
    lane_group = lax.broadcasted_iota(jnp.int32, blocks[0].shape, 1) // group
    width = 4 * group
    for bit in (2, 1):
        low = (lane_group & bit) == 0
        swapped = list(blocks)
        for at in range(4):
            if at & bit:
                continue
            here, there = blocks[at], blocks[at | bit]
            moving = jnp.where(low, there, here)
            if bit == 2:
                moved = pltpu.roll(moving, 2 * group, 1)
            else:
                moved = jnp.where(
                    low, pltpu.roll(moving, width - group, 1), pltpu.roll(moving, group, 1)
                )
            swapped[at] = jnp.where(low, here, moved)
            swapped[at | bit] = jnp.where(low, moved, there)
        blocks = swapped
    return blocks


def wide_projector(first_ref, second_ref, copies):
    return jnp.concatenate([first_ref[...]] * copies + [second_ref[...]] * copies, axis=0)


def pre_kernel(
    ids_ref,
    x_hbm,
    maskt_hbm,
    pmask_hbm,
    scale_hbm,
    first_hbm,
    second_hbm,
    gain_hbm,
    act_hbm,
    grad_hbm,
    sent_ref,
    scale_ref,
    first_ref,
    second_ref,
    gain_ref,
    normed_ref,
    scaled_ref,
    inv_ref,
    lanes_ref,
    wide_ref,
    tile_ref,
    x_ref,
    maskt_ref,
    pmask_ref,
    pairs_ref,
    sems,
):
    res, seqs = maskt_ref.shape
    pairs = act_hbm.shape[0]
    copies = [
        pltpu.make_async_copy(source, target, sems.at[at])
        for at, (source, target) in enumerate(
            (
                (x_hbm, x_ref),
                (maskt_hbm, maskt_ref),
                (pmask_hbm, pmask_ref),
                (scale_hbm, scale_ref),
                (first_hbm, first_ref),
                (second_hbm, second_ref),
                (gain_hbm, gain_ref),
                (act_hbm, pairs_ref.at[pl.ds(0, pairs), :]),
                (grad_hbm, pairs_ref.at[pl.ds(pairs, pairs), :]),
            )
        )
    ]
    for copy in copies:
        copy.start()
    for copy in copies:
        copy.wait()
    lanes = sent_ref.shape[2]
    group = lanes // res
    scaled, inv = norm_pieces(
        x_ref[...].astype(jnp.float32).reshape(seqs * res, x_ref.shape[2])
    )
    scaled_ref[...] = scaled
    inv_ref[...] = inv
    normed = (scaled * scale_ref[...]).astype(jnp.bfloat16)
    normed_ref[...] = normed
    wide = lax.dot_general(
        normed,
        wide_projector(first_ref, second_ref, res),
        (((1,), (1,)), ((), ())),
        preferred_element_type=jnp.float32,
    )
    for at in range(2):
        wide_ref[at] = wide[:, at * lanes : (at + 1) * lanes]
    tile_ref[...] = jnp.zeros(tile_ref.shape, jnp.float32)
    mask = maskt_ref[...].astype(jnp.float32)
    tile_ref[0:res, 0:seqs] = mask
    spread = (
        lax.broadcasted_iota(jnp.int32, (MASK_ROWS, lanes), 1) // group
        == lax.broadcasted_iota(jnp.int32, (MASK_ROWS, lanes), 0)
    ).astype(jnp.float32)
    mask_lanes = lax.dot_general(
        tile_ref[...], spread, (((0,), (0,)), ((), ())), preferred_element_type=jnp.float32
    )[:seqs]
    lanes_ref[...] = mask_lanes
    twice = jnp.concatenate([mask] * (lanes // seqs), axis=1)
    here = lax.broadcasted_iota(jnp.int32, (res, lanes), 1) // seqs == ids_ref[0]
    tile_ref[0:res, :] = jnp.where(here, twice, 0.0)
    tile_ref[res : 2 * res, 0 : pmask_ref.shape[1]] = pmask_ref[...].astype(jnp.float32)
    lane_group = lax.broadcasted_iota(jnp.int32, (seqs, lanes), 1) // group
    for at in range(2):
        both = wide_ref[at, pl.ds(0, seqs, stride=res), :]
        for r in range(1, res):
            both = jnp.where(
                lane_group == r, wide_ref[at, pl.ds(r, seqs, stride=res), :], both
            )
        sent_ref[0, at * seqs : (at + 1) * seqs, :] = (both * mask_lanes).astype(jnp.bfloat16)
    first_pair = 2 * seqs + MASK_ROWS
    sent_ref[0, 2 * seqs : first_pair, :] = tile_ref[...].astype(jnp.bfloat16)
    sent_ref[0, first_pair:, :] = pairs_ref[...]
    for at in range(1, sent_ref.shape[0]):
        sent_ref[at] = sent_ref[0]


def outer_kernel(
    sizes,
    ids_ref,
    near_ref,
    far_ref,
    other_near_ref,
    other_far_ref,
    wturn_ref,
    outer_ref,
    proj_out_ref,
    cnt_ref,
    pm_ref,
    got_ref,
    leftn_ref,
    mine_ref,
    turn_ref,
    maskt_ref,
    cntl_ref,
    pml_ref,
):
    seqs, res, pair_cols, width = sizes
    depths, cols = got_ref.shape[0], got_ref.shape[1]
    residues = cols * res
    lanes = res * width
    half_cols = pair_cols // res
    me_depth = ids_ref[0]
    me_col = ids_ref[1]
    f32, bf16 = jnp.float32, jnp.bfloat16

    for mine, other, owner in (
        (near_ref, other_near_ref, me_col % 2),
        (far_ref, other_far_ref, 1 - me_col % 2),
    ):
        for at in range(cols // 2):
            got_ref[me_depth, 2 * at + owner] = mine[at]
            got_ref[1 - me_depth, 2 * at + owner] = other[at]

    for e in range(depths):
        for k in range(cols):
            leftn_ref[e * seqs : (e + 1) * seqs, k * lanes : (k + 1) * lanes] = got_ref[
                e, k, 0:seqs, :
            ]
    for k in range(half_cols):
        block = jnp.concatenate(
            [
                got_ref[e, me_depth * half_cols + k, seqs : 2 * seqs, :]
                for e in range(depths)
            ],
            axis=0,
        ).astype(f32)
        turn_ref[k * lanes : (k + 1) * lanes, :] = block.T
    for d in range(width):
        mine_ref[d * pair_cols : (d + 1) * pair_cols, :] = turn_ref[
            pl.ds(d, pair_cols, stride=width), :
        ].astype(bf16)

    base = 2 * seqs
    pair_lane = lax.broadcasted_iota(jnp.int32, (pair_cols, lanes), 1)
    pair_row = lax.broadcasted_iota(jnp.int32, (pair_cols, lanes), 0)
    for k in range(cols):
        tiles = [got_ref[e, k, base : base + MASK_ROWS, :].astype(f32) for e in range(depths)]
        maskt_ref[k * res : (k + 1) * res, :] = tiles[0][0:res] + tiles[1][0:res]
        own = got_ref[me_depth, k, base : base + MASK_ROWS, :].astype(f32)
        for r in range(res):
            row = own[res + r : res + r + 1, :]
            first = (k * res + r) * pair_cols
            pml_ref[first : first + pair_cols, :] = jnp.where(
                pair_lane == pair_row, row, 0.0
            ).astype(bf16)
    maskt = maskt_ref[...]
    cols_mask = maskt_ref[pl.ds(pl.multiple_of(me_depth * pair_cols, pair_cols), pair_cols), :]
    for i in range(residues):
        cntl_ref[i * pair_cols : (i + 1) * pair_cols, :] = (maskt[i : i + 1, :] * cols_mask).astype(
            bf16
        )
    ones = jnp.ones((lanes, lanes), bf16)
    cnt_ref[...] = jnp.dot(cntl_ref[...], ones, preferred_element_type=f32)
    pm_ref[...] = jnp.dot(pml_ref[...], ones, preferred_element_type=f32).astype(bf16)

    for dh in range(width // 4):
        prod = jnp.dot(
            mine_ref[dh * 4 * pair_cols : (dh + 1) * 4 * pair_cols, :],
            leftn_ref[...],
            preferred_element_type=f32,
        )
        for k in range(cols):
            piece = prod[:, k * lanes : (k + 1) * lanes]
            turned = butterfly(
                [piece[a * pair_cols : (a + 1) * pair_cols] for a in range(4)], width
            )
            for il in range(res):
                first = (k * res + il) * pair_cols
                outer_ref[first : first + pair_cols, dh * lanes : (dh + 1) * lanes] = turned[
                    il
                ].astype(bf16)
    proj_out_ref[...] = jnp.dot(outer_ref[...], wturn_ref[...], preferred_element_type=f32)


def turn_kernel(sizes, ids_ref, near_ref, far_ref, rightt_ref, leftt_ref, turn_ref):
    seqs, res, _, width = sizes
    lanes = res * width
    residues = turn_ref.shape[0] // width
    me_col = ids_ref[1]
    for at, out in ((0, leftt_ref), (1, rightt_ref)):
        for blocks, owner in ((near_ref, me_col % 2), (far_ref, 1 - me_col % 2)):
            for place in range(blocks.shape[0]):
                block = blocks[place, at * seqs : (at + 1) * seqs, :].astype(jnp.float32)
                block = jnp.concatenate([block] * (lanes // seqs), axis=0)
                first = pl.multiple_of((2 * place + owner) * lanes, lanes)
                turn_ref[pl.ds(first, lanes), :] = block.T
        for d in range(width):
            out[d * residues : (d + 1) * residues, :] = turn_ref[
                pl.ds(d, residues, stride=width), :
            ].astype(jnp.bfloat16)


def transition_kernel(
    sizes,
    ids_ref,
    near_ref,
    far_ref,
    proj_out_ref,
    cnt_ref,
    pm_ref,
    gain_ref,
    hid_ref,
    back_ref,
    couple_ref,
    opm_ref,
    pn_ref,
    gh_ref,
    hidden_ref,
    mg_ref,
    pgot_ref,
    gmid_ref,
):
    seqs, res, pair_cols, width = sizes
    per = res * pair_cols
    cols = pgot_ref.shape[0]
    me_col = ids_ref[1]
    f32, bf16 = jnp.float32, jnp.bfloat16
    for mine, owner in ((near_ref, me_col % 2), (far_ref, 1 - me_col % 2)):
        for at in range(cols // 2):
            pgot_ref[2 * at + owner] = mine[at]
    gain = gain_ref[...]
    chunk = 2 * per
    for at in range(cols // 2):
        rows = slice(at * chunk, (at + 1) * chunk)
        act, grad = [
            jnp.concatenate(
                [pgot_ref[2 * at + b, w * per : (w + 1) * per, :] for b in range(2)], axis=0
            )
            for w in range(2)
        ]
        count = cnt_ref[rows, :]
        mid = act.astype(f32) + proj_out_ref[rows, :] / count
        scaled, inv = norm_pieces(mid)
        normed = (scaled * gain).astype(bf16)
        pn_ref[rows, :] = normed
        pre = jnp.dot(normed, hid_ref[...], preferred_element_type=f32)
        value, slope = silu_pieces(pre)
        hidden_ref[rows, :] = value.astype(bf16)
        masked = grad * pm_ref[rows, :]
        mg_ref[rows, :] = masked
        back = lax.dot_general(
            masked, back_ref[...], (((1,), (1,)), ((), ())), preferred_element_type=f32
        )
        ghid = (back * slope).astype(bf16)
        gh_ref[rows, :] = ghid
        gsc = (
            lax.dot_general(
                ghid, hid_ref[...], (((1,), (1,)), ((), ())), preferred_element_type=f32
            )
            * gain
        )
        gmid = grad.astype(f32) + standardize_adjoint(gsc, scaled, inv)
        gmid_ref[rows, :] = gmid
        opm_ref[rows, :] = (gmid / count).astype(bf16)
    couple_ref[...] = gmid_ref[pl.ds(pl.multiple_of(me_col * per, per), per), :].astype(bf16)


def projector_kernel(
    sizes,
    ids_ref,
    opm_ref,
    other_opm_ref,
    rightt_ref,
    leftt_ref,
    wout_ref,
    wturn_ref,
    normed_ref,
    lanes_ref,
    part_ref,
    spread_ref,
    gf_ref,
    grow_ref,
    gcol_ref,
    gor_ref,
    goc_ref,
    gs_ref,
):
    seqs, res, pair_cols, width = sizes
    depths, half = gf_ref.shape[0], gf_ref.shape[1]
    residues = half // pair_cols
    lanes = res * width
    me_depth = ids_ref[0]
    me_col = ids_ref[1]
    f32, bf16 = jnp.float32, jnp.bfloat16
    gf_ref[me_depth] = opm_ref[...].astype(f32)
    gf_ref[1 - me_depth] = other_opm_ref[...].astype(f32)

    for il in range(res):
        for e in range(depths):
            first = pl.multiple_of((me_col * res + il) * pair_cols, pair_cols)
            grow_ref[il * residues + e * pair_cols : il * residues + (e + 1) * pair_cols, :] = (
                gf_ref[e, pl.ds(first, pair_cols), :].astype(bf16)
            )
    my_half = (me_col * res) // pair_cols
    my_first = me_col * res - my_half * pair_cols
    for jl in range(res):
        gcol_ref[jl * residues : (jl + 1) * residues, :] = gf_ref[
            my_half, pl.ds(my_first + jl, residues, stride=pair_cols), :
        ].astype(bf16)
    for lhs, weight, out in ((grow_ref, wturn_ref, gor_ref), (gcol_ref, wout_ref, goc_ref)):
        for dh in range(width // 4):
            piece = lax.dot_general(
                lhs[...],
                weight[dh * lanes : (dh + 1) * lanes, :],
                (((1,), (1,)), ((), ())),
                preferred_element_type=f32,
            )
            turned = butterfly(
                [piece[a * residues : (a + 1) * residues] for a in range(4)], width
            )
            for dl in range(4):
                first = (dh * 4 + dl) * residues
                out[first : first + residues, :] = turned[dl].astype(bf16)
    mask_lanes = lanes_ref[...]
    lane_group = lax.broadcasted_iota(jnp.int32, (seqs, lanes), 1) // width
    for at, (lhs, rhs) in enumerate(((rightt_ref, gor_ref), (leftt_ref, goc_ref))):
        total = lax.dot_general(
            lhs[...], rhs[...], (((0,), (0,)), ((), ())), preferred_element_type=f32
        )[:seqs]
        total = (total * mask_lanes).astype(bf16).astype(f32)
        for r in range(res):
            gs_ref[at, pl.ds(r, seqs, stride=res), :] = jnp.where(lane_group == r, total, 0.0)
    spread = jnp.concatenate([gs_ref[0], gs_ref[1]], axis=1).astype(bf16)
    spread_ref[...] = spread
    cross = lax.dot_general(
        spread, normed_ref[...], (((0,), (0,)), ((), ())), preferred_element_type=f32
    )
    for at in range(2):
        total = cross[at * lanes : at * lanes + width]
        for r in range(1, res):
            total = total + cross[at * lanes + r * width : at * lanes + (r + 1) * width]
        part_ref[at * width : (at + 1) * width, :] = total.astype(bf16)


def out_weight_kernel(outer_ref, opm_ref, dout_ref, turn_ref):
    width = int(dout_ref.shape[0] ** 0.5 + 0.5)
    turn_ref[...] = lax.dot_general(
        outer_ref[...], opm_ref[...], (((0,), (0,)), ((), ())), preferred_element_type=jnp.float32
    )
    for c in range(width):
        dout_ref[c * width : (c + 1) * width, :] = turn_ref[
            pl.ds(c, width, stride=width), :
        ].astype(jnp.bfloat16)


def transition_weight_kernel(pn_ref, gh_ref, hidden_ref, mg_ref, dhid_ref, dback_ref):
    for lhs, rhs, out in ((pn_ref, gh_ref, dhid_ref), (hidden_ref, mg_ref, dback_ref)):
        out[...] = lax.dot_general(
            lhs[...], rhs[...], (((0,), (0,)), ((), ())), preferred_element_type=jnp.float32
        ).astype(jnp.bfloat16)


def sum_kernel(*refs):
    for mine, other, out in zip(refs[0:3], refs[3:6], refs[6:9]):
        out[...] = mine[...].astype(jnp.float32) + other[...].astype(jnp.float32)


def feature_kernel(
    copies, spread_ref, first_ref, second_ref, scale_ref, scaled_ref, inv_ref, feat_ref
):
    back = jnp.dot(
        spread_ref[...],
        wide_projector(first_ref, second_ref, copies),
        preferred_element_type=jnp.float32,
    )
    feat_ref[...] = standardize_adjoint(
        back * scale_ref[...], scaled_ref[...], inv_ref[...]
    ).astype(jnp.bfloat16)


def swap_depth(block):
    return lax.ppermute(block, "depth", [(0, 1), (1, 0)])


def pairwise_sum(blocks):
    while len(blocks) > 1:
        blocks = [blocks[at] + blocks[at + 1] for at in range(0, len(blocks), 2)]
    return blocks[0]


def swap_col(block, partner):
    count = lax.axis_size("col")
    return lax.ppermute(block, "col", [(at, at ^ partner) for at in range(count)])


def swap_both(block, partner):
    count = lax.axis_size("col")
    pairs = [
        (depth * count + at, (1 - depth) * count + (at ^ partner))
        for depth in range(2)
        for at in range(count)
    ]
    return lax.ppermute(block, ("depth", "col"), pairs)


def whole_plan(
    alignment_activations,
    alignment_mask,
    pair_activation_input,
    pair_update_mask,
    pair_output_gradient,
    layer_scale_factor,
    first_projector,
    second_projector,
    output_weight,
    pair_norm_gain,
    hidden_weight,
    back_weight,
):
    seqs, res, channels = alignment_activations.shape
    width = first_projector.shape[1]
    outer_width = width * width
    cols = lax.axis_size("col")
    depths = lax.axis_size("depth")
    residues = res * cols
    pair_cols, pair_width = pair_activation_input.shape[1:]
    hid = hidden_weight.shape[1]
    per = res * pair_cols
    lanes = res * width
    rows = 2 * seqs + MASK_ROWS
    line = cols // 2
    half = residues * pair_cols
    f32, bf16 = jnp.float32, jnp.bfloat16
    ids = jnp.stack([lax.axis_index("depth"), lax.axis_index("col")]).astype(jnp.int32)
    smem = pl.BlockSpec(memory_space=pltpu.SMEM)
    vmem = pl.BlockSpec(memory_space=pltpu.VMEM)
    params = pltpu.CompilerParams(vmem_limit_bytes=16 * 2**20)
    scale = layer_scale_factor.reshape(1, channels)
    first, second = first_projector.T, second_projector.T
    wturn = jnp.transpose(output_weight.reshape(width, width, pair_width), (1, 0, 2)).reshape(
        outer_width, pair_width
    )
    shape = jax.ShapeDtypeStruct
    sent, scale, first, second, gain, normed, scaled, inv, mask_lanes = pl.pallas_call(
        pre_kernel,
        out_shape=(
            shape((line, rows + 2 * per, pair_width), bf16),
            shape((1, channels), f32),
            shape((width, channels), bf16),
            shape((width, channels), bf16),
            shape((1, pair_width), f32),
            shape((seqs * res, channels), bf16),
            shape((seqs * res, channels), f32),
            shape((seqs * res, 1), f32),
            shape((seqs, lanes), f32),
        ),
        in_specs=[smem] + [pl.BlockSpec(memory_space=pltpu.HBM)] * 9,
        out_specs=[vmem] * 9,
        scratch_shapes=[
            pltpu.VMEM((2, seqs * res, lanes), f32),
            pltpu.VMEM((MASK_ROWS, lanes), f32),
            pltpu.VMEM((seqs, res, channels), bf16),
            pltpu.VMEM((res, seqs), jnp.int32),
            pltpu.VMEM((res, pair_cols), jnp.int32),
            pltpu.VMEM((2 * per, pair_width), bf16),
            pltpu.SemaphoreType.DMA((9,)),
        ],
        compiler_params=params,
        name="project",
    )(
        ids,
        *[
            pltpu.with_memory_space_constraint(array, pltpu.HBM)
            for array in (
                alignment_activations,
                alignment_mask.T,
                pair_update_mask,
                scale,
                first,
                second,
                pair_norm_gain.reshape(1, pair_width),
                pair_activation_input.reshape(per, pair_width),
                pair_output_gradient.reshape(per, pair_width),
            )
        ],
    )
    lines = [list(range(at, cols, 2)) for at in range(2)]

    def along_z(copies):
        return lax.all_to_all(copies, "col", 0, 0, axis_index_groups=lines)

    blocks = along_z(sent)
    near, pair_near = blocks[:, :rows], blocks[:, rows:]
    far = swap_col(near, Y_PARTNER)
    pair_far = swap_col(pair_near, Y_PARTNER)
    sizes = (seqs, res, pair_cols, width)
    outer, proj_out, cnt, pm = pl.pallas_call(
        functools.partial(outer_kernel, sizes),
        out_shape=(
            shape((half, outer_width), bf16),
            shape((half, pair_width), f32),
            shape((half, lanes), f32),
            shape((half, lanes), bf16),
        ),
        in_specs=[smem] + [vmem] * 5,
        out_specs=[vmem] * 4,
        scratch_shapes=[
            pltpu.VMEM((depths, cols, rows, pair_width), bf16),
            pltpu.VMEM((depths * seqs, residues * width), bf16),
            pltpu.VMEM((pair_cols * width, depths * seqs), bf16),
            pltpu.VMEM((pair_cols * width, depths * seqs), f32),
            pltpu.VMEM((residues, depths * seqs), f32),
            pltpu.VMEM((half, lanes), bf16),
            pltpu.VMEM((half, lanes), bf16),
        ],
        compiler_params=params,
        name="outer_products",
    )(ids, near, far, swap_depth(near), swap_depth(far), wturn)
    near, far, proj_out = lax.optimization_barrier((near, far, proj_out))
    rightt, leftt = pl.pallas_call(
        functools.partial(turn_kernel, sizes),
        out_shape=(
            shape((residues * width, depths * seqs), bf16),
            shape((residues * width, depths * seqs), bf16),
        ),
        in_specs=[smem] + [vmem] * 2,
        out_specs=[vmem] * 2,
        scratch_shapes=[pltpu.VMEM((residues * width, depths * seqs), f32)],
        compiler_params=params,
        name="turned",
    )(ids, near, far)
    pair_far, rightt, leftt, proj_out = lax.optimization_barrier(
        (pair_far, rightt, leftt, proj_out)
    )
    couple, opm, pn, gh, hidden, mg = pl.pallas_call(
        functools.partial(transition_kernel, sizes),
        out_shape=(
            shape((per, pair_width), bf16),
            shape((half, pair_width), bf16),
            shape((half, pair_width), bf16),
            shape((half, hid), bf16),
            shape((half, hid), bf16),
            shape((half, pair_width), bf16),
        ),
        in_specs=[smem] + [vmem] * 8,
        out_specs=[vmem] * 6,
        scratch_shapes=[
            pltpu.VMEM((cols, 2 * per, pair_width), bf16),
            pltpu.VMEM((half, pair_width), f32),
        ],
        compiler_params=params,
        name="transition",
    )(
        ids,
        pair_near,
        pair_far,
        proj_out,
        cnt,
        pm,
        gain,
        hidden_weight,
        back_weight,
    )
    dout = pl.pallas_call(
        out_weight_kernel,
        out_shape=shape((outer_width, pair_width), bf16),
        in_specs=[vmem] * 2,
        out_specs=vmem,
        scratch_shapes=[pltpu.VMEM((outer_width, pair_width), f32)],
        compiler_params=params,
        name="out_weight",
    )(outer, opm)
    dhid, dback = pl.pallas_call(
        transition_weight_kernel,
        out_shape=(shape((pair_width, hid), bf16), shape((hid, pair_width), bf16)),
        in_specs=[vmem] * 4,
        out_specs=[vmem] * 2,
        compiler_params=params,
        name="transition_weights",
    )(pn, gh, hidden, mg)
    other_opm, dout, dhid, dback = lax.optimization_barrier((swap_depth(opm), dout, dhid, dback))
    other_weights = [swap_depth(block) for block in (dout, dhid, dback)]
    part, spread = pl.pallas_call(
        functools.partial(projector_kernel, sizes),
        out_shape=(
            shape((2 * width, channels), bf16),
            shape((seqs * res, 2 * lanes), bf16),
        ),
        in_specs=[smem] + [vmem] * 8,
        out_specs=[vmem] * 2,
        scratch_shapes=[
            pltpu.VMEM((depths, half, pair_width), f32),
            pltpu.VMEM((res * residues, pair_width), bf16),
            pltpu.VMEM((res * residues, pair_width), bf16),
            pltpu.VMEM((residues * width, lanes), bf16),
            pltpu.VMEM((residues * width, lanes), bf16),
            pltpu.VMEM((2, seqs * res, lanes), f32),
        ],
        compiler_params=params,
        name="projector_parts",
    )(ids, opm, other_opm, rightt, leftt, output_weight, wturn, normed, mask_lanes)
    feat = pl.pallas_call(
        functools.partial(feature_kernel, res),
        out_shape=shape((seqs * res, channels), bf16),
        in_specs=[vmem] * 6,
        out_specs=vmem,
        compiler_params=params,
        name="features",
    )(spread, first, second, scale, scaled, inv)
    dout, dhid, dback = pl.pallas_call(
        sum_kernel,
        out_shape=(
            shape((outer_width, pair_width), f32),
            shape((pair_width, hid), f32),
            shape((hid, pair_width), f32),
        ),
        in_specs=[vmem] * 6,
        out_specs=[vmem] * 3,
        compiler_params=params,
        name="sums_over_depth",
    )(dout, dhid, dback, *other_weights)
    total = part.astype(f32)
    kept = lax.optimization_barrier(total.astype(bf16))
    near_ones = [swap_depth(kept), swap_col(kept, Y_PARTNER), swap_both(kept, Y_PARTNER)]
    near_ones, feat = lax.optimization_barrier((near_ones, feat))
    total = pairwise_sum([block.astype(f32) for block in [kept] + near_ones])
    kept = lax.optimization_barrier(total.astype(bf16))
    far_ones = along_z(jnp.broadcast_to(kept, (line,) + kept.shape))
    far_ones, dout, dhid, dback = lax.optimization_barrier((far_ones, dout, dhid, dback))
    total = pairwise_sum([far_ones[at].astype(f32) for at in range(line)])
    return (
        feat.reshape(seqs, res, channels),
        couple.reshape(res, pair_cols, pair_width),
        total[:width].T,
        total[width:].T,
        dout,
        dhid,
        dback,
    )


def on_device(alignment_activations, *others):
    cols = lax.axis_size("col")
    residues = alignment_activations.shape[1] * cols
    plan = whole_plan if cols == 8 and residues <= FEW_RESIDUES else split_plan
    return plan(alignment_activations, *others)


def solution(mesh):
    in_specs = (
        P(("group", "depth"), "col", None),
        P(("group", "depth"), "col"),
        P(("group", "col"), "depth", None),
        P(("group", "col"), "depth"),
        P(("group", "col"), "depth", None),
        P(),
        P(),
        P(),
        P(),
        P(),
        P(),
        P(),
    )
    out_specs = (
        P(("group", "depth"), "col", None),
        P(("group", "col"), "depth", None),
        P("group", None),
        P("group", None),
        P("group", None),
        P("group", None),
        P("group", None),
    )
    return jax.shard_map(
        on_device, mesh=mesh, in_specs=in_specs, out_specs=out_specs, check_vma=False
    )
```

```python
import functools

import jax
import jax.numpy as jnp
from jax import lax
from jax.experimental import pallas as pl
from jax.experimental.pallas import tpu as pltpu
from jax.sharding import PartitionSpec as P

epsilon = 1e-05
highest = lax.Precision.HIGHEST


def norm_pieces(entries_drawn):
    center = entries_drawn - jnp.mean(entries_drawn, axis=-1, keepdims=True)
    inv_std = lax.rsqrt(jnp.mean(center * center, axis=-1, keepdims=True) + epsilon)
    return (center * inv_std, inv_std)


def standardize_adjoint(grad_scaled, scaled, inv_std):
    mean_grad = jnp.mean(grad_scaled, axis=-1, keepdims=True)
    mean_cross = jnp.mean(grad_scaled * scaled, axis=-1, keepdims=True)
    return inv_std * (grad_scaled - mean_grad - scaled * mean_cross)


def silu_pieces(pre_act):
    sigma = jax.nn.sigmoid(pre_act)
    return (pre_act * sigma, sigma * (1.0 + pre_act * (1.0 - sigma)))


def split_plan(
    alignment_activations,
    alignment_mask,
    pair_activation_input,
    pair_update_mask,
    pair_output_gradient,
    layer_scale_factor,
    first_projector,
    second_projector,
    output_weight,
    pair_norm_gain,
    hidden_weight,
    back_weight,
):
    sequence_row_block, residue_row_block, channel_total = alignment_activations.shape
    proj_width = first_projector.shape[1]
    outer_width = proj_width * proj_width
    depth_count = lax.axis_size("depth")
    residues = residue_row_block * lax.axis_size("col")
    pair_cols = pair_activation_input.shape[1]
    pair_width = pair_activation_input.shape[2]
    col_block = min(64, pair_cols)
    block_count = pair_cols // col_block
    standardized_features, reciprocal_spread = norm_pieces(
        alignment_activations.astype(jnp.float32)
    )
    normalized_rows = (standardized_features * layer_scale_factor).astype(jnp.bfloat16)
    mask_floating = alignment_mask.astype(jnp.float32)
    left_proj = (
        jnp.dot(normalized_rows, first_projector, preferred_element_type=jnp.float32)
        * mask_floating[:, :, None]
    ).astype(jnp.bfloat16)
    right_proj = (
        jnp.dot(normalized_rows, second_projector, preferred_element_type=jnp.float32)
        * mask_floating[:, :, None]
    ).astype(jnp.bfloat16)
    right_flat = right_proj.reshape(sequence_row_block, residue_row_block * proj_width)
    mask_converted = alignment_mask.astype(jnp.bfloat16)
    seq_total = left_proj.shape[0]
    gathered, gathered_mask = (
        lax.all_gather(right_flat, "col", axis=1, tiled=True),
        lax.all_gather(mask_converted, "col", axis=1, tiled=True),
    )
    right_blocks = gathered.reshape(seq_total, depth_count, pair_cols, proj_width)
    mask_blocks = gathered_mask.reshape(seq_total, depth_count, pair_cols)
    block_depth = right_blocks.shape[1]
    out_wide = output_weight.astype(jnp.float32)

    def partial_outer(col_start):
        right_piece = lax.dynamic_slice_in_dim(right_blocks, col_start, col_block, 2)
        outer_part = jnp.einsum(
            "sic,sejd->iejcd", left_proj, right_piece, preferred_element_type=jnp.float32
        )
        return (
            outer_part.reshape(residue_row_block, block_depth, col_block, outer_width),
            right_piece,
        )

    def forward_step(step_index, loop_state):
        projected, pair_count = loop_state
        col_start = step_index * col_block
        outer_part, right_piece = partial_outer(col_start)
        mask_piece = lax.dynamic_slice_in_dim(mask_blocks, col_start, col_block, 2).astype(
            jnp.float32
        )
        count_part = jnp.einsum("si,sej->iej", mask_floating, mask_piece, precision=highest)
        outer_mine, count_mine = (
            lax.psum_scatter(
                outer_part.astype(jnp.bfloat16), "depth", scatter_dimension=1, tiled=True
            ).astype(jnp.float32),
            lax.psum_scatter(
                count_part.astype(jnp.bfloat16), "depth", scatter_dimension=1, tiled=True
            ).astype(jnp.float32),
        )
        proj_mine = jnp.dot(
            outer_mine.reshape(residue_row_block * col_block, outer_width),
            out_wide,
            precision=highest,
        )
        proj_mine = proj_mine.reshape(residue_row_block, col_block, pair_width)
        count_mine = count_mine.reshape(residue_row_block, col_block)
        projected = lax.dynamic_update_slice_in_dim(projected, proj_mine, col_start, 1)
        pair_count = lax.dynamic_update_slice_in_dim(pair_count, count_mine, col_start, 1)
        return (projected, pair_count)

    projected, pair_count = lax.fori_loop(
        0,
        block_count,
        forward_step,
        (
            jnp.zeros((residue_row_block, pair_cols, pair_width), jnp.float32),
            jnp.zeros((residue_row_block, pair_cols), jnp.float32),
        ),
    )
    count_column = pair_count.reshape(residue_row_block * pair_cols, 1)
    mid_act = (
        pair_activation_input.reshape(residue_row_block * pair_cols, pair_width).astype(jnp.float32)
        + projected.reshape(residue_row_block * pair_cols, pair_width) / count_column
    )
    pair_scaled, pair_inv = norm_pieces(mid_act)
    pair_normed = (pair_scaled * pair_norm_gain).astype(jnp.bfloat16)
    pre_act = jnp.dot(pair_normed, hidden_weight, preferred_element_type=jnp.float32)
    act_value, act_slope = silu_pieces(pre_act)
    hidden = act_value.astype(jnp.bfloat16)
    masked_grad = (
        pair_output_gradient * pair_update_mask.astype(jnp.bfloat16)[:, :, None]
    ).reshape(residue_row_block * pair_cols, pair_width)
    final_matrix_derivative = jnp.dot(hidden.T, masked_grad, preferred_element_type=jnp.float32)
    back_prod = jnp.dot(masked_grad, back_weight.T, preferred_element_type=jnp.float32)
    grad_hidden = (back_prod * act_slope).astype(jnp.bfloat16)
    middle_matrix_derivative = jnp.dot(
        pair_normed.T, grad_hidden, preferred_element_type=jnp.float32
    )
    grad_scaled = (
        jnp.dot(grad_hidden, hidden_weight.T, preferred_element_type=jnp.float32) * pair_norm_gain
    )
    grad_mid = pair_output_gradient.reshape(residue_row_block * pair_cols, pair_width).astype(
        jnp.float32
    ) + standardize_adjoint(grad_scaled, pair_scaled, pair_inv)
    couple_features_derivative = grad_mid.astype(jnp.bfloat16).reshape(
        residue_row_block, pair_cols, pair_width
    )
    grad_opm = (
        (grad_mid / count_column)
        .astype(jnp.bfloat16)
        .reshape(residue_row_block, pair_cols, pair_width)
    )
    full_opm = lax.all_gather(grad_opm, "depth", axis=1, tiled=True).reshape(
        residue_row_block, depth_count, pair_cols, pair_width
    )

    def backward_step(step_index, loop_state):
        grad_left_acc, grad_out, right_term = loop_state
        col_start = step_index * col_block
        outer_part, right_piece = partial_outer(col_start)
        opm_piece = lax.dynamic_slice_in_dim(full_opm, col_start, col_block, 2).reshape(
            residue_row_block * block_depth * col_block, pair_width
        )
        grad_out = grad_out + jnp.dot(
            outer_part.reshape(residue_row_block * block_depth * col_block, outer_width).T,
            opm_piece.astype(jnp.float32),
            precision=highest,
        )
        grad_outer = jnp.dot(opm_piece, output_weight.T, preferred_element_type=jnp.float32).astype(
            jnp.bfloat16
        )
        grad_outer = grad_outer.reshape(
            residue_row_block, block_depth, col_block, proj_width, proj_width
        )
        grad_left_acc = grad_left_acc + jnp.einsum(
            "iejcd,sejd->sic", grad_outer, right_piece, preferred_element_type=jnp.float32
        )
        piece_term = jnp.einsum(
            "iejcd,sic->ejsd", grad_outer, left_proj, preferred_element_type=jnp.float32
        )
        piece_term = piece_term.reshape(block_depth, col_block, seq_total * proj_width)
        right_term = lax.dynamic_update_slice_in_dim(right_term, piece_term, col_start, 1)
        return (grad_left_acc, grad_out, right_term)

    grad_left_acc, result_matrix_derivative, right_term = lax.fori_loop(
        0,
        block_count,
        backward_step,
        (
            jnp.zeros((seq_total, residue_row_block, proj_width), jnp.float32),
            jnp.zeros((outer_width, pair_width), jnp.float32),
            jnp.zeros((block_depth, pair_cols, seq_total * proj_width), jnp.float32),
        ),
    )
    grad_right_sum = lax.psum_scatter(
        right_term.reshape(residues, seq_total * proj_width), "col", scatter_dimension=0, tiled=True
    )
    grad_right_acc = jnp.transpose(
        grad_right_sum.reshape(residue_row_block, seq_total, proj_width), (1, 0, 2)
    )
    grad_left = (grad_left_acc * mask_floating[:, :, None]).astype(jnp.bfloat16)
    grad_right = (grad_right_acc * mask_floating[:, :, None]).astype(jnp.bfloat16)
    normed_rows = normalized_rows.reshape(sequence_row_block * residue_row_block, channel_total)
    first_projector_derivative = jnp.dot(
        normed_rows.T,
        grad_left.reshape(sequence_row_block * residue_row_block, proj_width),
        preferred_element_type=jnp.float32,
    )
    second_projector_derivative = jnp.dot(
        normed_rows.T,
        grad_right.reshape(sequence_row_block * residue_row_block, proj_width),
        preferred_element_type=jnp.float32,
    )
    standardized_derivative = jnp.dot(
        grad_left, first_projector.T, preferred_element_type=jnp.float32
    ) + jnp.dot(grad_right, second_projector.T, preferred_element_type=jnp.float32)
    features_derivative = standardize_adjoint(
        standardized_derivative * layer_scale_factor, standardized_features, reciprocal_spread
    ).astype(jnp.bfloat16)
    weight_sums = lax.psum(
        (
            first_projector_derivative,
            second_projector_derivative,
            result_matrix_derivative,
            middle_matrix_derivative,
            final_matrix_derivative,
        ),
        ("depth", "col"),
    )
    return (
        features_derivative,
        couple_features_derivative,
        weight_sums[0],
        weight_sums[1],
        weight_sums[2],
        weight_sums[3],
        weight_sums[4],
    )


FEW_RESIDUES = 32
MASK_ROWS = 16
Z_PARTNERS = (2, 4, 6)
Y_PARTNER = 1


def butterfly(blocks, group):
    lane_group = lax.broadcasted_iota(jnp.int32, blocks[0].shape, 1) // group
    width = 4 * group
    for bit in (2, 1):
        low = (lane_group & bit) == 0
        swapped = list(blocks)
        for at in range(4):
            if at & bit:
                continue
            here, there = blocks[at], blocks[at | bit]
            moving = jnp.where(low, there, here)
            if bit == 2:
                moved = pltpu.roll(moving, 2 * group, 1)
            else:
                moved = jnp.where(
                    low, pltpu.roll(moving, width - group, 1), pltpu.roll(moving, group, 1)
                )
            swapped[at] = jnp.where(low, here, moved)
            swapped[at | bit] = jnp.where(low, moved, there)
        blocks = swapped
    return blocks


def wide_projector(first_ref, second_ref, copies):
    return jnp.concatenate([first_ref[...]] * copies + [second_ref[...]] * copies, axis=0)


def pre_kernel(
    ids_ref,
    x_hbm,
    maskt_hbm,
    pmask_hbm,
    scale_hbm,
    first_hbm,
    second_hbm,
    gain_hbm,
    act_hbm,
    grad_hbm,
    sent_ref,
    scale_ref,
    first_ref,
    second_ref,
    gain_ref,
    normed_ref,
    scaled_ref,
    inv_ref,
    wide_ref,
    tile_ref,
    x_ref,
    maskt_ref,
    pmask_ref,
    sems,
):
    res, seqs = maskt_ref.shape
    pairs = act_hbm.shape[0]
    first_pair = 2 * seqs + MASK_ROWS
    copies = [
        pltpu.make_async_copy(source, target, sems.at[at])
        for at, (source, target) in enumerate(
            (
                (x_hbm, x_ref),
                (maskt_hbm, maskt_ref),
                (pmask_hbm, pmask_ref),
                (scale_hbm, scale_ref),
                (first_hbm, first_ref),
                (second_hbm, second_ref),
                (gain_hbm, gain_ref),
                (act_hbm, sent_ref.at[0, pl.ds(first_pair, pairs), :]),
                (grad_hbm, sent_ref.at[0, pl.ds(first_pair + pairs, pairs), :]),
            )
        )
    ]
    for copy in copies:
        copy.start()
    for copy in copies:
        copy.wait()
    lanes = sent_ref.shape[2]
    group = lanes // res
    scaled, inv = norm_pieces(
        x_ref[...].astype(jnp.float32).reshape(seqs * res, x_ref.shape[2])
    )
    scaled_ref[...] = scaled
    inv_ref[...] = inv
    normed = (scaled * scale_ref[...]).astype(jnp.bfloat16)
    normed_ref[...] = normed
    wide = lax.dot_general(
        normed,
        wide_projector(first_ref, second_ref, res),
        (((1,), (1,)), ((), ())),
        preferred_element_type=jnp.float32,
    )
    for at in range(2):
        wide_ref[at] = wide[:, at * lanes : (at + 1) * lanes]
    tile_ref[...] = jnp.zeros(tile_ref.shape, jnp.float32)
    mask = maskt_ref[...].astype(jnp.float32)
    tile_ref[0:res, 0:seqs] = mask
    spread = (
        lax.broadcasted_iota(jnp.int32, (MASK_ROWS, lanes), 1) // group
        == lax.broadcasted_iota(jnp.int32, (MASK_ROWS, lanes), 0)
    ).astype(jnp.float32)
    mask_lanes = lax.dot_general(
        tile_ref[...], spread, (((0,), (0,)), ((), ())), preferred_element_type=jnp.float32
    )[:seqs]
    twice = jnp.concatenate([mask] * (lanes // seqs), axis=1)
    here = lax.broadcasted_iota(jnp.int32, (res, lanes), 1) // seqs == ids_ref[0]
    tile_ref[0:res, :] = jnp.where(here, twice, 0.0)
    tile_ref[res : 2 * res, 0 : pmask_ref.shape[1]] = pmask_ref[...].astype(jnp.float32)
    lane_group = lax.broadcasted_iota(jnp.int32, (seqs, lanes), 1) // group
    for at in range(2):
        both = wide_ref[at, pl.ds(0, seqs, stride=res), :]
        for r in range(1, res):
            both = jnp.where(
                lane_group == r, wide_ref[at, pl.ds(r, seqs, stride=res), :], both
            )
        sent_ref[0, at * seqs : (at + 1) * seqs, :] = (both * mask_lanes).astype(jnp.bfloat16)
    sent_ref[0, 2 * seqs : first_pair, :] = tile_ref[...].astype(jnp.bfloat16)


def outer_kernel(
    sizes,
    orders,
    ids_ref,
    near_ref,
    far_ref,
    other_near_ref,
    other_far_ref,
    wturn_ref,
    outer_ref,
    proj_out_ref,
    cnt_ref,
    pm_ref,
    maskt_ref,
    got_ref,
    leftn_ref,
    mine_ref,
    turn_ref,
    cntl_ref,
    pml_ref,
):
    seqs, res, pair_cols, width = sizes
    depths, cols = got_ref.shape[0], got_ref.shape[1]
    residues = cols * res
    lanes = res * width
    half_cols = pair_cols // res
    me_depth = ids_ref[0]
    me_col = ids_ref[1]
    f32, bf16 = jnp.float32, jnp.bfloat16

    for order, mine, other in zip(orders, (near_ref, far_ref), (other_near_ref, other_far_ref)):
        for at, partner in enumerate(order):
            got_ref[me_depth, me_col ^ partner] = mine[at]
            got_ref[1 - me_depth, me_col ^ partner] = other[at]

    for e in range(depths):
        for k in range(cols):
            leftn_ref[e * seqs : (e + 1) * seqs, k * lanes : (k + 1) * lanes] = got_ref[
                e, k, 0:seqs, :
            ]
    for k in range(half_cols):
        block = jnp.concatenate(
            [
                got_ref[e, me_depth * half_cols + k, seqs : 2 * seqs, :]
                for e in range(depths)
            ],
            axis=0,
        ).astype(f32)
        turn_ref[k * lanes : (k + 1) * lanes, :] = block.T
    for d in range(width):
        mine_ref[d * pair_cols : (d + 1) * pair_cols, :] = turn_ref[
            pl.ds(d, pair_cols, stride=width), :
        ].astype(bf16)

    base = 2 * seqs
    pair_lane = lax.broadcasted_iota(jnp.int32, (pair_cols, lanes), 1)
    pair_row = lax.broadcasted_iota(jnp.int32, (pair_cols, lanes), 0)
    for k in range(cols):
        tiles = [got_ref[e, k, base : base + MASK_ROWS, :].astype(f32) for e in range(depths)]
        maskt_ref[k * res : (k + 1) * res, :] = tiles[0][0:res] + tiles[1][0:res]
        own = got_ref[me_depth, k, base : base + MASK_ROWS, :].astype(f32)
        for r in range(res):
            row = own[res + r : res + r + 1, :]
            first = (k * res + r) * pair_cols
            pml_ref[first : first + pair_cols, :] = jnp.where(
                pair_lane == pair_row, row, 0.0
            ).astype(bf16)
    maskt = maskt_ref[...]
    cols_mask = maskt_ref[pl.ds(pl.multiple_of(me_depth * pair_cols, pair_cols), pair_cols), :]
    for i in range(residues):
        cntl_ref[i * pair_cols : (i + 1) * pair_cols, :] = (maskt[i : i + 1, :] * cols_mask).astype(
            bf16
        )
    ones = jnp.ones((lanes, lanes), bf16)
    cnt_ref[...] = jnp.dot(cntl_ref[...], ones, preferred_element_type=f32)
    pm_ref[...] = jnp.dot(pml_ref[...], ones, preferred_element_type=f32).astype(bf16)

    for dh in range(width // 4):
        prod = jnp.dot(
            mine_ref[dh * 4 * pair_cols : (dh + 1) * 4 * pair_cols, :],
            leftn_ref[...],
            preferred_element_type=f32,
        )
        for k in range(cols):
            piece = prod[:, k * lanes : (k + 1) * lanes]
            turned = butterfly(
                [piece[a * pair_cols : (a + 1) * pair_cols] for a in range(4)], width
            )
            for il in range(res):
                first = (k * res + il) * pair_cols
                outer_ref[first : first + pair_cols, dh * lanes : (dh + 1) * lanes] = turned[
                    il
                ].astype(bf16)
    proj_out_ref[...] = jnp.dot(outer_ref[...], wturn_ref[...], preferred_element_type=f32)


def turn_kernel(
    sizes,
    orders,
    ids_ref,
    near_ref,
    far_ref,
    other_near_ref,
    other_far_ref,
    rightt_ref,
    leftt_ref,
    got_ref,
    turn_ref,
):
    seqs, res, _, width = sizes
    depths, cols = got_ref.shape[0], got_ref.shape[1]
    lanes = res * width
    residues = res * cols
    me_depth = ids_ref[0]
    me_col = ids_ref[1]
    for order, mine, other in zip(orders, (near_ref, far_ref), (other_near_ref, other_far_ref)):
        for at, partner in enumerate(order):
            got_ref[me_depth, me_col ^ partner] = mine[at, 0 : 2 * seqs, :]
            got_ref[1 - me_depth, me_col ^ partner] = other[at, 0 : 2 * seqs, :]
    for at, out in ((0, leftt_ref), (1, rightt_ref)):
        for k in range(cols):
            block = jnp.concatenate(
                [got_ref[e, k, at * seqs : (at + 1) * seqs, :] for e in range(depths)], axis=0
            ).astype(jnp.float32)
            turn_ref[k * lanes : (k + 1) * lanes, :] = block.T
        for d in range(width):
            out[d * residues : (d + 1) * residues, :] = turn_ref[
                pl.ds(d, residues, stride=width), :
            ].astype(jnp.bfloat16)


def transition_kernel(
    sizes,
    orders,
    ids_ref,
    near_ref,
    far_ref,
    proj_out_ref,
    cnt_ref,
    pm_ref,
    gain_ref,
    hid_ref,
    back_ref,
    couple_ref,
    opm_ref,
    pn_ref,
    gh_ref,
    hidden_ref,
    mg_ref,
    pgot_ref,
    gmid_ref,
):
    seqs, res, pair_cols, width = sizes
    per = res * pair_cols
    cols = pgot_ref.shape[0]
    me_col = ids_ref[1]
    f32, bf16 = jnp.float32, jnp.bfloat16
    for order, mine in zip(orders, (near_ref, far_ref)):
        for at, partner in enumerate(order):
            pgot_ref[me_col ^ partner] = mine[at]
    gain = gain_ref[...]
    chunk = 2 * per
    for at in range(cols // 2):
        rows = slice(at * chunk, (at + 1) * chunk)
        act, grad = [
            jnp.concatenate(
                [pgot_ref[2 * at + b, w * per : (w + 1) * per, :] for b in range(2)], axis=0
            )
            for w in range(2)
        ]
        count = cnt_ref[rows, :]
        mid = act.astype(f32) + proj_out_ref[rows, :] / count
        scaled, inv = norm_pieces(mid)
        normed = (scaled * gain).astype(bf16)
        pn_ref[rows, :] = normed
        pre = jnp.dot(normed, hid_ref[...], preferred_element_type=f32)
        value, slope = silu_pieces(pre)
        hidden_ref[rows, :] = value.astype(bf16)
        masked = grad * pm_ref[rows, :]
        mg_ref[rows, :] = masked
        back = lax.dot_general(
            masked, back_ref[...], (((1,), (1,)), ((), ())), preferred_element_type=f32
        )
        ghid = (back * slope).astype(bf16)
        gh_ref[rows, :] = ghid
        gsc = (
            lax.dot_general(
                ghid, hid_ref[...], (((1,), (1,)), ((), ())), preferred_element_type=f32
            )
            * gain
        )
        gmid = grad.astype(f32) + standardize_adjoint(gsc, scaled, inv)
        gmid_ref[rows, :] = gmid
        opm_ref[rows, :] = (gmid / count).astype(bf16)
    couple_ref[...] = gmid_ref[pl.ds(pl.multiple_of(me_col * per, per), per), :].astype(bf16)


def projector_kernel(
    sizes,
    ids_ref,
    opm_ref,
    other_opm_ref,
    rightt_ref,
    leftt_ref,
    wout_ref,
    wturn_ref,
    maskt_ref,
    normed_ref,
    far_normed_ref,
    other_normed_ref,
    other_far_normed_ref,
    part_ref,
    spread_ref,
    gf_ref,
    grow_ref,
    gcol_ref,
    gor_ref,
    goc_ref,
    gs_ref,
    rows_ref,
):
    seqs, res, pair_cols, width = sizes
    depths, half = gf_ref.shape[0], gf_ref.shape[1]
    residues = half // pair_cols
    lanes = res * width
    here = 2 * res
    me_depth = ids_ref[0]
    me_col = ids_ref[1]
    me_y = me_col % 2
    first_here = (me_col // 2) * here
    f32, bf16 = jnp.float32, jnp.bfloat16
    gf_ref[me_depth] = opm_ref[...].astype(f32)
    gf_ref[1 - me_depth] = other_opm_ref[...].astype(f32)
    for y, e, block in (
        (me_y, me_depth, normed_ref),
        (1 - me_y, me_depth, far_normed_ref),
        (me_y, 1 - me_depth, other_normed_ref),
        (1 - me_y, 1 - me_depth, other_far_normed_ref),
    ):
        rows_ref[y, e] = block[...]

    for il in range(here):
        for e in range(depths):
            first = pl.multiple_of((first_here + il) * pair_cols, pair_cols)
            grow_ref[il * residues + e * pair_cols : il * residues + (e + 1) * pair_cols, :] = (
                gf_ref[e, pl.ds(first, pair_cols), :].astype(bf16)
            )
    my_half = first_here // pair_cols
    my_first = first_here - my_half * pair_cols
    for jl in range(here):
        gcol_ref[jl * residues : (jl + 1) * residues, :] = gf_ref[
            my_half, pl.ds(my_first + jl, residues, stride=pair_cols), :
        ].astype(bf16)
    for lhs, weight, out in ((grow_ref, wturn_ref, gor_ref), (gcol_ref, wout_ref, goc_ref)):
        for dh in range(width // 4):
            piece = lax.dot_general(
                lhs[...],
                weight[dh * lanes : (dh + 1) * lanes, :],
                (((1,), (1,)), ((), ())),
                preferred_element_type=f32,
            )
            for y in range(2):
                turned = butterfly(
                    [
                        piece[(y * res + a) * residues : (y * res + a + 1) * residues]
                        for a in range(4)
                    ],
                    width,
                )
                for dl in range(4):
                    first = (dh * 4 + dl) * residues
                    out[first : first + residues, y * lanes : (y + 1) * lanes] = turned[dl].astype(
                        bf16
                    )
    group = lax.broadcasted_iota(jnp.int32, (here, here * width), 1) // width
    spread = (group == lax.broadcasted_iota(jnp.int32, (here, here * width), 0)).astype(f32)
    mask_lanes = lax.dot_general(
        maskt_ref[pl.ds(pl.multiple_of(first_here, here), here), :],
        spread,
        (((0,), (0,)), ((), ())),
        preferred_element_type=f32,
    )
    lane_group = lax.broadcasted_iota(jnp.int32, (seqs, lanes), 1) // width
    for at, (lhs, rhs) in enumerate(((rightt_ref, gor_ref), (leftt_ref, goc_ref))):
        total = lax.dot_general(
            lhs[...], rhs[...], (((0,), (0,)), ((), ())), preferred_element_type=f32
        )
        total = (total * mask_lanes).astype(bf16).astype(f32)
        for y in range(2):
            for e in range(depths):
                block = total[e * seqs : (e + 1) * seqs, y * lanes : (y + 1) * lanes]
                for r in range(res):
                    gs_ref[at, y, e, pl.ds(r, seqs, stride=res), :] = jnp.where(
                        lane_group == r, block, 0.0
                    )
    spread_ref[...] = jnp.concatenate(
        [gs_ref[0, me_y, me_depth], gs_ref[1, me_y, me_depth]], axis=1
    ).astype(bf16)
    rows = rows_ref.shape[2]
    for at in range(2):
        cross = lax.dot_general(
            gs_ref[at].reshape(2 * depths * rows, lanes).astype(bf16),
            rows_ref[...].reshape(2 * depths * rows, rows_ref.shape[3]),
            (((0,), (0,)), ((), ())),
            preferred_element_type=f32,
        )
        total = cross[:width]
        for r in range(1, res):
            total = total + cross[r * width : (r + 1) * width]
        part_ref[at * width : (at + 1) * width, :] = total.astype(bf16)


def out_weight_kernel(outer_ref, opm_ref, dout_ref, turn_ref):
    width = int(dout_ref.shape[0] ** 0.5 + 0.5)
    turn_ref[...] = lax.dot_general(
        outer_ref[...], opm_ref[...], (((0,), (0,)), ((), ())), preferred_element_type=jnp.float32
    )
    for c in range(width):
        dout_ref[c * width : (c + 1) * width, :] = turn_ref[
            pl.ds(c, width, stride=width), :
        ].astype(jnp.bfloat16)


def transition_weight_kernel(pn_ref, gh_ref, hidden_ref, mg_ref, dhid_ref, dback_ref):
    for lhs, rhs, out in ((pn_ref, gh_ref, dhid_ref), (hidden_ref, mg_ref, dback_ref)):
        out[...] = lax.dot_general(
            lhs[...], rhs[...], (((0,), (0,)), ((), ())), preferred_element_type=jnp.float32
        ).astype(jnp.bfloat16)


def sum_kernel(*refs):
    for mine, other, out in zip(refs[0:3], refs[3:6], refs[6:9]):
        out[...] = mine[...].astype(jnp.float32) + other[...].astype(jnp.float32)


def feature_kernel(
    copies, spread_ref, first_ref, second_ref, scale_ref, scaled_ref, inv_ref, feat_ref
):
    back = jnp.dot(
        spread_ref[...],
        wide_projector(first_ref, second_ref, copies),
        preferred_element_type=jnp.float32,
    )
    feat_ref[...] = standardize_adjoint(
        back * scale_ref[...], scaled_ref[...], inv_ref[...]
    ).astype(jnp.bfloat16)


def swap_depth(block):
    return lax.ppermute(block, "depth", [(0, 1), (1, 0)])


def pairwise_sum(blocks):
    while len(blocks) > 1:
        blocks = [blocks[at] + blocks[at + 1] for at in range(0, len(blocks), 2)]
    return blocks[0]


def swap_col(block, partner):
    count = lax.axis_size("col")
    return lax.ppermute(block, "col", [(at, at ^ partner) for at in range(count)])


def whole_plan(
    alignment_activations,
    alignment_mask,
    pair_activation_input,
    pair_update_mask,
    pair_output_gradient,
    layer_scale_factor,
    first_projector,
    second_projector,
    output_weight,
    pair_norm_gain,
    hidden_weight,
    back_weight,
):
    seqs, res, channels = alignment_activations.shape
    width = first_projector.shape[1]
    outer_width = width * width
    cols = lax.axis_size("col")
    depths = lax.axis_size("depth")
    residues = res * cols
    pair_cols, pair_width = pair_activation_input.shape[1:]
    hid = hidden_weight.shape[1]
    per = res * pair_cols
    lanes = res * width
    rows = 2 * seqs + MASK_ROWS
    half = residues * pair_cols
    f32, bf16 = jnp.float32, jnp.bfloat16
    ids = jnp.stack([lax.axis_index("depth"), lax.axis_index("col")]).astype(jnp.int32)
    smem = pl.BlockSpec(memory_space=pltpu.SMEM)
    vmem = pl.BlockSpec(memory_space=pltpu.VMEM)
    params = pltpu.CompilerParams(vmem_limit_bytes=16 * 2**20)
    scale = layer_scale_factor.reshape(1, channels)
    first, second = first_projector.T, second_projector.T
    wturn = jnp.transpose(output_weight.reshape(width, width, pair_width), (1, 0, 2)).reshape(
        outer_width, pair_width
    )
    shape = jax.ShapeDtypeStruct
    sent, scale, first, second, gain, normed, scaled, inv = pl.pallas_call(
        pre_kernel,
        out_shape=(
            shape((1, rows + 2 * per, pair_width), bf16),
            shape((1, channels), f32),
            shape((width, channels), bf16),
            shape((width, channels), bf16),
            shape((1, pair_width), f32),
            shape((seqs * res, channels), bf16),
            shape((seqs * res, channels), f32),
            shape((seqs * res, 1), f32),
        ),
        in_specs=[smem] + [pl.BlockSpec(memory_space=pltpu.HBM)] * 9,
        out_specs=[vmem] * 8,
        scratch_shapes=[
            pltpu.VMEM((2, seqs * res, lanes), f32),
            pltpu.VMEM((MASK_ROWS, lanes), f32),
            pltpu.VMEM((seqs, res, channels), bf16),
            pltpu.VMEM((res, seqs), jnp.int32),
            pltpu.VMEM((res, pair_cols), jnp.int32),
            pltpu.SemaphoreType.DMA((9,)),
        ],
        compiler_params=params,
        name="project",
    )(
        ids,
        *[
            pltpu.with_memory_space_constraint(array, pltpu.HBM)
            for array in (
                alignment_activations,
                alignment_mask.T,
                pair_update_mask,
                scale,
                first,
                second,
                pair_norm_gain.reshape(1, pair_width),
                pair_activation_input.reshape(per, pair_width),
                pair_output_gradient.reshape(per, pair_width),
            )
        ],
    )
    near_order = (0,) + Z_PARTNERS
    far_order = tuple(at ^ Y_PARTNER for at in near_order)
    blocks = lax.optimization_barrier(
        jnp.concatenate([sent] + [swap_col(sent, partner) for partner in Z_PARTNERS])
    )
    near, pair_near = blocks[:, :rows], blocks[:, rows:]
    far_normed = swap_col(normed, Y_PARTNER)
    other_normed, other_far_normed = swap_depth(normed), swap_depth(far_normed)
    near, far_normed, other_normed = lax.optimization_barrier((near, far_normed, other_normed))
    far = swap_col(near, Y_PARTNER)
    pair_far = swap_col(pair_near, Y_PARTNER)
    other_near, other_far = swap_depth(near), swap_depth(far)
    sizes = (seqs, res, pair_cols, width)
    orders = (near_order, far_order)
    outer, proj_out, cnt, pm, maskt = pl.pallas_call(
        functools.partial(outer_kernel, sizes, orders),
        out_shape=(
            shape((half, outer_width), bf16),
            shape((half, pair_width), f32),
            shape((half, lanes), f32),
            shape((half, lanes), bf16),
            shape((residues, depths * seqs), f32),
        ),
        in_specs=[smem] + [vmem] * 5,
        out_specs=[vmem] * 5,
        scratch_shapes=[
            pltpu.VMEM((depths, cols, rows, pair_width), bf16),
            pltpu.VMEM((depths * seqs, residues * width), bf16),
            pltpu.VMEM((pair_cols * width, depths * seqs), bf16),
            pltpu.VMEM((pair_cols * width, depths * seqs), f32),
            pltpu.VMEM((half, lanes), bf16),
            pltpu.VMEM((half, lanes), bf16),
        ],
        compiler_params=params,
        name="outer_products",
    )(ids, near, far, other_near, other_far, wturn)
    other_near, other_far, proj_out = lax.optimization_barrier((other_near, other_far, proj_out))
    rightt, leftt = pl.pallas_call(
        functools.partial(turn_kernel, sizes, orders),
        out_shape=(
            shape((residues * width, depths * seqs), bf16),
            shape((residues * width, depths * seqs), bf16),
        ),
        in_specs=[smem] + [vmem] * 4,
        out_specs=[vmem] * 2,
        scratch_shapes=[
            pltpu.VMEM((depths, cols, 2 * seqs, pair_width), bf16),
            pltpu.VMEM((residues * width, depths * seqs), f32),
        ],
        compiler_params=params,
        name="turned",
    )(ids, near, far, other_near, other_far)
    pair_far, rightt, leftt, proj_out, other_far_normed = lax.optimization_barrier(
        (pair_far, rightt, leftt, proj_out, other_far_normed)
    )
    couple, opm, pn, gh, hidden, mg = pl.pallas_call(
        functools.partial(transition_kernel, sizes, orders),
        out_shape=(
            shape((per, pair_width), bf16),
            shape((half, pair_width), bf16),
            shape((half, pair_width), bf16),
            shape((half, hid), bf16),
            shape((half, hid), bf16),
            shape((half, pair_width), bf16),
        ),
        in_specs=[smem] + [vmem] * 8,
        out_specs=[vmem] * 6,
        scratch_shapes=[
            pltpu.VMEM((cols, 2 * per, pair_width), bf16),
            pltpu.VMEM((half, pair_width), f32),
        ],
        compiler_params=params,
        name="transition",
    )(
        ids,
        pair_near,
        pair_far,
        proj_out,
        cnt,
        pm,
        gain,
        hidden_weight,
        back_weight,
    )
    dout = pl.pallas_call(
        out_weight_kernel,
        out_shape=shape((outer_width, pair_width), bf16),
        in_specs=[vmem] * 2,
        out_specs=vmem,
        scratch_shapes=[pltpu.VMEM((outer_width, pair_width), f32)],
        compiler_params=params,
        name="out_weight",
    )(outer, opm)
    dhid, dback = pl.pallas_call(
        transition_weight_kernel,
        out_shape=(shape((pair_width, hid), bf16), shape((hid, pair_width), bf16)),
        in_specs=[vmem] * 4,
        out_specs=[vmem] * 2,
        compiler_params=params,
        name="transition_weights",
    )(pn, gh, hidden, mg)
    other_opm, dout, dhid, dback = lax.optimization_barrier((swap_depth(opm), dout, dhid, dback))
    other_weights = [swap_depth(block) for block in (dout, dhid, dback)]
    part, spread = pl.pallas_call(
        functools.partial(projector_kernel, sizes),
        out_shape=(
            shape((2 * width, channels), bf16),
            shape((seqs * res, 2 * lanes), bf16),
        ),
        in_specs=[smem] + [vmem] * 11,
        out_specs=[vmem] * 2,
        scratch_shapes=[
            pltpu.VMEM((depths, half, pair_width), f32),
            pltpu.VMEM((2 * res * residues, pair_width), bf16),
            pltpu.VMEM((2 * res * residues, pair_width), bf16),
            pltpu.VMEM((residues * width, 2 * lanes), bf16),
            pltpu.VMEM((residues * width, 2 * lanes), bf16),
            pltpu.VMEM((2, 2, depths, seqs * res, lanes), f32),
            pltpu.VMEM((2, depths, seqs * res, channels), bf16),
        ],
        compiler_params=params,
        name="projector_parts",
    )(
        ids,
        opm,
        other_opm,
        rightt,
        leftt,
        output_weight,
        wturn,
        maskt,
        normed,
        far_normed,
        other_normed,
        other_far_normed,
    )
    feat = pl.pallas_call(
        functools.partial(feature_kernel, res),
        out_shape=shape((seqs * res, channels), bf16),
        in_specs=[vmem] * 6,
        out_specs=vmem,
        compiler_params=params,
        name="features",
    )(spread, first, second, scale, scaled, inv)
    dout, dhid, dback = pl.pallas_call(
        sum_kernel,
        out_shape=(
            shape((outer_width, pair_width), f32),
            shape((pair_width, hid), f32),
            shape((hid, pair_width), f32),
        ),
        in_specs=[vmem] * 6,
        out_specs=[vmem] * 3,
        compiler_params=params,
        name="sums_over_depth",
    )(dout, dhid, dback, *other_weights)
    came = [swap_col(part, partner) for partner in Z_PARTNERS]
    came, feat, dout, dhid, dback = lax.optimization_barrier((came, feat, dout, dhid, dback))
    total = pairwise_sum([block.astype(f32) for block in [part] + came])
    return (
        feat.reshape(seqs, res, channels),
        couple.reshape(res, pair_cols, pair_width),
        total[:width].T,
        total[width:].T,
        dout,
        dhid,
        dback,
    )


def on_device(alignment_activations, *others):
    cols = lax.axis_size("col")
    residues = alignment_activations.shape[1] * cols
    plan = whole_plan if cols == 8 and residues <= FEW_RESIDUES else split_plan
    return plan(alignment_activations, *others)


def solution(mesh):
    in_specs = (
        P(("group", "depth"), "col", None),
        P(("group", "depth"), "col"),
        P(("group", "col"), "depth", None),
        P(("group", "col"), "depth"),
        P(("group", "col"), "depth", None),
        P(),
        P(),
        P(),
        P(),
        P(),
        P(),
        P(),
    )
    out_specs = (
        P(("group", "depth"), "col", None),
        P(("group", "col"), "depth", None),
        P("group", None),
        P("group", None),
        P("group", None),
        P("group", None),
        P("group", None),
    )
    return jax.shard_map(
        on_device, mesh=mesh, in_specs=in_specs, out_specs=out_specs, check_vma=False
    )
```

```python
import functools

import jax
import jax.numpy as jnp
from jax import lax
from jax.experimental import pallas as pl
from jax.experimental.pallas import tpu as pltpu
from jax.sharding import PartitionSpec as P

epsilon = 1e-05
highest = lax.Precision.HIGHEST


def norm_pieces(entries_drawn):
    center = entries_drawn - jnp.mean(entries_drawn, axis=-1, keepdims=True)
    inv_std = lax.rsqrt(jnp.mean(center * center, axis=-1, keepdims=True) + epsilon)
    return (center * inv_std, inv_std)


def standardize_adjoint(grad_scaled, scaled, inv_std):
    mean_grad = jnp.mean(grad_scaled, axis=-1, keepdims=True)
    mean_cross = jnp.mean(grad_scaled * scaled, axis=-1, keepdims=True)
    return inv_std * (grad_scaled - mean_grad - scaled * mean_cross)


def silu_pieces(pre_act):
    sigma = jax.nn.sigmoid(pre_act)
    return (pre_act * sigma, sigma * (1.0 + pre_act * (1.0 - sigma)))


def split_plan(
    alignment_activations,
    alignment_mask,
    pair_activation_input,
    pair_update_mask,
    pair_output_gradient,
    layer_scale_factor,
    first_projector,
    second_projector,
    output_weight,
    pair_norm_gain,
    hidden_weight,
    back_weight,
):
    sequence_row_block, residue_row_block, channel_total = alignment_activations.shape
    proj_width = first_projector.shape[1]
    outer_width = proj_width * proj_width
    depth_count = lax.axis_size("depth")
    residues = residue_row_block * lax.axis_size("col")
    pair_cols = pair_activation_input.shape[1]
    pair_width = pair_activation_input.shape[2]
    col_block = min(64, pair_cols)
    block_count = pair_cols // col_block
    standardized_features, reciprocal_spread = norm_pieces(
        alignment_activations.astype(jnp.float32)
    )
    normalized_rows = (standardized_features * layer_scale_factor).astype(jnp.bfloat16)
    mask_floating = alignment_mask.astype(jnp.float32)
    left_proj = (
        jnp.dot(normalized_rows, first_projector, preferred_element_type=jnp.float32)
        * mask_floating[:, :, None]
    ).astype(jnp.bfloat16)
    right_proj = (
        jnp.dot(normalized_rows, second_projector, preferred_element_type=jnp.float32)
        * mask_floating[:, :, None]
    ).astype(jnp.bfloat16)
    right_flat = right_proj.reshape(sequence_row_block, residue_row_block * proj_width)
    mask_converted = alignment_mask.astype(jnp.bfloat16)
    seq_total = left_proj.shape[0]
    gathered, gathered_mask = (
        lax.all_gather(right_flat, "col", axis=1, tiled=True),
        lax.all_gather(mask_converted, "col", axis=1, tiled=True),
    )
    right_blocks = gathered.reshape(seq_total, depth_count, pair_cols, proj_width)
    mask_blocks = gathered_mask.reshape(seq_total, depth_count, pair_cols)
    block_depth = right_blocks.shape[1]
    out_wide = output_weight.astype(jnp.float32)

    def partial_outer(col_start):
        right_piece = lax.dynamic_slice_in_dim(right_blocks, col_start, col_block, 2)
        outer_part = jnp.einsum(
            "sic,sejd->iejcd", left_proj, right_piece, preferred_element_type=jnp.float32
        )
        return (
            outer_part.reshape(residue_row_block, block_depth, col_block, outer_width),
            right_piece,
        )

    def forward_step(step_index, loop_state):
        projected, pair_count = loop_state
        col_start = step_index * col_block
        outer_part, right_piece = partial_outer(col_start)
        mask_piece = lax.dynamic_slice_in_dim(mask_blocks, col_start, col_block, 2).astype(
            jnp.float32
        )
        count_part = jnp.einsum("si,sej->iej", mask_floating, mask_piece, precision=highest)
        outer_mine, count_mine = (
            lax.psum_scatter(
                outer_part.astype(jnp.bfloat16), "depth", scatter_dimension=1, tiled=True
            ).astype(jnp.float32),
            lax.psum_scatter(
                count_part.astype(jnp.bfloat16), "depth", scatter_dimension=1, tiled=True
            ).astype(jnp.float32),
        )
        proj_mine = jnp.dot(
            outer_mine.reshape(residue_row_block * col_block, outer_width),
            out_wide,
            precision=highest,
        )
        proj_mine = proj_mine.reshape(residue_row_block, col_block, pair_width)
        count_mine = count_mine.reshape(residue_row_block, col_block)
        projected = lax.dynamic_update_slice_in_dim(projected, proj_mine, col_start, 1)
        pair_count = lax.dynamic_update_slice_in_dim(pair_count, count_mine, col_start, 1)
        return (projected, pair_count)

    projected, pair_count = lax.fori_loop(
        0,
        block_count,
        forward_step,
        (
            jnp.zeros((residue_row_block, pair_cols, pair_width), jnp.float32),
            jnp.zeros((residue_row_block, pair_cols), jnp.float32),
        ),
    )
    count_column = pair_count.reshape(residue_row_block * pair_cols, 1)
    mid_act = (
        pair_activation_input.reshape(residue_row_block * pair_cols, pair_width).astype(jnp.float32)
        + projected.reshape(residue_row_block * pair_cols, pair_width) / count_column
    )
    pair_scaled, pair_inv = norm_pieces(mid_act)
    pair_normed = (pair_scaled * pair_norm_gain).astype(jnp.bfloat16)
    pre_act = jnp.dot(pair_normed, hidden_weight, preferred_element_type=jnp.float32)
    act_value, act_slope = silu_pieces(pre_act)
    hidden = act_value.astype(jnp.bfloat16)
    masked_grad = (
        pair_output_gradient * pair_update_mask.astype(jnp.bfloat16)[:, :, None]
    ).reshape(residue_row_block * pair_cols, pair_width)
    final_matrix_derivative = jnp.dot(hidden.T, masked_grad, preferred_element_type=jnp.float32)
    back_prod = jnp.dot(masked_grad, back_weight.T, preferred_element_type=jnp.float32)
    grad_hidden = (back_prod * act_slope).astype(jnp.bfloat16)
    middle_matrix_derivative = jnp.dot(
        pair_normed.T, grad_hidden, preferred_element_type=jnp.float32
    )
    grad_scaled = (
        jnp.dot(grad_hidden, hidden_weight.T, preferred_element_type=jnp.float32) * pair_norm_gain
    )
    grad_mid = pair_output_gradient.reshape(residue_row_block * pair_cols, pair_width).astype(
        jnp.float32
    ) + standardize_adjoint(grad_scaled, pair_scaled, pair_inv)
    couple_features_derivative = grad_mid.astype(jnp.bfloat16).reshape(
        residue_row_block, pair_cols, pair_width
    )
    grad_opm = (
        (grad_mid / count_column)
        .astype(jnp.bfloat16)
        .reshape(residue_row_block, pair_cols, pair_width)
    )
    full_opm = lax.all_gather(grad_opm, "depth", axis=1, tiled=True).reshape(
        residue_row_block, depth_count, pair_cols, pair_width
    )

    def backward_step(step_index, loop_state):
        grad_left_acc, grad_out, right_term = loop_state
        col_start = step_index * col_block
        outer_part, right_piece = partial_outer(col_start)
        opm_piece = lax.dynamic_slice_in_dim(full_opm, col_start, col_block, 2).reshape(
            residue_row_block * block_depth * col_block, pair_width
        )
        grad_out = grad_out + jnp.dot(
            outer_part.reshape(residue_row_block * block_depth * col_block, outer_width).T,
            opm_piece.astype(jnp.float32),
            precision=highest,
        )
        grad_outer = jnp.dot(opm_piece, output_weight.T, preferred_element_type=jnp.float32).astype(
            jnp.bfloat16
        )
        grad_outer = grad_outer.reshape(
            residue_row_block, block_depth, col_block, proj_width, proj_width
        )
        grad_left_acc = grad_left_acc + jnp.einsum(
            "iejcd,sejd->sic", grad_outer, right_piece, preferred_element_type=jnp.float32
        )
        piece_term = jnp.einsum(
            "iejcd,sic->ejsd", grad_outer, left_proj, preferred_element_type=jnp.float32
        )
        piece_term = piece_term.reshape(block_depth, col_block, seq_total * proj_width)
        right_term = lax.dynamic_update_slice_in_dim(right_term, piece_term, col_start, 1)
        return (grad_left_acc, grad_out, right_term)

    grad_left_acc, result_matrix_derivative, right_term = lax.fori_loop(
        0,
        block_count,
        backward_step,
        (
            jnp.zeros((seq_total, residue_row_block, proj_width), jnp.float32),
            jnp.zeros((outer_width, pair_width), jnp.float32),
            jnp.zeros((block_depth, pair_cols, seq_total * proj_width), jnp.float32),
        ),
    )
    grad_right_sum = lax.psum_scatter(
        right_term.reshape(residues, seq_total * proj_width), "col", scatter_dimension=0, tiled=True
    )
    grad_right_acc = jnp.transpose(
        grad_right_sum.reshape(residue_row_block, seq_total, proj_width), (1, 0, 2)
    )
    grad_left = (grad_left_acc * mask_floating[:, :, None]).astype(jnp.bfloat16)
    grad_right = (grad_right_acc * mask_floating[:, :, None]).astype(jnp.bfloat16)
    normed_rows = normalized_rows.reshape(sequence_row_block * residue_row_block, channel_total)
    first_projector_derivative = jnp.dot(
        normed_rows.T,
        grad_left.reshape(sequence_row_block * residue_row_block, proj_width),
        preferred_element_type=jnp.float32,
    )
    second_projector_derivative = jnp.dot(
        normed_rows.T,
        grad_right.reshape(sequence_row_block * residue_row_block, proj_width),
        preferred_element_type=jnp.float32,
    )
    standardized_derivative = jnp.dot(
        grad_left, first_projector.T, preferred_element_type=jnp.float32
    ) + jnp.dot(grad_right, second_projector.T, preferred_element_type=jnp.float32)
    features_derivative = standardize_adjoint(
        standardized_derivative * layer_scale_factor, standardized_features, reciprocal_spread
    ).astype(jnp.bfloat16)
    weight_sums = lax.psum(
        (
            first_projector_derivative,
            second_projector_derivative,
            result_matrix_derivative,
            middle_matrix_derivative,
            final_matrix_derivative,
        ),
        ("depth", "col"),
    )
    return (
        features_derivative,
        couple_features_derivative,
        weight_sums[0],
        weight_sums[1],
        weight_sums[2],
        weight_sums[3],
        weight_sums[4],
    )


FEW_RESIDUES = 32
MASK_ROWS = 16
Z_PARTNERS = (2, 4, 6)
Y_PARTNER = 1


def butterfly(blocks, group):
    lane_group = lax.broadcasted_iota(jnp.int32, blocks[0].shape, 1) // group
    width = 4 * group
    for bit in (2, 1):
        low = (lane_group & bit) == 0
        swapped = list(blocks)
        for at in range(4):
            if at & bit:
                continue
            here, there = blocks[at], blocks[at | bit]
            moving = jnp.where(low, there, here)
            if bit == 2:
                moved = pltpu.roll(moving, 2 * group, 1)
            else:
                moved = jnp.where(
                    low, pltpu.roll(moving, width - group, 1), pltpu.roll(moving, group, 1)
                )
            swapped[at] = jnp.where(low, here, moved)
            swapped[at | bit] = jnp.where(low, moved, there)
        blocks = swapped
    return blocks


def wide_projector(first_ref, second_ref, copies):
    return jnp.concatenate([first_ref[...]] * copies + [second_ref[...]] * copies, axis=0)


def pre_kernel(
    ids_ref,
    x_hbm,
    maskt_hbm,
    pmask_hbm,
    scale_hbm,
    first_hbm,
    second_hbm,
    gain_hbm,
    act_hbm,
    grad_hbm,
    sent_ref,
    scale_ref,
    first_ref,
    second_ref,
    gain_ref,
    normed_ref,
    scaled_ref,
    inv_ref,
    wide_ref,
    tile_ref,
    x_ref,
    maskt_ref,
    pmask_ref,
    sems,
):
    res, seqs = maskt_ref.shape
    pairs = act_hbm.shape[0]
    first_pair = 2 * seqs + MASK_ROWS
    copies = [
        pltpu.make_async_copy(source, target, sems.at[at])
        for at, (source, target) in enumerate(
            (
                (x_hbm, x_ref),
                (maskt_hbm, maskt_ref),
                (pmask_hbm, pmask_ref),
                (scale_hbm, scale_ref),
                (first_hbm, first_ref),
                (second_hbm, second_ref),
                (gain_hbm, gain_ref),
                (act_hbm, sent_ref.at[0, pl.ds(first_pair, pairs), :]),
                (grad_hbm, sent_ref.at[0, pl.ds(first_pair + pairs, pairs), :]),
            )
        )
    ]
    for copy in copies:
        copy.start()
    for copy in copies:
        copy.wait()
    lanes = sent_ref.shape[2]
    group = lanes // res
    scaled, inv = norm_pieces(
        x_ref[...].astype(jnp.float32).reshape(seqs * res, x_ref.shape[2])
    )
    scaled_ref[...] = scaled
    inv_ref[...] = inv
    normed = (scaled * scale_ref[...]).astype(jnp.bfloat16)
    normed_ref[...] = normed
    wide = lax.dot_general(
        normed,
        wide_projector(first_ref, second_ref, res),
        (((1,), (1,)), ((), ())),
        preferred_element_type=jnp.float32,
    )
    for at in range(2):
        wide_ref[at] = wide[:, at * lanes : (at + 1) * lanes]
    tile_ref[...] = jnp.zeros(tile_ref.shape, jnp.float32)
    mask = maskt_ref[...].astype(jnp.float32)
    tile_ref[0:res, 0:seqs] = mask
    spread = (
        lax.broadcasted_iota(jnp.int32, (MASK_ROWS, lanes), 1) // group
        == lax.broadcasted_iota(jnp.int32, (MASK_ROWS, lanes), 0)
    ).astype(jnp.float32)
    mask_lanes = lax.dot_general(
        tile_ref[...], spread, (((0,), (0,)), ((), ())), preferred_element_type=jnp.float32
    )[:seqs]
    twice = jnp.concatenate([mask] * (lanes // seqs), axis=1)
    here = lax.broadcasted_iota(jnp.int32, (res, lanes), 1) // seqs == ids_ref[0]
    tile_ref[0:res, :] = jnp.where(here, twice, 0.0)
    tile_ref[res : 2 * res, 0 : pmask_ref.shape[1]] = pmask_ref[...].astype(jnp.float32)
    lane_group = lax.broadcasted_iota(jnp.int32, (seqs, lanes), 1) // group
    for at in range(2):
        both = wide_ref[at, pl.ds(0, seqs, stride=res), :]
        for r in range(1, res):
            both = jnp.where(
                lane_group == r, wide_ref[at, pl.ds(r, seqs, stride=res), :], both
            )
        first = (seqs + MASK_ROWS, 0)[at]
        sent_ref[0, first : first + seqs, :] = (both * mask_lanes).astype(jnp.bfloat16)
    sent_ref[0, seqs : seqs + MASK_ROWS, :] = tile_ref[...].astype(jnp.bfloat16)


def place_projections(ids_ref, blocks, right_ref, left_ref, seqs):
    near_ref, other_near_ref, far_ref, other_far_ref = blocks
    me_depth = ids_ref[0]
    me_z, me_y = ids_ref[1] // 2, ids_ref[1] % 2
    rights = seqs + MASK_ROWS
    for at in range(near_ref.shape[0]):
        z = me_z ^ at
        right_ref[me_depth, 2 * z + me_y] = near_ref[at, 0:rights, :]
        right_ref[1 - me_depth, 2 * z + me_y] = other_near_ref[at, 0:rights, :]
        right_ref[me_depth, 2 * z + 1 - me_y] = far_ref[at]
        right_ref[1 - me_depth, 2 * z + 1 - me_y] = other_far_ref[at]
        if left_ref is not None:
            left_ref[me_depth, z] = near_ref[at, rights : rights + seqs, :]
            left_ref[1 - me_depth, z] = other_near_ref[at, rights : rights + seqs, :]


def outer_kernel(
    sizes,
    ids_ref,
    near_ref,
    other_near_ref,
    far_ref,
    other_far_ref,
    wturn_ref,
    outer_ref,
    proj_out_ref,
    cnt_ref,
    pm_ref,
    maskt_ref,
    right_ref,
    left_ref,
    leftn_ref,
    mine_ref,
    turn_ref,
    cntl_ref,
    pml_ref,
):
    seqs, res, pair_cols, width = sizes
    depths, cols = right_ref.shape[0], right_ref.shape[1]
    line = left_ref.shape[1]
    lanes = res * width
    half_cols = pair_cols // res
    me_depth = ids_ref[0]
    me_z, me_y = ids_ref[1] // 2, ids_ref[1] % 2
    f32, bf16 = jnp.float32, jnp.bfloat16
    place_projections(
        ids_ref, (near_ref, other_near_ref, far_ref, other_far_ref), right_ref, left_ref, seqs
    )
    for e in range(depths):
        for z in range(line):
            leftn_ref[e * seqs : (e + 1) * seqs, z * lanes : (z + 1) * lanes] = left_ref[e, z]
    for k in range(half_cols):
        block = jnp.concatenate(
            [right_ref[e, me_depth * half_cols + k, 0:seqs, :] for e in range(depths)], axis=0
        ).astype(f32)
        turn_ref[k * lanes : (k + 1) * lanes, :] = block.T
    for d in range(width):
        mine_ref[d * pair_cols : (d + 1) * pair_cols, :] = turn_ref[
            pl.ds(d, pair_cols, stride=width), :
        ].astype(bf16)

    for k in range(cols):
        tiles = [
            right_ref[e, k, seqs : seqs + MASK_ROWS, :].astype(f32) for e in range(depths)
        ]
        maskt_ref[k * res : (k + 1) * res, :] = tiles[0][0:res] + tiles[1][0:res]
    pair_lane = lax.broadcasted_iota(jnp.int32, (pair_cols, lanes), 1)
    pair_row = lax.broadcasted_iota(jnp.int32, (pair_cols, lanes), 0)
    cols_mask = maskt_ref[pl.ds(pl.multiple_of(me_depth * pair_cols, pair_cols), pair_cols), :]
    for z in range(line):
        tile = right_ref[me_depth, 2 * z + me_y, seqs : seqs + MASK_ROWS, :].astype(f32)
        other = right_ref[1 - me_depth, 2 * z + me_y, seqs : seqs + MASK_ROWS, :].astype(f32)
        for r in range(res):
            first = (z * res + r) * pair_cols
            pml_ref[first : first + pair_cols, :] = jnp.where(
                pair_lane == pair_row, tile[res + r : res + r + 1, :], 0.0
            ).astype(bf16)
            cntl_ref[first : first + pair_cols, :] = (
                (tile[r : r + 1, :] + other[r : r + 1, :]) * cols_mask
            ).astype(bf16)
    ones = jnp.ones((lanes, lanes), bf16)
    cnt_ref[...] = jnp.dot(cntl_ref[...], ones, preferred_element_type=f32)
    pm_ref[...] = jnp.dot(pml_ref[...], ones, preferred_element_type=f32).astype(bf16)

    for z2 in range(line // 2):
        prod = jnp.dot(
            mine_ref[...],
            leftn_ref[:, 2 * z2 * lanes : 2 * (z2 + 1) * lanes],
            preferred_element_type=f32,
        )
        for dh in range(width // 4):
            for b in range(2):
                piece = prod[
                    dh * 4 * pair_cols : (dh + 1) * 4 * pair_cols, b * lanes : (b + 1) * lanes
                ]
                turned = butterfly(
                    [piece[a * pair_cols : (a + 1) * pair_cols] for a in range(4)], width
                )
                for il in range(res):
                    first = ((2 * z2 + b) * res + il) * pair_cols
                    outer_ref[first : first + pair_cols, dh * lanes : (dh + 1) * lanes] = turned[
                        il
                    ].astype(bf16)
    proj_out_ref[...] = jnp.dot(outer_ref[...], wturn_ref[...], preferred_element_type=f32)


def turn_kernel(sizes, firsts, ids_ref, mine_ref, other_ref, *refs):
    seqs, res, _, width = sizes
    outs, got_ref, turn_ref = refs[:-2], refs[-2], refs[-1]
    line = mine_ref.shape[0]
    lanes = res * width
    me_depth = ids_ref[0]
    me_z = ids_ref[1] // 2
    for first, out in zip(firsts, outs):
        for at in range(line):
            got_ref[me_depth, me_z ^ at] = mine_ref[at, first : first + seqs, :]
            got_ref[1 - me_depth, me_z ^ at] = other_ref[at, first : first + seqs, :]
        for z in range(line):
            block = jnp.concatenate(
                [got_ref[e, z] for e in range(got_ref.shape[0])], axis=0
            ).astype(jnp.float32)
            turn_ref[z * lanes : (z + 1) * lanes, :] = block.T
        for d in range(width):
            out[d * line * res : (d + 1) * line * res, :] = turn_ref[
                pl.ds(d, line * res, stride=width), :
            ].astype(jnp.bfloat16)


def transition_kernel(
    sizes,
    ids_ref,
    near_ref,
    proj_out_ref,
    cnt_ref,
    pm_ref,
    gain_ref,
    hid_ref,
    back_ref,
    couple_ref,
    opm_ref,
    pn_ref,
    gh_ref,
    hidden_ref,
    mg_ref,
    pairs_ref,
    gmid_ref,
):
    seqs, res, pair_cols, width = sizes
    per = res * pair_cols
    line = pairs_ref.shape[0]
    me_z = ids_ref[1] // 2
    first_pair = 2 * seqs + MASK_ROWS
    f32, bf16 = jnp.float32, jnp.bfloat16
    for at in range(line):
        pairs_ref[me_z ^ at] = near_ref[at, first_pair:, :]
    gain = gain_ref[...]
    act, grad = [
        jnp.concatenate([pairs_ref[z, w * per : (w + 1) * per, :] for z in range(line)], axis=0)
        for w in range(2)
    ]
    count = cnt_ref[...]
    mid = act.astype(f32) + proj_out_ref[...] / count
    scaled, inv = norm_pieces(mid)
    normed = (scaled * gain).astype(bf16)
    pn_ref[...] = normed
    pre = jnp.dot(normed, hid_ref[...], preferred_element_type=f32)
    value, slope = silu_pieces(pre)
    hidden_ref[...] = value.astype(bf16)
    masked = grad * pm_ref[...]
    mg_ref[...] = masked
    back = lax.dot_general(
        masked, back_ref[...], (((1,), (1,)), ((), ())), preferred_element_type=f32
    )
    ghid = (back * slope).astype(bf16)
    gh_ref[...] = ghid
    gsc = (
        lax.dot_general(ghid, hid_ref[...], (((1,), (1,)), ((), ())), preferred_element_type=f32)
        * gain
    )
    gmid = grad.astype(f32) + standardize_adjoint(gsc, scaled, inv)
    gmid_ref[...] = gmid
    opm_ref[...] = (gmid / count).astype(bf16)
    couple_ref[...] = gmid_ref[pl.ds(pl.multiple_of(me_z * per, per), per), :].astype(bf16)


def weights_kernel(
    ids_ref, outer_ref, opm_ref, pn_ref, gh_ref, hidden_ref, mg_ref, keep_ref, give_ref, turn_ref, both_ref
):
    pair_width, hid = pn_ref.shape[1], gh_ref.shape[1]
    outer_width = outer_ref.shape[1]
    width = int(outer_width**0.5 + 0.5)

    def contract(lhs, rhs):
        return lax.dot_general(
            lhs[...], rhs[...], (((0,), (0,)), ((), ())), preferred_element_type=jnp.float32
        )

    turn_ref[...] = contract(outer_ref, opm_ref)
    for c in range(width):
        both_ref[0, c * width : (c + 1) * width, :] = turn_ref[
            pl.ds(c, width, stride=width), :
        ].astype(jnp.bfloat16)
    dhid = contract(pn_ref, gh_ref).astype(jnp.bfloat16)
    for at in range(hid // pair_width):
        both_ref[1, at * pair_width : (at + 1) * pair_width, :] = dhid[
            :, at * pair_width : (at + 1) * pair_width
        ]
    both_ref[1, hid:, :] = contract(hidden_ref, mg_ref).astype(jnp.bfloat16)
    keep_ref[...] = both_ref[ids_ref[0]]
    give_ref[...] = both_ref[1 - ids_ref[0]]


def weights_out_kernel(ids_ref, mine_ref, other_ref, dout_ref, dhid_ref, dback_ref, both_ref):
    pair_width, hid = dhid_ref.shape
    both_ref[ids_ref[0]] = mine_ref[...]
    both_ref[1 - ids_ref[0]] = other_ref[...]
    dout_ref[...] = both_ref[0].astype(jnp.float32)
    for at in range(hid // pair_width):
        dhid_ref[:, at * pair_width : (at + 1) * pair_width] = both_ref[
            1, at * pair_width : (at + 1) * pair_width, :
        ].astype(jnp.float32)
    dback_ref[...] = both_ref[1, hid:, :].astype(jnp.float32)


def spread_rows(block, res, width, out_ref):
    lane_group = lax.broadcasted_iota(jnp.int32, block.shape, 1) // width
    for r in range(res):
        out_ref[pl.ds(r, block.shape[0], stride=res), :] = jnp.where(lane_group == r, block, 0.0)


def projector_kernel(
    sizes,
    ids_ref,
    opm_ref,
    other_opm_ref,
    right_near_ref,
    right_far_ref,
    leftt_ref,
    wout_ref,
    wturn_ref,
    maskt_ref,
    normed_ref,
    far_normed_ref,
    other_normed_ref,
    other_far_normed_ref,
    part_ref,
    gleft_ref,
    gright_ref,
    gright_far_ref,
    gf_ref,
    grow_ref,
    gcol_ref,
    gon_ref,
    gof_ref,
    goc_ref,
    gl_ref,
    gr_ref,
    rows_ref,
    tot_ref,
):
    seqs, res, pair_cols, width = sizes
    depths, half = gf_ref.shape[0], gf_ref.shape[1]
    rows_here = half // pair_cols
    residues = depths * pair_cols
    lanes = res * width
    here = 2 * res
    me_depth = ids_ref[0]
    me_z, me_y = ids_ref[1] // 2, ids_ref[1] % 2
    f32, bf16 = jnp.float32, jnp.bfloat16
    gf_ref[me_depth] = opm_ref[...].astype(f32)
    gf_ref[1 - me_depth] = other_opm_ref[...].astype(f32)
    for y, e, block in (
        (me_y, me_depth, normed_ref),
        (1 - me_y, me_depth, far_normed_ref),
        (me_y, 1 - me_depth, other_normed_ref),
        (1 - me_y, 1 - me_depth, other_far_normed_ref),
    ):
        rows_ref[y, e] = block[...]

    line = rows_here // res
    for il in range(res):
        for at, y in enumerate((me_y, 1 - me_y)):
            for z in range(line):
                e, z_low = divmod(z, line // depths)
                first = (me_z * res + il) * pair_cols + z_low * here + y * res
                to = il * residues + at * rows_here + z * res
                grow_ref[to : to + res, :] = gf_ref[e, pl.ds(first, res), :]
    my_half = (me_z * here) // pair_cols
    my_first = me_z * here - my_half * pair_cols
    for jl in range(here):
        gcol_ref[jl * rows_here : (jl + 1) * rows_here, :] = gf_ref[
            my_half, pl.ds(my_first + jl, rows_here, stride=pair_cols), :
        ].astype(bf16)
    for dh in range(width // 4):
        piece = lax.dot_general(
            grow_ref[...].astype(bf16),
            wturn_ref[dh * lanes : (dh + 1) * lanes, :],
            (((1,), (1,)), ((), ())),
            preferred_element_type=f32,
        )
        turned = butterfly([piece[a * residues : (a + 1) * residues] for a in range(4)], width)
        for dl in range(4):
            rows = slice((dh * 4 + dl) * rows_here, (dh * 4 + dl + 1) * rows_here)
            gon_ref[rows, :] = turned[dl][:rows_here].astype(bf16)
            gof_ref[rows, :] = turned[dl][rows_here:].astype(bf16)
        piece = lax.dot_general(
            gcol_ref[...],
            wout_ref[dh * lanes : (dh + 1) * lanes, :],
            (((1,), (1,)), ((), ())),
            preferred_element_type=f32,
        )
        for y in range(2):
            turned = butterfly(
                [
                    piece[(y * res + a) * rows_here : (y * res + a + 1) * rows_here]
                    for a in range(4)
                ],
                width,
            )
            for dl in range(4):
                rows = slice((dh * 4 + dl) * rows_here, (dh * 4 + dl + 1) * rows_here)
                goc_ref[rows, y * lanes : (y + 1) * lanes] = turned[dl].astype(bf16)
    group = lax.broadcasted_iota(jnp.int32, (here, here * width), 1) // width
    spread = (group == lax.broadcasted_iota(jnp.int32, (here, here * width), 0)).astype(f32)
    mask_lanes = lax.dot_general(
        maskt_ref[pl.ds(pl.multiple_of(me_z * here, here), here), :],
        spread,
        (((0,), (0,)), ((), ())),
        preferred_element_type=f32,
    )
    mask_own = jnp.where(me_y == 0, mask_lanes[:, :lanes], mask_lanes[:, lanes:])
    left_near, left_far, right = [
        lax.dot_general(lhs[...], rhs[...], (((0,), (0,)), ((), ())), preferred_element_type=f32)
        for lhs, rhs in ((right_near_ref, gon_ref), (right_far_ref, gof_ref), (leftt_ref, goc_ref))
    ]
    left = ((left_near + left_far) * mask_own).astype(bf16).astype(f32)
    right = right * mask_lanes
    for e in range(depths):
        tot_ref[0, e] = left[e * seqs : (e + 1) * seqs]
        spread_rows(left[e * seqs : (e + 1) * seqs], res, width, gl_ref.at[e])
        for y in range(2):
            block = right[e * seqs : (e + 1) * seqs, y * lanes : (y + 1) * lanes]
            tot_ref[1 + y, e] = block
            spread_rows(block, res, width, gr_ref.at[y, e])
    gleft_ref[...] = tot_ref[0, me_depth]
    gright_ref[...] = tot_ref[1 + me_y, me_depth]
    gright_far_ref[...] = tot_ref[2 - me_y, me_depth]
    rows = rows_ref.shape[2]
    for at, (lhs, rhs, blocks) in enumerate(
        ((gl_ref[...], rows_ref[me_y], depths), (gr_ref[...], rows_ref[...], 2 * depths))
    ):
        cross = lax.dot_general(
            lhs.reshape(blocks * rows, lanes).astype(bf16),
            rhs.reshape(blocks * rows, rows_ref.shape[3]),
            (((0,), (0,)), ((), ())),
            preferred_element_type=f32,
        )
        total = cross[:width]
        for r in range(1, res):
            total = total + cross[r * width : (r + 1) * width]
        part_ref[at * width : (at + 1) * width, :] = total.astype(bf16)


def feature_kernel(
    sizes,
    gleft_ref,
    gright_ref,
    gright_came_ref,
    first_ref,
    second_ref,
    scale_ref,
    scaled_ref,
    inv_ref,
    feat_ref,
    gs_ref,
):
    res, width = sizes[1], sizes[3]
    spread_rows(gleft_ref[...], res, width, gs_ref.at[0])
    spread_rows(gright_ref[...] + gright_came_ref[...], res, width, gs_ref.at[1])
    back = jnp.dot(
        jnp.concatenate([gs_ref[0], gs_ref[1]], axis=1).astype(jnp.bfloat16),
        wide_projector(first_ref, second_ref, res),
        preferred_element_type=jnp.float32,
    )
    feat_ref[...] = standardize_adjoint(
        back * scale_ref[...], scaled_ref[...], inv_ref[...]
    ).astype(jnp.bfloat16)


def swap_depth(block):
    return lax.ppermute(block, "depth", [(0, 1), (1, 0)])


def pairwise_sum(blocks):
    while len(blocks) > 1:
        blocks = [blocks[at] + blocks[at + 1] for at in range(0, len(blocks), 2)]
    return blocks[0]


def swap_col(block, partner):
    count = lax.axis_size("col")
    return lax.ppermute(block, "col", [(at, at ^ partner) for at in range(count)])


def whole_plan(
    alignment_activations,
    alignment_mask,
    pair_activation_input,
    pair_update_mask,
    pair_output_gradient,
    layer_scale_factor,
    first_projector,
    second_projector,
    output_weight,
    pair_norm_gain,
    hidden_weight,
    back_weight,
):
    seqs, res, channels = alignment_activations.shape
    width = first_projector.shape[1]
    outer_width = width * width
    cols = lax.axis_size("col")
    depths = lax.axis_size("depth")
    residues = res * cols
    pair_cols, pair_width = pair_activation_input.shape[1:]
    hid = hidden_weight.shape[1]
    per = res * pair_cols
    lanes = res * width
    rights = seqs + MASK_ROWS
    rows = rights + seqs
    line = cols // 2
    half = line * res * pair_cols
    f32, bf16 = jnp.float32, jnp.bfloat16
    ids = jnp.stack([lax.axis_index("depth"), lax.axis_index("col")]).astype(jnp.int32)
    smem = pl.BlockSpec(memory_space=pltpu.SMEM)
    vmem = pl.BlockSpec(memory_space=pltpu.VMEM)
    params = pltpu.CompilerParams(vmem_limit_bytes=16 * 2**20)
    scale = layer_scale_factor.reshape(1, channels)
    first, second = first_projector.T, second_projector.T
    wturn = jnp.transpose(output_weight.reshape(width, width, pair_width), (1, 0, 2)).reshape(
        outer_width, pair_width
    )
    shape = jax.ShapeDtypeStruct
    sent, scale, first, second, gain, normed, scaled, inv = pl.pallas_call(
        pre_kernel,
        out_shape=(
            shape((1, rows + 2 * per, pair_width), bf16),
            shape((1, channels), f32),
            shape((width, channels), bf16),
            shape((width, channels), bf16),
            shape((1, pair_width), f32),
            shape((seqs * res, channels), bf16),
            shape((seqs * res, channels), f32),
            shape((seqs * res, 1), f32),
        ),
        in_specs=[smem] + [pl.BlockSpec(memory_space=pltpu.HBM)] * 9,
        out_specs=[vmem] * 8,
        scratch_shapes=[
            pltpu.VMEM((2, seqs * res, lanes), f32),
            pltpu.VMEM((MASK_ROWS, lanes), f32),
            pltpu.VMEM((seqs, res, channels), bf16),
            pltpu.VMEM((res, seqs), jnp.int32),
            pltpu.VMEM((res, pair_cols), jnp.int32),
            pltpu.SemaphoreType.DMA((9,)),
        ],
        compiler_params=params,
        name="project",
    )(
        ids,
        *[
            pltpu.with_memory_space_constraint(array, pltpu.HBM)
            for array in (
                alignment_activations,
                alignment_mask.T,
                pair_update_mask,
                scale,
                first,
                second,
                pair_norm_gain.reshape(1, pair_width),
                pair_activation_input.reshape(per, pair_width),
                pair_output_gradient.reshape(per, pair_width),
            )
        ],
    )
    near = lax.optimization_barrier(
        jnp.concatenate([sent] + [swap_col(sent, partner) for partner in Z_PARTNERS])
    )
    far_normed = swap_col(normed, Y_PARTNER)
    other_normed, other_far_normed = swap_depth(normed), swap_depth(far_normed)
    near, far_normed, other_normed = lax.optimization_barrier((near, far_normed, other_normed))
    sizes = (seqs, res, pair_cols, width)
    far = swap_col(near[:, :rights], Y_PARTNER)
    other_near = swap_depth(near[:, :rows])

    def turned(firsts, mine, other):
        return pl.pallas_call(
            functools.partial(turn_kernel, sizes, firsts),
            out_shape=(shape((line * res * width, depths * seqs), bf16),) * len(firsts),
            in_specs=[smem] + [vmem] * 2,
            out_specs=[vmem] * len(firsts),
            scratch_shapes=[
                pltpu.VMEM((depths, line, seqs, lanes), bf16),
                pltpu.VMEM((line * res * width, depths * seqs), f32),
            ],
            compiler_params=params,
            name="turned",
        )(ids, mine, other)

    right_near, leftt = turned((0, rights), near, other_near)
    far, right_near, leftt = lax.optimization_barrier((far, right_near, leftt))
    other_far = swap_depth(far)
    other_far, other_far_normed = lax.optimization_barrier((other_far, other_far_normed))
    outer, proj_out, cnt, pm, maskt = pl.pallas_call(
        functools.partial(outer_kernel, sizes),
        out_shape=(
            shape((half, outer_width), bf16),
            shape((half, pair_width), f32),
            shape((half, lanes), f32),
            shape((half, lanes), bf16),
            shape((residues, depths * seqs), f32),
        ),
        in_specs=[smem] + [vmem] * 5,
        out_specs=[vmem] * 5,
        scratch_shapes=[
            pltpu.VMEM((depths, cols, rights, lanes), bf16),
            pltpu.VMEM((depths, line, seqs, lanes), bf16),
            pltpu.VMEM((depths * seqs, line * lanes), bf16),
            pltpu.VMEM((pair_cols * width, depths * seqs), bf16),
            pltpu.VMEM((pair_cols * width, depths * seqs), f32),
            pltpu.VMEM((half, lanes), bf16),
            pltpu.VMEM((half, lanes), bf16),
        ],
        compiler_params=params,
        name="outer_products",
    )(ids, near, other_near, far, other_far, wturn)
    couple, opm, pn, gh, hidden, mg = pl.pallas_call(
        functools.partial(transition_kernel, sizes),
        out_shape=(
            shape((per, pair_width), bf16),
            shape((half, pair_width), bf16),
            shape((half, pair_width), bf16),
            shape((half, hid), bf16),
            shape((half, hid), bf16),
            shape((half, pair_width), bf16),
        ),
        in_specs=[smem] + [vmem] * 7,
        out_specs=[vmem] * 6,
        scratch_shapes=[
            pltpu.VMEM((line, 2 * per, pair_width), bf16),
            pltpu.VMEM((half, pair_width), f32),
        ],
        compiler_params=params,
        name="transition",
    )(ids, near, proj_out, cnt, pm, gain, hidden_weight, back_weight)
    other_opm = swap_depth(opm)
    other_far, opm = lax.optimization_barrier((other_far, opm))
    (right_far,) = turned((0,), far, other_far)
    weight_rows = outer_width
    keep, give = pl.pallas_call(
        weights_kernel,
        out_shape=(shape((weight_rows, pair_width), bf16),) * 2,
        in_specs=[smem] + [vmem] * 6,
        out_specs=[vmem] * 2,
        scratch_shapes=[
            pltpu.VMEM((outer_width, pair_width), f32),
            pltpu.VMEM((2, weight_rows, pair_width), bf16),
        ],
        compiler_params=params,
        name="weight_gradients",
    )(ids, outer, opm, pn, gh, hidden, mg)
    other_opm, right_far, keep, give = lax.optimization_barrier((other_opm, right_far, keep, give))
    part, gleft, gright, gright_far = pl.pallas_call(
        functools.partial(projector_kernel, sizes),
        out_shape=(
            shape((2 * width, channels), bf16),
            shape((seqs, lanes), f32),
            shape((seqs, lanes), f32),
            shape((seqs, lanes), f32),
        ),
        in_specs=[smem] + [vmem] * 12,
        out_specs=[vmem] * 4,
        scratch_shapes=[
            pltpu.VMEM((depths, half, pair_width), f32),
            pltpu.VMEM((res * residues, pair_width), f32),
            pltpu.VMEM((2 * res * line * res, pair_width), bf16),
            pltpu.VMEM((line * res * width, lanes), bf16),
            pltpu.VMEM((line * res * width, lanes), bf16),
            pltpu.VMEM((line * res * width, 2 * lanes), bf16),
            pltpu.VMEM((depths, seqs * res, lanes), f32),
            pltpu.VMEM((2, depths, seqs * res, lanes), f32),
            pltpu.VMEM((2, depths, seqs * res, channels), bf16),
            pltpu.VMEM((3, depths, seqs, lanes), f32),
        ],
        compiler_params=params,
        name="projector_parts",
    )(
        ids,
        opm,
        other_opm,
        right_near,
        right_far,
        leftt,
        output_weight,
        wturn,
        maskt,
        normed,
        far_normed,
        other_normed,
        other_far_normed,
    )

    given, part = lax.optimization_barrier((swap_depth(give), part))

    def rounded_sum(block, came):
        return (block.astype(f32) + came.astype(f32)).astype(bf16)

    came = [swap_col(part, partner) for partner in Z_PARTNERS]
    came[2], gright_far = lax.optimization_barrier((came[2], gright_far))
    weights = rounded_sum(keep, given)
    weights = rounded_sum(weights, swap_col(weights, Y_PARTNER))
    total = pairwise_sum([block.astype(f32) for block in [part] + came])
    part = lax.optimization_barrier(total.astype(bf16))
    total = part.astype(f32) + swap_col(part, Y_PARTNER).astype(f32)
    feat = pl.pallas_call(
        functools.partial(feature_kernel, sizes),
        out_shape=shape((seqs * res, channels), bf16),
        in_specs=[vmem] * 8,
        out_specs=vmem,
        scratch_shapes=[pltpu.VMEM((2, seqs * res, lanes), f32)],
        compiler_params=params,
        name="features",
    )(gleft, gright, swap_col(gright_far, Y_PARTNER), first, second, scale, scaled, inv)
    dout, dhid, dback = pl.pallas_call(
        weights_out_kernel,
        out_shape=(
            shape((outer_width, pair_width), f32),
            shape((pair_width, hid), f32),
            shape((hid, pair_width), f32),
        ),
        in_specs=[smem] + [vmem] * 2,
        out_specs=[vmem] * 3,
        scratch_shapes=[pltpu.VMEM((2, weight_rows, pair_width), bf16)],
        compiler_params=params,
        name="weights_out",
    )(ids, weights, swap_depth(weights))
    return (
        feat.reshape(seqs, res, channels),
        couple.reshape(res, pair_cols, pair_width),
        total[:width].T,
        total[width:].T,
        dout,
        dhid,
        dback,
    )


def on_device(alignment_activations, *others):
    cols = lax.axis_size("col")
    residues = alignment_activations.shape[1] * cols
    plan = whole_plan if cols == 8 and residues <= FEW_RESIDUES else split_plan
    return plan(alignment_activations, *others)


def solution(mesh):
    in_specs = (
        P(("group", "depth"), "col", None),
        P(("group", "depth"), "col"),
        P(("group", "col"), "depth", None),
        P(("group", "col"), "depth"),
        P(("group", "col"), "depth", None),
        P(),
        P(),
        P(),
        P(),
        P(),
        P(),
        P(),
    )
    out_specs = (
        P(("group", "depth"), "col", None),
        P(("group", "col"), "depth", None),
        P("group", None),
        P("group", None),
        P("group", None),
        P("group", None),
        P("group", None),
    )
    return jax.shard_map(
        on_device, mesh=mesh, in_specs=in_specs, out_specs=out_specs, check_vma=False
    )
```

```python
import functools

import jax
import jax.numpy as jnp
from jax import lax
from jax.experimental import pallas as pl
from jax.experimental.pallas import tpu as pltpu
from jax.sharding import PartitionSpec as P

epsilon = 1e-05
highest = lax.Precision.HIGHEST


def norm_pieces(entries_drawn):
    center = entries_drawn - jnp.mean(entries_drawn, axis=-1, keepdims=True)
    inv_std = lax.rsqrt(jnp.mean(center * center, axis=-1, keepdims=True) + epsilon)
    return (center * inv_std, inv_std)


def standardize_adjoint(grad_scaled, scaled, inv_std):
    mean_grad = jnp.mean(grad_scaled, axis=-1, keepdims=True)
    mean_cross = jnp.mean(grad_scaled * scaled, axis=-1, keepdims=True)
    return inv_std * (grad_scaled - mean_grad - scaled * mean_cross)


def silu_pieces(pre_act):
    sigma = jax.nn.sigmoid(pre_act)
    return (pre_act * sigma, sigma * (1.0 + pre_act * (1.0 - sigma)))


def split_plan(
    alignment_activations,
    alignment_mask,
    pair_activation_input,
    pair_update_mask,
    pair_output_gradient,
    layer_scale_factor,
    first_projector,
    second_projector,
    output_weight,
    pair_norm_gain,
    hidden_weight,
    back_weight,
):
    sequence_row_block, residue_row_block, channel_total = alignment_activations.shape
    proj_width = first_projector.shape[1]
    outer_width = proj_width * proj_width
    depth_count = lax.axis_size("depth")
    residues = residue_row_block * lax.axis_size("col")
    pair_cols = pair_activation_input.shape[1]
    pair_width = pair_activation_input.shape[2]
    col_block = min(64, pair_cols)
    block_count = pair_cols // col_block
    standardized_features, reciprocal_spread = norm_pieces(
        alignment_activations.astype(jnp.float32)
    )
    normalized_rows = (standardized_features * layer_scale_factor).astype(jnp.bfloat16)
    mask_floating = alignment_mask.astype(jnp.float32)
    left_proj = (
        jnp.dot(normalized_rows, first_projector, preferred_element_type=jnp.float32)
        * mask_floating[:, :, None]
    ).astype(jnp.bfloat16)
    right_proj = (
        jnp.dot(normalized_rows, second_projector, preferred_element_type=jnp.float32)
        * mask_floating[:, :, None]
    ).astype(jnp.bfloat16)
    right_flat = right_proj.reshape(sequence_row_block, residue_row_block * proj_width)
    mask_converted = alignment_mask.astype(jnp.bfloat16)
    seq_total = left_proj.shape[0]
    gathered, gathered_mask = (
        lax.all_gather(right_flat, "col", axis=1, tiled=True),
        lax.all_gather(mask_converted, "col", axis=1, tiled=True),
    )
    right_blocks = gathered.reshape(seq_total, depth_count, pair_cols, proj_width)
    mask_blocks = gathered_mask.reshape(seq_total, depth_count, pair_cols)
    block_depth = right_blocks.shape[1]
    out_wide = output_weight.astype(jnp.float32)

    def partial_outer(col_start):
        right_piece = lax.dynamic_slice_in_dim(right_blocks, col_start, col_block, 2)
        outer_part = jnp.einsum(
            "sic,sejd->iejcd", left_proj, right_piece, preferred_element_type=jnp.float32
        )
        return (
            outer_part.reshape(residue_row_block, block_depth, col_block, outer_width),
            right_piece,
        )

    def forward_step(step_index, loop_state):
        projected, pair_count = loop_state
        col_start = step_index * col_block
        outer_part, right_piece = partial_outer(col_start)
        mask_piece = lax.dynamic_slice_in_dim(mask_blocks, col_start, col_block, 2).astype(
            jnp.float32
        )
        count_part = jnp.einsum("si,sej->iej", mask_floating, mask_piece, precision=highest)
        outer_mine, count_mine = (
            lax.psum_scatter(
                outer_part.astype(jnp.bfloat16), "depth", scatter_dimension=1, tiled=True
            ).astype(jnp.float32),
            lax.psum_scatter(
                count_part.astype(jnp.bfloat16), "depth", scatter_dimension=1, tiled=True
            ).astype(jnp.float32),
        )
        proj_mine = jnp.dot(
            outer_mine.reshape(residue_row_block * col_block, outer_width),
            out_wide,
            precision=highest,
        )
        proj_mine = proj_mine.reshape(residue_row_block, col_block, pair_width)
        count_mine = count_mine.reshape(residue_row_block, col_block)
        projected = lax.dynamic_update_slice_in_dim(projected, proj_mine, col_start, 1)
        pair_count = lax.dynamic_update_slice_in_dim(pair_count, count_mine, col_start, 1)
        return (projected, pair_count)

    projected, pair_count = lax.fori_loop(
        0,
        block_count,
        forward_step,
        (
            jnp.zeros((residue_row_block, pair_cols, pair_width), jnp.float32),
            jnp.zeros((residue_row_block, pair_cols), jnp.float32),
        ),
    )
    count_column = pair_count.reshape(residue_row_block * pair_cols, 1)
    mid_act = (
        pair_activation_input.reshape(residue_row_block * pair_cols, pair_width).astype(jnp.float32)
        + projected.reshape(residue_row_block * pair_cols, pair_width) / count_column
    )
    pair_scaled, pair_inv = norm_pieces(mid_act)
    pair_normed = (pair_scaled * pair_norm_gain).astype(jnp.bfloat16)
    pre_act = jnp.dot(pair_normed, hidden_weight, preferred_element_type=jnp.float32)
    act_value, act_slope = silu_pieces(pre_act)
    hidden = act_value.astype(jnp.bfloat16)
    masked_grad = (
        pair_output_gradient * pair_update_mask.astype(jnp.bfloat16)[:, :, None]
    ).reshape(residue_row_block * pair_cols, pair_width)
    final_matrix_derivative = jnp.dot(hidden.T, masked_grad, preferred_element_type=jnp.float32)
    back_prod = jnp.dot(masked_grad, back_weight.T, preferred_element_type=jnp.float32)
    grad_hidden = (back_prod * act_slope).astype(jnp.bfloat16)
    middle_matrix_derivative = jnp.dot(
        pair_normed.T, grad_hidden, preferred_element_type=jnp.float32
    )
    grad_scaled = (
        jnp.dot(grad_hidden, hidden_weight.T, preferred_element_type=jnp.float32) * pair_norm_gain
    )
    grad_mid = pair_output_gradient.reshape(residue_row_block * pair_cols, pair_width).astype(
        jnp.float32
    ) + standardize_adjoint(grad_scaled, pair_scaled, pair_inv)
    couple_features_derivative = grad_mid.astype(jnp.bfloat16).reshape(
        residue_row_block, pair_cols, pair_width
    )
    grad_opm = (
        (grad_mid / count_column)
        .astype(jnp.bfloat16)
        .reshape(residue_row_block, pair_cols, pair_width)
    )
    full_opm = lax.all_gather(grad_opm, "depth", axis=1, tiled=True).reshape(
        residue_row_block, depth_count, pair_cols, pair_width
    )

    def backward_step(step_index, loop_state):
        grad_left_acc, grad_out, right_term = loop_state
        col_start = step_index * col_block
        outer_part, right_piece = partial_outer(col_start)
        opm_piece = lax.dynamic_slice_in_dim(full_opm, col_start, col_block, 2).reshape(
            residue_row_block * block_depth * col_block, pair_width
        )
        grad_out = grad_out + jnp.dot(
            outer_part.reshape(residue_row_block * block_depth * col_block, outer_width).T,
            opm_piece.astype(jnp.float32),
            precision=highest,
        )
        grad_outer = jnp.dot(opm_piece, output_weight.T, preferred_element_type=jnp.float32).astype(
            jnp.bfloat16
        )
        grad_outer = grad_outer.reshape(
            residue_row_block, block_depth, col_block, proj_width, proj_width
        )
        grad_left_acc = grad_left_acc + jnp.einsum(
            "iejcd,sejd->sic", grad_outer, right_piece, preferred_element_type=jnp.float32
        )
        piece_term = jnp.einsum(
            "iejcd,sic->ejsd", grad_outer, left_proj, preferred_element_type=jnp.float32
        )
        piece_term = piece_term.reshape(block_depth, col_block, seq_total * proj_width)
        right_term = lax.dynamic_update_slice_in_dim(right_term, piece_term, col_start, 1)
        return (grad_left_acc, grad_out, right_term)

    grad_left_acc, result_matrix_derivative, right_term = lax.fori_loop(
        0,
        block_count,
        backward_step,
        (
            jnp.zeros((seq_total, residue_row_block, proj_width), jnp.float32),
            jnp.zeros((outer_width, pair_width), jnp.float32),
            jnp.zeros((block_depth, pair_cols, seq_total * proj_width), jnp.float32),
        ),
    )
    grad_right_sum = lax.psum_scatter(
        right_term.reshape(residues, seq_total * proj_width), "col", scatter_dimension=0, tiled=True
    )
    grad_right_acc = jnp.transpose(
        grad_right_sum.reshape(residue_row_block, seq_total, proj_width), (1, 0, 2)
    )
    grad_left = (grad_left_acc * mask_floating[:, :, None]).astype(jnp.bfloat16)
    grad_right = (grad_right_acc * mask_floating[:, :, None]).astype(jnp.bfloat16)
    normed_rows = normalized_rows.reshape(sequence_row_block * residue_row_block, channel_total)
    first_projector_derivative = jnp.dot(
        normed_rows.T,
        grad_left.reshape(sequence_row_block * residue_row_block, proj_width),
        preferred_element_type=jnp.float32,
    )
    second_projector_derivative = jnp.dot(
        normed_rows.T,
        grad_right.reshape(sequence_row_block * residue_row_block, proj_width),
        preferred_element_type=jnp.float32,
    )
    standardized_derivative = jnp.dot(
        grad_left, first_projector.T, preferred_element_type=jnp.float32
    ) + jnp.dot(grad_right, second_projector.T, preferred_element_type=jnp.float32)
    features_derivative = standardize_adjoint(
        standardized_derivative * layer_scale_factor, standardized_features, reciprocal_spread
    ).astype(jnp.bfloat16)
    weight_sums = lax.psum(
        (
            first_projector_derivative,
            second_projector_derivative,
            result_matrix_derivative,
            middle_matrix_derivative,
            final_matrix_derivative,
        ),
        ("depth", "col"),
    )
    return (
        features_derivative,
        couple_features_derivative,
        weight_sums[0],
        weight_sums[1],
        weight_sums[2],
        weight_sums[3],
        weight_sums[4],
    )


FEW_RESIDUES = 32
MASK_ROWS = 16
Z_PARTNERS = (2, 4, 6)
Y_PARTNER = 1


def butterfly(blocks, group):
    lane_group = lax.broadcasted_iota(jnp.int32, blocks[0].shape, 1) // group
    width = 4 * group
    for bit in (2, 1):
        low = (lane_group & bit) == 0
        swapped = list(blocks)
        for at in range(4):
            if at & bit:
                continue
            here, there = blocks[at], blocks[at | bit]
            moving = jnp.where(low, there, here)
            if bit == 2:
                moved = pltpu.roll(moving, 2 * group, 1)
            else:
                moved = jnp.where(
                    low, pltpu.roll(moving, width - group, 1), pltpu.roll(moving, group, 1)
                )
            swapped[at] = jnp.where(low, here, moved)
            swapped[at | bit] = jnp.where(low, moved, there)
        blocks = swapped
    return blocks


def wide_projector(first_ref, second_ref, copies):
    return jnp.concatenate([first_ref[...]] * copies + [second_ref[...]] * copies, axis=0)


def pre_kernel(
    ids_ref,
    x_hbm,
    maskt_hbm,
    pmask_hbm,
    scale_hbm,
    first_hbm,
    second_hbm,
    gain_hbm,
    act_hbm,
    grad_hbm,
    sent_ref,
    scale_ref,
    first_ref,
    second_ref,
    gain_ref,
    normed_ref,
    scaled_ref,
    inv_ref,
    wide_ref,
    tile_ref,
    x_ref,
    maskt_ref,
    pmask_ref,
    sems,
):
    res, seqs = maskt_ref.shape
    pairs = act_hbm.shape[0]
    first_pair = 2 * seqs + MASK_ROWS
    copies = [
        pltpu.make_async_copy(source, target, sems.at[at])
        for at, (source, target) in enumerate(
            (
                (x_hbm, x_ref),
                (maskt_hbm, maskt_ref),
                (pmask_hbm, pmask_ref),
                (scale_hbm, scale_ref),
                (first_hbm, first_ref),
                (second_hbm, second_ref),
                (gain_hbm, gain_ref),
                (act_hbm, sent_ref.at[0, pl.ds(first_pair, pairs), :]),
                (grad_hbm, sent_ref.at[0, pl.ds(first_pair + pairs, pairs), :]),
            )
        )
    ]
    for copy in copies:
        copy.start()
    for copy in copies:
        copy.wait()
    lanes = sent_ref.shape[2]
    group = lanes // res
    scaled, inv = norm_pieces(
        x_ref[...].astype(jnp.float32).reshape(seqs * res, x_ref.shape[2])
    )
    scaled_ref[...] = scaled
    inv_ref[...] = inv
    normed = (scaled * scale_ref[...]).astype(jnp.bfloat16)
    normed_ref[...] = normed
    wide = lax.dot_general(
        normed,
        wide_projector(first_ref, second_ref, res),
        (((1,), (1,)), ((), ())),
        preferred_element_type=jnp.float32,
    )
    for at in range(2):
        wide_ref[at] = wide[:, at * lanes : (at + 1) * lanes]
    tile_ref[...] = jnp.zeros(tile_ref.shape, jnp.float32)
    mask = maskt_ref[...].astype(jnp.float32)
    tile_ref[0:res, 0:seqs] = mask
    spread = (
        lax.broadcasted_iota(jnp.int32, (MASK_ROWS, lanes), 1) // group
        == lax.broadcasted_iota(jnp.int32, (MASK_ROWS, lanes), 0)
    ).astype(jnp.float32)
    mask_lanes = lax.dot_general(
        tile_ref[...], spread, (((0,), (0,)), ((), ())), preferred_element_type=jnp.float32
    )[:seqs]
    twice = jnp.concatenate([mask] * (lanes // seqs), axis=1)
    here = lax.broadcasted_iota(jnp.int32, (res, lanes), 1) // seqs == ids_ref[0]
    tile_ref[0:res, :] = jnp.where(here, twice, 0.0)
    tile_ref[res : 2 * res, 0 : pmask_ref.shape[1]] = pmask_ref[...].astype(jnp.float32)
    lane_group = lax.broadcasted_iota(jnp.int32, (seqs, lanes), 1) // group
    for at in range(2):
        both = wide_ref[at, pl.ds(0, seqs, stride=res), :]
        for r in range(1, res):
            both = jnp.where(
                lane_group == r, wide_ref[at, pl.ds(r, seqs, stride=res), :], both
            )
        sent_ref[0, at * seqs : (at + 1) * seqs, :] = (both * mask_lanes).astype(jnp.bfloat16)
    sent_ref[0, 2 * seqs : first_pair, :] = tile_ref[...].astype(jnp.bfloat16)


def outer_kernel(
    sizes,
    orders,
    ids_ref,
    near_ref,
    far_ref,
    other_near_ref,
    other_far_ref,
    wturn_ref,
    outer_ref,
    proj_out_ref,
    cnt_ref,
    pm_ref,
    maskt_ref,
    got_ref,
    leftn_ref,
    mine_ref,
    turn_ref,
    cntl_ref,
    pml_ref,
):
    seqs, res, pair_cols, width = sizes
    depths, cols = got_ref.shape[0], got_ref.shape[1]
    residues = cols * res
    lanes = res * width
    half_cols = pair_cols // res
    me_depth = ids_ref[0]
    me_col = ids_ref[1]
    f32, bf16 = jnp.float32, jnp.bfloat16

    for order, mine, other in zip(orders, (near_ref, far_ref), (other_near_ref, other_far_ref)):
        for at, partner in enumerate(order):
            got_ref[me_depth, me_col ^ partner] = mine[at]
            got_ref[1 - me_depth, me_col ^ partner] = other[at]

    for e in range(depths):
        for k in range(cols):
            leftn_ref[e * seqs : (e + 1) * seqs, k * lanes : (k + 1) * lanes] = got_ref[
                e, k, 0:seqs, :
            ]
    for k in range(half_cols):
        block = jnp.concatenate(
            [
                got_ref[e, me_depth * half_cols + k, seqs : 2 * seqs, :]
                for e in range(depths)
            ],
            axis=0,
        ).astype(f32)
        turn_ref[k * lanes : (k + 1) * lanes, :] = block.T
    for d in range(width):
        mine_ref[d * pair_cols : (d + 1) * pair_cols, :] = turn_ref[
            pl.ds(d, pair_cols, stride=width), :
        ].astype(bf16)

    base = 2 * seqs
    pair_lane = lax.broadcasted_iota(jnp.int32, (pair_cols, lanes), 1)
    pair_row = lax.broadcasted_iota(jnp.int32, (pair_cols, lanes), 0)
    for k in range(cols):
        tiles = [got_ref[e, k, base : base + MASK_ROWS, :].astype(f32) for e in range(depths)]
        maskt_ref[k * res : (k + 1) * res, :] = tiles[0][0:res] + tiles[1][0:res]
        own = got_ref[me_depth, k, base : base + MASK_ROWS, :].astype(f32)
        for r in range(res):
            row = own[res + r : res + r + 1, :]
            first = (k * res + r) * pair_cols
            pml_ref[first : first + pair_cols, :] = jnp.where(
                pair_lane == pair_row, row, 0.0
            ).astype(bf16)
    maskt = maskt_ref[...]
    cols_mask = maskt_ref[pl.ds(pl.multiple_of(me_depth * pair_cols, pair_cols), pair_cols), :]
    for i in range(residues):
        cntl_ref[i * pair_cols : (i + 1) * pair_cols, :] = (maskt[i : i + 1, :] * cols_mask).astype(
            bf16
        )
    ones = jnp.ones((lanes, lanes), bf16)
    cnt_ref[...] = jnp.dot(cntl_ref[...], ones, preferred_element_type=f32)
    pm_ref[...] = jnp.dot(pml_ref[...], ones, preferred_element_type=f32).astype(bf16)

    for k2 in range(cols // 2):
        prod = jnp.dot(
            mine_ref[...],
            leftn_ref[:, 2 * k2 * lanes : 2 * (k2 + 1) * lanes],
            preferred_element_type=f32,
        )
        for dh in range(width // 4):
            for b in range(2):
                piece = prod[
                    dh * 4 * pair_cols : (dh + 1) * 4 * pair_cols, b * lanes : (b + 1) * lanes
                ]
                turned = butterfly(
                    [piece[a * pair_cols : (a + 1) * pair_cols] for a in range(4)], width
                )
                for il in range(res):
                    first = ((2 * k2 + b) * res + il) * pair_cols
                    outer_ref[first : first + pair_cols, dh * lanes : (dh + 1) * lanes] = turned[
                        il
                    ].astype(bf16)
    proj_out_ref[...] = jnp.dot(outer_ref[...], wturn_ref[...], preferred_element_type=f32)


def turn_kernel(
    sizes,
    orders,
    ids_ref,
    near_ref,
    far_ref,
    other_near_ref,
    other_far_ref,
    rightt_ref,
    leftt_ref,
    got_ref,
    turn_ref,
):
    seqs, res, _, width = sizes
    depths, cols = got_ref.shape[0], got_ref.shape[1]
    lanes = res * width
    residues = res * cols
    me_depth = ids_ref[0]
    me_col = ids_ref[1]
    for order, mine, other in zip(orders, (near_ref, far_ref), (other_near_ref, other_far_ref)):
        for at, partner in enumerate(order):
            got_ref[me_depth, me_col ^ partner] = mine[at, 0 : 2 * seqs, :]
            got_ref[1 - me_depth, me_col ^ partner] = other[at, 0 : 2 * seqs, :]
    for at, out in ((0, leftt_ref), (1, rightt_ref)):
        for k in range(cols):
            block = jnp.concatenate(
                [got_ref[e, k, at * seqs : (at + 1) * seqs, :] for e in range(depths)], axis=0
            ).astype(jnp.float32)
            turn_ref[k * lanes : (k + 1) * lanes, :] = block.T
        for d in range(width):
            out[d * residues : (d + 1) * residues, :] = turn_ref[
                pl.ds(d, residues, stride=width), :
            ].astype(jnp.bfloat16)


def transition_kernel(
    sizes,
    orders,
    ids_ref,
    near_ref,
    far_ref,
    proj_out_ref,
    cnt_ref,
    pm_ref,
    gain_ref,
    hid_ref,
    back_ref,
    couple_ref,
    opm_ref,
    pn_ref,
    gh_ref,
    hidden_ref,
    mg_ref,
    pgot_ref,
    gmid_ref,
):
    seqs, res, pair_cols, width = sizes
    per = res * pair_cols
    cols = pgot_ref.shape[0]
    me_col = ids_ref[1]
    f32, bf16 = jnp.float32, jnp.bfloat16
    for order, mine in zip(orders, (near_ref, far_ref)):
        for at, partner in enumerate(order):
            pgot_ref[me_col ^ partner] = mine[at]
    gain = gain_ref[...]
    chunk = 2 * per
    for at in range(cols // 2):
        rows = slice(at * chunk, (at + 1) * chunk)
        act, grad = [
            jnp.concatenate(
                [pgot_ref[2 * at + b, w * per : (w + 1) * per, :] for b in range(2)], axis=0
            )
            for w in range(2)
        ]
        count = cnt_ref[rows, :]
        mid = act.astype(f32) + proj_out_ref[rows, :] / count
        scaled, inv = norm_pieces(mid)
        normed = (scaled * gain).astype(bf16)
        pn_ref[rows, :] = normed
        pre = jnp.dot(normed, hid_ref[...], preferred_element_type=f32)
        value, slope = silu_pieces(pre)
        hidden_ref[rows, :] = value.astype(bf16)
        masked = grad * pm_ref[rows, :]
        mg_ref[rows, :] = masked
        back = lax.dot_general(
            masked, back_ref[...], (((1,), (1,)), ((), ())), preferred_element_type=f32
        )
        ghid = (back * slope).astype(bf16)
        gh_ref[rows, :] = ghid
        gsc = (
            lax.dot_general(
                ghid, hid_ref[...], (((1,), (1,)), ((), ())), preferred_element_type=f32
            )
            * gain
        )
        gmid = grad.astype(f32) + standardize_adjoint(gsc, scaled, inv)
        gmid_ref[rows, :] = gmid
        opm_ref[rows, :] = (gmid / count).astype(bf16)
    couple_ref[...] = gmid_ref[pl.ds(pl.multiple_of(me_col * per, per), per), :].astype(bf16)


def projector_kernel(
    sizes,
    ids_ref,
    opm_ref,
    other_opm_ref,
    rightt_ref,
    leftt_ref,
    wout_ref,
    wturn_ref,
    maskt_ref,
    normed_ref,
    far_normed_ref,
    other_normed_ref,
    other_far_normed_ref,
    part_ref,
    spread_ref,
    gf_ref,
    grow_ref,
    gcol_ref,
    gor_ref,
    goc_ref,
    gs_ref,
    rows_ref,
):
    seqs, res, pair_cols, width = sizes
    depths, half = gf_ref.shape[0], gf_ref.shape[1]
    residues = half // pair_cols
    lanes = res * width
    here = 2 * res
    me_depth = ids_ref[0]
    me_col = ids_ref[1]
    me_y = me_col % 2
    first_here = (me_col // 2) * here
    f32, bf16 = jnp.float32, jnp.bfloat16
    gf_ref[me_depth] = opm_ref[...].astype(f32)
    gf_ref[1 - me_depth] = other_opm_ref[...].astype(f32)
    for y, e, block in (
        (me_y, me_depth, normed_ref),
        (1 - me_y, me_depth, far_normed_ref),
        (me_y, 1 - me_depth, other_normed_ref),
        (1 - me_y, 1 - me_depth, other_far_normed_ref),
    ):
        rows_ref[y, e] = block[...]

    for il in range(here):
        for e in range(depths):
            first = pl.multiple_of((first_here + il) * pair_cols, pair_cols)
            grow_ref[il * residues + e * pair_cols : il * residues + (e + 1) * pair_cols, :] = (
                gf_ref[e, pl.ds(first, pair_cols), :].astype(bf16)
            )
    my_half = first_here // pair_cols
    my_first = first_here - my_half * pair_cols
    for jl in range(here):
        gcol_ref[jl * residues : (jl + 1) * residues, :] = gf_ref[
            my_half, pl.ds(my_first + jl, residues, stride=pair_cols), :
        ].astype(bf16)
    for lhs, weight, out in ((grow_ref, wturn_ref, gor_ref), (gcol_ref, wout_ref, goc_ref)):
        for dh in range(width // 4):
            piece = lax.dot_general(
                lhs[...],
                weight[dh * lanes : (dh + 1) * lanes, :],
                (((1,), (1,)), ((), ())),
                preferred_element_type=f32,
            )
            for y in range(2):
                turned = butterfly(
                    [
                        piece[(y * res + a) * residues : (y * res + a + 1) * residues]
                        for a in range(4)
                    ],
                    width,
                )
                for dl in range(4):
                    first = (dh * 4 + dl) * residues
                    out[first : first + residues, y * lanes : (y + 1) * lanes] = turned[dl].astype(
                        bf16
                    )
    group = lax.broadcasted_iota(jnp.int32, (here, here * width), 1) // width
    spread = (group == lax.broadcasted_iota(jnp.int32, (here, here * width), 0)).astype(f32)
    mask_lanes = lax.dot_general(
        maskt_ref[pl.ds(pl.multiple_of(first_here, here), here), :],
        spread,
        (((0,), (0,)), ((), ())),
        preferred_element_type=f32,
    )
    lane_group = lax.broadcasted_iota(jnp.int32, (seqs, lanes), 1) // width
    for at, (lhs, rhs) in enumerate(((rightt_ref, gor_ref), (leftt_ref, goc_ref))):
        total = lax.dot_general(
            lhs[...], rhs[...], (((0,), (0,)), ((), ())), preferred_element_type=f32
        )
        total = (total * mask_lanes).astype(bf16).astype(f32)
        for y in range(2):
            for e in range(depths):
                block = total[e * seqs : (e + 1) * seqs, y * lanes : (y + 1) * lanes]
                for r in range(res):
                    gs_ref[at, y, e, pl.ds(r, seqs, stride=res), :] = jnp.where(
                        lane_group == r, block, 0.0
                    )
    spread_ref[...] = jnp.concatenate(
        [gs_ref[0, me_y, me_depth], gs_ref[1, me_y, me_depth]], axis=1
    ).astype(bf16)
    rows = rows_ref.shape[2]
    for at in range(2):
        cross = lax.dot_general(
            gs_ref[at].reshape(2 * depths * rows, lanes).astype(bf16),
            rows_ref[...].reshape(2 * depths * rows, rows_ref.shape[3]),
            (((0,), (0,)), ((), ())),
            preferred_element_type=f32,
        )
        total = cross[:width]
        for r in range(1, res):
            total = total + cross[r * width : (r + 1) * width]
        part_ref[at * width : (at + 1) * width, :] = total.astype(bf16)


def weights_kernel(outer_ref, opm_ref, pn_ref, gh_ref, hidden_ref, mg_ref, out_ref, turn_ref):
    pair_width, hid = pn_ref.shape[1], gh_ref.shape[1]
    outer_width = outer_ref.shape[1]
    width = int(outer_width**0.5 + 0.5)

    def contract(lhs, rhs):
        return lax.dot_general(
            lhs[...], rhs[...], (((0,), (0,)), ((), ())), preferred_element_type=jnp.float32
        )

    turn_ref[...] = contract(outer_ref, opm_ref)
    for c in range(width):
        out_ref[c * width : (c + 1) * width, :] = turn_ref[
            pl.ds(c, width, stride=width), :
        ].astype(jnp.bfloat16)
    dhid = contract(pn_ref, gh_ref).astype(jnp.bfloat16)
    for at in range(hid // pair_width):
        first = outer_width + at * pair_width
        out_ref[first : first + pair_width, :] = dhid[:, at * pair_width : (at + 1) * pair_width]
    out_ref[outer_width + hid :, :] = contract(hidden_ref, mg_ref).astype(jnp.bfloat16)


def weights_sum_kernel(mine_ref, other_ref, dout_ref, dhid_ref, dback_ref):
    pair_width, hid = dhid_ref.shape
    outer_width = dout_ref.shape[0]

    def added(first, count):
        rows = slice(first, first + count)
        return mine_ref[rows, :].astype(jnp.float32) + other_ref[rows, :].astype(jnp.float32)

    dout_ref[...] = added(0, outer_width)
    for at in range(hid // pair_width):
        dhid_ref[:, at * pair_width : (at + 1) * pair_width] = added(
            outer_width + at * pair_width, pair_width
        )
    dback_ref[...] = added(outer_width + hid, hid)


def feature_kernel(
    copies, spread_ref, first_ref, second_ref, scale_ref, scaled_ref, inv_ref, feat_ref
):
    back = jnp.dot(
        spread_ref[...],
        wide_projector(first_ref, second_ref, copies),
        preferred_element_type=jnp.float32,
    )
    feat_ref[...] = standardize_adjoint(
        back * scale_ref[...], scaled_ref[...], inv_ref[...]
    ).astype(jnp.bfloat16)


def swap_depth(block):
    return lax.ppermute(block, "depth", [(0, 1), (1, 0)])


def pairwise_sum(blocks):
    while len(blocks) > 1:
        blocks = [blocks[at] + blocks[at + 1] for at in range(0, len(blocks), 2)]
    return blocks[0]


def swap_col(block, partner):
    count = lax.axis_size("col")
    return lax.ppermute(block, "col", [(at, at ^ partner) for at in range(count)])


def whole_plan(
    alignment_activations,
    alignment_mask,
    pair_activation_input,
    pair_update_mask,
    pair_output_gradient,
    layer_scale_factor,
    first_projector,
    second_projector,
    output_weight,
    pair_norm_gain,
    hidden_weight,
    back_weight,
):
    seqs, res, channels = alignment_activations.shape
    width = first_projector.shape[1]
    outer_width = width * width
    cols = lax.axis_size("col")
    depths = lax.axis_size("depth")
    residues = res * cols
    pair_cols, pair_width = pair_activation_input.shape[1:]
    hid = hidden_weight.shape[1]
    per = res * pair_cols
    lanes = res * width
    rows = 2 * seqs + MASK_ROWS
    half = residues * pair_cols
    f32, bf16 = jnp.float32, jnp.bfloat16
    ids = jnp.stack([lax.axis_index("depth"), lax.axis_index("col")]).astype(jnp.int32)
    smem = pl.BlockSpec(memory_space=pltpu.SMEM)
    vmem = pl.BlockSpec(memory_space=pltpu.VMEM)
    params = pltpu.CompilerParams(vmem_limit_bytes=16 * 2**20)
    scale = layer_scale_factor.reshape(1, channels)
    first, second = first_projector.T, second_projector.T
    wturn = jnp.transpose(output_weight.reshape(width, width, pair_width), (1, 0, 2)).reshape(
        outer_width, pair_width
    )
    shape = jax.ShapeDtypeStruct
    sent, scale, first, second, gain, normed, scaled, inv = pl.pallas_call(
        pre_kernel,
        out_shape=(
            shape((1, rows + 2 * per, pair_width), bf16),
            shape((1, channels), f32),
            shape((width, channels), bf16),
            shape((width, channels), bf16),
            shape((1, pair_width), f32),
            shape((seqs * res, channels), bf16),
            shape((seqs * res, channels), f32),
            shape((seqs * res, 1), f32),
        ),
        in_specs=[smem] + [pl.BlockSpec(memory_space=pltpu.HBM)] * 9,
        out_specs=[vmem] * 8,
        scratch_shapes=[
            pltpu.VMEM((2, seqs * res, lanes), f32),
            pltpu.VMEM((MASK_ROWS, lanes), f32),
            pltpu.VMEM((seqs, res, channels), bf16),
            pltpu.VMEM((res, seqs), jnp.int32),
            pltpu.VMEM((res, pair_cols), jnp.int32),
            pltpu.SemaphoreType.DMA((9,)),
        ],
        compiler_params=params,
        name="project",
    )(
        ids,
        *[
            pltpu.with_memory_space_constraint(array, pltpu.HBM)
            for array in (
                alignment_activations,
                alignment_mask.T,
                pair_update_mask,
                scale,
                first,
                second,
                pair_norm_gain.reshape(1, pair_width),
                pair_activation_input.reshape(per, pair_width),
                pair_output_gradient.reshape(per, pair_width),
            )
        ],
    )
    near_order = (0,) + Z_PARTNERS
    far_order = tuple(at ^ Y_PARTNER for at in near_order)
    blocks = lax.optimization_barrier(
        jnp.concatenate([sent] + [swap_col(sent, partner) for partner in Z_PARTNERS])
    )
    near, pair_near = blocks[:, :rows], blocks[:, rows:]
    far = swap_col(near, Y_PARTNER)
    pair_far = swap_col(pair_near, Y_PARTNER)
    far, normed = lax.optimization_barrier((far, normed))
    far_normed = swap_col(normed, Y_PARTNER)
    other_near, other_far = swap_depth(near), swap_depth(far)
    sizes = (seqs, res, pair_cols, width)
    orders = (near_order, far_order)
    outer, proj_out, cnt, pm, maskt = pl.pallas_call(
        functools.partial(outer_kernel, sizes, orders),
        out_shape=(
            shape((half, outer_width), bf16),
            shape((half, pair_width), f32),
            shape((half, lanes), f32),
            shape((half, lanes), bf16),
            shape((residues, depths * seqs), f32),
        ),
        in_specs=[smem] + [vmem] * 5,
        out_specs=[vmem] * 5,
        scratch_shapes=[
            pltpu.VMEM((depths, cols, rows, pair_width), bf16),
            pltpu.VMEM((depths * seqs, residues * width), bf16),
            pltpu.VMEM((pair_cols * width, depths * seqs), bf16),
            pltpu.VMEM((pair_cols * width, depths * seqs), f32),
            pltpu.VMEM((half, lanes), bf16),
            pltpu.VMEM((half, lanes), bf16),
        ],
        compiler_params=params,
        name="outer_products",
    )(ids, near, far, other_near, other_far, wturn)
    other_near, other_far, proj_out = lax.optimization_barrier((other_near, other_far, proj_out))
    rightt, leftt = pl.pallas_call(
        functools.partial(turn_kernel, sizes, orders),
        out_shape=(
            shape((residues * width, depths * seqs), bf16),
            shape((residues * width, depths * seqs), bf16),
        ),
        in_specs=[smem] + [vmem] * 4,
        out_specs=[vmem] * 2,
        scratch_shapes=[
            pltpu.VMEM((depths, cols, 2 * seqs, pair_width), bf16),
            pltpu.VMEM((residues * width, depths * seqs), f32),
        ],
        compiler_params=params,
        name="turned",
    )(ids, near, far, other_near, other_far)
    pair_far, rightt, leftt, proj_out = lax.optimization_barrier(
        (pair_far, rightt, leftt, proj_out)
    )
    couple, opm, pn, gh, hidden, mg = pl.pallas_call(
        functools.partial(transition_kernel, sizes, orders),
        out_shape=(
            shape((per, pair_width), bf16),
            shape((half, pair_width), bf16),
            shape((half, pair_width), bf16),
            shape((half, hid), bf16),
            shape((half, hid), bf16),
            shape((half, pair_width), bf16),
        ),
        in_specs=[smem] + [vmem] * 8,
        out_specs=[vmem] * 6,
        scratch_shapes=[
            pltpu.VMEM((cols, 2 * per, pair_width), bf16),
            pltpu.VMEM((half, pair_width), f32),
        ],
        compiler_params=params,
        name="transition",
    )(
        ids,
        pair_near,
        pair_far,
        proj_out,
        cnt,
        pm,
        gain,
        hidden_weight,
        back_weight,
    )
    opm, far_normed = lax.optimization_barrier((opm, far_normed))
    weights = pl.pallas_call(
        weights_kernel,
        out_shape=shape((outer_width + 2 * hid, pair_width), bf16),
        in_specs=[vmem] * 6,
        out_specs=vmem,
        scratch_shapes=[pltpu.VMEM((outer_width, pair_width), f32)],
        compiler_params=params,
        name="weight_gradients",
    )(outer, opm, pn, gh, hidden, mg)
    other_opm, other_normed, other_far_normed, weights = lax.optimization_barrier(
        (swap_depth(opm), swap_depth(normed), swap_depth(far_normed), weights)
    )
    part, spread = pl.pallas_call(
        functools.partial(projector_kernel, sizes),
        out_shape=(
            shape((2 * width, channels), bf16),
            shape((seqs * res, 2 * lanes), bf16),
        ),
        in_specs=[smem] + [vmem] * 11,
        out_specs=[vmem] * 2,
        scratch_shapes=[
            pltpu.VMEM((depths, half, pair_width), f32),
            pltpu.VMEM((2 * res * residues, pair_width), bf16),
            pltpu.VMEM((2 * res * residues, pair_width), bf16),
            pltpu.VMEM((residues * width, 2 * lanes), bf16),
            pltpu.VMEM((residues * width, 2 * lanes), bf16),
            pltpu.VMEM((2, 2, depths, seqs * res, lanes), f32),
            pltpu.VMEM((2, depths, seqs * res, channels), bf16),
        ],
        compiler_params=params,
        name="projector_parts",
    )(
        ids,
        opm,
        other_opm,
        rightt,
        leftt,
        output_weight,
        wturn,
        maskt,
        normed,
        far_normed,
        other_normed,
        other_far_normed,
    )
    feat = pl.pallas_call(
        functools.partial(feature_kernel, res),
        out_shape=shape((seqs * res, channels), bf16),
        in_specs=[vmem] * 6,
        out_specs=vmem,
        compiler_params=params,
        name="features",
    )(spread, first, second, scale, scaled, inv)
    came = [swap_col(part, partner) for partner in Z_PARTNERS]
    came[2], weights = lax.optimization_barrier((came[2], weights))
    dout, dhid, dback = pl.pallas_call(
        weights_sum_kernel,
        out_shape=(
            shape((outer_width, pair_width), f32),
            shape((pair_width, hid), f32),
            shape((hid, pair_width), f32),
        ),
        in_specs=[vmem] * 2,
        out_specs=[vmem] * 3,
        compiler_params=params,
        name="sums_over_depth",
    )(weights, swap_depth(weights))
    came, feat, dout, dhid, dback = lax.optimization_barrier((came, feat, dout, dhid, dback))
    total = pairwise_sum([block.astype(f32) for block in [part] + came])
    return (
        feat.reshape(seqs, res, channels),
        couple.reshape(res, pair_cols, pair_width),
        total[:width].T,
        total[width:].T,
        dout,
        dhid,
        dback,
    )


def on_device(alignment_activations, *others):
    cols = lax.axis_size("col")
    residues = alignment_activations.shape[1] * cols
    plan = whole_plan if cols == 8 and residues <= FEW_RESIDUES else split_plan
    return plan(alignment_activations, *others)


def solution(mesh):
    in_specs = (
        P(("group", "depth"), "col", None),
        P(("group", "depth"), "col"),
        P(("group", "col"), "depth", None),
        P(("group", "col"), "depth"),
        P(("group", "col"), "depth", None),
        P(),
        P(),
        P(),
        P(),
        P(),
        P(),
        P(),
    )
    out_specs = (
        P(("group", "depth"), "col", None),
        P(("group", "col"), "depth", None),
        P("group", None),
        P("group", None),
        P("group", None),
        P("group", None),
        P("group", None),
    )
    return jax.shard_map(
        on_device, mesh=mesh, in_specs=in_specs, out_specs=out_specs, check_vma=False
    )
```

```python
import functools

import jax
import jax.numpy as jnp
from jax import lax
from jax.experimental import pallas as pl
from jax.experimental.pallas import tpu as pltpu
from jax.sharding import PartitionSpec as P

epsilon = 1e-05
highest = lax.Precision.HIGHEST


def norm_pieces(entries_drawn):
    center = entries_drawn - jnp.mean(entries_drawn, axis=-1, keepdims=True)
    inv_std = lax.rsqrt(jnp.mean(center * center, axis=-1, keepdims=True) + epsilon)
    return (center * inv_std, inv_std)


def standardize_adjoint(grad_scaled, scaled, inv_std):
    mean_grad = jnp.mean(grad_scaled, axis=-1, keepdims=True)
    mean_cross = jnp.mean(grad_scaled * scaled, axis=-1, keepdims=True)
    return inv_std * (grad_scaled - mean_grad - scaled * mean_cross)


def silu_pieces(pre_act):
    sigma = jax.nn.sigmoid(pre_act)
    return (pre_act * sigma, sigma * (1.0 + pre_act * (1.0 - sigma)))


def split_plan(
    alignment_activations,
    alignment_mask,
    pair_activation_input,
    pair_update_mask,
    pair_output_gradient,
    layer_scale_factor,
    first_projector,
    second_projector,
    output_weight,
    pair_norm_gain,
    hidden_weight,
    back_weight,
):
    sequence_row_block, residue_row_block, channel_total = alignment_activations.shape
    proj_width = first_projector.shape[1]
    outer_width = proj_width * proj_width
    depth_count = lax.axis_size("depth")
    residues = residue_row_block * lax.axis_size("col")
    pair_cols = pair_activation_input.shape[1]
    pair_width = pair_activation_input.shape[2]
    col_block = min(64, pair_cols)
    block_count = pair_cols // col_block
    standardized_features, reciprocal_spread = norm_pieces(
        alignment_activations.astype(jnp.float32)
    )
    normalized_rows = (standardized_features * layer_scale_factor).astype(jnp.bfloat16)
    mask_floating = alignment_mask.astype(jnp.float32)
    left_proj = (
        jnp.dot(normalized_rows, first_projector, preferred_element_type=jnp.float32)
        * mask_floating[:, :, None]
    ).astype(jnp.bfloat16)
    right_proj = (
        jnp.dot(normalized_rows, second_projector, preferred_element_type=jnp.float32)
        * mask_floating[:, :, None]
    ).astype(jnp.bfloat16)
    right_flat = right_proj.reshape(sequence_row_block, residue_row_block * proj_width)
    mask_converted = alignment_mask.astype(jnp.bfloat16)
    seq_total = left_proj.shape[0]
    gathered, gathered_mask = (
        lax.all_gather(right_flat, "col", axis=1, tiled=True),
        lax.all_gather(mask_converted, "col", axis=1, tiled=True),
    )
    right_blocks = gathered.reshape(seq_total, depth_count, pair_cols, proj_width)
    mask_blocks = gathered_mask.reshape(seq_total, depth_count, pair_cols)
    block_depth = right_blocks.shape[1]
    out_wide = output_weight.astype(jnp.float32)

    def partial_outer(col_start):
        right_piece = lax.dynamic_slice_in_dim(right_blocks, col_start, col_block, 2)
        outer_part = jnp.einsum(
            "sic,sejd->iejcd", left_proj, right_piece, preferred_element_type=jnp.float32
        )
        return (
            outer_part.reshape(residue_row_block, block_depth, col_block, outer_width),
            right_piece,
        )

    def forward_step(step_index, loop_state):
        projected, pair_count = loop_state
        col_start = step_index * col_block
        outer_part, right_piece = partial_outer(col_start)
        mask_piece = lax.dynamic_slice_in_dim(mask_blocks, col_start, col_block, 2).astype(
            jnp.float32
        )
        count_part = jnp.einsum("si,sej->iej", mask_floating, mask_piece, precision=highest)
        outer_mine, count_mine = (
            lax.psum_scatter(
                outer_part.astype(jnp.bfloat16), "depth", scatter_dimension=1, tiled=True
            ).astype(jnp.float32),
            lax.psum_scatter(
                count_part.astype(jnp.bfloat16), "depth", scatter_dimension=1, tiled=True
            ).astype(jnp.float32),
        )
        proj_mine = jnp.dot(
            outer_mine.reshape(residue_row_block * col_block, outer_width),
            out_wide,
            precision=highest,
        )
        proj_mine = proj_mine.reshape(residue_row_block, col_block, pair_width)
        count_mine = count_mine.reshape(residue_row_block, col_block)
        projected = lax.dynamic_update_slice_in_dim(projected, proj_mine, col_start, 1)
        pair_count = lax.dynamic_update_slice_in_dim(pair_count, count_mine, col_start, 1)
        return (projected, pair_count)

    projected, pair_count = lax.fori_loop(
        0,
        block_count,
        forward_step,
        (
            jnp.zeros((residue_row_block, pair_cols, pair_width), jnp.float32),
            jnp.zeros((residue_row_block, pair_cols), jnp.float32),
        ),
    )
    count_column = pair_count.reshape(residue_row_block * pair_cols, 1)
    mid_act = (
        pair_activation_input.reshape(residue_row_block * pair_cols, pair_width).astype(jnp.float32)
        + projected.reshape(residue_row_block * pair_cols, pair_width) / count_column
    )
    pair_scaled, pair_inv = norm_pieces(mid_act)
    pair_normed = (pair_scaled * pair_norm_gain).astype(jnp.bfloat16)
    pre_act = jnp.dot(pair_normed, hidden_weight, preferred_element_type=jnp.float32)
    act_value, act_slope = silu_pieces(pre_act)
    hidden = act_value.astype(jnp.bfloat16)
    masked_grad = (
        pair_output_gradient * pair_update_mask.astype(jnp.bfloat16)[:, :, None]
    ).reshape(residue_row_block * pair_cols, pair_width)
    final_matrix_derivative = jnp.dot(hidden.T, masked_grad, preferred_element_type=jnp.float32)
    back_prod = jnp.dot(masked_grad, back_weight.T, preferred_element_type=jnp.float32)
    grad_hidden = (back_prod * act_slope).astype(jnp.bfloat16)
    middle_matrix_derivative = jnp.dot(
        pair_normed.T, grad_hidden, preferred_element_type=jnp.float32
    )
    grad_scaled = (
        jnp.dot(grad_hidden, hidden_weight.T, preferred_element_type=jnp.float32) * pair_norm_gain
    )
    grad_mid = pair_output_gradient.reshape(residue_row_block * pair_cols, pair_width).astype(
        jnp.float32
    ) + standardize_adjoint(grad_scaled, pair_scaled, pair_inv)
    couple_features_derivative = grad_mid.astype(jnp.bfloat16).reshape(
        residue_row_block, pair_cols, pair_width
    )
    grad_opm = (
        (grad_mid / count_column)
        .astype(jnp.bfloat16)
        .reshape(residue_row_block, pair_cols, pair_width)
    )
    full_opm = lax.all_gather(grad_opm, "depth", axis=1, tiled=True).reshape(
        residue_row_block, depth_count, pair_cols, pair_width
    )

    def backward_step(step_index, loop_state):
        grad_left_acc, grad_out, right_term = loop_state
        col_start = step_index * col_block
        outer_part, right_piece = partial_outer(col_start)
        opm_piece = lax.dynamic_slice_in_dim(full_opm, col_start, col_block, 2).reshape(
            residue_row_block * block_depth * col_block, pair_width
        )
        grad_out = grad_out + jnp.dot(
            outer_part.reshape(residue_row_block * block_depth * col_block, outer_width).T,
            opm_piece.astype(jnp.float32),
            precision=highest,
        )
        grad_outer = jnp.dot(opm_piece, output_weight.T, preferred_element_type=jnp.float32).astype(
            jnp.bfloat16
        )
        grad_outer = grad_outer.reshape(
            residue_row_block, block_depth, col_block, proj_width, proj_width
        )
        grad_left_acc = grad_left_acc + jnp.einsum(
            "iejcd,sejd->sic", grad_outer, right_piece, preferred_element_type=jnp.float32
        )
        piece_term = jnp.einsum(
            "iejcd,sic->ejsd", grad_outer, left_proj, preferred_element_type=jnp.float32
        )
        piece_term = piece_term.reshape(block_depth, col_block, seq_total * proj_width)
        right_term = lax.dynamic_update_slice_in_dim(right_term, piece_term, col_start, 1)
        return (grad_left_acc, grad_out, right_term)

    grad_left_acc, result_matrix_derivative, right_term = lax.fori_loop(
        0,
        block_count,
        backward_step,
        (
            jnp.zeros((seq_total, residue_row_block, proj_width), jnp.float32),
            jnp.zeros((outer_width, pair_width), jnp.float32),
            jnp.zeros((block_depth, pair_cols, seq_total * proj_width), jnp.float32),
        ),
    )
    grad_right_sum = lax.psum_scatter(
        right_term.reshape(residues, seq_total * proj_width), "col", scatter_dimension=0, tiled=True
    )
    grad_right_acc = jnp.transpose(
        grad_right_sum.reshape(residue_row_block, seq_total, proj_width), (1, 0, 2)
    )
    grad_left = (grad_left_acc * mask_floating[:, :, None]).astype(jnp.bfloat16)
    grad_right = (grad_right_acc * mask_floating[:, :, None]).astype(jnp.bfloat16)
    normed_rows = normalized_rows.reshape(sequence_row_block * residue_row_block, channel_total)
    first_projector_derivative = jnp.dot(
        normed_rows.T,
        grad_left.reshape(sequence_row_block * residue_row_block, proj_width),
        preferred_element_type=jnp.float32,
    )
    second_projector_derivative = jnp.dot(
        normed_rows.T,
        grad_right.reshape(sequence_row_block * residue_row_block, proj_width),
        preferred_element_type=jnp.float32,
    )
    standardized_derivative = jnp.dot(
        grad_left, first_projector.T, preferred_element_type=jnp.float32
    ) + jnp.dot(grad_right, second_projector.T, preferred_element_type=jnp.float32)
    features_derivative = standardize_adjoint(
        standardized_derivative * layer_scale_factor, standardized_features, reciprocal_spread
    ).astype(jnp.bfloat16)
    weight_sums = lax.psum(
        (
            first_projector_derivative,
            second_projector_derivative,
            result_matrix_derivative,
            middle_matrix_derivative,
            final_matrix_derivative,
        ),
        ("depth", "col"),
    )
    return (
        features_derivative,
        couple_features_derivative,
        weight_sums[0],
        weight_sums[1],
        weight_sums[2],
        weight_sums[3],
        weight_sums[4],
    )


FEW_RESIDUES = 32
MASK_ROWS = 16
Z_PARTNERS = (6, 4, 2)
Y_PARTNER = 1


def butterfly(blocks, group):
    lane_group = lax.broadcasted_iota(jnp.int32, blocks[0].shape, 1) // group
    width = 4 * group
    for bit in (2, 1):
        low = (lane_group & bit) == 0
        swapped = list(blocks)
        for at in range(4):
            if at & bit:
                continue
            here, there = blocks[at], blocks[at | bit]
            moving = jnp.where(low, there, here)
            if bit == 2:
                moved = pltpu.roll(moving, 2 * group, 1)
            else:
                moved = jnp.where(
                    low, pltpu.roll(moving, width - group, 1), pltpu.roll(moving, group, 1)
                )
            swapped[at] = jnp.where(low, here, moved)
            swapped[at | bit] = jnp.where(low, moved, there)
        blocks = swapped
    return blocks


def wide_projector(first_ref, second_ref, copies):
    return jnp.concatenate([first_ref[...]] * copies + [second_ref[...]] * copies, axis=0)


def pre_kernel(
    ids_ref,
    x_hbm,
    maskt_hbm,
    pmask_hbm,
    scale_hbm,
    first_hbm,
    second_hbm,
    gain_hbm,
    act_hbm,
    grad_hbm,
    sent_ref,
    scale_ref,
    first_ref,
    second_ref,
    gain_ref,
    normed_ref,
    scaled_ref,
    inv_ref,
    wide_ref,
    tile_ref,
    x_ref,
    maskt_ref,
    pmask_ref,
    sems,
):
    res, seqs = maskt_ref.shape
    pairs = act_hbm.shape[0]
    first_pair = 2 * seqs + MASK_ROWS
    copies = [
        pltpu.make_async_copy(source, target, sems.at[at])
        for at, (source, target) in enumerate(
            (
                (x_hbm, x_ref),
                (maskt_hbm, maskt_ref),
                (pmask_hbm, pmask_ref),
                (scale_hbm, scale_ref),
                (first_hbm, first_ref),
                (second_hbm, second_ref),
                (gain_hbm, gain_ref),
                (act_hbm, sent_ref.at[0, pl.ds(first_pair, pairs), :]),
                (grad_hbm, sent_ref.at[0, pl.ds(first_pair + pairs, pairs), :]),
            )
        )
    ]
    for copy in copies:
        copy.start()
    for copy in copies:
        copy.wait()
    lanes = sent_ref.shape[2]
    group = lanes // res
    scaled, inv = norm_pieces(
        x_ref[...].astype(jnp.float32).reshape(seqs * res, x_ref.shape[2])
    )
    scaled_ref[...] = scaled
    inv_ref[...] = inv
    normed = (scaled * scale_ref[...]).astype(jnp.bfloat16)
    normed_ref[...] = normed
    wide = lax.dot_general(
        normed,
        wide_projector(first_ref, second_ref, res),
        (((1,), (1,)), ((), ())),
        preferred_element_type=jnp.float32,
    )
    for at in range(2):
        wide_ref[at] = wide[:, at * lanes : (at + 1) * lanes]
    tile_ref[...] = jnp.zeros(tile_ref.shape, jnp.float32)
    mask = maskt_ref[...].astype(jnp.float32)
    tile_ref[0:res, 0:seqs] = mask
    spread = (
        lax.broadcasted_iota(jnp.int32, (MASK_ROWS, lanes), 1) // group
        == lax.broadcasted_iota(jnp.int32, (MASK_ROWS, lanes), 0)
    ).astype(jnp.float32)
    mask_lanes = lax.dot_general(
        tile_ref[...], spread, (((0,), (0,)), ((), ())), preferred_element_type=jnp.float32
    )[:seqs]
    twice = jnp.concatenate([mask] * (lanes // seqs), axis=1)
    here = lax.broadcasted_iota(jnp.int32, (res, lanes), 1) // seqs == ids_ref[0]
    tile_ref[0:res, :] = jnp.where(here, twice, 0.0)
    tile_ref[res : 2 * res, 0 : pmask_ref.shape[1]] = pmask_ref[...].astype(jnp.float32)
    lane_group = lax.broadcasted_iota(jnp.int32, (seqs, lanes), 1) // group
    for at in range(2):
        both = wide_ref[at, pl.ds(0, seqs, stride=res), :]
        for r in range(1, res):
            both = jnp.where(
                lane_group == r, wide_ref[at, pl.ds(r, seqs, stride=res), :], both
            )
        sent_ref[0, at * seqs : (at + 1) * seqs, :] = (both * mask_lanes).astype(jnp.bfloat16)
    sent_ref[0, 2 * seqs : first_pair, :] = tile_ref[...].astype(jnp.bfloat16)


def outer_kernel(
    sizes,
    orders,
    ids_ref,
    near_ref,
    far_ref,
    other_near_ref,
    other_far_ref,
    wturn_ref,
    outer_ref,
    proj_out_ref,
    cnt_ref,
    pm_ref,
    maskt_ref,
    got_ref,
    leftn_ref,
    mine_ref,
    turn_ref,
    cntl_ref,
    pml_ref,
):
    seqs, res, pair_cols, width = sizes
    depths, cols = got_ref.shape[0], got_ref.shape[1]
    residues = cols * res
    lanes = res * width
    half_cols = pair_cols // res
    me_depth = ids_ref[0]
    me_col = ids_ref[1]
    f32, bf16 = jnp.float32, jnp.bfloat16

    for order, mine, other in zip(orders, (near_ref, far_ref), (other_near_ref, other_far_ref)):
        for at, partner in enumerate(order):
            got_ref[me_depth, me_col ^ partner] = mine[at]
            got_ref[1 - me_depth, me_col ^ partner] = other[at]

    for e in range(depths):
        for k in range(cols):
            leftn_ref[e * seqs : (e + 1) * seqs, k * lanes : (k + 1) * lanes] = got_ref[
                e, k, 0:seqs, :
            ]
    for k in range(half_cols):
        block = jnp.concatenate(
            [
                got_ref[e, me_depth * half_cols + k, seqs : 2 * seqs, :]
                for e in range(depths)
            ],
            axis=0,
        ).astype(f32)
        turn_ref[k * lanes : (k + 1) * lanes, :] = block.T
    for d in range(width):
        mine_ref[d * pair_cols : (d + 1) * pair_cols, :] = turn_ref[
            pl.ds(d, pair_cols, stride=width), :
        ].astype(bf16)

    base = 2 * seqs
    pair_lane = lax.broadcasted_iota(jnp.int32, (pair_cols, lanes), 1)
    pair_row = lax.broadcasted_iota(jnp.int32, (pair_cols, lanes), 0)
    for k in range(cols):
        tiles = [got_ref[e, k, base : base + MASK_ROWS, :].astype(f32) for e in range(depths)]
        maskt_ref[k * res : (k + 1) * res, :] = tiles[0][0:res] + tiles[1][0:res]
        own = got_ref[me_depth, k, base : base + MASK_ROWS, :].astype(f32)
        for r in range(res):
            row = own[res + r : res + r + 1, :]
            first = (k * res + r) * pair_cols
            pml_ref[first : first + pair_cols, :] = jnp.where(
                pair_lane == pair_row, row, 0.0
            ).astype(bf16)
    maskt = maskt_ref[...]
    cols_mask = maskt_ref[pl.ds(pl.multiple_of(me_depth * pair_cols, pair_cols), pair_cols), :]
    for i in range(residues):
        cntl_ref[i * pair_cols : (i + 1) * pair_cols, :] = (maskt[i : i + 1, :] * cols_mask).astype(
            bf16
        )
    ones = jnp.ones((lanes, lanes), bf16)
    cnt_ref[...] = jnp.dot(cntl_ref[...], ones, preferred_element_type=f32)
    pm_ref[...] = jnp.dot(pml_ref[...], ones, preferred_element_type=f32).astype(bf16)

    for dh in range(width // 4):
        prod = jnp.dot(
            mine_ref[dh * 4 * pair_cols : (dh + 1) * 4 * pair_cols, :],
            leftn_ref[...],
            preferred_element_type=f32,
        )
        for k in range(cols):
            piece = prod[:, k * lanes : (k + 1) * lanes]
            turned = butterfly(
                [piece[a * pair_cols : (a + 1) * pair_cols] for a in range(4)], width
            )
            for il in range(res):
                first = (k * res + il) * pair_cols
                outer_ref[first : first + pair_cols, dh * lanes : (dh + 1) * lanes] = turned[
                    il
                ].astype(bf16)
    proj_out_ref[...] = jnp.dot(outer_ref[...], wturn_ref[...], preferred_element_type=f32)


def turn_kernel(
    sizes,
    orders,
    ids_ref,
    near_ref,
    far_ref,
    other_near_ref,
    other_far_ref,
    rightt_ref,
    leftt_ref,
    got_ref,
    turn_ref,
):
    seqs, res, _, width = sizes
    depths, cols = got_ref.shape[0], got_ref.shape[1]
    lanes = res * width
    residues = res * cols
    me_depth = ids_ref[0]
    me_col = ids_ref[1]
    for order, mine, other in zip(orders, (near_ref, far_ref), (other_near_ref, other_far_ref)):
        for at, partner in enumerate(order):
            got_ref[me_depth, me_col ^ partner] = mine[at, 0 : 2 * seqs, :]
            got_ref[1 - me_depth, me_col ^ partner] = other[at, 0 : 2 * seqs, :]
    for at, out in ((0, leftt_ref), (1, rightt_ref)):
        for k in range(cols):
            block = jnp.concatenate(
                [got_ref[e, k, at * seqs : (at + 1) * seqs, :] for e in range(depths)], axis=0
            ).astype(jnp.float32)
            turn_ref[k * lanes : (k + 1) * lanes, :] = block.T
        for d in range(width):
            out[d * residues : (d + 1) * residues, :] = turn_ref[
                pl.ds(d, residues, stride=width), :
            ].astype(jnp.bfloat16)


def transition_kernel(
    sizes,
    orders,
    ids_ref,
    near_ref,
    far_ref,
    proj_out_ref,
    cnt_ref,
    pm_ref,
    gain_ref,
    hid_ref,
    back_ref,
    couple_ref,
    opm_ref,
    pn_ref,
    gh_ref,
    hidden_ref,
    mg_ref,
    pgot_ref,
    gmid_ref,
):
    seqs, res, pair_cols, width = sizes
    per = res * pair_cols
    cols = pgot_ref.shape[0]
    me_col = ids_ref[1]
    f32, bf16 = jnp.float32, jnp.bfloat16
    for order, mine in zip(orders, (near_ref, far_ref)):
        for at, partner in enumerate(order):
            pgot_ref[me_col ^ partner] = mine[at]
    gain = gain_ref[...]
    chunk = 2 * per
    for at in range(cols // 2):
        rows = slice(at * chunk, (at + 1) * chunk)
        act, grad = [
            jnp.concatenate(
                [pgot_ref[2 * at + b, w * per : (w + 1) * per, :] for b in range(2)], axis=0
            )
            for w in range(2)
        ]
        count = cnt_ref[rows, :]
        mid = act.astype(f32) + proj_out_ref[rows, :] / count
        scaled, inv = norm_pieces(mid)
        normed = (scaled * gain).astype(bf16)
        pn_ref[rows, :] = normed
        pre = jnp.dot(normed, hid_ref[...], preferred_element_type=f32)
        value, slope = silu_pieces(pre)
        hidden_ref[rows, :] = value.astype(bf16)
        masked = grad * pm_ref[rows, :]
        mg_ref[rows, :] = masked
        back = lax.dot_general(
            masked, back_ref[...], (((1,), (1,)), ((), ())), preferred_element_type=f32
        )
        ghid = (back * slope).astype(bf16)
        gh_ref[rows, :] = ghid
        gsc = (
            lax.dot_general(
                ghid, hid_ref[...], (((1,), (1,)), ((), ())), preferred_element_type=f32
            )
            * gain
        )
        gmid = grad.astype(f32) + standardize_adjoint(gsc, scaled, inv)
        gmid_ref[rows, :] = gmid
        opm_ref[rows, :] = (gmid / count).astype(bf16)
    couple_ref[...] = gmid_ref[pl.ds(pl.multiple_of(me_col * per, per), per), :].astype(bf16)


def projector_kernel(
    sizes,
    ids_ref,
    opm_ref,
    other_opm_ref,
    rightt_ref,
    leftt_ref,
    wout_ref,
    wturn_ref,
    maskt_ref,
    normed_ref,
    far_normed_ref,
    other_normed_ref,
    other_far_normed_ref,
    part_ref,
    spread_ref,
    gf_ref,
    grow_ref,
    gcol_ref,
    gor_ref,
    goc_ref,
    gs_ref,
    rows_ref,
):
    seqs, res, pair_cols, width = sizes
    depths, half = gf_ref.shape[0], gf_ref.shape[1]
    residues = half // pair_cols
    lanes = res * width
    here = 2 * res
    me_depth = ids_ref[0]
    me_col = ids_ref[1]
    me_y = me_col % 2
    first_here = (me_col // 2) * here
    f32, bf16 = jnp.float32, jnp.bfloat16
    gf_ref[me_depth] = opm_ref[...].astype(f32)
    gf_ref[1 - me_depth] = other_opm_ref[...].astype(f32)
    for y, e, block in (
        (me_y, me_depth, normed_ref),
        (1 - me_y, me_depth, far_normed_ref),
        (me_y, 1 - me_depth, other_normed_ref),
        (1 - me_y, 1 - me_depth, other_far_normed_ref),
    ):
        rows_ref[y, e] = block[...]

    for il in range(here):
        for e in range(depths):
            first = pl.multiple_of((first_here + il) * pair_cols, pair_cols)
            grow_ref[il * residues + e * pair_cols : il * residues + (e + 1) * pair_cols, :] = (
                gf_ref[e, pl.ds(first, pair_cols), :].astype(bf16)
            )
    my_half = first_here // pair_cols
    my_first = first_here - my_half * pair_cols
    for jl in range(here):
        gcol_ref[jl * residues : (jl + 1) * residues, :] = gf_ref[
            my_half, pl.ds(my_first + jl, residues, stride=pair_cols), :
        ].astype(bf16)
    for lhs, weight, out in ((grow_ref, wturn_ref, gor_ref), (gcol_ref, wout_ref, goc_ref)):
        for dh in range(width // 4):
            piece = lax.dot_general(
                lhs[...],
                weight[dh * lanes : (dh + 1) * lanes, :],
                (((1,), (1,)), ((), ())),
                preferred_element_type=f32,
            )
            for y in range(2):
                turned = butterfly(
                    [
                        piece[(y * res + a) * residues : (y * res + a + 1) * residues]
                        for a in range(4)
                    ],
                    width,
                )
                for dl in range(4):
                    first = (dh * 4 + dl) * residues
                    out[first : first + residues, y * lanes : (y + 1) * lanes] = turned[dl].astype(
                        bf16
                    )
    group = lax.broadcasted_iota(jnp.int32, (here, here * width), 1) // width
    spread = (group == lax.broadcasted_iota(jnp.int32, (here, here * width), 0)).astype(f32)
    mask_lanes = lax.dot_general(
        maskt_ref[pl.ds(pl.multiple_of(first_here, here), here), :],
        spread,
        (((0,), (0,)), ((), ())),
        preferred_element_type=f32,
    )
    lane_group = lax.broadcasted_iota(jnp.int32, (seqs, lanes), 1) // width
    for at, (lhs, rhs) in enumerate(((rightt_ref, gor_ref), (leftt_ref, goc_ref))):
        total = lax.dot_general(
            lhs[...], rhs[...], (((0,), (0,)), ((), ())), preferred_element_type=f32
        )
        total = (total * mask_lanes).astype(bf16).astype(f32)
        for y in range(2):
            for e in range(depths):
                block = total[e * seqs : (e + 1) * seqs, y * lanes : (y + 1) * lanes]
                for r in range(res):
                    gs_ref[at, y, e, pl.ds(r, seqs, stride=res), :] = jnp.where(
                        lane_group == r, block, 0.0
                    )
    spread_ref[...] = jnp.concatenate(
        [gs_ref[0, me_y, me_depth], gs_ref[1, me_y, me_depth]], axis=1
    ).astype(bf16)
    rows = rows_ref.shape[2]
    for at in range(2):
        cross = lax.dot_general(
            gs_ref[at].reshape(2 * depths * rows, lanes).astype(bf16),
            rows_ref[...].reshape(2 * depths * rows, rows_ref.shape[3]),
            (((0,), (0,)), ((), ())),
            preferred_element_type=f32,
        )
        total = cross[:width]
        for r in range(1, res):
            total = total + cross[r * width : (r + 1) * width]
        part_ref[at * width : (at + 1) * width, :] = total.astype(bf16)


def weights_kernel(outer_ref, opm_ref, pn_ref, gh_ref, hidden_ref, mg_ref, out_ref, turn_ref):
    pair_width, hid = pn_ref.shape[1], gh_ref.shape[1]
    outer_width = outer_ref.shape[1]
    width = int(outer_width**0.5 + 0.5)

    def contract(lhs, rhs):
        return lax.dot_general(
            lhs[...], rhs[...], (((0,), (0,)), ((), ())), preferred_element_type=jnp.float32
        )

    turn_ref[...] = contract(outer_ref, opm_ref)
    for c in range(width):
        out_ref[c * width : (c + 1) * width, :] = turn_ref[
            pl.ds(c, width, stride=width), :
        ].astype(jnp.bfloat16)
    dhid = contract(pn_ref, gh_ref).astype(jnp.bfloat16)
    for at in range(hid // pair_width):
        first = outer_width + at * pair_width
        out_ref[first : first + pair_width, :] = dhid[:, at * pair_width : (at + 1) * pair_width]
    out_ref[outer_width + hid :, :] = contract(hidden_ref, mg_ref).astype(jnp.bfloat16)


def weights_sum_kernel(mine_ref, other_ref, dout_ref, dhid_ref, dback_ref):
    pair_width, hid = dhid_ref.shape
    outer_width = dout_ref.shape[0]

    def added(first, count):
        rows = slice(first, first + count)
        return mine_ref[rows, :].astype(jnp.float32) + other_ref[rows, :].astype(jnp.float32)

    dout_ref[...] = added(0, outer_width)
    for at in range(hid // pair_width):
        dhid_ref[:, at * pair_width : (at + 1) * pair_width] = added(
            outer_width + at * pair_width, pair_width
        )
    dback_ref[...] = added(outer_width + hid, hid)


def feature_kernel(
    copies, spread_ref, first_ref, second_ref, scale_ref, scaled_ref, inv_ref, feat_ref
):
    back = jnp.dot(
        spread_ref[...],
        wide_projector(first_ref, second_ref, copies),
        preferred_element_type=jnp.float32,
    )
    feat_ref[...] = standardize_adjoint(
        back * scale_ref[...], scaled_ref[...], inv_ref[...]
    ).astype(jnp.bfloat16)


def swap_depth(block):
    return lax.ppermute(block, "depth", [(0, 1), (1, 0)])


def pairwise_sum(blocks):
    while len(blocks) > 1:
        blocks = [blocks[at] + blocks[at + 1] for at in range(0, len(blocks), 2)]
    return blocks[0]


def swap_col(block, partner):
    count = lax.axis_size("col")
    return lax.ppermute(block, "col", [(at, at ^ partner) for at in range(count)])


def whole_plan(
    alignment_activations,
    alignment_mask,
    pair_activation_input,
    pair_update_mask,
    pair_output_gradient,
    layer_scale_factor,
    first_projector,
    second_projector,
    output_weight,
    pair_norm_gain,
    hidden_weight,
    back_weight,
):
    seqs, res, channels = alignment_activations.shape
    width = first_projector.shape[1]
    outer_width = width * width
    cols = lax.axis_size("col")
    depths = lax.axis_size("depth")
    residues = res * cols
    pair_cols, pair_width = pair_activation_input.shape[1:]
    hid = hidden_weight.shape[1]
    per = res * pair_cols
    lanes = res * width
    rows = 2 * seqs + MASK_ROWS
    half = residues * pair_cols
    f32, bf16 = jnp.float32, jnp.bfloat16
    ids = jnp.stack([lax.axis_index("depth"), lax.axis_index("col")]).astype(jnp.int32)
    smem = pl.BlockSpec(memory_space=pltpu.SMEM)
    vmem = pl.BlockSpec(memory_space=pltpu.VMEM)
    params = pltpu.CompilerParams(vmem_limit_bytes=16 * 2**20)
    scale = layer_scale_factor.reshape(1, channels)
    first, second = first_projector.T, second_projector.T
    wturn = jnp.transpose(output_weight.reshape(width, width, pair_width), (1, 0, 2)).reshape(
        outer_width, pair_width
    )
    shape = jax.ShapeDtypeStruct
    sent, scale, first, second, gain, normed, scaled, inv = pl.pallas_call(
        pre_kernel,
        out_shape=(
            shape((1, rows + 2 * per, pair_width), bf16),
            shape((1, channels), f32),
            shape((width, channels), bf16),
            shape((width, channels), bf16),
            shape((1, pair_width), f32),
            shape((seqs * res, channels), bf16),
            shape((seqs * res, channels), f32),
            shape((seqs * res, 1), f32),
        ),
        in_specs=[smem] + [pl.BlockSpec(memory_space=pltpu.HBM)] * 9,
        out_specs=[vmem] * 8,
        scratch_shapes=[
            pltpu.VMEM((2, seqs * res, lanes), f32),
            pltpu.VMEM((MASK_ROWS, lanes), f32),
            pltpu.VMEM((seqs, res, channels), bf16),
            pltpu.VMEM((res, seqs), jnp.int32),
            pltpu.VMEM((res, pair_cols), jnp.int32),
            pltpu.SemaphoreType.DMA((9,)),
        ],
        compiler_params=params,
        name="project",
    )(
        ids,
        *[
            pltpu.with_memory_space_constraint(array, pltpu.HBM)
            for array in (
                alignment_activations,
                alignment_mask.T,
                pair_update_mask,
                scale,
                first,
                second,
                pair_norm_gain.reshape(1, pair_width),
                pair_activation_input.reshape(per, pair_width),
                pair_output_gradient.reshape(per, pair_width),
            )
        ],
    )
    near_order = (0,) + Z_PARTNERS
    far_order = tuple(at ^ Y_PARTNER for at in near_order)
    blocks = lax.optimization_barrier(
        jnp.concatenate([sent] + [swap_col(sent, partner) for partner in Z_PARTNERS])
    )
    near, pair_near = blocks[:, :rows], blocks[:, rows:]
    far = swap_col(near, Y_PARTNER)
    pair_far = swap_col(pair_near, Y_PARTNER)
    far, normed = lax.optimization_barrier((far, normed))
    far_normed = swap_col(normed, Y_PARTNER)
    other_near, other_far = swap_depth(near), swap_depth(far)
    sizes = (seqs, res, pair_cols, width)
    orders = (near_order, far_order)
    outer, proj_out, cnt, pm, maskt = pl.pallas_call(
        functools.partial(outer_kernel, sizes, orders),
        out_shape=(
            shape((half, outer_width), bf16),
            shape((half, pair_width), f32),
            shape((half, lanes), f32),
            shape((half, lanes), bf16),
            shape((residues, depths * seqs), f32),
        ),
        in_specs=[smem] + [vmem] * 5,
        out_specs=[vmem] * 5,
        scratch_shapes=[
            pltpu.VMEM((depths, cols, rows, pair_width), bf16),
            pltpu.VMEM((depths * seqs, residues * width), bf16),
            pltpu.VMEM((pair_cols * width, depths * seqs), bf16),
            pltpu.VMEM((pair_cols * width, depths * seqs), f32),
            pltpu.VMEM((half, lanes), bf16),
            pltpu.VMEM((half, lanes), bf16),
        ],
        compiler_params=params,
        name="outer_products",
    )(ids, near, far, other_near, other_far, wturn)
    other_near, other_far, proj_out = lax.optimization_barrier((other_near, other_far, proj_out))
    rightt, leftt = pl.pallas_call(
        functools.partial(turn_kernel, sizes, orders),
        out_shape=(
            shape((residues * width, depths * seqs), bf16),
            shape((residues * width, depths * seqs), bf16),
        ),
        in_specs=[smem] + [vmem] * 4,
        out_specs=[vmem] * 2,
        scratch_shapes=[
            pltpu.VMEM((depths, cols, 2 * seqs, pair_width), bf16),
            pltpu.VMEM((residues * width, depths * seqs), f32),
        ],
        compiler_params=params,
        name="turned",
    )(ids, near, far, other_near, other_far)
    pair_far, rightt, leftt, proj_out = lax.optimization_barrier(
        (pair_far, rightt, leftt, proj_out)
    )
    couple, opm, pn, gh, hidden, mg = pl.pallas_call(
        functools.partial(transition_kernel, sizes, orders),
        out_shape=(
            shape((per, pair_width), bf16),
            shape((half, pair_width), bf16),
            shape((half, pair_width), bf16),
            shape((half, hid), bf16),
            shape((half, hid), bf16),
            shape((half, pair_width), bf16),
        ),
        in_specs=[smem] + [vmem] * 8,
        out_specs=[vmem] * 6,
        scratch_shapes=[
            pltpu.VMEM((cols, 2 * per, pair_width), bf16),
            pltpu.VMEM((half, pair_width), f32),
        ],
        compiler_params=params,
        name="transition",
    )(
        ids,
        pair_near,
        pair_far,
        proj_out,
        cnt,
        pm,
        gain,
        hidden_weight,
        back_weight,
    )
    opm, far_normed = lax.optimization_barrier((opm, far_normed))
    weights = pl.pallas_call(
        weights_kernel,
        out_shape=shape((outer_width + 2 * hid, pair_width), bf16),
        in_specs=[vmem] * 6,
        out_specs=vmem,
        scratch_shapes=[pltpu.VMEM((outer_width, pair_width), f32)],
        compiler_params=params,
        name="weight_gradients",
    )(outer, opm, pn, gh, hidden, mg)
    other_opm, other_normed, other_far_normed, weights = lax.optimization_barrier(
        (swap_depth(opm), swap_depth(normed), swap_depth(far_normed), weights)
    )
    part, spread = pl.pallas_call(
        functools.partial(projector_kernel, sizes),
        out_shape=(
            shape((2 * width, channels), bf16),
            shape((seqs * res, 2 * lanes), bf16),
        ),
        in_specs=[smem] + [vmem] * 11,
        out_specs=[vmem] * 2,
        scratch_shapes=[
            pltpu.VMEM((depths, half, pair_width), f32),
            pltpu.VMEM((2 * res * residues, pair_width), bf16),
            pltpu.VMEM((2 * res * residues, pair_width), bf16),
            pltpu.VMEM((residues * width, 2 * lanes), bf16),
            pltpu.VMEM((residues * width, 2 * lanes), bf16),
            pltpu.VMEM((2, 2, depths, seqs * res, lanes), f32),
            pltpu.VMEM((2, depths, seqs * res, channels), bf16),
        ],
        compiler_params=params,
        name="projector_parts",
    )(
        ids,
        opm,
        other_opm,
        rightt,
        leftt,
        output_weight,
        wturn,
        maskt,
        normed,
        far_normed,
        other_normed,
        other_far_normed,
    )
    feat = pl.pallas_call(
        functools.partial(feature_kernel, res),
        out_shape=shape((seqs * res, channels), bf16),
        in_specs=[vmem] * 6,
        out_specs=vmem,
        compiler_params=params,
        name="features",
    )(spread, first, second, scale, scaled, inv)
    part, weights = lax.optimization_barrier((part, weights))
    came = [swap_col(part, partner) for partner in Z_PARTNERS]
    dout, dhid, dback = pl.pallas_call(
        weights_sum_kernel,
        out_shape=(
            shape((outer_width, pair_width), f32),
            shape((pair_width, hid), f32),
            shape((hid, pair_width), f32),
        ),
        in_specs=[vmem] * 2,
        out_specs=[vmem] * 3,
        compiler_params=params,
        name="sums_over_depth",
    )(weights, swap_depth(weights))
    came, feat, dout, dhid, dback = lax.optimization_barrier((came, feat, dout, dhid, dback))
    total = pairwise_sum([block.astype(f32) for block in [part] + came])
    return (
        feat.reshape(seqs, res, channels),
        couple.reshape(res, pair_cols, pair_width),
        total[:width].T,
        total[width:].T,
        dout,
        dhid,
        dback,
    )


def on_device(alignment_activations, *others):
    cols = lax.axis_size("col")
    residues = alignment_activations.shape[1] * cols
    plan = whole_plan if cols == 8 and residues <= FEW_RESIDUES else split_plan
    return plan(alignment_activations, *others)


def solution(mesh):
    in_specs = (
        P(("group", "depth"), "col", None),
        P(("group", "depth"), "col"),
        P(("group", "col"), "depth", None),
        P(("group", "col"), "depth"),
        P(("group", "col"), "depth", None),
        P(),
        P(),
        P(),
        P(),
        P(),
        P(),
        P(),
    )
    out_specs = (
        P(("group", "depth"), "col", None),
        P(("group", "col"), "depth", None),
        P("group", None),
        P("group", None),
        P("group", None),
        P("group", None),
        P("group", None),
    )
    return jax.shard_map(
        on_device, mesh=mesh, in_specs=in_specs, out_specs=out_specs, check_vma=False
    )
```

```python
import functools

import jax
import jax.numpy as jnp
from jax import lax
from jax.experimental import pallas as pl
from jax.experimental.pallas import tpu as pltpu
from jax.sharding import PartitionSpec as P

epsilon = 1e-05
highest = lax.Precision.HIGHEST


def norm_pieces(entries_drawn):
    center = entries_drawn - jnp.mean(entries_drawn, axis=-1, keepdims=True)
    inv_std = lax.rsqrt(jnp.mean(center * center, axis=-1, keepdims=True) + epsilon)
    return (center * inv_std, inv_std)


def standardize_adjoint(grad_scaled, scaled, inv_std):
    mean_grad = jnp.mean(grad_scaled, axis=-1, keepdims=True)
    mean_cross = jnp.mean(grad_scaled * scaled, axis=-1, keepdims=True)
    return inv_std * (grad_scaled - mean_grad - scaled * mean_cross)


def silu_pieces(pre_act):
    sigma = jax.nn.sigmoid(pre_act)
    return (pre_act * sigma, sigma * (1.0 + pre_act * (1.0 - sigma)))


def split_plan(
    alignment_activations,
    alignment_mask,
    pair_activation_input,
    pair_update_mask,
    pair_output_gradient,
    layer_scale_factor,
    first_projector,
    second_projector,
    output_weight,
    pair_norm_gain,
    hidden_weight,
    back_weight,
):
    sequence_row_block, residue_row_block, channel_total = alignment_activations.shape
    proj_width = first_projector.shape[1]
    outer_width = proj_width * proj_width
    depth_count = lax.axis_size("depth")
    residues = residue_row_block * lax.axis_size("col")
    pair_cols = pair_activation_input.shape[1]
    pair_width = pair_activation_input.shape[2]
    col_block = min(64, pair_cols)
    block_count = pair_cols // col_block
    standardized_features, reciprocal_spread = norm_pieces(
        alignment_activations.astype(jnp.float32)
    )
    normalized_rows = (standardized_features * layer_scale_factor).astype(jnp.bfloat16)
    mask_floating = alignment_mask.astype(jnp.float32)
    left_proj = (
        jnp.dot(normalized_rows, first_projector, preferred_element_type=jnp.float32)
        * mask_floating[:, :, None]
    ).astype(jnp.bfloat16)
    right_proj = (
        jnp.dot(normalized_rows, second_projector, preferred_element_type=jnp.float32)
        * mask_floating[:, :, None]
    ).astype(jnp.bfloat16)
    right_flat = right_proj.reshape(sequence_row_block, residue_row_block * proj_width)
    mask_converted = alignment_mask.astype(jnp.bfloat16)
    seq_total = left_proj.shape[0]
    gathered, gathered_mask = (
        lax.all_gather(right_flat, "col", axis=1, tiled=True),
        lax.all_gather(mask_converted, "col", axis=1, tiled=True),
    )
    right_blocks = gathered.reshape(seq_total, depth_count, pair_cols, proj_width)
    mask_blocks = gathered_mask.reshape(seq_total, depth_count, pair_cols)
    block_depth = right_blocks.shape[1]
    out_wide = output_weight.astype(jnp.float32)

    def partial_outer(col_start):
        right_piece = lax.dynamic_slice_in_dim(right_blocks, col_start, col_block, 2)
        outer_part = jnp.einsum(
            "sic,sejd->iejcd", left_proj, right_piece, preferred_element_type=jnp.float32
        )
        return (
            outer_part.reshape(residue_row_block, block_depth, col_block, outer_width),
            right_piece,
        )

    def forward_step(step_index, loop_state):
        projected, pair_count = loop_state
        col_start = step_index * col_block
        outer_part, right_piece = partial_outer(col_start)
        mask_piece = lax.dynamic_slice_in_dim(mask_blocks, col_start, col_block, 2).astype(
            jnp.float32
        )
        count_part = jnp.einsum("si,sej->iej", mask_floating, mask_piece, precision=highest)
        outer_mine, count_mine = (
            lax.psum_scatter(
                outer_part.astype(jnp.bfloat16), "depth", scatter_dimension=1, tiled=True
            ).astype(jnp.float32),
            lax.psum_scatter(
                count_part.astype(jnp.bfloat16), "depth", scatter_dimension=1, tiled=True
            ).astype(jnp.float32),
        )
        proj_mine = jnp.dot(
            outer_mine.reshape(residue_row_block * col_block, outer_width),
            out_wide,
            precision=highest,
        )
        proj_mine = proj_mine.reshape(residue_row_block, col_block, pair_width)
        count_mine = count_mine.reshape(residue_row_block, col_block)
        projected = lax.dynamic_update_slice_in_dim(projected, proj_mine, col_start, 1)
        pair_count = lax.dynamic_update_slice_in_dim(pair_count, count_mine, col_start, 1)
        return (projected, pair_count)

    projected, pair_count = lax.fori_loop(
        0,
        block_count,
        forward_step,
        (
            jnp.zeros((residue_row_block, pair_cols, pair_width), jnp.float32),
            jnp.zeros((residue_row_block, pair_cols), jnp.float32),
        ),
    )
    count_column = pair_count.reshape(residue_row_block * pair_cols, 1)
    mid_act = (
        pair_activation_input.reshape(residue_row_block * pair_cols, pair_width).astype(jnp.float32)
        + projected.reshape(residue_row_block * pair_cols, pair_width) / count_column
    )
    pair_scaled, pair_inv = norm_pieces(mid_act)
    pair_normed = (pair_scaled * pair_norm_gain).astype(jnp.bfloat16)
    pre_act = jnp.dot(pair_normed, hidden_weight, preferred_element_type=jnp.float32)
    act_value, act_slope = silu_pieces(pre_act)
    hidden = act_value.astype(jnp.bfloat16)
    masked_grad = (
        pair_output_gradient * pair_update_mask.astype(jnp.bfloat16)[:, :, None]
    ).reshape(residue_row_block * pair_cols, pair_width)
    final_matrix_derivative = jnp.dot(hidden.T, masked_grad, preferred_element_type=jnp.float32)
    back_prod = jnp.dot(masked_grad, back_weight.T, preferred_element_type=jnp.float32)
    grad_hidden = (back_prod * act_slope).astype(jnp.bfloat16)
    middle_matrix_derivative = jnp.dot(
        pair_normed.T, grad_hidden, preferred_element_type=jnp.float32
    )
    grad_scaled = (
        jnp.dot(grad_hidden, hidden_weight.T, preferred_element_type=jnp.float32) * pair_norm_gain
    )
    grad_mid = pair_output_gradient.reshape(residue_row_block * pair_cols, pair_width).astype(
        jnp.float32
    ) + standardize_adjoint(grad_scaled, pair_scaled, pair_inv)
    couple_features_derivative = grad_mid.astype(jnp.bfloat16).reshape(
        residue_row_block, pair_cols, pair_width
    )
    grad_opm = (
        (grad_mid / count_column)
        .astype(jnp.bfloat16)
        .reshape(residue_row_block, pair_cols, pair_width)
    )
    full_opm = lax.all_gather(grad_opm, "depth", axis=1, tiled=True).reshape(
        residue_row_block, depth_count, pair_cols, pair_width
    )

    def backward_step(step_index, loop_state):
        grad_left_acc, grad_out, right_term = loop_state
        col_start = step_index * col_block
        outer_part, right_piece = partial_outer(col_start)
        opm_piece = lax.dynamic_slice_in_dim(full_opm, col_start, col_block, 2).reshape(
            residue_row_block * block_depth * col_block, pair_width
        )
        grad_out = grad_out + jnp.dot(
            outer_part.reshape(residue_row_block * block_depth * col_block, outer_width).T,
            opm_piece.astype(jnp.float32),
            precision=highest,
        )
        grad_outer = jnp.dot(opm_piece, output_weight.T, preferred_element_type=jnp.float32).astype(
            jnp.bfloat16
        )
        grad_outer = grad_outer.reshape(
            residue_row_block, block_depth, col_block, proj_width, proj_width
        )
        grad_left_acc = grad_left_acc + jnp.einsum(
            "iejcd,sejd->sic", grad_outer, right_piece, preferred_element_type=jnp.float32
        )
        piece_term = jnp.einsum(
            "iejcd,sic->ejsd", grad_outer, left_proj, preferred_element_type=jnp.float32
        )
        piece_term = piece_term.reshape(block_depth, col_block, seq_total * proj_width)
        right_term = lax.dynamic_update_slice_in_dim(right_term, piece_term, col_start, 1)
        return (grad_left_acc, grad_out, right_term)

    grad_left_acc, result_matrix_derivative, right_term = lax.fori_loop(
        0,
        block_count,
        backward_step,
        (
            jnp.zeros((seq_total, residue_row_block, proj_width), jnp.float32),
            jnp.zeros((outer_width, pair_width), jnp.float32),
            jnp.zeros((block_depth, pair_cols, seq_total * proj_width), jnp.float32),
        ),
    )
    grad_right_sum = lax.psum_scatter(
        right_term.reshape(residues, seq_total * proj_width), "col", scatter_dimension=0, tiled=True
    )
    grad_right_acc = jnp.transpose(
        grad_right_sum.reshape(residue_row_block, seq_total, proj_width), (1, 0, 2)
    )
    grad_left = (grad_left_acc * mask_floating[:, :, None]).astype(jnp.bfloat16)
    grad_right = (grad_right_acc * mask_floating[:, :, None]).astype(jnp.bfloat16)
    normed_rows = normalized_rows.reshape(sequence_row_block * residue_row_block, channel_total)
    first_projector_derivative = jnp.dot(
        normed_rows.T,
        grad_left.reshape(sequence_row_block * residue_row_block, proj_width),
        preferred_element_type=jnp.float32,
    )
    second_projector_derivative = jnp.dot(
        normed_rows.T,
        grad_right.reshape(sequence_row_block * residue_row_block, proj_width),
        preferred_element_type=jnp.float32,
    )
    standardized_derivative = jnp.dot(
        grad_left, first_projector.T, preferred_element_type=jnp.float32
    ) + jnp.dot(grad_right, second_projector.T, preferred_element_type=jnp.float32)
    features_derivative = standardize_adjoint(
        standardized_derivative * layer_scale_factor, standardized_features, reciprocal_spread
    ).astype(jnp.bfloat16)
    weight_sums = lax.psum(
        (
            first_projector_derivative,
            second_projector_derivative,
            result_matrix_derivative,
            middle_matrix_derivative,
            final_matrix_derivative,
        ),
        ("depth", "col"),
    )
    return (
        features_derivative,
        couple_features_derivative,
        weight_sums[0],
        weight_sums[1],
        weight_sums[2],
        weight_sums[3],
        weight_sums[4],
    )


FEW_RESIDUES = 32
MASK_ROWS = 16
Z_PARTNERS = (6, 4, 2)
Y_PARTNER = 1


def butterfly(blocks, group):
    lane_group = lax.broadcasted_iota(jnp.int32, blocks[0].shape, 1) // group
    width = 4 * group
    for bit in (2, 1):
        low = (lane_group & bit) == 0
        swapped = list(blocks)
        for at in range(4):
            if at & bit:
                continue
            here, there = blocks[at], blocks[at | bit]
            moving = jnp.where(low, there, here)
            if bit == 2:
                moved = pltpu.roll(moving, 2 * group, 1)
            else:
                moved = jnp.where(
                    low, pltpu.roll(moving, width - group, 1), pltpu.roll(moving, group, 1)
                )
            swapped[at] = jnp.where(low, here, moved)
            swapped[at | bit] = jnp.where(low, moved, there)
        blocks = swapped
    return blocks


def wide_projector(first_ref, second_ref, copies):
    return jnp.concatenate([first_ref[...]] * copies + [second_ref[...]] * copies, axis=0)


def pre_kernel(
    ids_ref,
    x_hbm,
    maskt_hbm,
    pmask_hbm,
    scale_hbm,
    first_hbm,
    second_hbm,
    gain_hbm,
    act_hbm,
    grad_hbm,
    sent_ref,
    scale_ref,
    first_ref,
    second_ref,
    gain_ref,
    normed_ref,
    scaled_ref,
    inv_ref,
    wide_ref,
    tile_ref,
    x_ref,
    maskt_ref,
    pmask_ref,
    sems,
):
    res, seqs = maskt_ref.shape
    pairs = act_hbm.shape[0]
    first_pair = 2 * seqs + MASK_ROWS
    copies = [
        pltpu.make_async_copy(source, target, sems.at[at])
        for at, (source, target) in enumerate(
            (
                (x_hbm, x_ref),
                (maskt_hbm, maskt_ref),
                (pmask_hbm, pmask_ref),
                (scale_hbm, scale_ref),
                (first_hbm, first_ref),
                (second_hbm, second_ref),
                (gain_hbm, gain_ref),
                (act_hbm, sent_ref.at[0, pl.ds(first_pair, pairs), :]),
                (grad_hbm, sent_ref.at[0, pl.ds(first_pair + pairs, pairs), :]),
            )
        )
    ]
    for copy in copies:
        copy.start()
    for copy in copies:
        copy.wait()
    lanes = sent_ref.shape[2]
    group = lanes // res
    scaled, inv = norm_pieces(
        x_ref[...].astype(jnp.float32).reshape(seqs * res, x_ref.shape[2])
    )
    scaled_ref[...] = scaled
    inv_ref[...] = inv
    normed = (scaled * scale_ref[...]).astype(jnp.bfloat16)
    normed_ref[...] = normed
    wide = lax.dot_general(
        normed,
        wide_projector(first_ref, second_ref, res),
        (((1,), (1,)), ((), ())),
        preferred_element_type=jnp.float32,
    )
    for at in range(2):
        wide_ref[at] = wide[:, at * lanes : (at + 1) * lanes]
    tile_ref[...] = jnp.zeros(tile_ref.shape, jnp.float32)
    mask = maskt_ref[...].astype(jnp.float32)
    tile_ref[0:res, 0:seqs] = mask
    spread = (
        lax.broadcasted_iota(jnp.int32, (MASK_ROWS, lanes), 1) // group
        == lax.broadcasted_iota(jnp.int32, (MASK_ROWS, lanes), 0)
    ).astype(jnp.float32)
    mask_lanes = lax.dot_general(
        tile_ref[...], spread, (((0,), (0,)), ((), ())), preferred_element_type=jnp.float32
    )[:seqs]
    twice = jnp.concatenate([mask] * (lanes // seqs), axis=1)
    here = lax.broadcasted_iota(jnp.int32, (res, lanes), 1) // seqs == ids_ref[0]
    tile_ref[0:res, :] = jnp.where(here, twice, 0.0)
    tile_ref[res : 2 * res, 0 : pmask_ref.shape[1]] = pmask_ref[...].astype(jnp.float32)
    lane_group = lax.broadcasted_iota(jnp.int32, (seqs, lanes), 1) // group
    for at in range(2):
        both = wide_ref[at, pl.ds(0, seqs, stride=res), :]
        for r in range(1, res):
            both = jnp.where(
                lane_group == r, wide_ref[at, pl.ds(r, seqs, stride=res), :], both
            )
        sent_ref[0, at * seqs : (at + 1) * seqs, :] = (both * mask_lanes).astype(jnp.bfloat16)
    sent_ref[0, 2 * seqs : first_pair, :] = tile_ref[...].astype(jnp.bfloat16)


def outer_kernel(
    sizes,
    orders,
    ids_ref,
    near_ref,
    far_ref,
    other_near_ref,
    other_far_ref,
    wturn_ref,
    outer_ref,
    proj_out_ref,
    cnt_ref,
    pm_ref,
    maskt_ref,
    got_ref,
    leftn_ref,
    mine_ref,
    turn_ref,
    cntl_ref,
    pml_ref,
):
    seqs, res, pair_cols, width = sizes
    depths, cols = got_ref.shape[0], got_ref.shape[1]
    residues = cols * res
    lanes = res * width
    half_cols = pair_cols // res
    me_depth = ids_ref[0]
    me_col = ids_ref[1]
    f32, bf16 = jnp.float32, jnp.bfloat16

    for order, mine, other in zip(orders, (near_ref, far_ref), (other_near_ref, other_far_ref)):
        for at, partner in enumerate(order):
            got_ref[me_depth, me_col ^ partner] = mine[at]
            got_ref[1 - me_depth, me_col ^ partner] = other[at]

    for e in range(depths):
        for k in range(cols):
            leftn_ref[e * seqs : (e + 1) * seqs, k * lanes : (k + 1) * lanes] = got_ref[
                e, k, 0:seqs, :
            ]
    for k in range(half_cols):
        block = jnp.concatenate(
            [
                got_ref[e, me_depth * half_cols + k, seqs : 2 * seqs, :]
                for e in range(depths)
            ],
            axis=0,
        ).astype(f32)
        turn_ref[k * lanes : (k + 1) * lanes, :] = block.T
    for d in range(width):
        mine_ref[d * pair_cols : (d + 1) * pair_cols, :] = turn_ref[
            pl.ds(d, pair_cols, stride=width), :
        ].astype(bf16)

    base = 2 * seqs
    pair_lane = lax.broadcasted_iota(jnp.int32, (pair_cols, lanes), 1)
    pair_row = lax.broadcasted_iota(jnp.int32, (pair_cols, lanes), 0)
    for k in range(cols):
        tiles = [got_ref[e, k, base : base + MASK_ROWS, :].astype(f32) for e in range(depths)]
        maskt_ref[k * res : (k + 1) * res, :] = tiles[0][0:res] + tiles[1][0:res]
        own = got_ref[me_depth, k, base : base + MASK_ROWS, :].astype(f32)
        for r in range(res):
            row = own[res + r : res + r + 1, :]
            first = (k * res + r) * pair_cols
            pml_ref[first : first + pair_cols, :] = jnp.where(
                pair_lane == pair_row, row, 0.0
            ).astype(bf16)
    maskt = maskt_ref[...]
    cols_mask = maskt_ref[pl.ds(pl.multiple_of(me_depth * pair_cols, pair_cols), pair_cols), :]
    for i in range(residues):
        cntl_ref[i * pair_cols : (i + 1) * pair_cols, :] = (maskt[i : i + 1, :] * cols_mask).astype(
            bf16
        )
    ones = jnp.ones((lanes, lanes), bf16)
    cnt_ref[...] = jnp.dot(cntl_ref[...], ones, preferred_element_type=f32)
    pm_ref[...] = jnp.dot(pml_ref[...], ones, preferred_element_type=f32).astype(bf16)

    for dh in range(width // 4):
        prod = jnp.dot(
            mine_ref[dh * 4 * pair_cols : (dh + 1) * 4 * pair_cols, :],
            leftn_ref[...],
            preferred_element_type=f32,
        )
        for k in range(cols):
            piece = prod[:, k * lanes : (k + 1) * lanes]
            turned = butterfly(
                [piece[a * pair_cols : (a + 1) * pair_cols] for a in range(4)], width
            )
            for il in range(res):
                first = (k * res + il) * pair_cols
                outer_ref[first : first + pair_cols, dh * lanes : (dh + 1) * lanes] = turned[
                    il
                ].astype(bf16)
    proj_out_ref[...] = jnp.dot(outer_ref[...], wturn_ref[...], preferred_element_type=f32)


def turn_kernel(
    sizes,
    orders,
    ids_ref,
    near_ref,
    far_ref,
    other_near_ref,
    other_far_ref,
    rightt_ref,
    leftt_ref,
    got_ref,
    turn_ref,
):
    seqs, res, _, width = sizes
    depths, cols = got_ref.shape[0], got_ref.shape[1]
    lanes = res * width
    residues = res * cols
    me_depth = ids_ref[0]
    me_col = ids_ref[1]
    for order, mine, other in zip(orders, (near_ref, far_ref), (other_near_ref, other_far_ref)):
        for at, partner in enumerate(order):
            got_ref[me_depth, me_col ^ partner] = mine[at, 0 : 2 * seqs, :]
            got_ref[1 - me_depth, me_col ^ partner] = other[at, 0 : 2 * seqs, :]
    for at, out in ((0, leftt_ref), (1, rightt_ref)):
        for k in range(cols):
            block = jnp.concatenate(
                [got_ref[e, k, at * seqs : (at + 1) * seqs, :] for e in range(depths)], axis=0
            ).astype(jnp.float32)
            turn_ref[k * lanes : (k + 1) * lanes, :] = block.T
        for d in range(width):
            out[d * residues : (d + 1) * residues, :] = turn_ref[
                pl.ds(d, residues, stride=width), :
            ].astype(jnp.bfloat16)


def transition_kernel(
    sizes,
    orders,
    ids_ref,
    near_ref,
    far_ref,
    proj_out_ref,
    cnt_ref,
    pm_ref,
    gain_ref,
    hid_ref,
    back_ref,
    couple_ref,
    opm_ref,
    pn_ref,
    gh_ref,
    hidden_ref,
    mg_ref,
    pgot_ref,
    gmid_ref,
):
    seqs, res, pair_cols, width = sizes
    per = res * pair_cols
    cols = pgot_ref.shape[0]
    me_col = ids_ref[1]
    f32, bf16 = jnp.float32, jnp.bfloat16
    for order, mine in zip(orders, (near_ref, far_ref)):
        for at, partner in enumerate(order):
            pgot_ref[me_col ^ partner] = mine[at]
    gain = gain_ref[...]
    chunk = 2 * per
    for at in range(cols // 2):
        rows = slice(at * chunk, (at + 1) * chunk)
        act, grad = [
            jnp.concatenate(
                [pgot_ref[2 * at + b, w * per : (w + 1) * per, :] for b in range(2)], axis=0
            )
            for w in range(2)
        ]
        count = cnt_ref[rows, :]
        mid = act.astype(f32) + proj_out_ref[rows, :] / count
        scaled, inv = norm_pieces(mid)
        normed = (scaled * gain).astype(bf16)
        pn_ref[rows, :] = normed
        pre = jnp.dot(normed, hid_ref[...], preferred_element_type=f32)
        value, slope = silu_pieces(pre)
        hidden_ref[rows, :] = value.astype(bf16)
        masked = grad * pm_ref[rows, :]
        mg_ref[rows, :] = masked
        back = lax.dot_general(
            masked, back_ref[...], (((1,), (1,)), ((), ())), preferred_element_type=f32
        )
        ghid = (back * slope).astype(bf16)
        gh_ref[rows, :] = ghid
        gsc = (
            lax.dot_general(
                ghid, hid_ref[...], (((1,), (1,)), ((), ())), preferred_element_type=f32
            )
            * gain
        )
        gmid = grad.astype(f32) + standardize_adjoint(gsc, scaled, inv)
        gmid_ref[rows, :] = gmid
        opm_ref[rows, :] = (gmid / count).astype(bf16)
    couple_ref[...] = gmid_ref[pl.ds(pl.multiple_of(me_col * per, per), per), :].astype(bf16)


def projector_kernel(
    sizes,
    ids_ref,
    opm_ref,
    other_opm_ref,
    rightt_ref,
    leftt_ref,
    wout_ref,
    wturn_ref,
    maskt_ref,
    normed_ref,
    far_normed_ref,
    other_normed_ref,
    other_far_normed_ref,
    part_ref,
    spread_ref,
    gf_ref,
    grow_ref,
    gcol_ref,
    gor_ref,
    goc_ref,
    gs_ref,
    rows_ref,
):
    seqs, res, pair_cols, width = sizes
    depths, half = gf_ref.shape[0], gf_ref.shape[1]
    residues = half // pair_cols
    lanes = res * width
    here = 2 * res
    me_depth = ids_ref[0]
    me_col = ids_ref[1]
    me_y = me_col % 2
    first_here = (me_col // 2) * here
    f32, bf16 = jnp.float32, jnp.bfloat16
    gf_ref[me_depth] = opm_ref[...].astype(f32)
    gf_ref[1 - me_depth] = other_opm_ref[...].astype(f32)
    for y, e, block in (
        (me_y, me_depth, normed_ref),
        (1 - me_y, me_depth, far_normed_ref),
        (me_y, 1 - me_depth, other_normed_ref),
        (1 - me_y, 1 - me_depth, other_far_normed_ref),
    ):
        rows_ref[y, e] = block[...]

    for il in range(here):
        for e in range(depths):
            first = pl.multiple_of((first_here + il) * pair_cols, pair_cols)
            grow_ref[il * residues + e * pair_cols : il * residues + (e + 1) * pair_cols, :] = (
                gf_ref[e, pl.ds(first, pair_cols), :].astype(bf16)
            )
    my_half = first_here // pair_cols
    my_first = first_here - my_half * pair_cols
    for jl in range(here):
        gcol_ref[jl * residues : (jl + 1) * residues, :] = gf_ref[
            my_half, pl.ds(my_first + jl, residues, stride=pair_cols), :
        ].astype(bf16)
    for lhs, weight, out in ((grow_ref, wturn_ref, gor_ref), (gcol_ref, wout_ref, goc_ref)):
        for dh in range(width // 4):
            piece = lax.dot_general(
                lhs[...],
                weight[dh * lanes : (dh + 1) * lanes, :],
                (((1,), (1,)), ((), ())),
                preferred_element_type=f32,
            )
            for y in range(2):
                turned = butterfly(
                    [
                        piece[(y * res + a) * residues : (y * res + a + 1) * residues]
                        for a in range(4)
                    ],
                    width,
                )
                for dl in range(4):
                    first = (dh * 4 + dl) * residues
                    out[first : first + residues, y * lanes : (y + 1) * lanes] = turned[dl].astype(
                        bf16
                    )
    group = lax.broadcasted_iota(jnp.int32, (here, here * width), 1) // width
    spread = (group == lax.broadcasted_iota(jnp.int32, (here, here * width), 0)).astype(f32)
    mask_lanes = lax.dot_general(
        maskt_ref[pl.ds(pl.multiple_of(first_here, here), here), :],
        spread,
        (((0,), (0,)), ((), ())),
        preferred_element_type=f32,
    )
    lane_group = lax.broadcasted_iota(jnp.int32, (seqs, lanes), 1) // width
    for at, (lhs, rhs) in enumerate(((rightt_ref, gor_ref), (leftt_ref, goc_ref))):
        total = lax.dot_general(
            lhs[...], rhs[...], (((0,), (0,)), ((), ())), preferred_element_type=f32
        )
        total = (total * mask_lanes).astype(bf16).astype(f32)
        for y in range(2):
            for e in range(depths):
                block = total[e * seqs : (e + 1) * seqs, y * lanes : (y + 1) * lanes]
                for r in range(res):
                    gs_ref[at, y, e, pl.ds(r, seqs, stride=res), :] = jnp.where(
                        lane_group == r, block, 0.0
                    )
    spread_ref[...] = jnp.concatenate(
        [gs_ref[0, me_y, me_depth], gs_ref[1, me_y, me_depth]], axis=1
    ).astype(bf16)
    rows = rows_ref.shape[2]
    for at in range(2):
        cross = lax.dot_general(
            gs_ref[at].reshape(2 * depths * rows, lanes).astype(bf16),
            rows_ref[...].reshape(2 * depths * rows, rows_ref.shape[3]),
            (((0,), (0,)), ((), ())),
            preferred_element_type=f32,
        )
        total = cross[:width]
        for r in range(1, res):
            total = total + cross[r * width : (r + 1) * width]
        part_ref[at * width : (at + 1) * width, :] = total.astype(bf16)


def weights_kernel(outer_ref, opm_ref, pn_ref, gh_ref, hidden_ref, mg_ref, out_ref, turn_ref):
    pair_width, hid = pn_ref.shape[1], gh_ref.shape[1]
    outer_width = outer_ref.shape[1]
    width = int(outer_width**0.5 + 0.5)

    def contract(lhs, rhs):
        return lax.dot_general(
            lhs[...], rhs[...], (((0,), (0,)), ((), ())), preferred_element_type=jnp.float32
        )

    turn_ref[...] = contract(outer_ref, opm_ref)
    for c in range(width):
        out_ref[c * width : (c + 1) * width, :] = turn_ref[
            pl.ds(c, width, stride=width), :
        ].astype(jnp.bfloat16)
    dhid = contract(pn_ref, gh_ref).astype(jnp.bfloat16)
    for at in range(hid // pair_width):
        first = outer_width + at * pair_width
        out_ref[first : first + pair_width, :] = dhid[:, at * pair_width : (at + 1) * pair_width]
    out_ref[outer_width + hid :, :] = contract(hidden_ref, mg_ref).astype(jnp.bfloat16)


def weights_sum_kernel(mine_ref, other_ref, dout_ref, dhid_ref, dback_ref):
    pair_width, hid = dhid_ref.shape
    outer_width = dout_ref.shape[0]

    def added(first, count):
        rows = slice(first, first + count)
        return mine_ref[rows, :].astype(jnp.float32) + other_ref[rows, :].astype(jnp.float32)

    dout_ref[...] = added(0, outer_width)
    for at in range(hid // pair_width):
        dhid_ref[:, at * pair_width : (at + 1) * pair_width] = added(
            outer_width + at * pair_width, pair_width
        )
    dback_ref[...] = added(outer_width + hid, hid)


def feature_kernel(
    copies, spread_ref, first_ref, second_ref, scale_ref, scaled_ref, inv_ref, feat_ref
):
    back = jnp.dot(
        spread_ref[...],
        wide_projector(first_ref, second_ref, copies),
        preferred_element_type=jnp.float32,
    )
    feat_ref[...] = standardize_adjoint(
        back * scale_ref[...], scaled_ref[...], inv_ref[...]
    ).astype(jnp.bfloat16)


def swap_depth(block):
    return lax.ppermute(block, "depth", [(0, 1), (1, 0)])


def pairwise_sum(blocks):
    while len(blocks) > 1:
        blocks = [blocks[at] + blocks[at + 1] for at in range(0, len(blocks), 2)]
    return blocks[0]


def swap_col(block, partner):
    count = lax.axis_size("col")
    return lax.ppermute(block, "col", [(at, at ^ partner) for at in range(count)])


def whole_plan(
    alignment_activations,
    alignment_mask,
    pair_activation_input,
    pair_update_mask,
    pair_output_gradient,
    layer_scale_factor,
    first_projector,
    second_projector,
    output_weight,
    pair_norm_gain,
    hidden_weight,
    back_weight,
):
    seqs, res, channels = alignment_activations.shape
    width = first_projector.shape[1]
    outer_width = width * width
    cols = lax.axis_size("col")
    depths = lax.axis_size("depth")
    residues = res * cols
    pair_cols, pair_width = pair_activation_input.shape[1:]
    hid = hidden_weight.shape[1]
    per = res * pair_cols
    lanes = res * width
    rows = 2 * seqs + MASK_ROWS
    half = residues * pair_cols
    f32, bf16 = jnp.float32, jnp.bfloat16
    ids = jnp.stack([lax.axis_index("depth"), lax.axis_index("col")]).astype(jnp.int32)
    smem = pl.BlockSpec(memory_space=pltpu.SMEM)
    vmem = pl.BlockSpec(memory_space=pltpu.VMEM)
    params = pltpu.CompilerParams(vmem_limit_bytes=16 * 2**20)
    scale = layer_scale_factor.reshape(1, channels)
    first, second = first_projector.T, second_projector.T
    wturn = jnp.transpose(output_weight.reshape(width, width, pair_width), (1, 0, 2)).reshape(
        outer_width, pair_width
    )
    shape = jax.ShapeDtypeStruct
    sent, scale, first, second, gain, normed, scaled, inv = pl.pallas_call(
        pre_kernel,
        out_shape=(
            shape((1, rows + 2 * per, pair_width), bf16),
            shape((1, channels), f32),
            shape((width, channels), bf16),
            shape((width, channels), bf16),
            shape((1, pair_width), f32),
            shape((seqs * res, channels), bf16),
            shape((seqs * res, channels), f32),
            shape((seqs * res, 1), f32),
        ),
        in_specs=[smem] + [pl.BlockSpec(memory_space=pltpu.HBM)] * 9,
        out_specs=[vmem] * 8,
        scratch_shapes=[
            pltpu.VMEM((2, seqs * res, lanes), f32),
            pltpu.VMEM((MASK_ROWS, lanes), f32),
            pltpu.VMEM((seqs, res, channels), bf16),
            pltpu.VMEM((res, seqs), jnp.int32),
            pltpu.VMEM((res, pair_cols), jnp.int32),
            pltpu.SemaphoreType.DMA((9,)),
        ],
        compiler_params=params,
        name="project",
    )(
        ids,
        *[
            pltpu.with_memory_space_constraint(array, pltpu.HBM)
            for array in (
                alignment_activations,
                alignment_mask.T,
                pair_update_mask,
                scale,
                first,
                second,
                pair_norm_gain.reshape(1, pair_width),
                pair_activation_input.reshape(per, pair_width),
                pair_output_gradient.reshape(per, pair_width),
            )
        ],
    )
    near_order = (0,) + Z_PARTNERS
    far_order = tuple(at ^ Y_PARTNER for at in near_order)
    blocks = lax.optimization_barrier(
        jnp.concatenate([sent] + [swap_col(sent, partner) for partner in Z_PARTNERS])
    )
    near, pair_near = blocks[:, :rows], blocks[:, rows:]
    far = swap_col(near, Y_PARTNER)
    pair_far = swap_col(pair_near, Y_PARTNER)
    other_near, other_far = swap_depth(near), swap_depth(far)
    sizes = (seqs, res, pair_cols, width)
    orders = (near_order, far_order)
    outer, proj_out, cnt, pm, maskt = pl.pallas_call(
        functools.partial(outer_kernel, sizes, orders),
        out_shape=(
            shape((half, outer_width), bf16),
            shape((half, pair_width), f32),
            shape((half, lanes), f32),
            shape((half, lanes), bf16),
            shape((residues, depths * seqs), f32),
        ),
        in_specs=[smem] + [vmem] * 5,
        out_specs=[vmem] * 5,
        scratch_shapes=[
            pltpu.VMEM((depths, cols, rows, pair_width), bf16),
            pltpu.VMEM((depths * seqs, residues * width), bf16),
            pltpu.VMEM((pair_cols * width, depths * seqs), bf16),
            pltpu.VMEM((pair_cols * width, depths * seqs), f32),
            pltpu.VMEM((half, lanes), bf16),
            pltpu.VMEM((half, lanes), bf16),
        ],
        compiler_params=params,
        name="outer_products",
    )(ids, near, far, other_near, other_far, wturn)
    normed, proj_out = lax.optimization_barrier((normed, proj_out))
    far_normed = swap_col(normed, Y_PARTNER)
    other_near, other_far, proj_out = lax.optimization_barrier((other_near, other_far, proj_out))
    rightt, leftt = pl.pallas_call(
        functools.partial(turn_kernel, sizes, orders),
        out_shape=(
            shape((residues * width, depths * seqs), bf16),
            shape((residues * width, depths * seqs), bf16),
        ),
        in_specs=[smem] + [vmem] * 4,
        out_specs=[vmem] * 2,
        scratch_shapes=[
            pltpu.VMEM((depths, cols, 2 * seqs, pair_width), bf16),
            pltpu.VMEM((residues * width, depths * seqs), f32),
        ],
        compiler_params=params,
        name="turned",
    )(ids, near, far, other_near, other_far)
    pair_far, rightt, leftt, proj_out = lax.optimization_barrier(
        (pair_far, rightt, leftt, proj_out)
    )
    couple, opm, pn, gh, hidden, mg = pl.pallas_call(
        functools.partial(transition_kernel, sizes, orders),
        out_shape=(
            shape((per, pair_width), bf16),
            shape((half, pair_width), bf16),
            shape((half, pair_width), bf16),
            shape((half, hid), bf16),
            shape((half, hid), bf16),
            shape((half, pair_width), bf16),
        ),
        in_specs=[smem] + [vmem] * 8,
        out_specs=[vmem] * 6,
        scratch_shapes=[
            pltpu.VMEM((cols, 2 * per, pair_width), bf16),
            pltpu.VMEM((half, pair_width), f32),
        ],
        compiler_params=params,
        name="transition",
    )(
        ids,
        pair_near,
        pair_far,
        proj_out,
        cnt,
        pm,
        gain,
        hidden_weight,
        back_weight,
    )
    opm, far_normed = lax.optimization_barrier((opm, far_normed))
    weights = pl.pallas_call(
        weights_kernel,
        out_shape=shape((outer_width + 2 * hid, pair_width), bf16),
        in_specs=[vmem] * 6,
        out_specs=vmem,
        scratch_shapes=[pltpu.VMEM((outer_width, pair_width), f32)],
        compiler_params=params,
        name="weight_gradients",
    )(outer, opm, pn, gh, hidden, mg)
    other_opm, other_normed, other_far_normed, weights = lax.optimization_barrier(
        (swap_depth(opm), swap_depth(normed), swap_depth(far_normed), weights)
    )
    part, spread = pl.pallas_call(
        functools.partial(projector_kernel, sizes),
        out_shape=(
            shape((2 * width, channels), bf16),
            shape((seqs * res, 2 * lanes), bf16),
        ),
        in_specs=[smem] + [vmem] * 11,
        out_specs=[vmem] * 2,
        scratch_shapes=[
            pltpu.VMEM((depths, half, pair_width), f32),
            pltpu.VMEM((2 * res * residues, pair_width), bf16),
            pltpu.VMEM((2 * res * residues, pair_width), bf16),
            pltpu.VMEM((residues * width, 2 * lanes), bf16),
            pltpu.VMEM((residues * width, 2 * lanes), bf16),
            pltpu.VMEM((2, 2, depths, seqs * res, lanes), f32),
            pltpu.VMEM((2, depths, seqs * res, channels), bf16),
        ],
        compiler_params=params,
        name="projector_parts",
    )(
        ids,
        opm,
        other_opm,
        rightt,
        leftt,
        output_weight,
        wturn,
        maskt,
        normed,
        far_normed,
        other_normed,
        other_far_normed,
    )
    feat = pl.pallas_call(
        functools.partial(feature_kernel, res),
        out_shape=shape((seqs * res, channels), bf16),
        in_specs=[vmem] * 6,
        out_specs=vmem,
        compiler_params=params,
        name="features",
    )(spread, first, second, scale, scaled, inv)
    part, weights = lax.optimization_barrier((part, weights))
    came = [swap_col(part, partner) for partner in Z_PARTNERS]
    dout, dhid, dback = pl.pallas_call(
        weights_sum_kernel,
        out_shape=(
            shape((outer_width, pair_width), f32),
            shape((pair_width, hid), f32),
            shape((hid, pair_width), f32),
        ),
        in_specs=[vmem] * 2,
        out_specs=[vmem] * 3,
        compiler_params=params,
        name="sums_over_depth",
    )(weights, swap_depth(weights))
    feat = feat.reshape(seqs, res, channels)
    came, feat, dout, dhid, dback = lax.optimization_barrier((came, feat, dout, dhid, dback))
    total = pairwise_sum([block.astype(f32) for block in [part] + came])
    return (
        feat,
        couple.reshape(res, pair_cols, pair_width),
        total[:width].T,
        total[width:].T,
        dout,
        dhid,
        dback,
    )


def on_device(alignment_activations, *others):
    cols = lax.axis_size("col")
    residues = alignment_activations.shape[1] * cols
    plan = whole_plan if cols == 8 and residues <= FEW_RESIDUES else split_plan
    return plan(alignment_activations, *others)


def solution(mesh):
    in_specs = (
        P(("group", "depth"), "col", None),
        P(("group", "depth"), "col"),
        P(("group", "col"), "depth", None),
        P(("group", "col"), "depth"),
        P(("group", "col"), "depth", None),
        P(),
        P(),
        P(),
        P(),
        P(),
        P(),
        P(),
    )
    out_specs = (
        P(("group", "depth"), "col", None),
        P(("group", "col"), "depth", None),
        P("group", None),
        P("group", None),
        P("group", None),
        P("group", None),
        P("group", None),
    )
    return jax.shard_map(
        on_device, mesh=mesh, in_specs=in_specs, out_specs=out_specs, check_vma=False
    )
```

```python
import functools

import jax
import jax.numpy as jnp
from jax import lax
from jax.experimental import pallas as pl
from jax.experimental.pallas import tpu as pltpu
from jax.sharding import PartitionSpec as P

epsilon = 1e-05
highest = lax.Precision.HIGHEST


def norm_pieces(entries_drawn):
    center = entries_drawn - jnp.mean(entries_drawn, axis=-1, keepdims=True)
    inv_std = lax.rsqrt(jnp.mean(center * center, axis=-1, keepdims=True) + epsilon)
    return (center * inv_std, inv_std)


def standardize_adjoint(grad_scaled, scaled, inv_std):
    mean_grad = jnp.mean(grad_scaled, axis=-1, keepdims=True)
    mean_cross = jnp.mean(grad_scaled * scaled, axis=-1, keepdims=True)
    return inv_std * (grad_scaled - mean_grad - scaled * mean_cross)


def silu_pieces(pre_act):
    sigma = jax.nn.sigmoid(pre_act)
    return (pre_act * sigma, sigma * (1.0 + pre_act * (1.0 - sigma)))


def split_plan(
    alignment_activations,
    alignment_mask,
    pair_activation_input,
    pair_update_mask,
    pair_output_gradient,
    layer_scale_factor,
    first_projector,
    second_projector,
    output_weight,
    pair_norm_gain,
    hidden_weight,
    back_weight,
):
    sequence_row_block, residue_row_block, channel_total = alignment_activations.shape
    proj_width = first_projector.shape[1]
    outer_width = proj_width * proj_width
    depth_count = lax.axis_size("depth")
    residues = residue_row_block * lax.axis_size("col")
    pair_cols = pair_activation_input.shape[1]
    pair_width = pair_activation_input.shape[2]
    col_block = min(64, pair_cols)
    block_count = pair_cols // col_block
    standardized_features, reciprocal_spread = norm_pieces(
        alignment_activations.astype(jnp.float32)
    )
    normalized_rows = (standardized_features * layer_scale_factor).astype(jnp.bfloat16)
    mask_floating = alignment_mask.astype(jnp.float32)
    left_proj = (
        jnp.dot(normalized_rows, first_projector, preferred_element_type=jnp.float32)
        * mask_floating[:, :, None]
    ).astype(jnp.bfloat16)
    right_proj = (
        jnp.dot(normalized_rows, second_projector, preferred_element_type=jnp.float32)
        * mask_floating[:, :, None]
    ).astype(jnp.bfloat16)
    right_flat = right_proj.reshape(sequence_row_block, residue_row_block * proj_width)
    mask_converted = alignment_mask.astype(jnp.bfloat16)
    seq_total = left_proj.shape[0]
    gathered, gathered_mask = (
        lax.all_gather(right_flat, "col", axis=1, tiled=True),
        lax.all_gather(mask_converted, "col", axis=1, tiled=True),
    )
    right_blocks = gathered.reshape(seq_total, depth_count, pair_cols, proj_width)
    mask_blocks = gathered_mask.reshape(seq_total, depth_count, pair_cols)
    block_depth = right_blocks.shape[1]
    out_wide = output_weight.astype(jnp.float32)

    def partial_outer(col_start):
        right_piece = lax.dynamic_slice_in_dim(right_blocks, col_start, col_block, 2)
        outer_part = jnp.einsum(
            "sic,sejd->iejcd", left_proj, right_piece, preferred_element_type=jnp.float32
        )
        return (
            outer_part.reshape(residue_row_block, block_depth, col_block, outer_width),
            right_piece,
        )

    def forward_step(step_index, loop_state):
        projected, pair_count = loop_state
        col_start = step_index * col_block
        outer_part, right_piece = partial_outer(col_start)
        mask_piece = lax.dynamic_slice_in_dim(mask_blocks, col_start, col_block, 2).astype(
            jnp.float32
        )
        count_part = jnp.einsum("si,sej->iej", mask_floating, mask_piece, precision=highest)
        outer_mine, count_mine = (
            lax.psum_scatter(
                outer_part.astype(jnp.bfloat16), "depth", scatter_dimension=1, tiled=True
            ).astype(jnp.float32),
            lax.psum_scatter(
                count_part.astype(jnp.bfloat16), "depth", scatter_dimension=1, tiled=True
            ).astype(jnp.float32),
        )
        proj_mine = jnp.dot(
            outer_mine.reshape(residue_row_block * col_block, outer_width),
            out_wide,
            precision=highest,
        )
        proj_mine = proj_mine.reshape(residue_row_block, col_block, pair_width)
        count_mine = count_mine.reshape(residue_row_block, col_block)
        projected = lax.dynamic_update_slice_in_dim(projected, proj_mine, col_start, 1)
        pair_count = lax.dynamic_update_slice_in_dim(pair_count, count_mine, col_start, 1)
        return (projected, pair_count)

    projected, pair_count = lax.fori_loop(
        0,
        block_count,
        forward_step,
        (
            jnp.zeros((residue_row_block, pair_cols, pair_width), jnp.float32),
            jnp.zeros((residue_row_block, pair_cols), jnp.float32),
        ),
    )
    count_column = pair_count.reshape(residue_row_block * pair_cols, 1)
    mid_act = (
        pair_activation_input.reshape(residue_row_block * pair_cols, pair_width).astype(jnp.float32)
        + projected.reshape(residue_row_block * pair_cols, pair_width) / count_column
    )
    pair_scaled, pair_inv = norm_pieces(mid_act)
    pair_normed = (pair_scaled * pair_norm_gain).astype(jnp.bfloat16)
    pre_act = jnp.dot(pair_normed, hidden_weight, preferred_element_type=jnp.float32)
    act_value, act_slope = silu_pieces(pre_act)
    hidden = act_value.astype(jnp.bfloat16)
    masked_grad = (
        pair_output_gradient * pair_update_mask.astype(jnp.bfloat16)[:, :, None]
    ).reshape(residue_row_block * pair_cols, pair_width)
    final_matrix_derivative = jnp.dot(hidden.T, masked_grad, preferred_element_type=jnp.float32)
    back_prod = jnp.dot(masked_grad, back_weight.T, preferred_element_type=jnp.float32)
    grad_hidden = (back_prod * act_slope).astype(jnp.bfloat16)
    middle_matrix_derivative = jnp.dot(
        pair_normed.T, grad_hidden, preferred_element_type=jnp.float32
    )
    grad_scaled = (
        jnp.dot(grad_hidden, hidden_weight.T, preferred_element_type=jnp.float32) * pair_norm_gain
    )
    grad_mid = pair_output_gradient.reshape(residue_row_block * pair_cols, pair_width).astype(
        jnp.float32
    ) + standardize_adjoint(grad_scaled, pair_scaled, pair_inv)
    couple_features_derivative = grad_mid.astype(jnp.bfloat16).reshape(
        residue_row_block, pair_cols, pair_width
    )
    grad_opm = (
        (grad_mid / count_column)
        .astype(jnp.bfloat16)
        .reshape(residue_row_block, pair_cols, pair_width)
    )
    full_opm = lax.all_gather(grad_opm, "depth", axis=1, tiled=True).reshape(
        residue_row_block, depth_count, pair_cols, pair_width
    )

    def backward_step(step_index, loop_state):
        grad_left_acc, grad_out, right_term = loop_state
        col_start = step_index * col_block
        outer_part, right_piece = partial_outer(col_start)
        opm_piece = lax.dynamic_slice_in_dim(full_opm, col_start, col_block, 2).reshape(
            residue_row_block * block_depth * col_block, pair_width
        )
        grad_out = grad_out + jnp.dot(
            outer_part.reshape(residue_row_block * block_depth * col_block, outer_width).T,
            opm_piece.astype(jnp.float32),
            precision=highest,
        )
        grad_outer = jnp.dot(opm_piece, output_weight.T, preferred_element_type=jnp.float32).astype(
            jnp.bfloat16
        )
        grad_outer = grad_outer.reshape(
            residue_row_block, block_depth, col_block, proj_width, proj_width
        )
        grad_left_acc = grad_left_acc + jnp.einsum(
            "iejcd,sejd->sic", grad_outer, right_piece, preferred_element_type=jnp.float32
        )
        piece_term = jnp.einsum(
            "iejcd,sic->ejsd", grad_outer, left_proj, preferred_element_type=jnp.float32
        )
        piece_term = piece_term.reshape(block_depth, col_block, seq_total * proj_width)
        right_term = lax.dynamic_update_slice_in_dim(right_term, piece_term, col_start, 1)
        return (grad_left_acc, grad_out, right_term)

    grad_left_acc, result_matrix_derivative, right_term = lax.fori_loop(
        0,
        block_count,
        backward_step,
        (
            jnp.zeros((seq_total, residue_row_block, proj_width), jnp.float32),
            jnp.zeros((outer_width, pair_width), jnp.float32),
            jnp.zeros((block_depth, pair_cols, seq_total * proj_width), jnp.float32),
        ),
    )
    grad_right_sum = lax.psum_scatter(
        right_term.reshape(residues, seq_total * proj_width), "col", scatter_dimension=0, tiled=True
    )
    grad_right_acc = jnp.transpose(
        grad_right_sum.reshape(residue_row_block, seq_total, proj_width), (1, 0, 2)
    )
    grad_left = (grad_left_acc * mask_floating[:, :, None]).astype(jnp.bfloat16)
    grad_right = (grad_right_acc * mask_floating[:, :, None]).astype(jnp.bfloat16)
    normed_rows = normalized_rows.reshape(sequence_row_block * residue_row_block, channel_total)
    first_projector_derivative = jnp.dot(
        normed_rows.T,
        grad_left.reshape(sequence_row_block * residue_row_block, proj_width),
        preferred_element_type=jnp.float32,
    )
    second_projector_derivative = jnp.dot(
        normed_rows.T,
        grad_right.reshape(sequence_row_block * residue_row_block, proj_width),
        preferred_element_type=jnp.float32,
    )
    standardized_derivative = jnp.dot(
        grad_left, first_projector.T, preferred_element_type=jnp.float32
    ) + jnp.dot(grad_right, second_projector.T, preferred_element_type=jnp.float32)
    features_derivative = standardize_adjoint(
        standardized_derivative * layer_scale_factor, standardized_features, reciprocal_spread
    ).astype(jnp.bfloat16)
    weight_sums = lax.psum(
        (
            first_projector_derivative,
            second_projector_derivative,
            result_matrix_derivative,
            middle_matrix_derivative,
            final_matrix_derivative,
        ),
        ("depth", "col"),
    )
    return (
        features_derivative,
        couple_features_derivative,
        weight_sums[0],
        weight_sums[1],
        weight_sums[2],
        weight_sums[3],
        weight_sums[4],
    )


FEW_RESIDUES = 32
MASK_ROWS = 16
Z_PARTNERS = (6, 4, 2)
Y_PARTNER = 1


def butterfly(blocks, group):
    lane_group = lax.broadcasted_iota(jnp.int32, blocks[0].shape, 1) // group
    width = 4 * group
    for bit in (2, 1):
        low = (lane_group & bit) == 0
        swapped = list(blocks)
        for at in range(4):
            if at & bit:
                continue
            here, there = blocks[at], blocks[at | bit]
            moving = jnp.where(low, there, here)
            if bit == 2:
                moved = pltpu.roll(moving, 2 * group, 1)
            else:
                moved = jnp.where(
                    low, pltpu.roll(moving, width - group, 1), pltpu.roll(moving, group, 1)
                )
            swapped[at] = jnp.where(low, here, moved)
            swapped[at | bit] = jnp.where(low, moved, there)
        blocks = swapped
    return blocks


def wide_projector(first_ref, second_ref, copies):
    return jnp.concatenate([first_ref[...]] * copies + [second_ref[...]] * copies, axis=0)


def pre_kernel(
    ids_ref,
    x_hbm,
    maskt_hbm,
    pmask_hbm,
    scale_hbm,
    first_hbm,
    second_hbm,
    gain_hbm,
    act_hbm,
    grad_hbm,
    sent_ref,
    scale_ref,
    first_ref,
    second_ref,
    gain_ref,
    normed_ref,
    scaled_ref,
    inv_ref,
    wide_ref,
    tile_ref,
    x_ref,
    maskt_ref,
    pmask_ref,
    sems,
):
    res, seqs = maskt_ref.shape
    pairs = act_hbm.shape[0]
    first_pair = 2 * seqs + MASK_ROWS
    copies = [
        pltpu.make_async_copy(source, target, sems.at[at])
        for at, (source, target) in enumerate(
            (
                (x_hbm, x_ref),
                (maskt_hbm, maskt_ref),
                (pmask_hbm, pmask_ref),
                (scale_hbm, scale_ref),
                (first_hbm, first_ref),
                (second_hbm, second_ref),
                (gain_hbm, gain_ref),
                (act_hbm, sent_ref.at[0, pl.ds(first_pair, pairs), :]),
                (grad_hbm, sent_ref.at[0, pl.ds(first_pair + pairs, pairs), :]),
            )
        )
    ]
    for copy in copies:
        copy.start()
    for copy in copies:
        copy.wait()
    lanes = sent_ref.shape[2]
    group = lanes // res
    channels = x_ref.shape[2]
    rows = x_ref[...].astype(jnp.float32).reshape(seqs * res, channels)
    for at in range(channels // lanes):
        wide_ref[at] = rows[:, at * lanes : (at + 1) * lanes]
    scaled, inv = norm_pieces(
        jnp.concatenate(
            [
                jnp.concatenate(
                    [wide_ref[at, pl.ds(r, seqs, stride=res), :] for r in range(res)], axis=0
                )
                for at in range(channels // lanes)
            ],
            axis=1,
        )
    )
    scaled_ref[...] = scaled
    inv_ref[...] = inv
    normed = (scaled * scale_ref[...]).astype(jnp.bfloat16)
    normed_ref[...] = normed
    wide = lax.dot_general(
        normed,
        wide_projector(first_ref, second_ref, res),
        (((1,), (1,)), ((), ())),
        preferred_element_type=jnp.float32,
    )
    tile_ref[...] = jnp.zeros(tile_ref.shape, jnp.float32)
    mask = maskt_ref[...].astype(jnp.float32)
    tile_ref[0:res, 0:seqs] = mask
    spread = (
        lax.broadcasted_iota(jnp.int32, (MASK_ROWS, lanes), 1) // group
        == lax.broadcasted_iota(jnp.int32, (MASK_ROWS, lanes), 0)
    ).astype(jnp.float32)
    mask_lanes = lax.dot_general(
        tile_ref[...], spread, (((0,), (0,)), ((), ())), preferred_element_type=jnp.float32
    )[:seqs]
    twice = jnp.concatenate([mask] * (lanes // seqs), axis=1)
    here = lax.broadcasted_iota(jnp.int32, (res, lanes), 1) // seqs == ids_ref[0]
    tile_ref[0:res, :] = jnp.where(here, twice, 0.0)
    tile_ref[res : 2 * res, 0 : pmask_ref.shape[1]] = pmask_ref[...].astype(jnp.float32)
    lane_group = lax.broadcasted_iota(jnp.int32, (seqs, lanes), 1) // group
    for at in range(2):
        part = wide[:, at * lanes : (at + 1) * lanes]
        both = part[0:seqs]
        for r in range(1, res):
            both = jnp.where(lane_group == r, part[r * seqs : (r + 1) * seqs], both)
        sent_ref[0, at * seqs : (at + 1) * seqs, :] = (both * mask_lanes).astype(jnp.bfloat16)
    sent_ref[0, 2 * seqs : first_pair, :] = tile_ref[...].astype(jnp.bfloat16)


def outer_kernel(
    sizes,
    orders,
    ids_ref,
    near_ref,
    far_ref,
    other_near_ref,
    other_far_ref,
    wturn_ref,
    outer_ref,
    proj_out_ref,
    cnt_ref,
    pm_ref,
    maskt_ref,
    got_ref,
    leftn_ref,
    mine_ref,
    turn_ref,
    cntl_ref,
    pml_ref,
):
    seqs, res, pair_cols, width = sizes
    depths, cols = got_ref.shape[0], got_ref.shape[1]
    residues = cols * res
    lanes = res * width
    half_cols = pair_cols // res
    me_depth = ids_ref[0]
    me_col = ids_ref[1]
    f32, bf16 = jnp.float32, jnp.bfloat16

    for order, mine, other in zip(orders, (near_ref, far_ref), (other_near_ref, other_far_ref)):
        for at, partner in enumerate(order):
            got_ref[me_depth, me_col ^ partner] = mine[at]
            got_ref[1 - me_depth, me_col ^ partner] = other[at]

    for e in range(depths):
        for k in range(cols):
            leftn_ref[e * seqs : (e + 1) * seqs, k * lanes : (k + 1) * lanes] = got_ref[
                e, k, 0:seqs, :
            ]
    for k in range(half_cols):
        block = jnp.concatenate(
            [
                got_ref[e, me_depth * half_cols + k, seqs : 2 * seqs, :]
                for e in range(depths)
            ],
            axis=0,
        ).astype(f32)
        turn_ref[k * lanes : (k + 1) * lanes, :] = block.T
    for d in range(width):
        mine_ref[d * pair_cols : (d + 1) * pair_cols, :] = turn_ref[
            pl.ds(d, pair_cols, stride=width), :
        ].astype(bf16)

    base = 2 * seqs
    pair_lane = lax.broadcasted_iota(jnp.int32, (pair_cols, lanes), 1)
    pair_row = lax.broadcasted_iota(jnp.int32, (pair_cols, lanes), 0)
    for k in range(cols):
        tiles = [got_ref[e, k, base : base + MASK_ROWS, :].astype(f32) for e in range(depths)]
        maskt_ref[k * res : (k + 1) * res, :] = tiles[0][0:res] + tiles[1][0:res]
        own = got_ref[me_depth, k, base : base + MASK_ROWS, :].astype(f32)
        for r in range(res):
            row = own[res + r : res + r + 1, :]
            first = (k * res + r) * pair_cols
            pml_ref[first : first + pair_cols, :] = jnp.where(
                pair_lane == pair_row, row, 0.0
            ).astype(bf16)
    maskt = maskt_ref[...]
    cols_mask = maskt_ref[pl.ds(pl.multiple_of(me_depth * pair_cols, pair_cols), pair_cols), :]
    for i in range(residues):
        cntl_ref[i * pair_cols : (i + 1) * pair_cols, :] = (maskt[i : i + 1, :] * cols_mask).astype(
            bf16
        )
    ones = jnp.ones((lanes, lanes), bf16)
    cnt_ref[...] = 1.0 / jnp.dot(cntl_ref[...], ones, preferred_element_type=f32)
    pm_ref[...] = jnp.dot(pml_ref[...], ones, preferred_element_type=f32).astype(bf16)

    for dh in range(width // 4):
        prod = jnp.dot(
            mine_ref[dh * 4 * pair_cols : (dh + 1) * 4 * pair_cols, :],
            leftn_ref[...],
            preferred_element_type=f32,
        )
        for k in range(cols):
            piece = prod[:, k * lanes : (k + 1) * lanes]
            turned = butterfly(
                [piece[a * pair_cols : (a + 1) * pair_cols] for a in range(4)], width
            )
            for il in range(res):
                first = (k * res + il) * pair_cols
                outer_ref[first : first + pair_cols, dh * lanes : (dh + 1) * lanes] = turned[
                    il
                ].astype(bf16)
    proj_out_ref[...] = jnp.dot(outer_ref[...], wturn_ref[...], preferred_element_type=f32)


def turn_kernel(sizes, ids_ref, mine_ref, other_ref, left_ref, right_ref, got_ref, turn_ref, tmp_ref):
    seqs, res, _, width = sizes
    depths, line = got_ref.shape[0], got_ref.shape[1]
    lanes = res * width
    me_depth = ids_ref[0]
    me_z = ids_ref[1] // 2
    for at, partner in enumerate((0,) + Z_PARTNERS):
        z = me_z ^ (partner // 2)
        got_ref[me_depth, z] = mine_ref[at, 0 : 2 * seqs, :]
        got_ref[1 - me_depth, z] = other_ref[at, 0 : 2 * seqs, :]
    for at, out in enumerate((left_ref, right_ref)):
        for z in range(line):
            block = jnp.concatenate(
                [got_ref[e, z, at * seqs : (at + 1) * seqs, :] for e in range(depths)], axis=0
            ).astype(jnp.float32)
            turn_ref[z * lanes : (z + 1) * lanes, :] = block.T
        for d in range(width):
            tmp_ref[d * line * res : (d + 1) * line * res, :] = turn_ref[
                pl.ds(d, line * res, stride=width), :
            ]
        for z in range(line):
            rows = slice(z * lanes, (z + 1) * lanes)
            out[:, rows] = tmp_ref[rows, :].T.astype(jnp.bfloat16)


def transition_kernel(
    sizes,
    orders,
    ids_ref,
    near_ref,
    far_ref,
    proj_out_ref,
    cnt_ref,
    pm_ref,
    gain_ref,
    hid_ref,
    back_ref,
    couple_ref,
    opm_ref,
    pn_ref,
    gh_ref,
    hidden_ref,
    mg_ref,
    pgot_ref,
    gmid_ref,
):
    seqs, res, pair_cols, width = sizes
    per = res * pair_cols
    cols = pgot_ref.shape[0]
    me_col = ids_ref[1]
    f32, bf16 = jnp.float32, jnp.bfloat16
    for order, mine in zip(orders, (near_ref, far_ref)):
        for at, partner in enumerate(order):
            pgot_ref[me_col ^ partner] = mine[at]
    gain = gain_ref[...]
    chunk = 2 * per
    for at in range(cols // 2):
        rows = slice(at * chunk, (at + 1) * chunk)
        act, grad = [
            jnp.concatenate(
                [pgot_ref[2 * at + b, w * per : (w + 1) * per, :] for b in range(2)], axis=0
            )
            for w in range(2)
        ]
        inv_count = cnt_ref[rows, :]
        mid = act.astype(f32) + proj_out_ref[rows, :] * inv_count
        scaled, inv = norm_pieces(mid)
        normed = (scaled * gain).astype(bf16)
        pn_ref[rows, :] = normed
        pre = jnp.dot(normed, hid_ref[...], preferred_element_type=f32)
        sigma = 0.5 + 0.5 * jnp.tanh(0.5 * pre)
        value = pre * sigma
        slope = sigma + value * (1.0 - sigma)
        hidden_ref[rows, :] = value.astype(bf16)
        masked = grad * pm_ref[rows, :]
        mg_ref[rows, :] = masked
        back = lax.dot_general(
            masked, back_ref[...], (((1,), (1,)), ((), ())), preferred_element_type=f32
        )
        ghid = (back * slope).astype(bf16)
        gh_ref[rows, :] = ghid
        gsc = (
            lax.dot_general(
                ghid, hid_ref[...], (((1,), (1,)), ((), ())), preferred_element_type=f32
            )
            * gain
        )
        gmid = grad.astype(f32) + standardize_adjoint(gsc, scaled, inv)
        gmid_ref[rows, :] = gmid
        opm_ref[rows, :] = (gmid * inv_count).astype(bf16)
    couple_ref[...] = gmid_ref[pl.ds(pl.multiple_of(me_col * per, per), per), :].astype(bf16)


def projector_kernel(
    sizes,
    ids_ref,
    opm_ref,
    other_opm_ref,
    left_near_ref,
    right_near_ref,
    left_far_ref,
    right_far_ref,
    wout_ref,
    wturn_ref,
    maskt_ref,
    normed_ref,
    far_normed_ref,
    other_normed_ref,
    other_far_normed_ref,
    part_ref,
    grads_ref,
    gf_ref,
    grow_ref,
    gcol_ref,
    gon_ref,
    gof_ref,
    gcn_ref,
    gcf_ref,
    tot_ref,
    rows_ref,
):
    seqs, res, pair_cols, width = sizes
    depths, half = gf_ref.shape[0], gf_ref.shape[1]
    residues = half // pair_cols
    lanes = res * width
    here = 2 * res
    line = residues // here
    near = line * res
    me_depth = ids_ref[0]
    me_z, me_y = ids_ref[1] // 2, ids_ref[1] % 2
    first_here = me_z * here
    f32, bf16 = jnp.float32, jnp.bfloat16
    gf_ref[me_depth] = opm_ref[...].astype(f32)
    gf_ref[1 - me_depth] = other_opm_ref[...].astype(f32)
    for y, e, block in (
        (me_y, me_depth, normed_ref),
        (1 - me_y, me_depth, far_normed_ref),
        (me_y, 1 - me_depth, other_normed_ref),
        (1 - me_y, 1 - me_depth, other_far_normed_ref),
    ):
        for r in range(res):
            rows_ref[y, r, e] = block[r * seqs : (r + 1) * seqs, :]

    my_half = first_here // pair_cols
    my_first = first_here - my_half * pair_cols
    for at in range(here):
        for w, y in enumerate((me_y, 1 - me_y)):
            for z in range(line):
                to = at * residues + w * near + z * res
                e, z_low = divmod(z, line // depths)
                grow_ref[to : to + res, :] = gf_ref[
                    e, pl.ds((first_here + at) * pair_cols + z_low * here + y * res, res), :
                ]
                gcol_ref[to : to + res, :] = gf_ref[
                    my_half,
                    pl.ds((z * here + y * res) * pair_cols + my_first + at, res, stride=pair_cols),
                    :,
                ]
    for lhs, weight, outs in (
        (grow_ref, wturn_ref, (gon_ref, gof_ref)),
        (gcol_ref, wout_ref, (gcn_ref, gcf_ref)),
    ):
        operand = lhs[...].astype(bf16)
        for dh in range(width // 4):
            piece = lax.dot_general(
                operand,
                weight[dh * lanes : (dh + 1) * lanes, :],
                (((1,), (1,)), ((), ())),
                preferred_element_type=f32,
            )
            for y in range(2):
                turned = butterfly(
                    [
                        piece[(y * res + a) * residues : (y * res + a + 1) * residues]
                        for a in range(4)
                    ],
                    width,
                )
                for dl in range(4):
                    first = (dh * 4 + dl) * near
                    for w, out in enumerate(outs):
                        out[first : first + near, y * lanes : (y + 1) * lanes] = turned[dl][
                            w * near : (w + 1) * near
                        ].astype(bf16)
    group = lax.broadcasted_iota(jnp.int32, (here, here * width), 1) // width
    spread = (group == lax.broadcasted_iota(jnp.int32, (here, here * width), 0)).astype(f32)
    mask_lanes = lax.dot_general(
        maskt_ref[pl.ds(pl.multiple_of(first_here, here), here), :],
        spread,
        (((0,), (0,)), ((), ())),
        preferred_element_type=f32,
    )
    for at, (near_lhs, near_rhs, far_lhs, far_rhs) in enumerate(
        (
            (right_near_ref, gon_ref, right_far_ref, gof_ref),
            (left_near_ref, gcn_ref, left_far_ref, gcf_ref),
        )
    ):
        total = jnp.dot(near_lhs[...], near_rhs[...], preferred_element_type=f32) + jnp.dot(
            far_lhs[...], far_rhs[...], preferred_element_type=f32
        )
        total = (total * mask_lanes).astype(bf16).astype(f32)
        sums = jnp.zeros((width, rows_ref.shape[4]), f32)
        for y in range(2):
            block = total[:, y * lanes : (y + 1) * lanes]
            for e in range(depths):
                tot_ref[at, y, e] = block[e * seqs : (e + 1) * seqs]
            turned = block.T.astype(bf16)
            for r in range(res):
                sums = sums + jnp.dot(
                    turned[r * width : (r + 1) * width],
                    rows_ref[y, r].reshape(depths * seqs, rows_ref.shape[4]),
                    preferred_element_type=f32,
                )
        part_ref[at * width : (at + 1) * width, :] = sums.astype(bf16)
        grads_ref[at] = tot_ref[at, me_y, me_depth]


def weights_kernel(outer_ref, opm_ref, pn_ref, gh_ref, hidden_ref, mg_ref, out_ref, turn_ref):
    pair_width, hid = pn_ref.shape[1], gh_ref.shape[1]
    outer_width = outer_ref.shape[1]
    width = int(outer_width**0.5 + 0.5)

    def contract(lhs, rhs):
        return lax.dot_general(
            lhs[...], rhs[...], (((0,), (0,)), ((), ())), preferred_element_type=jnp.float32
        )

    turn_ref[...] = contract(outer_ref, opm_ref)
    for c in range(width):
        out_ref[c * width : (c + 1) * width, :] = turn_ref[
            pl.ds(c, width, stride=width), :
        ].astype(jnp.bfloat16)
    dhid = contract(pn_ref, gh_ref).astype(jnp.bfloat16)
    for at in range(hid // pair_width):
        first = outer_width + at * pair_width
        out_ref[first : first + pair_width, :] = dhid[:, at * pair_width : (at + 1) * pair_width]
    out_ref[outer_width + hid :, :] = contract(hidden_ref, mg_ref).astype(jnp.bfloat16)


def weights_sum_kernel(mine_ref, other_ref, dout_ref, dhid_ref, dback_ref):
    pair_width, hid = dhid_ref.shape
    outer_width = dout_ref.shape[0]

    def added(first, count):
        rows = slice(first, first + count)
        return mine_ref[rows, :].astype(jnp.float32) + other_ref[rows, :].astype(jnp.float32)

    dout_ref[...] = added(0, outer_width)
    for at in range(hid // pair_width):
        dhid_ref[:, at * pair_width : (at + 1) * pair_width] = added(
            outer_width + at * pair_width, pair_width
        )
    dback_ref[...] = added(outer_width + hid, hid)


def feature_kernel(
    sizes, grads_ref, first_ref, second_ref, scale_ref, scaled_ref, inv_ref, feat_ref, rows_ref
):
    seqs, res, _, width = sizes
    lanes = res * width
    lane_group = lax.broadcasted_iota(jnp.int32, (seqs, lanes), 1) // width
    spread = jnp.concatenate(
        [
            jnp.concatenate(
                [jnp.where(lane_group == r, grads_ref[at], 0.0) for r in range(res)], axis=0
            )
            for at in range(2)
        ],
        axis=1,
    ).astype(jnp.bfloat16)
    back = jnp.dot(
        spread, wide_projector(first_ref, second_ref, res), preferred_element_type=jnp.float32
    )
    feat = standardize_adjoint(back * scale_ref[...], scaled_ref[...], inv_ref[...])
    for at in range(rows_ref.shape[0]):
        for r in range(res):
            rows_ref[at, pl.ds(r, seqs, stride=res), :] = feat[
                r * seqs : (r + 1) * seqs, at * lanes : (at + 1) * lanes
            ]
        feat_ref[:, at * lanes : (at + 1) * lanes] = rows_ref[at].astype(jnp.bfloat16)


def swap_depth(block):
    return lax.ppermute(block, "depth", [(0, 1), (1, 0)])


def pairwise_sum(blocks):
    while len(blocks) > 1:
        blocks = [blocks[at] + blocks[at + 1] for at in range(0, len(blocks), 2)]
    return blocks[0]


def swap_col(block, partner):
    count = lax.axis_size("col")
    return lax.ppermute(block, "col", [(at, at ^ partner) for at in range(count)])


def whole_plan(
    alignment_activations,
    alignment_mask,
    pair_activation_input,
    pair_update_mask,
    pair_output_gradient,
    layer_scale_factor,
    first_projector,
    second_projector,
    output_weight,
    pair_norm_gain,
    hidden_weight,
    back_weight,
):
    seqs, res, channels = alignment_activations.shape
    width = first_projector.shape[1]
    outer_width = width * width
    cols = lax.axis_size("col")
    depths = lax.axis_size("depth")
    residues = res * cols
    pair_cols, pair_width = pair_activation_input.shape[1:]
    hid = hidden_weight.shape[1]
    per = res * pair_cols
    lanes = res * width
    rows = 2 * seqs + MASK_ROWS
    half = residues * pair_cols
    line = cols // 2
    f32, bf16 = jnp.float32, jnp.bfloat16
    ids = jnp.stack([lax.axis_index("depth"), lax.axis_index("col")]).astype(jnp.int32)
    smem = pl.BlockSpec(memory_space=pltpu.SMEM)
    vmem = pl.BlockSpec(memory_space=pltpu.VMEM)
    params = pltpu.CompilerParams(vmem_limit_bytes=16 * 2**20)
    scale = layer_scale_factor.reshape(1, channels)
    first, second = first_projector.T, second_projector.T
    wturn = jnp.transpose(output_weight.reshape(width, width, pair_width), (1, 0, 2)).reshape(
        outer_width, pair_width
    )
    shape = jax.ShapeDtypeStruct
    sent, scale, first, second, gain, normed, scaled, inv = pl.pallas_call(
        pre_kernel,
        out_shape=(
            shape((1, rows + 2 * per, pair_width), bf16),
            shape((1, channels), f32),
            shape((width, channels), bf16),
            shape((width, channels), bf16),
            shape((1, pair_width), f32),
            shape((seqs * res, channels), bf16),
            shape((seqs * res, channels), f32),
            shape((seqs * res, 1), f32),
        ),
        in_specs=[smem] + [pl.BlockSpec(memory_space=pltpu.HBM)] * 9,
        out_specs=[vmem] * 8,
        scratch_shapes=[
            pltpu.VMEM((2, seqs * res, lanes), f32),
            pltpu.VMEM((MASK_ROWS, lanes), f32),
            pltpu.VMEM((seqs, res, channels), bf16),
            pltpu.VMEM((res, seqs), jnp.int32),
            pltpu.VMEM((res, pair_cols), jnp.int32),
            pltpu.SemaphoreType.DMA((9,)),
        ],
        compiler_params=params,
        name="project",
    )(
        ids,
        *[
            pltpu.with_memory_space_constraint(array, pltpu.HBM)
            for array in (
                alignment_activations,
                alignment_mask.T,
                pair_update_mask,
                scale,
                first,
                second,
                pair_norm_gain.reshape(1, pair_width),
                pair_activation_input.reshape(per, pair_width),
                pair_output_gradient.reshape(per, pair_width),
            )
        ],
    )
    near_order = (0,) + Z_PARTNERS
    far_order = tuple(at ^ Y_PARTNER for at in near_order)
    blocks = lax.optimization_barrier(
        jnp.concatenate([sent] + [swap_col(sent, partner) for partner in Z_PARTNERS])
    )
    near, pair_near = blocks[:, :rows], blocks[:, rows:]
    far = swap_col(near, Y_PARTNER)
    other_near = swap_depth(near)
    sizes = (seqs, res, pair_cols, width)

    def turned(mine, other):
        return pl.pallas_call(
            functools.partial(turn_kernel, sizes),
            out_shape=(shape((depths * seqs, line * lanes), bf16),) * 2,
            in_specs=[smem] + [vmem] * 2,
            out_specs=[vmem] * 2,
            scratch_shapes=[
                pltpu.VMEM((depths, line, 2 * seqs, pair_width), bf16),
                pltpu.VMEM((line * lanes, depths * seqs), f32),
                pltpu.VMEM((line * lanes, depths * seqs), f32),
            ],
            compiler_params=params,
            name="turned",
        )(ids, mine, other)

    left_near, right_near = turned(near, other_near)
    far, left_near, right_near = lax.optimization_barrier((far, left_near, right_near))
    other_far = swap_depth(far)
    pair_far = swap_col(pair_near, Y_PARTNER)
    orders = (near_order, far_order)
    outer, proj_out, cnt, pm, maskt = pl.pallas_call(
        functools.partial(outer_kernel, sizes, orders),
        out_shape=(
            shape((half, outer_width), bf16),
            shape((half, pair_width), f32),
            shape((half, lanes), f32),
            shape((half, lanes), bf16),
            shape((residues, depths * seqs), f32),
        ),
        in_specs=[smem] + [vmem] * 5,
        out_specs=[vmem] * 5,
        scratch_shapes=[
            pltpu.VMEM((depths, cols, rows, pair_width), bf16),
            pltpu.VMEM((depths * seqs, residues * width), bf16),
            pltpu.VMEM((pair_cols * width, depths * seqs), bf16),
            pltpu.VMEM((pair_cols * width, depths * seqs), f32),
            pltpu.VMEM((half, lanes), bf16),
            pltpu.VMEM((half, lanes), bf16),
        ],
        compiler_params=params,
        name="outer_products",
    )(ids, near, far, other_near, other_far, wturn)
    normed, proj_out = lax.optimization_barrier((normed, proj_out))
    far_normed = swap_col(normed, Y_PARTNER)
    other_far, proj_out = lax.optimization_barrier((other_far, proj_out))
    left_far, right_far = turned(far, other_far)
    pair_far, left_far, right_far, proj_out = lax.optimization_barrier(
        (pair_far, left_far, right_far, proj_out)
    )
    couple, opm, pn, gh, hidden, mg = pl.pallas_call(
        functools.partial(transition_kernel, sizes, orders),
        out_shape=(
            shape((per, pair_width), bf16),
            shape((half, pair_width), bf16),
            shape((half, pair_width), bf16),
            shape((half, hid), bf16),
            shape((half, hid), bf16),
            shape((half, pair_width), bf16),
        ),
        in_specs=[smem] + [vmem] * 8,
        out_specs=[vmem] * 6,
        scratch_shapes=[
            pltpu.VMEM((cols, 2 * per, pair_width), bf16),
            pltpu.VMEM((half, pair_width), f32),
        ],
        compiler_params=params,
        name="transition",
    )(
        ids,
        pair_near,
        pair_far,
        proj_out,
        cnt,
        pm,
        gain,
        hidden_weight,
        back_weight,
    )
    opm, far_normed = lax.optimization_barrier((opm, far_normed))
    weights = pl.pallas_call(
        weights_kernel,
        out_shape=shape((outer_width + 2 * hid, pair_width), bf16),
        in_specs=[vmem] * 6,
        out_specs=vmem,
        scratch_shapes=[pltpu.VMEM((outer_width, pair_width), f32)],
        compiler_params=params,
        name="weight_gradients",
    )(outer, opm, pn, gh, hidden, mg)
    other_opm, other_normed, other_far_normed, weights = lax.optimization_barrier(
        (swap_depth(opm), swap_depth(normed), swap_depth(far_normed), weights)
    )
    part, grads = pl.pallas_call(
        functools.partial(projector_kernel, sizes),
        out_shape=(
            shape((2 * width, channels), bf16),
            shape((2, seqs, lanes), f32),
        ),
        in_specs=[smem] + [vmem] * 13,
        out_specs=[vmem] * 2,
        scratch_shapes=[
            pltpu.VMEM((depths, half, pair_width), f32),
            pltpu.VMEM((2 * res * residues, pair_width), f32),
            pltpu.VMEM((2 * res * residues, pair_width), f32),
            pltpu.VMEM((line * lanes, 2 * lanes), bf16),
            pltpu.VMEM((line * lanes, 2 * lanes), bf16),
            pltpu.VMEM((line * lanes, 2 * lanes), bf16),
            pltpu.VMEM((line * lanes, 2 * lanes), bf16),
            pltpu.VMEM((2, 2, depths, seqs, lanes), f32),
            pltpu.VMEM((2, res, depths, seqs, channels), bf16),
        ],
        compiler_params=params,
        name="projector_parts",
    )(
        ids,
        opm,
        other_opm,
        left_near,
        right_near,
        left_far,
        right_far,
        output_weight,
        wturn,
        maskt,
        normed,
        far_normed,
        other_normed,
        other_far_normed,
    )
    feat = pl.pallas_call(
        functools.partial(feature_kernel, sizes),
        out_shape=shape((seqs * res, channels), bf16),
        in_specs=[vmem] * 6,
        out_specs=vmem,
        scratch_shapes=[pltpu.VMEM((channels // lanes, seqs * res, lanes), f32)],
        compiler_params=params,
        name="features",
    )(grads, first, second, scale, scaled, inv)
    part, weights = lax.optimization_barrier((part, weights))
    came = [swap_col(part, partner) for partner in Z_PARTNERS]
    dout, dhid, dback = pl.pallas_call(
        weights_sum_kernel,
        out_shape=(
            shape((outer_width, pair_width), f32),
            shape((pair_width, hid), f32),
            shape((hid, pair_width), f32),
        ),
        in_specs=[vmem] * 2,
        out_specs=[vmem] * 3,
        compiler_params=params,
        name="sums_over_depth",
    )(weights, swap_depth(weights))
    feat = feat.reshape(seqs, res, channels)
    came, feat, dout, dhid, dback = lax.optimization_barrier((came, feat, dout, dhid, dback))
    total = pairwise_sum([block.astype(f32) for block in [part] + came])
    return (
        feat,
        couple.reshape(res, pair_cols, pair_width),
        total[:width].T,
        total[width:].T,
        dout,
        dhid,
        dback,
    )


def on_device(alignment_activations, *others):
    cols = lax.axis_size("col")
    residues = alignment_activations.shape[1] * cols
    plan = whole_plan if cols == 8 and residues <= FEW_RESIDUES else split_plan
    return plan(alignment_activations, *others)


def solution(mesh):
    in_specs = (
        P(("group", "depth"), "col", None),
        P(("group", "depth"), "col"),
        P(("group", "col"), "depth", None),
        P(("group", "col"), "depth"),
        P(("group", "col"), "depth", None),
        P(),
        P(),
        P(),
        P(),
        P(),
        P(),
        P(),
    )
    out_specs = (
        P(("group", "depth"), "col", None),
        P(("group", "col"), "depth", None),
        P("group", None),
        P("group", None),
        P("group", None),
        P("group", None),
        P("group", None),
    )
    return jax.shard_map(
        on_device, mesh=mesh, in_specs=in_specs, out_specs=out_specs, check_vma=False
    )
```

```python
import functools

import jax
import jax.numpy as jnp
from jax import lax
from jax.experimental import pallas as pl
from jax.experimental.pallas import tpu as pltpu
from jax.sharding import PartitionSpec as P

epsilon = 1e-05
highest = lax.Precision.HIGHEST


def norm_pieces(entries_drawn):
    center = entries_drawn - jnp.mean(entries_drawn, axis=-1, keepdims=True)
    inv_std = lax.rsqrt(jnp.mean(center * center, axis=-1, keepdims=True) + epsilon)
    return (center * inv_std, inv_std)


def standardize_adjoint(grad_scaled, scaled, inv_std):
    mean_grad = jnp.mean(grad_scaled, axis=-1, keepdims=True)
    mean_cross = jnp.mean(grad_scaled * scaled, axis=-1, keepdims=True)
    return inv_std * (grad_scaled - mean_grad - scaled * mean_cross)


def silu_pieces(pre_act):
    sigma = jax.nn.sigmoid(pre_act)
    return (pre_act * sigma, sigma * (1.0 + pre_act * (1.0 - sigma)))


def split_plan(
    alignment_activations,
    alignment_mask,
    pair_activation_input,
    pair_update_mask,
    pair_output_gradient,
    layer_scale_factor,
    first_projector,
    second_projector,
    output_weight,
    pair_norm_gain,
    hidden_weight,
    back_weight,
):
    sequence_row_block, residue_row_block, channel_total = alignment_activations.shape
    proj_width = first_projector.shape[1]
    outer_width = proj_width * proj_width
    depth_count = lax.axis_size("depth")
    residues = residue_row_block * lax.axis_size("col")
    pair_cols = pair_activation_input.shape[1]
    pair_width = pair_activation_input.shape[2]
    col_block = min(64, pair_cols)
    block_count = pair_cols // col_block
    standardized_features, reciprocal_spread = norm_pieces(
        alignment_activations.astype(jnp.float32)
    )
    normalized_rows = (standardized_features * layer_scale_factor).astype(jnp.bfloat16)
    mask_floating = alignment_mask.astype(jnp.float32)
    left_proj = (
        jnp.dot(normalized_rows, first_projector, preferred_element_type=jnp.float32)
        * mask_floating[:, :, None]
    ).astype(jnp.bfloat16)
    right_proj = (
        jnp.dot(normalized_rows, second_projector, preferred_element_type=jnp.float32)
        * mask_floating[:, :, None]
    ).astype(jnp.bfloat16)
    right_flat = right_proj.reshape(sequence_row_block, residue_row_block * proj_width)
    mask_converted = alignment_mask.astype(jnp.bfloat16)
    seq_total = left_proj.shape[0]
    gathered, gathered_mask = (
        lax.all_gather(right_flat, "col", axis=1, tiled=True),
        lax.all_gather(mask_converted, "col", axis=1, tiled=True),
    )
    right_blocks = gathered.reshape(seq_total, depth_count, pair_cols, proj_width)
    mask_blocks = gathered_mask.reshape(seq_total, depth_count, pair_cols)
    block_depth = right_blocks.shape[1]
    out_wide = output_weight.astype(jnp.float32)

    def partial_outer(col_start):
        right_piece = lax.dynamic_slice_in_dim(right_blocks, col_start, col_block, 2)
        outer_part = jnp.einsum(
            "sic,sejd->iejcd", left_proj, right_piece, preferred_element_type=jnp.float32
        )
        return (
            outer_part.reshape(residue_row_block, block_depth, col_block, outer_width),
            right_piece,
        )

    def forward_step(step_index, loop_state):
        projected, pair_count = loop_state
        col_start = step_index * col_block
        outer_part, right_piece = partial_outer(col_start)
        mask_piece = lax.dynamic_slice_in_dim(mask_blocks, col_start, col_block, 2).astype(
            jnp.float32
        )
        count_part = jnp.einsum("si,sej->iej", mask_floating, mask_piece, precision=highest)
        outer_mine, count_mine = (
            lax.psum_scatter(
                outer_part.astype(jnp.bfloat16), "depth", scatter_dimension=1, tiled=True
            ).astype(jnp.float32),
            lax.psum_scatter(
                count_part.astype(jnp.bfloat16), "depth", scatter_dimension=1, tiled=True
            ).astype(jnp.float32),
        )
        proj_mine = jnp.dot(
            outer_mine.reshape(residue_row_block * col_block, outer_width),
            out_wide,
            precision=highest,
        )
        proj_mine = proj_mine.reshape(residue_row_block, col_block, pair_width)
        count_mine = count_mine.reshape(residue_row_block, col_block)
        projected = lax.dynamic_update_slice_in_dim(projected, proj_mine, col_start, 1)
        pair_count = lax.dynamic_update_slice_in_dim(pair_count, count_mine, col_start, 1)
        return (projected, pair_count)

    projected, pair_count = lax.fori_loop(
        0,
        block_count,
        forward_step,
        (
            jnp.zeros((residue_row_block, pair_cols, pair_width), jnp.float32),
            jnp.zeros((residue_row_block, pair_cols), jnp.float32),
        ),
    )
    count_column = pair_count.reshape(residue_row_block * pair_cols, 1)
    mid_act = (
        pair_activation_input.reshape(residue_row_block * pair_cols, pair_width).astype(jnp.float32)
        + projected.reshape(residue_row_block * pair_cols, pair_width) / count_column
    )
    pair_scaled, pair_inv = norm_pieces(mid_act)
    pair_normed = (pair_scaled * pair_norm_gain).astype(jnp.bfloat16)
    pre_act = jnp.dot(pair_normed, hidden_weight, preferred_element_type=jnp.float32)
    act_value, act_slope = silu_pieces(pre_act)
    hidden = act_value.astype(jnp.bfloat16)
    masked_grad = (
        pair_output_gradient * pair_update_mask.astype(jnp.bfloat16)[:, :, None]
    ).reshape(residue_row_block * pair_cols, pair_width)
    final_matrix_derivative = jnp.dot(hidden.T, masked_grad, preferred_element_type=jnp.float32)
    back_prod = jnp.dot(masked_grad, back_weight.T, preferred_element_type=jnp.float32)
    grad_hidden = (back_prod * act_slope).astype(jnp.bfloat16)
    middle_matrix_derivative = jnp.dot(
        pair_normed.T, grad_hidden, preferred_element_type=jnp.float32
    )
    grad_scaled = (
        jnp.dot(grad_hidden, hidden_weight.T, preferred_element_type=jnp.float32) * pair_norm_gain
    )
    grad_mid = pair_output_gradient.reshape(residue_row_block * pair_cols, pair_width).astype(
        jnp.float32
    ) + standardize_adjoint(grad_scaled, pair_scaled, pair_inv)
    couple_features_derivative = grad_mid.astype(jnp.bfloat16).reshape(
        residue_row_block, pair_cols, pair_width
    )
    grad_opm = (
        (grad_mid / count_column)
        .astype(jnp.bfloat16)
        .reshape(residue_row_block, pair_cols, pair_width)
    )
    full_opm = lax.all_gather(grad_opm, "depth", axis=1, tiled=True).reshape(
        residue_row_block, depth_count, pair_cols, pair_width
    )

    def backward_step(step_index, loop_state):
        grad_left_acc, grad_out, right_term = loop_state
        col_start = step_index * col_block
        outer_part, right_piece = partial_outer(col_start)
        opm_piece = lax.dynamic_slice_in_dim(full_opm, col_start, col_block, 2).reshape(
            residue_row_block * block_depth * col_block, pair_width
        )
        grad_out = grad_out + jnp.dot(
            outer_part.reshape(residue_row_block * block_depth * col_block, outer_width).T,
            opm_piece.astype(jnp.float32),
            precision=highest,
        )
        grad_outer = jnp.dot(opm_piece, output_weight.T, preferred_element_type=jnp.float32).astype(
            jnp.bfloat16
        )
        grad_outer = grad_outer.reshape(
            residue_row_block, block_depth, col_block, proj_width, proj_width
        )
        grad_left_acc = grad_left_acc + jnp.einsum(
            "iejcd,sejd->sic", grad_outer, right_piece, preferred_element_type=jnp.float32
        )
        piece_term = jnp.einsum(
            "iejcd,sic->ejsd", grad_outer, left_proj, preferred_element_type=jnp.float32
        )
        piece_term = piece_term.reshape(block_depth, col_block, seq_total * proj_width)
        right_term = lax.dynamic_update_slice_in_dim(right_term, piece_term, col_start, 1)
        return (grad_left_acc, grad_out, right_term)

    grad_left_acc, result_matrix_derivative, right_term = lax.fori_loop(
        0,
        block_count,
        backward_step,
        (
            jnp.zeros((seq_total, residue_row_block, proj_width), jnp.float32),
            jnp.zeros((outer_width, pair_width), jnp.float32),
            jnp.zeros((block_depth, pair_cols, seq_total * proj_width), jnp.float32),
        ),
    )
    grad_right_sum = lax.psum_scatter(
        right_term.reshape(residues, seq_total * proj_width), "col", scatter_dimension=0, tiled=True
    )
    grad_right_acc = jnp.transpose(
        grad_right_sum.reshape(residue_row_block, seq_total, proj_width), (1, 0, 2)
    )
    grad_left = (grad_left_acc * mask_floating[:, :, None]).astype(jnp.bfloat16)
    grad_right = (grad_right_acc * mask_floating[:, :, None]).astype(jnp.bfloat16)
    normed_rows = normalized_rows.reshape(sequence_row_block * residue_row_block, channel_total)
    first_projector_derivative = jnp.dot(
        normed_rows.T,
        grad_left.reshape(sequence_row_block * residue_row_block, proj_width),
        preferred_element_type=jnp.float32,
    )
    second_projector_derivative = jnp.dot(
        normed_rows.T,
        grad_right.reshape(sequence_row_block * residue_row_block, proj_width),
        preferred_element_type=jnp.float32,
    )
    standardized_derivative = jnp.dot(
        grad_left, first_projector.T, preferred_element_type=jnp.float32
    ) + jnp.dot(grad_right, second_projector.T, preferred_element_type=jnp.float32)
    features_derivative = standardize_adjoint(
        standardized_derivative * layer_scale_factor, standardized_features, reciprocal_spread
    ).astype(jnp.bfloat16)
    weight_sums = lax.psum(
        (
            first_projector_derivative,
            second_projector_derivative,
            result_matrix_derivative,
            middle_matrix_derivative,
            final_matrix_derivative,
        ),
        ("depth", "col"),
    )
    return (
        features_derivative,
        couple_features_derivative,
        weight_sums[0],
        weight_sums[1],
        weight_sums[2],
        weight_sums[3],
        weight_sums[4],
    )


FEW_RESIDUES = 32
MASK_ROWS = 16
Z_PARTNERS = (6, 4, 2)
Y_PARTNER = 1


def butterfly(blocks, group):
    lane_group = lax.broadcasted_iota(jnp.int32, blocks[0].shape, 1) // group
    width = 4 * group
    for bit in (2, 1):
        low = (lane_group & bit) == 0
        swapped = list(blocks)
        for at in range(4):
            if at & bit:
                continue
            here, there = blocks[at], blocks[at | bit]
            moving = jnp.where(low, there, here)
            if bit == 2:
                moved = pltpu.roll(moving, 2 * group, 1)
            else:
                moved = jnp.where(
                    low, pltpu.roll(moving, width - group, 1), pltpu.roll(moving, group, 1)
                )
            swapped[at] = jnp.where(low, here, moved)
            swapped[at | bit] = jnp.where(low, moved, there)
        blocks = swapped
    return blocks


def wide_projector(first_ref, second_ref, copies):
    return jnp.concatenate([first_ref[...]] * copies + [second_ref[...]] * copies, axis=0)


def pre_kernel(
    ids_ref,
    x_hbm,
    maskt_hbm,
    pmask_hbm,
    scale_hbm,
    first_hbm,
    second_hbm,
    gain_hbm,
    act_hbm,
    grad_hbm,
    sent_ref,
    scale_ref,
    first_ref,
    second_ref,
    gain_ref,
    normed_ref,
    scaled_ref,
    inv_ref,
    wide_ref,
    tile_ref,
    x_ref,
    maskt_ref,
    pmask_ref,
    sems,
):
    res, seqs = maskt_ref.shape
    pairs = act_hbm.shape[0]
    first_pair = 2 * seqs + MASK_ROWS
    copies = [
        pltpu.make_async_copy(source, target, sems.at[at])
        for at, (source, target) in enumerate(
            (
                (x_hbm, x_ref),
                (maskt_hbm, maskt_ref),
                (pmask_hbm, pmask_ref),
                (scale_hbm, scale_ref),
                (first_hbm, first_ref),
                (second_hbm, second_ref),
                (gain_hbm, gain_ref),
                (act_hbm, sent_ref.at[0, pl.ds(first_pair, pairs), :]),
                (grad_hbm, sent_ref.at[0, pl.ds(first_pair + pairs, pairs), :]),
            )
        )
    ]
    for copy in copies:
        copy.start()
    for copy in copies:
        copy.wait()
    lanes = sent_ref.shape[2]
    group = lanes // res
    scaled, inv = norm_pieces(
        x_ref[...].astype(jnp.float32).reshape(seqs * res, x_ref.shape[2])
    )
    scaled_ref[...] = scaled
    inv_ref[...] = inv
    normed = (scaled * scale_ref[...]).astype(jnp.bfloat16)
    normed_ref[...] = normed
    wide = lax.dot_general(
        normed,
        wide_projector(first_ref, second_ref, res),
        (((1,), (1,)), ((), ())),
        preferred_element_type=jnp.float32,
    )
    for at in range(2):
        wide_ref[at] = wide[:, at * lanes : (at + 1) * lanes]
    tile_ref[...] = jnp.zeros(tile_ref.shape, jnp.float32)
    mask = maskt_ref[...].astype(jnp.float32)
    tile_ref[0:res, 0:seqs] = mask
    spread = (
        lax.broadcasted_iota(jnp.int32, (MASK_ROWS, lanes), 1) // group
        == lax.broadcasted_iota(jnp.int32, (MASK_ROWS, lanes), 0)
    ).astype(jnp.float32)
    mask_lanes = lax.dot_general(
        tile_ref[...], spread, (((0,), (0,)), ((), ())), preferred_element_type=jnp.float32
    )[:seqs]
    twice = jnp.concatenate([mask] * (lanes // seqs), axis=1)
    here = lax.broadcasted_iota(jnp.int32, (res, lanes), 1) // seqs == ids_ref[0]
    tile_ref[0:res, :] = jnp.where(here, twice, 0.0)
    tile_ref[res : 2 * res, 0 : pmask_ref.shape[1]] = pmask_ref[...].astype(jnp.float32)
    lane_group = lax.broadcasted_iota(jnp.int32, (seqs, lanes), 1) // group
    for at in range(2):
        both = wide_ref[at, pl.ds(0, seqs, stride=res), :]
        for r in range(1, res):
            both = jnp.where(
                lane_group == r, wide_ref[at, pl.ds(r, seqs, stride=res), :], both
            )
        sent_ref[0, at * seqs : (at + 1) * seqs, :] = (both * mask_lanes).astype(jnp.bfloat16)
    sent_ref[0, 2 * seqs : first_pair, :] = tile_ref[...].astype(jnp.bfloat16)


def outer_kernel(
    sizes,
    orders,
    ids_ref,
    near_ref,
    far_ref,
    other_near_ref,
    other_far_ref,
    wturn_ref,
    outer_ref,
    proj_out_ref,
    cnt_ref,
    pm_ref,
    maskt_ref,
    got_ref,
    leftn_ref,
    mine_ref,
    turn_ref,
    cntl_ref,
    pml_ref,
):
    seqs, res, pair_cols, width = sizes
    depths, cols = got_ref.shape[0], got_ref.shape[1]
    residues = cols * res
    lanes = res * width
    half_cols = pair_cols // res
    me_depth = ids_ref[0]
    me_col = ids_ref[1]
    f32, bf16 = jnp.float32, jnp.bfloat16

    for order, mine, other in zip(orders, (near_ref, far_ref), (other_near_ref, other_far_ref)):
        for at, partner in enumerate(order):
            got_ref[me_depth, me_col ^ partner] = mine[at]
            got_ref[1 - me_depth, me_col ^ partner] = other[at]

    for e in range(depths):
        for k in range(cols):
            leftn_ref[e * seqs : (e + 1) * seqs, k * lanes : (k + 1) * lanes] = got_ref[
                e, k, 0:seqs, :
            ]
    for k in range(half_cols):
        block = jnp.concatenate(
            [
                got_ref[e, me_depth * half_cols + k, seqs : 2 * seqs, :]
                for e in range(depths)
            ],
            axis=0,
        ).astype(f32)
        turn_ref[k * lanes : (k + 1) * lanes, :] = block.T
    for d in range(width):
        mine_ref[d * pair_cols : (d + 1) * pair_cols, :] = turn_ref[
            pl.ds(d, pair_cols, stride=width), :
        ].astype(bf16)

    base = 2 * seqs
    pair_lane = lax.broadcasted_iota(jnp.int32, (pair_cols, lanes), 1)
    pair_row = lax.broadcasted_iota(jnp.int32, (pair_cols, lanes), 0)
    for k in range(cols):
        tiles = [got_ref[e, k, base : base + MASK_ROWS, :].astype(f32) for e in range(depths)]
        maskt_ref[k * res : (k + 1) * res, :] = tiles[0][0:res] + tiles[1][0:res]
        own = got_ref[me_depth, k, base : base + MASK_ROWS, :].astype(f32)
        for r in range(res):
            row = own[res + r : res + r + 1, :]
            first = (k * res + r) * pair_cols
            pml_ref[first : first + pair_cols, :] = jnp.where(
                pair_lane == pair_row, row, 0.0
            ).astype(bf16)
    maskt = maskt_ref[...]
    cols_mask = maskt_ref[pl.ds(pl.multiple_of(me_depth * pair_cols, pair_cols), pair_cols), :]
    for i in range(residues):
        cntl_ref[i * pair_cols : (i + 1) * pair_cols, :] = (maskt[i : i + 1, :] * cols_mask).astype(
            bf16
        )
    ones = jnp.ones((lanes, lanes), bf16)
    cnt_ref[...] = jnp.dot(cntl_ref[...], ones, preferred_element_type=f32)
    pm_ref[...] = jnp.dot(pml_ref[...], ones, preferred_element_type=f32).astype(bf16)

    for dh in range(width // 4):
        prod = jnp.dot(
            mine_ref[dh * 4 * pair_cols : (dh + 1) * 4 * pair_cols, :],
            leftn_ref[...],
            preferred_element_type=f32,
        )
        for k in range(cols):
            piece = prod[:, k * lanes : (k + 1) * lanes]
            turned = butterfly(
                [piece[a * pair_cols : (a + 1) * pair_cols] for a in range(4)], width
            )
            for il in range(res):
                first = (k * res + il) * pair_cols
                outer_ref[first : first + pair_cols, dh * lanes : (dh + 1) * lanes] = turned[
                    il
                ].astype(bf16)
    proj_out_ref[...] = jnp.dot(outer_ref[...], wturn_ref[...], preferred_element_type=f32)


def turn_kernel(
    sizes,
    orders,
    ids_ref,
    near_ref,
    far_ref,
    other_near_ref,
    other_far_ref,
    rightt_ref,
    leftt_ref,
    got_ref,
    turn_ref,
):
    seqs, res, _, width = sizes
    depths, cols = got_ref.shape[0], got_ref.shape[1]
    lanes = res * width
    residues = res * cols
    me_depth = ids_ref[0]
    me_col = ids_ref[1]
    for order, mine, other in zip(orders, (near_ref, far_ref), (other_near_ref, other_far_ref)):
        for at, partner in enumerate(order):
            got_ref[me_depth, me_col ^ partner] = mine[at, 0 : 2 * seqs, :]
            got_ref[1 - me_depth, me_col ^ partner] = other[at, 0 : 2 * seqs, :]
    for at, out in ((0, leftt_ref), (1, rightt_ref)):
        for k in range(cols):
            block = jnp.concatenate(
                [got_ref[e, k, at * seqs : (at + 1) * seqs, :] for e in range(depths)], axis=0
            ).astype(jnp.float32)
            turn_ref[k * lanes : (k + 1) * lanes, :] = block.T
        for d in range(width):
            out[d * residues : (d + 1) * residues, :] = turn_ref[
                pl.ds(d, residues, stride=width), :
            ].astype(jnp.bfloat16)


def transition_kernel(
    sizes,
    orders,
    ids_ref,
    near_ref,
    far_ref,
    proj_out_ref,
    cnt_ref,
    pm_ref,
    gain_ref,
    hid_ref,
    back_ref,
    couple_ref,
    opm_ref,
    pn_ref,
    gh_ref,
    hidden_ref,
    mg_ref,
    pgot_ref,
    gmid_ref,
):
    seqs, res, pair_cols, width = sizes
    per = res * pair_cols
    cols = pgot_ref.shape[0]
    me_col = ids_ref[1]
    f32, bf16 = jnp.float32, jnp.bfloat16
    for order, mine in zip(orders, (near_ref, far_ref)):
        for at, partner in enumerate(order):
            pgot_ref[me_col ^ partner] = mine[at]
    gain = gain_ref[...]
    chunk = 2 * per
    for at in range(cols // 2):
        rows = slice(at * chunk, (at + 1) * chunk)
        act, grad = [
            jnp.concatenate(
                [pgot_ref[2 * at + b, w * per : (w + 1) * per, :] for b in range(2)], axis=0
            )
            for w in range(2)
        ]
        count = cnt_ref[rows, :]
        mid = act.astype(f32) + proj_out_ref[rows, :] / count
        scaled, inv = norm_pieces(mid)
        normed = (scaled * gain).astype(bf16)
        pn_ref[rows, :] = normed
        pre = jnp.dot(normed, hid_ref[...], preferred_element_type=f32)
        value, slope = silu_pieces(pre)
        hidden_ref[rows, :] = value.astype(bf16)
        masked = grad * pm_ref[rows, :]
        mg_ref[rows, :] = masked
        back = lax.dot_general(
            masked, back_ref[...], (((1,), (1,)), ((), ())), preferred_element_type=f32
        )
        ghid = (back * slope).astype(bf16)
        gh_ref[rows, :] = ghid
        gsc = (
            lax.dot_general(
                ghid, hid_ref[...], (((1,), (1,)), ((), ())), preferred_element_type=f32
            )
            * gain
        )
        gmid = grad.astype(f32) + standardize_adjoint(gsc, scaled, inv)
        gmid_ref[rows, :] = gmid
        opm_ref[rows, :] = (gmid / count).astype(bf16)
    couple_ref[...] = gmid_ref[pl.ds(pl.multiple_of(me_col * per, per), per), :].astype(bf16)


def projector_kernel(
    sizes,
    ids_ref,
    opm_ref,
    other_opm_ref,
    rightt_ref,
    leftt_ref,
    wout_ref,
    wturn_ref,
    maskt_ref,
    normed_ref,
    far_normed_ref,
    other_normed_ref,
    other_far_normed_ref,
    part_ref,
    spread_ref,
    gf_ref,
    grow_ref,
    gcol_ref,
    gor_ref,
    goc_ref,
    gs_ref,
    rows_ref,
):
    seqs, res, pair_cols, width = sizes
    depths, half = gf_ref.shape[0], gf_ref.shape[1]
    residues = half // pair_cols
    lanes = res * width
    here = 2 * res
    me_depth = ids_ref[0]
    me_col = ids_ref[1]
    me_y = me_col % 2
    first_here = (me_col // 2) * here
    f32, bf16 = jnp.float32, jnp.bfloat16
    gf_ref[me_depth] = opm_ref[...].astype(f32)
    gf_ref[1 - me_depth] = other_opm_ref[...].astype(f32)
    for y, e, block in (
        (me_y, me_depth, normed_ref),
        (1 - me_y, me_depth, far_normed_ref),
        (me_y, 1 - me_depth, other_normed_ref),
        (1 - me_y, 1 - me_depth, other_far_normed_ref),
    ):
        rows_ref[y, e] = block[...]

    for il in range(here):
        for e in range(depths):
            first = pl.multiple_of((first_here + il) * pair_cols, pair_cols)
            grow_ref[il * residues + e * pair_cols : il * residues + (e + 1) * pair_cols, :] = (
                gf_ref[e, pl.ds(first, pair_cols), :].astype(bf16)
            )
    my_half = first_here // pair_cols
    my_first = first_here - my_half * pair_cols
    for jl in range(here):
        gcol_ref[jl * residues : (jl + 1) * residues, :] = gf_ref[
            my_half, pl.ds(my_first + jl, residues, stride=pair_cols), :
        ].astype(bf16)
    for lhs, weight, out in ((grow_ref, wturn_ref, gor_ref), (gcol_ref, wout_ref, goc_ref)):
        for dh in range(width // 4):
            piece = lax.dot_general(
                lhs[...],
                weight[dh * lanes : (dh + 1) * lanes, :],
                (((1,), (1,)), ((), ())),
                preferred_element_type=f32,
            )
            for y in range(2):
                turned = butterfly(
                    [
                        piece[(y * res + a) * residues : (y * res + a + 1) * residues]
                        for a in range(4)
                    ],
                    width,
                )
                for dl in range(4):
                    first = (dh * 4 + dl) * residues
                    out[first : first + residues, y * lanes : (y + 1) * lanes] = turned[dl].astype(
                        bf16
                    )
    group = lax.broadcasted_iota(jnp.int32, (here, here * width), 1) // width
    spread = (group == lax.broadcasted_iota(jnp.int32, (here, here * width), 0)).astype(f32)
    mask_lanes = lax.dot_general(
        maskt_ref[pl.ds(pl.multiple_of(first_here, here), here), :],
        spread,
        (((0,), (0,)), ((), ())),
        preferred_element_type=f32,
    )
    lane_group = lax.broadcasted_iota(jnp.int32, (seqs, lanes), 1) // width
    for at, (lhs, rhs) in enumerate(((rightt_ref, gor_ref), (leftt_ref, goc_ref))):
        total = lax.dot_general(
            lhs[...], rhs[...], (((0,), (0,)), ((), ())), preferred_element_type=f32
        )
        total = (total * mask_lanes).astype(bf16).astype(f32)
        for y in range(2):
            for e in range(depths):
                block = total[e * seqs : (e + 1) * seqs, y * lanes : (y + 1) * lanes]
                for r in range(res):
                    gs_ref[at, y, e, pl.ds(r, seqs, stride=res), :] = jnp.where(
                        lane_group == r, block, 0.0
                    )
    spread_ref[...] = jnp.concatenate(
        [gs_ref[0, me_y, me_depth], gs_ref[1, me_y, me_depth]], axis=1
    ).astype(bf16)
    rows = rows_ref.shape[2]
    for at in range(2):
        cross = lax.dot_general(
            gs_ref[at].reshape(2 * depths * rows, lanes).astype(bf16),
            rows_ref[...].reshape(2 * depths * rows, rows_ref.shape[3]),
            (((0,), (0,)), ((), ())),
            preferred_element_type=f32,
        )
        total = cross[:width]
        for r in range(1, res):
            total = total + cross[r * width : (r + 1) * width]
        part_ref[at * width : (at + 1) * width, :] = total.astype(bf16)


def weights_kernel(outer_ref, opm_ref, pn_ref, gh_ref, hidden_ref, mg_ref, out_ref, turn_ref):
    pair_width, hid = pn_ref.shape[1], gh_ref.shape[1]
    outer_width = outer_ref.shape[1]
    width = int(outer_width**0.5 + 0.5)

    def contract(lhs, rhs):
        return lax.dot_general(
            lhs[...], rhs[...], (((0,), (0,)), ((), ())), preferred_element_type=jnp.float32
        )

    turn_ref[...] = contract(outer_ref, opm_ref)
    for c in range(width):
        out_ref[c * width : (c + 1) * width, :] = turn_ref[
            pl.ds(c, width, stride=width), :
        ].astype(jnp.bfloat16)
    dhid = contract(pn_ref, gh_ref).astype(jnp.bfloat16)
    for at in range(hid // pair_width):
        first = outer_width + at * pair_width
        out_ref[first : first + pair_width, :] = dhid[:, at * pair_width : (at + 1) * pair_width]
    out_ref[outer_width + hid :, :] = contract(hidden_ref, mg_ref).astype(jnp.bfloat16)


def weights_sum_kernel(mine_ref, other_ref, dout_ref, dhid_ref, dback_ref):
    pair_width, hid = dhid_ref.shape
    outer_width = dout_ref.shape[0]

    def added(first, count):
        rows = slice(first, first + count)
        return mine_ref[rows, :].astype(jnp.float32) + other_ref[rows, :].astype(jnp.float32)

    dout_ref[...] = added(0, outer_width)
    for at in range(hid // pair_width):
        dhid_ref[:, at * pair_width : (at + 1) * pair_width] = added(
            outer_width + at * pair_width, pair_width
        )
    dback_ref[...] = added(outer_width + hid, hid)


def feature_kernel(
    copies, spread_ref, first_ref, second_ref, scale_ref, scaled_ref, inv_ref, feat_ref
):
    back = jnp.dot(
        spread_ref[...],
        wide_projector(first_ref, second_ref, copies),
        preferred_element_type=jnp.float32,
    )
    feat_ref[...] = standardize_adjoint(
        back * scale_ref[...], scaled_ref[...], inv_ref[...]
    ).astype(jnp.bfloat16)


def swap_line(block, partners):
    count = lax.axis_size("col")
    pairs = [
        (depth * count + at, depth * count + (at ^ partner))
        for depth, partner in enumerate(partners)
        if partner is not None
        for at in range(count)
    ]
    return lax.ppermute(block, ("depth", "col"), pairs)


def swap_depth(block):
    return lax.ppermute(block, "depth", [(0, 1), (1, 0)])


def pairwise_sum(blocks):
    while len(blocks) > 1:
        blocks = [blocks[at] + blocks[at + 1] for at in range(0, len(blocks), 2)]
    return blocks[0]


def swap_col(block, partner):
    count = lax.axis_size("col")
    return lax.ppermute(block, "col", [(at, at ^ partner) for at in range(count)])


def whole_plan(
    alignment_activations,
    alignment_mask,
    pair_activation_input,
    pair_update_mask,
    pair_output_gradient,
    layer_scale_factor,
    first_projector,
    second_projector,
    output_weight,
    pair_norm_gain,
    hidden_weight,
    back_weight,
):
    seqs, res, channels = alignment_activations.shape
    width = first_projector.shape[1]
    outer_width = width * width
    cols = lax.axis_size("col")
    depths = lax.axis_size("depth")
    residues = res * cols
    pair_cols, pair_width = pair_activation_input.shape[1:]
    hid = hidden_weight.shape[1]
    per = res * pair_cols
    lanes = res * width
    rows = 2 * seqs + MASK_ROWS
    half = residues * pair_cols
    f32, bf16 = jnp.float32, jnp.bfloat16
    ids = jnp.stack([lax.axis_index("depth"), lax.axis_index("col")]).astype(jnp.int32)
    smem = pl.BlockSpec(memory_space=pltpu.SMEM)
    vmem = pl.BlockSpec(memory_space=pltpu.VMEM)
    params = pltpu.CompilerParams(vmem_limit_bytes=16 * 2**20)
    scale = layer_scale_factor.reshape(1, channels)
    first, second = first_projector.T, second_projector.T
    wturn = jnp.transpose(output_weight.reshape(width, width, pair_width), (1, 0, 2)).reshape(
        outer_width, pair_width
    )
    shape = jax.ShapeDtypeStruct
    sent, scale, first, second, gain, normed, scaled, inv = pl.pallas_call(
        pre_kernel,
        out_shape=(
            shape((1, rows + 2 * per, pair_width), bf16),
            shape((1, channels), f32),
            shape((width, channels), bf16),
            shape((width, channels), bf16),
            shape((1, pair_width), f32),
            shape((seqs * res, channels), bf16),
            shape((seqs * res, channels), f32),
            shape((seqs * res, 1), f32),
        ),
        in_specs=[smem] + [pl.BlockSpec(memory_space=pltpu.HBM)] * 9,
        out_specs=[vmem] * 8,
        scratch_shapes=[
            pltpu.VMEM((2, seqs * res, lanes), f32),
            pltpu.VMEM((MASK_ROWS, lanes), f32),
            pltpu.VMEM((seqs, res, channels), bf16),
            pltpu.VMEM((res, seqs), jnp.int32),
            pltpu.VMEM((res, pair_cols), jnp.int32),
            pltpu.SemaphoreType.DMA((9,)),
        ],
        compiler_params=params,
        name="project",
    )(
        ids,
        *[
            pltpu.with_memory_space_constraint(array, pltpu.HBM)
            for array in (
                alignment_activations,
                alignment_mask.T,
                pair_update_mask,
                scale,
                first,
                second,
                pair_norm_gain.reshape(1, pair_width),
                pair_activation_input.reshape(per, pair_width),
                pair_output_gradient.reshape(per, pair_width),
            )
        ],
    )
    near_order = (0,) + Z_PARTNERS
    far_order = tuple(at ^ Y_PARTNER for at in near_order)
    blocks = lax.optimization_barrier(
        jnp.concatenate([sent] + [swap_col(sent, partner) for partner in Z_PARTNERS])
    )
    half_normed = seqs * res // 2
    far_normed_a = swap_col(normed[:half_normed], Y_PARTNER)
    blocks, far_normed_a = lax.optimization_barrier((blocks, far_normed_a))
    near, pair_near = blocks[:, :rows], blocks[:, rows:]
    far = swap_col(near, Y_PARTNER)
    pair_far = swap_col(pair_near, Y_PARTNER)
    far, normed_b = lax.optimization_barrier((far, normed[half_normed:]))
    far_normed_b = swap_col(normed_b, Y_PARTNER)
    other_near, other_far = swap_depth(near), swap_depth(far)
    sizes = (seqs, res, pair_cols, width)
    orders = (near_order, far_order)
    outer, proj_out, cnt, pm, maskt = pl.pallas_call(
        functools.partial(outer_kernel, sizes, orders),
        out_shape=(
            shape((half, outer_width), bf16),
            shape((half, pair_width), f32),
            shape((half, lanes), f32),
            shape((half, lanes), bf16),
            shape((residues, depths * seqs), f32),
        ),
        in_specs=[smem] + [vmem] * 5,
        out_specs=[vmem] * 5,
        scratch_shapes=[
            pltpu.VMEM((depths, cols, rows, pair_width), bf16),
            pltpu.VMEM((depths * seqs, residues * width), bf16),
            pltpu.VMEM((pair_cols * width, depths * seqs), bf16),
            pltpu.VMEM((pair_cols * width, depths * seqs), f32),
            pltpu.VMEM((half, lanes), bf16),
            pltpu.VMEM((half, lanes), bf16),
        ],
        compiler_params=params,
        name="outer_products",
    )(ids, near, far, other_near, other_far, wturn)
    other_near, other_far, proj_out = lax.optimization_barrier((other_near, other_far, proj_out))
    rightt, leftt = pl.pallas_call(
        functools.partial(turn_kernel, sizes, orders),
        out_shape=(
            shape((residues * width, depths * seqs), bf16),
            shape((residues * width, depths * seqs), bf16),
        ),
        in_specs=[smem] + [vmem] * 4,
        out_specs=[vmem] * 2,
        scratch_shapes=[
            pltpu.VMEM((depths, cols, 2 * seqs, pair_width), bf16),
            pltpu.VMEM((residues * width, depths * seqs), f32),
        ],
        compiler_params=params,
        name="turned",
    )(ids, near, far, other_near, other_far)
    pair_far, rightt, leftt, proj_out = lax.optimization_barrier(
        (pair_far, rightt, leftt, proj_out)
    )
    couple, opm, pn, gh, hidden, mg = pl.pallas_call(
        functools.partial(transition_kernel, sizes, orders),
        out_shape=(
            shape((per, pair_width), bf16),
            shape((half, pair_width), bf16),
            shape((half, pair_width), bf16),
            shape((half, hid), bf16),
            shape((half, hid), bf16),
            shape((half, pair_width), bf16),
        ),
        in_specs=[smem] + [vmem] * 8,
        out_specs=[vmem] * 6,
        scratch_shapes=[
            pltpu.VMEM((cols, 2 * per, pair_width), bf16),
            pltpu.VMEM((half, pair_width), f32),
        ],
        compiler_params=params,
        name="transition",
    )(
        ids,
        pair_near,
        pair_far,
        proj_out,
        cnt,
        pm,
        gain,
        hidden_weight,
        back_weight,
    )
    opm, far_normed_b = lax.optimization_barrier((opm, far_normed_b))
    far_normed = jnp.concatenate([far_normed_a, far_normed_b])
    weights = pl.pallas_call(
        weights_kernel,
        out_shape=shape((outer_width + 2 * hid, pair_width), bf16),
        in_specs=[vmem] * 6,
        out_specs=vmem,
        scratch_shapes=[pltpu.VMEM((outer_width, pair_width), f32)],
        compiler_params=params,
        name="weight_gradients",
    )(outer, opm, pn, gh, hidden, mg)
    other_opm, other_normed, other_far_normed, weights = lax.optimization_barrier(
        (swap_depth(opm), swap_depth(normed), swap_depth(far_normed), weights)
    )
    part, spread = pl.pallas_call(
        functools.partial(projector_kernel, sizes),
        out_shape=(
            shape((2 * width, channels), bf16),
            shape((seqs * res, 2 * lanes), bf16),
        ),
        in_specs=[smem] + [vmem] * 11,
        out_specs=[vmem] * 2,
        scratch_shapes=[
            pltpu.VMEM((depths, half, pair_width), f32),
            pltpu.VMEM((2 * res * residues, pair_width), bf16),
            pltpu.VMEM((2 * res * residues, pair_width), bf16),
            pltpu.VMEM((residues * width, 2 * lanes), bf16),
            pltpu.VMEM((residues * width, 2 * lanes), bf16),
            pltpu.VMEM((2, 2, depths, seqs * res, lanes), f32),
            pltpu.VMEM((2, depths, seqs * res, channels), bf16),
        ],
        compiler_params=params,
        name="projector_parts",
    )(
        ids,
        opm,
        other_opm,
        rightt,
        leftt,
        output_weight,
        wturn,
        maskt,
        normed,
        far_normed,
        other_normed,
        other_far_normed,
    )
    feat = pl.pallas_call(
        functools.partial(feature_kernel, res),
        out_shape=shape((seqs * res, channels), bf16),
        in_specs=[vmem] * 6,
        out_specs=vmem,
        compiler_params=params,
        name="features",
    )(spread, first, second, scale, scaled, inv)
    part, weights = lax.optimization_barrier((part, weights))
    dout, dhid, dback = pl.pallas_call(
        weights_sum_kernel,
        out_shape=(
            shape((outer_width, pair_width), f32),
            shape((pair_width, hid), f32),
            shape((hid, pair_width), f32),
        ),
        in_specs=[vmem] * 2,
        out_specs=[vmem] * 3,
        compiler_params=params,
        name="sums_over_depth",
    )(weights, swap_depth(weights))
    came_a = swap_line(part, Z_PARTNERS[:2])
    came_b = swap_line(part, (None, Z_PARTNERS[2]))
    feat = feat.reshape(seqs, res, channels)
    came_a, came_b, feat = lax.optimization_barrier((came_a, came_b, feat))
    kept = jnp.where(lax.axis_index("depth") == 0, part, came_b)
    kept = lax.optimization_barrier((kept.astype(f32) + came_a.astype(f32)).astype(bf16))
    came = swap_depth(kept)
    came, dout, dhid, dback = lax.optimization_barrier((came, dout, dhid, dback))
    total = kept.astype(f32) + came.astype(f32)
    return (
        feat,
        couple.reshape(res, pair_cols, pair_width),
        total[:width].T,
        total[width:].T,
        dout,
        dhid,
        dback,
    )


def on_device(alignment_activations, *others):
    cols = lax.axis_size("col")
    residues = alignment_activations.shape[1] * cols
    plan = whole_plan if cols == 8 and residues <= FEW_RESIDUES else split_plan
    return plan(alignment_activations, *others)


def solution(mesh):
    in_specs = (
        P(("group", "depth"), "col", None),
        P(("group", "depth"), "col"),
        P(("group", "col"), "depth", None),
        P(("group", "col"), "depth"),
        P(("group", "col"), "depth", None),
        P(),
        P(),
        P(),
        P(),
        P(),
        P(),
        P(),
    )
    out_specs = (
        P(("group", "depth"), "col", None),
        P(("group", "col"), "depth", None),
        P("group", None),
        P("group", None),
        P("group", None),
        P("group", None),
        P("group", None),
    )
    return jax.shard_map(
        on_device, mesh=mesh, in_specs=in_specs, out_specs=out_specs, check_vma=False
    )
```

```python
import functools

import jax
import jax.numpy as jnp
from jax import lax
from jax.experimental import pallas as pl
from jax.experimental.pallas import tpu as pltpu
from jax.sharding import PartitionSpec as P

epsilon = 1e-05
highest = lax.Precision.HIGHEST


def norm_pieces(entries_drawn):
    center = entries_drawn - jnp.mean(entries_drawn, axis=-1, keepdims=True)
    inv_std = lax.rsqrt(jnp.mean(center * center, axis=-1, keepdims=True) + epsilon)
    return (center * inv_std, inv_std)


def standardize_adjoint(grad_scaled, scaled, inv_std):
    mean_grad = jnp.mean(grad_scaled, axis=-1, keepdims=True)
    mean_cross = jnp.mean(grad_scaled * scaled, axis=-1, keepdims=True)
    return inv_std * (grad_scaled - mean_grad - scaled * mean_cross)


def silu_pieces(pre_act):
    sigma = jax.nn.sigmoid(pre_act)
    return (pre_act * sigma, sigma * (1.0 + pre_act * (1.0 - sigma)))


def split_plan(
    alignment_activations,
    alignment_mask,
    pair_activation_input,
    pair_update_mask,
    pair_output_gradient,
    layer_scale_factor,
    first_projector,
    second_projector,
    output_weight,
    pair_norm_gain,
    hidden_weight,
    back_weight,
):
    sequence_row_block, residue_row_block, channel_total = alignment_activations.shape
    proj_width = first_projector.shape[1]
    outer_width = proj_width * proj_width
    depth_count = lax.axis_size("depth")
    residues = residue_row_block * lax.axis_size("col")
    pair_cols = pair_activation_input.shape[1]
    pair_width = pair_activation_input.shape[2]
    col_block = min(64, pair_cols)
    block_count = pair_cols // col_block
    standardized_features, reciprocal_spread = norm_pieces(
        alignment_activations.astype(jnp.float32)
    )
    normalized_rows = (standardized_features * layer_scale_factor).astype(jnp.bfloat16)
    mask_floating = alignment_mask.astype(jnp.float32)
    left_proj = (
        jnp.dot(normalized_rows, first_projector, preferred_element_type=jnp.float32)
        * mask_floating[:, :, None]
    ).astype(jnp.bfloat16)
    right_proj = (
        jnp.dot(normalized_rows, second_projector, preferred_element_type=jnp.float32)
        * mask_floating[:, :, None]
    ).astype(jnp.bfloat16)
    right_flat = right_proj.reshape(sequence_row_block, residue_row_block * proj_width)
    mask_converted = alignment_mask.astype(jnp.bfloat16)
    seq_total = left_proj.shape[0]
    gathered, gathered_mask = (
        lax.all_gather(right_flat, "col", axis=1, tiled=True),
        lax.all_gather(mask_converted, "col", axis=1, tiled=True),
    )
    right_blocks = gathered.reshape(seq_total, depth_count, pair_cols, proj_width)
    mask_blocks = gathered_mask.reshape(seq_total, depth_count, pair_cols)
    block_depth = right_blocks.shape[1]
    out_wide = output_weight.astype(jnp.float32)

    def partial_outer(col_start):
        right_piece = lax.dynamic_slice_in_dim(right_blocks, col_start, col_block, 2)
        outer_part = jnp.einsum(
            "sic,sejd->iejcd", left_proj, right_piece, preferred_element_type=jnp.float32
        )
        return (
            outer_part.reshape(residue_row_block, block_depth, col_block, outer_width),
            right_piece,
        )

    def forward_step(step_index, loop_state):
        projected, pair_count = loop_state
        col_start = step_index * col_block
        outer_part, right_piece = partial_outer(col_start)
        mask_piece = lax.dynamic_slice_in_dim(mask_blocks, col_start, col_block, 2).astype(
            jnp.float32
        )
        count_part = jnp.einsum("si,sej->iej", mask_floating, mask_piece, precision=highest)
        outer_mine, count_mine = (
            lax.psum_scatter(
                outer_part.astype(jnp.bfloat16), "depth", scatter_dimension=1, tiled=True
            ).astype(jnp.float32),
            lax.psum_scatter(
                count_part.astype(jnp.bfloat16), "depth", scatter_dimension=1, tiled=True
            ).astype(jnp.float32),
        )
        proj_mine = jnp.dot(
            outer_mine.reshape(residue_row_block * col_block, outer_width),
            out_wide,
            precision=highest,
        )
        proj_mine = proj_mine.reshape(residue_row_block, col_block, pair_width)
        count_mine = count_mine.reshape(residue_row_block, col_block)
        projected = lax.dynamic_update_slice_in_dim(projected, proj_mine, col_start, 1)
        pair_count = lax.dynamic_update_slice_in_dim(pair_count, count_mine, col_start, 1)
        return (projected, pair_count)

    projected, pair_count = lax.fori_loop(
        0,
        block_count,
        forward_step,
        (
            jnp.zeros((residue_row_block, pair_cols, pair_width), jnp.float32),
            jnp.zeros((residue_row_block, pair_cols), jnp.float32),
        ),
    )
    count_column = pair_count.reshape(residue_row_block * pair_cols, 1)
    mid_act = (
        pair_activation_input.reshape(residue_row_block * pair_cols, pair_width).astype(jnp.float32)
        + projected.reshape(residue_row_block * pair_cols, pair_width) / count_column
    )
    pair_scaled, pair_inv = norm_pieces(mid_act)
    pair_normed = (pair_scaled * pair_norm_gain).astype(jnp.bfloat16)
    pre_act = jnp.dot(pair_normed, hidden_weight, preferred_element_type=jnp.float32)
    act_value, act_slope = silu_pieces(pre_act)
    hidden = act_value.astype(jnp.bfloat16)
    masked_grad = (
        pair_output_gradient * pair_update_mask.astype(jnp.bfloat16)[:, :, None]
    ).reshape(residue_row_block * pair_cols, pair_width)
    final_matrix_derivative = jnp.dot(hidden.T, masked_grad, preferred_element_type=jnp.float32)
    back_prod = jnp.dot(masked_grad, back_weight.T, preferred_element_type=jnp.float32)
    grad_hidden = (back_prod * act_slope).astype(jnp.bfloat16)
    middle_matrix_derivative = jnp.dot(
        pair_normed.T, grad_hidden, preferred_element_type=jnp.float32
    )
    grad_scaled = (
        jnp.dot(grad_hidden, hidden_weight.T, preferred_element_type=jnp.float32) * pair_norm_gain
    )
    grad_mid = pair_output_gradient.reshape(residue_row_block * pair_cols, pair_width).astype(
        jnp.float32
    ) + standardize_adjoint(grad_scaled, pair_scaled, pair_inv)
    couple_features_derivative = grad_mid.astype(jnp.bfloat16).reshape(
        residue_row_block, pair_cols, pair_width
    )
    grad_opm = (
        (grad_mid / count_column)
        .astype(jnp.bfloat16)
        .reshape(residue_row_block, pair_cols, pair_width)
    )
    full_opm = lax.all_gather(grad_opm, "depth", axis=1, tiled=True).reshape(
        residue_row_block, depth_count, pair_cols, pair_width
    )

    def backward_step(step_index, loop_state):
        grad_left_acc, grad_out, right_term = loop_state
        col_start = step_index * col_block
        outer_part, right_piece = partial_outer(col_start)
        opm_piece = lax.dynamic_slice_in_dim(full_opm, col_start, col_block, 2).reshape(
            residue_row_block * block_depth * col_block, pair_width
        )
        grad_out = grad_out + jnp.dot(
            outer_part.reshape(residue_row_block * block_depth * col_block, outer_width).T,
            opm_piece.astype(jnp.float32),
            precision=highest,
        )
        grad_outer = jnp.dot(opm_piece, output_weight.T, preferred_element_type=jnp.float32).astype(
            jnp.bfloat16
        )
        grad_outer = grad_outer.reshape(
            residue_row_block, block_depth, col_block, proj_width, proj_width
        )
        grad_left_acc = grad_left_acc + jnp.einsum(
            "iejcd,sejd->sic", grad_outer, right_piece, preferred_element_type=jnp.float32
        )
        piece_term = jnp.einsum(
            "iejcd,sic->ejsd", grad_outer, left_proj, preferred_element_type=jnp.float32
        )
        piece_term = piece_term.reshape(block_depth, col_block, seq_total * proj_width)
        right_term = lax.dynamic_update_slice_in_dim(right_term, piece_term, col_start, 1)
        return (grad_left_acc, grad_out, right_term)

    grad_left_acc, result_matrix_derivative, right_term = lax.fori_loop(
        0,
        block_count,
        backward_step,
        (
            jnp.zeros((seq_total, residue_row_block, proj_width), jnp.float32),
            jnp.zeros((outer_width, pair_width), jnp.float32),
            jnp.zeros((block_depth, pair_cols, seq_total * proj_width), jnp.float32),
        ),
    )
    grad_right_sum = lax.psum_scatter(
        right_term.reshape(residues, seq_total * proj_width), "col", scatter_dimension=0, tiled=True
    )
    grad_right_acc = jnp.transpose(
        grad_right_sum.reshape(residue_row_block, seq_total, proj_width), (1, 0, 2)
    )
    grad_left = (grad_left_acc * mask_floating[:, :, None]).astype(jnp.bfloat16)
    grad_right = (grad_right_acc * mask_floating[:, :, None]).astype(jnp.bfloat16)
    normed_rows = normalized_rows.reshape(sequence_row_block * residue_row_block, channel_total)
    first_projector_derivative = jnp.dot(
        normed_rows.T,
        grad_left.reshape(sequence_row_block * residue_row_block, proj_width),
        preferred_element_type=jnp.float32,
    )
    second_projector_derivative = jnp.dot(
        normed_rows.T,
        grad_right.reshape(sequence_row_block * residue_row_block, proj_width),
        preferred_element_type=jnp.float32,
    )
    standardized_derivative = jnp.dot(
        grad_left, first_projector.T, preferred_element_type=jnp.float32
    ) + jnp.dot(grad_right, second_projector.T, preferred_element_type=jnp.float32)
    features_derivative = standardize_adjoint(
        standardized_derivative * layer_scale_factor, standardized_features, reciprocal_spread
    ).astype(jnp.bfloat16)
    weight_sums = lax.psum(
        (
            first_projector_derivative,
            second_projector_derivative,
            result_matrix_derivative,
            middle_matrix_derivative,
            final_matrix_derivative,
        ),
        ("depth", "col"),
    )
    return (
        features_derivative,
        couple_features_derivative,
        weight_sums[0],
        weight_sums[1],
        weight_sums[2],
        weight_sums[3],
        weight_sums[4],
    )


FEW_RESIDUES = 32
MASK_ROWS = 16
Z_PARTNERS = (6, 4, 2)
Y_PARTNER = 1


def butterfly(blocks, group):
    lane_group = lax.broadcasted_iota(jnp.int32, blocks[0].shape, 1) // group
    width = 4 * group
    for bit in (2, 1):
        low = (lane_group & bit) == 0
        swapped = list(blocks)
        for at in range(4):
            if at & bit:
                continue
            here, there = blocks[at], blocks[at | bit]
            moving = jnp.where(low, there, here)
            if bit == 2:
                moved = pltpu.roll(moving, 2 * group, 1)
            else:
                moved = jnp.where(
                    low, pltpu.roll(moving, width - group, 1), pltpu.roll(moving, group, 1)
                )
            swapped[at] = jnp.where(low, here, moved)
            swapped[at | bit] = jnp.where(low, moved, there)
        blocks = swapped
    return blocks


def wide_projector(first_ref, second_ref, copies):
    return jnp.concatenate([first_ref[...]] * copies + [second_ref[...]] * copies, axis=0)


def pre_kernel(
    ids_ref,
    x_hbm,
    maskt_hbm,
    pmask_hbm,
    scale_hbm,
    first_hbm,
    second_hbm,
    gain_hbm,
    act_hbm,
    grad_hbm,
    sent_ref,
    scale_ref,
    first_ref,
    second_ref,
    gain_ref,
    normed_ref,
    scaled_ref,
    inv_ref,
    wide_ref,
    tile_ref,
    x_ref,
    maskt_ref,
    pmask_ref,
    sems,
):
    res, seqs = maskt_ref.shape
    pairs = act_hbm.shape[0]
    first_pair = 2 * seqs + MASK_ROWS
    copies = [
        pltpu.make_async_copy(source, target, sems.at[at])
        for at, (source, target) in enumerate(
            (
                (x_hbm, x_ref),
                (maskt_hbm, maskt_ref),
                (pmask_hbm, pmask_ref),
                (scale_hbm, scale_ref),
                (first_hbm, first_ref),
                (second_hbm, second_ref),
                (gain_hbm, gain_ref),
                (act_hbm, sent_ref.at[0, pl.ds(first_pair, pairs), :]),
                (grad_hbm, sent_ref.at[0, pl.ds(first_pair + pairs, pairs), :]),
            )
        )
    ]
    for copy in copies:
        copy.start()
    for copy in copies:
        copy.wait()
    lanes = sent_ref.shape[2]
    group = lanes // res
    scaled, inv = norm_pieces(
        x_ref[...].astype(jnp.float32).reshape(seqs * res, x_ref.shape[2])
    )
    scaled_ref[...] = scaled
    inv_ref[...] = inv
    normed = (scaled * scale_ref[...]).astype(jnp.bfloat16)
    normed_ref[...] = normed
    wide = lax.dot_general(
        normed,
        wide_projector(first_ref, second_ref, res),
        (((1,), (1,)), ((), ())),
        preferred_element_type=jnp.float32,
    )
    for at in range(2):
        wide_ref[at] = wide[:, at * lanes : (at + 1) * lanes]
    tile_ref[...] = jnp.zeros(tile_ref.shape, jnp.float32)
    mask = maskt_ref[...].astype(jnp.float32)
    tile_ref[0:res, 0:seqs] = mask
    spread = (
        lax.broadcasted_iota(jnp.int32, (MASK_ROWS, lanes), 1) // group
        == lax.broadcasted_iota(jnp.int32, (MASK_ROWS, lanes), 0)
    ).astype(jnp.float32)
    mask_lanes = lax.dot_general(
        tile_ref[...], spread, (((0,), (0,)), ((), ())), preferred_element_type=jnp.float32
    )[:seqs]
    twice = jnp.concatenate([mask] * (lanes // seqs), axis=1)
    here = lax.broadcasted_iota(jnp.int32, (res, lanes), 1) // seqs == ids_ref[0]
    tile_ref[0:res, :] = jnp.where(here, twice, 0.0)
    tile_ref[res : 2 * res, 0 : pmask_ref.shape[1]] = pmask_ref[...].astype(jnp.float32)
    lane_group = lax.broadcasted_iota(jnp.int32, (seqs, lanes), 1) // group
    for at in range(2):
        both = wide_ref[at, pl.ds(0, seqs, stride=res), :]
        for r in range(1, res):
            both = jnp.where(
                lane_group == r, wide_ref[at, pl.ds(r, seqs, stride=res), :], both
            )
        sent_ref[0, at * seqs : (at + 1) * seqs, :] = (both * mask_lanes).astype(jnp.bfloat16)
    sent_ref[0, 2 * seqs : first_pair, :] = tile_ref[...].astype(jnp.bfloat16)


def outer_kernel(
    sizes,
    orders,
    ids_ref,
    near_ref,
    far_ref,
    other_near_ref,
    other_far_ref,
    wturn_ref,
    outer_ref,
    proj_out_ref,
    cnt_ref,
    pm_ref,
    maskt_ref,
    got_ref,
    leftn_ref,
    mine_ref,
    turn_ref,
    cntl_ref,
    pml_ref,
):
    seqs, res, pair_cols, width = sizes
    depths, cols = got_ref.shape[0], got_ref.shape[1]
    residues = cols * res
    lanes = res * width
    half_cols = pair_cols // res
    me_depth = ids_ref[0]
    me_col = ids_ref[1]
    f32, bf16 = jnp.float32, jnp.bfloat16

    for order, mine, other in zip(orders, (near_ref, far_ref), (other_near_ref, other_far_ref)):
        for at, partner in enumerate(order):
            got_ref[me_depth, me_col ^ partner] = mine[at]
            got_ref[1 - me_depth, me_col ^ partner] = other[at]

    for e in range(depths):
        for k in range(cols):
            leftn_ref[e * seqs : (e + 1) * seqs, k * lanes : (k + 1) * lanes] = got_ref[
                e, k, 0:seqs, :
            ]
    for k in range(half_cols):
        block = jnp.concatenate(
            [
                got_ref[e, me_depth * half_cols + k, seqs : 2 * seqs, :]
                for e in range(depths)
            ],
            axis=0,
        ).astype(f32)
        turn_ref[k * lanes : (k + 1) * lanes, :] = block.T
    for d in range(width):
        mine_ref[d * pair_cols : (d + 1) * pair_cols, :] = turn_ref[
            pl.ds(d, pair_cols, stride=width), :
        ].astype(bf16)

    base = 2 * seqs
    pair_lane = lax.broadcasted_iota(jnp.int32, (pair_cols, lanes), 1)
    pair_row = lax.broadcasted_iota(jnp.int32, (pair_cols, lanes), 0)
    for k in range(cols):
        tiles = [got_ref[e, k, base : base + MASK_ROWS, :].astype(f32) for e in range(depths)]
        maskt_ref[k * res : (k + 1) * res, :] = tiles[0][0:res] + tiles[1][0:res]
        own = got_ref[me_depth, k, base : base + MASK_ROWS, :].astype(f32)
        for r in range(res):
            row = own[res + r : res + r + 1, :]
            first = (k * res + r) * pair_cols
            pml_ref[first : first + pair_cols, :] = jnp.where(
                pair_lane == pair_row, row, 0.0
            ).astype(bf16)
    maskt = maskt_ref[...]
    cols_mask = maskt_ref[pl.ds(pl.multiple_of(me_depth * pair_cols, pair_cols), pair_cols), :]
    for i in range(residues):
        cntl_ref[i * pair_cols : (i + 1) * pair_cols, :] = (maskt[i : i + 1, :] * cols_mask).astype(
            bf16
        )
    ones = jnp.ones((lanes, lanes), bf16)
    cnt_ref[...] = jnp.dot(cntl_ref[...], ones, preferred_element_type=f32)
    pm_ref[...] = jnp.dot(pml_ref[...], ones, preferred_element_type=f32).astype(bf16)

    def outer_step(dh, carry):
        first_row = pl.multiple_of(dh * 4 * pair_cols, 4 * pair_cols)
        first_lane = pl.multiple_of(dh * lanes, lanes)
        prod = jnp.dot(
            mine_ref[pl.ds(first_row, 4 * pair_cols), :],
            leftn_ref[...],
            preferred_element_type=f32,
        )
        for k in range(cols):
            piece = prod[:, k * lanes : (k + 1) * lanes]
            turned = butterfly(
                [piece[a * pair_cols : (a + 1) * pair_cols] for a in range(4)], width
            )
            for il in range(res):
                first = (k * res + il) * pair_cols
                outer_ref[first : first + pair_cols, pl.ds(first_lane, lanes)] = turned[
                    il
                ].astype(bf16)
        return carry

    lax.fori_loop(0, width // 4, outer_step, 0, unroll=2)
    proj_out_ref[...] = jnp.dot(outer_ref[...], wturn_ref[...], preferred_element_type=f32)


def turn_kernel(
    sizes,
    orders,
    ids_ref,
    near_ref,
    far_ref,
    other_near_ref,
    other_far_ref,
    rightt_ref,
    leftt_ref,
    got_ref,
    turn_ref,
):
    seqs, res, _, width = sizes
    depths, cols = got_ref.shape[0], got_ref.shape[1]
    lanes = res * width
    residues = res * cols
    me_depth = ids_ref[0]
    me_col = ids_ref[1]
    for order, mine, other in zip(orders, (near_ref, far_ref), (other_near_ref, other_far_ref)):
        for at, partner in enumerate(order):
            got_ref[me_depth, me_col ^ partner] = mine[at, 0 : 2 * seqs, :]
            got_ref[1 - me_depth, me_col ^ partner] = other[at, 0 : 2 * seqs, :]
    for at, out in ((0, leftt_ref), (1, rightt_ref)):

        def turn_step(k, carry, at=at):
            block = jnp.concatenate(
                [got_ref[e, k, at * seqs : (at + 1) * seqs, :] for e in range(depths)], axis=0
            ).astype(jnp.float32)
            turn_ref[pl.ds(pl.multiple_of(k * lanes, lanes), lanes), :] = block.T
            return carry

        def order_step(d, carry, out=out):
            out[pl.ds(pl.multiple_of(d * residues, residues), residues), :] = turn_ref[
                pl.ds(d, residues, stride=width), :
            ].astype(jnp.bfloat16)
            return carry

        lax.fori_loop(0, cols, turn_step, 0, unroll=2)
        lax.fori_loop(0, width, order_step, 0, unroll=8)


def transition_kernel(
    sizes,
    orders,
    ids_ref,
    near_ref,
    far_ref,
    proj_out_ref,
    cnt_ref,
    pm_ref,
    gain_ref,
    hid_ref,
    back_ref,
    couple_ref,
    opm_ref,
    pn_ref,
    gh_ref,
    hidden_ref,
    mg_ref,
    pgot_ref,
    gmid_ref,
):
    seqs, res, pair_cols, width = sizes
    per = res * pair_cols
    cols = pgot_ref.shape[0]
    me_col = ids_ref[1]
    f32, bf16 = jnp.float32, jnp.bfloat16
    for order, mine in zip(orders, (near_ref, far_ref)):
        for at, partner in enumerate(order):
            pgot_ref[me_col ^ partner] = mine[at]
    gain = gain_ref[...]
    chunk = 2 * per
    def chunk_step(at, carry):
        rows = pl.ds(pl.multiple_of(at * chunk, chunk), chunk)
        act, grad = [
            jnp.concatenate(
                [pgot_ref[2 * at + b, w * per : (w + 1) * per, :] for b in range(2)], axis=0
            )
            for w in range(2)
        ]
        count = cnt_ref[rows, :]
        mid = act.astype(f32) + proj_out_ref[rows, :] / count
        scaled, inv = norm_pieces(mid)
        normed = (scaled * gain).astype(bf16)
        pn_ref[rows, :] = normed
        pre = jnp.dot(normed, hid_ref[...], preferred_element_type=f32)
        value, slope = silu_pieces(pre)
        hidden_ref[rows, :] = value.astype(bf16)
        masked = grad * pm_ref[rows, :]
        mg_ref[rows, :] = masked
        back = lax.dot_general(
            masked, back_ref[...], (((1,), (1,)), ((), ())), preferred_element_type=f32
        )
        ghid = (back * slope).astype(bf16)
        gh_ref[rows, :] = ghid
        gsc = (
            lax.dot_general(
                ghid, hid_ref[...], (((1,), (1,)), ((), ())), preferred_element_type=f32
            )
            * gain
        )
        gmid = grad.astype(f32) + standardize_adjoint(gsc, scaled, inv)
        gmid_ref[rows, :] = gmid
        opm_ref[rows, :] = (gmid / count).astype(bf16)
        return carry

    lax.fori_loop(0, cols // 2, chunk_step, 0, unroll=2)
    couple_ref[...] = gmid_ref[pl.ds(pl.multiple_of(me_col * per, per), per), :].astype(bf16)


def projector_kernel(
    sizes,
    ids_ref,
    opm_ref,
    other_opm_ref,
    rightt_ref,
    leftt_ref,
    wout_ref,
    wturn_ref,
    maskt_ref,
    normed_ref,
    far_normed_ref,
    other_normed_ref,
    other_far_normed_ref,
    part_ref,
    spread_ref,
    gf_ref,
    grow_ref,
    gcol_ref,
    gor_ref,
    goc_ref,
    gs_ref,
    rows_ref,
):
    seqs, res, pair_cols, width = sizes
    depths, half = gf_ref.shape[0], gf_ref.shape[1]
    residues = half // pair_cols
    lanes = res * width
    here = 2 * res
    me_depth = ids_ref[0]
    me_col = ids_ref[1]
    me_y = me_col % 2
    first_here = (me_col // 2) * here
    f32, bf16 = jnp.float32, jnp.bfloat16
    gf_ref[me_depth] = opm_ref[...].astype(f32)
    gf_ref[1 - me_depth] = other_opm_ref[...].astype(f32)
    for y, e, block in (
        (me_y, me_depth, normed_ref),
        (1 - me_y, me_depth, far_normed_ref),
        (me_y, 1 - me_depth, other_normed_ref),
        (1 - me_y, 1 - me_depth, other_far_normed_ref),
    ):
        rows_ref[y, e] = block[...]

    for il in range(here):
        for e in range(depths):
            first = pl.multiple_of((first_here + il) * pair_cols, pair_cols)
            grow_ref[il * residues + e * pair_cols : il * residues + (e + 1) * pair_cols, :] = (
                gf_ref[e, pl.ds(first, pair_cols), :].astype(bf16)
            )
    my_half = first_here // pair_cols
    my_first = first_here - my_half * pair_cols
    for jl in range(here):
        gcol_ref[jl * residues : (jl + 1) * residues, :] = gf_ref[
            my_half, pl.ds(my_first + jl, residues, stride=pair_cols), :
        ].astype(bf16)
    def outer_gradient_step(dh, carry):
        first_row = pl.multiple_of(dh * lanes, lanes)
        for lhs, weight, out in ((grow_ref, wturn_ref, gor_ref), (gcol_ref, wout_ref, goc_ref)):
            piece = lax.dot_general(
                lhs[...],
                weight[pl.ds(first_row, lanes), :],
                (((1,), (1,)), ((), ())),
                preferred_element_type=f32,
            )
            for y in range(2):
                turned = butterfly(
                    [
                        piece[(y * res + a) * residues : (y * res + a + 1) * residues]
                        for a in range(4)
                    ],
                    width,
                )
                for dl in range(4):
                    first = pl.multiple_of((dh * 4 + dl) * residues, residues)
                    out[pl.ds(first, residues), y * lanes : (y + 1) * lanes] = turned[dl].astype(
                        bf16
                    )
        return carry

    lax.fori_loop(0, width // 4, outer_gradient_step, 0, unroll=2)
    group = lax.broadcasted_iota(jnp.int32, (here, here * width), 1) // width
    spread = (group == lax.broadcasted_iota(jnp.int32, (here, here * width), 0)).astype(f32)
    mask_lanes = lax.dot_general(
        maskt_ref[pl.ds(pl.multiple_of(first_here, here), here), :],
        spread,
        (((0,), (0,)), ((), ())),
        preferred_element_type=f32,
    )
    lane_group = lax.broadcasted_iota(jnp.int32, (seqs, lanes), 1) // width
    for at, (lhs, rhs) in enumerate(((rightt_ref, gor_ref), (leftt_ref, goc_ref))):
        total = lax.dot_general(
            lhs[...], rhs[...], (((0,), (0,)), ((), ())), preferred_element_type=f32
        )
        total = (total * mask_lanes).astype(bf16).astype(f32)
        for y in range(2):
            for e in range(depths):
                block = total[e * seqs : (e + 1) * seqs, y * lanes : (y + 1) * lanes]
                for r in range(res):
                    gs_ref[at, y, e, pl.ds(r, seqs, stride=res), :] = jnp.where(
                        lane_group == r, block, 0.0
                    )
    spread_ref[...] = jnp.concatenate(
        [gs_ref[0, me_y, me_depth], gs_ref[1, me_y, me_depth]], axis=1
    ).astype(bf16)
    rows = rows_ref.shape[2]
    for at in range(2):
        cross = lax.dot_general(
            gs_ref[at].reshape(2 * depths * rows, lanes).astype(bf16),
            rows_ref[...].reshape(2 * depths * rows, rows_ref.shape[3]),
            (((0,), (0,)), ((), ())),
            preferred_element_type=f32,
        )
        total = cross[:width]
        for r in range(1, res):
            total = total + cross[r * width : (r + 1) * width]
        part_ref[at * width : (at + 1) * width, :] = total.astype(bf16)


def weights_kernel(outer_ref, opm_ref, pn_ref, gh_ref, hidden_ref, mg_ref, out_ref, turn_ref):
    pair_width, hid = pn_ref.shape[1], gh_ref.shape[1]
    outer_width = outer_ref.shape[1]
    width = int(outer_width**0.5 + 0.5)

    def contract(lhs, rhs):
        return lax.dot_general(
            lhs[...], rhs[...], (((0,), (0,)), ((), ())), preferred_element_type=jnp.float32
        )

    turn_ref[...] = contract(outer_ref, opm_ref)
    for c in range(width):
        out_ref[c * width : (c + 1) * width, :] = turn_ref[
            pl.ds(c, width, stride=width), :
        ].astype(jnp.bfloat16)
    dhid = contract(pn_ref, gh_ref).astype(jnp.bfloat16)
    for at in range(hid // pair_width):
        first = outer_width + at * pair_width
        out_ref[first : first + pair_width, :] = dhid[:, at * pair_width : (at + 1) * pair_width]
    out_ref[outer_width + hid :, :] = contract(hidden_ref, mg_ref).astype(jnp.bfloat16)


def weights_sum_kernel(mine_ref, other_ref, dout_ref, dhid_ref, dback_ref):
    pair_width, hid = dhid_ref.shape
    outer_width = dout_ref.shape[0]

    def added(first, count):
        rows = slice(first, first + count)
        return mine_ref[rows, :].astype(jnp.float32) + other_ref[rows, :].astype(jnp.float32)

    dout_ref[...] = added(0, outer_width)
    for at in range(hid // pair_width):
        dhid_ref[:, at * pair_width : (at + 1) * pair_width] = added(
            outer_width + at * pair_width, pair_width
        )
    dback_ref[...] = added(outer_width + hid, hid)


def feature_kernel(
    copies, spread_ref, first_ref, second_ref, scale_ref, scaled_ref, inv_ref, feat_ref
):
    back = jnp.dot(
        spread_ref[...],
        wide_projector(first_ref, second_ref, copies),
        preferred_element_type=jnp.float32,
    )
    feat_ref[...] = standardize_adjoint(
        back * scale_ref[...], scaled_ref[...], inv_ref[...]
    ).astype(jnp.bfloat16)


def swap_line(block, partners):
    count = lax.axis_size("col")
    pairs = [
        (depth * count + at, depth * count + (at ^ partner))
        for depth, partner in enumerate(partners)
        if partner is not None
        for at in range(count)
    ]
    return lax.ppermute(block, ("depth", "col"), pairs)


def swap_depth(block):
    return lax.ppermute(block, "depth", [(0, 1), (1, 0)])


def pairwise_sum(blocks):
    while len(blocks) > 1:
        blocks = [blocks[at] + blocks[at + 1] for at in range(0, len(blocks), 2)]
    return blocks[0]


def swap_col(block, partner):
    count = lax.axis_size("col")
    return lax.ppermute(block, "col", [(at, at ^ partner) for at in range(count)])


def whole_plan(
    alignment_activations,
    alignment_mask,
    pair_activation_input,
    pair_update_mask,
    pair_output_gradient,
    layer_scale_factor,
    first_projector,
    second_projector,
    output_weight,
    pair_norm_gain,
    hidden_weight,
    back_weight,
):
    seqs, res, channels = alignment_activations.shape
    width = first_projector.shape[1]
    outer_width = width * width
    cols = lax.axis_size("col")
    depths = lax.axis_size("depth")
    residues = res * cols
    pair_cols, pair_width = pair_activation_input.shape[1:]
    hid = hidden_weight.shape[1]
    per = res * pair_cols
    lanes = res * width
    rows = 2 * seqs + MASK_ROWS
    half = residues * pair_cols
    f32, bf16 = jnp.float32, jnp.bfloat16
    ids = jnp.stack([lax.axis_index("depth"), lax.axis_index("col")]).astype(jnp.int32)
    smem = pl.BlockSpec(memory_space=pltpu.SMEM)
    vmem = pl.BlockSpec(memory_space=pltpu.VMEM)
    params = pltpu.CompilerParams(vmem_limit_bytes=16 * 2**20)
    scale = layer_scale_factor.reshape(1, channels)
    first, second = first_projector.T, second_projector.T
    wturn = jnp.transpose(output_weight.reshape(width, width, pair_width), (1, 0, 2)).reshape(
        outer_width, pair_width
    )
    shape = jax.ShapeDtypeStruct
    sent, scale, first, second, gain, normed, scaled, inv = pl.pallas_call(
        pre_kernel,
        out_shape=(
            shape((1, rows + 2 * per, pair_width), bf16),
            shape((1, channels), f32),
            shape((width, channels), bf16),
            shape((width, channels), bf16),
            shape((1, pair_width), f32),
            shape((seqs * res, channels), bf16),
            shape((seqs * res, channels), f32),
            shape((seqs * res, 1), f32),
        ),
        in_specs=[smem] + [pl.BlockSpec(memory_space=pltpu.HBM)] * 9,
        out_specs=[vmem] * 8,
        scratch_shapes=[
            pltpu.VMEM((2, seqs * res, lanes), f32),
            pltpu.VMEM((MASK_ROWS, lanes), f32),
            pltpu.VMEM((seqs, res, channels), bf16),
            pltpu.VMEM((res, seqs), jnp.int32),
            pltpu.VMEM((res, pair_cols), jnp.int32),
            pltpu.SemaphoreType.DMA((9,)),
        ],
        compiler_params=params,
        name="project",
    )(
        ids,
        *[
            pltpu.with_memory_space_constraint(array, pltpu.HBM)
            for array in (
                alignment_activations,
                alignment_mask.T,
                pair_update_mask,
                scale,
                first,
                second,
                pair_norm_gain.reshape(1, pair_width),
                pair_activation_input.reshape(per, pair_width),
                pair_output_gradient.reshape(per, pair_width),
            )
        ],
    )
    near_order = (0,) + Z_PARTNERS
    far_order = tuple(at ^ Y_PARTNER for at in near_order)
    blocks = lax.optimization_barrier(
        jnp.concatenate([sent] + [swap_col(sent, partner) for partner in Z_PARTNERS])
    )
    half_normed = seqs * res // 2
    far_normed_a = swap_col(normed[:half_normed], Y_PARTNER)
    blocks, far_normed_a = lax.optimization_barrier((blocks, far_normed_a))
    near, pair_near = blocks[:, :rows], blocks[:, rows:]
    far = swap_col(near, Y_PARTNER)
    pair_far = swap_col(pair_near, Y_PARTNER)
    far, normed_b = lax.optimization_barrier((far, normed[half_normed:]))
    far_normed_b = swap_col(normed_b, Y_PARTNER)
    other_near, other_far = swap_depth(near), swap_depth(far)
    sizes = (seqs, res, pair_cols, width)
    orders = (near_order, far_order)
    outer, proj_out, cnt, pm, maskt = pl.pallas_call(
        functools.partial(outer_kernel, sizes, orders),
        out_shape=(
            shape((half, outer_width), bf16),
            shape((half, pair_width), f32),
            shape((half, lanes), f32),
            shape((half, lanes), bf16),
            shape((residues, depths * seqs), f32),
        ),
        in_specs=[smem] + [vmem] * 5,
        out_specs=[vmem] * 5,
        scratch_shapes=[
            pltpu.VMEM((depths, cols, rows, pair_width), bf16),
            pltpu.VMEM((depths * seqs, residues * width), bf16),
            pltpu.VMEM((pair_cols * width, depths * seqs), bf16),
            pltpu.VMEM((pair_cols * width, depths * seqs), f32),
            pltpu.VMEM((half, lanes), bf16),
            pltpu.VMEM((half, lanes), bf16),
        ],
        compiler_params=params,
        name="outer_products",
    )(ids, near, far, other_near, other_far, wturn)
    other_near, other_far, proj_out = lax.optimization_barrier((other_near, other_far, proj_out))
    rightt, leftt = pl.pallas_call(
        functools.partial(turn_kernel, sizes, orders),
        out_shape=(
            shape((residues * width, depths * seqs), bf16),
            shape((residues * width, depths * seqs), bf16),
        ),
        in_specs=[smem] + [vmem] * 4,
        out_specs=[vmem] * 2,
        scratch_shapes=[
            pltpu.VMEM((depths, cols, 2 * seqs, pair_width), bf16),
            pltpu.VMEM((residues * width, depths * seqs), f32),
        ],
        compiler_params=params,
        name="turned",
    )(ids, near, far, other_near, other_far)
    pair_far, rightt, leftt, proj_out = lax.optimization_barrier(
        (pair_far, rightt, leftt, proj_out)
    )
    couple, opm, pn, gh, hidden, mg = pl.pallas_call(
        functools.partial(transition_kernel, sizes, orders),
        out_shape=(
            shape((per, pair_width), bf16),
            shape((half, pair_width), bf16),
            shape((half, pair_width), bf16),
            shape((half, hid), bf16),
            shape((half, hid), bf16),
            shape((half, pair_width), bf16),
        ),
        in_specs=[smem] + [vmem] * 8,
        out_specs=[vmem] * 6,
        scratch_shapes=[
            pltpu.VMEM((cols, 2 * per, pair_width), bf16),
            pltpu.VMEM((half, pair_width), f32),
        ],
        compiler_params=params,
        name="transition",
    )(
        ids,
        pair_near,
        pair_far,
        proj_out,
        cnt,
        pm,
        gain,
        hidden_weight,
        back_weight,
    )
    opm, far_normed_b = lax.optimization_barrier((opm, far_normed_b))
    far_normed = jnp.concatenate([far_normed_a, far_normed_b])
    weights = pl.pallas_call(
        weights_kernel,
        out_shape=shape((outer_width + 2 * hid, pair_width), bf16),
        in_specs=[vmem] * 6,
        out_specs=vmem,
        scratch_shapes=[pltpu.VMEM((outer_width, pair_width), f32)],
        compiler_params=params,
        name="weight_gradients",
    )(outer, opm, pn, gh, hidden, mg)
    other_opm, other_normed, other_far_normed, weights = lax.optimization_barrier(
        (swap_depth(opm), swap_depth(normed), swap_depth(far_normed), weights)
    )
    part, spread = pl.pallas_call(
        functools.partial(projector_kernel, sizes),
        out_shape=(
            shape((2 * width, channels), bf16),
            shape((seqs * res, 2 * lanes), bf16),
        ),
        in_specs=[smem] + [vmem] * 11,
        out_specs=[vmem] * 2,
        scratch_shapes=[
            pltpu.VMEM((depths, half, pair_width), f32),
            pltpu.VMEM((2 * res * residues, pair_width), bf16),
            pltpu.VMEM((2 * res * residues, pair_width), bf16),
            pltpu.VMEM((residues * width, 2 * lanes), bf16),
            pltpu.VMEM((residues * width, 2 * lanes), bf16),
            pltpu.VMEM((2, 2, depths, seqs * res, lanes), f32),
            pltpu.VMEM((2, depths, seqs * res, channels), bf16),
        ],
        compiler_params=params,
        name="projector_parts",
    )(
        ids,
        opm,
        other_opm,
        rightt,
        leftt,
        output_weight,
        wturn,
        maskt,
        normed,
        far_normed,
        other_normed,
        other_far_normed,
    )
    feat = pl.pallas_call(
        functools.partial(feature_kernel, res),
        out_shape=shape((seqs * res, channels), bf16),
        in_specs=[vmem] * 6,
        out_specs=vmem,
        compiler_params=params,
        name="features",
    )(spread, first, second, scale, scaled, inv)
    part, weights = lax.optimization_barrier((part, weights))
    dout, dhid, dback = pl.pallas_call(
        weights_sum_kernel,
        out_shape=(
            shape((outer_width, pair_width), f32),
            shape((pair_width, hid), f32),
            shape((hid, pair_width), f32),
        ),
        in_specs=[vmem] * 2,
        out_specs=[vmem] * 3,
        compiler_params=params,
        name="sums_over_depth",
    )(weights, swap_depth(weights))
    came_a = swap_line(part, (Z_PARTNERS[0], Z_PARTNERS[2]))
    came_b = swap_line(part, (None, Z_PARTNERS[1]))
    feat = feat.reshape(seqs, res, channels)
    came_a, came_b, feat = lax.optimization_barrier((came_a, came_b, feat))
    kept = jnp.where(lax.axis_index("depth") == 0, part, came_b)
    kept = lax.optimization_barrier((kept.astype(f32) + came_a.astype(f32)).astype(bf16))
    came = swap_depth(kept)
    came, dout, dhid, dback = lax.optimization_barrier((came, dout, dhid, dback))
    total = kept.astype(f32) + came.astype(f32)
    return (
        feat,
        couple.reshape(res, pair_cols, pair_width),
        total[:width].T,
        total[width:].T,
        dout,
        dhid,
        dback,
    )


def on_device(alignment_activations, *others):
    cols = lax.axis_size("col")
    residues = alignment_activations.shape[1] * cols
    plan = whole_plan if cols == 8 and residues <= FEW_RESIDUES else split_plan
    return plan(alignment_activations, *others)


def solution(mesh):
    in_specs = (
        P(("group", "depth"), "col", None),
        P(("group", "depth"), "col"),
        P(("group", "col"), "depth", None),
        P(("group", "col"), "depth"),
        P(("group", "col"), "depth", None),
        P(),
        P(),
        P(),
        P(),
        P(),
        P(),
        P(),
    )
    out_specs = (
        P(("group", "depth"), "col", None),
        P(("group", "col"), "depth", None),
        P("group", None),
        P("group", None),
        P("group", None),
        P("group", None),
        P("group", None),
    )
    return jax.shard_map(
        on_device, mesh=mesh, in_specs=in_specs, out_specs=out_specs, check_vma=False
    )
```

```python
import functools

import jax
import jax.numpy as jnp
from jax import lax
from jax.experimental import pallas as pl
from jax.experimental.pallas import tpu as pltpu
from jax.sharding import PartitionSpec as P

epsilon = 1e-05
highest = lax.Precision.HIGHEST


def norm_pieces(entries_drawn):
    center = entries_drawn - jnp.mean(entries_drawn, axis=-1, keepdims=True)
    inv_std = lax.rsqrt(jnp.mean(center * center, axis=-1, keepdims=True) + epsilon)
    return (center * inv_std, inv_std)


def standardize_adjoint(grad_scaled, scaled, inv_std):
    mean_grad = jnp.mean(grad_scaled, axis=-1, keepdims=True)
    mean_cross = jnp.mean(grad_scaled * scaled, axis=-1, keepdims=True)
    return inv_std * (grad_scaled - mean_grad - scaled * mean_cross)


def silu_pieces(pre_act):
    sigma = jax.nn.sigmoid(pre_act)
    return (pre_act * sigma, sigma * (1.0 + pre_act * (1.0 - sigma)))


def split_plan(
    alignment_activations,
    alignment_mask,
    pair_activation_input,
    pair_update_mask,
    pair_output_gradient,
    layer_scale_factor,
    first_projector,
    second_projector,
    output_weight,
    pair_norm_gain,
    hidden_weight,
    back_weight,
):
    sequence_row_block, residue_row_block, channel_total = alignment_activations.shape
    proj_width = first_projector.shape[1]
    outer_width = proj_width * proj_width
    depth_count = lax.axis_size("depth")
    residues = residue_row_block * lax.axis_size("col")
    pair_cols = pair_activation_input.shape[1]
    pair_width = pair_activation_input.shape[2]
    col_block = min(64, pair_cols)
    block_count = pair_cols // col_block
    standardized_features, reciprocal_spread = norm_pieces(
        alignment_activations.astype(jnp.float32)
    )
    normalized_rows = (standardized_features * layer_scale_factor).astype(jnp.bfloat16)
    mask_floating = alignment_mask.astype(jnp.float32)
    left_proj = (
        jnp.dot(normalized_rows, first_projector, preferred_element_type=jnp.float32)
        * mask_floating[:, :, None]
    ).astype(jnp.bfloat16)
    right_proj = (
        jnp.dot(normalized_rows, second_projector, preferred_element_type=jnp.float32)
        * mask_floating[:, :, None]
    ).astype(jnp.bfloat16)
    right_flat = right_proj.reshape(sequence_row_block, residue_row_block * proj_width)
    mask_converted = alignment_mask.astype(jnp.bfloat16)
    seq_total = left_proj.shape[0]
    gathered, gathered_mask = (
        lax.all_gather(right_flat, "col", axis=1, tiled=True),
        lax.all_gather(mask_converted, "col", axis=1, tiled=True),
    )
    right_blocks = gathered.reshape(seq_total, depth_count, pair_cols, proj_width)
    mask_blocks = gathered_mask.reshape(seq_total, depth_count, pair_cols)
    block_depth = right_blocks.shape[1]
    out_wide = output_weight.astype(jnp.float32)

    def partial_outer(col_start):
        right_piece = lax.dynamic_slice_in_dim(right_blocks, col_start, col_block, 2)
        outer_part = jnp.einsum(
            "sic,sejd->iejcd", left_proj, right_piece, preferred_element_type=jnp.float32
        )
        return (
            outer_part.reshape(residue_row_block, block_depth, col_block, outer_width),
            right_piece,
        )

    def forward_step(step_index, loop_state):
        projected, pair_count = loop_state
        col_start = step_index * col_block
        outer_part, right_piece = partial_outer(col_start)
        mask_piece = lax.dynamic_slice_in_dim(mask_blocks, col_start, col_block, 2).astype(
            jnp.float32
        )
        count_part = jnp.einsum("si,sej->iej", mask_floating, mask_piece, precision=highest)
        outer_mine, count_mine = (
            lax.psum_scatter(
                outer_part.astype(jnp.bfloat16), "depth", scatter_dimension=1, tiled=True
            ).astype(jnp.float32),
            lax.psum_scatter(
                count_part.astype(jnp.bfloat16), "depth", scatter_dimension=1, tiled=True
            ).astype(jnp.float32),
        )
        proj_mine = jnp.dot(
            outer_mine.reshape(residue_row_block * col_block, outer_width),
            out_wide,
            precision=highest,
        )
        proj_mine = proj_mine.reshape(residue_row_block, col_block, pair_width)
        count_mine = count_mine.reshape(residue_row_block, col_block)
        projected = lax.dynamic_update_slice_in_dim(projected, proj_mine, col_start, 1)
        pair_count = lax.dynamic_update_slice_in_dim(pair_count, count_mine, col_start, 1)
        return (projected, pair_count)

    projected, pair_count = lax.fori_loop(
        0,
        block_count,
        forward_step,
        (
            jnp.zeros((residue_row_block, pair_cols, pair_width), jnp.float32),
            jnp.zeros((residue_row_block, pair_cols), jnp.float32),
        ),
    )
    count_column = pair_count.reshape(residue_row_block * pair_cols, 1)
    mid_act = (
        pair_activation_input.reshape(residue_row_block * pair_cols, pair_width).astype(jnp.float32)
        + projected.reshape(residue_row_block * pair_cols, pair_width) / count_column
    )
    pair_scaled, pair_inv = norm_pieces(mid_act)
    pair_normed = (pair_scaled * pair_norm_gain).astype(jnp.bfloat16)
    pre_act = jnp.dot(pair_normed, hidden_weight, preferred_element_type=jnp.float32)
    act_value, act_slope = silu_pieces(pre_act)
    hidden = act_value.astype(jnp.bfloat16)
    masked_grad = (
        pair_output_gradient * pair_update_mask.astype(jnp.bfloat16)[:, :, None]
    ).reshape(residue_row_block * pair_cols, pair_width)
    final_matrix_derivative = jnp.dot(hidden.T, masked_grad, preferred_element_type=jnp.float32)
    back_prod = jnp.dot(masked_grad, back_weight.T, preferred_element_type=jnp.float32)
    grad_hidden = (back_prod * act_slope).astype(jnp.bfloat16)
    middle_matrix_derivative = jnp.dot(
        pair_normed.T, grad_hidden, preferred_element_type=jnp.float32
    )
    grad_scaled = (
        jnp.dot(grad_hidden, hidden_weight.T, preferred_element_type=jnp.float32) * pair_norm_gain
    )
    grad_mid = pair_output_gradient.reshape(residue_row_block * pair_cols, pair_width).astype(
        jnp.float32
    ) + standardize_adjoint(grad_scaled, pair_scaled, pair_inv)
    couple_features_derivative = grad_mid.astype(jnp.bfloat16).reshape(
        residue_row_block, pair_cols, pair_width
    )
    grad_opm = (
        (grad_mid / count_column)
        .astype(jnp.bfloat16)
        .reshape(residue_row_block, pair_cols, pair_width)
    )
    full_opm = lax.all_gather(grad_opm, "depth", axis=1, tiled=True).reshape(
        residue_row_block, depth_count, pair_cols, pair_width
    )

    def backward_step(step_index, loop_state):
        grad_left_acc, grad_out, right_term = loop_state
        col_start = step_index * col_block
        outer_part, right_piece = partial_outer(col_start)
        opm_piece = lax.dynamic_slice_in_dim(full_opm, col_start, col_block, 2).reshape(
            residue_row_block * block_depth * col_block, pair_width
        )
        grad_out = grad_out + jnp.dot(
            outer_part.reshape(residue_row_block * block_depth * col_block, outer_width).T,
            opm_piece.astype(jnp.float32),
            precision=highest,
        )
        grad_outer = jnp.dot(opm_piece, output_weight.T, preferred_element_type=jnp.float32).astype(
            jnp.bfloat16
        )
        grad_outer = grad_outer.reshape(
            residue_row_block, block_depth, col_block, proj_width, proj_width
        )
        grad_left_acc = grad_left_acc + jnp.einsum(
            "iejcd,sejd->sic", grad_outer, right_piece, preferred_element_type=jnp.float32
        )
        piece_term = jnp.einsum(
            "iejcd,sic->ejsd", grad_outer, left_proj, preferred_element_type=jnp.float32
        )
        piece_term = piece_term.reshape(block_depth, col_block, seq_total * proj_width)
        right_term = lax.dynamic_update_slice_in_dim(right_term, piece_term, col_start, 1)
        return (grad_left_acc, grad_out, right_term)

    grad_left_acc, result_matrix_derivative, right_term = lax.fori_loop(
        0,
        block_count,
        backward_step,
        (
            jnp.zeros((seq_total, residue_row_block, proj_width), jnp.float32),
            jnp.zeros((outer_width, pair_width), jnp.float32),
            jnp.zeros((block_depth, pair_cols, seq_total * proj_width), jnp.float32),
        ),
    )
    grad_right_sum = lax.psum_scatter(
        right_term.reshape(residues, seq_total * proj_width), "col", scatter_dimension=0, tiled=True
    )
    grad_right_acc = jnp.transpose(
        grad_right_sum.reshape(residue_row_block, seq_total, proj_width), (1, 0, 2)
    )
    grad_left = (grad_left_acc * mask_floating[:, :, None]).astype(jnp.bfloat16)
    grad_right = (grad_right_acc * mask_floating[:, :, None]).astype(jnp.bfloat16)
    normed_rows = normalized_rows.reshape(sequence_row_block * residue_row_block, channel_total)
    first_projector_derivative = jnp.dot(
        normed_rows.T,
        grad_left.reshape(sequence_row_block * residue_row_block, proj_width),
        preferred_element_type=jnp.float32,
    )
    second_projector_derivative = jnp.dot(
        normed_rows.T,
        grad_right.reshape(sequence_row_block * residue_row_block, proj_width),
        preferred_element_type=jnp.float32,
    )
    standardized_derivative = jnp.dot(
        grad_left, first_projector.T, preferred_element_type=jnp.float32
    ) + jnp.dot(grad_right, second_projector.T, preferred_element_type=jnp.float32)
    features_derivative = standardize_adjoint(
        standardized_derivative * layer_scale_factor, standardized_features, reciprocal_spread
    ).astype(jnp.bfloat16)
    weight_sums = lax.psum(
        (
            first_projector_derivative,
            second_projector_derivative,
            result_matrix_derivative,
            middle_matrix_derivative,
            final_matrix_derivative,
        ),
        ("depth", "col"),
    )
    return (
        features_derivative,
        couple_features_derivative,
        weight_sums[0],
        weight_sums[1],
        weight_sums[2],
        weight_sums[3],
        weight_sums[4],
    )


FEW_RESIDUES = 32
MASK_ROWS = 16
Z_PARTNERS = (6, 4, 2)
Y_PARTNER = 1


def butterfly(blocks, group):
    lane_group = lax.broadcasted_iota(jnp.int32, blocks[0].shape, 1) // group
    width = 4 * group
    for bit in (2, 1):
        low = (lane_group & bit) == 0
        swapped = list(blocks)
        for at in range(4):
            if at & bit:
                continue
            here, there = blocks[at], blocks[at | bit]
            moving = jnp.where(low, there, here)
            if bit == 2:
                moved = pltpu.roll(moving, 2 * group, 1)
            else:
                moved = jnp.where(
                    low, pltpu.roll(moving, width - group, 1), pltpu.roll(moving, group, 1)
                )
            swapped[at] = jnp.where(low, here, moved)
            swapped[at | bit] = jnp.where(low, moved, there)
        blocks = swapped
    return blocks


def wide_projector(first_ref, second_ref, copies):
    return jnp.concatenate([first_ref[...]] * copies + [second_ref[...]] * copies, axis=0)


def pre_kernel(
    ids_ref,
    x_hbm,
    maskt_hbm,
    pmask_hbm,
    scale_hbm,
    first_hbm,
    second_hbm,
    gain_hbm,
    act_hbm,
    grad_hbm,
    sent_ref,
    scale_ref,
    first_ref,
    second_ref,
    gain_ref,
    normed_ref,
    scaled_ref,
    inv_ref,
    wide_ref,
    tile_ref,
    x_ref,
    maskt_ref,
    pmask_ref,
    sems,
):
    res, seqs = maskt_ref.shape
    pairs = act_hbm.shape[0]
    first_pair = 2 * seqs + MASK_ROWS
    copies = [
        pltpu.make_async_copy(source, target, sems.at[at])
        for at, (source, target) in enumerate(
            (
                (x_hbm, x_ref),
                (maskt_hbm, maskt_ref),
                (pmask_hbm, pmask_ref),
                (scale_hbm, scale_ref),
                (first_hbm, first_ref),
                (second_hbm, second_ref),
                (gain_hbm, gain_ref),
                (act_hbm, sent_ref.at[0, pl.ds(first_pair, pairs), :]),
                (grad_hbm, sent_ref.at[0, pl.ds(first_pair + pairs, pairs), :]),
            )
        )
    ]
    for copy in copies:
        copy.start()
    for copy in copies[1:6]:
        copy.wait()
    lanes = sent_ref.shape[2]
    group = lanes // res
    tile_ref[...] = jnp.zeros(tile_ref.shape, jnp.float32)
    mask = maskt_ref[...].astype(jnp.float32)
    tile_ref[0:res, 0:seqs] = mask
    spread = (
        lax.broadcasted_iota(jnp.int32, (MASK_ROWS, lanes), 1) // group
        == lax.broadcasted_iota(jnp.int32, (MASK_ROWS, lanes), 0)
    ).astype(jnp.bfloat16)
    mask_lanes = lax.dot_general(
        tile_ref[...].astype(jnp.bfloat16),
        spread,
        (((0,), (0,)), ((), ())),
        preferred_element_type=jnp.float32,
    )[:seqs]
    twice = jnp.concatenate([mask] * (lanes // seqs), axis=1)
    here = lax.broadcasted_iota(jnp.int32, (res, lanes), 1) // seqs == ids_ref[0]
    tile_ref[0:res, :] = jnp.where(here, twice, 0.0)
    tile_ref[res : 2 * res, 0 : pmask_ref.shape[1]] = pmask_ref[...].astype(jnp.float32)
    sent_ref[0, 2 * seqs : first_pair, :] = tile_ref[...].astype(jnp.bfloat16)
    lane_group = lax.broadcasted_iota(jnp.int32, (seqs, lanes), 1) // group
    projector = wide_projector(first_ref, second_ref, res)
    copies[0].wait()
    scaled, inv = norm_pieces(
        x_ref[...].astype(jnp.float32).reshape(seqs * res, x_ref.shape[2])
    )
    normed = (scaled * scale_ref[...]).astype(jnp.bfloat16)
    wide = lax.dot_general(
        normed, projector, (((1,), (1,)), ((), ())), preferred_element_type=jnp.float32
    )
    for at in range(2):
        wide_ref[at] = wide[:, at * lanes : (at + 1) * lanes]
    scaled_ref[...] = scaled
    inv_ref[...] = inv
    normed_ref[...] = normed
    for at in range(2):
        both = wide_ref[at, pl.ds(0, seqs, stride=res), :]
        for r in range(1, res):
            both = jnp.where(
                lane_group == r, wide_ref[at, pl.ds(r, seqs, stride=res), :], both
            )
        sent_ref[0, at * seqs : (at + 1) * seqs, :] = (both * mask_lanes).astype(jnp.bfloat16)
    for copy in copies[6:]:
        copy.wait()


def outer_kernel(
    sizes,
    orders,
    ids_ref,
    near_ref,
    far_ref,
    other_near_ref,
    other_far_ref,
    wturn_ref,
    outer_ref,
    proj_out_ref,
    cnt_ref,
    pm_ref,
    maskt_ref,
    got_ref,
    leftn_ref,
    mine_ref,
    turn_ref,
    cntl_ref,
    pml_ref,
):
    seqs, res, pair_cols, width = sizes
    depths, cols = got_ref.shape[0], got_ref.shape[1]
    residues = cols * res
    lanes = res * width
    half_cols = pair_cols // res
    me_depth = ids_ref[0]
    me_col = ids_ref[1]
    f32, bf16 = jnp.float32, jnp.bfloat16

    for order, mine, other in zip(orders, (near_ref, far_ref), (other_near_ref, other_far_ref)):
        for at, partner in enumerate(order):
            got_ref[me_depth, me_col ^ partner] = mine[at]
            got_ref[1 - me_depth, me_col ^ partner] = other[at]

    for e in range(depths):
        for k in range(cols):
            leftn_ref[e * seqs : (e + 1) * seqs, k * lanes : (k + 1) * lanes] = got_ref[
                e, k, 0:seqs, :
            ]
    for k in range(half_cols):
        block = jnp.concatenate(
            [
                got_ref[e, me_depth * half_cols + k, seqs : 2 * seqs, :]
                for e in range(depths)
            ],
            axis=0,
        ).astype(f32)
        turn_ref[k * lanes : (k + 1) * lanes, :] = block.T
    for d in range(width):
        mine_ref[d * pair_cols : (d + 1) * pair_cols, :] = turn_ref[
            pl.ds(d, pair_cols, stride=width), :
        ].astype(bf16)

    base = 2 * seqs
    pair_lane = lax.broadcasted_iota(jnp.int32, (pair_cols, lanes), 1)
    pair_row = lax.broadcasted_iota(jnp.int32, (pair_cols, lanes), 0)
    for k in range(cols):
        tiles = [got_ref[e, k, base : base + MASK_ROWS, :].astype(f32) for e in range(depths)]
        maskt_ref[k * res : (k + 1) * res, :] = tiles[0][0:res] + tiles[1][0:res]
        own = got_ref[me_depth, k, base : base + MASK_ROWS, :].astype(f32)
        for r in range(res):
            row = own[res + r : res + r + 1, :]
            first = (k * res + r) * pair_cols
            pml_ref[first : first + pair_cols, :] = jnp.where(
                pair_lane == pair_row, row, 0.0
            ).astype(bf16)
    maskt = maskt_ref[...]
    cols_mask = maskt_ref[pl.ds(pl.multiple_of(me_depth * pair_cols, pair_cols), pair_cols), :]
    for i in range(residues):
        cntl_ref[i * pair_cols : (i + 1) * pair_cols, :] = (maskt[i : i + 1, :] * cols_mask).astype(
            bf16
        )
    ones = jnp.ones((lanes, lanes), bf16)
    cnt_ref[...] = jnp.dot(cntl_ref[...], ones, preferred_element_type=f32)
    pm_ref[...] = jnp.dot(pml_ref[...], ones, preferred_element_type=f32).astype(bf16)

    for dh in range(width // 4):
        prod = jnp.dot(
            mine_ref[dh * 4 * pair_cols : (dh + 1) * 4 * pair_cols, :],
            leftn_ref[...],
            preferred_element_type=f32,
        )
        for k in range(cols):
            piece = prod[:, k * lanes : (k + 1) * lanes]
            turned = butterfly(
                [piece[a * pair_cols : (a + 1) * pair_cols] for a in range(4)], width
            )
            for il in range(res):
                first = (k * res + il) * pair_cols
                outer_ref[first : first + pair_cols, dh * lanes : (dh + 1) * lanes] = turned[
                    il
                ].astype(bf16)
        if dh % 2:
            both = slice((dh - 1) * lanes, (dh + 1) * lanes)
            added = jnp.dot(outer_ref[:, both], wturn_ref[both, :], preferred_element_type=f32)
            if dh > 1:
                added = added + proj_out_ref[...]
            proj_out_ref[...] = added


def turn_kernel(
    sizes,
    orders,
    ids_ref,
    near_ref,
    far_ref,
    other_near_ref,
    other_far_ref,
    rightt_ref,
    leftt_ref,
    got_ref,
    turn_ref,
):
    seqs, res, _, width = sizes
    depths, cols = got_ref.shape[0], got_ref.shape[1]
    lanes = res * width
    residues = res * cols
    me_depth = ids_ref[0]
    me_col = ids_ref[1]
    for order, mine, other in zip(orders, (near_ref, far_ref), (other_near_ref, other_far_ref)):
        for at, partner in enumerate(order):
            got_ref[me_depth, me_col ^ partner] = mine[at, 0 : 2 * seqs, :]
            got_ref[1 - me_depth, me_col ^ partner] = other[at, 0 : 2 * seqs, :]
    for at, out in ((0, leftt_ref), (1, rightt_ref)):
        for k in range(cols):
            block = jnp.concatenate(
                [got_ref[e, k, at * seqs : (at + 1) * seqs, :] for e in range(depths)], axis=0
            ).astype(jnp.float32)
            turn_ref[k * lanes : (k + 1) * lanes, :] = block.T
        for d in range(width):
            out[d * residues : (d + 1) * residues, :] = turn_ref[
                pl.ds(d, residues, stride=width), :
            ].astype(jnp.bfloat16)


def transition_kernel(
    sizes,
    orders,
    ids_ref,
    near_ref,
    far_ref,
    proj_out_ref,
    cnt_ref,
    pm_ref,
    gain_ref,
    hid_ref,
    back_ref,
    couple_ref,
    opm_ref,
    pn_ref,
    gh_ref,
    hidden_ref,
    mg_ref,
    pgot_ref,
    gmid_ref,
):
    seqs, res, pair_cols, width = sizes
    per = res * pair_cols
    cols = pgot_ref.shape[0]
    me_col = ids_ref[1]
    f32, bf16 = jnp.float32, jnp.bfloat16
    for order, mine in zip(orders, (near_ref, far_ref)):
        for at, partner in enumerate(order):
            pgot_ref[me_col ^ partner] = mine[at]
    gain = gain_ref[...]
    chunk = 2 * per
    for at in range(cols // 2):
        rows = slice(at * chunk, (at + 1) * chunk)
        act, grad = [
            jnp.concatenate(
                [pgot_ref[2 * at + b, w * per : (w + 1) * per, :] for b in range(2)], axis=0
            )
            for w in range(2)
        ]
        count = cnt_ref[rows, :]
        mid = act.astype(f32) + proj_out_ref[rows, :] / count
        scaled, inv = norm_pieces(mid)
        normed = (scaled * gain).astype(bf16)
        pn_ref[rows, :] = normed
        pre = jnp.dot(normed, hid_ref[...], preferred_element_type=f32)
        value, slope = silu_pieces(pre)
        hidden_ref[rows, :] = value.astype(bf16)
        masked = grad * pm_ref[rows, :]
        mg_ref[rows, :] = masked
        back = lax.dot_general(
            masked, back_ref[...], (((1,), (1,)), ((), ())), preferred_element_type=f32
        )
        ghid = (back * slope).astype(bf16)
        gh_ref[rows, :] = ghid
        gsc = (
            lax.dot_general(
                ghid, hid_ref[...], (((1,), (1,)), ((), ())), preferred_element_type=f32
            )
            * gain
        )
        gmid = grad.astype(f32) + standardize_adjoint(gsc, scaled, inv)
        gmid_ref[rows, :] = gmid
        opm_ref[rows, :] = (gmid / count).astype(bf16)
    couple_ref[...] = gmid_ref[pl.ds(pl.multiple_of(me_col * per, per), per), :].astype(bf16)


def projector_kernel(
    sizes,
    ids_ref,
    opm_ref,
    other_opm_ref,
    rightt_ref,
    leftt_ref,
    wout_ref,
    wturn_ref,
    maskt_ref,
    normed_ref,
    far_normed_ref,
    other_normed_ref,
    other_far_normed_ref,
    part_ref,
    spread_ref,
    gf_ref,
    grow_ref,
    gcol_ref,
    gor_ref,
    goc_ref,
    gs_ref,
    rows_ref,
):
    seqs, res, pair_cols, width = sizes
    depths, half = gf_ref.shape[0], gf_ref.shape[1]
    residues = half // pair_cols
    lanes = res * width
    here = 2 * res
    me_depth = ids_ref[0]
    me_col = ids_ref[1]
    me_y = me_col % 2
    first_here = (me_col // 2) * here
    f32, bf16 = jnp.float32, jnp.bfloat16
    gf_ref[me_depth] = opm_ref[...].astype(f32)
    gf_ref[1 - me_depth] = other_opm_ref[...].astype(f32)
    for y, e, block in (
        (me_y, me_depth, normed_ref),
        (1 - me_y, me_depth, far_normed_ref),
        (me_y, 1 - me_depth, other_normed_ref),
        (1 - me_y, 1 - me_depth, other_far_normed_ref),
    ):
        rows_ref[y, e] = block[...]

    for il in range(here):
        for e in range(depths):
            first = pl.multiple_of((first_here + il) * pair_cols, pair_cols)
            grow_ref[il * residues + e * pair_cols : il * residues + (e + 1) * pair_cols, :] = (
                gf_ref[e, pl.ds(first, pair_cols), :].astype(bf16)
            )
    my_half = first_here // pair_cols
    my_first = first_here - my_half * pair_cols
    for jl in range(here):
        gcol_ref[jl * residues : (jl + 1) * residues, :] = gf_ref[
            my_half, pl.ds(my_first + jl, residues, stride=pair_cols), :
        ].astype(bf16)
    totals = [None, None]
    for dh in range(width // 4):
        for at, (lhs, weight, out, turned_ref) in enumerate(
            ((grow_ref, wturn_ref, gor_ref, rightt_ref), (gcol_ref, wout_ref, goc_ref, leftt_ref))
        ):
            piece = lax.dot_general(
                lhs[...],
                weight[dh * lanes : (dh + 1) * lanes, :],
                (((1,), (1,)), ((), ())),
                preferred_element_type=f32,
            )
            for y in range(2):
                turned = butterfly(
                    [
                        piece[(y * res + a) * residues : (y * res + a + 1) * residues]
                        for a in range(4)
                    ],
                    width,
                )
                for dl in range(4):
                    first = (dh * 4 + dl) * residues
                    out[first : first + residues, y * lanes : (y + 1) * lanes] = turned[dl].astype(
                        bf16
                    )
            if dh % 2:
                rows = slice((dh - 1) * 4 * residues, (dh + 1) * 4 * residues)
                added = lax.dot_general(
                    turned_ref[rows, :],
                    out[rows, :],
                    (((0,), (0,)), ((), ())),
                    preferred_element_type=f32,
                )
                totals[at] = added if totals[at] is None else totals[at] + added
    group = lax.broadcasted_iota(jnp.int32, (here, here * width), 1) // width
    spread = (group == lax.broadcasted_iota(jnp.int32, (here, here * width), 0)).astype(f32)
    mask_lanes = lax.dot_general(
        maskt_ref[pl.ds(pl.multiple_of(first_here, here), here), :],
        spread,
        (((0,), (0,)), ((), ())),
        preferred_element_type=f32,
    )
    lane_group = lax.broadcasted_iota(jnp.int32, (seqs, lanes), 1) // width
    for at, total in enumerate(totals):
        total = (total * mask_lanes).astype(bf16).astype(f32)
        for y in range(2):
            for e in range(depths):
                block = total[e * seqs : (e + 1) * seqs, y * lanes : (y + 1) * lanes]
                for r in range(res):
                    gs_ref[at, y, e, pl.ds(r, seqs, stride=res), :] = jnp.where(
                        lane_group == r, block, 0.0
                    )
    spread_ref[...] = jnp.concatenate(
        [gs_ref[0, me_y, me_depth], gs_ref[1, me_y, me_depth]], axis=1
    ).astype(bf16)
    rows = rows_ref.shape[2]
    for at in range(2):
        cross = lax.dot_general(
            gs_ref[at].reshape(2 * depths * rows, lanes).astype(bf16),
            rows_ref[...].reshape(2 * depths * rows, rows_ref.shape[3]),
            (((0,), (0,)), ((), ())),
            preferred_element_type=f32,
        )
        total = cross[:width]
        for r in range(1, res):
            total = total + cross[r * width : (r + 1) * width]
        part_ref[at * width : (at + 1) * width, :] = total.astype(bf16)


def weights_kernel(outer_ref, opm_ref, pn_ref, gh_ref, hidden_ref, mg_ref, out_ref, turn_ref):
    pair_width, hid = pn_ref.shape[1], gh_ref.shape[1]
    outer_width = outer_ref.shape[1]
    width = int(outer_width**0.5 + 0.5)

    def contract(lhs, rhs):
        return lax.dot_general(
            lhs[...], rhs[...], (((0,), (0,)), ((), ())), preferred_element_type=jnp.float32
        )

    turn_ref[...] = contract(outer_ref, opm_ref)
    for c in range(width):
        out_ref[c * width : (c + 1) * width, :] = turn_ref[
            pl.ds(c, width, stride=width), :
        ].astype(jnp.bfloat16)
    dhid = contract(pn_ref, gh_ref).astype(jnp.bfloat16)
    for at in range(hid // pair_width):
        first = outer_width + at * pair_width
        out_ref[first : first + pair_width, :] = dhid[:, at * pair_width : (at + 1) * pair_width]
    out_ref[outer_width + hid :, :] = contract(hidden_ref, mg_ref).astype(jnp.bfloat16)


def weights_sum_kernel(mine_ref, other_ref, dout_ref, dhid_ref, dback_ref):
    pair_width, hid = dhid_ref.shape
    outer_width = dout_ref.shape[0]

    def added(first, count):
        rows = slice(first, first + count)
        return mine_ref[rows, :].astype(jnp.float32) + other_ref[rows, :].astype(jnp.float32)

    dout_ref[...] = added(0, outer_width)
    for at in range(hid // pair_width):
        dhid_ref[:, at * pair_width : (at + 1) * pair_width] = added(
            outer_width + at * pair_width, pair_width
        )
    dback_ref[...] = added(outer_width + hid, hid)


def feature_kernel(
    copies, spread_ref, first_ref, second_ref, scale_ref, scaled_ref, inv_ref, feat_ref
):
    back = jnp.dot(
        spread_ref[...],
        wide_projector(first_ref, second_ref, copies),
        preferred_element_type=jnp.float32,
    )
    feat_ref[...] = standardize_adjoint(
        back * scale_ref[...], scaled_ref[...], inv_ref[...]
    ).astype(jnp.bfloat16)


def swap_line(block, partners):
    count = lax.axis_size("col")
    pairs = [
        (depth * count + at, depth * count + (at ^ partner))
        for depth, partner in enumerate(partners)
        if partner is not None
        for at in range(count)
    ]
    return lax.ppermute(block, ("depth", "col"), pairs)


def swap_depth(block):
    return lax.ppermute(block, "depth", [(0, 1), (1, 0)])


def pairwise_sum(blocks):
    while len(blocks) > 1:
        blocks = [blocks[at] + blocks[at + 1] for at in range(0, len(blocks), 2)]
    return blocks[0]


def swap_col(block, partner):
    count = lax.axis_size("col")
    return lax.ppermute(block, "col", [(at, at ^ partner) for at in range(count)])


def whole_plan(
    alignment_activations,
    alignment_mask,
    pair_activation_input,
    pair_update_mask,
    pair_output_gradient,
    layer_scale_factor,
    first_projector,
    second_projector,
    output_weight,
    pair_norm_gain,
    hidden_weight,
    back_weight,
):
    seqs, res, channels = alignment_activations.shape
    width = first_projector.shape[1]
    outer_width = width * width
    cols = lax.axis_size("col")
    depths = lax.axis_size("depth")
    residues = res * cols
    pair_cols, pair_width = pair_activation_input.shape[1:]
    hid = hidden_weight.shape[1]
    per = res * pair_cols
    lanes = res * width
    rows = 2 * seqs + MASK_ROWS
    half = residues * pair_cols
    f32, bf16 = jnp.float32, jnp.bfloat16
    ids = jnp.stack([lax.axis_index("depth"), lax.axis_index("col")]).astype(jnp.int32)
    smem = pl.BlockSpec(memory_space=pltpu.SMEM)
    vmem = pl.BlockSpec(memory_space=pltpu.VMEM)
    params = pltpu.CompilerParams(vmem_limit_bytes=16 * 2**20)
    scale = layer_scale_factor.reshape(1, channels)
    first, second = first_projector.T, second_projector.T
    wturn = jnp.transpose(output_weight.reshape(width, width, pair_width), (1, 0, 2)).reshape(
        outer_width, pair_width
    )
    shape = jax.ShapeDtypeStruct
    sent, scale, first, second, gain, normed, scaled, inv = pl.pallas_call(
        pre_kernel,
        out_shape=(
            shape((1, rows + 2 * per, pair_width), bf16),
            shape((1, channels), f32),
            shape((width, channels), bf16),
            shape((width, channels), bf16),
            shape((1, pair_width), f32),
            shape((seqs * res, channels), bf16),
            shape((seqs * res, channels), f32),
            shape((seqs * res, 1), f32),
        ),
        in_specs=[smem] + [pl.BlockSpec(memory_space=pltpu.HBM)] * 9,
        out_specs=[vmem] * 8,
        scratch_shapes=[
            pltpu.VMEM((2, seqs * res, lanes), f32),
            pltpu.VMEM((MASK_ROWS, lanes), f32),
            pltpu.VMEM((seqs, res, channels), bf16),
            pltpu.VMEM((res, seqs), jnp.int32),
            pltpu.VMEM((res, pair_cols), jnp.int32),
            pltpu.SemaphoreType.DMA((9,)),
        ],
        compiler_params=params,
        name="project",
    )(
        ids,
        *[
            pltpu.with_memory_space_constraint(array, pltpu.HBM)
            for array in (
                alignment_activations,
                alignment_mask.T,
                pair_update_mask,
                scale,
                first,
                second,
                pair_norm_gain.reshape(1, pair_width),
                pair_activation_input.reshape(per, pair_width),
                pair_output_gradient.reshape(per, pair_width),
            )
        ],
    )
    near_order = (0,) + Z_PARTNERS
    far_order = tuple(at ^ Y_PARTNER for at in near_order)
    blocks = lax.optimization_barrier(
        jnp.concatenate([sent] + [swap_col(sent, partner) for partner in Z_PARTNERS])
    )
    half_normed = seqs * res // 2
    far_normed_a = swap_col(normed[:half_normed], Y_PARTNER)
    blocks, far_normed_a = lax.optimization_barrier((blocks, far_normed_a))
    near, pair_near = blocks[:, :rows], blocks[:, rows:]
    far = swap_col(near, Y_PARTNER)
    pair_far = swap_col(pair_near, Y_PARTNER)
    far, normed_b = lax.optimization_barrier((far, normed[half_normed:]))
    far_normed_b = swap_col(normed_b, Y_PARTNER)
    other_near, other_far = swap_depth(near), swap_depth(far)
    sizes = (seqs, res, pair_cols, width)
    orders = (near_order, far_order)
    outer, proj_out, cnt, pm, maskt = pl.pallas_call(
        functools.partial(outer_kernel, sizes, orders),
        out_shape=(
            shape((half, outer_width), bf16),
            shape((half, pair_width), f32),
            shape((half, lanes), f32),
            shape((half, lanes), bf16),
            shape((residues, depths * seqs), f32),
        ),
        in_specs=[smem] + [vmem] * 5,
        out_specs=[vmem] * 5,
        scratch_shapes=[
            pltpu.VMEM((depths, cols, rows, pair_width), bf16),
            pltpu.VMEM((depths * seqs, residues * width), bf16),
            pltpu.VMEM((pair_cols * width, depths * seqs), bf16),
            pltpu.VMEM((pair_cols * width, depths * seqs), f32),
            pltpu.VMEM((half, lanes), bf16),
            pltpu.VMEM((half, lanes), bf16),
        ],
        compiler_params=params,
        name="outer_products",
    )(ids, near, far, other_near, other_far, wturn)
    other_near, other_far, proj_out = lax.optimization_barrier((other_near, other_far, proj_out))
    rightt, leftt = pl.pallas_call(
        functools.partial(turn_kernel, sizes, orders),
        out_shape=(
            shape((residues * width, depths * seqs), bf16),
            shape((residues * width, depths * seqs), bf16),
        ),
        in_specs=[smem] + [vmem] * 4,
        out_specs=[vmem] * 2,
        scratch_shapes=[
            pltpu.VMEM((depths, cols, 2 * seqs, pair_width), bf16),
            pltpu.VMEM((residues * width, depths * seqs), f32),
        ],
        compiler_params=params,
        name="turned",
    )(ids, near, far, other_near, other_far)
    pair_far, rightt, leftt, proj_out = lax.optimization_barrier(
        (pair_far, rightt, leftt, proj_out)
    )
    couple, opm, pn, gh, hidden, mg = pl.pallas_call(
        functools.partial(transition_kernel, sizes, orders),
        out_shape=(
            shape((per, pair_width), bf16),
            shape((half, pair_width), bf16),
            shape((half, pair_width), bf16),
            shape((half, hid), bf16),
            shape((half, hid), bf16),
            shape((half, pair_width), bf16),
        ),
        in_specs=[smem] + [vmem] * 8,
        out_specs=[vmem] * 6,
        scratch_shapes=[
            pltpu.VMEM((cols, 2 * per, pair_width), bf16),
            pltpu.VMEM((half, pair_width), f32),
        ],
        compiler_params=params,
        name="transition",
    )(
        ids,
        pair_near,
        pair_far,
        proj_out,
        cnt,
        pm,
        gain,
        hidden_weight,
        back_weight,
    )
    opm, far_normed_b = lax.optimization_barrier((opm, far_normed_b))
    far_normed = jnp.concatenate([far_normed_a, far_normed_b])
    weights = pl.pallas_call(
        weights_kernel,
        out_shape=shape((outer_width + 2 * hid, pair_width), bf16),
        in_specs=[vmem] * 6,
        out_specs=vmem,
        scratch_shapes=[pltpu.VMEM((outer_width, pair_width), f32)],
        compiler_params=params,
        name="weight_gradients",
    )(outer, opm, pn, gh, hidden, mg)
    other_opm, other_normed, other_far_normed, weights = lax.optimization_barrier(
        (swap_depth(opm), swap_depth(normed), swap_depth(far_normed), weights)
    )
    part, spread = pl.pallas_call(
        functools.partial(projector_kernel, sizes),
        out_shape=(
            shape((2 * width, channels), bf16),
            shape((seqs * res, 2 * lanes), bf16),
        ),
        in_specs=[smem] + [vmem] * 11,
        out_specs=[vmem] * 2,
        scratch_shapes=[
            pltpu.VMEM((depths, half, pair_width), f32),
            pltpu.VMEM((2 * res * residues, pair_width), bf16),
            pltpu.VMEM((2 * res * residues, pair_width), bf16),
            pltpu.VMEM((residues * width, 2 * lanes), bf16),
            pltpu.VMEM((residues * width, 2 * lanes), bf16),
            pltpu.VMEM((2, 2, depths, seqs * res, lanes), f32),
            pltpu.VMEM((2, depths, seqs * res, channels), bf16),
        ],
        compiler_params=params,
        name="projector_parts",
    )(
        ids,
        opm,
        other_opm,
        rightt,
        leftt,
        output_weight,
        wturn,
        maskt,
        normed,
        far_normed,
        other_normed,
        other_far_normed,
    )
    feat = pl.pallas_call(
        functools.partial(feature_kernel, res),
        out_shape=shape((seqs * res, channels), bf16),
        in_specs=[vmem] * 6,
        out_specs=vmem,
        compiler_params=params,
        name="features",
    )(spread, first, second, scale, scaled, inv)
    part, weights = lax.optimization_barrier((part, weights))
    dout, dhid, dback = pl.pallas_call(
        weights_sum_kernel,
        out_shape=(
            shape((outer_width, pair_width), f32),
            shape((pair_width, hid), f32),
            shape((hid, pair_width), f32),
        ),
        in_specs=[vmem] * 2,
        out_specs=[vmem] * 3,
        compiler_params=params,
        name="sums_over_depth",
    )(weights, swap_depth(weights))
    came_a = swap_line(part, Z_PARTNERS[:2])
    came_b = swap_line(part, (None, Z_PARTNERS[2]))
    feat = feat.reshape(seqs, res, channels)
    came_a, came_b, feat = lax.optimization_barrier((came_a, came_b, feat))
    kept = jnp.where(lax.axis_index("depth") == 0, part, came_b)
    kept = lax.optimization_barrier((kept.astype(f32) + came_a.astype(f32)).astype(bf16))
    came = swap_depth(kept)
    came, dout, dhid, dback = lax.optimization_barrier((came, dout, dhid, dback))
    total = kept.astype(f32) + came.astype(f32)
    return (
        feat,
        couple.reshape(res, pair_cols, pair_width),
        total[:width].T,
        total[width:].T,
        dout,
        dhid,
        dback,
    )


def on_device(alignment_activations, *others):
    cols = lax.axis_size("col")
    residues = alignment_activations.shape[1] * cols
    plan = whole_plan if cols == 8 and residues <= FEW_RESIDUES else split_plan
    return plan(alignment_activations, *others)


def solution(mesh):
    in_specs = (
        P(("group", "depth"), "col", None),
        P(("group", "depth"), "col"),
        P(("group", "col"), "depth", None),
        P(("group", "col"), "depth"),
        P(("group", "col"), "depth", None),
        P(),
        P(),
        P(),
        P(),
        P(),
        P(),
        P(),
    )
    out_specs = (
        P(("group", "depth"), "col", None),
        P(("group", "col"), "depth", None),
        P("group", None),
        P("group", None),
        P("group", None),
        P("group", None),
        P("group", None),
    )
    return jax.shard_map(
        on_device, mesh=mesh, in_specs=in_specs, out_specs=out_specs, check_vma=False
    )
```

```python
import functools

import jax
import jax.numpy as jnp
from jax import lax
from jax.experimental import pallas as pl
from jax.experimental.pallas import tpu as pltpu
from jax.sharding import PartitionSpec as P

epsilon = 1e-05
highest = lax.Precision.HIGHEST


def norm_pieces(entries_drawn):
    center = entries_drawn - jnp.mean(entries_drawn, axis=-1, keepdims=True)
    inv_std = lax.rsqrt(jnp.mean(center * center, axis=-1, keepdims=True) + epsilon)
    return (center * inv_std, inv_std)


def standardize_adjoint(grad_scaled, scaled, inv_std):
    mean_grad = jnp.mean(grad_scaled, axis=-1, keepdims=True)
    mean_cross = jnp.mean(grad_scaled * scaled, axis=-1, keepdims=True)
    return inv_std * (grad_scaled - mean_grad - scaled * mean_cross)


def silu_pieces(pre_act):
    sigma = jax.nn.sigmoid(pre_act)
    return (pre_act * sigma, sigma * (1.0 + pre_act * (1.0 - sigma)))


def split_plan(
    alignment_activations,
    alignment_mask,
    pair_activation_input,
    pair_update_mask,
    pair_output_gradient,
    layer_scale_factor,
    first_projector,
    second_projector,
    output_weight,
    pair_norm_gain,
    hidden_weight,
    back_weight,
):
    sequence_row_block, residue_row_block, channel_total = alignment_activations.shape
    proj_width = first_projector.shape[1]
    outer_width = proj_width * proj_width
    depth_count = lax.axis_size("depth")
    residues = residue_row_block * lax.axis_size("col")
    pair_cols = pair_activation_input.shape[1]
    pair_width = pair_activation_input.shape[2]
    col_block = min(64, pair_cols)
    block_count = pair_cols // col_block
    standardized_features, reciprocal_spread = norm_pieces(
        alignment_activations.astype(jnp.float32)
    )
    normalized_rows = (standardized_features * layer_scale_factor).astype(jnp.bfloat16)
    mask_floating = alignment_mask.astype(jnp.float32)
    left_proj = (
        jnp.dot(normalized_rows, first_projector, preferred_element_type=jnp.float32)
        * mask_floating[:, :, None]
    ).astype(jnp.bfloat16)
    right_proj = (
        jnp.dot(normalized_rows, second_projector, preferred_element_type=jnp.float32)
        * mask_floating[:, :, None]
    ).astype(jnp.bfloat16)
    right_flat = right_proj.reshape(sequence_row_block, residue_row_block * proj_width)
    mask_converted = alignment_mask.astype(jnp.bfloat16)
    seq_total = left_proj.shape[0]
    gathered, gathered_mask = (
        lax.all_gather(right_flat, "col", axis=1, tiled=True),
        lax.all_gather(mask_converted, "col", axis=1, tiled=True),
    )
    right_blocks = gathered.reshape(seq_total, depth_count, pair_cols, proj_width)
    mask_blocks = gathered_mask.reshape(seq_total, depth_count, pair_cols)
    block_depth = right_blocks.shape[1]
    out_wide = output_weight.astype(jnp.float32)

    def partial_outer(col_start):
        right_piece = lax.dynamic_slice_in_dim(right_blocks, col_start, col_block, 2)
        outer_part = jnp.einsum(
            "sic,sejd->iejcd", left_proj, right_piece, preferred_element_type=jnp.float32
        )
        return (
            outer_part.reshape(residue_row_block, block_depth, col_block, outer_width),
            right_piece,
        )

    def forward_step(step_index, loop_state):
        projected, pair_count = loop_state
        col_start = step_index * col_block
        outer_part, right_piece = partial_outer(col_start)
        mask_piece = lax.dynamic_slice_in_dim(mask_blocks, col_start, col_block, 2).astype(
            jnp.float32
        )
        count_part = jnp.einsum("si,sej->iej", mask_floating, mask_piece, precision=highest)
        outer_mine, count_mine = (
            lax.psum_scatter(
                outer_part.astype(jnp.bfloat16), "depth", scatter_dimension=1, tiled=True
            ).astype(jnp.float32),
            lax.psum_scatter(
                count_part.astype(jnp.bfloat16), "depth", scatter_dimension=1, tiled=True
            ).astype(jnp.float32),
        )
        proj_mine = jnp.dot(
            outer_mine.reshape(residue_row_block * col_block, outer_width),
            out_wide,
            precision=highest,
        )
        proj_mine = proj_mine.reshape(residue_row_block, col_block, pair_width)
        count_mine = count_mine.reshape(residue_row_block, col_block)
        projected = lax.dynamic_update_slice_in_dim(projected, proj_mine, col_start, 1)
        pair_count = lax.dynamic_update_slice_in_dim(pair_count, count_mine, col_start, 1)
        return (projected, pair_count)

    projected, pair_count = lax.fori_loop(
        0,
        block_count,
        forward_step,
        (
            jnp.zeros((residue_row_block, pair_cols, pair_width), jnp.float32),
            jnp.zeros((residue_row_block, pair_cols), jnp.float32),
        ),
    )
    count_column = pair_count.reshape(residue_row_block * pair_cols, 1)
    mid_act = (
        pair_activation_input.reshape(residue_row_block * pair_cols, pair_width).astype(jnp.float32)
        + projected.reshape(residue_row_block * pair_cols, pair_width) / count_column
    )
    pair_scaled, pair_inv = norm_pieces(mid_act)
    pair_normed = (pair_scaled * pair_norm_gain).astype(jnp.bfloat16)
    pre_act = jnp.dot(pair_normed, hidden_weight, preferred_element_type=jnp.float32)
    act_value, act_slope = silu_pieces(pre_act)
    hidden = act_value.astype(jnp.bfloat16)
    masked_grad = (
        pair_output_gradient * pair_update_mask.astype(jnp.bfloat16)[:, :, None]
    ).reshape(residue_row_block * pair_cols, pair_width)
    final_matrix_derivative = jnp.dot(hidden.T, masked_grad, preferred_element_type=jnp.float32)
    back_prod = jnp.dot(masked_grad, back_weight.T, preferred_element_type=jnp.float32)
    grad_hidden = (back_prod * act_slope).astype(jnp.bfloat16)
    middle_matrix_derivative = jnp.dot(
        pair_normed.T, grad_hidden, preferred_element_type=jnp.float32
    )
    grad_scaled = (
        jnp.dot(grad_hidden, hidden_weight.T, preferred_element_type=jnp.float32) * pair_norm_gain
    )
    grad_mid = pair_output_gradient.reshape(residue_row_block * pair_cols, pair_width).astype(
        jnp.float32
    ) + standardize_adjoint(grad_scaled, pair_scaled, pair_inv)
    couple_features_derivative = grad_mid.astype(jnp.bfloat16).reshape(
        residue_row_block, pair_cols, pair_width
    )
    grad_opm = (
        (grad_mid / count_column)
        .astype(jnp.bfloat16)
        .reshape(residue_row_block, pair_cols, pair_width)
    )
    full_opm = lax.all_gather(grad_opm, "depth", axis=1, tiled=True).reshape(
        residue_row_block, depth_count, pair_cols, pair_width
    )

    def backward_step(step_index, loop_state):
        grad_left_acc, grad_out, right_term = loop_state
        col_start = step_index * col_block
        outer_part, right_piece = partial_outer(col_start)
        opm_piece = lax.dynamic_slice_in_dim(full_opm, col_start, col_block, 2).reshape(
            residue_row_block * block_depth * col_block, pair_width
        )
        grad_out = grad_out + jnp.dot(
            outer_part.reshape(residue_row_block * block_depth * col_block, outer_width).T,
            opm_piece.astype(jnp.float32),
            precision=highest,
        )
        grad_outer = jnp.dot(opm_piece, output_weight.T, preferred_element_type=jnp.float32).astype(
            jnp.bfloat16
        )
        grad_outer = grad_outer.reshape(
            residue_row_block, block_depth, col_block, proj_width, proj_width
        )
        grad_left_acc = grad_left_acc + jnp.einsum(
            "iejcd,sejd->sic", grad_outer, right_piece, preferred_element_type=jnp.float32
        )
        piece_term = jnp.einsum(
            "iejcd,sic->ejsd", grad_outer, left_proj, preferred_element_type=jnp.float32
        )
        piece_term = piece_term.reshape(block_depth, col_block, seq_total * proj_width)
        right_term = lax.dynamic_update_slice_in_dim(right_term, piece_term, col_start, 1)
        return (grad_left_acc, grad_out, right_term)

    grad_left_acc, result_matrix_derivative, right_term = lax.fori_loop(
        0,
        block_count,
        backward_step,
        (
            jnp.zeros((seq_total, residue_row_block, proj_width), jnp.float32),
            jnp.zeros((outer_width, pair_width), jnp.float32),
            jnp.zeros((block_depth, pair_cols, seq_total * proj_width), jnp.float32),
        ),
    )
    grad_right_sum = lax.psum_scatter(
        right_term.reshape(residues, seq_total * proj_width), "col", scatter_dimension=0, tiled=True
    )
    grad_right_acc = jnp.transpose(
        grad_right_sum.reshape(residue_row_block, seq_total, proj_width), (1, 0, 2)
    )
    grad_left = (grad_left_acc * mask_floating[:, :, None]).astype(jnp.bfloat16)
    grad_right = (grad_right_acc * mask_floating[:, :, None]).astype(jnp.bfloat16)
    normed_rows = normalized_rows.reshape(sequence_row_block * residue_row_block, channel_total)
    first_projector_derivative = jnp.dot(
        normed_rows.T,
        grad_left.reshape(sequence_row_block * residue_row_block, proj_width),
        preferred_element_type=jnp.float32,
    )
    second_projector_derivative = jnp.dot(
        normed_rows.T,
        grad_right.reshape(sequence_row_block * residue_row_block, proj_width),
        preferred_element_type=jnp.float32,
    )
    standardized_derivative = jnp.dot(
        grad_left, first_projector.T, preferred_element_type=jnp.float32
    ) + jnp.dot(grad_right, second_projector.T, preferred_element_type=jnp.float32)
    features_derivative = standardize_adjoint(
        standardized_derivative * layer_scale_factor, standardized_features, reciprocal_spread
    ).astype(jnp.bfloat16)
    weight_sums = lax.psum(
        (
            first_projector_derivative,
            second_projector_derivative,
            result_matrix_derivative,
            middle_matrix_derivative,
            final_matrix_derivative,
        ),
        ("depth", "col"),
    )
    return (
        features_derivative,
        couple_features_derivative,
        weight_sums[0],
        weight_sums[1],
        weight_sums[2],
        weight_sums[3],
        weight_sums[4],
    )


FEW_RESIDUES = 32
MASK_ROWS = 16
Z_PARTNERS = (6, 4, 2)
Y_PARTNER = 1


def butterfly(blocks, group):
    lane_group = lax.broadcasted_iota(jnp.int32, blocks[0].shape, 1) // group
    width = 4 * group
    for bit in (2, 1):
        low = (lane_group & bit) == 0
        swapped = list(blocks)
        for at in range(4):
            if at & bit:
                continue
            here, there = blocks[at], blocks[at | bit]
            moving = jnp.where(low, there, here)
            if bit == 2:
                moved = pltpu.roll(moving, 2 * group, 1)
            else:
                moved = jnp.where(
                    low, pltpu.roll(moving, width - group, 1), pltpu.roll(moving, group, 1)
                )
            swapped[at] = jnp.where(low, here, moved)
            swapped[at | bit] = jnp.where(low, moved, there)
        blocks = swapped
    return blocks


def wide_projector(first_ref, second_ref, copies):
    return jnp.concatenate([first_ref[...]] * copies + [second_ref[...]] * copies, axis=0)


def pre_kernel(
    ids_ref,
    x_hbm,
    maskt_hbm,
    pmask_hbm,
    scale_hbm,
    first_hbm,
    second_hbm,
    gain_hbm,
    act_hbm,
    grad_hbm,
    sent_ref,
    scale_ref,
    first_ref,
    second_ref,
    gain_ref,
    normed_ref,
    scaled_ref,
    inv_ref,
    wide_ref,
    tile_ref,
    x_ref,
    maskt_ref,
    pmask_ref,
    sems,
):
    res, seqs = maskt_ref.shape
    pairs = act_hbm.shape[0]
    first_pair = 2 * seqs + MASK_ROWS
    copies = [
        pltpu.make_async_copy(source, target, sems.at[at])
        for at, (source, target) in enumerate(
            (
                (x_hbm, x_ref),
                (maskt_hbm, maskt_ref),
                (pmask_hbm, pmask_ref),
                (scale_hbm, scale_ref),
                (first_hbm, first_ref),
                (second_hbm, second_ref),
                (gain_hbm, gain_ref),
                (act_hbm, sent_ref.at[0, pl.ds(first_pair, pairs), :]),
                (grad_hbm, sent_ref.at[0, pl.ds(first_pair + pairs, pairs), :]),
            )
        )
    ]
    for copy in copies:
        copy.start()
    for copy in copies:
        copy.wait()
    lanes = sent_ref.shape[2]
    group = lanes // res
    scaled, inv = norm_pieces(
        x_ref[...].astype(jnp.float32).reshape(seqs * res, x_ref.shape[2])
    )
    scaled_ref[...] = scaled
    inv_ref[...] = inv
    normed = (scaled * scale_ref[...]).astype(jnp.bfloat16)
    normed_ref[...] = normed
    wide = lax.dot_general(
        normed,
        wide_projector(first_ref, second_ref, res),
        (((1,), (1,)), ((), ())),
        preferred_element_type=jnp.float32,
    )
    for at in range(2):
        wide_ref[at] = wide[:, at * lanes : (at + 1) * lanes]
    tile_ref[...] = jnp.zeros(tile_ref.shape, jnp.float32)
    mask = maskt_ref[...].astype(jnp.float32)
    tile_ref[0:res, 0:seqs] = mask
    spread = (
        lax.broadcasted_iota(jnp.int32, (MASK_ROWS, lanes), 1) // group
        == lax.broadcasted_iota(jnp.int32, (MASK_ROWS, lanes), 0)
    ).astype(jnp.float32)
    mask_lanes = lax.dot_general(
        tile_ref[...], spread, (((0,), (0,)), ((), ())), preferred_element_type=jnp.float32
    )[:seqs]
    twice = jnp.concatenate([mask] * (lanes // seqs), axis=1)
    here = lax.broadcasted_iota(jnp.int32, (res, lanes), 1) // seqs == ids_ref[0]
    tile_ref[0:res, :] = jnp.where(here, twice, 0.0)
    tile_ref[res : 2 * res, 0 : pmask_ref.shape[1]] = pmask_ref[...].astype(jnp.float32)
    lane_group = lax.broadcasted_iota(jnp.int32, (seqs, lanes), 1) // group
    for at in range(2):
        both = wide_ref[at, pl.ds(0, seqs, stride=res), :]
        for r in range(1, res):
            both = jnp.where(
                lane_group == r, wide_ref[at, pl.ds(r, seqs, stride=res), :], both
            )
        sent_ref[0, at * seqs : (at + 1) * seqs, :] = (both * mask_lanes).astype(jnp.bfloat16)
    sent_ref[0, 2 * seqs : first_pair, :] = tile_ref[...].astype(jnp.bfloat16)


def by_owner(ids_ref, z, near_ref, far_ref):
    step = z ^ (ids_ref[1] // 2)
    place = (near_ref.shape[0] - step) % near_ref.shape[0]
    near, far = near_ref[place], far_ref[place]
    first = ids_ref[1] % 2 == 0
    return jnp.where(first, near, far), jnp.where(first, far, near)


def outer_kernel(
    sizes,
    ids_ref,
    near_ref,
    far_ref,
    other_near_ref,
    other_far_ref,
    wturn_ref,
    outer_ref,
    proj_out_ref,
    cnt_ref,
    pm_ref,
    maskt_ref,
    rightt_ref,
    leftt_ref,
    leftn_ref,
    mine_ref,
    turnl_ref,
    turnr_ref,
    cntl_ref,
    pml_ref,
):
    seqs, res, pair_cols, width = sizes
    line = near_ref.shape[0]
    cols = 2 * line
    residues = cols * res
    lanes = res * width
    me_depth = ids_ref[0]
    lower = me_depth == 0
    f32, bf16 = jnp.float32, jnp.bfloat16

    for z in range(line):
        mine = by_owner(ids_ref, z, near_ref, far_ref)
        other = by_owner(ids_ref, z, other_near_ref, other_far_ref)
        for y in range(2):
            lanes_k = slice((2 * z + y) * lanes, (2 * z + y + 1) * lanes)
            both = jnp.concatenate(
                [
                    jnp.where(lower, mine[y], other[y]),
                    jnp.where(lower, other[y], mine[y]),
                ],
                axis=0,
            )
            rows = both.shape[0] // 2
            left = jnp.concatenate([both[0:seqs], both[rows : rows + seqs]], axis=0)
            right = jnp.concatenate(
                [both[seqs : 2 * seqs], both[rows + seqs : rows + 2 * seqs]], axis=0
            )
            leftn_ref[:, lanes_k] = left
            turnl_ref[lanes_k, :] = left.astype(f32).T
            turnr_ref[lanes_k, :] = right.astype(f32).T
            tiles = [
                both[first + 2 * seqs : first + 2 * seqs + MASK_ROWS].astype(f32)
                for first in (0, rows)
            ]
            maskt_ref[(2 * z + y) * res : (2 * z + y + 1) * res, :] = (
                tiles[0][0:res] + tiles[1][0:res]
            )
            own = mine[y][2 * seqs : 2 * seqs + MASK_ROWS].astype(f32)
            pair_lane = lax.broadcasted_iota(jnp.int32, (pair_cols, lanes), 1)
            pair_row = lax.broadcasted_iota(jnp.int32, (pair_cols, lanes), 0)
            for r in range(res):
                first = ((2 * z + y) * res + r) * pair_cols
                pml_ref[first : first + pair_cols, :] = jnp.where(
                    pair_lane == pair_row, own[res + r : res + r + 1, :], 0.0
                ).astype(bf16)
    for d in range(width):
        mine_ref[d * pair_cols : (d + 1) * pair_cols, :] = turnr_ref[
            pl.ds(me_depth * pair_cols * width + d, pair_cols, stride=width), :
        ].astype(bf16)
    for turned, out in ((turnl_ref, leftt_ref), (turnr_ref, rightt_ref)):
        for d in range(width):
            out[d * residues : (d + 1) * residues, :] = turned[
                pl.ds(d, residues, stride=width), :
            ].astype(bf16)

    maskt = maskt_ref[...]
    cols_mask = maskt_ref[pl.ds(pl.multiple_of(me_depth * pair_cols, pair_cols), pair_cols), :]
    for i in range(residues):
        cntl_ref[i * pair_cols : (i + 1) * pair_cols, :] = (maskt[i : i + 1, :] * cols_mask).astype(
            bf16
        )
    ones = jnp.ones((lanes, lanes), bf16)
    cnt_ref[...] = jnp.dot(cntl_ref[...], ones, preferred_element_type=f32)
    pm_ref[...] = jnp.dot(pml_ref[...], ones, preferred_element_type=f32).astype(bf16)

    for dh in range(width // 4):
        prod = jnp.dot(
            mine_ref[dh * 4 * pair_cols : (dh + 1) * 4 * pair_cols, :],
            leftn_ref[...],
            preferred_element_type=f32,
        )
        for k in range(cols):
            piece = prod[:, k * lanes : (k + 1) * lanes]
            turned = butterfly(
                [piece[a * pair_cols : (a + 1) * pair_cols] for a in range(4)], width
            )
            for il in range(res):
                first = (k * res + il) * pair_cols
                outer_ref[first : first + pair_cols, dh * lanes : (dh + 1) * lanes] = turned[
                    il
                ].astype(bf16)
    proj_out_ref[...] = jnp.dot(outer_ref[...], wturn_ref[...], preferred_element_type=f32)


def transition_kernel(
    sizes,
    ids_ref,
    near_ref,
    far_ref,
    proj_out_ref,
    cnt_ref,
    pm_ref,
    gain_ref,
    hid_ref,
    back_ref,
    couple_ref,
    opm_ref,
    pn_ref,
    gh_ref,
    hidden_ref,
    mg_ref,
    gmid_ref,
):
    seqs, res, pair_cols, width = sizes
    per = res * pair_cols
    cols = 2 * near_ref.shape[0]
    me_col = ids_ref[1]
    f32, bf16 = jnp.float32, jnp.bfloat16
    gain = gain_ref[...]
    chunk = 2 * per
    for at in range(cols // 2):
        rows = slice(at * chunk, (at + 1) * chunk)
        blocks = by_owner(ids_ref, at, near_ref, far_ref)
        act, grad = [
            jnp.concatenate([block[w * per : (w + 1) * per] for block in blocks], axis=0)
            for w in range(2)
        ]
        count = cnt_ref[rows, :]
        mid = act.astype(f32) + proj_out_ref[rows, :] / count
        scaled, inv = norm_pieces(mid)
        normed = (scaled * gain).astype(bf16)
        pn_ref[rows, :] = normed
        pre = jnp.dot(normed, hid_ref[...], preferred_element_type=f32)
        value, slope = silu_pieces(pre)
        hidden_ref[rows, :] = value.astype(bf16)
        masked = grad * pm_ref[rows, :]
        mg_ref[rows, :] = masked
        back = lax.dot_general(
            masked, back_ref[...], (((1,), (1,)), ((), ())), preferred_element_type=f32
        )
        ghid = (back * slope).astype(bf16)
        gh_ref[rows, :] = ghid
        gsc = (
            lax.dot_general(
                ghid, hid_ref[...], (((1,), (1,)), ((), ())), preferred_element_type=f32
            )
            * gain
        )
        gmid = grad.astype(f32) + standardize_adjoint(gsc, scaled, inv)
        gmid_ref[rows, :] = gmid
        opm_ref[rows, :] = (gmid / count).astype(bf16)
    couple_ref[...] = gmid_ref[pl.ds(pl.multiple_of(me_col * per, per), per), :].astype(bf16)


def projector_kernel(
    sizes,
    ids_ref,
    opm_ref,
    other_opm_ref,
    rightt_ref,
    leftt_ref,
    wout_ref,
    wturn_ref,
    maskt_ref,
    normed_ref,
    far_normed_ref,
    other_normed_ref,
    other_far_normed_ref,
    part_ref,
    spread_ref,
    gf_ref,
    grow_ref,
    gcol_ref,
    gor_ref,
    goc_ref,
    gs_ref,
    rows_ref,
):
    seqs, res, pair_cols, width = sizes
    depths, half = rows_ref.shape[1], gf_ref.shape[0]
    residues = half // pair_cols
    lanes = res * width
    here = 2 * res
    me_depth = ids_ref[0]
    me_col = ids_ref[1]
    me_y = me_col % 2
    first_here = (me_col // 2) * here
    f32, bf16 = jnp.float32, jnp.bfloat16
    my_half = first_here // pair_cols
    gf_ref[...] = jnp.where(my_half == me_depth, opm_ref[...], other_opm_ref[...]).astype(f32)
    for y, e, block in (
        (me_y, me_depth, normed_ref),
        (1 - me_y, me_depth, far_normed_ref),
        (me_y, 1 - me_depth, other_normed_ref),
        (1 - me_y, 1 - me_depth, other_far_normed_ref),
    ):
        rows_ref[y, e] = block[...]

    for il in range(here):
        first = pl.multiple_of((first_here + il) * pair_cols, pair_cols)
        for e, block in ((me_depth, opm_ref), (1 - me_depth, other_opm_ref)):
            to = pl.multiple_of(il * residues + e * pair_cols, pair_cols)
            grow_ref[pl.ds(to, pair_cols), :] = block[pl.ds(first, pair_cols), :]
    my_first = first_here - my_half * pair_cols
    for jl in range(here):
        gcol_ref[jl * residues : (jl + 1) * residues, :] = gf_ref[
            pl.ds(my_first + jl, residues, stride=pair_cols), :
        ].astype(bf16)
    for lhs, weight, out in ((grow_ref, wturn_ref, gor_ref), (gcol_ref, wout_ref, goc_ref)):
        for dh in range(width // 4):
            piece = lax.dot_general(
                lhs[...],
                weight[dh * lanes : (dh + 1) * lanes, :],
                (((1,), (1,)), ((), ())),
                preferred_element_type=f32,
            )
            for y in range(2):
                turned = butterfly(
                    [
                        piece[(y * res + a) * residues : (y * res + a + 1) * residues]
                        for a in range(4)
                    ],
                    width,
                )
                for dl in range(4):
                    first = (dh * 4 + dl) * residues
                    out[first : first + residues, y * lanes : (y + 1) * lanes] = turned[dl].astype(
                        bf16
                    )
    group = lax.broadcasted_iota(jnp.int32, (here, here * width), 1) // width
    spread = (group == lax.broadcasted_iota(jnp.int32, (here, here * width), 0)).astype(f32)
    mask_lanes = lax.dot_general(
        maskt_ref[pl.ds(pl.multiple_of(first_here, here), here), :],
        spread,
        (((0,), (0,)), ((), ())),
        preferred_element_type=f32,
    )
    lane_group = lax.broadcasted_iota(jnp.int32, (seqs, lanes), 1) // width
    for at, (lhs, rhs) in enumerate(((rightt_ref, gor_ref), (leftt_ref, goc_ref))):
        total = lax.dot_general(
            lhs[...], rhs[...], (((0,), (0,)), ((), ())), preferred_element_type=f32
        )
        total = (total * mask_lanes).astype(bf16).astype(f32)
        for y in range(2):
            for e in range(depths):
                block = total[e * seqs : (e + 1) * seqs, y * lanes : (y + 1) * lanes]
                for r in range(res):
                    gs_ref[at, y, e, pl.ds(r, seqs, stride=res), :] = jnp.where(
                        lane_group == r, block, 0.0
                    )
    spread_ref[...] = jnp.concatenate(
        [gs_ref[0, me_y, me_depth], gs_ref[1, me_y, me_depth]], axis=1
    ).astype(bf16)
    rows = rows_ref.shape[2]
    for at in range(2):
        cross = lax.dot_general(
            gs_ref[at].reshape(2 * depths * rows, lanes).astype(bf16),
            rows_ref[...].reshape(2 * depths * rows, rows_ref.shape[3]),
            (((0,), (0,)), ((), ())),
            preferred_element_type=f32,
        )
        total = cross[:width]
        for r in range(1, res):
            total = total + cross[r * width : (r + 1) * width]
        part_ref[at * width : (at + 1) * width, :] = total.astype(bf16)


def weights_kernel(outer_ref, opm_ref, pn_ref, gh_ref, hidden_ref, mg_ref, out_ref, turn_ref):
    pair_width, hid = pn_ref.shape[1], gh_ref.shape[1]
    outer_width = outer_ref.shape[1]
    width = int(outer_width**0.5 + 0.5)

    def contract(lhs, rhs):
        return lax.dot_general(
            lhs[...], rhs[...], (((0,), (0,)), ((), ())), preferred_element_type=jnp.float32
        )

    turn_ref[...] = contract(outer_ref, opm_ref)
    for c in range(width):
        out_ref[c * width : (c + 1) * width, :] = turn_ref[
            pl.ds(c, width, stride=width), :
        ].astype(jnp.bfloat16)
    dhid = contract(pn_ref, gh_ref).astype(jnp.bfloat16)
    for at in range(hid // pair_width):
        first = outer_width + at * pair_width
        out_ref[first : first + pair_width, :] = dhid[:, at * pair_width : (at + 1) * pair_width]
    out_ref[outer_width + hid :, :] = contract(hidden_ref, mg_ref).astype(jnp.bfloat16)


def weights_sum_kernel(mine_ref, other_ref, dout_ref, dhid_ref, dback_ref):
    pair_width, hid = dhid_ref.shape
    outer_width = dout_ref.shape[0]

    def added(first, count):
        rows = slice(first, first + count)
        return mine_ref[rows, :].astype(jnp.float32) + other_ref[rows, :].astype(jnp.float32)

    dout_ref[...] = added(0, outer_width)
    for at in range(hid // pair_width):
        dhid_ref[:, at * pair_width : (at + 1) * pair_width] = added(
            outer_width + at * pair_width, pair_width
        )
    dback_ref[...] = added(outer_width + hid, hid)


def feature_kernel(
    copies, spread_ref, first_ref, second_ref, scale_ref, scaled_ref, inv_ref, feat_ref
):
    back = jnp.dot(
        spread_ref[...],
        wide_projector(first_ref, second_ref, copies),
        preferred_element_type=jnp.float32,
    )
    feat_ref[...] = standardize_adjoint(
        back * scale_ref[...], scaled_ref[...], inv_ref[...]
    ).astype(jnp.bfloat16)


def swap_line(block, partners):
    count = lax.axis_size("col")
    pairs = [
        (depth * count + at, depth * count + (at ^ partner))
        for depth, partner in enumerate(partners)
        if partner is not None
        for at in range(count)
    ]
    return lax.ppermute(block, ("depth", "col"), pairs)


def swap_depth(block):
    return lax.ppermute(block, "depth", [(0, 1), (1, 0)])


def pairwise_sum(blocks):
    while len(blocks) > 1:
        blocks = [blocks[at] + blocks[at + 1] for at in range(0, len(blocks), 2)]
    return blocks[0]


def swap_col(block, partner):
    count = lax.axis_size("col")
    return lax.ppermute(block, "col", [(at, at ^ partner) for at in range(count)])


def whole_plan(
    alignment_activations,
    alignment_mask,
    pair_activation_input,
    pair_update_mask,
    pair_output_gradient,
    layer_scale_factor,
    first_projector,
    second_projector,
    output_weight,
    pair_norm_gain,
    hidden_weight,
    back_weight,
):
    seqs, res, channels = alignment_activations.shape
    width = first_projector.shape[1]
    outer_width = width * width
    cols = lax.axis_size("col")
    depths = lax.axis_size("depth")
    residues = res * cols
    pair_cols, pair_width = pair_activation_input.shape[1:]
    hid = hidden_weight.shape[1]
    per = res * pair_cols
    lanes = res * width
    rows = 2 * seqs + MASK_ROWS
    half = residues * pair_cols
    f32, bf16 = jnp.float32, jnp.bfloat16
    ids = jnp.stack([lax.axis_index("depth"), lax.axis_index("col")]).astype(jnp.int32)
    smem = pl.BlockSpec(memory_space=pltpu.SMEM)
    vmem = pl.BlockSpec(memory_space=pltpu.VMEM)
    params = pltpu.CompilerParams(vmem_limit_bytes=16 * 2**20)
    scale = layer_scale_factor.reshape(1, channels)
    first, second = first_projector.T, second_projector.T
    wturn = jnp.transpose(output_weight.reshape(width, width, pair_width), (1, 0, 2)).reshape(
        outer_width, pair_width
    )
    shape = jax.ShapeDtypeStruct
    sent, scale, first, second, gain, normed, scaled, inv = pl.pallas_call(
        pre_kernel,
        out_shape=(
            shape((1, rows + 2 * per, pair_width), bf16),
            shape((1, channels), f32),
            shape((width, channels), bf16),
            shape((width, channels), bf16),
            shape((1, pair_width), f32),
            shape((seqs * res, channels), bf16),
            shape((seqs * res, channels), f32),
            shape((seqs * res, 1), f32),
        ),
        in_specs=[smem] + [pl.BlockSpec(memory_space=pltpu.HBM)] * 9,
        out_specs=[vmem] * 8,
        scratch_shapes=[
            pltpu.VMEM((2, seqs * res, lanes), f32),
            pltpu.VMEM((MASK_ROWS, lanes), f32),
            pltpu.VMEM((seqs, res, channels), bf16),
            pltpu.VMEM((res, seqs), jnp.int32),
            pltpu.VMEM((res, pair_cols), jnp.int32),
            pltpu.SemaphoreType.DMA((9,)),
        ],
        compiler_params=params,
        name="project",
    )(
        ids,
        *[
            pltpu.with_memory_space_constraint(array, pltpu.HBM)
            for array in (
                alignment_activations,
                alignment_mask.T,
                pair_update_mask,
                scale,
                first,
                second,
                pair_norm_gain.reshape(1, pair_width),
                pair_activation_input.reshape(per, pair_width),
                pair_output_gradient.reshape(per, pair_width),
            )
        ],
    )
    blocks = lax.optimization_barrier(
        jnp.concatenate([sent] + [swap_col(sent, partner) for partner in Z_PARTNERS])
    )
    half_normed = seqs * res // 2
    far_normed_a = swap_col(normed[:half_normed], Y_PARTNER)
    blocks, far_normed_a = lax.optimization_barrier((blocks, far_normed_a))
    near, pair_near = blocks[:, :rows], blocks[:, rows:]
    far = swap_col(near, Y_PARTNER)
    pair_far = swap_col(pair_near, Y_PARTNER)
    other_near, other_far = swap_depth(near), swap_depth(far)
    sizes = (seqs, res, pair_cols, width)
    outer, proj_out, cnt, pm, maskt, rightt, leftt = pl.pallas_call(
        functools.partial(outer_kernel, sizes),
        out_shape=(
            shape((half, outer_width), bf16),
            shape((half, pair_width), f32),
            shape((half, lanes), f32),
            shape((half, lanes), bf16),
            shape((residues, depths * seqs), f32),
            shape((residues * width, depths * seqs), bf16),
            shape((residues * width, depths * seqs), bf16),
        ),
        in_specs=[smem] + [vmem] * 5,
        out_specs=[vmem] * 7,
        scratch_shapes=[
            pltpu.VMEM((depths * seqs, residues * width), bf16),
            pltpu.VMEM((pair_cols * width, depths * seqs), bf16),
            pltpu.VMEM((residues * width, depths * seqs), f32),
            pltpu.VMEM((residues * width, depths * seqs), f32),
            pltpu.VMEM((half, lanes), bf16),
            pltpu.VMEM((half, lanes), bf16),
        ],
        compiler_params=params,
        name="outer_products",
    )(ids, near, far, other_near, other_far, wturn)
    normed_b, proj_out = lax.optimization_barrier((normed[half_normed:], proj_out))
    far_normed_b = swap_col(normed_b, Y_PARTNER)
    pair_far, proj_out = lax.optimization_barrier((pair_far, proj_out))
    couple, opm, pn, gh, hidden, mg = pl.pallas_call(
        functools.partial(transition_kernel, sizes),
        out_shape=(
            shape((per, pair_width), bf16),
            shape((half, pair_width), bf16),
            shape((half, pair_width), bf16),
            shape((half, hid), bf16),
            shape((half, hid), bf16),
            shape((half, pair_width), bf16),
        ),
        in_specs=[smem] + [vmem] * 8,
        out_specs=[vmem] * 6,
        scratch_shapes=[
            pltpu.VMEM((half, pair_width), f32),
        ],
        compiler_params=params,
        name="transition",
    )(
        ids,
        pair_near,
        pair_far,
        proj_out,
        cnt,
        pm,
        gain,
        hidden_weight,
        back_weight,
    )
    opm, far_normed_b = lax.optimization_barrier((opm, far_normed_b))
    far_normed = jnp.concatenate([far_normed_a, far_normed_b])
    weights = pl.pallas_call(
        weights_kernel,
        out_shape=shape((outer_width + 2 * hid, pair_width), bf16),
        in_specs=[vmem] * 6,
        out_specs=vmem,
        scratch_shapes=[pltpu.VMEM((outer_width, pair_width), f32)],
        compiler_params=params,
        name="weight_gradients",
    )(outer, opm, pn, gh, hidden, mg)
    other_opm, other_normed, other_far_normed, weights = lax.optimization_barrier(
        (swap_depth(opm), swap_depth(normed), swap_depth(far_normed), weights)
    )
    part, spread = pl.pallas_call(
        functools.partial(projector_kernel, sizes),
        out_shape=(
            shape((2 * width, channels), bf16),
            shape((seqs * res, 2 * lanes), bf16),
        ),
        in_specs=[smem] + [vmem] * 11,
        out_specs=[vmem] * 2,
        scratch_shapes=[
            pltpu.VMEM((half, pair_width), f32),
            pltpu.VMEM((2 * res * residues, pair_width), bf16),
            pltpu.VMEM((2 * res * residues, pair_width), bf16),
            pltpu.VMEM((residues * width, 2 * lanes), bf16),
            pltpu.VMEM((residues * width, 2 * lanes), bf16),
            pltpu.VMEM((2, 2, depths, seqs * res, lanes), f32),
            pltpu.VMEM((2, depths, seqs * res, channels), bf16),
        ],
        compiler_params=params,
        name="projector_parts",
    )(
        ids,
        opm,
        other_opm,
        rightt,
        leftt,
        output_weight,
        wturn,
        maskt,
        normed,
        far_normed,
        other_normed,
        other_far_normed,
    )
    feat = pl.pallas_call(
        functools.partial(feature_kernel, res),
        out_shape=shape((seqs * res, channels), bf16),
        in_specs=[vmem] * 6,
        out_specs=vmem,
        compiler_params=params,
        name="features",
    )(spread, first, second, scale, scaled, inv)
    part, weights = lax.optimization_barrier((part, weights))
    dout, dhid, dback = pl.pallas_call(
        weights_sum_kernel,
        out_shape=(
            shape((outer_width, pair_width), f32),
            shape((pair_width, hid), f32),
            shape((hid, pair_width), f32),
        ),
        in_specs=[vmem] * 2,
        out_specs=[vmem] * 3,
        compiler_params=params,
        name="sums_over_depth",
    )(weights, swap_depth(weights))
    came_a = swap_line(part, Z_PARTNERS[:2])
    came_b = swap_line(part, (None, Z_PARTNERS[2]))
    feat = feat.reshape(seqs, res, channels)
    came_a, came_b, feat = lax.optimization_barrier((came_a, came_b, feat))
    kept = jnp.where(lax.axis_index("depth") == 0, part, came_b)
    kept = lax.optimization_barrier((kept.astype(f32) + came_a.astype(f32)).astype(bf16))
    came = swap_depth(kept)
    came, dout, dhid, dback = lax.optimization_barrier((came, dout, dhid, dback))
    total = kept.astype(f32) + came.astype(f32)
    return (
        feat,
        couple.reshape(res, pair_cols, pair_width),
        total[:width].T,
        total[width:].T,
        dout,
        dhid,
        dback,
    )


def on_device(alignment_activations, *others):
    cols = lax.axis_size("col")
    residues = alignment_activations.shape[1] * cols
    plan = whole_plan if cols == 8 and residues <= FEW_RESIDUES else split_plan
    return plan(alignment_activations, *others)


def solution(mesh):
    in_specs = (
        P(("group", "depth"), "col", None),
        P(("group", "depth"), "col"),
        P(("group", "col"), "depth", None),
        P(("group", "col"), "depth"),
        P(("group", "col"), "depth", None),
        P(),
        P(),
        P(),
        P(),
        P(),
        P(),
        P(),
    )
    out_specs = (
        P(("group", "depth"), "col", None),
        P(("group", "col"), "depth", None),
        P("group", None),
        P("group", None),
        P("group", None),
        P("group", None),
        P("group", None),
    )
    return jax.shard_map(
        on_device, mesh=mesh, in_specs=in_specs, out_specs=out_specs, check_vma=False
    )
```

```python
import functools

import jax
import jax.numpy as jnp
from jax import lax
from jax.experimental import pallas as pl
from jax.experimental.pallas import tpu as pltpu
from jax.sharding import PartitionSpec as P

epsilon = 1e-05
highest = lax.Precision.HIGHEST


def norm_pieces(entries_drawn):
    center = entries_drawn - jnp.mean(entries_drawn, axis=-1, keepdims=True)
    inv_std = lax.rsqrt(jnp.mean(center * center, axis=-1, keepdims=True) + epsilon)
    return (center * inv_std, inv_std)


def standardize_adjoint(grad_scaled, scaled, inv_std):
    mean_grad = jnp.mean(grad_scaled, axis=-1, keepdims=True)
    mean_cross = jnp.mean(grad_scaled * scaled, axis=-1, keepdims=True)
    return inv_std * (grad_scaled - mean_grad - scaled * mean_cross)


def silu_pieces(pre_act):
    sigma = jax.nn.sigmoid(pre_act)
    return (pre_act * sigma, sigma * (1.0 + pre_act * (1.0 - sigma)))


def split_plan(
    alignment_activations,
    alignment_mask,
    pair_activation_input,
    pair_update_mask,
    pair_output_gradient,
    layer_scale_factor,
    first_projector,
    second_projector,
    output_weight,
    pair_norm_gain,
    hidden_weight,
    back_weight,
):
    sequence_row_block, residue_row_block, channel_total = alignment_activations.shape
    proj_width = first_projector.shape[1]
    outer_width = proj_width * proj_width
    depth_count = lax.axis_size("depth")
    residues = residue_row_block * lax.axis_size("col")
    pair_cols = pair_activation_input.shape[1]
    pair_width = pair_activation_input.shape[2]
    col_block = min(64, pair_cols)
    block_count = pair_cols // col_block
    standardized_features, reciprocal_spread = norm_pieces(
        alignment_activations.astype(jnp.float32)
    )
    normalized_rows = (standardized_features * layer_scale_factor).astype(jnp.bfloat16)
    mask_floating = alignment_mask.astype(jnp.float32)
    left_proj = (
        jnp.dot(normalized_rows, first_projector, preferred_element_type=jnp.float32)
        * mask_floating[:, :, None]
    ).astype(jnp.bfloat16)
    right_proj = (
        jnp.dot(normalized_rows, second_projector, preferred_element_type=jnp.float32)
        * mask_floating[:, :, None]
    ).astype(jnp.bfloat16)
    right_flat = right_proj.reshape(sequence_row_block, residue_row_block * proj_width)
    mask_converted = alignment_mask.astype(jnp.bfloat16)
    seq_total = left_proj.shape[0]
    gathered, gathered_mask = (
        lax.all_gather(right_flat, "col", axis=1, tiled=True),
        lax.all_gather(mask_converted, "col", axis=1, tiled=True),
    )
    right_blocks = gathered.reshape(seq_total, depth_count, pair_cols, proj_width)
    mask_blocks = gathered_mask.reshape(seq_total, depth_count, pair_cols)
    block_depth = right_blocks.shape[1]
    out_wide = output_weight.astype(jnp.float32)

    def partial_outer(col_start):
        right_piece = lax.dynamic_slice_in_dim(right_blocks, col_start, col_block, 2)
        outer_part = jnp.einsum(
            "sic,sejd->iejcd", left_proj, right_piece, preferred_element_type=jnp.float32
        )
        return (
            outer_part.reshape(residue_row_block, block_depth, col_block, outer_width),
            right_piece,
        )

    def forward_step(step_index, loop_state):
        projected, pair_count = loop_state
        col_start = step_index * col_block
        outer_part, right_piece = partial_outer(col_start)
        mask_piece = lax.dynamic_slice_in_dim(mask_blocks, col_start, col_block, 2).astype(
            jnp.float32
        )
        count_part = jnp.einsum("si,sej->iej", mask_floating, mask_piece, precision=highest)
        outer_mine, count_mine = (
            lax.psum_scatter(
                outer_part.astype(jnp.bfloat16), "depth", scatter_dimension=1, tiled=True
            ).astype(jnp.float32),
            lax.psum_scatter(
                count_part.astype(jnp.bfloat16), "depth", scatter_dimension=1, tiled=True
            ).astype(jnp.float32),
        )
        proj_mine = jnp.dot(
            outer_mine.reshape(residue_row_block * col_block, outer_width),
            out_wide,
            precision=highest,
        )
        proj_mine = proj_mine.reshape(residue_row_block, col_block, pair_width)
        count_mine = count_mine.reshape(residue_row_block, col_block)
        projected = lax.dynamic_update_slice_in_dim(projected, proj_mine, col_start, 1)
        pair_count = lax.dynamic_update_slice_in_dim(pair_count, count_mine, col_start, 1)
        return (projected, pair_count)

    projected, pair_count = lax.fori_loop(
        0,
        block_count,
        forward_step,
        (
            jnp.zeros((residue_row_block, pair_cols, pair_width), jnp.float32),
            jnp.zeros((residue_row_block, pair_cols), jnp.float32),
        ),
    )
    count_column = pair_count.reshape(residue_row_block * pair_cols, 1)
    mid_act = (
        pair_activation_input.reshape(residue_row_block * pair_cols, pair_width).astype(jnp.float32)
        + projected.reshape(residue_row_block * pair_cols, pair_width) / count_column
    )
    pair_scaled, pair_inv = norm_pieces(mid_act)
    pair_normed = (pair_scaled * pair_norm_gain).astype(jnp.bfloat16)
    pre_act = jnp.dot(pair_normed, hidden_weight, preferred_element_type=jnp.float32)
    act_value, act_slope = silu_pieces(pre_act)
    hidden = act_value.astype(jnp.bfloat16)
    masked_grad = (
        pair_output_gradient * pair_update_mask.astype(jnp.bfloat16)[:, :, None]
    ).reshape(residue_row_block * pair_cols, pair_width)
    final_matrix_derivative = jnp.dot(hidden.T, masked_grad, preferred_element_type=jnp.float32)
    back_prod = jnp.dot(masked_grad, back_weight.T, preferred_element_type=jnp.float32)
    grad_hidden = (back_prod * act_slope).astype(jnp.bfloat16)
    middle_matrix_derivative = jnp.dot(
        pair_normed.T, grad_hidden, preferred_element_type=jnp.float32
    )
    grad_scaled = (
        jnp.dot(grad_hidden, hidden_weight.T, preferred_element_type=jnp.float32) * pair_norm_gain
    )
    grad_mid = pair_output_gradient.reshape(residue_row_block * pair_cols, pair_width).astype(
        jnp.float32
    ) + standardize_adjoint(grad_scaled, pair_scaled, pair_inv)
    couple_features_derivative = grad_mid.astype(jnp.bfloat16).reshape(
        residue_row_block, pair_cols, pair_width
    )
    grad_opm = (
        (grad_mid / count_column)
        .astype(jnp.bfloat16)
        .reshape(residue_row_block, pair_cols, pair_width)
    )
    full_opm = lax.all_gather(grad_opm, "depth", axis=1, tiled=True).reshape(
        residue_row_block, depth_count, pair_cols, pair_width
    )

    def backward_step(step_index, loop_state):
        grad_left_acc, grad_out, right_term = loop_state
        col_start = step_index * col_block
        outer_part, right_piece = partial_outer(col_start)
        opm_piece = lax.dynamic_slice_in_dim(full_opm, col_start, col_block, 2).reshape(
            residue_row_block * block_depth * col_block, pair_width
        )
        grad_out = grad_out + jnp.dot(
            outer_part.reshape(residue_row_block * block_depth * col_block, outer_width).T,
            opm_piece.astype(jnp.float32),
            precision=highest,
        )
        grad_outer = jnp.dot(opm_piece, output_weight.T, preferred_element_type=jnp.float32).astype(
            jnp.bfloat16
        )
        grad_outer = grad_outer.reshape(
            residue_row_block, block_depth, col_block, proj_width, proj_width
        )
        grad_left_acc = grad_left_acc + jnp.einsum(
            "iejcd,sejd->sic", grad_outer, right_piece, preferred_element_type=jnp.float32
        )
        piece_term = jnp.einsum(
            "iejcd,sic->ejsd", grad_outer, left_proj, preferred_element_type=jnp.float32
        )
        piece_term = piece_term.reshape(block_depth, col_block, seq_total * proj_width)
        right_term = lax.dynamic_update_slice_in_dim(right_term, piece_term, col_start, 1)
        return (grad_left_acc, grad_out, right_term)

    grad_left_acc, result_matrix_derivative, right_term = lax.fori_loop(
        0,
        block_count,
        backward_step,
        (
            jnp.zeros((seq_total, residue_row_block, proj_width), jnp.float32),
            jnp.zeros((outer_width, pair_width), jnp.float32),
            jnp.zeros((block_depth, pair_cols, seq_total * proj_width), jnp.float32),
        ),
    )
    grad_right_sum = lax.psum_scatter(
        right_term.reshape(residues, seq_total * proj_width), "col", scatter_dimension=0, tiled=True
    )
    grad_right_acc = jnp.transpose(
        grad_right_sum.reshape(residue_row_block, seq_total, proj_width), (1, 0, 2)
    )
    grad_left = (grad_left_acc * mask_floating[:, :, None]).astype(jnp.bfloat16)
    grad_right = (grad_right_acc * mask_floating[:, :, None]).astype(jnp.bfloat16)
    normed_rows = normalized_rows.reshape(sequence_row_block * residue_row_block, channel_total)
    first_projector_derivative = jnp.dot(
        normed_rows.T,
        grad_left.reshape(sequence_row_block * residue_row_block, proj_width),
        preferred_element_type=jnp.float32,
    )
    second_projector_derivative = jnp.dot(
        normed_rows.T,
        grad_right.reshape(sequence_row_block * residue_row_block, proj_width),
        preferred_element_type=jnp.float32,
    )
    standardized_derivative = jnp.dot(
        grad_left, first_projector.T, preferred_element_type=jnp.float32
    ) + jnp.dot(grad_right, second_projector.T, preferred_element_type=jnp.float32)
    features_derivative = standardize_adjoint(
        standardized_derivative * layer_scale_factor, standardized_features, reciprocal_spread
    ).astype(jnp.bfloat16)
    weight_sums = lax.psum(
        (
            first_projector_derivative,
            second_projector_derivative,
            result_matrix_derivative,
            middle_matrix_derivative,
            final_matrix_derivative,
        ),
        ("depth", "col"),
    )
    return (
        features_derivative,
        couple_features_derivative,
        weight_sums[0],
        weight_sums[1],
        weight_sums[2],
        weight_sums[3],
        weight_sums[4],
    )


FEW_RESIDUES = 32
MASK_ROWS = 16
Z_PARTNERS = (6, 4, 2)
Y_PARTNER = 1


def butterfly(blocks, group):
    lane_group = lax.broadcasted_iota(jnp.int32, blocks[0].shape, 1) // group
    width = 4 * group
    for bit in (2, 1):
        low = (lane_group & bit) == 0
        swapped = list(blocks)
        for at in range(4):
            if at & bit:
                continue
            here, there = blocks[at], blocks[at | bit]
            moving = jnp.where(low, there, here)
            if bit == 2:
                moved = pltpu.roll(moving, 2 * group, 1)
            else:
                moved = jnp.where(
                    low, pltpu.roll(moving, width - group, 1), pltpu.roll(moving, group, 1)
                )
            swapped[at] = jnp.where(low, here, moved)
            swapped[at | bit] = jnp.where(low, moved, there)
        blocks = swapped
    return blocks


def wide_projector(first_ref, second_ref, copies):
    return jnp.concatenate([first_ref[...]] * copies + [second_ref[...]] * copies, axis=0)


def pre_kernel(
    ids_ref,
    x_hbm,
    maskt_hbm,
    pmask_hbm,
    scale_hbm,
    first_hbm,
    second_hbm,
    gain_hbm,
    act_hbm,
    grad_hbm,
    sent_ref,
    scale_ref,
    first_ref,
    second_ref,
    gain_ref,
    normed_ref,
    scaled_ref,
    inv_ref,
    wide_ref,
    tile_ref,
    x_ref,
    maskt_ref,
    pmask_ref,
    sems,
):
    res, seqs = maskt_ref.shape
    pairs = act_hbm.shape[0]
    first_pair = 2 * seqs + MASK_ROWS
    copies = [
        pltpu.make_async_copy(source, target, sems.at[at])
        for at, (source, target) in enumerate(
            (
                (x_hbm, x_ref),
                (maskt_hbm, maskt_ref),
                (pmask_hbm, pmask_ref),
                (scale_hbm, scale_ref),
                (first_hbm, first_ref),
                (second_hbm, second_ref),
                (gain_hbm, gain_ref),
                (act_hbm, sent_ref.at[0, pl.ds(first_pair, pairs), :]),
                (grad_hbm, sent_ref.at[0, pl.ds(first_pair + pairs, pairs), :]),
            )
        )
    ]
    for copy in copies:
        copy.start()
    for copy in copies:
        copy.wait()
    lanes = sent_ref.shape[2]
    group = lanes // res
    scaled, inv = norm_pieces(
        x_ref[...].astype(jnp.float32).reshape(seqs * res, x_ref.shape[2])
    )
    scaled_ref[...] = scaled
    inv_ref[...] = inv
    normed = (scaled * scale_ref[...]).astype(jnp.bfloat16)
    normed_ref[...] = normed
    wide = lax.dot_general(
        normed,
        wide_projector(first_ref, second_ref, res),
        (((1,), (1,)), ((), ())),
        preferred_element_type=jnp.float32,
    )
    for at in range(2):
        wide_ref[at] = wide[:, at * lanes : (at + 1) * lanes]
    tile_ref[...] = jnp.zeros(tile_ref.shape, jnp.float32)
    mask = maskt_ref[...].astype(jnp.float32)
    tile_ref[0:res, 0:seqs] = mask
    spread = (
        lax.broadcasted_iota(jnp.int32, (MASK_ROWS, lanes), 1) // group
        == lax.broadcasted_iota(jnp.int32, (MASK_ROWS, lanes), 0)
    ).astype(jnp.float32)
    mask_lanes = lax.dot_general(
        tile_ref[...], spread, (((0,), (0,)), ((), ())), preferred_element_type=jnp.float32
    )[:seqs]
    twice = jnp.concatenate([mask] * (lanes // seqs), axis=1)
    here = lax.broadcasted_iota(jnp.int32, (res, lanes), 1) // seqs == ids_ref[0]
    tile_ref[0:res, :] = jnp.where(here, twice, 0.0)
    tile_ref[res : 2 * res, 0 : pmask_ref.shape[1]] = pmask_ref[...].astype(jnp.float32)
    lane_group = lax.broadcasted_iota(jnp.int32, (seqs, lanes), 1) // group
    for at in range(2):
        both = wide_ref[at, pl.ds(0, seqs, stride=res), :]
        for r in range(1, res):
            both = jnp.where(
                lane_group == r, wide_ref[at, pl.ds(r, seqs, stride=res), :], both
            )
        sent_ref[0, at * seqs : (at + 1) * seqs, :] = (both * mask_lanes).astype(jnp.bfloat16)
    sent_ref[0, 2 * seqs : first_pair, :] = tile_ref[...].astype(jnp.bfloat16)


def by_owner(ids_ref, z, near_ref, far_ref):
    step = z ^ (ids_ref[1] // 2)
    place = (near_ref.shape[0] - step) % near_ref.shape[0]
    near, far = near_ref[place], far_ref[place]
    first = ids_ref[1] % 2 == 0
    return jnp.where(first, near, far), jnp.where(first, far, near)


def outer_kernel(
    sizes,
    ids_ref,
    near_ref,
    far_ref,
    other_near_ref,
    other_far_ref,
    wturn_ref,
    outer_ref,
    proj_out_ref,
    cnt_ref,
    pm_ref,
    maskt_ref,
    rightt_ref,
    leftt_ref,
    leftn_ref,
    mine_ref,
    turnl_ref,
    turnr_ref,
    cntl_ref,
    pml_ref,
):
    seqs, res, pair_cols, width = sizes
    line = near_ref.shape[0]
    cols = 2 * line
    residues = cols * res
    lanes = res * width
    me_depth = ids_ref[0]
    lower = me_depth == 0
    f32, bf16 = jnp.float32, jnp.bfloat16

    for z in range(line):
        mine = by_owner(ids_ref, z, near_ref, far_ref)
        other = by_owner(ids_ref, z, other_near_ref, other_far_ref)
        for y in range(2):
            lanes_k = slice((2 * z + y) * lanes, (2 * z + y + 1) * lanes)
            place = y * line + z
            lanes_p = slice(place * lanes, (place + 1) * lanes)
            both = jnp.concatenate(
                [
                    jnp.where(lower, mine[y], other[y]),
                    jnp.where(lower, other[y], mine[y]),
                ],
                axis=0,
            )
            rows = both.shape[0] // 2
            left = jnp.concatenate([both[0:seqs], both[rows : rows + seqs]], axis=0)
            right = jnp.concatenate(
                [both[seqs : 2 * seqs], both[rows + seqs : rows + 2 * seqs]], axis=0
            )
            leftn_ref[:, lanes_p] = left
            turnl_ref[lanes_p, :] = left.astype(f32).T
            turnr_ref[lanes_k, :] = right.astype(f32).T
            tiles = [
                both[first + 2 * seqs : first + 2 * seqs + MASK_ROWS].astype(f32)
                for first in (0, rows)
            ]
            maskt_ref[(2 * z + y) * res : (2 * z + y + 1) * res, :] = (
                tiles[0][0:res] + tiles[1][0:res]
            )
            own = mine[y][2 * seqs : 2 * seqs + MASK_ROWS].astype(f32)
            pair_lane = lax.broadcasted_iota(jnp.int32, (pair_cols, lanes), 1)
            pair_row = lax.broadcasted_iota(jnp.int32, (pair_cols, lanes), 0)
            for r in range(res):
                first = (place * res + r) * pair_cols
                pml_ref[first : first + pair_cols, :] = jnp.where(
                    pair_lane == pair_row, own[res + r : res + r + 1, :], 0.0
                ).astype(bf16)
    for d in range(width):
        mine_ref[d * pair_cols : (d + 1) * pair_cols, :] = turnr_ref[
            pl.ds(me_depth * pair_cols * width + d, pair_cols, stride=width), :
        ].astype(bf16)
    for turned, out in ((turnl_ref, leftt_ref), (turnr_ref, rightt_ref)):
        for d in range(width):
            out[d * residues : (d + 1) * residues, :] = turned[
                pl.ds(d, residues, stride=width), :
            ].astype(bf16)

    maskt = maskt_ref[...]
    cols_mask = maskt_ref[pl.ds(pl.multiple_of(me_depth * pair_cols, pair_cols), pair_cols), :]
    for i in range(residues):
        z, y, r = i // (2 * res), i // res % 2, i % res
        first = ((y * line + z) * res + r) * pair_cols
        cntl_ref[first : first + pair_cols, :] = (maskt[i : i + 1, :] * cols_mask).astype(bf16)
    ones = jnp.ones((lanes, lanes), bf16)
    cnt_ref[...] = jnp.dot(cntl_ref[...], ones, preferred_element_type=f32)
    pm_ref[...] = jnp.dot(pml_ref[...], ones, preferred_element_type=f32).astype(bf16)

    for dh in range(width // 4):
        prod = jnp.dot(
            mine_ref[dh * 4 * pair_cols : (dh + 1) * 4 * pair_cols, :],
            leftn_ref[...],
            preferred_element_type=f32,
        )
        for k in range(cols):
            piece = prod[:, k * lanes : (k + 1) * lanes]
            turned = butterfly(
                [piece[a * pair_cols : (a + 1) * pair_cols] for a in range(4)], width
            )
            for il in range(res):
                first = (k * res + il) * pair_cols
                outer_ref[first : first + pair_cols, dh * lanes : (dh + 1) * lanes] = turned[
                    il
                ].astype(bf16)
    proj_out_ref[...] = jnp.dot(outer_ref[...], wturn_ref[...], preferred_element_type=f32)


def transition_kernel(
    sizes,
    near,
    ids_ref,
    blocks_ref,
    proj_out_ref,
    cnt_ref,
    pm_ref,
    gain_ref,
    hid_ref,
    back_ref,
    opm_ref,
    pn_ref,
    gh_ref,
    hidden_ref,
    mg_ref,
    *couple,
):
    _, res, pair_cols, _ = sizes
    per = res * pair_cols
    line = blocks_ref.shape[0]
    me_z, me_y = ids_ref[1] // 2, ids_ref[1] % 2
    f32, bf16 = jnp.float32, jnp.bfloat16
    gain = gain_ref[...]
    chunk = 2 * per
    half = line * per
    first_row = (me_y if near else 1 - me_y) * half
    for at in range(line // 2):
        rows = slice(at * chunk, (at + 1) * chunk)
        there = pl.ds(pl.multiple_of(first_row + at * chunk, chunk), chunk)
        blocks = [
            blocks_ref[(line - (z ^ me_z)) % line]
            for z in (2 * at, 2 * at + 1)
        ]
        act, grad = [
            jnp.concatenate([block[w * per : (w + 1) * per] for block in blocks], axis=0)
            for w in range(2)
        ]
        count = cnt_ref[there, :]
        mid = act.astype(f32) + proj_out_ref[there, :] / count
        scaled, inv = norm_pieces(mid)
        normed = (scaled * gain).astype(bf16)
        pn_ref[rows, :] = normed
        pre = jnp.dot(normed, hid_ref[...], preferred_element_type=f32)
        value, slope = silu_pieces(pre)
        hidden_ref[rows, :] = value.astype(bf16)
        masked = grad * pm_ref[there, :]
        mg_ref[rows, :] = masked
        back = lax.dot_general(
            masked, back_ref[...], (((1,), (1,)), ((), ())), preferred_element_type=f32
        )
        ghid = (back * slope).astype(bf16)
        gh_ref[rows, :] = ghid
        gsc = (
            lax.dot_general(
                ghid, hid_ref[...], (((1,), (1,)), ((), ())), preferred_element_type=f32
            )
            * gain
        )
        gmid = grad.astype(f32) + standardize_adjoint(gsc, scaled, inv)
        opm_ref[rows, :] = (gmid / count).astype(bf16)
        if near:
            couple[1][rows, :] = gmid.astype(bf16)
    if near:
        couple[0][...] = couple[1][pl.ds(pl.multiple_of(me_z * per, per), per), :]


def projector_kernel(
    sizes,
    ids_ref,
    opm_ref,
    other_opm_ref,
    rightt_ref,
    leftt_ref,
    wout_ref,
    wturn_ref,
    maskt_ref,
    normed_ref,
    far_normed_ref,
    other_normed_ref,
    other_far_normed_ref,
    part_ref,
    spread_ref,
    gf_ref,
    grow_ref,
    gcol_ref,
    gor_ref,
    goc_ref,
    gs_ref,
    rows_ref,
):
    seqs, res, pair_cols, width = sizes
    depths, half = rows_ref.shape[1], gf_ref.shape[0]
    residues = half // pair_cols
    lanes = res * width
    here = 2 * res
    me_depth = ids_ref[0]
    me_col = ids_ref[1]
    me_y = me_col % 2
    me_z = me_col // 2
    first_here = me_z * here
    f32, bf16 = jnp.float32, jnp.bfloat16
    my_half = first_here // pair_cols
    mine = jnp.where(my_half == me_depth, opm_ref[...], other_opm_ref[...]).astype(f32)
    quarter = half // 2
    for w, y in enumerate((me_y, 1 - me_y)):
        gf_ref[pl.ds(pl.multiple_of(y * quarter, quarter), quarter), :] = mine[
            w * quarter : (w + 1) * quarter
        ]
    for y, e, block in (
        (me_y, me_depth, normed_ref),
        (1 - me_y, me_depth, far_normed_ref),
        (me_y, 1 - me_depth, other_normed_ref),
        (1 - me_y, 1 - me_depth, other_far_normed_ref),
    ):
        rows_ref[y, e] = block[...]

    for w, y in enumerate((me_y, 1 - me_y)):
        for r in range(res):
            first = pl.multiple_of(w * quarter + (me_z * res + r) * pair_cols, pair_cols)
            for e, block in ((me_depth, opm_ref), (1 - me_depth, other_opm_ref)):
                to = pl.multiple_of((y * res + r) * residues + e * pair_cols, pair_cols)
                grow_ref[pl.ds(to, pair_cols), :] = block[pl.ds(first, pair_cols), :]
    my_first = first_here - my_half * pair_cols
    for jl in range(here):
        gcol_ref[jl * residues : (jl + 1) * residues, :] = gf_ref[
            pl.ds(my_first + jl, residues, stride=pair_cols), :
        ].astype(bf16)
    for lhs, weight, out in ((grow_ref, wturn_ref, gor_ref), (gcol_ref, wout_ref, goc_ref)):
        for dh in range(width // 4):
            piece = lax.dot_general(
                lhs[...],
                weight[dh * lanes : (dh + 1) * lanes, :],
                (((1,), (1,)), ((), ())),
                preferred_element_type=f32,
            )
            for y in range(2):
                turned = butterfly(
                    [
                        piece[(y * res + a) * residues : (y * res + a + 1) * residues]
                        for a in range(4)
                    ],
                    width,
                )
                for dl in range(4):
                    first = (dh * 4 + dl) * residues
                    out[first : first + residues, y * lanes : (y + 1) * lanes] = turned[dl].astype(
                        bf16
                    )
    group = lax.broadcasted_iota(jnp.int32, (here, here * width), 1) // width
    spread = (group == lax.broadcasted_iota(jnp.int32, (here, here * width), 0)).astype(f32)
    mask_lanes = lax.dot_general(
        maskt_ref[pl.ds(pl.multiple_of(first_here, here), here), :],
        spread,
        (((0,), (0,)), ((), ())),
        preferred_element_type=f32,
    )
    lane_group = lax.broadcasted_iota(jnp.int32, (seqs, lanes), 1) // width
    for at, (lhs, rhs) in enumerate(((rightt_ref, gor_ref), (leftt_ref, goc_ref))):
        total = lax.dot_general(
            lhs[...], rhs[...], (((0,), (0,)), ((), ())), preferred_element_type=f32
        )
        total = (total * mask_lanes).astype(bf16).astype(f32)
        for y in range(2):
            for e in range(depths):
                block = total[e * seqs : (e + 1) * seqs, y * lanes : (y + 1) * lanes]
                for r in range(res):
                    gs_ref[at, y, e, pl.ds(r, seqs, stride=res), :] = jnp.where(
                        lane_group == r, block, 0.0
                    )
    spread_ref[...] = jnp.concatenate(
        [gs_ref[0, me_y, me_depth], gs_ref[1, me_y, me_depth]], axis=1
    ).astype(bf16)
    rows = rows_ref.shape[2]
    for at in range(2):
        cross = lax.dot_general(
            gs_ref[at].reshape(2 * depths * rows, lanes).astype(bf16),
            rows_ref[...].reshape(2 * depths * rows, rows_ref.shape[3]),
            (((0,), (0,)), ((), ())),
            preferred_element_type=f32,
        )
        total = cross[:width]
        for r in range(1, res):
            total = total + cross[r * width : (r + 1) * width]
        part_ref[at * width : (at + 1) * width, :] = total.astype(bf16)


def weights_kernel(ids_ref, outer_ref, *refs):
    near, far, (out_ref, turn_ref) = refs[0:5], refs[5:10], refs[10:]
    half, pair_width = near[1].shape
    hid = near[2].shape[1]
    outer_width = outer_ref.shape[1]
    width = int(outer_width**0.5 + 0.5)
    me_y = ids_ref[1] % 2

    def contract(lhs, rhs):
        return lax.dot_general(
            lhs, rhs, (((0,), (0,)), ((), ())), preferred_element_type=jnp.float32
        )

    turn_ref[...] = sum(
        contract(outer_ref[pl.ds(pl.multiple_of(y * half, half), half), :], refs_y[0][...])
        for y, refs_y in ((me_y, near), (1 - me_y, far))
    )
    for c in range(width):
        out_ref[c * width : (c + 1) * width, :] = turn_ref[
            pl.ds(c, width, stride=width), :
        ].astype(jnp.bfloat16)
    dhid = sum(contract(refs_y[1][...], refs_y[2][...]) for refs_y in (near, far))
    for at in range(hid // pair_width):
        first = outer_width + at * pair_width
        out_ref[first : first + pair_width, :] = dhid[
            :, at * pair_width : (at + 1) * pair_width
        ].astype(jnp.bfloat16)
    out_ref[outer_width + hid :, :] = sum(
        contract(refs_y[3][...], refs_y[4][...]) for refs_y in (near, far)
    ).astype(jnp.bfloat16)


def weights_sum_kernel(mine_ref, other_ref, dout_ref, dhid_ref, dback_ref):
    pair_width, hid = dhid_ref.shape
    outer_width = dout_ref.shape[0]

    def added(first, count):
        rows = slice(first, first + count)
        return mine_ref[rows, :].astype(jnp.float32) + other_ref[rows, :].astype(jnp.float32)

    dout_ref[...] = added(0, outer_width)
    for at in range(hid // pair_width):
        dhid_ref[:, at * pair_width : (at + 1) * pair_width] = added(
            outer_width + at * pair_width, pair_width
        )
    dback_ref[...] = added(outer_width + hid, hid)


def feature_kernel(
    copies, spread_ref, first_ref, second_ref, scale_ref, scaled_ref, inv_ref, feat_ref
):
    back = jnp.dot(
        spread_ref[...],
        wide_projector(first_ref, second_ref, copies),
        preferred_element_type=jnp.float32,
    )
    feat_ref[...] = standardize_adjoint(
        back * scale_ref[...], scaled_ref[...], inv_ref[...]
    ).astype(jnp.bfloat16)


def swap_line(block, partners):
    count = lax.axis_size("col")
    pairs = [
        (depth * count + at, depth * count + (at ^ partner))
        for depth, partner in enumerate(partners)
        if partner is not None
        for at in range(count)
    ]
    return lax.ppermute(block, ("depth", "col"), pairs)


def swap_depth(block):
    return lax.ppermute(block, "depth", [(0, 1), (1, 0)])


def pairwise_sum(blocks):
    while len(blocks) > 1:
        blocks = [blocks[at] + blocks[at + 1] for at in range(0, len(blocks), 2)]
    return blocks[0]


def swap_col(block, partner):
    count = lax.axis_size("col")
    return lax.ppermute(block, "col", [(at, at ^ partner) for at in range(count)])


def whole_plan(
    alignment_activations,
    alignment_mask,
    pair_activation_input,
    pair_update_mask,
    pair_output_gradient,
    layer_scale_factor,
    first_projector,
    second_projector,
    output_weight,
    pair_norm_gain,
    hidden_weight,
    back_weight,
):
    seqs, res, channels = alignment_activations.shape
    width = first_projector.shape[1]
    outer_width = width * width
    cols = lax.axis_size("col")
    depths = lax.axis_size("depth")
    residues = res * cols
    pair_cols, pair_width = pair_activation_input.shape[1:]
    hid = hidden_weight.shape[1]
    per = res * pair_cols
    lanes = res * width
    rows = 2 * seqs + MASK_ROWS
    half = residues * pair_cols
    line = cols // 2
    f32, bf16 = jnp.float32, jnp.bfloat16
    ids = jnp.stack([lax.axis_index("depth"), lax.axis_index("col")]).astype(jnp.int32)
    smem = pl.BlockSpec(memory_space=pltpu.SMEM)
    vmem = pl.BlockSpec(memory_space=pltpu.VMEM)
    params = pltpu.CompilerParams(vmem_limit_bytes=16 * 2**20)
    scale = layer_scale_factor.reshape(1, channels)
    first, second = first_projector.T, second_projector.T
    wturn = jnp.transpose(output_weight.reshape(width, width, pair_width), (1, 0, 2)).reshape(
        outer_width, pair_width
    )
    shape = jax.ShapeDtypeStruct
    sent, scale, first, second, gain, normed, scaled, inv = pl.pallas_call(
        pre_kernel,
        out_shape=(
            shape((1, rows + 2 * per, pair_width), bf16),
            shape((1, channels), f32),
            shape((width, channels), bf16),
            shape((width, channels), bf16),
            shape((1, pair_width), f32),
            shape((seqs * res, channels), bf16),
            shape((seqs * res, channels), f32),
            shape((seqs * res, 1), f32),
        ),
        in_specs=[smem] + [pl.BlockSpec(memory_space=pltpu.HBM)] * 9,
        out_specs=[vmem] * 8,
        scratch_shapes=[
            pltpu.VMEM((2, seqs * res, lanes), f32),
            pltpu.VMEM((MASK_ROWS, lanes), f32),
            pltpu.VMEM((seqs, res, channels), bf16),
            pltpu.VMEM((res, seqs), jnp.int32),
            pltpu.VMEM((res, pair_cols), jnp.int32),
            pltpu.SemaphoreType.DMA((9,)),
        ],
        compiler_params=params,
        name="project",
    )(
        ids,
        *[
            pltpu.with_memory_space_constraint(array, pltpu.HBM)
            for array in (
                alignment_activations,
                alignment_mask.T,
                pair_update_mask,
                scale,
                first,
                second,
                pair_norm_gain.reshape(1, pair_width),
                pair_activation_input.reshape(per, pair_width),
                pair_output_gradient.reshape(per, pair_width),
            )
        ],
    )
    blocks = lax.optimization_barrier(
        jnp.concatenate([sent] + [swap_col(sent, partner) for partner in Z_PARTNERS])
    )
    far_normed = swap_col(normed, Y_PARTNER)
    blocks, far_normed = lax.optimization_barrier((blocks, far_normed))
    near, pair_near = blocks[:, :rows], blocks[:, rows:]
    far = swap_col(near, Y_PARTNER)
    pair_far = swap_col(pair_near, Y_PARTNER)
    other_near, other_far = swap_depth(near), swap_depth(far)
    sizes = (seqs, res, pair_cols, width)
    outer, proj_out, cnt, pm, maskt, rightt, leftt = pl.pallas_call(
        functools.partial(outer_kernel, sizes),
        out_shape=(
            shape((half, outer_width), bf16),
            shape((half, pair_width), f32),
            shape((half, lanes), f32),
            shape((half, lanes), bf16),
            shape((residues, depths * seqs), f32),
            shape((residues * width, depths * seqs), bf16),
            shape((residues * width, depths * seqs), bf16),
        ),
        in_specs=[smem] + [vmem] * 5,
        out_specs=[vmem] * 7,
        scratch_shapes=[
            pltpu.VMEM((depths * seqs, residues * width), bf16),
            pltpu.VMEM((pair_cols * width, depths * seqs), bf16),
            pltpu.VMEM((residues * width, depths * seqs), f32),
            pltpu.VMEM((residues * width, depths * seqs), f32),
            pltpu.VMEM((half, lanes), bf16),
            pltpu.VMEM((half, lanes), bf16),
        ],
        compiler_params=params,
        name="outer_products",
    )(ids, near, far, other_near, other_far, wturn)

    def transition(near, blocks):
        rows_out = line * per
        return pl.pallas_call(
            functools.partial(transition_kernel, sizes, near),
            out_shape=(
                shape((rows_out, pair_width), bf16),
                shape((rows_out, pair_width), bf16),
                shape((rows_out, hid), bf16),
                shape((rows_out, hid), bf16),
                shape((rows_out, pair_width), bf16),
            )
            + ((shape((per, pair_width), bf16),) if near else ()),
            in_specs=[smem] + [vmem] * 7,
            out_specs=[vmem] * (6 if near else 5),
            scratch_shapes=[pltpu.VMEM((rows_out, pair_width), bf16)] if near else [],
            compiler_params=params,
            name="transition",
        )(ids, blocks, proj_out, cnt, pm, gain, hidden_weight, back_weight)

    *near_arrays, couple = transition(True, pair_near)
    pair_far, near_arrays = lax.optimization_barrier((pair_far, near_arrays))
    far_arrays = transition(False, pair_far)
    opm = jnp.concatenate([near_arrays[0], far_arrays[0]])
    weights = pl.pallas_call(
        weights_kernel,
        out_shape=shape((outer_width + 2 * hid, pair_width), bf16),
        in_specs=[smem] + [vmem] * 11,
        out_specs=vmem,
        scratch_shapes=[pltpu.VMEM((outer_width, pair_width), f32)],
        compiler_params=params,
        name="weight_gradients",
    )(ids, outer, *near_arrays, *far_arrays)
    other_opm, other_normed, other_far_normed, weights = lax.optimization_barrier(
        (swap_depth(opm), swap_depth(normed), swap_depth(far_normed), weights)
    )
    part, spread = pl.pallas_call(
        functools.partial(projector_kernel, sizes),
        out_shape=(
            shape((2 * width, channels), bf16),
            shape((seqs * res, 2 * lanes), bf16),
        ),
        in_specs=[smem] + [vmem] * 11,
        out_specs=[vmem] * 2,
        scratch_shapes=[
            pltpu.VMEM((half, pair_width), f32),
            pltpu.VMEM((2 * res * residues, pair_width), bf16),
            pltpu.VMEM((2 * res * residues, pair_width), bf16),
            pltpu.VMEM((residues * width, 2 * lanes), bf16),
            pltpu.VMEM((residues * width, 2 * lanes), bf16),
            pltpu.VMEM((2, 2, depths, seqs * res, lanes), f32),
            pltpu.VMEM((2, depths, seqs * res, channels), bf16),
        ],
        compiler_params=params,
        name="projector_parts",
    )(
        ids,
        opm,
        other_opm,
        rightt,
        leftt,
        output_weight,
        wturn,
        maskt,
        normed,
        far_normed,
        other_normed,
        other_far_normed,
    )
    feat = pl.pallas_call(
        functools.partial(feature_kernel, res),
        out_shape=shape((seqs * res, channels), bf16),
        in_specs=[vmem] * 6,
        out_specs=vmem,
        compiler_params=params,
        name="features",
    )(spread, first, second, scale, scaled, inv)
    part, weights = lax.optimization_barrier((part, weights))
    dout, dhid, dback = pl.pallas_call(
        weights_sum_kernel,
        out_shape=(
            shape((outer_width, pair_width), f32),
            shape((pair_width, hid), f32),
            shape((hid, pair_width), f32),
        ),
        in_specs=[vmem] * 2,
        out_specs=[vmem] * 3,
        compiler_params=params,
        name="sums_over_depth",
    )(weights, swap_depth(weights))
    came_a = swap_line(part, Z_PARTNERS[:2])
    came_b = swap_line(part, (None, Z_PARTNERS[2]))
    feat = feat.reshape(seqs, res, channels)
    came_a, came_b, feat = lax.optimization_barrier((came_a, came_b, feat))
    kept = jnp.where(lax.axis_index("depth") == 0, part, came_b)
    kept = lax.optimization_barrier((kept.astype(f32) + came_a.astype(f32)).astype(bf16))
    came = swap_depth(kept)
    came, dout, dhid, dback = lax.optimization_barrier((came, dout, dhid, dback))
    total = kept.astype(f32) + came.astype(f32)
    return (
        feat,
        couple.reshape(res, pair_cols, pair_width),
        total[:width].T,
        total[width:].T,
        dout,
        dhid,
        dback,
    )


def on_device(alignment_activations, *others):
    cols = lax.axis_size("col")
    residues = alignment_activations.shape[1] * cols
    plan = whole_plan if cols == 8 and residues <= FEW_RESIDUES else split_plan
    return plan(alignment_activations, *others)


def solution(mesh):
    in_specs = (
        P(("group", "depth"), "col", None),
        P(("group", "depth"), "col"),
        P(("group", "col"), "depth", None),
        P(("group", "col"), "depth"),
        P(("group", "col"), "depth", None),
        P(),
        P(),
        P(),
        P(),
        P(),
        P(),
        P(),
    )
    out_specs = (
        P(("group", "depth"), "col", None),
        P(("group", "col"), "depth", None),
        P("group", None),
        P("group", None),
        P("group", None),
        P("group", None),
        P("group", None),
    )
    return jax.shard_map(
        on_device, mesh=mesh, in_specs=in_specs, out_specs=out_specs, check_vma=False
    )
```

```python
import functools

import jax
import jax.numpy as jnp
from jax import lax
from jax.experimental import pallas as pl
from jax.experimental.pallas import tpu as pltpu
from jax.sharding import PartitionSpec as P

epsilon = 1e-05
highest = lax.Precision.HIGHEST


def norm_pieces(entries_drawn):
    center = entries_drawn - jnp.mean(entries_drawn, axis=-1, keepdims=True)
    inv_std = lax.rsqrt(jnp.mean(center * center, axis=-1, keepdims=True) + epsilon)
    return (center * inv_std, inv_std)


def standardize_adjoint(grad_scaled, scaled, inv_std):
    mean_grad = jnp.mean(grad_scaled, axis=-1, keepdims=True)
    mean_cross = jnp.mean(grad_scaled * scaled, axis=-1, keepdims=True)
    return inv_std * (grad_scaled - mean_grad - scaled * mean_cross)


def silu_pieces(pre_act):
    sigma = jax.nn.sigmoid(pre_act)
    return (pre_act * sigma, sigma * (1.0 + pre_act * (1.0 - sigma)))


def split_plan(
    alignment_activations,
    alignment_mask,
    pair_activation_input,
    pair_update_mask,
    pair_output_gradient,
    layer_scale_factor,
    first_projector,
    second_projector,
    output_weight,
    pair_norm_gain,
    hidden_weight,
    back_weight,
):
    sequence_row_block, residue_row_block, channel_total = alignment_activations.shape
    proj_width = first_projector.shape[1]
    outer_width = proj_width * proj_width
    depth_count = lax.axis_size("depth")
    residues = residue_row_block * lax.axis_size("col")
    pair_cols = pair_activation_input.shape[1]
    pair_width = pair_activation_input.shape[2]
    col_block = min(64, pair_cols)
    block_count = pair_cols // col_block
    standardized_features, reciprocal_spread = norm_pieces(
        alignment_activations.astype(jnp.float32)
    )
    normalized_rows = (standardized_features * layer_scale_factor).astype(jnp.bfloat16)
    mask_floating = alignment_mask.astype(jnp.float32)
    left_proj = (
        jnp.dot(normalized_rows, first_projector, preferred_element_type=jnp.float32)
        * mask_floating[:, :, None]
    ).astype(jnp.bfloat16)
    right_proj = (
        jnp.dot(normalized_rows, second_projector, preferred_element_type=jnp.float32)
        * mask_floating[:, :, None]
    ).astype(jnp.bfloat16)
    right_flat = right_proj.reshape(sequence_row_block, residue_row_block * proj_width)
    mask_converted = alignment_mask.astype(jnp.bfloat16)
    seq_total = left_proj.shape[0]
    gathered, gathered_mask = (
        lax.all_gather(right_flat, "col", axis=1, tiled=True),
        lax.all_gather(mask_converted, "col", axis=1, tiled=True),
    )
    right_blocks = gathered.reshape(seq_total, depth_count, pair_cols, proj_width)
    mask_blocks = gathered_mask.reshape(seq_total, depth_count, pair_cols)
    block_depth = right_blocks.shape[1]
    out_wide = output_weight.astype(jnp.float32)

    def partial_outer(col_start):
        right_piece = lax.dynamic_slice_in_dim(right_blocks, col_start, col_block, 2)
        outer_part = jnp.einsum(
            "sic,sejd->iejcd", left_proj, right_piece, preferred_element_type=jnp.float32
        )
        return (
            outer_part.reshape(residue_row_block, block_depth, col_block, outer_width),
            right_piece,
        )

    def forward_step(step_index, loop_state):
        projected, pair_count = loop_state
        col_start = step_index * col_block
        outer_part, right_piece = partial_outer(col_start)
        mask_piece = lax.dynamic_slice_in_dim(mask_blocks, col_start, col_block, 2).astype(
            jnp.float32
        )
        count_part = jnp.einsum("si,sej->iej", mask_floating, mask_piece, precision=highest)
        outer_mine, count_mine = (
            lax.psum_scatter(
                outer_part.astype(jnp.bfloat16), "depth", scatter_dimension=1, tiled=True
            ).astype(jnp.float32),
            lax.psum_scatter(
                count_part.astype(jnp.bfloat16), "depth", scatter_dimension=1, tiled=True
            ).astype(jnp.float32),
        )
        proj_mine = jnp.dot(
            outer_mine.reshape(residue_row_block * col_block, outer_width),
            out_wide,
            precision=highest,
        )
        proj_mine = proj_mine.reshape(residue_row_block, col_block, pair_width)
        count_mine = count_mine.reshape(residue_row_block, col_block)
        projected = lax.dynamic_update_slice_in_dim(projected, proj_mine, col_start, 1)
        pair_count = lax.dynamic_update_slice_in_dim(pair_count, count_mine, col_start, 1)
        return (projected, pair_count)

    projected, pair_count = lax.fori_loop(
        0,
        block_count,
        forward_step,
        (
            jnp.zeros((residue_row_block, pair_cols, pair_width), jnp.float32),
            jnp.zeros((residue_row_block, pair_cols), jnp.float32),
        ),
    )
    count_column = pair_count.reshape(residue_row_block * pair_cols, 1)
    mid_act = (
        pair_activation_input.reshape(residue_row_block * pair_cols, pair_width).astype(jnp.float32)
        + projected.reshape(residue_row_block * pair_cols, pair_width) / count_column
    )
    pair_scaled, pair_inv = norm_pieces(mid_act)
    pair_normed = (pair_scaled * pair_norm_gain).astype(jnp.bfloat16)
    pre_act = jnp.dot(pair_normed, hidden_weight, preferred_element_type=jnp.float32)
    act_value, act_slope = silu_pieces(pre_act)
    hidden = act_value.astype(jnp.bfloat16)
    masked_grad = (
        pair_output_gradient * pair_update_mask.astype(jnp.bfloat16)[:, :, None]
    ).reshape(residue_row_block * pair_cols, pair_width)
    final_matrix_derivative = jnp.dot(hidden.T, masked_grad, preferred_element_type=jnp.float32)
    back_prod = jnp.dot(masked_grad, back_weight.T, preferred_element_type=jnp.float32)
    grad_hidden = (back_prod * act_slope).astype(jnp.bfloat16)
    middle_matrix_derivative = jnp.dot(
        pair_normed.T, grad_hidden, preferred_element_type=jnp.float32
    )
    grad_scaled = (
        jnp.dot(grad_hidden, hidden_weight.T, preferred_element_type=jnp.float32) * pair_norm_gain
    )
    grad_mid = pair_output_gradient.reshape(residue_row_block * pair_cols, pair_width).astype(
        jnp.float32
    ) + standardize_adjoint(grad_scaled, pair_scaled, pair_inv)
    couple_features_derivative = grad_mid.astype(jnp.bfloat16).reshape(
        residue_row_block, pair_cols, pair_width
    )
    grad_opm = (
        (grad_mid / count_column)
        .astype(jnp.bfloat16)
        .reshape(residue_row_block, pair_cols, pair_width)
    )
    full_opm = lax.all_gather(grad_opm, "depth", axis=1, tiled=True).reshape(
        residue_row_block, depth_count, pair_cols, pair_width
    )

    def backward_step(step_index, loop_state):
        grad_left_acc, grad_out, right_term = loop_state
        col_start = step_index * col_block
        outer_part, right_piece = partial_outer(col_start)
        opm_piece = lax.dynamic_slice_in_dim(full_opm, col_start, col_block, 2).reshape(
            residue_row_block * block_depth * col_block, pair_width
        )
        grad_out = grad_out + jnp.dot(
            outer_part.reshape(residue_row_block * block_depth * col_block, outer_width).T,
            opm_piece.astype(jnp.float32),
            precision=highest,
        )
        grad_outer = jnp.dot(opm_piece, output_weight.T, preferred_element_type=jnp.float32).astype(
            jnp.bfloat16
        )
        grad_outer = grad_outer.reshape(
            residue_row_block, block_depth, col_block, proj_width, proj_width
        )
        grad_left_acc = grad_left_acc + jnp.einsum(
            "iejcd,sejd->sic", grad_outer, right_piece, preferred_element_type=jnp.float32
        )
        piece_term = jnp.einsum(
            "iejcd,sic->ejsd", grad_outer, left_proj, preferred_element_type=jnp.float32
        )
        piece_term = piece_term.reshape(block_depth, col_block, seq_total * proj_width)
        right_term = lax.dynamic_update_slice_in_dim(right_term, piece_term, col_start, 1)
        return (grad_left_acc, grad_out, right_term)

    grad_left_acc, result_matrix_derivative, right_term = lax.fori_loop(
        0,
        block_count,
        backward_step,
        (
            jnp.zeros((seq_total, residue_row_block, proj_width), jnp.float32),
            jnp.zeros((outer_width, pair_width), jnp.float32),
            jnp.zeros((block_depth, pair_cols, seq_total * proj_width), jnp.float32),
        ),
    )
    grad_right_sum = lax.psum_scatter(
        right_term.reshape(residues, seq_total * proj_width), "col", scatter_dimension=0, tiled=True
    )
    grad_right_acc = jnp.transpose(
        grad_right_sum.reshape(residue_row_block, seq_total, proj_width), (1, 0, 2)
    )
    grad_left = (grad_left_acc * mask_floating[:, :, None]).astype(jnp.bfloat16)
    grad_right = (grad_right_acc * mask_floating[:, :, None]).astype(jnp.bfloat16)
    normed_rows = normalized_rows.reshape(sequence_row_block * residue_row_block, channel_total)
    first_projector_derivative = jnp.dot(
        normed_rows.T,
        grad_left.reshape(sequence_row_block * residue_row_block, proj_width),
        preferred_element_type=jnp.float32,
    )
    second_projector_derivative = jnp.dot(
        normed_rows.T,
        grad_right.reshape(sequence_row_block * residue_row_block, proj_width),
        preferred_element_type=jnp.float32,
    )
    standardized_derivative = jnp.dot(
        grad_left, first_projector.T, preferred_element_type=jnp.float32
    ) + jnp.dot(grad_right, second_projector.T, preferred_element_type=jnp.float32)
    features_derivative = standardize_adjoint(
        standardized_derivative * layer_scale_factor, standardized_features, reciprocal_spread
    ).astype(jnp.bfloat16)
    weight_sums = lax.psum(
        (
            first_projector_derivative,
            second_projector_derivative,
            result_matrix_derivative,
            middle_matrix_derivative,
            final_matrix_derivative,
        ),
        ("depth", "col"),
    )
    return (
        features_derivative,
        couple_features_derivative,
        weight_sums[0],
        weight_sums[1],
        weight_sums[2],
        weight_sums[3],
        weight_sums[4],
    )


FEW_RESIDUES = 32
MASK_ROWS = 16
Z_PARTNERS = (6, 4, 2)
Y_PARTNER = 1


def butterfly(blocks, group):
    lane_group = lax.broadcasted_iota(jnp.int32, blocks[0].shape, 1) // group
    width = 4 * group
    for bit in (2, 1):
        low = (lane_group & bit) == 0
        swapped = list(blocks)
        for at in range(4):
            if at & bit:
                continue
            here, there = blocks[at], blocks[at | bit]
            moving = jnp.where(low, there, here)
            if bit == 2:
                moved = pltpu.roll(moving, 2 * group, 1)
            else:
                moved = jnp.where(
                    low, pltpu.roll(moving, width - group, 1), pltpu.roll(moving, group, 1)
                )
            swapped[at] = jnp.where(low, here, moved)
            swapped[at | bit] = jnp.where(low, moved, there)
        blocks = swapped
    return blocks


def wide_projector(first_ref, second_ref, copies):
    return jnp.concatenate([first_ref[...]] * copies + [second_ref[...]] * copies, axis=0)


def pre_kernel(
    ids_ref,
    x_hbm,
    maskt_hbm,
    pmask_hbm,
    scale_hbm,
    first_hbm,
    second_hbm,
    gain_hbm,
    act_hbm,
    grad_hbm,
    sent_ref,
    scale_ref,
    first_ref,
    second_ref,
    gain_ref,
    normed_ref,
    scaled_ref,
    inv_ref,
    wide_ref,
    tile_ref,
    x_ref,
    maskt_ref,
    pmask_ref,
    sems,
):
    res, seqs = maskt_ref.shape
    pairs = act_hbm.shape[0]
    first_pair = 2 * seqs + MASK_ROWS
    copies = [
        pltpu.make_async_copy(source, target, sems.at[at])
        for at, (source, target) in enumerate(
            (
                (x_hbm, x_ref),
                (maskt_hbm, maskt_ref),
                (pmask_hbm, pmask_ref),
                (scale_hbm, scale_ref),
                (first_hbm, first_ref),
                (second_hbm, second_ref),
                (gain_hbm, gain_ref),
                (act_hbm, sent_ref.at[0, pl.ds(first_pair, pairs), :]),
                (grad_hbm, sent_ref.at[0, pl.ds(first_pair + pairs, pairs), :]),
            )
        )
    ]
    for copy in copies:
        copy.start()
    for copy in copies:
        copy.wait()
    lanes = sent_ref.shape[2]
    group = lanes // res
    scaled, inv = norm_pieces(
        x_ref[...].astype(jnp.float32).reshape(seqs * res, x_ref.shape[2])
    )
    scaled_ref[...] = scaled
    inv_ref[...] = inv
    normed = (scaled * scale_ref[...]).astype(jnp.bfloat16)
    normed_ref[...] = normed
    wide = lax.dot_general(
        normed,
        wide_projector(first_ref, second_ref, res),
        (((1,), (1,)), ((), ())),
        preferred_element_type=jnp.float32,
    )
    for at in range(2):
        wide_ref[at] = wide[:, at * lanes : (at + 1) * lanes]
    tile_ref[...] = jnp.zeros(tile_ref.shape, jnp.float32)
    mask = maskt_ref[...].astype(jnp.float32)
    tile_ref[0:res, 0:seqs] = mask
    spread = (
        lax.broadcasted_iota(jnp.int32, (MASK_ROWS, lanes), 1) // group
        == lax.broadcasted_iota(jnp.int32, (MASK_ROWS, lanes), 0)
    ).astype(jnp.float32)
    mask_lanes = lax.dot_general(
        tile_ref[...], spread, (((0,), (0,)), ((), ())), preferred_element_type=jnp.float32
    )[:seqs]
    twice = jnp.concatenate([mask] * (lanes // seqs), axis=1)
    here = lax.broadcasted_iota(jnp.int32, (res, lanes), 1) // seqs == ids_ref[0]
    tile_ref[0:res, :] = jnp.where(here, twice, 0.0)
    tile_ref[res : 2 * res, 0 : pmask_ref.shape[1]] = pmask_ref[...].astype(jnp.float32)
    lane_group = lax.broadcasted_iota(jnp.int32, (seqs, lanes), 1) // group
    for at in range(2):
        both = wide_ref[at, pl.ds(0, seqs, stride=res), :]
        for r in range(1, res):
            both = jnp.where(
                lane_group == r, wide_ref[at, pl.ds(r, seqs, stride=res), :], both
            )
        sent_ref[0, at * seqs : (at + 1) * seqs, :] = (both * mask_lanes).astype(jnp.bfloat16)
    sent_ref[0, 2 * seqs : first_pair, :] = tile_ref[...].astype(jnp.bfloat16)


def by_owner(ids_ref, z, near_ref, far_ref):
    step = z ^ (ids_ref[1] // 2)
    place = (near_ref.shape[0] - step) % near_ref.shape[0]
    near, far = near_ref[place], far_ref[place]
    first = ids_ref[1] % 2 == 0
    return jnp.where(first, near, far), jnp.where(first, far, near)


def outer_kernel(
    sizes,
    ids_ref,
    near_ref,
    far_ref,
    other_near_ref,
    other_far_ref,
    wturn_ref,
    outer_ref,
    proj_out_ref,
    cnt_ref,
    pm_ref,
    maskt_ref,
    rightt_ref,
    leftt_ref,
    leftn_ref,
    mine_ref,
    turnl_ref,
    turnr_ref,
    cntl_ref,
    pml_ref,
):
    seqs, res, pair_cols, width = sizes
    line = near_ref.shape[0]
    cols = 2 * line
    residues = cols * res
    lanes = res * width
    me_depth = ids_ref[0]
    lower = me_depth == 0
    f32, bf16 = jnp.float32, jnp.bfloat16

    for z in range(line):
        mine = by_owner(ids_ref, z, near_ref, far_ref)
        other = by_owner(ids_ref, z, other_near_ref, other_far_ref)
        for y in range(2):
            lanes_k = slice((2 * z + y) * lanes, (2 * z + y + 1) * lanes)
            both = jnp.concatenate(
                [
                    jnp.where(lower, mine[y], other[y]),
                    jnp.where(lower, other[y], mine[y]),
                ],
                axis=0,
            )
            rows = both.shape[0] // 2
            left = jnp.concatenate([both[0:seqs], both[rows : rows + seqs]], axis=0)
            right = jnp.concatenate(
                [both[seqs : 2 * seqs], both[rows + seqs : rows + 2 * seqs]], axis=0
            )
            leftn_ref[:, lanes_k] = left
            turnl_ref[lanes_k, :] = left.astype(f32).T
            turnr_ref[lanes_k, :] = right.astype(f32).T
            tiles = [
                both[first + 2 * seqs : first + 2 * seqs + MASK_ROWS].astype(f32)
                for first in (0, rows)
            ]
            maskt_ref[(2 * z + y) * res : (2 * z + y + 1) * res, :] = (
                tiles[0][0:res] + tiles[1][0:res]
            )
            own = mine[y][2 * seqs : 2 * seqs + MASK_ROWS].astype(f32)
            pair_lane = lax.broadcasted_iota(jnp.int32, (pair_cols, lanes), 1)
            pair_row = lax.broadcasted_iota(jnp.int32, (pair_cols, lanes), 0)
            for r in range(res):
                first = ((2 * z + y) * res + r) * pair_cols
                pml_ref[first : first + pair_cols, :] = jnp.where(
                    pair_lane == pair_row, own[res + r : res + r + 1, :], 0.0
                ).astype(bf16)
    for d in range(width):
        mine_ref[d * pair_cols : (d + 1) * pair_cols, :] = turnr_ref[
            pl.ds(me_depth * pair_cols * width + d, pair_cols, stride=width), :
        ].astype(bf16)
    for turned, out in ((turnl_ref, leftt_ref), (turnr_ref, rightt_ref)):
        for d in range(width):
            out[d * residues : (d + 1) * residues, :] = turned[
                pl.ds(d, residues, stride=width), :
            ].astype(bf16)

    maskt = maskt_ref[...]
    cols_mask = maskt_ref[pl.ds(pl.multiple_of(me_depth * pair_cols, pair_cols), pair_cols), :]
    for i in range(residues):
        cntl_ref[i * pair_cols : (i + 1) * pair_cols, :] = (maskt[i : i + 1, :] * cols_mask).astype(
            bf16
        )
    ones = jnp.ones((lanes, lanes), bf16)
    cnt_ref[...] = jnp.dot(cntl_ref[...], ones, preferred_element_type=f32)
    pm_ref[...] = jnp.dot(pml_ref[...], ones, preferred_element_type=f32).astype(bf16)

    for dh in range(width // 4):
        prod = jnp.dot(
            mine_ref[dh * 4 * pair_cols : (dh + 1) * 4 * pair_cols, :],
            leftn_ref[...],
            preferred_element_type=f32,
        )
        for k in range(cols):
            piece = prod[:, k * lanes : (k + 1) * lanes]
            turned = butterfly(
                [piece[a * pair_cols : (a + 1) * pair_cols] for a in range(4)], width
            )
            for il in range(res):
                first = (k * res + il) * pair_cols
                outer_ref[first : first + pair_cols, dh * lanes : (dh + 1) * lanes] = turned[
                    il
                ].astype(bf16)
    proj_out_ref[...] = jnp.dot(outer_ref[...], wturn_ref[...], preferred_element_type=f32)


def transition_kernel(
    sizes,
    ids_ref,
    near_ref,
    far_ref,
    proj_out_ref,
    cnt_ref,
    pm_ref,
    gain_ref,
    hid_ref,
    back_ref,
    couple_ref,
    opm_ref,
    pn_ref,
    gh_ref,
    hidden_ref,
    mg_ref,
    gmid_ref,
):
    seqs, res, pair_cols, width = sizes
    per = res * pair_cols
    cols = 2 * near_ref.shape[0]
    me_col = ids_ref[1]
    f32, bf16 = jnp.float32, jnp.bfloat16
    gain = gain_ref[...]
    chunk = 2 * per
    for at in range(cols // 2):
        rows = slice(at * chunk, (at + 1) * chunk)
        blocks = by_owner(ids_ref, at, near_ref, far_ref)
        act, grad = [
            jnp.concatenate([block[w * per : (w + 1) * per] for block in blocks], axis=0)
            for w in range(2)
        ]
        count = cnt_ref[rows, :]
        mid = act.astype(f32) + proj_out_ref[rows, :] / count
        scaled, inv = norm_pieces(mid)
        normed = (scaled * gain).astype(bf16)
        pn_ref[rows, :] = normed
        pre = jnp.dot(normed, hid_ref[...], preferred_element_type=f32)
        value, slope = silu_pieces(pre)
        hidden_ref[rows, :] = value.astype(bf16)
        masked = grad * pm_ref[rows, :]
        mg_ref[rows, :] = masked
        back = lax.dot_general(
            masked, back_ref[...], (((1,), (1,)), ((), ())), preferred_element_type=f32
        )
        ghid = (back * slope).astype(bf16)
        gh_ref[rows, :] = ghid
        gsc = (
            lax.dot_general(
                ghid, hid_ref[...], (((1,), (1,)), ((), ())), preferred_element_type=f32
            )
            * gain
        )
        gmid = grad.astype(f32) + standardize_adjoint(gsc, scaled, inv)
        gmid_ref[rows, :] = gmid
        opm_ref[rows, :] = (gmid / count).astype(bf16)
    couple_ref[...] = gmid_ref[pl.ds(pl.multiple_of(me_col * per, per), per), :].astype(bf16)


def projector_kernel(
    sizes,
    ids_ref,
    opm_ref,
    other_opm_ref,
    rightt_ref,
    leftt_ref,
    wout_ref,
    wturn_ref,
    maskt_ref,
    normed_ref,
    far_normed_ref,
    other_normed_ref,
    other_far_normed_ref,
    part_ref,
    spread_ref,
    gf_ref,
    grow_ref,
    gcol_ref,
    gor_ref,
    goc_ref,
    gs_ref,
    rows_ref,
):
    seqs, res, pair_cols, width = sizes
    depths, half = rows_ref.shape[1], gf_ref.shape[0]
    residues = half // pair_cols
    lanes = res * width
    here = 2 * res
    me_depth = ids_ref[0]
    me_col = ids_ref[1]
    me_y = me_col % 2
    first_here = (me_col // 2) * here
    f32, bf16 = jnp.float32, jnp.bfloat16
    my_half = first_here // pair_cols
    gf_ref[...] = jnp.where(my_half == me_depth, opm_ref[...], other_opm_ref[...]).astype(f32)
    for y, e, block in (
        (me_y, me_depth, normed_ref),
        (1 - me_y, me_depth, far_normed_ref),
        (me_y, 1 - me_depth, other_normed_ref),
        (1 - me_y, 1 - me_depth, other_far_normed_ref),
    ):
        rows_ref[y, e] = block[...]

    for il in range(here):
        first = pl.multiple_of((first_here + il) * pair_cols, pair_cols)
        for e, block in ((me_depth, opm_ref), (1 - me_depth, other_opm_ref)):
            to = pl.multiple_of(il * residues + e * pair_cols, pair_cols)
            grow_ref[pl.ds(to, pair_cols), :] = block[pl.ds(first, pair_cols), :]
    my_first = first_here - my_half * pair_cols
    for jl in range(here):
        gcol_ref[jl * residues : (jl + 1) * residues, :] = gf_ref[
            pl.ds(my_first + jl, residues, stride=pair_cols), :
        ].astype(bf16)
    for lhs, weight, out in ((grow_ref, wturn_ref, gor_ref), (gcol_ref, wout_ref, goc_ref)):
        for dh in range(width // 4):
            piece = lax.dot_general(
                lhs[...],
                weight[dh * lanes : (dh + 1) * lanes, :],
                (((1,), (1,)), ((), ())),
                preferred_element_type=f32,
            )
            for y in range(2):
                turned = butterfly(
                    [
                        piece[(y * res + a) * residues : (y * res + a + 1) * residues]
                        for a in range(4)
                    ],
                    width,
                )
                for dl in range(4):
                    first = (dh * 4 + dl) * residues
                    out[first : first + residues, y * lanes : (y + 1) * lanes] = turned[dl].astype(
                        bf16
                    )
    group = lax.broadcasted_iota(jnp.int32, (here, here * width), 1) // width
    spread = (group == lax.broadcasted_iota(jnp.int32, (here, here * width), 0)).astype(f32)
    mask_lanes = lax.dot_general(
        maskt_ref[pl.ds(pl.multiple_of(first_here, here), here), :],
        spread,
        (((0,), (0,)), ((), ())),
        preferred_element_type=f32,
    )
    lane_group = lax.broadcasted_iota(jnp.int32, (seqs, lanes), 1) // width
    for at, (lhs, rhs) in enumerate(((rightt_ref, gor_ref), (leftt_ref, goc_ref))):
        total = lax.dot_general(
            lhs[...], rhs[...], (((0,), (0,)), ((), ())), preferred_element_type=f32
        )
        total = (total * mask_lanes).astype(bf16).astype(f32)
        for y in range(2):
            for e in range(depths):
                block = total[e * seqs : (e + 1) * seqs, y * lanes : (y + 1) * lanes]
                for r in range(res):
                    gs_ref[at, y, e, pl.ds(r, seqs, stride=res), :] = jnp.where(
                        lane_group == r, block, 0.0
                    )
    spread_ref[...] = jnp.concatenate(
        [gs_ref[0, me_y, me_depth], gs_ref[1, me_y, me_depth]], axis=1
    ).astype(bf16)
    rows = rows_ref.shape[2]
    for at in range(2):
        cross = lax.dot_general(
            gs_ref[at].reshape(2 * depths * rows, lanes).astype(bf16),
            rows_ref[...].reshape(2 * depths * rows, rows_ref.shape[3]),
            (((0,), (0,)), ((), ())),
            preferred_element_type=f32,
        )
        total = cross[:width]
        for r in range(1, res):
            total = total + cross[r * width : (r + 1) * width]
        part_ref[at * width : (at + 1) * width, :] = total.astype(bf16)


def weights_kernel(outer_ref, opm_ref, pn_ref, gh_ref, hidden_ref, mg_ref, out_ref, turn_ref):
    pair_width, hid = pn_ref.shape[1], gh_ref.shape[1]
    outer_width = outer_ref.shape[1]
    width = int(outer_width**0.5 + 0.5)

    def contract(lhs, rhs):
        return lax.dot_general(
            lhs[...], rhs[...], (((0,), (0,)), ((), ())), preferred_element_type=jnp.float32
        )

    turn_ref[...] = contract(outer_ref, opm_ref)
    for c in range(width):
        out_ref[c * width : (c + 1) * width, :] = turn_ref[
            pl.ds(c, width, stride=width), :
        ].astype(jnp.bfloat16)
    dhid = contract(pn_ref, gh_ref).astype(jnp.bfloat16)
    for at in range(hid // pair_width):
        first = outer_width + at * pair_width
        out_ref[first : first + pair_width, :] = dhid[:, at * pair_width : (at + 1) * pair_width]
    out_ref[outer_width + hid :, :] = contract(hidden_ref, mg_ref).astype(jnp.bfloat16)


def weights_sum_kernel(mine_ref, other_ref, dout_ref, dhid_ref, dback_ref):
    pair_width, hid = dhid_ref.shape
    outer_width = dout_ref.shape[0]

    def added(first, count):
        rows = slice(first, first + count)
        return mine_ref[rows, :].astype(jnp.float32) + other_ref[rows, :].astype(jnp.float32)

    dout_ref[...] = added(0, outer_width)
    for at in range(hid // pair_width):
        dhid_ref[:, at * pair_width : (at + 1) * pair_width] = added(
            outer_width + at * pair_width, pair_width
        )
    dback_ref[...] = added(outer_width + hid, hid)


def feature_kernel(
    copies,
    spread_ref,
    first_ref,
    second_ref,
    scale_ref,
    scaled_ref,
    inv_ref,
    held_ref,
    feat_ref,
    couple_ref,
):
    back = jnp.dot(
        spread_ref[...],
        wide_projector(first_ref, second_ref, copies),
        preferred_element_type=jnp.float32,
    )
    feat_ref[...] = standardize_adjoint(
        back * scale_ref[...], scaled_ref[...], inv_ref[...]
    ).astype(jnp.bfloat16)
    couple_ref[...] = held_ref[...]


def swap_line(block, partners):
    count = lax.axis_size("col")
    pairs = [
        (depth * count + at, depth * count + (at ^ partner))
        for depth, partner in enumerate(partners)
        if partner is not None
        for at in range(count)
    ]
    return lax.ppermute(block, ("depth", "col"), pairs)


def swap_depth(block):
    return lax.ppermute(block, "depth", [(0, 1), (1, 0)])


def pairwise_sum(blocks):
    while len(blocks) > 1:
        blocks = [blocks[at] + blocks[at + 1] for at in range(0, len(blocks), 2)]
    return blocks[0]


def swap_col(block, partner):
    count = lax.axis_size("col")
    return lax.ppermute(block, "col", [(at, at ^ partner) for at in range(count)])


def whole_plan(
    alignment_activations,
    alignment_mask,
    pair_activation_input,
    pair_update_mask,
    pair_output_gradient,
    layer_scale_factor,
    first_projector,
    second_projector,
    output_weight,
    pair_norm_gain,
    hidden_weight,
    back_weight,
):
    seqs, res, channels = alignment_activations.shape
    width = first_projector.shape[1]
    outer_width = width * width
    cols = lax.axis_size("col")
    depths = lax.axis_size("depth")
    residues = res * cols
    pair_cols, pair_width = pair_activation_input.shape[1:]
    hid = hidden_weight.shape[1]
    per = res * pair_cols
    lanes = res * width
    rows = 2 * seqs + MASK_ROWS
    half = residues * pair_cols
    f32, bf16 = jnp.float32, jnp.bfloat16
    ids = jnp.stack([lax.axis_index("depth"), lax.axis_index("col")]).astype(jnp.int32)
    smem = pl.BlockSpec(memory_space=pltpu.SMEM)
    vmem = pl.BlockSpec(memory_space=pltpu.VMEM)
    params = pltpu.CompilerParams(vmem_limit_bytes=16 * 2**20)
    scale = layer_scale_factor.reshape(1, channels)
    first, second = first_projector.T, second_projector.T
    wturn = jnp.transpose(output_weight.reshape(width, width, pair_width), (1, 0, 2)).reshape(
        outer_width, pair_width
    )
    shape = jax.ShapeDtypeStruct
    sent, scale, first, second, gain, normed, scaled, inv = pl.pallas_call(
        pre_kernel,
        out_shape=(
            shape((1, rows + 2 * per, pair_width), bf16),
            shape((1, channels), f32),
            shape((width, channels), bf16),
            shape((width, channels), bf16),
            shape((1, pair_width), f32),
            shape((seqs * res, channels), bf16),
            shape((seqs * res, channels), f32),
            shape((seqs * res, 1), f32),
        ),
        in_specs=[smem] + [pl.BlockSpec(memory_space=pltpu.HBM)] * 9,
        out_specs=[vmem] * 8,
        scratch_shapes=[
            pltpu.VMEM((2, seqs * res, lanes), f32),
            pltpu.VMEM((MASK_ROWS, lanes), f32),
            pltpu.VMEM((seqs, res, channels), bf16),
            pltpu.VMEM((res, seqs), jnp.int32),
            pltpu.VMEM((res, pair_cols), jnp.int32),
            pltpu.SemaphoreType.DMA((9,)),
        ],
        compiler_params=params,
        name="project",
    )(
        ids,
        *[
            pltpu.with_memory_space_constraint(array, pltpu.HBM)
            for array in (
                alignment_activations,
                alignment_mask.T,
                pair_update_mask,
                scale,
                first,
                second,
                pair_norm_gain.reshape(1, pair_width),
                pair_activation_input.reshape(per, pair_width),
                pair_output_gradient.reshape(per, pair_width),
            )
        ],
    )
    blocks = lax.optimization_barrier(
        jnp.concatenate([sent] + [swap_col(sent, partner) for partner in Z_PARTNERS])
    )
    early_rows = seqs * res * 3 // 4
    far_normed_a = swap_col(normed[:early_rows], Y_PARTNER)
    blocks, far_normed_a = lax.optimization_barrier((blocks, far_normed_a))
    near, pair_near = blocks[:, :rows], blocks[:, rows:]
    far = swap_col(near, Y_PARTNER)
    pair_far = swap_col(pair_near, Y_PARTNER)
    other_near, other_far = swap_depth(near), swap_depth(far)
    sizes = (seqs, res, pair_cols, width)
    outer, proj_out, cnt, pm, maskt, rightt, leftt = pl.pallas_call(
        functools.partial(outer_kernel, sizes),
        out_shape=(
            shape((half, outer_width), bf16),
            shape((half, pair_width), f32),
            shape((half, lanes), f32),
            shape((half, lanes), bf16),
            shape((residues, depths * seqs), f32),
            shape((residues * width, depths * seqs), bf16),
            shape((residues * width, depths * seqs), bf16),
        ),
        in_specs=[smem] + [vmem] * 5,
        out_specs=[vmem] * 7,
        scratch_shapes=[
            pltpu.VMEM((depths * seqs, residues * width), bf16),
            pltpu.VMEM((pair_cols * width, depths * seqs), bf16),
            pltpu.VMEM((residues * width, depths * seqs), f32),
            pltpu.VMEM((residues * width, depths * seqs), f32),
            pltpu.VMEM((half, lanes), bf16),
            pltpu.VMEM((half, lanes), bf16),
        ],
        compiler_params=params,
        name="outer_products",
    )(ids, near, far, other_near, other_far, wturn)
    normed_b, proj_out = lax.optimization_barrier((normed[early_rows:], proj_out))
    far_normed_b = swap_col(normed_b, Y_PARTNER)
    pair_far, proj_out = lax.optimization_barrier((pair_far, proj_out))
    held, opm, pn, gh, hidden, mg = pl.pallas_call(
        functools.partial(transition_kernel, sizes),
        out_shape=(
            shape((per, pair_width), bf16),
            shape((half, pair_width), bf16),
            shape((half, pair_width), bf16),
            shape((half, hid), bf16),
            shape((half, hid), bf16),
            shape((half, pair_width), bf16),
        ),
        in_specs=[smem] + [vmem] * 8,
        out_specs=[vmem] * 6,
        scratch_shapes=[
            pltpu.VMEM((half, pair_width), f32),
        ],
        compiler_params=params,
        name="transition",
    )(
        ids,
        pair_near,
        pair_far,
        proj_out,
        cnt,
        pm,
        gain,
        hidden_weight,
        back_weight,
    )
    opm, far_normed_b = lax.optimization_barrier((opm, far_normed_b))
    far_normed = jnp.concatenate([far_normed_a, far_normed_b])
    weights = pl.pallas_call(
        weights_kernel,
        out_shape=shape((outer_width + 2 * hid, pair_width), bf16),
        in_specs=[vmem] * 6,
        out_specs=vmem,
        scratch_shapes=[pltpu.VMEM((outer_width, pair_width), f32)],
        compiler_params=params,
        name="weight_gradients",
    )(outer, opm, pn, gh, hidden, mg)
    other_opm, other_normed, other_far_normed, weights = lax.optimization_barrier(
        (swap_depth(opm), swap_depth(normed), swap_depth(far_normed), weights)
    )
    part, spread = pl.pallas_call(
        functools.partial(projector_kernel, sizes),
        out_shape=(
            shape((2 * width, channels), bf16),
            shape((seqs * res, 2 * lanes), bf16),
        ),
        in_specs=[smem] + [vmem] * 11,
        out_specs=[vmem] * 2,
        scratch_shapes=[
            pltpu.VMEM((half, pair_width), f32),
            pltpu.VMEM((2 * res * residues, pair_width), bf16),
            pltpu.VMEM((2 * res * residues, pair_width), bf16),
            pltpu.VMEM((residues * width, 2 * lanes), bf16),
            pltpu.VMEM((residues * width, 2 * lanes), bf16),
            pltpu.VMEM((2, 2, depths, seqs * res, lanes), f32),
            pltpu.VMEM((2, depths, seqs * res, channels), bf16),
        ],
        compiler_params=params,
        name="projector_parts",
    )(
        ids,
        opm,
        other_opm,
        rightt,
        leftt,
        output_weight,
        wturn,
        maskt,
        normed,
        far_normed,
        other_normed,
        other_far_normed,
    )
    feat, couple = pl.pallas_call(
        functools.partial(feature_kernel, res),
        out_shape=(shape((seqs * res, channels), bf16), shape((per, pair_width), bf16)),
        in_specs=[vmem] * 7,
        out_specs=[vmem] * 2,
        compiler_params=params,
        name="features",
    )(spread, first, second, scale, scaled, inv, held)
    part, weights = lax.optimization_barrier((part, weights))
    dout, dhid, dback = pl.pallas_call(
        weights_sum_kernel,
        out_shape=(
            shape((outer_width, pair_width), f32),
            shape((pair_width, hid), f32),
            shape((hid, pair_width), f32),
        ),
        in_specs=[vmem] * 2,
        out_specs=[vmem] * 3,
        compiler_params=params,
        name="sums_over_depth",
    )(weights, swap_depth(weights))
    came_a = swap_line(part, Z_PARTNERS[:2])
    came_b = swap_line(part, (None, Z_PARTNERS[2]))
    feat = feat.reshape(seqs, res, channels)
    came_a, came_b, feat, couple = lax.optimization_barrier((came_a, came_b, feat, couple))
    kept = jnp.where(lax.axis_index("depth") == 0, part, came_b)
    kept = lax.optimization_barrier((kept.astype(f32) + came_a.astype(f32)).astype(bf16))
    came = swap_depth(kept)
    came, dout, dhid, dback = lax.optimization_barrier((came, dout, dhid, dback))
    total = kept.astype(f32) + came.astype(f32)
    return (
        feat,
        couple.reshape(res, pair_cols, pair_width),
        total[:width].T,
        total[width:].T,
        dout,
        dhid,
        dback,
    )


def on_device(alignment_activations, *others):
    cols = lax.axis_size("col")
    residues = alignment_activations.shape[1] * cols
    plan = whole_plan if cols == 8 and residues <= FEW_RESIDUES else split_plan
    return plan(alignment_activations, *others)


def solution(mesh):
    in_specs = (
        P(("group", "depth"), "col", None),
        P(("group", "depth"), "col"),
        P(("group", "col"), "depth", None),
        P(("group", "col"), "depth"),
        P(("group", "col"), "depth", None),
        P(),
        P(),
        P(),
        P(),
        P(),
        P(),
        P(),
    )
    out_specs = (
        P(("group", "depth"), "col", None),
        P(("group", "col"), "depth", None),
        P("group", None),
        P("group", None),
        P("group", None),
        P("group", None),
        P("group", None),
    )
    return jax.shard_map(
        on_device, mesh=mesh, in_specs=in_specs, out_specs=out_specs, check_vma=False
    )
```

```python
import functools

import jax
import jax.numpy as jnp
from jax import lax
from jax.experimental import pallas as pl
from jax.experimental.pallas import tpu as pltpu
from jax.sharding import PartitionSpec as P

epsilon = 1e-05
highest = lax.Precision.HIGHEST


def norm_pieces(entries_drawn):
    center = entries_drawn - jnp.mean(entries_drawn, axis=-1, keepdims=True)
    inv_std = lax.rsqrt(jnp.mean(center * center, axis=-1, keepdims=True) + epsilon)
    return (center * inv_std, inv_std)


def standardize_adjoint(grad_scaled, scaled, inv_std):
    mean_grad = jnp.mean(grad_scaled, axis=-1, keepdims=True)
    mean_cross = jnp.mean(grad_scaled * scaled, axis=-1, keepdims=True)
    return inv_std * (grad_scaled - mean_grad - scaled * mean_cross)


def silu_pieces(pre_act):
    sigma = jax.nn.sigmoid(pre_act)
    return (pre_act * sigma, sigma * (1.0 + pre_act * (1.0 - sigma)))


def split_plan(
    alignment_activations,
    alignment_mask,
    pair_activation_input,
    pair_update_mask,
    pair_output_gradient,
    layer_scale_factor,
    first_projector,
    second_projector,
    output_weight,
    pair_norm_gain,
    hidden_weight,
    back_weight,
):
    sequence_row_block, residue_row_block, channel_total = alignment_activations.shape
    proj_width = first_projector.shape[1]
    outer_width = proj_width * proj_width
    depth_count = lax.axis_size("depth")
    residues = residue_row_block * lax.axis_size("col")
    pair_cols = pair_activation_input.shape[1]
    pair_width = pair_activation_input.shape[2]
    col_block = min(64, pair_cols)
    block_count = pair_cols // col_block
    standardized_features, reciprocal_spread = norm_pieces(
        alignment_activations.astype(jnp.float32)
    )
    normalized_rows = (standardized_features * layer_scale_factor).astype(jnp.bfloat16)
    mask_floating = alignment_mask.astype(jnp.float32)
    left_proj = (
        jnp.dot(normalized_rows, first_projector, preferred_element_type=jnp.float32)
        * mask_floating[:, :, None]
    ).astype(jnp.bfloat16)
    right_proj = (
        jnp.dot(normalized_rows, second_projector, preferred_element_type=jnp.float32)
        * mask_floating[:, :, None]
    ).astype(jnp.bfloat16)
    right_flat = right_proj.reshape(sequence_row_block, residue_row_block * proj_width)
    mask_converted = alignment_mask.astype(jnp.bfloat16)
    seq_total = left_proj.shape[0]
    gathered, gathered_mask = (
        lax.all_gather(right_flat, "col", axis=1, tiled=True),
        lax.all_gather(mask_converted, "col", axis=1, tiled=True),
    )
    right_blocks = gathered.reshape(seq_total, depth_count, pair_cols, proj_width)
    mask_blocks = gathered_mask.reshape(seq_total, depth_count, pair_cols)
    block_depth = right_blocks.shape[1]
    out_wide = output_weight.astype(jnp.float32)

    def partial_outer(col_start):
        right_piece = lax.dynamic_slice_in_dim(right_blocks, col_start, col_block, 2)
        outer_part = jnp.einsum(
            "sic,sejd->iejcd", left_proj, right_piece, preferred_element_type=jnp.float32
        )
        return (
            outer_part.reshape(residue_row_block, block_depth, col_block, outer_width),
            right_piece,
        )

    def forward_step(step_index, loop_state):
        projected, pair_count = loop_state
        col_start = step_index * col_block
        outer_part, right_piece = partial_outer(col_start)
        mask_piece = lax.dynamic_slice_in_dim(mask_blocks, col_start, col_block, 2).astype(
            jnp.float32
        )
        count_part = jnp.einsum("si,sej->iej", mask_floating, mask_piece, precision=highest)
        outer_mine, count_mine = (
            lax.psum_scatter(
                outer_part.astype(jnp.bfloat16), "depth", scatter_dimension=1, tiled=True
            ).astype(jnp.float32),
            lax.psum_scatter(
                count_part.astype(jnp.bfloat16), "depth", scatter_dimension=1, tiled=True
            ).astype(jnp.float32),
        )
        proj_mine = jnp.dot(
            outer_mine.reshape(residue_row_block * col_block, outer_width),
            out_wide,
            precision=highest,
        )
        proj_mine = proj_mine.reshape(residue_row_block, col_block, pair_width)
        count_mine = count_mine.reshape(residue_row_block, col_block)
        projected = lax.dynamic_update_slice_in_dim(projected, proj_mine, col_start, 1)
        pair_count = lax.dynamic_update_slice_in_dim(pair_count, count_mine, col_start, 1)
        return (projected, pair_count)

    projected, pair_count = lax.fori_loop(
        0,
        block_count,
        forward_step,
        (
            jnp.zeros((residue_row_block, pair_cols, pair_width), jnp.float32),
            jnp.zeros((residue_row_block, pair_cols), jnp.float32),
        ),
    )
    count_column = pair_count.reshape(residue_row_block * pair_cols, 1)
    mid_act = (
        pair_activation_input.reshape(residue_row_block * pair_cols, pair_width).astype(jnp.float32)
        + projected.reshape(residue_row_block * pair_cols, pair_width) / count_column
    )
    pair_scaled, pair_inv = norm_pieces(mid_act)
    pair_normed = (pair_scaled * pair_norm_gain).astype(jnp.bfloat16)
    pre_act = jnp.dot(pair_normed, hidden_weight, preferred_element_type=jnp.float32)
    act_value, act_slope = silu_pieces(pre_act)
    hidden = act_value.astype(jnp.bfloat16)
    masked_grad = (
        pair_output_gradient * pair_update_mask.astype(jnp.bfloat16)[:, :, None]
    ).reshape(residue_row_block * pair_cols, pair_width)
    final_matrix_derivative = jnp.dot(hidden.T, masked_grad, preferred_element_type=jnp.float32)
    back_prod = jnp.dot(masked_grad, back_weight.T, preferred_element_type=jnp.float32)
    grad_hidden = (back_prod * act_slope).astype(jnp.bfloat16)
    middle_matrix_derivative = jnp.dot(
        pair_normed.T, grad_hidden, preferred_element_type=jnp.float32
    )
    grad_scaled = (
        jnp.dot(grad_hidden, hidden_weight.T, preferred_element_type=jnp.float32) * pair_norm_gain
    )
    grad_mid = pair_output_gradient.reshape(residue_row_block * pair_cols, pair_width).astype(
        jnp.float32
    ) + standardize_adjoint(grad_scaled, pair_scaled, pair_inv)
    couple_features_derivative = grad_mid.astype(jnp.bfloat16).reshape(
        residue_row_block, pair_cols, pair_width
    )
    grad_opm = (
        (grad_mid / count_column)
        .astype(jnp.bfloat16)
        .reshape(residue_row_block, pair_cols, pair_width)
    )
    full_opm = lax.all_gather(grad_opm, "depth", axis=1, tiled=True).reshape(
        residue_row_block, depth_count, pair_cols, pair_width
    )

    def backward_step(step_index, loop_state):
        grad_left_acc, grad_out, right_term = loop_state
        col_start = step_index * col_block
        outer_part, right_piece = partial_outer(col_start)
        opm_piece = lax.dynamic_slice_in_dim(full_opm, col_start, col_block, 2).reshape(
            residue_row_block * block_depth * col_block, pair_width
        )
        grad_out = grad_out + jnp.dot(
            outer_part.reshape(residue_row_block * block_depth * col_block, outer_width).T,
            opm_piece.astype(jnp.float32),
            precision=highest,
        )
        grad_outer = jnp.dot(opm_piece, output_weight.T, preferred_element_type=jnp.float32).astype(
            jnp.bfloat16
        )
        grad_outer = grad_outer.reshape(
            residue_row_block, block_depth, col_block, proj_width, proj_width
        )
        grad_left_acc = grad_left_acc + jnp.einsum(
            "iejcd,sejd->sic", grad_outer, right_piece, preferred_element_type=jnp.float32
        )
        piece_term = jnp.einsum(
            "iejcd,sic->ejsd", grad_outer, left_proj, preferred_element_type=jnp.float32
        )
        piece_term = piece_term.reshape(block_depth, col_block, seq_total * proj_width)
        right_term = lax.dynamic_update_slice_in_dim(right_term, piece_term, col_start, 1)
        return (grad_left_acc, grad_out, right_term)

    grad_left_acc, result_matrix_derivative, right_term = lax.fori_loop(
        0,
        block_count,
        backward_step,
        (
            jnp.zeros((seq_total, residue_row_block, proj_width), jnp.float32),
            jnp.zeros((outer_width, pair_width), jnp.float32),
            jnp.zeros((block_depth, pair_cols, seq_total * proj_width), jnp.float32),
        ),
    )
    grad_right_sum = lax.psum_scatter(
        right_term.reshape(residues, seq_total * proj_width), "col", scatter_dimension=0, tiled=True
    )
    grad_right_acc = jnp.transpose(
        grad_right_sum.reshape(residue_row_block, seq_total, proj_width), (1, 0, 2)
    )
    grad_left = (grad_left_acc * mask_floating[:, :, None]).astype(jnp.bfloat16)
    grad_right = (grad_right_acc * mask_floating[:, :, None]).astype(jnp.bfloat16)
    normed_rows = normalized_rows.reshape(sequence_row_block * residue_row_block, channel_total)
    first_projector_derivative = jnp.dot(
        normed_rows.T,
        grad_left.reshape(sequence_row_block * residue_row_block, proj_width),
        preferred_element_type=jnp.float32,
    )
    second_projector_derivative = jnp.dot(
        normed_rows.T,
        grad_right.reshape(sequence_row_block * residue_row_block, proj_width),
        preferred_element_type=jnp.float32,
    )
    standardized_derivative = jnp.dot(
        grad_left, first_projector.T, preferred_element_type=jnp.float32
    ) + jnp.dot(grad_right, second_projector.T, preferred_element_type=jnp.float32)
    features_derivative = standardize_adjoint(
        standardized_derivative * layer_scale_factor, standardized_features, reciprocal_spread
    ).astype(jnp.bfloat16)
    weight_sums = lax.psum(
        (
            first_projector_derivative,
            second_projector_derivative,
            result_matrix_derivative,
            middle_matrix_derivative,
            final_matrix_derivative,
        ),
        ("depth", "col"),
    )
    return (
        features_derivative,
        couple_features_derivative,
        weight_sums[0],
        weight_sums[1],
        weight_sums[2],
        weight_sums[3],
        weight_sums[4],
    )


FEW_RESIDUES = 32
MASK_ROWS = 16
Z_PARTNERS = (6, 4, 2)
Y_PARTNER = 1


def butterfly(blocks, group):
    lane_group = lax.broadcasted_iota(jnp.int32, blocks[0].shape, 1) // group
    width = 4 * group
    for bit in (2, 1):
        low = (lane_group & bit) == 0
        swapped = list(blocks)
        for at in range(4):
            if at & bit:
                continue
            here, there = blocks[at], blocks[at | bit]
            moving = jnp.where(low, there, here)
            if bit == 2:
                moved = pltpu.roll(moving, 2 * group, 1)
            else:
                moved = jnp.where(
                    low, pltpu.roll(moving, width - group, 1), pltpu.roll(moving, group, 1)
                )
            swapped[at] = jnp.where(low, here, moved)
            swapped[at | bit] = jnp.where(low, moved, there)
        blocks = swapped
    return blocks


def wide_projector(first_ref, second_ref, copies):
    return jnp.concatenate([first_ref[...]] * copies + [second_ref[...]] * copies, axis=0)


def pre_kernel(
    ids_ref,
    x_hbm,
    maskt_hbm,
    pmask_hbm,
    scale_hbm,
    first_hbm,
    second_hbm,
    gain_hbm,
    act_hbm,
    grad_hbm,
    sent_ref,
    scale_ref,
    first_ref,
    second_ref,
    gain_ref,
    normed_ref,
    scaled_ref,
    inv_ref,
    wide_ref,
    tile_ref,
    x_ref,
    maskt_ref,
    pmask_ref,
    sems,
):
    res, seqs = maskt_ref.shape
    pairs = act_hbm.shape[0]
    first_pair = 2 * seqs + MASK_ROWS
    copies = [
        pltpu.make_async_copy(source, target, sems.at[at])
        for at, (source, target) in enumerate(
            (
                (x_hbm, x_ref),
                (maskt_hbm, maskt_ref),
                (pmask_hbm, pmask_ref),
                (scale_hbm, scale_ref),
                (first_hbm, first_ref),
                (second_hbm, second_ref),
                (gain_hbm, gain_ref),
                (act_hbm, sent_ref.at[0, pl.ds(first_pair, pairs), :]),
                (grad_hbm, sent_ref.at[0, pl.ds(first_pair + pairs, pairs), :]),
            )
        )
    ]
    for copy in copies:
        copy.start()
    for copy in copies:
        copy.wait()
    lanes = sent_ref.shape[2]
    group = lanes // res
    scaled, inv = norm_pieces(
        x_ref[...].astype(jnp.float32).reshape(seqs * res, x_ref.shape[2])
    )
    scaled_ref[...] = scaled
    inv_ref[...] = inv
    normed = (scaled * scale_ref[...]).astype(jnp.bfloat16)
    normed_ref[...] = normed
    wide = lax.dot_general(
        normed,
        wide_projector(first_ref, second_ref, res),
        (((1,), (1,)), ((), ())),
        preferred_element_type=jnp.float32,
    )
    for at in range(2):
        wide_ref[at] = wide[:, at * lanes : (at + 1) * lanes]
    tile_ref[...] = jnp.zeros(tile_ref.shape, jnp.float32)
    mask = maskt_ref[...].astype(jnp.float32)
    tile_ref[0:res, 0:seqs] = mask
    spread = (
        lax.broadcasted_iota(jnp.int32, (MASK_ROWS, lanes), 1) // group
        == lax.broadcasted_iota(jnp.int32, (MASK_ROWS, lanes), 0)
    ).astype(jnp.float32)
    mask_lanes = lax.dot_general(
        tile_ref[...], spread, (((0,), (0,)), ((), ())), preferred_element_type=jnp.float32
    )[:seqs]
    twice = jnp.concatenate([mask] * (lanes // seqs), axis=1)
    here = lax.broadcasted_iota(jnp.int32, (res, lanes), 1) // seqs == ids_ref[0]
    tile_ref[0:res, :] = jnp.where(here, twice, 0.0)
    tile_ref[res : 2 * res, 0 : pmask_ref.shape[1]] = pmask_ref[...].astype(jnp.float32)
    lane_group = lax.broadcasted_iota(jnp.int32, (seqs, lanes), 1) // group
    for at in range(2):
        both = wide_ref[at, pl.ds(0, seqs, stride=res), :]
        for r in range(1, res):
            both = jnp.where(
                lane_group == r, wide_ref[at, pl.ds(r, seqs, stride=res), :], both
            )
        sent_ref[0, at * seqs : (at + 1) * seqs, :] = (both * mask_lanes).astype(jnp.bfloat16)
    sent_ref[0, 2 * seqs : first_pair, :] = tile_ref[...].astype(jnp.bfloat16)


def by_owner(ids_ref, z, near_ref, far_ref):
    step = z ^ (ids_ref[1] // 2)
    place = (near_ref.shape[0] - step) % near_ref.shape[0]
    near, far = near_ref[place], far_ref[place]
    first = ids_ref[1] % 2 == 0
    return jnp.where(first, near, far), jnp.where(first, far, near)


def outer_kernel(
    sizes,
    ids_ref,
    near_ref,
    far_ref,
    other_near_ref,
    other_far_ref,
    wturn_ref,
    outer_ref,
    proj_out_ref,
    cnt_ref,
    pm_ref,
    maskt_ref,
    rightt_ref,
    leftt_ref,
    leftn_ref,
    mine_ref,
    turnl_ref,
    turnr_ref,
    cntl_ref,
    pml_ref,
):
    seqs, res, pair_cols, width = sizes
    line = near_ref.shape[0]
    cols = 2 * line
    residues = cols * res
    lanes = res * width
    me_depth = ids_ref[0]
    lower = me_depth == 0
    f32, bf16 = jnp.float32, jnp.bfloat16

    for z in range(line):
        mine = by_owner(ids_ref, z, near_ref, far_ref)
        other = by_owner(ids_ref, z, other_near_ref, other_far_ref)
        for y in range(2):
            lanes_k = slice((2 * z + y) * lanes, (2 * z + y + 1) * lanes)
            both = jnp.concatenate(
                [
                    jnp.where(lower, mine[y], other[y]),
                    jnp.where(lower, other[y], mine[y]),
                ],
                axis=0,
            )
            rows = both.shape[0] // 2
            left = jnp.concatenate([both[0:seqs], both[rows : rows + seqs]], axis=0)
            right = jnp.concatenate(
                [both[seqs : 2 * seqs], both[rows + seqs : rows + 2 * seqs]], axis=0
            )
            leftn_ref[:, lanes_k] = left
            turnl_ref[lanes_k, :] = left.astype(f32).T
            turnr_ref[lanes_k, :] = right.astype(f32).T
            tiles = [
                both[first + 2 * seqs : first + 2 * seqs + MASK_ROWS].astype(f32)
                for first in (0, rows)
            ]
            maskt_ref[(2 * z + y) * res : (2 * z + y + 1) * res, :] = (
                tiles[0][0:res] + tiles[1][0:res]
            )
            own = mine[y][2 * seqs : 2 * seqs + MASK_ROWS].astype(f32)
            pair_lane = lax.broadcasted_iota(jnp.int32, (pair_cols, lanes), 1)
            pair_row = lax.broadcasted_iota(jnp.int32, (pair_cols, lanes), 0)
            for r in range(res):
                first = ((2 * z + y) * res + r) * pair_cols
                pml_ref[first : first + pair_cols, :] = jnp.where(
                    pair_lane == pair_row, own[res + r : res + r + 1, :], 0.0
                ).astype(bf16)
    for d in range(width):
        mine_ref[d * pair_cols : (d + 1) * pair_cols, :] = turnr_ref[
            pl.ds(me_depth * pair_cols * width + d, pair_cols, stride=width), :
        ].astype(bf16)
    for turned, out in ((turnl_ref, leftt_ref), (turnr_ref, rightt_ref)):
        for d in range(width):
            out[d * residues : (d + 1) * residues, :] = turned[
                pl.ds(d, residues, stride=width), :
            ].astype(bf16)

    maskt = maskt_ref[...]
    cols_mask = maskt_ref[pl.ds(pl.multiple_of(me_depth * pair_cols, pair_cols), pair_cols), :]
    for i in range(residues):
        cntl_ref[i * pair_cols : (i + 1) * pair_cols, :] = (maskt[i : i + 1, :] * cols_mask).astype(
            bf16
        )
    ones = jnp.ones((lanes, lanes), bf16)
    cnt_ref[...] = jnp.dot(cntl_ref[...], ones, preferred_element_type=f32)
    pm_ref[...] = jnp.dot(pml_ref[...], ones, preferred_element_type=f32).astype(bf16)

    for dh in range(width // 4):
        prod = jnp.dot(
            mine_ref[dh * 4 * pair_cols : (dh + 1) * 4 * pair_cols, :],
            leftn_ref[...],
            preferred_element_type=f32,
        )
        for k in range(cols):
            piece = prod[:, k * lanes : (k + 1) * lanes]
            turned = butterfly(
                [piece[a * pair_cols : (a + 1) * pair_cols] for a in range(4)], width
            )
            for il in range(res):
                first = (k * res + il) * pair_cols
                outer_ref[first : first + pair_cols, dh * lanes : (dh + 1) * lanes] = turned[
                    il
                ].astype(bf16)
    proj_out_ref[...] = jnp.dot(outer_ref[...], wturn_ref[...], preferred_element_type=f32)


def transition_kernel(
    sizes,
    ids_ref,
    near_ref,
    far_ref,
    proj_out_ref,
    cnt_ref,
    pm_ref,
    gain_ref,
    hid_ref,
    back_ref,
    couple_ref,
    opm_ref,
    pn_ref,
    gh_ref,
    hidden_ref,
    mg_ref,
    gmid_ref,
):
    seqs, res, pair_cols, width = sizes
    per = res * pair_cols
    cols = 2 * near_ref.shape[0]
    me_col = ids_ref[1]
    f32, bf16 = jnp.float32, jnp.bfloat16
    gain = gain_ref[...]
    chunk = 2 * per
    for at in range(cols // 2):
        rows = slice(at * chunk, (at + 1) * chunk)
        blocks = by_owner(ids_ref, at, near_ref, far_ref)
        act, grad = [
            jnp.concatenate([block[w * per : (w + 1) * per] for block in blocks], axis=0)
            for w in range(2)
        ]
        count = cnt_ref[rows, :]
        mid = act.astype(f32) + proj_out_ref[rows, :] / count
        scaled, inv = norm_pieces(mid)
        normed = (scaled * gain).astype(bf16)
        pn_ref[rows, :] = normed
        pre = jnp.dot(normed, hid_ref[...], preferred_element_type=f32)
        value, slope = silu_pieces(pre)
        hidden_ref[rows, :] = value.astype(bf16)
        masked = grad * pm_ref[rows, :]
        mg_ref[rows, :] = masked
        back = lax.dot_general(
            masked, back_ref[...], (((1,), (1,)), ((), ())), preferred_element_type=f32
        )
        ghid = (back * slope).astype(bf16)
        gh_ref[rows, :] = ghid
        gsc = (
            lax.dot_general(
                ghid, hid_ref[...], (((1,), (1,)), ((), ())), preferred_element_type=f32
            )
            * gain
        )
        gmid = grad.astype(f32) + standardize_adjoint(gsc, scaled, inv)
        gmid_ref[rows, :] = gmid
        opm_ref[rows, :] = (gmid / count).astype(bf16)
    couple_ref[...] = gmid_ref[pl.ds(pl.multiple_of(me_col * per, per), per), :].astype(bf16)


def projector_kernel(
    sizes,
    ids_ref,
    opm_ref,
    other_opm_ref,
    rightt_ref,
    leftt_ref,
    wout_ref,
    wturn_ref,
    maskt_ref,
    normed_ref,
    far_normed_ref,
    other_normed_ref,
    other_far_normed_ref,
    part_ref,
    spread_ref,
    gf_ref,
    grow_ref,
    gcol_ref,
    gor_ref,
    goc_ref,
    gs_ref,
    rows_ref,
):
    seqs, res, pair_cols, width = sizes
    depths, half = rows_ref.shape[1], gf_ref.shape[0]
    residues = half // pair_cols
    lanes = res * width
    here = 2 * res
    me_depth = ids_ref[0]
    me_col = ids_ref[1]
    me_y = me_col % 2
    first_here = (me_col // 2) * here
    f32, bf16 = jnp.float32, jnp.bfloat16
    my_half = first_here // pair_cols
    gf_ref[...] = jnp.where(my_half == me_depth, opm_ref[...], other_opm_ref[...]).astype(f32)
    for y, e, block in (
        (me_y, me_depth, normed_ref),
        (1 - me_y, me_depth, far_normed_ref),
        (me_y, 1 - me_depth, other_normed_ref),
        (1 - me_y, 1 - me_depth, other_far_normed_ref),
    ):
        rows_ref[y, e] = block[...]

    for il in range(here):
        first = pl.multiple_of((first_here + il) * pair_cols, pair_cols)
        for e, block in ((me_depth, opm_ref), (1 - me_depth, other_opm_ref)):
            to = pl.multiple_of(il * residues + e * pair_cols, pair_cols)
            grow_ref[pl.ds(to, pair_cols), :] = block[pl.ds(first, pair_cols), :]
    my_first = first_here - my_half * pair_cols
    for jl in range(here):
        gcol_ref[jl * residues : (jl + 1) * residues, :] = gf_ref[
            pl.ds(my_first + jl, residues, stride=pair_cols), :
        ].astype(bf16)
    for lhs, weight, out in ((grow_ref, wturn_ref, gor_ref), (gcol_ref, wout_ref, goc_ref)):
        for dh in range(width // 4):
            piece = lax.dot_general(
                lhs[...],
                weight[dh * lanes : (dh + 1) * lanes, :],
                (((1,), (1,)), ((), ())),
                preferred_element_type=f32,
            )
            for y in range(2):
                turned = butterfly(
                    [
                        piece[(y * res + a) * residues : (y * res + a + 1) * residues]
                        for a in range(4)
                    ],
                    width,
                )
                for dl in range(4):
                    first = (dh * 4 + dl) * residues
                    out[first : first + residues, y * lanes : (y + 1) * lanes] = turned[dl].astype(
                        bf16
                    )
    group = lax.broadcasted_iota(jnp.int32, (here, here * width), 1) // width
    spread = (group == lax.broadcasted_iota(jnp.int32, (here, here * width), 0)).astype(f32)
    mask_lanes = lax.dot_general(
        maskt_ref[pl.ds(pl.multiple_of(first_here, here), here), :],
        spread,
        (((0,), (0,)), ((), ())),
        preferred_element_type=f32,
    )
    lane_group = lax.broadcasted_iota(jnp.int32, (seqs, lanes), 1) // width
    for at, (lhs, rhs) in enumerate(((rightt_ref, gor_ref), (leftt_ref, goc_ref))):
        total = lax.dot_general(
            lhs[...], rhs[...], (((0,), (0,)), ((), ())), preferred_element_type=f32
        )
        total = (total * mask_lanes).astype(bf16).astype(f32)
        for y in range(2):
            for e in range(depths):
                block = total[e * seqs : (e + 1) * seqs, y * lanes : (y + 1) * lanes]
                for r in range(res):
                    gs_ref[at, y, e, pl.ds(r, seqs, stride=res), :] = jnp.where(
                        lane_group == r, block, 0.0
                    )
    spread_ref[...] = jnp.concatenate(
        [gs_ref[0, me_y, me_depth], gs_ref[1, me_y, me_depth]], axis=1
    ).astype(bf16)
    rows = rows_ref.shape[2]
    for at in range(2):
        cross = lax.dot_general(
            gs_ref[at].reshape(2 * depths * rows, lanes).astype(bf16),
            rows_ref[...].reshape(2 * depths * rows, rows_ref.shape[3]),
            (((0,), (0,)), ((), ())),
            preferred_element_type=f32,
        )
        total = cross[:width]
        for r in range(1, res):
            total = total + cross[r * width : (r + 1) * width]
        part_ref[at * width : (at + 1) * width, :] = total.astype(bf16)


def weights_kernel(outer_ref, opm_ref, pn_ref, gh_ref, hidden_ref, mg_ref, out_ref, turn_ref):
    pair_width, hid = pn_ref.shape[1], gh_ref.shape[1]
    outer_width = outer_ref.shape[1]
    width = int(outer_width**0.5 + 0.5)

    def contract(lhs, rhs):
        return lax.dot_general(
            lhs[...], rhs[...], (((0,), (0,)), ((), ())), preferred_element_type=jnp.float32
        )

    turn_ref[...] = contract(outer_ref, opm_ref)
    for c in range(width):
        out_ref[c * width : (c + 1) * width, :] = turn_ref[
            pl.ds(c, width, stride=width), :
        ].astype(jnp.bfloat16)
    dhid = contract(pn_ref, gh_ref).astype(jnp.bfloat16)
    for at in range(hid // pair_width):
        first = outer_width + at * pair_width
        out_ref[first : first + pair_width, :] = dhid[:, at * pair_width : (at + 1) * pair_width]
    out_ref[outer_width + hid :, :] = contract(hidden_ref, mg_ref).astype(jnp.bfloat16)


def weights_sum_kernel(mine_ref, other_ref, dout_ref, dhid_ref, dback_ref):
    pair_width, hid = dhid_ref.shape
    outer_width = dout_ref.shape[0]

    def added(first, count):
        rows = slice(first, first + count)
        return mine_ref[rows, :].astype(jnp.float32) + other_ref[rows, :].astype(jnp.float32)

    dout_ref[...] = added(0, outer_width)
    for at in range(hid // pair_width):
        dhid_ref[:, at * pair_width : (at + 1) * pair_width] = added(
            outer_width + at * pair_width, pair_width
        )
    dback_ref[...] = added(outer_width + hid, hid)


def feature_kernel(
    copies,
    spread_ref,
    first_ref,
    second_ref,
    scale_ref,
    scaled_ref,
    inv_ref,
    held_ref,
    feat_ref,
    couple_ref,
):
    back = jnp.dot(
        spread_ref[...],
        wide_projector(first_ref, second_ref, copies),
        preferred_element_type=jnp.float32,
    )
    feat_ref[...] = standardize_adjoint(
        back * scale_ref[...], scaled_ref[...], inv_ref[...]
    ).astype(jnp.bfloat16)
    couple_ref[...] = held_ref[...]


def swap_line(block, partners):
    count = lax.axis_size("col")
    pairs = [
        (depth * count + at, depth * count + (at ^ partner))
        for depth, partner in enumerate(partners)
        if partner is not None
        for at in range(count)
    ]
    return lax.ppermute(block, ("depth", "col"), pairs)


def swap_depth(block):
    return lax.ppermute(block, "depth", [(0, 1), (1, 0)])


def pairwise_sum(blocks):
    while len(blocks) > 1:
        blocks = [blocks[at] + blocks[at + 1] for at in range(0, len(blocks), 2)]
    return blocks[0]


def swap_col(block, partner):
    count = lax.axis_size("col")
    return lax.ppermute(block, "col", [(at, at ^ partner) for at in range(count)])


def whole_plan(
    alignment_activations,
    alignment_mask,
    pair_activation_input,
    pair_update_mask,
    pair_output_gradient,
    layer_scale_factor,
    first_projector,
    second_projector,
    output_weight,
    pair_norm_gain,
    hidden_weight,
    back_weight,
):
    seqs, res, channels = alignment_activations.shape
    width = first_projector.shape[1]
    outer_width = width * width
    cols = lax.axis_size("col")
    depths = lax.axis_size("depth")
    residues = res * cols
    pair_cols, pair_width = pair_activation_input.shape[1:]
    hid = hidden_weight.shape[1]
    per = res * pair_cols
    lanes = res * width
    rows = 2 * seqs + MASK_ROWS
    half = residues * pair_cols
    f32, bf16 = jnp.float32, jnp.bfloat16
    ids = jnp.stack([lax.axis_index("depth"), lax.axis_index("col")]).astype(jnp.int32)
    smem = pl.BlockSpec(memory_space=pltpu.SMEM)
    vmem = pl.BlockSpec(memory_space=pltpu.VMEM)
    params = pltpu.CompilerParams(vmem_limit_bytes=16 * 2**20)
    scale = layer_scale_factor.reshape(1, channels)
    first, second = first_projector.T, second_projector.T
    wturn = jnp.transpose(output_weight.reshape(width, width, pair_width), (1, 0, 2)).reshape(
        outer_width, pair_width
    )
    shape = jax.ShapeDtypeStruct
    sent, scale, first, second, gain, normed, scaled, inv = pl.pallas_call(
        pre_kernel,
        out_shape=(
            shape((1, rows + 2 * per, pair_width), bf16),
            shape((1, channels), f32),
            shape((width, channels), bf16),
            shape((width, channels), bf16),
            shape((1, pair_width), f32),
            shape((seqs * res, channels), bf16),
            shape((seqs * res, channels), f32),
            shape((seqs * res, 1), f32),
        ),
        in_specs=[smem] + [pl.BlockSpec(memory_space=pltpu.HBM)] * 9,
        out_specs=[vmem] * 8,
        scratch_shapes=[
            pltpu.VMEM((2, seqs * res, lanes), f32),
            pltpu.VMEM((MASK_ROWS, lanes), f32),
            pltpu.VMEM((seqs, res, channels), bf16),
            pltpu.VMEM((res, seqs), jnp.int32),
            pltpu.VMEM((res, pair_cols), jnp.int32),
            pltpu.SemaphoreType.DMA((9,)),
        ],
        compiler_params=params,
        name="project",
    )(
        ids,
        *[
            pltpu.with_memory_space_constraint(array, pltpu.HBM)
            for array in (
                alignment_activations,
                alignment_mask.T,
                pair_update_mask,
                scale,
                first,
                second,
                pair_norm_gain.reshape(1, pair_width),
                pair_activation_input.reshape(per, pair_width),
                pair_output_gradient.reshape(per, pair_width),
            )
        ],
    )
    blocks = lax.optimization_barrier(
        jnp.concatenate([sent] + [swap_col(sent, partner) for partner in Z_PARTNERS])
    )
    far_normed = swap_col(normed, Y_PARTNER)
    blocks, far_normed = lax.optimization_barrier((blocks, far_normed))
    near, pair_near = blocks[:, :rows], blocks[:, rows:]
    far = swap_col(near, Y_PARTNER)
    pair_far = swap_col(pair_near, Y_PARTNER)
    other_near, other_far = swap_depth(near), swap_depth(far)
    sizes = (seqs, res, pair_cols, width)
    outer, proj_out, cnt, pm, maskt, rightt, leftt = pl.pallas_call(
        functools.partial(outer_kernel, sizes),
        out_shape=(
            shape((half, outer_width), bf16),
            shape((half, pair_width), f32),
            shape((half, lanes), f32),
            shape((half, lanes), bf16),
            shape((residues, depths * seqs), f32),
            shape((residues * width, depths * seqs), bf16),
            shape((residues * width, depths * seqs), bf16),
        ),
        in_specs=[smem] + [vmem] * 5,
        out_specs=[vmem] * 7,
        scratch_shapes=[
            pltpu.VMEM((depths * seqs, residues * width), bf16),
            pltpu.VMEM((pair_cols * width, depths * seqs), bf16),
            pltpu.VMEM((residues * width, depths * seqs), f32),
            pltpu.VMEM((residues * width, depths * seqs), f32),
            pltpu.VMEM((half, lanes), bf16),
            pltpu.VMEM((half, lanes), bf16),
        ],
        compiler_params=params,
        name="outer_products",
    )(ids, near, far, other_near, other_far, wturn)
    normed_again, far_again, proj_out = lax.optimization_barrier((normed, far_normed, proj_out))
    other_normed, other_far_normed = swap_depth(normed_again), swap_depth(far_again)
    pair_far, proj_out, other_normed, other_far_normed = lax.optimization_barrier(
        (pair_far, proj_out, other_normed, other_far_normed)
    )
    held, opm, pn, gh, hidden, mg = pl.pallas_call(
        functools.partial(transition_kernel, sizes),
        out_shape=(
            shape((per, pair_width), bf16),
            shape((half, pair_width), bf16),
            shape((half, pair_width), bf16),
            shape((half, hid), bf16),
            shape((half, hid), bf16),
            shape((half, pair_width), bf16),
        ),
        in_specs=[smem] + [vmem] * 8,
        out_specs=[vmem] * 6,
        scratch_shapes=[
            pltpu.VMEM((half, pair_width), f32),
        ],
        compiler_params=params,
        name="transition",
    )(
        ids,
        pair_near,
        pair_far,
        proj_out,
        cnt,
        pm,
        gain,
        hidden_weight,
        back_weight,
    )
    weights = pl.pallas_call(
        weights_kernel,
        out_shape=shape((outer_width + 2 * hid, pair_width), bf16),
        in_specs=[vmem] * 6,
        out_specs=vmem,
        scratch_shapes=[pltpu.VMEM((outer_width, pair_width), f32)],
        compiler_params=params,
        name="weight_gradients",
    )(outer, opm, pn, gh, hidden, mg)
    other_opm, weights = lax.optimization_barrier((swap_depth(opm), weights))
    part, spread = pl.pallas_call(
        functools.partial(projector_kernel, sizes),
        out_shape=(
            shape((2 * width, channels), bf16),
            shape((seqs * res, 2 * lanes), bf16),
        ),
        in_specs=[smem] + [vmem] * 11,
        out_specs=[vmem] * 2,
        scratch_shapes=[
            pltpu.VMEM((half, pair_width), f32),
            pltpu.VMEM((2 * res * residues, pair_width), bf16),
            pltpu.VMEM((2 * res * residues, pair_width), bf16),
            pltpu.VMEM((residues * width, 2 * lanes), bf16),
            pltpu.VMEM((residues * width, 2 * lanes), bf16),
            pltpu.VMEM((2, 2, depths, seqs * res, lanes), f32),
            pltpu.VMEM((2, depths, seqs * res, channels), bf16),
        ],
        compiler_params=params,
        name="projector_parts",
    )(
        ids,
        opm,
        other_opm,
        rightt,
        leftt,
        output_weight,
        wturn,
        maskt,
        normed,
        far_normed,
        other_normed,
        other_far_normed,
    )
    feat, couple = pl.pallas_call(
        functools.partial(feature_kernel, res),
        out_shape=(shape((seqs * res, channels), bf16), shape((per, pair_width), bf16)),
        in_specs=[vmem] * 7,
        out_specs=[vmem] * 2,
        compiler_params=params,
        name="features",
    )(spread, first, second, scale, scaled, inv, held)
    part, weights = lax.optimization_barrier((part, weights))
    dout, dhid, dback = pl.pallas_call(
        weights_sum_kernel,
        out_shape=(
            shape((outer_width, pair_width), f32),
            shape((pair_width, hid), f32),
            shape((hid, pair_width), f32),
        ),
        in_specs=[vmem] * 2,
        out_specs=[vmem] * 3,
        compiler_params=params,
        name="sums_over_depth",
    )(weights, swap_depth(weights))
    came_a = swap_line(part, Z_PARTNERS[:2])
    came_b = swap_line(part, (None, Z_PARTNERS[2]))
    feat = feat.reshape(seqs, res, channels)
    came_a, came_b, feat, couple = lax.optimization_barrier((came_a, came_b, feat, couple))
    kept = jnp.where(lax.axis_index("depth") == 0, part, came_b)
    kept = lax.optimization_barrier((kept.astype(f32) + came_a.astype(f32)).astype(bf16))
    came = swap_depth(kept)
    came, dout, dhid, dback = lax.optimization_barrier((came, dout, dhid, dback))
    total = kept.astype(f32) + came.astype(f32)
    return (
        feat,
        couple.reshape(res, pair_cols, pair_width),
        total[:width].T,
        total[width:].T,
        dout,
        dhid,
        dback,
    )


def on_device(alignment_activations, *others):
    cols = lax.axis_size("col")
    residues = alignment_activations.shape[1] * cols
    plan = whole_plan if cols == 8 and residues <= FEW_RESIDUES else split_plan
    return plan(alignment_activations, *others)


def solution(mesh):
    in_specs = (
        P(("group", "depth"), "col", None),
        P(("group", "depth"), "col"),
        P(("group", "col"), "depth", None),
        P(("group", "col"), "depth"),
        P(("group", "col"), "depth", None),
        P(),
        P(),
        P(),
        P(),
        P(),
        P(),
        P(),
    )
    out_specs = (
        P(("group", "depth"), "col", None),
        P(("group", "col"), "depth", None),
        P("group", None),
        P("group", None),
        P("group", None),
        P("group", None),
        P("group", None),
    )
    return jax.shard_map(
        on_device, mesh=mesh, in_specs=in_specs, out_specs=out_specs, check_vma=False
    )
```

```python
import functools

import jax
import jax.numpy as jnp
from jax import lax
from jax.experimental import pallas as pl
from jax.experimental.pallas import tpu as pltpu
from jax.sharding import PartitionSpec as P

epsilon = 1e-05
highest = lax.Precision.HIGHEST


def norm_pieces(entries_drawn):
    center = entries_drawn - jnp.mean(entries_drawn, axis=-1, keepdims=True)
    inv_std = lax.rsqrt(jnp.mean(center * center, axis=-1, keepdims=True) + epsilon)
    return (center * inv_std, inv_std)


def standardize_adjoint(grad_scaled, scaled, inv_std):
    mean_grad = jnp.mean(grad_scaled, axis=-1, keepdims=True)
    mean_cross = jnp.mean(grad_scaled * scaled, axis=-1, keepdims=True)
    return inv_std * (grad_scaled - mean_grad - scaled * mean_cross)


def silu_pieces(pre_act):
    sigma = jax.nn.sigmoid(pre_act)
    return (pre_act * sigma, sigma * (1.0 + pre_act * (1.0 - sigma)))


def split_plan(
    alignment_activations,
    alignment_mask,
    pair_activation_input,
    pair_update_mask,
    pair_output_gradient,
    layer_scale_factor,
    first_projector,
    second_projector,
    output_weight,
    pair_norm_gain,
    hidden_weight,
    back_weight,
):
    sequence_row_block, residue_row_block, channel_total = alignment_activations.shape
    proj_width = first_projector.shape[1]
    outer_width = proj_width * proj_width
    depth_count = lax.axis_size("depth")
    residues = residue_row_block * lax.axis_size("col")
    pair_cols = pair_activation_input.shape[1]
    pair_width = pair_activation_input.shape[2]
    col_block = min(64, pair_cols)
    block_count = pair_cols // col_block
    standardized_features, reciprocal_spread = norm_pieces(
        alignment_activations.astype(jnp.float32)
    )
    normalized_rows = (standardized_features * layer_scale_factor).astype(jnp.bfloat16)
    mask_floating = alignment_mask.astype(jnp.float32)
    left_proj = (
        jnp.dot(normalized_rows, first_projector, preferred_element_type=jnp.float32)
        * mask_floating[:, :, None]
    ).astype(jnp.bfloat16)
    right_proj = (
        jnp.dot(normalized_rows, second_projector, preferred_element_type=jnp.float32)
        * mask_floating[:, :, None]
    ).astype(jnp.bfloat16)
    right_flat = right_proj.reshape(sequence_row_block, residue_row_block * proj_width)
    mask_converted = alignment_mask.astype(jnp.bfloat16)
    seq_total = left_proj.shape[0]
    gathered, gathered_mask = (
        lax.all_gather(right_flat, "col", axis=1, tiled=True),
        lax.all_gather(mask_converted, "col", axis=1, tiled=True),
    )
    right_blocks = gathered.reshape(seq_total, depth_count, pair_cols, proj_width)
    mask_blocks = gathered_mask.reshape(seq_total, depth_count, pair_cols)
    block_depth = right_blocks.shape[1]
    out_wide = output_weight.astype(jnp.float32)

    def partial_outer(col_start):
        right_piece = lax.dynamic_slice_in_dim(right_blocks, col_start, col_block, 2)
        outer_part = jnp.einsum(
            "sic,sejd->iejcd", left_proj, right_piece, preferred_element_type=jnp.float32
        )
        return (
            outer_part.reshape(residue_row_block, block_depth, col_block, outer_width),
            right_piece,
        )

    def forward_step(step_index, loop_state):
        projected, pair_count = loop_state
        col_start = step_index * col_block
        outer_part, right_piece = partial_outer(col_start)
        mask_piece = lax.dynamic_slice_in_dim(mask_blocks, col_start, col_block, 2).astype(
            jnp.float32
        )
        count_part = jnp.einsum("si,sej->iej", mask_floating, mask_piece, precision=highest)
        outer_mine, count_mine = (
            lax.psum_scatter(
                outer_part.astype(jnp.bfloat16), "depth", scatter_dimension=1, tiled=True
            ).astype(jnp.float32),
            lax.psum_scatter(
                count_part.astype(jnp.bfloat16), "depth", scatter_dimension=1, tiled=True
            ).astype(jnp.float32),
        )
        proj_mine = jnp.dot(
            outer_mine.reshape(residue_row_block * col_block, outer_width),
            out_wide,
            precision=highest,
        )
        proj_mine = proj_mine.reshape(residue_row_block, col_block, pair_width)
        count_mine = count_mine.reshape(residue_row_block, col_block)
        projected = lax.dynamic_update_slice_in_dim(projected, proj_mine, col_start, 1)
        pair_count = lax.dynamic_update_slice_in_dim(pair_count, count_mine, col_start, 1)
        return (projected, pair_count)

    projected, pair_count = lax.fori_loop(
        0,
        block_count,
        forward_step,
        (
            jnp.zeros((residue_row_block, pair_cols, pair_width), jnp.float32),
            jnp.zeros((residue_row_block, pair_cols), jnp.float32),
        ),
    )
    count_column = pair_count.reshape(residue_row_block * pair_cols, 1)
    mid_act = (
        pair_activation_input.reshape(residue_row_block * pair_cols, pair_width).astype(jnp.float32)
        + projected.reshape(residue_row_block * pair_cols, pair_width) / count_column
    )
    pair_scaled, pair_inv = norm_pieces(mid_act)
    pair_normed = (pair_scaled * pair_norm_gain).astype(jnp.bfloat16)
    pre_act = jnp.dot(pair_normed, hidden_weight, preferred_element_type=jnp.float32)
    act_value, act_slope = silu_pieces(pre_act)
    hidden = act_value.astype(jnp.bfloat16)
    masked_grad = (
        pair_output_gradient * pair_update_mask.astype(jnp.bfloat16)[:, :, None]
    ).reshape(residue_row_block * pair_cols, pair_width)
    final_matrix_derivative = jnp.dot(hidden.T, masked_grad, preferred_element_type=jnp.float32)
    back_prod = jnp.dot(masked_grad, back_weight.T, preferred_element_type=jnp.float32)
    grad_hidden = (back_prod * act_slope).astype(jnp.bfloat16)
    middle_matrix_derivative = jnp.dot(
        pair_normed.T, grad_hidden, preferred_element_type=jnp.float32
    )
    grad_scaled = (
        jnp.dot(grad_hidden, hidden_weight.T, preferred_element_type=jnp.float32) * pair_norm_gain
    )
    grad_mid = pair_output_gradient.reshape(residue_row_block * pair_cols, pair_width).astype(
        jnp.float32
    ) + standardize_adjoint(grad_scaled, pair_scaled, pair_inv)
    couple_features_derivative = grad_mid.astype(jnp.bfloat16).reshape(
        residue_row_block, pair_cols, pair_width
    )
    grad_opm = (
        (grad_mid / count_column)
        .astype(jnp.bfloat16)
        .reshape(residue_row_block, pair_cols, pair_width)
    )
    full_opm = lax.all_gather(grad_opm, "depth", axis=1, tiled=True).reshape(
        residue_row_block, depth_count, pair_cols, pair_width
    )

    def backward_step(step_index, loop_state):
        grad_left_acc, grad_out, right_term = loop_state
        col_start = step_index * col_block
        outer_part, right_piece = partial_outer(col_start)
        opm_piece = lax.dynamic_slice_in_dim(full_opm, col_start, col_block, 2).reshape(
            residue_row_block * block_depth * col_block, pair_width
        )
        grad_out = grad_out + jnp.dot(
            outer_part.reshape(residue_row_block * block_depth * col_block, outer_width).T,
            opm_piece.astype(jnp.float32),
            precision=highest,
        )
        grad_outer = jnp.dot(opm_piece, output_weight.T, preferred_element_type=jnp.float32).astype(
            jnp.bfloat16
        )
        grad_outer = grad_outer.reshape(
            residue_row_block, block_depth, col_block, proj_width, proj_width
        )
        grad_left_acc = grad_left_acc + jnp.einsum(
            "iejcd,sejd->sic", grad_outer, right_piece, preferred_element_type=jnp.float32
        )
        piece_term = jnp.einsum(
            "iejcd,sic->ejsd", grad_outer, left_proj, preferred_element_type=jnp.float32
        )
        piece_term = piece_term.reshape(block_depth, col_block, seq_total * proj_width)
        right_term = lax.dynamic_update_slice_in_dim(right_term, piece_term, col_start, 1)
        return (grad_left_acc, grad_out, right_term)

    grad_left_acc, result_matrix_derivative, right_term = lax.fori_loop(
        0,
        block_count,
        backward_step,
        (
            jnp.zeros((seq_total, residue_row_block, proj_width), jnp.float32),
            jnp.zeros((outer_width, pair_width), jnp.float32),
            jnp.zeros((block_depth, pair_cols, seq_total * proj_width), jnp.float32),
        ),
    )
    grad_right_sum = lax.psum_scatter(
        right_term.reshape(residues, seq_total * proj_width), "col", scatter_dimension=0, tiled=True
    )
    grad_right_acc = jnp.transpose(
        grad_right_sum.reshape(residue_row_block, seq_total, proj_width), (1, 0, 2)
    )
    grad_left = (grad_left_acc * mask_floating[:, :, None]).astype(jnp.bfloat16)
    grad_right = (grad_right_acc * mask_floating[:, :, None]).astype(jnp.bfloat16)
    normed_rows = normalized_rows.reshape(sequence_row_block * residue_row_block, channel_total)
    first_projector_derivative = jnp.dot(
        normed_rows.T,
        grad_left.reshape(sequence_row_block * residue_row_block, proj_width),
        preferred_element_type=jnp.float32,
    )
    second_projector_derivative = jnp.dot(
        normed_rows.T,
        grad_right.reshape(sequence_row_block * residue_row_block, proj_width),
        preferred_element_type=jnp.float32,
    )
    standardized_derivative = jnp.dot(
        grad_left, first_projector.T, preferred_element_type=jnp.float32
    ) + jnp.dot(grad_right, second_projector.T, preferred_element_type=jnp.float32)
    features_derivative = standardize_adjoint(
        standardized_derivative * layer_scale_factor, standardized_features, reciprocal_spread
    ).astype(jnp.bfloat16)
    weight_sums = lax.psum(
        (
            first_projector_derivative,
            second_projector_derivative,
            result_matrix_derivative,
            middle_matrix_derivative,
            final_matrix_derivative,
        ),
        ("depth", "col"),
    )
    return (
        features_derivative,
        couple_features_derivative,
        weight_sums[0],
        weight_sums[1],
        weight_sums[2],
        weight_sums[3],
        weight_sums[4],
    )


FEW_RESIDUES = 32
MASK_ROWS = 16
Z_PARTNERS = (2, 4, 6)
Y_PARTNER = 1


def butterfly(blocks, group):
    lane_group = lax.broadcasted_iota(jnp.int32, blocks[0].shape, 1) // group
    width = 4 * group
    for bit in (2, 1):
        low = (lane_group & bit) == 0
        swapped = list(blocks)
        for at in range(4):
            if at & bit:
                continue
            here, there = blocks[at], blocks[at | bit]
            moving = jnp.where(low, there, here)
            if bit == 2:
                moved = pltpu.roll(moving, 2 * group, 1)
            else:
                moved = jnp.where(
                    low, pltpu.roll(moving, width - group, 1), pltpu.roll(moving, group, 1)
                )
            swapped[at] = jnp.where(low, here, moved)
            swapped[at | bit] = jnp.where(low, moved, there)
        blocks = swapped
    return blocks


def wide_projector(first_ref, second_ref, copies):
    return jnp.concatenate([first_ref[...]] * copies + [second_ref[...]] * copies, axis=0)


def pre_kernel(
    ids_ref,
    x_hbm,
    maskt_hbm,
    pmask_hbm,
    scale_hbm,
    first_hbm,
    second_hbm,
    gain_hbm,
    act_hbm,
    grad_hbm,
    sent_ref,
    scale_ref,
    first_ref,
    second_ref,
    gain_ref,
    normed_ref,
    scaled_ref,
    inv_ref,
    wide_ref,
    tile_ref,
    x_ref,
    maskt_ref,
    pmask_ref,
    sems,
):
    res, seqs = maskt_ref.shape
    pairs = act_hbm.shape[0]
    first_pair = 2 * seqs + MASK_ROWS
    copies = [
        pltpu.make_async_copy(source, target, sems.at[at])
        for at, (source, target) in enumerate(
            (
                (x_hbm, x_ref),
                (maskt_hbm, maskt_ref),
                (pmask_hbm, pmask_ref),
                (scale_hbm, scale_ref),
                (first_hbm, first_ref),
                (second_hbm, second_ref),
                (gain_hbm, gain_ref),
                (act_hbm, sent_ref.at[0, pl.ds(first_pair, pairs), :]),
                (grad_hbm, sent_ref.at[0, pl.ds(first_pair + pairs, pairs), :]),
            )
        )
    ]
    for copy in copies:
        copy.start()
    for copy in copies:
        copy.wait()
    lanes = sent_ref.shape[2]
    group = lanes // res
    scaled, inv = norm_pieces(
        x_ref[...].astype(jnp.float32).reshape(seqs * res, x_ref.shape[2])
    )
    scaled_ref[...] = scaled
    inv_ref[...] = inv
    normed = (scaled * scale_ref[...]).astype(jnp.bfloat16)
    normed_ref[...] = normed
    wide = lax.dot_general(
        normed,
        wide_projector(first_ref, second_ref, res),
        (((1,), (1,)), ((), ())),
        preferred_element_type=jnp.float32,
    )
    for at in range(2):
        wide_ref[at] = wide[:, at * lanes : (at + 1) * lanes]
    tile_ref[...] = jnp.zeros(tile_ref.shape, jnp.float32)
    mask = maskt_ref[...].astype(jnp.float32)
    tile_ref[0:res, 0:seqs] = mask
    spread = (
        lax.broadcasted_iota(jnp.int32, (MASK_ROWS, lanes), 1) // group
        == lax.broadcasted_iota(jnp.int32, (MASK_ROWS, lanes), 0)
    ).astype(jnp.float32)
    mask_lanes = lax.dot_general(
        tile_ref[...], spread, (((0,), (0,)), ((), ())), preferred_element_type=jnp.float32
    )[:seqs]
    twice = jnp.concatenate([mask] * (lanes // seqs), axis=1)
    here = lax.broadcasted_iota(jnp.int32, (res, lanes), 1) // seqs == ids_ref[0]
    tile_ref[0:res, :] = jnp.where(here, twice, 0.0)
    tile_ref[res : 2 * res, 0 : pmask_ref.shape[1]] = pmask_ref[...].astype(jnp.float32)
    lane_group = lax.broadcasted_iota(jnp.int32, (seqs, lanes), 1) // group
    for at in range(2):
        both = wide_ref[at, pl.ds(0, seqs, stride=res), :]
        for r in range(1, res):
            both = jnp.where(
                lane_group == r, wide_ref[at, pl.ds(r, seqs, stride=res), :], both
            )
        sent_ref[0, at * seqs : (at + 1) * seqs, :] = (both * mask_lanes).astype(jnp.bfloat16)
    sent_ref[0, 2 * seqs : first_pair, :] = tile_ref[...].astype(jnp.bfloat16)


def by_owner(ids_ref, z, near_ref, far_ref):
    step = z ^ (ids_ref[1] // 2)
    near, far = near_ref[step], far_ref[step]
    first = ids_ref[1] % 2 == 0
    return jnp.where(first, near, far), jnp.where(first, far, near)


def outer_kernel(
    sizes,
    ids_ref,
    near_ref,
    far_ref,
    other_near_ref,
    other_far_ref,
    wturn_ref,
    outer_ref,
    proj_out_ref,
    cnt_ref,
    pm_ref,
    maskt_ref,
    rightt_ref,
    leftt_ref,
    leftn_ref,
    mine_ref,
    turnl_ref,
    turnr_ref,
    cntl_ref,
    pml_ref,
):
    seqs, res, pair_cols, width = sizes
    line = near_ref.shape[0]
    cols = 2 * line
    residues = cols * res
    lanes = res * width
    me_depth = ids_ref[0]
    lower = me_depth == 0
    f32, bf16 = jnp.float32, jnp.bfloat16

    for z in range(line):
        mine = by_owner(ids_ref, z, near_ref, far_ref)
        other = by_owner(ids_ref, z, other_near_ref, other_far_ref)
        for y in range(2):
            lanes_k = slice((2 * z + y) * lanes, (2 * z + y + 1) * lanes)
            both = jnp.concatenate(
                [
                    jnp.where(lower, mine[y], other[y]),
                    jnp.where(lower, other[y], mine[y]),
                ],
                axis=0,
            )
            rows = both.shape[0] // 2
            left = jnp.concatenate([both[0:seqs], both[rows : rows + seqs]], axis=0)
            right = jnp.concatenate(
                [both[seqs : 2 * seqs], both[rows + seqs : rows + 2 * seqs]], axis=0
            )
            leftn_ref[:, lanes_k] = left
            turnl_ref[lanes_k, :] = left.astype(f32).T
            turnr_ref[lanes_k, :] = right.astype(f32).T
            tiles = [
                both[first + 2 * seqs : first + 2 * seqs + MASK_ROWS].astype(f32)
                for first in (0, rows)
            ]
            maskt_ref[(2 * z + y) * res : (2 * z + y + 1) * res, :] = (
                tiles[0][0:res] + tiles[1][0:res]
            )
            own = mine[y][2 * seqs : 2 * seqs + MASK_ROWS].astype(f32)
            pair_lane = lax.broadcasted_iota(jnp.int32, (pair_cols, lanes), 1)
            pair_row = lax.broadcasted_iota(jnp.int32, (pair_cols, lanes), 0)
            for r in range(res):
                first = ((2 * z + y) * res + r) * pair_cols
                pml_ref[first : first + pair_cols, :] = jnp.where(
                    pair_lane == pair_row, own[res + r : res + r + 1, :], 0.0
                ).astype(bf16)
    for d in range(width):
        mine_ref[d * pair_cols : (d + 1) * pair_cols, :] = turnr_ref[
            pl.ds(me_depth * pair_cols * width + d, pair_cols, stride=width), :
        ].astype(bf16)
    for turned, out in ((turnl_ref, leftt_ref), (turnr_ref, rightt_ref)):
        for d in range(width):
            out[d * residues : (d + 1) * residues, :] = turned[
                pl.ds(d, residues, stride=width), :
            ].astype(bf16)

    maskt = maskt_ref[...]
    cols_mask = maskt_ref[pl.ds(pl.multiple_of(me_depth * pair_cols, pair_cols), pair_cols), :]
    for i in range(residues):
        cntl_ref[i * pair_cols : (i + 1) * pair_cols, :] = (maskt[i : i + 1, :] * cols_mask).astype(
            bf16
        )
    ones = jnp.ones((lanes, lanes), bf16)
    cnt_ref[...] = jnp.dot(cntl_ref[...], ones, preferred_element_type=f32)
    pm_ref[...] = jnp.dot(pml_ref[...], ones, preferred_element_type=f32).astype(bf16)

    for dh in range(width // 4):
        prod = jnp.dot(
            mine_ref[dh * 4 * pair_cols : (dh + 1) * 4 * pair_cols, :],
            leftn_ref[...],
            preferred_element_type=f32,
        )
        for k in range(cols):
            piece = prod[:, k * lanes : (k + 1) * lanes]
            turned = butterfly(
                [piece[a * pair_cols : (a + 1) * pair_cols] for a in range(4)], width
            )
            for il in range(res):
                first = (k * res + il) * pair_cols
                outer_ref[first : first + pair_cols, dh * lanes : (dh + 1) * lanes] = turned[
                    il
                ].astype(bf16)
    proj_out_ref[...] = jnp.dot(outer_ref[...], wturn_ref[...], preferred_element_type=f32)


def transition_kernel(
    sizes,
    ids_ref,
    near_ref,
    far_ref,
    proj_out_ref,
    cnt_ref,
    pm_ref,
    gain_ref,
    hid_ref,
    back_ref,
    couple_ref,
    opm_ref,
    pn_ref,
    gh_ref,
    hidden_ref,
    mg_ref,
    gmid_ref,
):
    seqs, res, pair_cols, width = sizes
    per = res * pair_cols
    cols = 2 * near_ref.shape[0]
    me_col = ids_ref[1]
    f32, bf16 = jnp.float32, jnp.bfloat16
    gain = gain_ref[...]
    chunk = 2 * per
    for at in range(cols // 2):
        rows = slice(at * chunk, (at + 1) * chunk)
        blocks = by_owner(ids_ref, at, near_ref, far_ref)
        act, grad = [
            jnp.concatenate([block[w * per : (w + 1) * per] for block in blocks], axis=0)
            for w in range(2)
        ]
        count = cnt_ref[rows, :]
        mid = act.astype(f32) + proj_out_ref[rows, :] / count
        scaled, inv = norm_pieces(mid)
        normed = (scaled * gain).astype(bf16)
        pn_ref[rows, :] = normed
        pre = jnp.dot(normed, hid_ref[...], preferred_element_type=f32)
        value, slope = silu_pieces(pre)
        hidden_ref[rows, :] = value.astype(bf16)
        masked = grad * pm_ref[rows, :]
        mg_ref[rows, :] = masked
        back = lax.dot_general(
            masked, back_ref[...], (((1,), (1,)), ((), ())), preferred_element_type=f32
        )
        ghid = (back * slope).astype(bf16)
        gh_ref[rows, :] = ghid
        gsc = (
            lax.dot_general(
                ghid, hid_ref[...], (((1,), (1,)), ((), ())), preferred_element_type=f32
            )
            * gain
        )
        gmid = grad.astype(f32) + standardize_adjoint(gsc, scaled, inv)
        gmid_ref[rows, :] = gmid
        opm_ref[rows, :] = (gmid / count).astype(bf16)
    couple_ref[...] = gmid_ref[pl.ds(pl.multiple_of(me_col * per, per), per), :].astype(bf16)


def projector_kernel(
    sizes,
    ids_ref,
    opm_ref,
    other_opm_ref,
    rightt_ref,
    leftt_ref,
    wout_ref,
    wturn_ref,
    maskt_ref,
    normed_ref,
    far_normed_ref,
    other_normed_ref,
    other_far_normed_ref,
    part_ref,
    spread_ref,
    gf_ref,
    grow_ref,
    gcol_ref,
    gor_ref,
    goc_ref,
    gs_ref,
    rows_ref,
):
    seqs, res, pair_cols, width = sizes
    depths, half = rows_ref.shape[1], gf_ref.shape[0]
    residues = half // pair_cols
    lanes = res * width
    here = 2 * res
    me_depth = ids_ref[0]
    me_col = ids_ref[1]
    me_y = me_col % 2
    first_here = (me_col // 2) * here
    f32, bf16 = jnp.float32, jnp.bfloat16
    my_half = first_here // pair_cols
    gf_ref[...] = jnp.where(my_half == me_depth, opm_ref[...], other_opm_ref[...]).astype(f32)
    for y, e, block in (
        (me_y, me_depth, normed_ref),
        (1 - me_y, me_depth, far_normed_ref),
        (me_y, 1 - me_depth, other_normed_ref),
        (1 - me_y, 1 - me_depth, other_far_normed_ref),
    ):
        rows_ref[y, e] = block[...]

    for il in range(here):
        first = pl.multiple_of((first_here + il) * pair_cols, pair_cols)
        for e, block in ((me_depth, opm_ref), (1 - me_depth, other_opm_ref)):
            to = pl.multiple_of(il * residues + e * pair_cols, pair_cols)
            grow_ref[pl.ds(to, pair_cols), :] = block[pl.ds(first, pair_cols), :]
    my_first = first_here - my_half * pair_cols
    for jl in range(here):
        gcol_ref[jl * residues : (jl + 1) * residues, :] = gf_ref[
            pl.ds(my_first + jl, residues, stride=pair_cols), :
        ].astype(bf16)
    for lhs, weight, out in ((grow_ref, wturn_ref, gor_ref), (gcol_ref, wout_ref, goc_ref)):
        for dh in range(width // 4):
            piece = lax.dot_general(
                lhs[...],
                weight[dh * lanes : (dh + 1) * lanes, :],
                (((1,), (1,)), ((), ())),
                preferred_element_type=f32,
            )
            for y in range(2):
                turned = butterfly(
                    [
                        piece[(y * res + a) * residues : (y * res + a + 1) * residues]
                        for a in range(4)
                    ],
                    width,
                )
                for dl in range(4):
                    first = (dh * 4 + dl) * residues
                    out[first : first + residues, y * lanes : (y + 1) * lanes] = turned[dl].astype(
                        bf16
                    )
    group = lax.broadcasted_iota(jnp.int32, (here, here * width), 1) // width
    spread = (group == lax.broadcasted_iota(jnp.int32, (here, here * width), 0)).astype(f32)
    mask_lanes = lax.dot_general(
        maskt_ref[pl.ds(pl.multiple_of(first_here, here), here), :],
        spread,
        (((0,), (0,)), ((), ())),
        preferred_element_type=f32,
    )
    lane_group = lax.broadcasted_iota(jnp.int32, (seqs, lanes), 1) // width
    for at, (lhs, rhs) in enumerate(((rightt_ref, gor_ref), (leftt_ref, goc_ref))):
        total = lax.dot_general(
            lhs[...], rhs[...], (((0,), (0,)), ((), ())), preferred_element_type=f32
        )
        total = (total * mask_lanes).astype(bf16).astype(f32)
        for y in range(2):
            for e in range(depths):
                block = total[e * seqs : (e + 1) * seqs, y * lanes : (y + 1) * lanes]
                for r in range(res):
                    gs_ref[at, y, e, pl.ds(r, seqs, stride=res), :] = jnp.where(
                        lane_group == r, block, 0.0
                    )
    spread_ref[...] = jnp.concatenate(
        [gs_ref[0, me_y, me_depth], gs_ref[1, me_y, me_depth]], axis=1
    ).astype(bf16)
    rows = rows_ref.shape[2]
    for at in range(2):
        cross = lax.dot_general(
            gs_ref[at].reshape(2 * depths * rows, lanes).astype(bf16),
            rows_ref[...].reshape(2 * depths * rows, rows_ref.shape[3]),
            (((0,), (0,)), ((), ())),
            preferred_element_type=f32,
        )
        total = cross[:width]
        for r in range(1, res):
            total = total + cross[r * width : (r + 1) * width]
        part_ref[at * width : (at + 1) * width, :] = total.astype(bf16)


def weights_kernel(outer_ref, opm_ref, pn_ref, gh_ref, hidden_ref, mg_ref, out_ref, turn_ref):
    pair_width, hid = pn_ref.shape[1], gh_ref.shape[1]
    outer_width = outer_ref.shape[1]
    width = int(outer_width**0.5 + 0.5)

    def contract(lhs, rhs):
        return lax.dot_general(
            lhs[...], rhs[...], (((0,), (0,)), ((), ())), preferred_element_type=jnp.float32
        )

    turn_ref[...] = contract(outer_ref, opm_ref)
    for c in range(width):
        out_ref[c * width : (c + 1) * width, :] = turn_ref[
            pl.ds(c, width, stride=width), :
        ].astype(jnp.bfloat16)
    dhid = contract(pn_ref, gh_ref).astype(jnp.bfloat16)
    for at in range(hid // pair_width):
        first = outer_width + at * pair_width
        out_ref[first : first + pair_width, :] = dhid[:, at * pair_width : (at + 1) * pair_width]
    out_ref[outer_width + hid :, :] = contract(hidden_ref, mg_ref).astype(jnp.bfloat16)


def weights_sum_kernel(mine_ref, other_ref, dout_ref, dhid_ref, dback_ref):
    pair_width, hid = dhid_ref.shape
    outer_width = dout_ref.shape[0]

    def added(first, count):
        rows = slice(first, first + count)
        return mine_ref[rows, :].astype(jnp.float32) + other_ref[rows, :].astype(jnp.float32)

    dout_ref[...] = added(0, outer_width)
    for at in range(hid // pair_width):
        dhid_ref[:, at * pair_width : (at + 1) * pair_width] = added(
            outer_width + at * pair_width, pair_width
        )
    dback_ref[...] = added(outer_width + hid, hid)


def feature_kernel(
    copies,
    spread_ref,
    first_ref,
    second_ref,
    scale_ref,
    scaled_ref,
    inv_ref,
    held_ref,
    feat_ref,
    couple_ref,
):
    back = jnp.dot(
        spread_ref[...],
        wide_projector(first_ref, second_ref, copies),
        preferred_element_type=jnp.float32,
    )
    feat_ref[...] = standardize_adjoint(
        back * scale_ref[...], scaled_ref[...], inv_ref[...]
    ).astype(jnp.bfloat16)
    couple_ref[...] = held_ref[...]


def swap_line(block, partners):
    count = lax.axis_size("col")
    pairs = [
        (depth * count + at, depth * count + (at ^ partner))
        for depth, partner in enumerate(partners)
        if partner is not None
        for at in range(count)
    ]
    return lax.ppermute(block, ("depth", "col"), pairs)


def swap_depth(block):
    return lax.ppermute(block, "depth", [(0, 1), (1, 0)])


def pairwise_sum(blocks):
    while len(blocks) > 1:
        blocks = [blocks[at] + blocks[at + 1] for at in range(0, len(blocks), 2)]
    return blocks[0]


def swap_col(block, partner):
    count = lax.axis_size("col")
    return lax.ppermute(block, "col", [(at, at ^ partner) for at in range(count)])


def whole_plan(
    alignment_activations,
    alignment_mask,
    pair_activation_input,
    pair_update_mask,
    pair_output_gradient,
    layer_scale_factor,
    first_projector,
    second_projector,
    output_weight,
    pair_norm_gain,
    hidden_weight,
    back_weight,
):
    seqs, res, channels = alignment_activations.shape
    width = first_projector.shape[1]
    outer_width = width * width
    cols = lax.axis_size("col")
    depths = lax.axis_size("depth")
    residues = res * cols
    pair_cols, pair_width = pair_activation_input.shape[1:]
    hid = hidden_weight.shape[1]
    per = res * pair_cols
    lanes = res * width
    rows = 2 * seqs + MASK_ROWS
    half = residues * pair_cols
    f32, bf16 = jnp.float32, jnp.bfloat16
    ids = jnp.stack([lax.axis_index("depth"), lax.axis_index("col")]).astype(jnp.int32)
    smem = pl.BlockSpec(memory_space=pltpu.SMEM)
    vmem = pl.BlockSpec(memory_space=pltpu.VMEM)
    params = pltpu.CompilerParams(vmem_limit_bytes=16 * 2**20)
    scale = layer_scale_factor.reshape(1, channels)
    first, second = first_projector.T, second_projector.T
    wturn = jnp.transpose(output_weight.reshape(width, width, pair_width), (1, 0, 2)).reshape(
        outer_width, pair_width
    )
    shape = jax.ShapeDtypeStruct
    sent, scale, first, second, gain, normed, scaled, inv = pl.pallas_call(
        pre_kernel,
        out_shape=(
            shape((1, rows + 2 * per, pair_width), bf16),
            shape((1, channels), f32),
            shape((width, channels), bf16),
            shape((width, channels), bf16),
            shape((1, pair_width), f32),
            shape((seqs * res, channels), bf16),
            shape((seqs * res, channels), f32),
            shape((seqs * res, 1), f32),
        ),
        in_specs=[smem] + [pl.BlockSpec(memory_space=pltpu.HBM)] * 9,
        out_specs=[vmem] * 8,
        scratch_shapes=[
            pltpu.VMEM((2, seqs * res, lanes), f32),
            pltpu.VMEM((MASK_ROWS, lanes), f32),
            pltpu.VMEM((seqs, res, channels), bf16),
            pltpu.VMEM((res, seqs), jnp.int32),
            pltpu.VMEM((res, pair_cols), jnp.int32),
            pltpu.SemaphoreType.DMA((9,)),
        ],
        compiler_params=params,
        name="project",
    )(
        ids,
        *[
            pltpu.with_memory_space_constraint(array, pltpu.HBM)
            for array in (
                alignment_activations,
                alignment_mask.T,
                pair_update_mask,
                scale,
                first,
                second,
                pair_norm_gain.reshape(1, pair_width),
                pair_activation_input.reshape(per, pair_width),
                pair_output_gradient.reshape(per, pair_width),
            )
        ],
    )
    blocks = lax.optimization_barrier(
        jnp.concatenate([sent] + [swap_col(sent, partner) for partner in Z_PARTNERS])
    )
    far_normed = swap_col(normed, Y_PARTNER)
    blocks, far_normed = lax.optimization_barrier((blocks, far_normed))
    near, pair_near = blocks[:, :rows], blocks[:, rows:]
    far = swap_col(near, Y_PARTNER)
    pair_far = swap_col(pair_near, Y_PARTNER)
    other_near, other_far = swap_depth(near), swap_depth(far)
    sizes = (seqs, res, pair_cols, width)
    outer, proj_out, cnt, pm, maskt, rightt, leftt = pl.pallas_call(
        functools.partial(outer_kernel, sizes),
        out_shape=(
            shape((half, outer_width), bf16),
            shape((half, pair_width), f32),
            shape((half, lanes), f32),
            shape((half, lanes), bf16),
            shape((residues, depths * seqs), f32),
            shape((residues * width, depths * seqs), bf16),
            shape((residues * width, depths * seqs), bf16),
        ),
        in_specs=[smem] + [vmem] * 5,
        out_specs=[vmem] * 7,
        scratch_shapes=[
            pltpu.VMEM((depths * seqs, residues * width), bf16),
            pltpu.VMEM((pair_cols * width, depths * seqs), bf16),
            pltpu.VMEM((residues * width, depths * seqs), f32),
            pltpu.VMEM((residues * width, depths * seqs), f32),
            pltpu.VMEM((half, lanes), bf16),
            pltpu.VMEM((half, lanes), bf16),
        ],
        compiler_params=params,
        name="outer_products",
    )(ids, near, far, other_near, other_far, wturn)
    normed_again, far_again, proj_out = lax.optimization_barrier((normed, far_normed, proj_out))
    other_normed, other_far_normed = swap_depth(normed_again), swap_depth(far_again)
    pair_far, proj_out, other_normed, other_far_normed = lax.optimization_barrier(
        (pair_far, proj_out, other_normed, other_far_normed)
    )
    held, opm, pn, gh, hidden, mg = pl.pallas_call(
        functools.partial(transition_kernel, sizes),
        out_shape=(
            shape((per, pair_width), bf16),
            shape((half, pair_width), bf16),
            shape((half, pair_width), bf16),
            shape((half, hid), bf16),
            shape((half, hid), bf16),
            shape((half, pair_width), bf16),
        ),
        in_specs=[smem] + [vmem] * 8,
        out_specs=[vmem] * 6,
        scratch_shapes=[
            pltpu.VMEM((half, pair_width), f32),
        ],
        compiler_params=params,
        name="transition",
    )(
        ids,
        pair_near,
        pair_far,
        proj_out,
        cnt,
        pm,
        gain,
        hidden_weight,
        back_weight,
    )
    weights = pl.pallas_call(
        weights_kernel,
        out_shape=shape((outer_width + 2 * hid, pair_width), bf16),
        in_specs=[vmem] * 6,
        out_specs=vmem,
        scratch_shapes=[pltpu.VMEM((outer_width, pair_width), f32)],
        compiler_params=params,
        name="weight_gradients",
    )(outer, opm, pn, gh, hidden, mg)
    other_opm, weights = lax.optimization_barrier((swap_depth(opm), weights))
    part, spread = pl.pallas_call(
        functools.partial(projector_kernel, sizes),
        out_shape=(
            shape((2 * width, channels), bf16),
            shape((seqs * res, 2 * lanes), bf16),
        ),
        in_specs=[smem] + [vmem] * 11,
        out_specs=[vmem] * 2,
        scratch_shapes=[
            pltpu.VMEM((half, pair_width), f32),
            pltpu.VMEM((2 * res * residues, pair_width), bf16),
            pltpu.VMEM((2 * res * residues, pair_width), bf16),
            pltpu.VMEM((residues * width, 2 * lanes), bf16),
            pltpu.VMEM((residues * width, 2 * lanes), bf16),
            pltpu.VMEM((2, 2, depths, seqs * res, lanes), f32),
            pltpu.VMEM((2, depths, seqs * res, channels), bf16),
        ],
        compiler_params=params,
        name="projector_parts",
    )(
        ids,
        opm,
        other_opm,
        rightt,
        leftt,
        output_weight,
        wturn,
        maskt,
        normed,
        far_normed,
        other_normed,
        other_far_normed,
    )
    feat, couple = pl.pallas_call(
        functools.partial(feature_kernel, res),
        out_shape=(shape((seqs * res, channels), bf16), shape((per, pair_width), bf16)),
        in_specs=[vmem] * 7,
        out_specs=[vmem] * 2,
        compiler_params=params,
        name="features",
    )(spread, first, second, scale, scaled, inv, held)
    part, weights = lax.optimization_barrier((part, weights))
    dout, dhid, dback = pl.pallas_call(
        weights_sum_kernel,
        out_shape=(
            shape((outer_width, pair_width), f32),
            shape((pair_width, hid), f32),
            shape((hid, pair_width), f32),
        ),
        in_specs=[vmem] * 2,
        out_specs=[vmem] * 3,
        compiler_params=params,
        name="sums_over_depth",
    )(weights, swap_depth(weights))
    came_b = swap_line(part, (None, Z_PARTNERS[0]))
    came_a = swap_line(part, (Z_PARTNERS[2], Z_PARTNERS[1]))
    feat = feat.reshape(seqs, res, channels)
    came_b, came_a, feat, couple = lax.optimization_barrier((came_b, came_a, feat, couple))
    kept = jnp.where(lax.axis_index("depth") == 0, part, came_b)
    kept = lax.optimization_barrier((kept.astype(f32) + came_a.astype(f32)).astype(bf16))
    came = swap_depth(kept)
    came, dout, dhid, dback = lax.optimization_barrier((came, dout, dhid, dback))
    total = kept.astype(f32) + came.astype(f32)
    return (
        feat,
        couple.reshape(res, pair_cols, pair_width),
        total[:width].T,
        total[width:].T,
        dout,
        dhid,
        dback,
    )


def on_device(alignment_activations, *others):
    cols = lax.axis_size("col")
    residues = alignment_activations.shape[1] * cols
    plan = whole_plan if cols == 8 and residues <= FEW_RESIDUES else split_plan
    return plan(alignment_activations, *others)


def solution(mesh):
    in_specs = (
        P(("group", "depth"), "col", None),
        P(("group", "depth"), "col"),
        P(("group", "col"), "depth", None),
        P(("group", "col"), "depth"),
        P(("group", "col"), "depth", None),
        P(),
        P(),
        P(),
        P(),
        P(),
        P(),
        P(),
    )
    out_specs = (
        P(("group", "depth"), "col", None),
        P(("group", "col"), "depth", None),
        P("group", None),
        P("group", None),
        P("group", None),
        P("group", None),
        P("group", None),
    )
    return jax.shard_map(
        on_device, mesh=mesh, in_specs=in_specs, out_specs=out_specs, check_vma=False
    )
```

```python
import functools

import jax
import jax.numpy as jnp
from jax import lax
from jax.experimental import pallas as pl
from jax.experimental.pallas import tpu as pltpu
from jax.sharding import PartitionSpec as P

epsilon = 1e-05
highest = lax.Precision.HIGHEST


def norm_pieces(entries_drawn):
    center = entries_drawn - jnp.mean(entries_drawn, axis=-1, keepdims=True)
    inv_std = lax.rsqrt(jnp.mean(center * center, axis=-1, keepdims=True) + epsilon)
    return (center * inv_std, inv_std)


def standardize_adjoint(grad_scaled, scaled, inv_std):
    mean_grad = jnp.mean(grad_scaled, axis=-1, keepdims=True)
    mean_cross = jnp.mean(grad_scaled * scaled, axis=-1, keepdims=True)
    return inv_std * (grad_scaled - mean_grad - scaled * mean_cross)


def silu_pieces(pre_act):
    sigma = jax.nn.sigmoid(pre_act)
    return (pre_act * sigma, sigma * (1.0 + pre_act * (1.0 - sigma)))


def split_plan(
    alignment_activations,
    alignment_mask,
    pair_activation_input,
    pair_update_mask,
    pair_output_gradient,
    layer_scale_factor,
    first_projector,
    second_projector,
    output_weight,
    pair_norm_gain,
    hidden_weight,
    back_weight,
):
    sequence_row_block, residue_row_block, channel_total = alignment_activations.shape
    proj_width = first_projector.shape[1]
    outer_width = proj_width * proj_width
    depth_count = lax.axis_size("depth")
    residues = residue_row_block * lax.axis_size("col")
    pair_cols = pair_activation_input.shape[1]
    pair_width = pair_activation_input.shape[2]
    col_block = min(64, pair_cols)
    block_count = pair_cols // col_block
    standardized_features, reciprocal_spread = norm_pieces(
        alignment_activations.astype(jnp.float32)
    )
    normalized_rows = (standardized_features * layer_scale_factor).astype(jnp.bfloat16)
    mask_floating = alignment_mask.astype(jnp.float32)
    left_proj = (
        jnp.dot(normalized_rows, first_projector, preferred_element_type=jnp.float32)
        * mask_floating[:, :, None]
    ).astype(jnp.bfloat16)
    right_proj = (
        jnp.dot(normalized_rows, second_projector, preferred_element_type=jnp.float32)
        * mask_floating[:, :, None]
    ).astype(jnp.bfloat16)
    right_flat = right_proj.reshape(sequence_row_block, residue_row_block * proj_width)
    mask_converted = alignment_mask.astype(jnp.bfloat16)
    seq_total = left_proj.shape[0]
    gathered, gathered_mask = (
        lax.all_gather(right_flat, "col", axis=1, tiled=True),
        lax.all_gather(mask_converted, "col", axis=1, tiled=True),
    )
    right_blocks = gathered.reshape(seq_total, depth_count, pair_cols, proj_width)
    mask_blocks = gathered_mask.reshape(seq_total, depth_count, pair_cols)
    block_depth = right_blocks.shape[1]
    out_wide = output_weight.astype(jnp.float32)

    def partial_outer(col_start):
        right_piece = lax.dynamic_slice_in_dim(right_blocks, col_start, col_block, 2)
        outer_part = jnp.einsum(
            "sic,sejd->iejcd", left_proj, right_piece, preferred_element_type=jnp.float32
        )
        return (
            outer_part.reshape(residue_row_block, block_depth, col_block, outer_width),
            right_piece,
        )

    def forward_step(step_index, loop_state):
        projected, pair_count = loop_state
        col_start = step_index * col_block
        outer_part, right_piece = partial_outer(col_start)
        mask_piece = lax.dynamic_slice_in_dim(mask_blocks, col_start, col_block, 2).astype(
            jnp.float32
        )
        count_part = jnp.einsum("si,sej->iej", mask_floating, mask_piece, precision=highest)
        outer_mine, count_mine = (
            lax.psum_scatter(
                outer_part.astype(jnp.bfloat16), "depth", scatter_dimension=1, tiled=True
            ).astype(jnp.float32),
            lax.psum_scatter(
                count_part.astype(jnp.bfloat16), "depth", scatter_dimension=1, tiled=True
            ).astype(jnp.float32),
        )
        proj_mine = jnp.dot(
            outer_mine.reshape(residue_row_block * col_block, outer_width),
            out_wide,
            precision=highest,
        )
        proj_mine = proj_mine.reshape(residue_row_block, col_block, pair_width)
        count_mine = count_mine.reshape(residue_row_block, col_block)
        projected = lax.dynamic_update_slice_in_dim(projected, proj_mine, col_start, 1)
        pair_count = lax.dynamic_update_slice_in_dim(pair_count, count_mine, col_start, 1)
        return (projected, pair_count)

    projected, pair_count = lax.fori_loop(
        0,
        block_count,
        forward_step,
        (
            jnp.zeros((residue_row_block, pair_cols, pair_width), jnp.float32),
            jnp.zeros((residue_row_block, pair_cols), jnp.float32),
        ),
    )
    count_column = pair_count.reshape(residue_row_block * pair_cols, 1)
    mid_act = (
        pair_activation_input.reshape(residue_row_block * pair_cols, pair_width).astype(jnp.float32)
        + projected.reshape(residue_row_block * pair_cols, pair_width) / count_column
    )
    pair_scaled, pair_inv = norm_pieces(mid_act)
    pair_normed = (pair_scaled * pair_norm_gain).astype(jnp.bfloat16)
    pre_act = jnp.dot(pair_normed, hidden_weight, preferred_element_type=jnp.float32)
    act_value, act_slope = silu_pieces(pre_act)
    hidden = act_value.astype(jnp.bfloat16)
    masked_grad = (
        pair_output_gradient * pair_update_mask.astype(jnp.bfloat16)[:, :, None]
    ).reshape(residue_row_block * pair_cols, pair_width)
    final_matrix_derivative = jnp.dot(hidden.T, masked_grad, preferred_element_type=jnp.float32)
    back_prod = jnp.dot(masked_grad, back_weight.T, preferred_element_type=jnp.float32)
    grad_hidden = (back_prod * act_slope).astype(jnp.bfloat16)
    middle_matrix_derivative = jnp.dot(
        pair_normed.T, grad_hidden, preferred_element_type=jnp.float32
    )
    grad_scaled = (
        jnp.dot(grad_hidden, hidden_weight.T, preferred_element_type=jnp.float32) * pair_norm_gain
    )
    grad_mid = pair_output_gradient.reshape(residue_row_block * pair_cols, pair_width).astype(
        jnp.float32
    ) + standardize_adjoint(grad_scaled, pair_scaled, pair_inv)
    couple_features_derivative = grad_mid.astype(jnp.bfloat16).reshape(
        residue_row_block, pair_cols, pair_width
    )
    grad_opm = (
        (grad_mid / count_column)
        .astype(jnp.bfloat16)
        .reshape(residue_row_block, pair_cols, pair_width)
    )
    full_opm = lax.all_gather(grad_opm, "depth", axis=1, tiled=True).reshape(
        residue_row_block, depth_count, pair_cols, pair_width
    )

    def backward_step(step_index, loop_state):
        grad_left_acc, grad_out, right_term = loop_state
        col_start = step_index * col_block
        outer_part, right_piece = partial_outer(col_start)
        opm_piece = lax.dynamic_slice_in_dim(full_opm, col_start, col_block, 2).reshape(
            residue_row_block * block_depth * col_block, pair_width
        )
        grad_out = grad_out + jnp.dot(
            outer_part.reshape(residue_row_block * block_depth * col_block, outer_width).T,
            opm_piece.astype(jnp.float32),
            precision=highest,
        )
        grad_outer = jnp.dot(opm_piece, output_weight.T, preferred_element_type=jnp.float32).astype(
            jnp.bfloat16
        )
        grad_outer = grad_outer.reshape(
            residue_row_block, block_depth, col_block, proj_width, proj_width
        )
        grad_left_acc = grad_left_acc + jnp.einsum(
            "iejcd,sejd->sic", grad_outer, right_piece, preferred_element_type=jnp.float32
        )
        piece_term = jnp.einsum(
            "iejcd,sic->ejsd", grad_outer, left_proj, preferred_element_type=jnp.float32
        )
        piece_term = piece_term.reshape(block_depth, col_block, seq_total * proj_width)
        right_term = lax.dynamic_update_slice_in_dim(right_term, piece_term, col_start, 1)
        return (grad_left_acc, grad_out, right_term)

    grad_left_acc, result_matrix_derivative, right_term = lax.fori_loop(
        0,
        block_count,
        backward_step,
        (
            jnp.zeros((seq_total, residue_row_block, proj_width), jnp.float32),
            jnp.zeros((outer_width, pair_width), jnp.float32),
            jnp.zeros((block_depth, pair_cols, seq_total * proj_width), jnp.float32),
        ),
    )
    grad_right_sum = lax.psum_scatter(
        right_term.reshape(residues, seq_total * proj_width), "col", scatter_dimension=0, tiled=True
    )
    grad_right_acc = jnp.transpose(
        grad_right_sum.reshape(residue_row_block, seq_total, proj_width), (1, 0, 2)
    )
    grad_left = (grad_left_acc * mask_floating[:, :, None]).astype(jnp.bfloat16)
    grad_right = (grad_right_acc * mask_floating[:, :, None]).astype(jnp.bfloat16)
    normed_rows = normalized_rows.reshape(sequence_row_block * residue_row_block, channel_total)
    first_projector_derivative = jnp.dot(
        normed_rows.T,
        grad_left.reshape(sequence_row_block * residue_row_block, proj_width),
        preferred_element_type=jnp.float32,
    )
    second_projector_derivative = jnp.dot(
        normed_rows.T,
        grad_right.reshape(sequence_row_block * residue_row_block, proj_width),
        preferred_element_type=jnp.float32,
    )
    standardized_derivative = jnp.dot(
        grad_left, first_projector.T, preferred_element_type=jnp.float32
    ) + jnp.dot(grad_right, second_projector.T, preferred_element_type=jnp.float32)
    features_derivative = standardize_adjoint(
        standardized_derivative * layer_scale_factor, standardized_features, reciprocal_spread
    ).astype(jnp.bfloat16)
    weight_sums = lax.psum(
        (
            first_projector_derivative,
            second_projector_derivative,
            result_matrix_derivative,
            middle_matrix_derivative,
            final_matrix_derivative,
        ),
        ("depth", "col"),
    )
    return (
        features_derivative,
        couple_features_derivative,
        weight_sums[0],
        weight_sums[1],
        weight_sums[2],
        weight_sums[3],
        weight_sums[4],
    )


FEW_RESIDUES = 32
MASK_ROWS = 16
Z_PARTNERS = (2, 4, 6)
Y_PARTNER = 1


def butterfly(blocks, group):
    lane_group = lax.broadcasted_iota(jnp.int32, blocks[0].shape, 1) // group
    width = 4 * group
    for bit in (2, 1):
        low = (lane_group & bit) == 0
        swapped = list(blocks)
        for at in range(4):
            if at & bit:
                continue
            here, there = blocks[at], blocks[at | bit]
            moving = jnp.where(low, there, here)
            if bit == 2:
                moved = pltpu.roll(moving, 2 * group, 1)
            else:
                moved = jnp.where(
                    low, pltpu.roll(moving, width - group, 1), pltpu.roll(moving, group, 1)
                )
            swapped[at] = jnp.where(low, here, moved)
            swapped[at | bit] = jnp.where(low, moved, there)
        blocks = swapped
    return blocks


def wide_projector(first_ref, second_ref, copies):
    return jnp.concatenate([first_ref[...]] * copies + [second_ref[...]] * copies, axis=0)


def pre_kernel(
    ids_ref,
    x_hbm,
    maskt_hbm,
    pmask_hbm,
    scale_hbm,
    first_hbm,
    second_hbm,
    gain_hbm,
    act_hbm,
    grad_hbm,
    sent_ref,
    scale_ref,
    first_ref,
    second_ref,
    gain_ref,
    normed_ref,
    scaled_ref,
    inv_ref,
    wide_ref,
    tile_ref,
    x_ref,
    maskt_ref,
    pmask_ref,
    sems,
):
    res, seqs = maskt_ref.shape
    pairs = act_hbm.shape[0]
    first_pair = 2 * seqs + MASK_ROWS
    copies = [
        pltpu.make_async_copy(source, target, sems.at[at])
        for at, (source, target) in enumerate(
            (
                (x_hbm, x_ref),
                (maskt_hbm, maskt_ref),
                (pmask_hbm, pmask_ref),
                (scale_hbm, scale_ref),
                (first_hbm, first_ref),
                (second_hbm, second_ref),
                (gain_hbm, gain_ref),
                (act_hbm, sent_ref.at[0, pl.ds(first_pair, pairs), :]),
                (grad_hbm, sent_ref.at[0, pl.ds(first_pair + pairs, pairs), :]),
            )
        )
    ]
    for copy in copies:
        copy.start()
    for copy in copies:
        copy.wait()
    lanes = sent_ref.shape[2]
    group = lanes // res
    scaled, inv = norm_pieces(
        x_ref[...].astype(jnp.float32).reshape(seqs * res, x_ref.shape[2])
    )
    scaled_ref[...] = scaled
    inv_ref[...] = inv
    normed = (scaled * scale_ref[...]).astype(jnp.bfloat16)
    normed_ref[...] = normed
    wide = lax.dot_general(
        normed,
        wide_projector(first_ref, second_ref, res),
        (((1,), (1,)), ((), ())),
        preferred_element_type=jnp.float32,
    )
    for at in range(2):
        wide_ref[at] = wide[:, at * lanes : (at + 1) * lanes]
    tile_ref[...] = jnp.zeros(tile_ref.shape, jnp.float32)
    mask = maskt_ref[...].astype(jnp.float32)
    tile_ref[0:res, 0:seqs] = mask
    spread = (
        lax.broadcasted_iota(jnp.int32, (MASK_ROWS, lanes), 1) // group
        == lax.broadcasted_iota(jnp.int32, (MASK_ROWS, lanes), 0)
    ).astype(jnp.float32)
    mask_lanes = lax.dot_general(
        tile_ref[...], spread, (((0,), (0,)), ((), ())), preferred_element_type=jnp.float32
    )[:seqs]
    twice = jnp.concatenate([mask] * (lanes // seqs), axis=1)
    here = lax.broadcasted_iota(jnp.int32, (res, lanes), 1) // seqs == ids_ref[0]
    tile_ref[0:res, :] = jnp.where(here, twice, 0.0)
    tile_ref[res : 2 * res, 0 : pmask_ref.shape[1]] = pmask_ref[...].astype(jnp.float32)
    lane_group = lax.broadcasted_iota(jnp.int32, (seqs, lanes), 1) // group
    for at in range(2):
        both = wide_ref[at, pl.ds(0, seqs, stride=res), :]
        for r in range(1, res):
            both = jnp.where(
                lane_group == r, wide_ref[at, pl.ds(r, seqs, stride=res), :], both
            )
        sent_ref[0, at * seqs : (at + 1) * seqs, :] = (both * mask_lanes).astype(jnp.bfloat16)
    sent_ref[0, 2 * seqs : first_pair, :] = tile_ref[...].astype(jnp.bfloat16)


def by_owner(ids_ref, z, near_ref, far_ref):
    step = z ^ (ids_ref[1] // 2)
    near, far = near_ref[step], far_ref[step]
    first = ids_ref[1] % 2 == 0
    return jnp.where(first, near, far), jnp.where(first, far, near)


def outer_kernel(
    sizes,
    ids_ref,
    near_ref,
    far_ref,
    other_near_ref,
    other_far_ref,
    wturn_ref,
    outer_ref,
    proj_out_ref,
    cnt_ref,
    pm_ref,
    maskt_ref,
    rightt_ref,
    leftt_ref,
    leftn_ref,
    mine_ref,
    turnl_ref,
    turnr_ref,
    cntl_ref,
    pml_ref,
):
    seqs, res, pair_cols, width = sizes
    line = near_ref.shape[0]
    cols = 2 * line
    residues = cols * res
    lanes = res * width
    me_depth = ids_ref[0]
    lower = me_depth == 0
    f32, bf16 = jnp.float32, jnp.bfloat16

    for z in range(line):
        mine = by_owner(ids_ref, z, near_ref, far_ref)
        other = by_owner(ids_ref, z, other_near_ref, other_far_ref)
        for y in range(2):
            lanes_k = slice((2 * z + y) * lanes, (2 * z + y + 1) * lanes)
            both = jnp.concatenate(
                [
                    jnp.where(lower, mine[y], other[y]),
                    jnp.where(lower, other[y], mine[y]),
                ],
                axis=0,
            )
            rows = both.shape[0] // 2
            left = jnp.concatenate([both[0:seqs], both[rows : rows + seqs]], axis=0)
            right = jnp.concatenate(
                [both[seqs : 2 * seqs], both[rows + seqs : rows + 2 * seqs]], axis=0
            )
            leftn_ref[:, lanes_k] = left
            turnl_ref[lanes_k, :] = left.astype(f32).T
            turnr_ref[lanes_k, :] = right.astype(f32).T
            tiles = [
                both[first + 2 * seqs : first + 2 * seqs + MASK_ROWS].astype(f32)
                for first in (0, rows)
            ]
            maskt_ref[(2 * z + y) * res : (2 * z + y + 1) * res, :] = (
                tiles[0][0:res] + tiles[1][0:res]
            )
            own = mine[y][2 * seqs : 2 * seqs + MASK_ROWS].astype(f32)
            pair_lane = lax.broadcasted_iota(jnp.int32, (pair_cols, lanes), 1)
            pair_row = lax.broadcasted_iota(jnp.int32, (pair_cols, lanes), 0)
            for r in range(res):
                first = ((2 * z + y) * res + r) * pair_cols
                pml_ref[first : first + pair_cols, :] = jnp.where(
                    pair_lane == pair_row, own[res + r : res + r + 1, :], 0.0
                ).astype(bf16)
    for d in range(width):
        mine_ref[d * pair_cols : (d + 1) * pair_cols, :] = turnr_ref[
            pl.ds(me_depth * pair_cols * width + d, pair_cols, stride=width), :
        ].astype(bf16)
    for turned, out in ((turnl_ref, leftt_ref), (turnr_ref, rightt_ref)):
        for d in range(width):
            out[d * residues : (d + 1) * residues, :] = turned[
                pl.ds(d, residues, stride=width), :
            ].astype(bf16)

    maskt = maskt_ref[...]
    cols_mask = maskt_ref[pl.ds(pl.multiple_of(me_depth * pair_cols, pair_cols), pair_cols), :]
    for i in range(residues):
        cntl_ref[i * pair_cols : (i + 1) * pair_cols, :] = (maskt[i : i + 1, :] * cols_mask).astype(
            bf16
        )
    ones = jnp.ones((lanes, lanes), bf16)
    cnt_ref[...] = jnp.dot(cntl_ref[...], ones, preferred_element_type=f32)
    pm_ref[...] = jnp.dot(pml_ref[...], ones, preferred_element_type=f32).astype(bf16)

    for dh in range(width // 4):
        prod = jnp.dot(
            mine_ref[dh * 4 * pair_cols : (dh + 1) * 4 * pair_cols, :],
            leftn_ref[...],
            preferred_element_type=f32,
        )
        for k in range(cols):
            piece = prod[:, k * lanes : (k + 1) * lanes]
            turned = butterfly(
                [piece[a * pair_cols : (a + 1) * pair_cols] for a in range(4)], width
            )
            for il in range(res):
                first = (k * res + il) * pair_cols
                outer_ref[first : first + pair_cols, dh * lanes : (dh + 1) * lanes] = turned[
                    il
                ].astype(bf16)
    proj_out_ref[...] = jnp.dot(outer_ref[...], wturn_ref[...], preferred_element_type=f32)


def transition_kernel(
    sizes,
    ids_ref,
    near_ref,
    far_ref,
    proj_out_ref,
    cnt_ref,
    pm_ref,
    gain_ref,
    hid_ref,
    back_ref,
    couple_ref,
    opm_ref,
    pn_ref,
    gh_ref,
    hidden_ref,
    mg_ref,
    gmid_ref,
):
    seqs, res, pair_cols, width = sizes
    per = res * pair_cols
    cols = 2 * near_ref.shape[0]
    me_col = ids_ref[1]
    f32, bf16 = jnp.float32, jnp.bfloat16
    gain = gain_ref[...]
    chunk = 2 * per
    for at in range(cols // 2):
        rows = slice(at * chunk, (at + 1) * chunk)
        blocks = by_owner(ids_ref, at, near_ref, far_ref)
        act, grad = [
            jnp.concatenate([block[w * per : (w + 1) * per] for block in blocks], axis=0)
            for w in range(2)
        ]
        count = cnt_ref[rows, :]
        mid = act.astype(f32) + proj_out_ref[rows, :] / count
        scaled, inv = norm_pieces(mid)
        normed = (scaled * gain).astype(bf16)
        pn_ref[rows, :] = normed
        pre = jnp.dot(normed, hid_ref[...], preferred_element_type=f32)
        value, slope = silu_pieces(pre)
        hidden_ref[rows, :] = value.astype(bf16)
        masked = grad * pm_ref[rows, :]
        mg_ref[rows, :] = masked
        back = lax.dot_general(
            masked, back_ref[...], (((1,), (1,)), ((), ())), preferred_element_type=f32
        )
        ghid = (back * slope).astype(bf16)
        gh_ref[rows, :] = ghid
        gsc = (
            lax.dot_general(
                ghid, hid_ref[...], (((1,), (1,)), ((), ())), preferred_element_type=f32
            )
            * gain
        )
        gmid = grad.astype(f32) + standardize_adjoint(gsc, scaled, inv)
        gmid_ref[rows, :] = gmid
        opm_ref[rows, :] = (gmid / count).astype(bf16)
    couple_ref[...] = gmid_ref[pl.ds(pl.multiple_of(me_col * per, per), per), :].astype(bf16)


def projector_kernel(
    sizes,
    ids_ref,
    opm_ref,
    other_opm_ref,
    rightt_ref,
    leftt_ref,
    wout_ref,
    wturn_ref,
    maskt_ref,
    normed_ref,
    far_normed_ref,
    other_normed_ref,
    other_far_normed_ref,
    part_ref,
    spread_ref,
    gf_ref,
    grow_ref,
    gcol_ref,
    gor_ref,
    goc_ref,
    gs_ref,
    rows_ref,
):
    seqs, res, pair_cols, width = sizes
    depths, half = rows_ref.shape[1], gf_ref.shape[0]
    residues = half // pair_cols
    lanes = res * width
    here = 2 * res
    me_depth = ids_ref[0]
    me_col = ids_ref[1]
    me_y = me_col % 2
    first_here = (me_col // 2) * here
    f32, bf16 = jnp.float32, jnp.bfloat16
    my_half = first_here // pair_cols
    gf_ref[...] = jnp.where(my_half == me_depth, opm_ref[...], other_opm_ref[...]).astype(f32)
    for y, e, block in (
        (me_y, me_depth, normed_ref),
        (1 - me_y, me_depth, far_normed_ref),
        (me_y, 1 - me_depth, other_normed_ref),
        (1 - me_y, 1 - me_depth, other_far_normed_ref),
    ):
        rows_ref[y, e] = block[...]

    for il in range(here):
        first = pl.multiple_of((first_here + il) * pair_cols, pair_cols)
        for e, block in ((me_depth, opm_ref), (1 - me_depth, other_opm_ref)):
            to = pl.multiple_of(il * residues + e * pair_cols, pair_cols)
            grow_ref[pl.ds(to, pair_cols), :] = block[pl.ds(first, pair_cols), :]
    my_first = first_here - my_half * pair_cols
    for jl in range(here):
        gcol_ref[jl * residues : (jl + 1) * residues, :] = gf_ref[
            pl.ds(my_first + jl, residues, stride=pair_cols), :
        ].astype(bf16)
    for lhs, weight, out in ((grow_ref, wturn_ref, gor_ref), (gcol_ref, wout_ref, goc_ref)):
        for dh in range(width // 4):
            piece = lax.dot_general(
                lhs[...],
                weight[dh * lanes : (dh + 1) * lanes, :],
                (((1,), (1,)), ((), ())),
                preferred_element_type=f32,
            )
            for y in range(2):
                turned = butterfly(
                    [
                        piece[(y * res + a) * residues : (y * res + a + 1) * residues]
                        for a in range(4)
                    ],
                    width,
                )
                for dl in range(4):
                    first = (dh * 4 + dl) * residues
                    out[first : first + residues, y * lanes : (y + 1) * lanes] = turned[dl].astype(
                        bf16
                    )
    group = lax.broadcasted_iota(jnp.int32, (here, here * width), 1) // width
    spread = (group == lax.broadcasted_iota(jnp.int32, (here, here * width), 0)).astype(f32)
    mask_lanes = lax.dot_general(
        maskt_ref[pl.ds(pl.multiple_of(first_here, here), here), :],
        spread,
        (((0,), (0,)), ((), ())),
        preferred_element_type=f32,
    )
    lane_group = lax.broadcasted_iota(jnp.int32, (seqs, lanes), 1) // width
    for at, (lhs, rhs) in enumerate(((rightt_ref, gor_ref), (leftt_ref, goc_ref))):
        total = lax.dot_general(
            lhs[...], rhs[...], (((0,), (0,)), ((), ())), preferred_element_type=f32
        )
        total = (total * mask_lanes).astype(bf16).astype(f32)
        for y in range(2):
            for e in range(depths):
                block = total[e * seqs : (e + 1) * seqs, y * lanes : (y + 1) * lanes]
                for r in range(res):
                    gs_ref[at, y, e, pl.ds(r, seqs, stride=res), :] = jnp.where(
                        lane_group == r, block, 0.0
                    )
    spread_ref[...] = jnp.concatenate(
        [gs_ref[0, me_y, me_depth], gs_ref[1, me_y, me_depth]], axis=1
    ).astype(bf16)
    rows = rows_ref.shape[2]
    for at in range(2):
        cross = lax.dot_general(
            gs_ref[at].reshape(2 * depths * rows, lanes).astype(bf16),
            rows_ref[...].reshape(2 * depths * rows, rows_ref.shape[3]),
            (((0,), (0,)), ((), ())),
            preferred_element_type=f32,
        )
        total = cross[:width]
        for r in range(1, res):
            total = total + cross[r * width : (r + 1) * width]
        part_ref[at * width : (at + 1) * width, :] = total.astype(bf16)


def weights_kernel(outer_ref, opm_ref, pn_ref, gh_ref, hidden_ref, mg_ref, out_ref, turn_ref):
    pair_width, hid = pn_ref.shape[1], gh_ref.shape[1]
    outer_width = outer_ref.shape[1]
    width = int(outer_width**0.5 + 0.5)

    def contract(lhs, rhs):
        return lax.dot_general(
            lhs[...], rhs[...], (((0,), (0,)), ((), ())), preferred_element_type=jnp.float32
        )

    turn_ref[...] = contract(outer_ref, opm_ref)
    for c in range(width):
        out_ref[c * width : (c + 1) * width, :] = turn_ref[
            pl.ds(c, width, stride=width), :
        ].astype(jnp.bfloat16)
    dhid = contract(pn_ref, gh_ref).astype(jnp.bfloat16)
    for at in range(hid // pair_width):
        first = outer_width + at * pair_width
        out_ref[first : first + pair_width, :] = dhid[:, at * pair_width : (at + 1) * pair_width]
    out_ref[outer_width + hid :, :] = contract(hidden_ref, mg_ref).astype(jnp.bfloat16)


def finish_kernel(
    copies,
    spread_ref,
    first_ref,
    second_ref,
    scale_ref,
    scaled_ref,
    inv_ref,
    held_ref,
    mine_ref,
    other_ref,
    feat_ref,
    couple_ref,
    dout_ref,
    dhid_ref,
    dback_ref,
):
    back = jnp.dot(
        spread_ref[...],
        wide_projector(first_ref, second_ref, copies),
        preferred_element_type=jnp.float32,
    )
    feat = standardize_adjoint(back * scale_ref[...], scaled_ref[...], inv_ref[...])
    feat_ref[...] = feat.reshape(feat_ref.shape).astype(jnp.bfloat16)
    couple_ref[...] = held_ref[...]
    pair_width, hid = dhid_ref.shape
    outer_width = dout_ref.shape[0]

    def added(first, count):
        rows = slice(first, first + count)
        return mine_ref[rows, :].astype(jnp.float32) + other_ref[rows, :].astype(jnp.float32)

    dout_ref[...] = added(0, outer_width)
    for at in range(hid // pair_width):
        dhid_ref[:, at * pair_width : (at + 1) * pair_width] = added(
            outer_width + at * pair_width, pair_width
        )
    dback_ref[...] = added(outer_width + hid, hid)


def swap_line(block, partners):
    count = lax.axis_size("col")
    pairs = [
        (depth * count + at, depth * count + (at ^ partner))
        for depth, partner in enumerate(partners)
        if partner is not None
        for at in range(count)
    ]
    return lax.ppermute(block, ("depth", "col"), pairs)


def swap_depth(block):
    return lax.ppermute(block, "depth", [(0, 1), (1, 0)])


def pairwise_sum(blocks):
    while len(blocks) > 1:
        blocks = [blocks[at] + blocks[at + 1] for at in range(0, len(blocks), 2)]
    return blocks[0]


def swap_col(block, partner):
    count = lax.axis_size("col")
    return lax.ppermute(block, "col", [(at, at ^ partner) for at in range(count)])


def whole_plan(
    alignment_activations,
    alignment_mask,
    pair_activation_input,
    pair_update_mask,
    pair_output_gradient,
    layer_scale_factor,
    first_projector,
    second_projector,
    output_weight,
    pair_norm_gain,
    hidden_weight,
    back_weight,
):
    seqs, res, channels = alignment_activations.shape
    width = first_projector.shape[1]
    outer_width = width * width
    cols = lax.axis_size("col")
    depths = lax.axis_size("depth")
    residues = res * cols
    pair_cols, pair_width = pair_activation_input.shape[1:]
    hid = hidden_weight.shape[1]
    per = res * pair_cols
    lanes = res * width
    rows = 2 * seqs + MASK_ROWS
    half = residues * pair_cols
    f32, bf16 = jnp.float32, jnp.bfloat16
    ids = jnp.stack([lax.axis_index("depth"), lax.axis_index("col")]).astype(jnp.int32)
    smem = pl.BlockSpec(memory_space=pltpu.SMEM)
    vmem = pl.BlockSpec(memory_space=pltpu.VMEM)
    params = pltpu.CompilerParams(vmem_limit_bytes=16 * 2**20)
    scale = layer_scale_factor.reshape(1, channels)
    first, second = first_projector.T, second_projector.T
    wturn = jnp.transpose(output_weight.reshape(width, width, pair_width), (1, 0, 2)).reshape(
        outer_width, pair_width
    )
    shape = jax.ShapeDtypeStruct
    sent, scale, first, second, gain, normed, scaled, inv = pl.pallas_call(
        pre_kernel,
        out_shape=(
            shape((1, rows + 2 * per, pair_width), bf16),
            shape((1, channels), f32),
            shape((width, channels), bf16),
            shape((width, channels), bf16),
            shape((1, pair_width), f32),
            shape((seqs * res, channels), bf16),
            shape((seqs * res, channels), f32),
            shape((seqs * res, 1), f32),
        ),
        in_specs=[smem] + [pl.BlockSpec(memory_space=pltpu.HBM)] * 9,
        out_specs=[vmem] * 8,
        scratch_shapes=[
            pltpu.VMEM((2, seqs * res, lanes), f32),
            pltpu.VMEM((MASK_ROWS, lanes), f32),
            pltpu.VMEM((seqs, res, channels), bf16),
            pltpu.VMEM((res, seqs), jnp.int32),
            pltpu.VMEM((res, pair_cols), jnp.int32),
            pltpu.SemaphoreType.DMA((9,)),
        ],
        compiler_params=params,
        name="project",
    )(
        ids,
        *[
            pltpu.with_memory_space_constraint(array, pltpu.HBM)
            for array in (
                alignment_activations,
                alignment_mask.T,
                pair_update_mask,
                scale,
                first,
                second,
                pair_norm_gain.reshape(1, pair_width),
                pair_activation_input.reshape(per, pair_width),
                pair_output_gradient.reshape(per, pair_width),
            )
        ],
    )
    blocks = lax.optimization_barrier(
        jnp.concatenate([sent] + [swap_col(sent, partner) for partner in Z_PARTNERS])
    )
    far_normed = swap_col(normed, Y_PARTNER)
    blocks, far_normed = lax.optimization_barrier((blocks, far_normed))
    near, pair_near = blocks[:, :rows], blocks[:, rows:]
    far = swap_col(near, Y_PARTNER)
    pair_far = swap_col(pair_near, Y_PARTNER)
    other_near, other_far = swap_depth(near), swap_depth(far)
    sizes = (seqs, res, pair_cols, width)
    outer, proj_out, cnt, pm, maskt, rightt, leftt = pl.pallas_call(
        functools.partial(outer_kernel, sizes),
        out_shape=(
            shape((half, outer_width), bf16),
            shape((half, pair_width), f32),
            shape((half, lanes), f32),
            shape((half, lanes), bf16),
            shape((residues, depths * seqs), f32),
            shape((residues * width, depths * seqs), bf16),
            shape((residues * width, depths * seqs), bf16),
        ),
        in_specs=[smem] + [vmem] * 5,
        out_specs=[vmem] * 7,
        scratch_shapes=[
            pltpu.VMEM((depths * seqs, residues * width), bf16),
            pltpu.VMEM((pair_cols * width, depths * seqs), bf16),
            pltpu.VMEM((residues * width, depths * seqs), f32),
            pltpu.VMEM((residues * width, depths * seqs), f32),
            pltpu.VMEM((half, lanes), bf16),
            pltpu.VMEM((half, lanes), bf16),
        ],
        compiler_params=params,
        name="outer_products",
    )(ids, near, far, other_near, other_far, wturn)
    normed_again, far_again, proj_out = lax.optimization_barrier((normed, far_normed, proj_out))
    other_normed, other_far_normed = swap_depth(normed_again), swap_depth(far_again)
    pair_far, proj_out, other_normed, other_far_normed = lax.optimization_barrier(
        (pair_far, proj_out, other_normed, other_far_normed)
    )
    held, opm, pn, gh, hidden, mg = pl.pallas_call(
        functools.partial(transition_kernel, sizes),
        out_shape=(
            shape((per, pair_width), bf16),
            shape((half, pair_width), bf16),
            shape((half, pair_width), bf16),
            shape((half, hid), bf16),
            shape((half, hid), bf16),
            shape((half, pair_width), bf16),
        ),
        in_specs=[smem] + [vmem] * 8,
        out_specs=[vmem] * 6,
        scratch_shapes=[
            pltpu.VMEM((half, pair_width), f32),
        ],
        compiler_params=params,
        name="transition",
    )(
        ids,
        pair_near,
        pair_far,
        proj_out,
        cnt,
        pm,
        gain,
        hidden_weight,
        back_weight,
    )
    weights = pl.pallas_call(
        weights_kernel,
        out_shape=shape((outer_width + 2 * hid, pair_width), bf16),
        in_specs=[vmem] * 6,
        out_specs=vmem,
        scratch_shapes=[pltpu.VMEM((outer_width, pair_width), f32)],
        compiler_params=params,
        name="weight_gradients",
    )(outer, opm, pn, gh, hidden, mg)
    other_opm, weights = lax.optimization_barrier((swap_depth(opm), weights))
    part, spread = pl.pallas_call(
        functools.partial(projector_kernel, sizes),
        out_shape=(
            shape((2 * width, channels), bf16),
            shape((seqs * res, 2 * lanes), bf16),
        ),
        in_specs=[smem] + [vmem] * 11,
        out_specs=[vmem] * 2,
        scratch_shapes=[
            pltpu.VMEM((half, pair_width), f32),
            pltpu.VMEM((2 * res * residues, pair_width), bf16),
            pltpu.VMEM((2 * res * residues, pair_width), bf16),
            pltpu.VMEM((residues * width, 2 * lanes), bf16),
            pltpu.VMEM((residues * width, 2 * lanes), bf16),
            pltpu.VMEM((2, 2, depths, seqs * res, lanes), f32),
            pltpu.VMEM((2, depths, seqs * res, channels), bf16),
        ],
        compiler_params=params,
        name="projector_parts",
    )(
        ids,
        opm,
        other_opm,
        rightt,
        leftt,
        output_weight,
        wturn,
        maskt,
        normed,
        far_normed,
        other_normed,
        other_far_normed,
    )
    part, weights = lax.optimization_barrier((part, weights))
    feat, couple, dout, dhid, dback = pl.pallas_call(
        functools.partial(finish_kernel, res),
        out_shape=(
            shape((seqs, res, channels), bf16),
            shape((per, pair_width), bf16),
            shape((outer_width, pair_width), f32),
            shape((pair_width, hid), f32),
            shape((hid, pair_width), f32),
        ),
        in_specs=[vmem] * 9,
        out_specs=[vmem] * 5,
        compiler_params=params,
        name="finish",
    )(spread, first, second, scale, scaled, inv, held, weights, swap_depth(weights))
    came_b = swap_line(part, (None, Z_PARTNERS[0]))
    came_a = swap_line(part, (Z_PARTNERS[2], Z_PARTNERS[1]))
    came_b, came_a = lax.optimization_barrier((came_b, came_a))
    kept = jnp.where(lax.axis_index("depth") == 0, part, came_b)
    kept = lax.optimization_barrier((kept.astype(f32) + came_a.astype(f32)).astype(bf16))
    came = swap_depth(kept)
    came, feat, couple, dout, dhid, dback = lax.optimization_barrier(
        (came, feat, couple, dout, dhid, dback)
    )
    total = kept.astype(f32) + came.astype(f32)
    return (
        feat,
        couple.reshape(res, pair_cols, pair_width),
        total[:width].T,
        total[width:].T,
        dout,
        dhid,
        dback,
    )


def on_device(alignment_activations, *others):
    cols = lax.axis_size("col")
    residues = alignment_activations.shape[1] * cols
    plan = whole_plan if cols == 8 and residues <= FEW_RESIDUES else split_plan
    return plan(alignment_activations, *others)


def solution(mesh):
    in_specs = (
        P(("group", "depth"), "col", None),
        P(("group", "depth"), "col"),
        P(("group", "col"), "depth", None),
        P(("group", "col"), "depth"),
        P(("group", "col"), "depth", None),
        P(),
        P(),
        P(),
        P(),
        P(),
        P(),
        P(),
    )
    out_specs = (
        P(("group", "depth"), "col", None),
        P(("group", "col"), "depth", None),
        P("group", None),
        P("group", None),
        P("group", None),
        P("group", None),
        P("group", None),
    )
    return jax.shard_map(
        on_device, mesh=mesh, in_specs=in_specs, out_specs=out_specs, check_vma=False
    )
```

```python
import functools

import jax
import jax.numpy as jnp
from jax import lax
from jax.experimental import pallas as pl
from jax.experimental.pallas import tpu as pltpu
from jax.sharding import PartitionSpec as P

epsilon = 1e-05
highest = lax.Precision.HIGHEST


def norm_pieces(entries_drawn):
    center = entries_drawn - jnp.mean(entries_drawn, axis=-1, keepdims=True)
    inv_std = lax.rsqrt(jnp.mean(center * center, axis=-1, keepdims=True) + epsilon)
    return (center * inv_std, inv_std)


def standardize_adjoint(grad_scaled, scaled, inv_std):
    mean_grad = jnp.mean(grad_scaled, axis=-1, keepdims=True)
    mean_cross = jnp.mean(grad_scaled * scaled, axis=-1, keepdims=True)
    return inv_std * (grad_scaled - mean_grad - scaled * mean_cross)


def silu_pieces(pre_act):
    sigma = jax.nn.sigmoid(pre_act)
    return (pre_act * sigma, sigma * (1.0 + pre_act * (1.0 - sigma)))


def split_plan(
    alignment_activations,
    alignment_mask,
    pair_activation_input,
    pair_update_mask,
    pair_output_gradient,
    layer_scale_factor,
    first_projector,
    second_projector,
    output_weight,
    pair_norm_gain,
    hidden_weight,
    back_weight,
):
    sequence_row_block, residue_row_block, channel_total = alignment_activations.shape
    proj_width = first_projector.shape[1]
    outer_width = proj_width * proj_width
    depth_count = lax.axis_size("depth")
    residues = residue_row_block * lax.axis_size("col")
    pair_cols = pair_activation_input.shape[1]
    pair_width = pair_activation_input.shape[2]
    col_block = min(64, pair_cols)
    block_count = pair_cols // col_block
    standardized_features, reciprocal_spread = norm_pieces(
        alignment_activations.astype(jnp.float32)
    )
    normalized_rows = (standardized_features * layer_scale_factor).astype(jnp.bfloat16)
    mask_floating = alignment_mask.astype(jnp.float32)
    left_proj = (
        jnp.dot(normalized_rows, first_projector, preferred_element_type=jnp.float32)
        * mask_floating[:, :, None]
    ).astype(jnp.bfloat16)
    right_proj = (
        jnp.dot(normalized_rows, second_projector, preferred_element_type=jnp.float32)
        * mask_floating[:, :, None]
    ).astype(jnp.bfloat16)
    right_flat = right_proj.reshape(sequence_row_block, residue_row_block * proj_width)
    mask_converted = alignment_mask.astype(jnp.bfloat16)
    seq_total = left_proj.shape[0]
    gathered, gathered_mask = (
        lax.all_gather(right_flat, "col", axis=1, tiled=True),
        lax.all_gather(mask_converted, "col", axis=1, tiled=True),
    )
    right_blocks = gathered.reshape(seq_total, depth_count, pair_cols, proj_width)
    mask_blocks = gathered_mask.reshape(seq_total, depth_count, pair_cols)
    block_depth = right_blocks.shape[1]
    out_wide = output_weight.astype(jnp.float32)

    def partial_outer(col_start):
        right_piece = lax.dynamic_slice_in_dim(right_blocks, col_start, col_block, 2)
        outer_part = jnp.einsum(
            "sic,sejd->iejcd", left_proj, right_piece, preferred_element_type=jnp.float32
        )
        return (
            outer_part.reshape(residue_row_block, block_depth, col_block, outer_width),
            right_piece,
        )

    def forward_step(step_index, loop_state):
        projected, pair_count = loop_state
        col_start = step_index * col_block
        outer_part, right_piece = partial_outer(col_start)
        mask_piece = lax.dynamic_slice_in_dim(mask_blocks, col_start, col_block, 2).astype(
            jnp.float32
        )
        count_part = jnp.einsum("si,sej->iej", mask_floating, mask_piece, precision=highest)
        outer_mine, count_mine = (
            lax.psum_scatter(
                outer_part.astype(jnp.bfloat16), "depth", scatter_dimension=1, tiled=True
            ).astype(jnp.float32),
            lax.psum_scatter(
                count_part.astype(jnp.bfloat16), "depth", scatter_dimension=1, tiled=True
            ).astype(jnp.float32),
        )
        proj_mine = jnp.dot(
            outer_mine.reshape(residue_row_block * col_block, outer_width),
            out_wide,
            precision=highest,
        )
        proj_mine = proj_mine.reshape(residue_row_block, col_block, pair_width)
        count_mine = count_mine.reshape(residue_row_block, col_block)
        projected = lax.dynamic_update_slice_in_dim(projected, proj_mine, col_start, 1)
        pair_count = lax.dynamic_update_slice_in_dim(pair_count, count_mine, col_start, 1)
        return (projected, pair_count)

    projected, pair_count = lax.fori_loop(
        0,
        block_count,
        forward_step,
        (
            jnp.zeros((residue_row_block, pair_cols, pair_width), jnp.float32),
            jnp.zeros((residue_row_block, pair_cols), jnp.float32),
        ),
    )
    count_column = pair_count.reshape(residue_row_block * pair_cols, 1)
    mid_act = (
        pair_activation_input.reshape(residue_row_block * pair_cols, pair_width).astype(jnp.float32)
        + projected.reshape(residue_row_block * pair_cols, pair_width) / count_column
    )
    pair_scaled, pair_inv = norm_pieces(mid_act)
    pair_normed = (pair_scaled * pair_norm_gain).astype(jnp.bfloat16)
    pre_act = jnp.dot(pair_normed, hidden_weight, preferred_element_type=jnp.float32)
    act_value, act_slope = silu_pieces(pre_act)
    hidden = act_value.astype(jnp.bfloat16)
    masked_grad = (
        pair_output_gradient * pair_update_mask.astype(jnp.bfloat16)[:, :, None]
    ).reshape(residue_row_block * pair_cols, pair_width)
    final_matrix_derivative = jnp.dot(hidden.T, masked_grad, preferred_element_type=jnp.float32)
    back_prod = jnp.dot(masked_grad, back_weight.T, preferred_element_type=jnp.float32)
    grad_hidden = (back_prod * act_slope).astype(jnp.bfloat16)
    middle_matrix_derivative = jnp.dot(
        pair_normed.T, grad_hidden, preferred_element_type=jnp.float32
    )
    grad_scaled = (
        jnp.dot(grad_hidden, hidden_weight.T, preferred_element_type=jnp.float32) * pair_norm_gain
    )
    grad_mid = pair_output_gradient.reshape(residue_row_block * pair_cols, pair_width).astype(
        jnp.float32
    ) + standardize_adjoint(grad_scaled, pair_scaled, pair_inv)
    couple_features_derivative = grad_mid.astype(jnp.bfloat16).reshape(
        residue_row_block, pair_cols, pair_width
    )
    grad_opm = (
        (grad_mid / count_column)
        .astype(jnp.bfloat16)
        .reshape(residue_row_block, pair_cols, pair_width)
    )
    full_opm = lax.all_gather(grad_opm, "depth", axis=1, tiled=True).reshape(
        residue_row_block, depth_count, pair_cols, pair_width
    )

    def backward_step(step_index, loop_state):
        grad_left_acc, grad_out, right_term = loop_state
        col_start = step_index * col_block
        outer_part, right_piece = partial_outer(col_start)
        opm_piece = lax.dynamic_slice_in_dim(full_opm, col_start, col_block, 2).reshape(
            residue_row_block * block_depth * col_block, pair_width
        )
        grad_out = grad_out + jnp.dot(
            outer_part.reshape(residue_row_block * block_depth * col_block, outer_width).T,
            opm_piece.astype(jnp.float32),
            precision=highest,
        )
        grad_outer = jnp.dot(opm_piece, output_weight.T, preferred_element_type=jnp.float32).astype(
            jnp.bfloat16
        )
        grad_outer = grad_outer.reshape(
            residue_row_block, block_depth, col_block, proj_width, proj_width
        )
        grad_left_acc = grad_left_acc + jnp.einsum(
            "iejcd,sejd->sic", grad_outer, right_piece, preferred_element_type=jnp.float32
        )
        piece_term = jnp.einsum(
            "iejcd,sic->ejsd", grad_outer, left_proj, preferred_element_type=jnp.float32
        )
        piece_term = piece_term.reshape(block_depth, col_block, seq_total * proj_width)
        right_term = lax.dynamic_update_slice_in_dim(right_term, piece_term, col_start, 1)
        return (grad_left_acc, grad_out, right_term)

    grad_left_acc, result_matrix_derivative, right_term = lax.fori_loop(
        0,
        block_count,
        backward_step,
        (
            jnp.zeros((seq_total, residue_row_block, proj_width), jnp.float32),
            jnp.zeros((outer_width, pair_width), jnp.float32),
            jnp.zeros((block_depth, pair_cols, seq_total * proj_width), jnp.float32),
        ),
    )
    grad_right_sum = lax.psum_scatter(
        right_term.reshape(residues, seq_total * proj_width), "col", scatter_dimension=0, tiled=True
    )
    grad_right_acc = jnp.transpose(
        grad_right_sum.reshape(residue_row_block, seq_total, proj_width), (1, 0, 2)
    )
    grad_left = (grad_left_acc * mask_floating[:, :, None]).astype(jnp.bfloat16)
    grad_right = (grad_right_acc * mask_floating[:, :, None]).astype(jnp.bfloat16)
    normed_rows = normalized_rows.reshape(sequence_row_block * residue_row_block, channel_total)
    first_projector_derivative = jnp.dot(
        normed_rows.T,
        grad_left.reshape(sequence_row_block * residue_row_block, proj_width),
        preferred_element_type=jnp.float32,
    )
    second_projector_derivative = jnp.dot(
        normed_rows.T,
        grad_right.reshape(sequence_row_block * residue_row_block, proj_width),
        preferred_element_type=jnp.float32,
    )
    standardized_derivative = jnp.dot(
        grad_left, first_projector.T, preferred_element_type=jnp.float32
    ) + jnp.dot(grad_right, second_projector.T, preferred_element_type=jnp.float32)
    features_derivative = standardize_adjoint(
        standardized_derivative * layer_scale_factor, standardized_features, reciprocal_spread
    ).astype(jnp.bfloat16)
    weight_sums = lax.psum(
        (
            first_projector_derivative,
            second_projector_derivative,
            result_matrix_derivative,
            middle_matrix_derivative,
            final_matrix_derivative,
        ),
        ("depth", "col"),
    )
    return (
        features_derivative,
        couple_features_derivative,
        weight_sums[0],
        weight_sums[1],
        weight_sums[2],
        weight_sums[3],
        weight_sums[4],
    )


FEW_RESIDUES = 32
MASK_ROWS = 16
Z_PARTNERS = (2, 4, 6)
Y_PARTNER = 1


def butterfly(blocks, group):
    lane_group = lax.broadcasted_iota(jnp.int32, blocks[0].shape, 1) // group
    width = 4 * group
    for bit in (2, 1):
        low = (lane_group & bit) == 0
        swapped = list(blocks)
        for at in range(4):
            if at & bit:
                continue
            here, there = blocks[at], blocks[at | bit]
            moving = jnp.where(low, there, here)
            if bit == 2:
                moved = pltpu.roll(moving, 2 * group, 1)
            else:
                moved = jnp.where(
                    low, pltpu.roll(moving, width - group, 1), pltpu.roll(moving, group, 1)
                )
            swapped[at] = jnp.where(low, here, moved)
            swapped[at | bit] = jnp.where(low, moved, there)
        blocks = swapped
    return blocks


def wide_projector(first_ref, second_ref, copies):
    return jnp.concatenate([first_ref[...]] * copies + [second_ref[...]] * copies, axis=0)


def pre_kernel(
    ids_ref,
    x_hbm,
    maskt_hbm,
    pmask_hbm,
    scale_hbm,
    first_hbm,
    second_hbm,
    gain_hbm,
    act_hbm,
    grad_hbm,
    sent_ref,
    scale_ref,
    first_ref,
    second_ref,
    gain_ref,
    normed_ref,
    scaled_ref,
    inv_ref,
    wide_ref,
    tile_ref,
    x_ref,
    maskt_ref,
    pmask_ref,
    sems,
):
    res, seqs = maskt_ref.shape
    pairs = act_hbm.shape[0]
    first_pair = 2 * seqs + MASK_ROWS
    copies = [
        pltpu.make_async_copy(source, target, sems.at[at])
        for at, (source, target) in enumerate(
            (
                (x_hbm, x_ref),
                (maskt_hbm, maskt_ref),
                (pmask_hbm, pmask_ref),
                (scale_hbm, scale_ref),
                (first_hbm, first_ref),
                (second_hbm, second_ref),
                (gain_hbm, gain_ref),
                (act_hbm, sent_ref.at[0, pl.ds(first_pair, pairs), :]),
                (grad_hbm, sent_ref.at[0, pl.ds(first_pair + pairs, pairs), :]),
            )
        )
    ]
    for copy in copies:
        copy.start()
    for copy in copies:
        copy.wait()
    lanes = sent_ref.shape[2]
    group = lanes // res
    scaled, inv = norm_pieces(
        x_ref[...].astype(jnp.float32).reshape(seqs * res, x_ref.shape[2])
    )
    scaled_ref[...] = scaled
    inv_ref[...] = inv
    normed = (scaled * scale_ref[...]).astype(jnp.bfloat16)
    normed_ref[...] = normed
    wide = lax.dot_general(
        normed,
        wide_projector(first_ref, second_ref, res),
        (((1,), (1,)), ((), ())),
        preferred_element_type=jnp.float32,
    )
    for at in range(2):
        wide_ref[at] = wide[:, at * lanes : (at + 1) * lanes]
    tile_ref[...] = jnp.zeros(tile_ref.shape, jnp.float32)
    mask = maskt_ref[...].astype(jnp.float32)
    tile_ref[0:res, 0:seqs] = mask
    spread = (
        lax.broadcasted_iota(jnp.int32, (MASK_ROWS, lanes), 1) // group
        == lax.broadcasted_iota(jnp.int32, (MASK_ROWS, lanes), 0)
    ).astype(jnp.float32)
    mask_lanes = lax.dot_general(
        tile_ref[...], spread, (((0,), (0,)), ((), ())), preferred_element_type=jnp.float32
    )[:seqs]
    twice = jnp.concatenate([mask] * (lanes // seqs), axis=1)
    here = lax.broadcasted_iota(jnp.int32, (res, lanes), 1) // seqs == ids_ref[0]
    tile_ref[0:res, :] = jnp.where(here, twice, 0.0)
    tile_ref[res : 2 * res, 0 : pmask_ref.shape[1]] = pmask_ref[...].astype(jnp.float32)
    lane_group = lax.broadcasted_iota(jnp.int32, (seqs, lanes), 1) // group
    for at in range(2):
        both = wide_ref[at, pl.ds(0, seqs, stride=res), :]
        for r in range(1, res):
            both = jnp.where(
                lane_group == r, wide_ref[at, pl.ds(r, seqs, stride=res), :], both
            )
        sent_ref[0, at * seqs : (at + 1) * seqs, :] = (both * mask_lanes).astype(jnp.bfloat16)
    sent_ref[0, 2 * seqs : first_pair, :] = tile_ref[...].astype(jnp.bfloat16)


def by_owner(ids_ref, z, near_ref, far_ref):
    step = z ^ (ids_ref[1] // 2)
    near, far = near_ref[step], far_ref[step]
    first = ids_ref[1] % 2 == 0
    return jnp.where(first, near, far), jnp.where(first, far, near)


def outer_kernel(
    sizes,
    ids_ref,
    near_ref,
    far_ref,
    other_near_ref,
    other_far_ref,
    wturn_ref,
    outer_ref,
    proj_out_ref,
    cnt_ref,
    pm_ref,
    maskt_ref,
    rightt_ref,
    leftt_ref,
    leftn_ref,
    mine_ref,
    turnl_ref,
    turnr_ref,
    cntl_ref,
    pml_ref,
):
    seqs, res, pair_cols, width = sizes
    line = near_ref.shape[0]
    cols = 2 * line
    residues = cols * res
    lanes = res * width
    me_depth = ids_ref[0]
    lower = me_depth == 0
    f32, bf16 = jnp.float32, jnp.bfloat16

    for z in range(line):
        mine = by_owner(ids_ref, z, near_ref, far_ref)
        other = by_owner(ids_ref, z, other_near_ref, other_far_ref)
        for y in range(2):
            lanes_k = slice((2 * z + y) * lanes, (2 * z + y + 1) * lanes)
            both = jnp.concatenate(
                [
                    jnp.where(lower, mine[y], other[y]),
                    jnp.where(lower, other[y], mine[y]),
                ],
                axis=0,
            )
            rows = both.shape[0] // 2
            left = jnp.concatenate([both[0:seqs], both[rows : rows + seqs]], axis=0)
            right = jnp.concatenate(
                [both[seqs : 2 * seqs], both[rows + seqs : rows + 2 * seqs]], axis=0
            )
            leftn_ref[:, lanes_k] = left
            turnl_ref[lanes_k, :] = left.astype(f32).T
            turnr_ref[lanes_k, :] = right.astype(f32).T
            tiles = [
                both[first + 2 * seqs : first + 2 * seqs + MASK_ROWS].astype(f32)
                for first in (0, rows)
            ]
            maskt_ref[(2 * z + y) * res : (2 * z + y + 1) * res, :] = (
                tiles[0][0:res] + tiles[1][0:res]
            )
            own = mine[y][2 * seqs : 2 * seqs + MASK_ROWS].astype(f32)
            pair_lane = lax.broadcasted_iota(jnp.int32, (pair_cols, lanes), 1)
            pair_row = lax.broadcasted_iota(jnp.int32, (pair_cols, lanes), 0)
            for r in range(res):
                first = ((2 * z + y) * res + r) * pair_cols
                pml_ref[first : first + pair_cols, :] = jnp.where(
                    pair_lane == pair_row, own[res + r : res + r + 1, :], 0.0
                ).astype(bf16)
    for d in range(width):
        mine_ref[d * pair_cols : (d + 1) * pair_cols, :] = turnr_ref[
            pl.ds(me_depth * pair_cols * width + d, pair_cols, stride=width), :
        ].astype(bf16)
    for turned, out in ((turnl_ref, leftt_ref), (turnr_ref, rightt_ref)):
        for d in range(width):
            out[d * residues : (d + 1) * residues, :] = turned[
                pl.ds(d, residues, stride=width), :
            ].astype(bf16)

    maskt = maskt_ref[...]
    cols_mask = maskt_ref[pl.ds(pl.multiple_of(me_depth * pair_cols, pair_cols), pair_cols), :]
    for i in range(residues):
        cntl_ref[i * pair_cols : (i + 1) * pair_cols, :] = (maskt[i : i + 1, :] * cols_mask).astype(
            bf16
        )
    ones = jnp.ones((lanes, lanes), bf16)
    cnt_ref[...] = jnp.dot(cntl_ref[...], ones, preferred_element_type=f32)
    pm_ref[...] = jnp.dot(pml_ref[...], ones, preferred_element_type=f32).astype(bf16)

    for dh in range(width // 4):
        prod = jnp.dot(
            mine_ref[dh * 4 * pair_cols : (dh + 1) * 4 * pair_cols, :],
            leftn_ref[...],
            preferred_element_type=f32,
        )
        for k in range(cols):
            piece = prod[:, k * lanes : (k + 1) * lanes]
            turned = butterfly(
                [piece[a * pair_cols : (a + 1) * pair_cols] for a in range(4)], width
            )
            for il in range(res):
                first = (k * res + il) * pair_cols
                outer_ref[first : first + pair_cols, dh * lanes : (dh + 1) * lanes] = turned[
                    il
                ].astype(bf16)
    proj_out_ref[...] = jnp.dot(outer_ref[...], wturn_ref[...], preferred_element_type=f32)


def transition_kernel(
    sizes,
    ids_ref,
    near_ref,
    far_ref,
    proj_out_ref,
    cnt_ref,
    pm_ref,
    gain_ref,
    hid_ref,
    back_ref,
    couple_ref,
    opm_ref,
    pn_ref,
    gh_ref,
    hidden_ref,
    mg_ref,
    gmid_ref,
):
    seqs, res, pair_cols, width = sizes
    per = res * pair_cols
    cols = 2 * near_ref.shape[0]
    me_col = ids_ref[1]
    f32, bf16 = jnp.float32, jnp.bfloat16
    gain = gain_ref[...]
    chunk = 2 * per
    for at in range(cols // 2):
        rows = slice(at * chunk, (at + 1) * chunk)
        blocks = by_owner(ids_ref, at, near_ref, far_ref)
        act, grad = [
            jnp.concatenate([block[w * per : (w + 1) * per] for block in blocks], axis=0)
            for w in range(2)
        ]
        count = cnt_ref[rows, :]
        mid = act.astype(f32) + proj_out_ref[rows, :] / count
        scaled, inv = norm_pieces(mid)
        normed = (scaled * gain).astype(bf16)
        pn_ref[rows, :] = normed
        pre = jnp.dot(normed, hid_ref[...], preferred_element_type=f32)
        value, slope = silu_pieces(pre)
        hidden_ref[rows, :] = value.astype(bf16)
        masked = grad * pm_ref[rows, :]
        mg_ref[rows, :] = masked
        back = lax.dot_general(
            masked, back_ref[...], (((1,), (1,)), ((), ())), preferred_element_type=f32
        )
        ghid = (back * slope).astype(bf16)
        gh_ref[rows, :] = ghid
        gsc = (
            lax.dot_general(
                ghid, hid_ref[...], (((1,), (1,)), ((), ())), preferred_element_type=f32
            )
            * gain
        )
        gmid = grad.astype(f32) + standardize_adjoint(gsc, scaled, inv)
        gmid_ref[rows, :] = gmid
        opm_ref[rows, :] = (gmid / count).astype(bf16)
    couple_ref[...] = gmid_ref[pl.ds(pl.multiple_of(me_col * per, per), per), :].astype(bf16)


def projector_kernel(
    sizes,
    ids_ref,
    opm_ref,
    other_opm_ref,
    rightt_ref,
    leftt_ref,
    wout_ref,
    wturn_ref,
    maskt_ref,
    normed_ref,
    far_normed_ref,
    other_normed_ref,
    other_far_normed_ref,
    part_ref,
    spread_ref,
    gf_ref,
    grow_ref,
    gcol_ref,
    gor_ref,
    goc_ref,
    gs_ref,
    rows_ref,
):
    seqs, res, pair_cols, width = sizes
    depths, half = rows_ref.shape[1], gf_ref.shape[0]
    residues = half // pair_cols
    lanes = res * width
    here = 2 * res
    me_depth = ids_ref[0]
    me_col = ids_ref[1]
    me_y = me_col % 2
    first_here = (me_col // 2) * here
    f32, bf16 = jnp.float32, jnp.bfloat16
    my_half = first_here // pair_cols
    gf_ref[...] = jnp.where(my_half == me_depth, opm_ref[...], other_opm_ref[...]).astype(f32)
    for y, e, block in (
        (me_y, me_depth, normed_ref),
        (1 - me_y, me_depth, far_normed_ref),
        (me_y, 1 - me_depth, other_normed_ref),
        (1 - me_y, 1 - me_depth, other_far_normed_ref),
    ):
        rows_ref[y, e] = block[...]

    for il in range(here):
        first = pl.multiple_of((first_here + il) * pair_cols, pair_cols)
        for e, block in ((me_depth, opm_ref), (1 - me_depth, other_opm_ref)):
            to = pl.multiple_of(il * residues + e * pair_cols, pair_cols)
            grow_ref[pl.ds(to, pair_cols), :] = block[pl.ds(first, pair_cols), :]
    my_first = first_here - my_half * pair_cols
    for jl in range(here):
        gcol_ref[jl * residues : (jl + 1) * residues, :] = gf_ref[
            pl.ds(my_first + jl, residues, stride=pair_cols), :
        ].astype(bf16)
    for lhs, weight, out in ((grow_ref, wturn_ref, gor_ref), (gcol_ref, wout_ref, goc_ref)):
        for dh in range(width // 4):
            piece = lax.dot_general(
                lhs[...],
                weight[dh * lanes : (dh + 1) * lanes, :],
                (((1,), (1,)), ((), ())),
                preferred_element_type=f32,
            )
            for y in range(2):
                turned = butterfly(
                    [
                        piece[(y * res + a) * residues : (y * res + a + 1) * residues]
                        for a in range(4)
                    ],
                    width,
                )
                for dl in range(4):
                    first = (dh * 4 + dl) * residues
                    out[first : first + residues, y * lanes : (y + 1) * lanes] = turned[dl].astype(
                        bf16
                    )
    group = lax.broadcasted_iota(jnp.int32, (here, here * width), 1) // width
    spread = (group == lax.broadcasted_iota(jnp.int32, (here, here * width), 0)).astype(f32)
    mask_lanes = lax.dot_general(
        maskt_ref[pl.ds(pl.multiple_of(first_here, here), here), :],
        spread,
        (((0,), (0,)), ((), ())),
        preferred_element_type=f32,
    )
    lane_group = lax.broadcasted_iota(jnp.int32, (seqs, lanes), 1) // width
    for at, (lhs, rhs) in enumerate(((rightt_ref, gor_ref), (leftt_ref, goc_ref))):
        total = lax.dot_general(
            lhs[...], rhs[...], (((0,), (0,)), ((), ())), preferred_element_type=f32
        )
        total = (total * mask_lanes).astype(bf16).astype(f32)
        for y in range(2):
            for e in range(depths):
                block = total[e * seqs : (e + 1) * seqs, y * lanes : (y + 1) * lanes]
                for r in range(res):
                    gs_ref[at, y, e, pl.ds(r, seqs, stride=res), :] = jnp.where(
                        lane_group == r, block, 0.0
                    )
    spread_ref[...] = jnp.concatenate(
        [gs_ref[0, me_y, me_depth], gs_ref[1, me_y, me_depth]], axis=1
    ).astype(bf16)
    rows = rows_ref.shape[2]
    for at in range(2):
        cross = lax.dot_general(
            gs_ref[at].reshape(2 * depths * rows, lanes).astype(bf16),
            rows_ref[...].reshape(2 * depths * rows, rows_ref.shape[3]),
            (((0,), (0,)), ((), ())),
            preferred_element_type=f32,
        )
        total = cross[:width]
        for r in range(1, res):
            total = total + cross[r * width : (r + 1) * width]
        part_ref[at * width : (at + 1) * width, :] = total.astype(bf16)


def weights_kernel(outer_ref, opm_ref, pn_ref, gh_ref, hidden_ref, mg_ref, out_ref, turn_ref):
    pair_width, hid = pn_ref.shape[1], gh_ref.shape[1]
    outer_width = outer_ref.shape[1]
    width = int(outer_width**0.5 + 0.5)

    def contract(lhs, rhs):
        return lax.dot_general(
            lhs[...], rhs[...], (((0,), (0,)), ((), ())), preferred_element_type=jnp.float32
        )

    turn_ref[...] = contract(outer_ref, opm_ref)
    for c in range(width):
        out_ref[c * width : (c + 1) * width, :] = turn_ref[
            pl.ds(c, width, stride=width), :
        ].astype(jnp.bfloat16)
    dhid = contract(pn_ref, gh_ref).astype(jnp.bfloat16)
    for at in range(hid // pair_width):
        first = outer_width + at * pair_width
        out_ref[first : first + pair_width, :] = dhid[:, at * pair_width : (at + 1) * pair_width]
    out_ref[outer_width + hid :, :] = contract(hidden_ref, mg_ref).astype(jnp.bfloat16)


def weights_sum_kernel(mine_ref, other_ref, dout_ref, dhid_ref, dback_ref):
    pair_width, hid = dhid_ref.shape
    outer_width = dout_ref.shape[0]

    def added(first, count):
        rows = slice(first, first + count)
        return mine_ref[rows, :].astype(jnp.float32) + other_ref[rows, :].astype(jnp.float32)

    dout_ref[...] = added(0, outer_width)
    for at in range(hid // pair_width):
        dhid_ref[:, at * pair_width : (at + 1) * pair_width] = added(
            outer_width + at * pair_width, pair_width
        )
    dback_ref[...] = added(outer_width + hid, hid)


def feature_kernel(
    copies,
    spread_ref,
    first_ref,
    second_ref,
    scale_ref,
    scaled_ref,
    inv_ref,
    held_ref,
    feat_ref,
    couple_ref,
):
    back = jnp.dot(
        spread_ref[...],
        wide_projector(first_ref, second_ref, copies),
        preferred_element_type=jnp.float32,
    )
    feat = standardize_adjoint(back * scale_ref[...], scaled_ref[...], inv_ref[...])
    feat_ref[...] = feat.reshape(feat_ref.shape).astype(jnp.bfloat16)
    couple_ref[...] = held_ref[...]


def swap_depth(block):
    return lax.ppermute(block, "depth", [(0, 1), (1, 0)])


def pairwise_sum(blocks):
    while len(blocks) > 1:
        blocks = [blocks[at] + blocks[at + 1] for at in range(0, len(blocks), 2)]
    return blocks[0]


def swap_col(block, partner):
    count = lax.axis_size("col")
    return lax.ppermute(block, "col", [(at, at ^ partner) for at in range(count)])


def whole_plan(
    alignment_activations,
    alignment_mask,
    pair_activation_input,
    pair_update_mask,
    pair_output_gradient,
    layer_scale_factor,
    first_projector,
    second_projector,
    output_weight,
    pair_norm_gain,
    hidden_weight,
    back_weight,
):
    seqs, res, channels = alignment_activations.shape
    width = first_projector.shape[1]
    outer_width = width * width
    cols = lax.axis_size("col")
    depths = lax.axis_size("depth")
    residues = res * cols
    pair_cols, pair_width = pair_activation_input.shape[1:]
    hid = hidden_weight.shape[1]
    per = res * pair_cols
    lanes = res * width
    rows = 2 * seqs + MASK_ROWS
    half = residues * pair_cols
    f32, bf16 = jnp.float32, jnp.bfloat16
    ids = jnp.stack([lax.axis_index("depth"), lax.axis_index("col")]).astype(jnp.int32)
    smem = pl.BlockSpec(memory_space=pltpu.SMEM)
    vmem = pl.BlockSpec(memory_space=pltpu.VMEM)
    params = pltpu.CompilerParams(vmem_limit_bytes=16 * 2**20)
    scale = layer_scale_factor.reshape(1, channels)
    first, second = first_projector.T, second_projector.T
    wturn = jnp.transpose(output_weight.reshape(width, width, pair_width), (1, 0, 2)).reshape(
        outer_width, pair_width
    )
    shape = jax.ShapeDtypeStruct
    sent, scale, first, second, gain, normed, scaled, inv = pl.pallas_call(
        pre_kernel,
        out_shape=(
            shape((1, rows + 2 * per, pair_width), bf16),
            shape((1, channels), f32),
            shape((width, channels), bf16),
            shape((width, channels), bf16),
            shape((1, pair_width), f32),
            shape((seqs * res, channels), bf16),
            shape((seqs * res, channels), f32),
            shape((seqs * res, 1), f32),
        ),
        in_specs=[smem] + [pl.BlockSpec(memory_space=pltpu.HBM)] * 9,
        out_specs=[vmem] * 8,
        scratch_shapes=[
            pltpu.VMEM((2, seqs * res, lanes), f32),
            pltpu.VMEM((MASK_ROWS, lanes), f32),
            pltpu.VMEM((seqs, res, channels), bf16),
            pltpu.VMEM((res, seqs), jnp.int32),
            pltpu.VMEM((res, pair_cols), jnp.int32),
            pltpu.SemaphoreType.DMA((9,)),
        ],
        compiler_params=params,
        name="project",
    )(
        ids,
        *[
            pltpu.with_memory_space_constraint(array, pltpu.HBM)
            for array in (
                alignment_activations,
                alignment_mask.T,
                pair_update_mask,
                scale,
                first,
                second,
                pair_norm_gain.reshape(1, pair_width),
                pair_activation_input.reshape(per, pair_width),
                pair_output_gradient.reshape(per, pair_width),
            )
        ],
    )
    blocks = lax.optimization_barrier(
        jnp.concatenate([sent] + [swap_col(sent, partner) for partner in Z_PARTNERS])
    )
    far_normed = swap_col(normed, Y_PARTNER)
    blocks, far_normed = lax.optimization_barrier((blocks, far_normed))
    near, pair_near = blocks[:, :rows], blocks[:, rows:]
    far = swap_col(near, Y_PARTNER)
    pair_far = swap_col(pair_near, Y_PARTNER)
    other_near, other_far = swap_depth(near), swap_depth(far)
    sizes = (seqs, res, pair_cols, width)
    outer, proj_out, cnt, pm, maskt, rightt, leftt = pl.pallas_call(
        functools.partial(outer_kernel, sizes),
        out_shape=(
            shape((half, outer_width), bf16),
            shape((half, pair_width), f32),
            shape((half, lanes), f32),
            shape((half, lanes), bf16),
            shape((residues, depths * seqs), f32),
            shape((residues * width, depths * seqs), bf16),
            shape((residues * width, depths * seqs), bf16),
        ),
        in_specs=[smem] + [vmem] * 5,
        out_specs=[vmem] * 7,
        scratch_shapes=[
            pltpu.VMEM((depths * seqs, residues * width), bf16),
            pltpu.VMEM((pair_cols * width, depths * seqs), bf16),
            pltpu.VMEM((residues * width, depths * seqs), f32),
            pltpu.VMEM((residues * width, depths * seqs), f32),
            pltpu.VMEM((half, lanes), bf16),
            pltpu.VMEM((half, lanes), bf16),
        ],
        compiler_params=params,
        name="outer_products",
    )(ids, near, far, other_near, other_far, wturn)
    normed_again, far_again, proj_out = lax.optimization_barrier((normed, far_normed, proj_out))
    other_normed, other_far_normed = swap_depth(normed_again), swap_depth(far_again)
    pair_far, proj_out, other_normed, other_far_normed = lax.optimization_barrier(
        (pair_far, proj_out, other_normed, other_far_normed)
    )
    held, opm, pn, gh, hidden, mg = pl.pallas_call(
        functools.partial(transition_kernel, sizes),
        out_shape=(
            shape((per, pair_width), bf16),
            shape((half, pair_width), bf16),
            shape((half, pair_width), bf16),
            shape((half, hid), bf16),
            shape((half, hid), bf16),
            shape((half, pair_width), bf16),
        ),
        in_specs=[smem] + [vmem] * 8,
        out_specs=[vmem] * 6,
        scratch_shapes=[
            pltpu.VMEM((half, pair_width), f32),
        ],
        compiler_params=params,
        name="transition",
    )(
        ids,
        pair_near,
        pair_far,
        proj_out,
        cnt,
        pm,
        gain,
        hidden_weight,
        back_weight,
    )
    weights = pl.pallas_call(
        weights_kernel,
        out_shape=shape((outer_width + 2 * hid, pair_width), bf16),
        in_specs=[vmem] * 6,
        out_specs=vmem,
        scratch_shapes=[pltpu.VMEM((outer_width, pair_width), f32)],
        compiler_params=params,
        name="weight_gradients",
    )(outer, opm, pn, gh, hidden, mg)
    other_opm, weights = lax.optimization_barrier((swap_depth(opm), weights))
    part, spread = pl.pallas_call(
        functools.partial(projector_kernel, sizes),
        out_shape=(
            shape((2 * width, channels), bf16),
            shape((seqs * res, 2 * lanes), bf16),
        ),
        in_specs=[smem] + [vmem] * 11,
        out_specs=[vmem] * 2,
        scratch_shapes=[
            pltpu.VMEM((half, pair_width), f32),
            pltpu.VMEM((2 * res * residues, pair_width), bf16),
            pltpu.VMEM((2 * res * residues, pair_width), bf16),
            pltpu.VMEM((residues * width, 2 * lanes), bf16),
            pltpu.VMEM((residues * width, 2 * lanes), bf16),
            pltpu.VMEM((2, 2, depths, seqs * res, lanes), f32),
            pltpu.VMEM((2, depths, seqs * res, channels), bf16),
        ],
        compiler_params=params,
        name="projector_parts",
    )(
        ids,
        opm,
        other_opm,
        rightt,
        leftt,
        output_weight,
        wturn,
        maskt,
        normed,
        far_normed,
        other_normed,
        other_far_normed,
    )
    feat, couple = pl.pallas_call(
        functools.partial(feature_kernel, res),
        out_shape=(shape((seqs, res, channels), bf16), shape((per, pair_width), bf16)),
        in_specs=[vmem] * 7,
        out_specs=[vmem] * 2,
        compiler_params=params,
        name="features",
    )(spread, first, second, scale, scaled, inv, held)
    part, weights = lax.optimization_barrier((part, weights))
    dout, dhid, dback = pl.pallas_call(
        weights_sum_kernel,
        out_shape=(
            shape((outer_width, pair_width), f32),
            shape((pair_width, hid), f32),
            shape((hid, pair_width), f32),
        ),
        in_specs=[vmem] * 2,
        out_specs=[vmem] * 3,
        compiler_params=params,
        name="sums_over_depth",
    )(weights, swap_depth(weights))
    came = swap_col(part, Z_PARTNERS[1])
    came, feat, couple = lax.optimization_barrier((came, feat, couple))
    kept = lax.optimization_barrier((part.astype(f32) + came.astype(f32)).astype(bf16))
    came = swap_col(kept, Z_PARTNERS[0])
    came, dout, dhid, dback = lax.optimization_barrier((came, dout, dhid, dback))
    total = kept.astype(f32) + came.astype(f32)
    return (
        feat,
        couple.reshape(res, pair_cols, pair_width),
        total[:width].T,
        total[width:].T,
        dout,
        dhid,
        dback,
    )


def on_device(alignment_activations, *others):
    cols = lax.axis_size("col")
    residues = alignment_activations.shape[1] * cols
    plan = whole_plan if cols == 8 and residues <= FEW_RESIDUES else split_plan
    return plan(alignment_activations, *others)


def solution(mesh):
    in_specs = (
        P(("group", "depth"), "col", None),
        P(("group", "depth"), "col"),
        P(("group", "col"), "depth", None),
        P(("group", "col"), "depth"),
        P(("group", "col"), "depth", None),
        P(),
        P(),
        P(),
        P(),
        P(),
        P(),
        P(),
    )
    out_specs = (
        P(("group", "depth"), "col", None),
        P(("group", "col"), "depth", None),
        P("group", None),
        P("group", None),
        P("group", None),
        P("group", None),
        P("group", None),
    )
    return jax.shard_map(
        on_device, mesh=mesh, in_specs=in_specs, out_specs=out_specs, check_vma=False
    )
```

```python
import functools

import jax
import jax.numpy as jnp
from jax import lax
from jax.experimental import pallas as pl
from jax.experimental.pallas import tpu as pltpu
from jax.sharding import PartitionSpec as P

epsilon = 1e-05
highest = lax.Precision.HIGHEST


def norm_pieces(entries_drawn):
    center = entries_drawn - jnp.mean(entries_drawn, axis=-1, keepdims=True)
    inv_std = lax.rsqrt(jnp.mean(center * center, axis=-1, keepdims=True) + epsilon)
    return (center * inv_std, inv_std)


def standardize_adjoint(grad_scaled, scaled, inv_std):
    mean_grad = jnp.mean(grad_scaled, axis=-1, keepdims=True)
    mean_cross = jnp.mean(grad_scaled * scaled, axis=-1, keepdims=True)
    return inv_std * (grad_scaled - mean_grad - scaled * mean_cross)


def silu_pieces(pre_act):
    sigma = jax.nn.sigmoid(pre_act)
    return (pre_act * sigma, sigma * (1.0 + pre_act * (1.0 - sigma)))


def split_plan(
    alignment_activations,
    alignment_mask,
    pair_activation_input,
    pair_update_mask,
    pair_output_gradient,
    layer_scale_factor,
    first_projector,
    second_projector,
    output_weight,
    pair_norm_gain,
    hidden_weight,
    back_weight,
):
    sequence_row_block, residue_row_block, channel_total = alignment_activations.shape
    proj_width = first_projector.shape[1]
    outer_width = proj_width * proj_width
    depth_count = lax.axis_size("depth")
    residues = residue_row_block * lax.axis_size("col")
    pair_cols = pair_activation_input.shape[1]
    pair_width = pair_activation_input.shape[2]
    col_block = min(64, pair_cols)
    block_count = pair_cols // col_block
    standardized_features, reciprocal_spread = norm_pieces(
        alignment_activations.astype(jnp.float32)
    )
    normalized_rows = (standardized_features * layer_scale_factor).astype(jnp.bfloat16)
    mask_floating = alignment_mask.astype(jnp.float32)
    left_proj = (
        jnp.dot(normalized_rows, first_projector, preferred_element_type=jnp.float32)
        * mask_floating[:, :, None]
    ).astype(jnp.bfloat16)
    right_proj = (
        jnp.dot(normalized_rows, second_projector, preferred_element_type=jnp.float32)
        * mask_floating[:, :, None]
    ).astype(jnp.bfloat16)
    right_flat = right_proj.reshape(sequence_row_block, residue_row_block * proj_width)
    mask_converted = alignment_mask.astype(jnp.bfloat16)
    seq_total = left_proj.shape[0]
    gathered, gathered_mask = (
        lax.all_gather(right_flat, "col", axis=1, tiled=True),
        lax.all_gather(mask_converted, "col", axis=1, tiled=True),
    )
    right_blocks = gathered.reshape(seq_total, depth_count, pair_cols, proj_width)
    mask_blocks = gathered_mask.reshape(seq_total, depth_count, pair_cols)
    block_depth = right_blocks.shape[1]
    out_wide = output_weight.astype(jnp.float32)

    def partial_outer(col_start):
        right_piece = lax.dynamic_slice_in_dim(right_blocks, col_start, col_block, 2)
        outer_part = jnp.einsum(
            "sic,sejd->iejcd", left_proj, right_piece, preferred_element_type=jnp.float32
        )
        return (
            outer_part.reshape(residue_row_block, block_depth, col_block, outer_width),
            right_piece,
        )

    def forward_step(step_index, loop_state):
        projected, pair_count = loop_state
        col_start = step_index * col_block
        outer_part, right_piece = partial_outer(col_start)
        mask_piece = lax.dynamic_slice_in_dim(mask_blocks, col_start, col_block, 2).astype(
            jnp.float32
        )
        count_part = jnp.einsum("si,sej->iej", mask_floating, mask_piece, precision=highest)
        outer_mine, count_mine = (
            lax.psum_scatter(
                outer_part.astype(jnp.bfloat16), "depth", scatter_dimension=1, tiled=True
            ).astype(jnp.float32),
            lax.psum_scatter(
                count_part.astype(jnp.bfloat16), "depth", scatter_dimension=1, tiled=True
            ).astype(jnp.float32),
        )
        proj_mine = jnp.dot(
            outer_mine.reshape(residue_row_block * col_block, outer_width),
            out_wide,
            precision=highest,
        )
        proj_mine = proj_mine.reshape(residue_row_block, col_block, pair_width)
        count_mine = count_mine.reshape(residue_row_block, col_block)
        projected = lax.dynamic_update_slice_in_dim(projected, proj_mine, col_start, 1)
        pair_count = lax.dynamic_update_slice_in_dim(pair_count, count_mine, col_start, 1)
        return (projected, pair_count)

    projected, pair_count = lax.fori_loop(
        0,
        block_count,
        forward_step,
        (
            jnp.zeros((residue_row_block, pair_cols, pair_width), jnp.float32),
            jnp.zeros((residue_row_block, pair_cols), jnp.float32),
        ),
    )
    count_column = pair_count.reshape(residue_row_block * pair_cols, 1)
    mid_act = (
        pair_activation_input.reshape(residue_row_block * pair_cols, pair_width).astype(jnp.float32)
        + projected.reshape(residue_row_block * pair_cols, pair_width) / count_column
    )
    pair_scaled, pair_inv = norm_pieces(mid_act)
    pair_normed = (pair_scaled * pair_norm_gain).astype(jnp.bfloat16)
    pre_act = jnp.dot(pair_normed, hidden_weight, preferred_element_type=jnp.float32)
    act_value, act_slope = silu_pieces(pre_act)
    hidden = act_value.astype(jnp.bfloat16)
    masked_grad = (
        pair_output_gradient * pair_update_mask.astype(jnp.bfloat16)[:, :, None]
    ).reshape(residue_row_block * pair_cols, pair_width)
    final_matrix_derivative = jnp.dot(hidden.T, masked_grad, preferred_element_type=jnp.float32)
    back_prod = jnp.dot(masked_grad, back_weight.T, preferred_element_type=jnp.float32)
    grad_hidden = (back_prod * act_slope).astype(jnp.bfloat16)
    middle_matrix_derivative = jnp.dot(
        pair_normed.T, grad_hidden, preferred_element_type=jnp.float32
    )
    grad_scaled = (
        jnp.dot(grad_hidden, hidden_weight.T, preferred_element_type=jnp.float32) * pair_norm_gain
    )
    grad_mid = pair_output_gradient.reshape(residue_row_block * pair_cols, pair_width).astype(
        jnp.float32
    ) + standardize_adjoint(grad_scaled, pair_scaled, pair_inv)
    couple_features_derivative = grad_mid.astype(jnp.bfloat16).reshape(
        residue_row_block, pair_cols, pair_width
    )
    grad_opm = (
        (grad_mid / count_column)
        .astype(jnp.bfloat16)
        .reshape(residue_row_block, pair_cols, pair_width)
    )
    full_opm = lax.all_gather(grad_opm, "depth", axis=1, tiled=True).reshape(
        residue_row_block, depth_count, pair_cols, pair_width
    )

    def backward_step(step_index, loop_state):
        grad_left_acc, grad_out, right_term = loop_state
        col_start = step_index * col_block
        outer_part, right_piece = partial_outer(col_start)
        opm_piece = lax.dynamic_slice_in_dim(full_opm, col_start, col_block, 2).reshape(
            residue_row_block * block_depth * col_block, pair_width
        )
        grad_out = grad_out + jnp.dot(
            outer_part.reshape(residue_row_block * block_depth * col_block, outer_width).T,
            opm_piece.astype(jnp.float32),
            precision=highest,
        )
        grad_outer = jnp.dot(opm_piece, output_weight.T, preferred_element_type=jnp.float32).astype(
            jnp.bfloat16
        )
        grad_outer = grad_outer.reshape(
            residue_row_block, block_depth, col_block, proj_width, proj_width
        )
        grad_left_acc = grad_left_acc + jnp.einsum(
            "iejcd,sejd->sic", grad_outer, right_piece, preferred_element_type=jnp.float32
        )
        piece_term = jnp.einsum(
            "iejcd,sic->ejsd", grad_outer, left_proj, preferred_element_type=jnp.float32
        )
        piece_term = piece_term.reshape(block_depth, col_block, seq_total * proj_width)
        right_term = lax.dynamic_update_slice_in_dim(right_term, piece_term, col_start, 1)
        return (grad_left_acc, grad_out, right_term)

    grad_left_acc, result_matrix_derivative, right_term = lax.fori_loop(
        0,
        block_count,
        backward_step,
        (
            jnp.zeros((seq_total, residue_row_block, proj_width), jnp.float32),
            jnp.zeros((outer_width, pair_width), jnp.float32),
            jnp.zeros((block_depth, pair_cols, seq_total * proj_width), jnp.float32),
        ),
    )
    grad_right_sum = lax.psum_scatter(
        right_term.reshape(residues, seq_total * proj_width), "col", scatter_dimension=0, tiled=True
    )
    grad_right_acc = jnp.transpose(
        grad_right_sum.reshape(residue_row_block, seq_total, proj_width), (1, 0, 2)
    )
    grad_left = (grad_left_acc * mask_floating[:, :, None]).astype(jnp.bfloat16)
    grad_right = (grad_right_acc * mask_floating[:, :, None]).astype(jnp.bfloat16)
    normed_rows = normalized_rows.reshape(sequence_row_block * residue_row_block, channel_total)
    first_projector_derivative = jnp.dot(
        normed_rows.T,
        grad_left.reshape(sequence_row_block * residue_row_block, proj_width),
        preferred_element_type=jnp.float32,
    )
    second_projector_derivative = jnp.dot(
        normed_rows.T,
        grad_right.reshape(sequence_row_block * residue_row_block, proj_width),
        preferred_element_type=jnp.float32,
    )
    standardized_derivative = jnp.dot(
        grad_left, first_projector.T, preferred_element_type=jnp.float32
    ) + jnp.dot(grad_right, second_projector.T, preferred_element_type=jnp.float32)
    features_derivative = standardize_adjoint(
        standardized_derivative * layer_scale_factor, standardized_features, reciprocal_spread
    ).astype(jnp.bfloat16)
    weight_sums = lax.psum(
        (
            first_projector_derivative,
            second_projector_derivative,
            result_matrix_derivative,
            middle_matrix_derivative,
            final_matrix_derivative,
        ),
        ("depth", "col"),
    )
    return (
        features_derivative,
        couple_features_derivative,
        weight_sums[0],
        weight_sums[1],
        weight_sums[2],
        weight_sums[3],
        weight_sums[4],
    )


FEW_RESIDUES = 32
MASK_ROWS = 16
Z_PARTNERS = (2, 4, 6)
Y_PARTNER = 1


def butterfly(blocks, group):
    lane_group = lax.broadcasted_iota(jnp.int32, blocks[0].shape, 1) // group
    width = 4 * group
    for bit in (2, 1):
        low = (lane_group & bit) == 0
        swapped = list(blocks)
        for at in range(4):
            if at & bit:
                continue
            here, there = blocks[at], blocks[at | bit]
            moving = jnp.where(low, there, here)
            if bit == 2:
                moved = pltpu.roll(moving, 2 * group, 1)
            else:
                moved = jnp.where(
                    low, pltpu.roll(moving, width - group, 1), pltpu.roll(moving, group, 1)
                )
            swapped[at] = jnp.where(low, here, moved)
            swapped[at | bit] = jnp.where(low, moved, there)
        blocks = swapped
    return blocks


def wide_projector(first_ref, second_ref, copies):
    return jnp.concatenate([first_ref[...]] * copies + [second_ref[...]] * copies, axis=0)


def pre_kernel(
    ids_ref,
    x_hbm,
    maskt_hbm,
    pmask_hbm,
    scale_hbm,
    first_hbm,
    second_hbm,
    gain_hbm,
    act_hbm,
    grad_hbm,
    sent_ref,
    scale_ref,
    first_ref,
    second_ref,
    gain_ref,
    normed_ref,
    scaled_ref,
    inv_ref,
    wide_ref,
    tile_ref,
    x_ref,
    maskt_ref,
    pmask_ref,
    sems,
):
    res, seqs = maskt_ref.shape
    pairs = act_hbm.shape[0]
    first_pair = 2 * seqs + MASK_ROWS
    copies = [
        pltpu.make_async_copy(source, target, sems.at[at])
        for at, (source, target) in enumerate(
            (
                (x_hbm, x_ref),
                (maskt_hbm, maskt_ref),
                (pmask_hbm, pmask_ref),
                (scale_hbm, scale_ref),
                (first_hbm, first_ref),
                (second_hbm, second_ref),
                (gain_hbm, gain_ref),
                (act_hbm, sent_ref.at[0, pl.ds(first_pair, pairs), :]),
                (grad_hbm, sent_ref.at[0, pl.ds(first_pair + pairs, pairs), :]),
            )
        )
    ]
    for copy in copies:
        copy.start()
    for copy in copies:
        copy.wait()
    lanes = sent_ref.shape[2]
    group = lanes // res
    scaled, inv = norm_pieces(
        x_ref[...].astype(jnp.float32).reshape(seqs * res, x_ref.shape[2])
    )
    scaled_ref[...] = scaled
    inv_ref[...] = inv
    normed = (scaled * scale_ref[...]).astype(jnp.bfloat16)
    normed_ref[...] = normed
    wide = lax.dot_general(
        normed,
        wide_projector(first_ref, second_ref, res),
        (((1,), (1,)), ((), ())),
        preferred_element_type=jnp.float32,
    )
    for at in range(2):
        wide_ref[at] = wide[:, at * lanes : (at + 1) * lanes]
    tile_ref[...] = jnp.zeros(tile_ref.shape, jnp.float32)
    mask = maskt_ref[...].astype(jnp.float32)
    tile_ref[0:res, 0:seqs] = mask
    spread = (
        lax.broadcasted_iota(jnp.int32, (MASK_ROWS, lanes), 1) // group
        == lax.broadcasted_iota(jnp.int32, (MASK_ROWS, lanes), 0)
    ).astype(jnp.float32)
    mask_lanes = lax.dot_general(
        tile_ref[...], spread, (((0,), (0,)), ((), ())), preferred_element_type=jnp.float32
    )[:seqs]
    twice = jnp.concatenate([mask] * (lanes // seqs), axis=1)
    here = lax.broadcasted_iota(jnp.int32, (res, lanes), 1) // seqs == ids_ref[0]
    tile_ref[0:res, :] = jnp.where(here, twice, 0.0)
    tile_ref[res : 2 * res, 0 : pmask_ref.shape[1]] = pmask_ref[...].astype(jnp.float32)
    lane_group = lax.broadcasted_iota(jnp.int32, (seqs, lanes), 1) // group
    for at in range(2):
        both = wide_ref[at, pl.ds(0, seqs, stride=res), :]
        for r in range(1, res):
            both = jnp.where(
                lane_group == r, wide_ref[at, pl.ds(r, seqs, stride=res), :], both
            )
        sent_ref[0, at * seqs : (at + 1) * seqs, :] = (both * mask_lanes).astype(jnp.bfloat16)
    sent_ref[0, 2 * seqs : first_pair, :] = tile_ref[...].astype(jnp.bfloat16)


def by_owner(ids_ref, z, near_ref, far_ref):
    step = z ^ (ids_ref[1] // 2)
    near, far = near_ref[step], far_ref[step]
    first = ids_ref[1] % 2 == 0
    return jnp.where(first, near, far), jnp.where(first, far, near)


def outer_kernel(
    sizes,
    ids_ref,
    near_ref,
    far_ref,
    other_near_ref,
    other_far_ref,
    wturn_ref,
    outer_ref,
    proj_out_ref,
    cnt_ref,
    pm_ref,
    maskt_ref,
    rightt_ref,
    leftt_ref,
    leftn_ref,
    mine_ref,
    turnl_ref,
    turnr_ref,
    cntl_ref,
    pml_ref,
):
    seqs, res, pair_cols, width = sizes
    line = near_ref.shape[0]
    cols = 2 * line
    residues = cols * res
    lanes = res * width
    me_depth = ids_ref[0]
    lower = me_depth == 0
    f32, bf16 = jnp.float32, jnp.bfloat16

    for z in range(line):
        mine = by_owner(ids_ref, z, near_ref, far_ref)
        other = by_owner(ids_ref, z, other_near_ref, other_far_ref)
        for y in range(2):
            lanes_k = slice((2 * z + y) * lanes, (2 * z + y + 1) * lanes)
            both = jnp.concatenate(
                [
                    jnp.where(lower, mine[y], other[y]),
                    jnp.where(lower, other[y], mine[y]),
                ],
                axis=0,
            )
            rows = both.shape[0] // 2
            left = jnp.concatenate([both[0:seqs], both[rows : rows + seqs]], axis=0)
            right = jnp.concatenate(
                [both[seqs : 2 * seqs], both[rows + seqs : rows + 2 * seqs]], axis=0
            )
            leftn_ref[:, lanes_k] = left
            turnl_ref[lanes_k, :] = left.astype(f32).T
            turnr_ref[lanes_k, :] = right.astype(f32).T
            tiles = [
                both[first + 2 * seqs : first + 2 * seqs + MASK_ROWS].astype(f32)
                for first in (0, rows)
            ]
            maskt_ref[(2 * z + y) * res : (2 * z + y + 1) * res, :] = (
                tiles[0][0:res] + tiles[1][0:res]
            )
            own = mine[y][2 * seqs : 2 * seqs + MASK_ROWS].astype(f32)
            pair_lane = lax.broadcasted_iota(jnp.int32, (pair_cols, lanes), 1)
            pair_row = lax.broadcasted_iota(jnp.int32, (pair_cols, lanes), 0)
            for r in range(res):
                first = ((2 * z + y) * res + r) * pair_cols
                pml_ref[first : first + pair_cols, :] = jnp.where(
                    pair_lane == pair_row, own[res + r : res + r + 1, :], 0.0
                ).astype(bf16)
    for d in range(width):
        mine_ref[d * pair_cols : (d + 1) * pair_cols, :] = turnr_ref[
            pl.ds(me_depth * pair_cols * width + d, pair_cols, stride=width), :
        ].astype(bf16)
    for turned, out in ((turnl_ref, leftt_ref), (turnr_ref, rightt_ref)):
        for d in range(width):
            out[d * residues : (d + 1) * residues, :] = turned[
                pl.ds(d, residues, stride=width), :
            ].astype(bf16)

    maskt = maskt_ref[...]
    cols_mask = maskt_ref[pl.ds(pl.multiple_of(me_depth * pair_cols, pair_cols), pair_cols), :]
    for i in range(residues):
        cntl_ref[i * pair_cols : (i + 1) * pair_cols, :] = (maskt[i : i + 1, :] * cols_mask).astype(
            bf16
        )
    ones = jnp.ones((lanes, lanes), bf16)
    cnt_ref[...] = jnp.dot(cntl_ref[...], ones, preferred_element_type=f32)
    pm_ref[...] = jnp.dot(pml_ref[...], ones, preferred_element_type=f32).astype(bf16)

    for dh in range(width // 4):
        prod = jnp.dot(
            mine_ref[dh * 4 * pair_cols : (dh + 1) * 4 * pair_cols, :],
            leftn_ref[...],
            preferred_element_type=f32,
        )
        for k in range(cols):
            piece = prod[:, k * lanes : (k + 1) * lanes]
            turned = butterfly(
                [piece[a * pair_cols : (a + 1) * pair_cols] for a in range(4)], width
            )
            for il in range(res):
                first = (k * res + il) * pair_cols
                outer_ref[first : first + pair_cols, dh * lanes : (dh + 1) * lanes] = turned[
                    il
                ].astype(bf16)
    proj_out_ref[...] = jnp.dot(outer_ref[...], wturn_ref[...], preferred_element_type=f32)


def transition_kernel(
    sizes,
    ids_ref,
    near_ref,
    far_ref,
    proj_out_ref,
    cnt_ref,
    pm_ref,
    gain_ref,
    hid_ref,
    back_ref,
    couple_ref,
    opm_ref,
    pn_ref,
    gh_ref,
    hidden_ref,
    mg_ref,
    gmid_ref,
):
    seqs, res, pair_cols, width = sizes
    per = res * pair_cols
    cols = 2 * near_ref.shape[0]
    me_col = ids_ref[1]
    f32, bf16 = jnp.float32, jnp.bfloat16
    gain = gain_ref[...]
    chunk = 2 * per
    for at in range(cols // 2):
        rows = slice(at * chunk, (at + 1) * chunk)
        blocks = by_owner(ids_ref, at, near_ref, far_ref)
        act, grad = [
            jnp.concatenate([block[w * per : (w + 1) * per] for block in blocks], axis=0)
            for w in range(2)
        ]
        count = cnt_ref[rows, :]
        mid = act.astype(f32) + proj_out_ref[rows, :] / count
        scaled, inv = norm_pieces(mid)
        normed = (scaled * gain).astype(bf16)
        pn_ref[rows, :] = normed
        pre = jnp.dot(normed, hid_ref[...], preferred_element_type=f32)
        value, slope = silu_pieces(pre)
        hidden_ref[rows, :] = value.astype(bf16)
        masked = grad * pm_ref[rows, :]
        mg_ref[rows, :] = masked
        back = lax.dot_general(
            masked, back_ref[...], (((1,), (1,)), ((), ())), preferred_element_type=f32
        )
        ghid = (back * slope).astype(bf16)
        gh_ref[rows, :] = ghid
        gsc = (
            lax.dot_general(
                ghid, hid_ref[...], (((1,), (1,)), ((), ())), preferred_element_type=f32
            )
            * gain
        )
        gmid = grad.astype(f32) + standardize_adjoint(gsc, scaled, inv)
        gmid_ref[rows, :] = gmid
        opm_ref[rows, :] = (gmid / count).astype(bf16)
    couple_ref[...] = gmid_ref[pl.ds(pl.multiple_of(me_col * per, per), per), :].astype(bf16)


def projector_kernel(
    sizes,
    ids_ref,
    opm_ref,
    other_opm_ref,
    rightt_ref,
    leftt_ref,
    wout_ref,
    wturn_ref,
    maskt_ref,
    normed_ref,
    far_normed_ref,
    other_normed_ref,
    other_far_normed_ref,
    part_ref,
    spread_ref,
    gf_ref,
    grow_ref,
    gcol_ref,
    gor_ref,
    goc_ref,
    gs_ref,
    rows_ref,
):
    seqs, res, pair_cols, width = sizes
    depths, half = rows_ref.shape[1], gf_ref.shape[0]
    residues = half // pair_cols
    lanes = res * width
    here = 2 * res
    me_depth = ids_ref[0]
    me_col = ids_ref[1]
    me_y = me_col % 2
    first_here = (me_col // 2) * here
    f32, bf16 = jnp.float32, jnp.bfloat16
    my_half = first_here // pair_cols
    gf_ref[...] = jnp.where(my_half == me_depth, opm_ref[...], other_opm_ref[...]).astype(f32)
    for y, e, block in (
        (me_y, me_depth, normed_ref),
        (1 - me_y, me_depth, far_normed_ref),
        (me_y, 1 - me_depth, other_normed_ref),
        (1 - me_y, 1 - me_depth, other_far_normed_ref),
    ):
        rows_ref[y, e] = block[...]

    for il in range(here):
        first = pl.multiple_of((first_here + il) * pair_cols, pair_cols)
        for e, block in ((me_depth, opm_ref), (1 - me_depth, other_opm_ref)):
            to = pl.multiple_of(il * residues + e * pair_cols, pair_cols)
            grow_ref[pl.ds(to, pair_cols), :] = block[pl.ds(first, pair_cols), :]
    my_first = first_here - my_half * pair_cols
    for jl in range(here):
        gcol_ref[jl * residues : (jl + 1) * residues, :] = gf_ref[
            pl.ds(my_first + jl, residues, stride=pair_cols), :
        ].astype(bf16)
    for lhs, weight, out in ((grow_ref, wturn_ref, gor_ref), (gcol_ref, wout_ref, goc_ref)):
        for dh in range(width // 4):
            piece = lax.dot_general(
                lhs[...],
                weight[dh * lanes : (dh + 1) * lanes, :],
                (((1,), (1,)), ((), ())),
                preferred_element_type=f32,
            )
            for y in range(2):
                turned = butterfly(
                    [
                        piece[(y * res + a) * residues : (y * res + a + 1) * residues]
                        for a in range(4)
                    ],
                    width,
                )
                for dl in range(4):
                    first = (dh * 4 + dl) * residues
                    out[first : first + residues, y * lanes : (y + 1) * lanes] = turned[dl].astype(
                        bf16
                    )
    group = lax.broadcasted_iota(jnp.int32, (here, here * width), 1) // width
    spread = (group == lax.broadcasted_iota(jnp.int32, (here, here * width), 0)).astype(f32)
    mask_lanes = lax.dot_general(
        maskt_ref[pl.ds(pl.multiple_of(first_here, here), here), :],
        spread,
        (((0,), (0,)), ((), ())),
        preferred_element_type=f32,
    )
    lane_group = lax.broadcasted_iota(jnp.int32, (seqs, lanes), 1) // width
    for at, (lhs, rhs) in enumerate(((rightt_ref, gor_ref), (leftt_ref, goc_ref))):
        total = lax.dot_general(
            lhs[...], rhs[...], (((0,), (0,)), ((), ())), preferred_element_type=f32
        )
        total = (total * mask_lanes).astype(bf16).astype(f32)
        for y in range(2):
            for e in range(depths):
                block = total[e * seqs : (e + 1) * seqs, y * lanes : (y + 1) * lanes]
                for r in range(res):
                    gs_ref[at, y, e, pl.ds(r, seqs, stride=res), :] = jnp.where(
                        lane_group == r, block, 0.0
                    )
    spread_ref[...] = jnp.concatenate(
        [gs_ref[0, me_y, me_depth], gs_ref[1, me_y, me_depth]], axis=1
    ).astype(bf16)
    rows = rows_ref.shape[2]
    for at in range(2):
        cross = lax.dot_general(
            gs_ref[at].reshape(2 * depths * rows, lanes).astype(bf16),
            rows_ref[...].reshape(2 * depths * rows, rows_ref.shape[3]),
            (((0,), (0,)), ((), ())),
            preferred_element_type=f32,
        )
        total = cross[:width]
        for r in range(1, res):
            total = total + cross[r * width : (r + 1) * width]
        part_ref[at * width : (at + 1) * width, :] = total.astype(bf16)


def weights_kernel(outer_ref, opm_ref, pn_ref, gh_ref, hidden_ref, mg_ref, out_ref, turn_ref):
    pair_width, hid = pn_ref.shape[1], gh_ref.shape[1]
    outer_width = outer_ref.shape[1]
    width = int(outer_width**0.5 + 0.5)

    def contract(lhs, rhs):
        return lax.dot_general(
            lhs[...], rhs[...], (((0,), (0,)), ((), ())), preferred_element_type=jnp.float32
        )

    turn_ref[...] = contract(outer_ref, opm_ref)
    for c in range(width):
        out_ref[c * width : (c + 1) * width, :] = turn_ref[
            pl.ds(c, width, stride=width), :
        ].astype(jnp.bfloat16)
    dhid = contract(pn_ref, gh_ref).astype(jnp.bfloat16)
    for at in range(hid // pair_width):
        first = outer_width + at * pair_width
        out_ref[first : first + pair_width, :] = dhid[:, at * pair_width : (at + 1) * pair_width]
    out_ref[outer_width + hid :, :] = contract(hidden_ref, mg_ref).astype(jnp.bfloat16)


def weights_sum_kernel(mine_ref, other_ref, dout_ref, dhid_ref, dback_ref):
    pair_width, hid = dhid_ref.shape
    outer_width = dout_ref.shape[0]

    def added(first, count):
        rows = slice(first, first + count)
        return mine_ref[rows, :].astype(jnp.float32) + other_ref[rows, :].astype(jnp.float32)

    dout_ref[...] = added(0, outer_width)
    for at in range(hid // pair_width):
        dhid_ref[:, at * pair_width : (at + 1) * pair_width] = added(
            outer_width + at * pair_width, pair_width
        )
    dback_ref[...] = added(outer_width + hid, hid)


def feature_kernel(
    copies,
    spread_ref,
    first_ref,
    second_ref,
    scale_ref,
    scaled_ref,
    inv_ref,
    held_ref,
    feat_ref,
    couple_ref,
):
    back = jnp.dot(
        spread_ref[...],
        wide_projector(first_ref, second_ref, copies),
        preferred_element_type=jnp.float32,
    )
    feat = standardize_adjoint(back * scale_ref[...], scaled_ref[...], inv_ref[...])
    feat_ref[...] = feat.reshape(feat_ref.shape).astype(jnp.bfloat16)
    couple_ref[...] = held_ref[...]


def swap_line(block, partners):
    count = lax.axis_size("col")
    pairs = [
        (depth * count + at, depth * count + (at ^ partner))
        for depth, partner in enumerate(partners)
        if partner is not None
        for at in range(count)
    ]
    return lax.ppermute(block, ("depth", "col"), pairs)


def swap_depth(block):
    return lax.ppermute(block, "depth", [(0, 1), (1, 0)])


def pairwise_sum(blocks):
    while len(blocks) > 1:
        blocks = [blocks[at] + blocks[at + 1] for at in range(0, len(blocks), 2)]
    return blocks[0]


def swap_col(block, partner):
    count = lax.axis_size("col")
    return lax.ppermute(block, "col", [(at, at ^ partner) for at in range(count)])


def whole_plan(
    alignment_activations,
    alignment_mask,
    pair_activation_input,
    pair_update_mask,
    pair_output_gradient,
    layer_scale_factor,
    first_projector,
    second_projector,
    output_weight,
    pair_norm_gain,
    hidden_weight,
    back_weight,
):
    seqs, res, channels = alignment_activations.shape
    width = first_projector.shape[1]
    outer_width = width * width
    cols = lax.axis_size("col")
    depths = lax.axis_size("depth")
    residues = res * cols
    pair_cols, pair_width = pair_activation_input.shape[1:]
    hid = hidden_weight.shape[1]
    per = res * pair_cols
    lanes = res * width
    rows = 2 * seqs + MASK_ROWS
    half = residues * pair_cols
    f32, bf16 = jnp.float32, jnp.bfloat16
    ids = jnp.stack([lax.axis_index("depth"), lax.axis_index("col")]).astype(jnp.int32)
    smem = pl.BlockSpec(memory_space=pltpu.SMEM)
    vmem = pl.BlockSpec(memory_space=pltpu.VMEM)
    params = pltpu.CompilerParams(vmem_limit_bytes=16 * 2**20)
    scale = layer_scale_factor.reshape(1, channels)
    first, second = first_projector.T, second_projector.T
    wturn = jnp.transpose(output_weight.reshape(width, width, pair_width), (1, 0, 2)).reshape(
        outer_width, pair_width
    )
    shape = jax.ShapeDtypeStruct
    sent, scale, first, second, gain, normed, scaled, inv = pl.pallas_call(
        pre_kernel,
        out_shape=(
            shape((1, rows + 2 * per, pair_width), bf16),
            shape((1, channels), f32),
            shape((width, channels), bf16),
            shape((width, channels), bf16),
            shape((1, pair_width), f32),
            shape((seqs * res, channels), bf16),
            shape((seqs * res, channels), f32),
            shape((seqs * res, 1), f32),
        ),
        in_specs=[smem] + [pl.BlockSpec(memory_space=pltpu.HBM)] * 9,
        out_specs=[vmem] * 8,
        scratch_shapes=[
            pltpu.VMEM((2, seqs * res, lanes), f32),
            pltpu.VMEM((MASK_ROWS, lanes), f32),
            pltpu.VMEM((seqs, res, channels), bf16),
            pltpu.VMEM((res, seqs), jnp.int32),
            pltpu.VMEM((res, pair_cols), jnp.int32),
            pltpu.SemaphoreType.DMA((9,)),
        ],
        compiler_params=params,
        name="project",
    )(
        ids,
        *[
            pltpu.with_memory_space_constraint(array, pltpu.HBM)
            for array in (
                alignment_activations,
                alignment_mask.T,
                pair_update_mask,
                scale,
                first,
                second,
                pair_norm_gain.reshape(1, pair_width),
                pair_activation_input.reshape(per, pair_width),
                pair_output_gradient.reshape(per, pair_width),
            )
        ],
    )
    blocks = lax.optimization_barrier(
        jnp.concatenate([sent] + [swap_col(sent, partner) for partner in Z_PARTNERS])
    )
    far_normed = swap_col(normed, Y_PARTNER)
    blocks, far_normed = lax.optimization_barrier((blocks, far_normed))
    near, pair_near = blocks[:, :rows], blocks[:, rows:]
    far = swap_col(near, Y_PARTNER)
    pair_far = swap_col(pair_near, Y_PARTNER)
    other_near, other_far = swap_depth(near), swap_depth(far)
    sizes = (seqs, res, pair_cols, width)
    outer, proj_out, cnt, pm, maskt, rightt, leftt = pl.pallas_call(
        functools.partial(outer_kernel, sizes),
        out_shape=(
            shape((half, outer_width), bf16),
            shape((half, pair_width), f32),
            shape((half, lanes), f32),
            shape((half, lanes), bf16),
            shape((residues, depths * seqs), f32),
            shape((residues * width, depths * seqs), bf16),
            shape((residues * width, depths * seqs), bf16),
        ),
        in_specs=[smem] + [vmem] * 5,
        out_specs=[vmem] * 7,
        scratch_shapes=[
            pltpu.VMEM((depths * seqs, residues * width), bf16),
            pltpu.VMEM((pair_cols * width, depths * seqs), bf16),
            pltpu.VMEM((residues * width, depths * seqs), f32),
            pltpu.VMEM((residues * width, depths * seqs), f32),
            pltpu.VMEM((half, lanes), bf16),
            pltpu.VMEM((half, lanes), bf16),
        ],
        compiler_params=params,
        name="outer_products",
    )(ids, near, far, other_near, other_far, wturn)
    normed_again, far_again, proj_out = lax.optimization_barrier((normed, far_normed, proj_out))
    other_normed, other_far_normed = swap_depth(normed_again), swap_depth(far_again)
    pair_far, proj_out, other_normed, other_far_normed = lax.optimization_barrier(
        (pair_far, proj_out, other_normed, other_far_normed)
    )
    held, opm, pn, gh, hidden, mg = pl.pallas_call(
        functools.partial(transition_kernel, sizes),
        out_shape=(
            shape((per, pair_width), bf16),
            shape((half, pair_width), bf16),
            shape((half, pair_width), bf16),
            shape((half, hid), bf16),
            shape((half, hid), bf16),
            shape((half, pair_width), bf16),
        ),
        in_specs=[smem] + [vmem] * 8,
        out_specs=[vmem] * 6,
        scratch_shapes=[
            pltpu.VMEM((half, pair_width), f32),
        ],
        compiler_params=params,
        name="transition",
    )(
        ids,
        pair_near,
        pair_far,
        proj_out,
        cnt,
        pm,
        gain,
        hidden_weight,
        back_weight,
    )
    weights = pl.pallas_call(
        weights_kernel,
        out_shape=shape((outer_width + 2 * hid, pair_width), bf16),
        in_specs=[vmem] * 6,
        out_specs=vmem,
        scratch_shapes=[pltpu.VMEM((outer_width, pair_width), f32)],
        compiler_params=params,
        name="weight_gradients",
    )(outer, opm, pn, gh, hidden, mg)
    other_opm, weights = lax.optimization_barrier((swap_depth(opm), weights))
    part, spread = pl.pallas_call(
        functools.partial(projector_kernel, sizes),
        out_shape=(
            shape((2 * width, channels), bf16),
            shape((seqs * res, 2 * lanes), bf16),
        ),
        in_specs=[smem] + [vmem] * 11,
        out_specs=[vmem] * 2,
        scratch_shapes=[
            pltpu.VMEM((half, pair_width), f32),
            pltpu.VMEM((2 * res * residues, pair_width), bf16),
            pltpu.VMEM((2 * res * residues, pair_width), bf16),
            pltpu.VMEM((residues * width, 2 * lanes), bf16),
            pltpu.VMEM((residues * width, 2 * lanes), bf16),
            pltpu.VMEM((2, 2, depths, seqs * res, lanes), f32),
            pltpu.VMEM((2, depths, seqs * res, channels), bf16),
        ],
        compiler_params=params,
        name="projector_parts",
    )(
        ids,
        opm,
        other_opm,
        rightt,
        leftt,
        output_weight,
        wturn,
        maskt,
        normed,
        far_normed,
        other_normed,
        other_far_normed,
    )
    feat, couple = pl.pallas_call(
        functools.partial(feature_kernel, res),
        out_shape=(shape((seqs, res, channels), bf16), shape((per, pair_width), bf16)),
        in_specs=[vmem] * 7,
        out_specs=[vmem] * 2,
        compiler_params=params,
        name="features",
    )(spread, first, second, scale, scaled, inv, held)
    part, weights = lax.optimization_barrier((part, weights))
    dout, dhid, dback = pl.pallas_call(
        weights_sum_kernel,
        out_shape=(
            shape((outer_width, pair_width), f32),
            shape((pair_width, hid), f32),
            shape((hid, pair_width), f32),
        ),
        in_specs=[vmem] * 2,
        out_specs=[vmem] * 3,
        compiler_params=params,
        name="sums_over_depth",
    )(weights, swap_depth(weights))
    came_b = swap_line(part, (None, Z_PARTNERS[0]))
    came_a = swap_line(part, (Z_PARTNERS[2], Z_PARTNERS[1]))
    came_b, came_a, feat, couple = lax.optimization_barrier((came_b, came_a, feat, couple))
    kept = jnp.where(lax.axis_index("depth") == 0, part, came_b)
    kept = lax.optimization_barrier((kept.astype(f32) + came_a.astype(f32)).astype(bf16))
    came = swap_depth(kept)
    came, dout, dhid, dback = lax.optimization_barrier((came, dout, dhid, dback))
    total = kept.astype(f32) + came.astype(f32)
    return (
        feat,
        couple.reshape(res, pair_cols, pair_width),
        total[:width].T,
        total[width:].T,
        dout,
        dhid,
        dback,
    )


def on_device(alignment_activations, *others):
    cols = lax.axis_size("col")
    residues = alignment_activations.shape[1] * cols
    plan = whole_plan if cols == 8 and residues <= FEW_RESIDUES else split_plan
    return plan(alignment_activations, *others)


def solution(mesh):
    in_specs = (
        P(("group", "depth"), "col", None),
        P(("group", "depth"), "col"),
        P(("group", "col"), "depth", None),
        P(("group", "col"), "depth"),
        P(("group", "col"), "depth", None),
        P(),
        P(),
        P(),
        P(),
        P(),
        P(),
        P(),
    )
    out_specs = (
        P(("group", "depth"), "col", None),
        P(("group", "col"), "depth", None),
        P("group", None),
        P("group", None),
        P("group", None),
        P("group", None),
        P("group", None),
    )
    return jax.shard_map(
        on_device, mesh=mesh, in_specs=in_specs, out_specs=out_specs, check_vma=False
    )
```

```python
import functools

import jax
import jax.numpy as jnp
from jax import lax
from jax.experimental import pallas as pl
from jax.experimental.pallas import tpu as pltpu
from jax.sharding import PartitionSpec as P

epsilon = 1e-05
highest = lax.Precision.HIGHEST


def norm_pieces(entries_drawn):
    center = entries_drawn - jnp.mean(entries_drawn, axis=-1, keepdims=True)
    inv_std = lax.rsqrt(jnp.mean(center * center, axis=-1, keepdims=True) + epsilon)
    return (center * inv_std, inv_std)


def standardize_adjoint(grad_scaled, scaled, inv_std):
    mean_grad = jnp.mean(grad_scaled, axis=-1, keepdims=True)
    mean_cross = jnp.mean(grad_scaled * scaled, axis=-1, keepdims=True)
    return inv_std * (grad_scaled - mean_grad - scaled * mean_cross)


def silu_pieces(pre_act):
    sigma = jax.nn.sigmoid(pre_act)
    return (pre_act * sigma, sigma * (1.0 + pre_act * (1.0 - sigma)))


def split_plan(
    alignment_activations,
    alignment_mask,
    pair_activation_input,
    pair_update_mask,
    pair_output_gradient,
    layer_scale_factor,
    first_projector,
    second_projector,
    output_weight,
    pair_norm_gain,
    hidden_weight,
    back_weight,
):
    sequence_row_block, residue_row_block, channel_total = alignment_activations.shape
    proj_width = first_projector.shape[1]
    outer_width = proj_width * proj_width
    depth_count = lax.axis_size("depth")
    residues = residue_row_block * lax.axis_size("col")
    pair_cols = pair_activation_input.shape[1]
    pair_width = pair_activation_input.shape[2]
    col_block = min(64, pair_cols)
    block_count = pair_cols // col_block
    standardized_features, reciprocal_spread = norm_pieces(
        alignment_activations.astype(jnp.float32)
    )
    normalized_rows = (standardized_features * layer_scale_factor).astype(jnp.bfloat16)
    mask_floating = alignment_mask.astype(jnp.float32)
    left_proj = (
        jnp.dot(normalized_rows, first_projector, preferred_element_type=jnp.float32)
        * mask_floating[:, :, None]
    ).astype(jnp.bfloat16)
    right_proj = (
        jnp.dot(normalized_rows, second_projector, preferred_element_type=jnp.float32)
        * mask_floating[:, :, None]
    ).astype(jnp.bfloat16)
    right_flat = right_proj.reshape(sequence_row_block, residue_row_block * proj_width)
    mask_converted = alignment_mask.astype(jnp.bfloat16)
    seq_total = left_proj.shape[0]
    gathered, gathered_mask = (
        lax.all_gather(right_flat, "col", axis=1, tiled=True),
        lax.all_gather(mask_converted, "col", axis=1, tiled=True),
    )
    right_blocks = gathered.reshape(seq_total, depth_count, pair_cols, proj_width)
    mask_blocks = gathered_mask.reshape(seq_total, depth_count, pair_cols)
    block_depth = right_blocks.shape[1]
    out_wide = output_weight.astype(jnp.float32)

    def partial_outer(col_start):
        right_piece = lax.dynamic_slice_in_dim(right_blocks, col_start, col_block, 2)
        outer_part = jnp.einsum(
            "sic,sejd->iejcd", left_proj, right_piece, preferred_element_type=jnp.float32
        )
        return (
            outer_part.reshape(residue_row_block, block_depth, col_block, outer_width),
            right_piece,
        )

    def forward_step(step_index, loop_state):
        projected, pair_count = loop_state
        col_start = step_index * col_block
        outer_part, right_piece = partial_outer(col_start)
        mask_piece = lax.dynamic_slice_in_dim(mask_blocks, col_start, col_block, 2).astype(
            jnp.float32
        )
        count_part = jnp.einsum("si,sej->iej", mask_floating, mask_piece, precision=highest)
        outer_mine, count_mine = (
            lax.psum_scatter(
                outer_part.astype(jnp.bfloat16), "depth", scatter_dimension=1, tiled=True
            ).astype(jnp.float32),
            lax.psum_scatter(
                count_part.astype(jnp.bfloat16), "depth", scatter_dimension=1, tiled=True
            ).astype(jnp.float32),
        )
        proj_mine = jnp.dot(
            outer_mine.reshape(residue_row_block * col_block, outer_width),
            out_wide,
            precision=highest,
        )
        proj_mine = proj_mine.reshape(residue_row_block, col_block, pair_width)
        count_mine = count_mine.reshape(residue_row_block, col_block)
        projected = lax.dynamic_update_slice_in_dim(projected, proj_mine, col_start, 1)
        pair_count = lax.dynamic_update_slice_in_dim(pair_count, count_mine, col_start, 1)
        return (projected, pair_count)

    projected, pair_count = lax.fori_loop(
        0,
        block_count,
        forward_step,
        (
            jnp.zeros((residue_row_block, pair_cols, pair_width), jnp.float32),
            jnp.zeros((residue_row_block, pair_cols), jnp.float32),
        ),
    )
    count_column = pair_count.reshape(residue_row_block * pair_cols, 1)
    mid_act = (
        pair_activation_input.reshape(residue_row_block * pair_cols, pair_width).astype(jnp.float32)
        + projected.reshape(residue_row_block * pair_cols, pair_width) / count_column
    )
    pair_scaled, pair_inv = norm_pieces(mid_act)
    pair_normed = (pair_scaled * pair_norm_gain).astype(jnp.bfloat16)
    pre_act = jnp.dot(pair_normed, hidden_weight, preferred_element_type=jnp.float32)
    act_value, act_slope = silu_pieces(pre_act)
    hidden = act_value.astype(jnp.bfloat16)
    masked_grad = (
        pair_output_gradient * pair_update_mask.astype(jnp.bfloat16)[:, :, None]
    ).reshape(residue_row_block * pair_cols, pair_width)
    final_matrix_derivative = jnp.dot(hidden.T, masked_grad, preferred_element_type=jnp.float32)
    back_prod = jnp.dot(masked_grad, back_weight.T, preferred_element_type=jnp.float32)
    grad_hidden = (back_prod * act_slope).astype(jnp.bfloat16)
    middle_matrix_derivative = jnp.dot(
        pair_normed.T, grad_hidden, preferred_element_type=jnp.float32
    )
    grad_scaled = (
        jnp.dot(grad_hidden, hidden_weight.T, preferred_element_type=jnp.float32) * pair_norm_gain
    )
    grad_mid = pair_output_gradient.reshape(residue_row_block * pair_cols, pair_width).astype(
        jnp.float32
    ) + standardize_adjoint(grad_scaled, pair_scaled, pair_inv)
    couple_features_derivative = grad_mid.astype(jnp.bfloat16).reshape(
        residue_row_block, pair_cols, pair_width
    )
    grad_opm = (
        (grad_mid / count_column)
        .astype(jnp.bfloat16)
        .reshape(residue_row_block, pair_cols, pair_width)
    )
    full_opm = lax.all_gather(grad_opm, "depth", axis=1, tiled=True).reshape(
        residue_row_block, depth_count, pair_cols, pair_width
    )

    def backward_step(step_index, loop_state):
        grad_left_acc, grad_out, right_term = loop_state
        col_start = step_index * col_block
        outer_part, right_piece = partial_outer(col_start)
        opm_piece = lax.dynamic_slice_in_dim(full_opm, col_start, col_block, 2).reshape(
            residue_row_block * block_depth * col_block, pair_width
        )
        grad_out = grad_out + jnp.dot(
            outer_part.reshape(residue_row_block * block_depth * col_block, outer_width).T,
            opm_piece.astype(jnp.float32),
            precision=highest,
        )
        grad_outer = jnp.dot(opm_piece, output_weight.T, preferred_element_type=jnp.float32).astype(
            jnp.bfloat16
        )
        grad_outer = grad_outer.reshape(
            residue_row_block, block_depth, col_block, proj_width, proj_width
        )
        grad_left_acc = grad_left_acc + jnp.einsum(
            "iejcd,sejd->sic", grad_outer, right_piece, preferred_element_type=jnp.float32
        )
        piece_term = jnp.einsum(
            "iejcd,sic->ejsd", grad_outer, left_proj, preferred_element_type=jnp.float32
        )
        piece_term = piece_term.reshape(block_depth, col_block, seq_total * proj_width)
        right_term = lax.dynamic_update_slice_in_dim(right_term, piece_term, col_start, 1)
        return (grad_left_acc, grad_out, right_term)

    grad_left_acc, result_matrix_derivative, right_term = lax.fori_loop(
        0,
        block_count,
        backward_step,
        (
            jnp.zeros((seq_total, residue_row_block, proj_width), jnp.float32),
            jnp.zeros((outer_width, pair_width), jnp.float32),
            jnp.zeros((block_depth, pair_cols, seq_total * proj_width), jnp.float32),
        ),
    )
    grad_right_sum = lax.psum_scatter(
        right_term.reshape(residues, seq_total * proj_width), "col", scatter_dimension=0, tiled=True
    )
    grad_right_acc = jnp.transpose(
        grad_right_sum.reshape(residue_row_block, seq_total, proj_width), (1, 0, 2)
    )
    grad_left = (grad_left_acc * mask_floating[:, :, None]).astype(jnp.bfloat16)
    grad_right = (grad_right_acc * mask_floating[:, :, None]).astype(jnp.bfloat16)
    normed_rows = normalized_rows.reshape(sequence_row_block * residue_row_block, channel_total)
    first_projector_derivative = jnp.dot(
        normed_rows.T,
        grad_left.reshape(sequence_row_block * residue_row_block, proj_width),
        preferred_element_type=jnp.float32,
    )
    second_projector_derivative = jnp.dot(
        normed_rows.T,
        grad_right.reshape(sequence_row_block * residue_row_block, proj_width),
        preferred_element_type=jnp.float32,
    )
    standardized_derivative = jnp.dot(
        grad_left, first_projector.T, preferred_element_type=jnp.float32
    ) + jnp.dot(grad_right, second_projector.T, preferred_element_type=jnp.float32)
    features_derivative = standardize_adjoint(
        standardized_derivative * layer_scale_factor, standardized_features, reciprocal_spread
    ).astype(jnp.bfloat16)
    weight_sums = lax.psum(
        (
            first_projector_derivative,
            second_projector_derivative,
            result_matrix_derivative,
            middle_matrix_derivative,
            final_matrix_derivative,
        ),
        ("depth", "col"),
    )
    return (
        features_derivative,
        couple_features_derivative,
        weight_sums[0],
        weight_sums[1],
        weight_sums[2],
        weight_sums[3],
        weight_sums[4],
    )


FEW_RESIDUES = 32
MASK_ROWS = 16
Z_PARTNERS = (2, 4, 6)
Y_PARTNER = 1


def butterfly(blocks, group):
    lane_group = lax.broadcasted_iota(jnp.int32, blocks[0].shape, 1) // group
    width = 4 * group
    for bit in (2, 1):
        low = (lane_group & bit) == 0
        swapped = list(blocks)
        for at in range(4):
            if at & bit:
                continue
            here, there = blocks[at], blocks[at | bit]
            moving = jnp.where(low, there, here)
            if bit == 2:
                moved = pltpu.roll(moving, 2 * group, 1)
            else:
                moved = jnp.where(
                    low, pltpu.roll(moving, width - group, 1), pltpu.roll(moving, group, 1)
                )
            swapped[at] = jnp.where(low, here, moved)
            swapped[at | bit] = jnp.where(low, moved, there)
        blocks = swapped
    return blocks


def wide_projector(first_ref, second_ref, copies):
    return jnp.concatenate([first_ref[...]] * copies + [second_ref[...]] * copies, axis=0)


def pre_kernel(
    ids_ref,
    x_hbm,
    maskt_hbm,
    pmask_hbm,
    scale_hbm,
    first_hbm,
    second_hbm,
    gain_hbm,
    act_hbm,
    grad_hbm,
    sent_ref,
    scale_ref,
    first_ref,
    second_ref,
    gain_ref,
    normed_ref,
    scaled_ref,
    inv_ref,
    wide_ref,
    tile_ref,
    x_ref,
    maskt_ref,
    pmask_ref,
    sems,
):
    res, seqs = maskt_ref.shape
    pairs = act_hbm.shape[0]
    first_pair = 2 * seqs + MASK_ROWS
    copies = [
        pltpu.make_async_copy(source, target, sems.at[at])
        for at, (source, target) in enumerate(
            (
                (x_hbm, x_ref),
                (maskt_hbm, maskt_ref),
                (pmask_hbm, pmask_ref),
                (scale_hbm, scale_ref),
                (first_hbm, first_ref),
                (second_hbm, second_ref),
                (gain_hbm, gain_ref),
                (act_hbm, sent_ref.at[0, pl.ds(first_pair, pairs), :]),
                (grad_hbm, sent_ref.at[0, pl.ds(first_pair + pairs, pairs), :]),
            )
        )
    ]
    for copy in copies:
        copy.start()
    for copy in copies:
        copy.wait()
    lanes = sent_ref.shape[2]
    group = lanes // res
    scaled, inv = norm_pieces(
        x_ref[...].astype(jnp.float32).reshape(seqs * res, x_ref.shape[2])
    )
    scaled_ref[...] = scaled
    inv_ref[...] = inv
    normed = (scaled * scale_ref[...]).astype(jnp.bfloat16)
    normed_ref[...] = normed
    wide = lax.dot_general(
        normed,
        wide_projector(first_ref, second_ref, res),
        (((1,), (1,)), ((), ())),
        preferred_element_type=jnp.float32,
    )
    for at in range(2):
        wide_ref[at] = wide[:, at * lanes : (at + 1) * lanes]
    tile_ref[...] = jnp.zeros(tile_ref.shape, jnp.float32)
    mask = maskt_ref[...].astype(jnp.float32)
    tile_ref[0:res, 0:seqs] = mask
    spread = (
        lax.broadcasted_iota(jnp.int32, (MASK_ROWS, lanes), 1) // group
        == lax.broadcasted_iota(jnp.int32, (MASK_ROWS, lanes), 0)
    ).astype(jnp.float32)
    mask_lanes = lax.dot_general(
        tile_ref[...], spread, (((0,), (0,)), ((), ())), preferred_element_type=jnp.float32
    )[:seqs]
    twice = jnp.concatenate([mask] * (lanes // seqs), axis=1)
    here = lax.broadcasted_iota(jnp.int32, (res, lanes), 1) // seqs == ids_ref[0]
    tile_ref[0:res, :] = jnp.where(here, twice, 0.0)
    tile_ref[res : 2 * res, 0 : pmask_ref.shape[1]] = pmask_ref[...].astype(jnp.float32)
    lane_group = lax.broadcasted_iota(jnp.int32, (seqs, lanes), 1) // group
    for at in range(2):
        both = wide_ref[at, pl.ds(0, seqs, stride=res), :]
        for r in range(1, res):
            both = jnp.where(
                lane_group == r, wide_ref[at, pl.ds(r, seqs, stride=res), :], both
            )
        sent_ref[0, at * seqs : (at + 1) * seqs, :] = (both * mask_lanes).astype(jnp.bfloat16)
    sent_ref[0, 2 * seqs : first_pair, :] = tile_ref[...].astype(jnp.bfloat16)


def by_owner(ids_ref, z, near_ref, far_ref):
    step = z ^ (ids_ref[1] // 2)
    near, far = near_ref[step], far_ref[step]
    first = ids_ref[1] % 2 == 0
    return jnp.where(first, near, far), jnp.where(first, far, near)


def outer_kernel(
    sizes,
    ids_ref,
    near_ref,
    far_ref,
    other_near_ref,
    other_far_ref,
    wturn_ref,
    outer_ref,
    proj_out_ref,
    cnt_ref,
    pm_ref,
    maskt_ref,
    rightt_ref,
    leftt_ref,
    leftn_ref,
    mine_ref,
    turnl_ref,
    turnr_ref,
    cntl_ref,
    pml_ref,
):
    seqs, res, pair_cols, width = sizes
    line = near_ref.shape[0]
    cols = 2 * line
    residues = cols * res
    lanes = res * width
    me_depth = ids_ref[0]
    lower = me_depth == 0
    f32, bf16 = jnp.float32, jnp.bfloat16

    for z in range(line):
        mine = by_owner(ids_ref, z, near_ref, far_ref)
        other = by_owner(ids_ref, z, other_near_ref, other_far_ref)
        for y in range(2):
            lanes_k = slice((2 * z + y) * lanes, (2 * z + y + 1) * lanes)
            both = jnp.concatenate(
                [
                    jnp.where(lower, mine[y], other[y]),
                    jnp.where(lower, other[y], mine[y]),
                ],
                axis=0,
            )
            rows = both.shape[0] // 2
            left = jnp.concatenate([both[0:seqs], both[rows : rows + seqs]], axis=0)
            right = jnp.concatenate(
                [both[seqs : 2 * seqs], both[rows + seqs : rows + 2 * seqs]], axis=0
            )
            leftn_ref[:, lanes_k] = left
            turnl_ref[lanes_k, :] = left.astype(f32).T
            turnr_ref[lanes_k, :] = right.astype(f32).T
            tiles = [
                both[first + 2 * seqs : first + 2 * seqs + MASK_ROWS].astype(f32)
                for first in (0, rows)
            ]
            maskt_ref[(2 * z + y) * res : (2 * z + y + 1) * res, :] = (
                tiles[0][0:res] + tiles[1][0:res]
            )
            own = mine[y][2 * seqs : 2 * seqs + MASK_ROWS].astype(f32)
            pair_lane = lax.broadcasted_iota(jnp.int32, (pair_cols, lanes), 1)
            pair_row = lax.broadcasted_iota(jnp.int32, (pair_cols, lanes), 0)
            for r in range(res):
                first = ((2 * z + y) * res + r) * pair_cols
                pml_ref[first : first + pair_cols, :] = jnp.where(
                    pair_lane == pair_row, own[res + r : res + r + 1, :], 0.0
                ).astype(bf16)
    for d in range(width):
        mine_ref[d * pair_cols : (d + 1) * pair_cols, :] = turnr_ref[
            pl.ds(me_depth * pair_cols * width + d, pair_cols, stride=width), :
        ].astype(bf16)
    for turned, out in ((turnl_ref, leftt_ref), (turnr_ref, rightt_ref)):
        for d in range(width):
            out[d * residues : (d + 1) * residues, :] = turned[
                pl.ds(d, residues, stride=width), :
            ].astype(bf16)

    maskt = maskt_ref[...]
    cols_mask = maskt_ref[pl.ds(pl.multiple_of(me_depth * pair_cols, pair_cols), pair_cols), :]
    for i in range(residues):
        cntl_ref[i * pair_cols : (i + 1) * pair_cols, :] = (maskt[i : i + 1, :] * cols_mask).astype(
            bf16
        )
    ones = jnp.ones((lanes, lanes), bf16)
    cnt_ref[...] = jnp.dot(cntl_ref[...], ones, preferred_element_type=f32)
    pm_ref[...] = jnp.dot(pml_ref[...], ones, preferred_element_type=f32).astype(bf16)

    for dh in range(width // 4):
        prod = jnp.dot(
            mine_ref[dh * 4 * pair_cols : (dh + 1) * 4 * pair_cols, :],
            leftn_ref[...],
            preferred_element_type=f32,
        )
        for k in range(cols):
            piece = prod[:, k * lanes : (k + 1) * lanes]
            turned = butterfly(
                [piece[a * pair_cols : (a + 1) * pair_cols] for a in range(4)], width
            )
            for il in range(res):
                first = (k * res + il) * pair_cols
                outer_ref[first : first + pair_cols, dh * lanes : (dh + 1) * lanes] = turned[
                    il
                ].astype(bf16)
    proj_out_ref[...] = jnp.dot(outer_ref[...], wturn_ref[...], preferred_element_type=f32)


def transition_kernel(
    sizes,
    ids_ref,
    near_ref,
    far_ref,
    proj_out_ref,
    cnt_ref,
    pm_ref,
    gain_ref,
    hid_ref,
    back_ref,
    couple_ref,
    opm_ref,
    pn_ref,
    gh_ref,
    hidden_ref,
    mg_ref,
    gmid_ref,
):
    seqs, res, pair_cols, width = sizes
    per = res * pair_cols
    cols = 2 * near_ref.shape[0]
    me_col = ids_ref[1]
    f32, bf16 = jnp.float32, jnp.bfloat16
    gain = gain_ref[...]
    chunk = 2 * per
    for at in range(cols // 2):
        rows = slice(at * chunk, (at + 1) * chunk)
        blocks = by_owner(ids_ref, at, near_ref, far_ref)
        act, grad = [
            jnp.concatenate([block[w * per : (w + 1) * per] for block in blocks], axis=0)
            for w in range(2)
        ]
        count = cnt_ref[rows, :]
        mid = act.astype(f32) + proj_out_ref[rows, :] / count
        scaled, inv = norm_pieces(mid)
        normed = (scaled * gain).astype(bf16)
        pn_ref[rows, :] = normed
        pre = jnp.dot(normed, hid_ref[...], preferred_element_type=f32)
        value, slope = silu_pieces(pre)
        hidden_ref[rows, :] = value.astype(bf16)
        masked = grad * pm_ref[rows, :]
        mg_ref[rows, :] = masked
        back = lax.dot_general(
            masked, back_ref[...], (((1,), (1,)), ((), ())), preferred_element_type=f32
        )
        ghid = (back * slope).astype(bf16)
        gh_ref[rows, :] = ghid
        gsc = (
            lax.dot_general(
                ghid, hid_ref[...], (((1,), (1,)), ((), ())), preferred_element_type=f32
            )
            * gain
        )
        gmid = grad.astype(f32) + standardize_adjoint(gsc, scaled, inv)
        gmid_ref[rows, :] = gmid
        opm_ref[rows, :] = (gmid / count).astype(bf16)
    couple_ref[...] = gmid_ref[pl.ds(pl.multiple_of(me_col * per, per), per), :].astype(bf16)


def projector_kernel(
    sizes,
    ids_ref,
    opm_ref,
    other_opm_ref,
    rightt_ref,
    leftt_ref,
    wout_ref,
    wturn_ref,
    maskt_ref,
    normed_ref,
    far_normed_ref,
    other_normed_ref,
    part_ref,
    spread_ref,
    gf_ref,
    grow_ref,
    gcol_ref,
    gor_ref,
    goc_ref,
    gs_ref,
    rows_ref,
):
    seqs, res, pair_cols, width = sizes
    depths, half = rows_ref.shape[1], gf_ref.shape[0]
    residues = half // pair_cols
    lanes = res * width
    here = 2 * res
    me_depth = ids_ref[0]
    me_col = ids_ref[1]
    me_y = me_col % 2
    first_here = (me_col // 2) * here
    f32, bf16 = jnp.float32, jnp.bfloat16
    my_half = first_here // pair_cols
    gf_ref[...] = jnp.where(my_half == me_depth, opm_ref[...], other_opm_ref[...]).astype(f32)
    rows = rows_ref.shape[2]
    rows_ref[me_y, me_depth] = normed_ref[...]
    rows_ref[1 - me_y, me_depth] = far_normed_ref[...]
    rows_ref[me_y, 1 - me_depth] = other_normed_ref[0:rows, :]
    rows_ref[1 - me_y, 1 - me_depth] = other_normed_ref[rows:, :]

    for il in range(here):
        first = pl.multiple_of((first_here + il) * pair_cols, pair_cols)
        for e, block in ((me_depth, opm_ref), (1 - me_depth, other_opm_ref)):
            to = pl.multiple_of(il * residues + e * pair_cols, pair_cols)
            grow_ref[pl.ds(to, pair_cols), :] = block[pl.ds(first, pair_cols), :]
    my_first = first_here - my_half * pair_cols
    for jl in range(here):
        gcol_ref[jl * residues : (jl + 1) * residues, :] = gf_ref[
            pl.ds(my_first + jl, residues, stride=pair_cols), :
        ].astype(bf16)
    for lhs, weight, out in ((grow_ref, wturn_ref, gor_ref), (gcol_ref, wout_ref, goc_ref)):
        for dh in range(width // 4):
            piece = lax.dot_general(
                lhs[...],
                weight[dh * lanes : (dh + 1) * lanes, :],
                (((1,), (1,)), ((), ())),
                preferred_element_type=f32,
            )
            for y in range(2):
                turned = butterfly(
                    [
                        piece[(y * res + a) * residues : (y * res + a + 1) * residues]
                        for a in range(4)
                    ],
                    width,
                )
                for dl in range(4):
                    first = (dh * 4 + dl) * residues
                    out[first : first + residues, y * lanes : (y + 1) * lanes] = turned[dl].astype(
                        bf16
                    )
    group = lax.broadcasted_iota(jnp.int32, (here, here * width), 1) // width
    spread = (group == lax.broadcasted_iota(jnp.int32, (here, here * width), 0)).astype(f32)
    mask_lanes = lax.dot_general(
        maskt_ref[pl.ds(pl.multiple_of(first_here, here), here), :],
        spread,
        (((0,), (0,)), ((), ())),
        preferred_element_type=f32,
    )
    lane_group = lax.broadcasted_iota(jnp.int32, (seqs, lanes), 1) // width
    for at, (lhs, rhs) in enumerate(((rightt_ref, gor_ref), (leftt_ref, goc_ref))):
        total = lax.dot_general(
            lhs[...], rhs[...], (((0,), (0,)), ((), ())), preferred_element_type=f32
        )
        total = (total * mask_lanes).astype(bf16).astype(f32)
        for y in range(2):
            for e in range(depths):
                block = total[e * seqs : (e + 1) * seqs, y * lanes : (y + 1) * lanes]
                for r in range(res):
                    gs_ref[at, y, e, pl.ds(r, seqs, stride=res), :] = jnp.where(
                        lane_group == r, block, 0.0
                    )
    spread_ref[...] = jnp.concatenate(
        [gs_ref[0, me_y, me_depth], gs_ref[1, me_y, me_depth]], axis=1
    ).astype(bf16)
    rows = rows_ref.shape[2]
    for at in range(2):
        cross = lax.dot_general(
            gs_ref[at].reshape(2 * depths * rows, lanes).astype(bf16),
            rows_ref[...].reshape(2 * depths * rows, rows_ref.shape[3]),
            (((0,), (0,)), ((), ())),
            preferred_element_type=f32,
        )
        total = cross[:width]
        for r in range(1, res):
            total = total + cross[r * width : (r + 1) * width]
        part_ref[at * width : (at + 1) * width, :] = total.astype(bf16)


def weights_kernel(outer_ref, opm_ref, pn_ref, gh_ref, hidden_ref, mg_ref, out_ref, turn_ref):
    pair_width, hid = pn_ref.shape[1], gh_ref.shape[1]
    outer_width = outer_ref.shape[1]
    width = int(outer_width**0.5 + 0.5)

    def contract(lhs, rhs):
        return lax.dot_general(
            lhs[...], rhs[...], (((0,), (0,)), ((), ())), preferred_element_type=jnp.float32
        )

    turn_ref[...] = contract(outer_ref, opm_ref)
    for c in range(width):
        out_ref[c * width : (c + 1) * width, :] = turn_ref[
            pl.ds(c, width, stride=width), :
        ].astype(jnp.bfloat16)
    dhid = contract(pn_ref, gh_ref).astype(jnp.bfloat16)
    for at in range(hid // pair_width):
        first = outer_width + at * pair_width
        out_ref[first : first + pair_width, :] = dhid[:, at * pair_width : (at + 1) * pair_width]
    out_ref[outer_width + hid :, :] = contract(hidden_ref, mg_ref).astype(jnp.bfloat16)


def weights_sum_kernel(mine_ref, other_ref, dout_ref, dhid_ref, dback_ref):
    pair_width, hid = dhid_ref.shape
    outer_width = dout_ref.shape[0]

    def added(first, count):
        rows = slice(first, first + count)
        return mine_ref[rows, :].astype(jnp.float32) + other_ref[rows, :].astype(jnp.float32)

    dout_ref[...] = added(0, outer_width)
    for at in range(hid // pair_width):
        dhid_ref[:, at * pair_width : (at + 1) * pair_width] = added(
            outer_width + at * pair_width, pair_width
        )
    dback_ref[...] = added(outer_width + hid, hid)


def feature_kernel(
    copies,
    spread_ref,
    first_ref,
    second_ref,
    scale_ref,
    scaled_ref,
    inv_ref,
    held_ref,
    feat_ref,
    couple_ref,
):
    back = jnp.dot(
        spread_ref[...],
        wide_projector(first_ref, second_ref, copies),
        preferred_element_type=jnp.float32,
    )
    feat = standardize_adjoint(back * scale_ref[...], scaled_ref[...], inv_ref[...])
    feat_ref[...] = feat.reshape(feat_ref.shape).astype(jnp.bfloat16)
    couple_ref[...] = held_ref[...]


def swap_line(block, partners):
    count = lax.axis_size("col")
    pairs = [
        (depth * count + at, depth * count + (at ^ partner))
        for depth, partner in enumerate(partners)
        if partner is not None
        for at in range(count)
    ]
    return lax.ppermute(block, ("depth", "col"), pairs)


def swap_depth(block):
    return lax.ppermute(block, "depth", [(0, 1), (1, 0)])


def pairwise_sum(blocks):
    while len(blocks) > 1:
        blocks = [blocks[at] + blocks[at + 1] for at in range(0, len(blocks), 2)]
    return blocks[0]


def swap_col(block, partner):
    count = lax.axis_size("col")
    return lax.ppermute(block, "col", [(at, at ^ partner) for at in range(count)])


def whole_plan(
    alignment_activations,
    alignment_mask,
    pair_activation_input,
    pair_update_mask,
    pair_output_gradient,
    layer_scale_factor,
    first_projector,
    second_projector,
    output_weight,
    pair_norm_gain,
    hidden_weight,
    back_weight,
):
    seqs, res, channels = alignment_activations.shape
    width = first_projector.shape[1]
    outer_width = width * width
    cols = lax.axis_size("col")
    depths = lax.axis_size("depth")
    residues = res * cols
    pair_cols, pair_width = pair_activation_input.shape[1:]
    hid = hidden_weight.shape[1]
    per = res * pair_cols
    lanes = res * width
    rows = 2 * seqs + MASK_ROWS
    half = residues * pair_cols
    f32, bf16 = jnp.float32, jnp.bfloat16
    ids = jnp.stack([lax.axis_index("depth"), lax.axis_index("col")]).astype(jnp.int32)
    smem = pl.BlockSpec(memory_space=pltpu.SMEM)
    vmem = pl.BlockSpec(memory_space=pltpu.VMEM)
    params = pltpu.CompilerParams(vmem_limit_bytes=16 * 2**20)
    scale = layer_scale_factor.reshape(1, channels)
    first, second = first_projector.T, second_projector.T
    wturn = jnp.transpose(output_weight.reshape(width, width, pair_width), (1, 0, 2)).reshape(
        outer_width, pair_width
    )
    shape = jax.ShapeDtypeStruct
    sent, scale, first, second, gain, normed, scaled, inv = pl.pallas_call(
        pre_kernel,
        out_shape=(
            shape((1, rows + 2 * per, pair_width), bf16),
            shape((1, channels), f32),
            shape((width, channels), bf16),
            shape((width, channels), bf16),
            shape((1, pair_width), f32),
            shape((seqs * res, channels), bf16),
            shape((seqs * res, channels), f32),
            shape((seqs * res, 1), f32),
        ),
        in_specs=[smem] + [pl.BlockSpec(memory_space=pltpu.HBM)] * 9,
        out_specs=[vmem] * 8,
        scratch_shapes=[
            pltpu.VMEM((2, seqs * res, lanes), f32),
            pltpu.VMEM((MASK_ROWS, lanes), f32),
            pltpu.VMEM((seqs, res, channels), bf16),
            pltpu.VMEM((res, seqs), jnp.int32),
            pltpu.VMEM((res, pair_cols), jnp.int32),
            pltpu.SemaphoreType.DMA((9,)),
        ],
        compiler_params=params,
        name="project",
    )(
        ids,
        *[
            pltpu.with_memory_space_constraint(array, pltpu.HBM)
            for array in (
                alignment_activations,
                alignment_mask.T,
                pair_update_mask,
                scale,
                first,
                second,
                pair_norm_gain.reshape(1, pair_width),
                pair_activation_input.reshape(per, pair_width),
                pair_output_gradient.reshape(per, pair_width),
            )
        ],
    )
    blocks = lax.optimization_barrier(
        jnp.concatenate([sent] + [swap_col(sent, partner) for partner in Z_PARTNERS])
    )
    far_normed = swap_col(normed, Y_PARTNER)
    blocks, far_normed = lax.optimization_barrier((blocks, far_normed))
    near, pair_near = blocks[:, :rows], blocks[:, rows:]
    far = swap_col(near, Y_PARTNER)
    pair_far = swap_col(pair_near, Y_PARTNER)
    other_near, other_far = swap_depth(near), swap_depth(far)
    sizes = (seqs, res, pair_cols, width)
    outer, proj_out, cnt, pm, maskt, rightt, leftt = pl.pallas_call(
        functools.partial(outer_kernel, sizes),
        out_shape=(
            shape((half, outer_width), bf16),
            shape((half, pair_width), f32),
            shape((half, lanes), f32),
            shape((half, lanes), bf16),
            shape((residues, depths * seqs), f32),
            shape((residues * width, depths * seqs), bf16),
            shape((residues * width, depths * seqs), bf16),
        ),
        in_specs=[smem] + [vmem] * 5,
        out_specs=[vmem] * 7,
        scratch_shapes=[
            pltpu.VMEM((depths * seqs, residues * width), bf16),
            pltpu.VMEM((pair_cols * width, depths * seqs), bf16),
            pltpu.VMEM((residues * width, depths * seqs), f32),
            pltpu.VMEM((residues * width, depths * seqs), f32),
            pltpu.VMEM((half, lanes), bf16),
            pltpu.VMEM((half, lanes), bf16),
        ],
        compiler_params=params,
        name="outer_products",
    )(ids, near, far, other_near, other_far, wturn)
    other_normed = swap_depth(jnp.concatenate([normed, far_normed]))
    pair_far, proj_out, other_normed = lax.optimization_barrier((pair_far, proj_out, other_normed))
    held, opm, pn, gh, hidden, mg = pl.pallas_call(
        functools.partial(transition_kernel, sizes),
        out_shape=(
            shape((per, pair_width), bf16),
            shape((half, pair_width), bf16),
            shape((half, pair_width), bf16),
            shape((half, hid), bf16),
            shape((half, hid), bf16),
            shape((half, pair_width), bf16),
        ),
        in_specs=[smem] + [vmem] * 8,
        out_specs=[vmem] * 6,
        scratch_shapes=[
            pltpu.VMEM((half, pair_width), f32),
        ],
        compiler_params=params,
        name="transition",
    )(
        ids,
        pair_near,
        pair_far,
        proj_out,
        cnt,
        pm,
        gain,
        hidden_weight,
        back_weight,
    )
    weights = pl.pallas_call(
        weights_kernel,
        out_shape=shape((outer_width + 2 * hid, pair_width), bf16),
        in_specs=[vmem] * 6,
        out_specs=vmem,
        scratch_shapes=[pltpu.VMEM((outer_width, pair_width), f32)],
        compiler_params=params,
        name="weight_gradients",
    )(outer, opm, pn, gh, hidden, mg)
    other_opm, weights = lax.optimization_barrier((swap_depth(opm), weights))
    part, spread = pl.pallas_call(
        functools.partial(projector_kernel, sizes),
        out_shape=(
            shape((2 * width, channels), bf16),
            shape((seqs * res, 2 * lanes), bf16),
        ),
        in_specs=[smem] + [vmem] * 10,
        out_specs=[vmem] * 2,
        scratch_shapes=[
            pltpu.VMEM((half, pair_width), f32),
            pltpu.VMEM((2 * res * residues, pair_width), bf16),
            pltpu.VMEM((2 * res * residues, pair_width), bf16),
            pltpu.VMEM((residues * width, 2 * lanes), bf16),
            pltpu.VMEM((residues * width, 2 * lanes), bf16),
            pltpu.VMEM((2, 2, depths, seqs * res, lanes), f32),
            pltpu.VMEM((2, depths, seqs * res, channels), bf16),
        ],
        compiler_params=params,
        name="projector_parts",
    )(
        ids,
        opm,
        other_opm,
        rightt,
        leftt,
        output_weight,
        wturn,
        maskt,
        normed,
        far_normed,
        other_normed,
    )
    feat, couple = pl.pallas_call(
        functools.partial(feature_kernel, res),
        out_shape=(shape((seqs, res, channels), bf16), shape((per, pair_width), bf16)),
        in_specs=[vmem] * 7,
        out_specs=[vmem] * 2,
        compiler_params=params,
        name="features",
    )(spread, first, second, scale, scaled, inv, held)
    part, weights = lax.optimization_barrier((part, weights))
    dout, dhid, dback = pl.pallas_call(
        weights_sum_kernel,
        out_shape=(
            shape((outer_width, pair_width), f32),
            shape((pair_width, hid), f32),
            shape((hid, pair_width), f32),
        ),
        in_specs=[vmem] * 2,
        out_specs=[vmem] * 3,
        compiler_params=params,
        name="sums_over_depth",
    )(weights, swap_depth(weights))
    came_b = swap_line(part, (None, Z_PARTNERS[0]))
    came_a = swap_line(part, (Z_PARTNERS[2], Z_PARTNERS[1]))
    came_b, came_a, feat, couple = lax.optimization_barrier((came_b, came_a, feat, couple))
    kept = jnp.where(lax.axis_index("depth") == 0, part, came_b)
    kept = lax.optimization_barrier((kept.astype(f32) + came_a.astype(f32)).astype(bf16))
    came = swap_depth(kept)
    came, dout, dhid, dback = lax.optimization_barrier((came, dout, dhid, dback))
    total = kept.astype(f32) + came.astype(f32)
    return (
        feat,
        couple.reshape(res, pair_cols, pair_width),
        total[:width].T,
        total[width:].T,
        dout,
        dhid,
        dback,
    )


def on_device(alignment_activations, *others):
    cols = lax.axis_size("col")
    residues = alignment_activations.shape[1] * cols
    plan = whole_plan if cols == 8 and residues <= FEW_RESIDUES else split_plan
    return plan(alignment_activations, *others)


def solution(mesh):
    in_specs = (
        P(("group", "depth"), "col", None),
        P(("group", "depth"), "col"),
        P(("group", "col"), "depth", None),
        P(("group", "col"), "depth"),
        P(("group", "col"), "depth", None),
        P(),
        P(),
        P(),
        P(),
        P(),
        P(),
        P(),
    )
    out_specs = (
        P(("group", "depth"), "col", None),
        P(("group", "col"), "depth", None),
        P("group", None),
        P("group", None),
        P("group", None),
        P("group", None),
        P("group", None),
    )
    return jax.shard_map(
        on_device, mesh=mesh, in_specs=in_specs, out_specs=out_specs, check_vma=False
    )
```
